128 devices in a mesh: ctx: 16 (over y_lo, z, core), fsdp: 8 (over x, y_hi).
Axes of the slice: x: 4, y: 4 (y_hi: 2, y_lo: 2; y = y_hi * 2 + y_lo), z: 4, core: 2. Of those that a mesh axis runs over, the one named last changes fastest.
Arguments:
- tokens: bfloat16 [8, 2048, 1536], P('fsdp', 'ctx'), may hold values from -6 to 6
- cotangent: bfloat16 [8, 2048, 1536], P('fsdp', 'ctx'), may hold values from -6 to 6
- pair_of: int32 [16], replicated, may hold values from 0 to 15, each once
- routes: int32 [1, 8, 2048, 4], P(None, 'fsdp', 'ctx'), may hold values from 0 to 15, all different within a row; in each aligned block of 128 rows (0 to 127, 128 to 255, ..., all dimensions but the last counted through in order) at most 36 rows name the same one
- attn_gain: bfloat16 [1, 1536], P(None, ('ctx', 'fsdp')), may hold values from 0.5 to 1.5
- moe_gain: bfloat16 [1, 1536], P(None, ('ctx', 'fsdp')), may hold values from 0.5 to 1.5
- w_query: bfloat16 [1, 1536, 1536], P(None, ('ctx', 'fsdp')), may hold values from -0.15625 to 0.15625
- w_key: bfloat16 [1, 1536, 256], P(None, ('ctx', 'fsdp')), may hold values from -0.15625 to 0.15625
- w_value: bfloat16 [1, 1536, 256], P(None, ('ctx', 'fsdp')), may hold values from -0.15625 to 0.15625
- w_out: bfloat16 [1, 1536, 1536], P(None, ('ctx', 'fsdp')), may hold values from -3 to 3
- w_router: bfloat16 [1, 1536, 16], P(None, ('ctx', 'fsdp')), may hold values from -0.078125 to 0.078125
- w_gate: bfloat16 [1, 16, 1536, 768], P(None, 'fsdp', 'ctx'), may hold values from -0.15625 to 0.15625
- w_up: bfloat16 [1, 16, 1536, 768], P(None, 'fsdp', 'ctx'), may hold values from -0.15625 to 0.15625
- w_down: bfloat16 [1, 16, 1536, 768], P(None, 'fsdp', 'ctx'), may hold values from -0.21875 to 0.21875
Outputs:
- output: bfloat16 [8, 2048, 1536], P('fsdp', 'ctx')
- input_grad: float32 [8, 2048, 1536], P('fsdp', 'ctx')
- attn_gain_grad: float32 [1, 1536], P(None, ('ctx', 'fsdp'))
- moe_gain_grad: float32 [1, 1536], P(None, ('ctx', 'fsdp'))
- w_query_grad: float32 [1, 1536, 1536], P(None, ('ctx', 'fsdp'))
- w_key_grad: float32 [1, 1536, 256], P(None, ('ctx', 'fsdp'))
- w_value_grad: float32 [1, 1536, 256], P(None, ('ctx', 'fsdp'))
- w_out_grad: float32 [1, 1536, 1536], P(None, ('ctx', 'fsdp'))
- w_router_grad: float32 [1, 1536, 16], P(None, ('ctx', 'fsdp'))
- w_gate_grad: float32 [1, 16, 1536, 768], P(None, 'fsdp', 'ctx')
- w_up_grad: float32 [1, 16, 1536, 768], P(None, 'fsdp', 'ctx')
- w_down_grad: float32 [1, 16, 1536, 768], P(None, 'fsdp', 'ctx')
The draws below stay inside these ranges and needn't reach their ends.
Inputs may be any that keep to these rules, and one draw needn't show every extreme that they name: `routes`: in each layer every row names 4 different experts; in the rows of one device (aligned blocks of 128 rows of one layer) no expert is named more than 36 times, a bound that some block reaches in every draw. `pair_of`: A permutation of the ctx indices.
All inputs are finite; a program needn't handle non-finite values.
Results may differ from the reference program's by a relative error of at most 0.02.
Values may be sent and summed in bfloat16 or wider, within the bound.
No kernel may reach another device: no remote copies, remote signals or barrier semaphores. Data moves between devices by JAX's collectives and lax.ppermute only.
A program may use at most 192 MiB of HBM per device.

```python
import math
import jax
import jax.numpy as jnp
import numpy as np
from jax import lax

D = 1536
H = 12
KVH = 2
HD = 128
FF = 768
TOPK = 4
TOK_DEV = 128
LAYERS = 1
QW = 1536
KW = 256
LEN = 2048
NSEQ = 8
EXPERTS = 16
CAP = 36
N_CTX = 16


def block_scale(own_key, dims, pieces, smallest, high):
    def one(dim, parts):
        draws = jax.random.uniform(jax.random.fold_in(jax.random.fold_in(own_key, 6), dim), (parts,), jnp.float32, smallest / len(pieces), high / len(pieces))
        return jnp.repeat(jnp.exp(draws), dims[dim] // parts).reshape((-1,) + (1,) * (len(dims) - dim - 1))

    loudness = one(*pieces[0])
    for cut in pieces[1:]:
        loudness = loudness * one(*cut)
    return loudness


def deal_out(key, own, number, rows, number_of, top, bound, slope):
    order = jax.random.permutation(key, number_of)
    heavy_load, common = shares(number_of, rows * top, bound, slope, True), shares(number_of, rows * top, bound, slope, False)
    places = jnp.arange(number_of)

    def named(lengths, offset_by):
        used = int((lengths > 0).sum())
        fixed = max(1, used // 4)
        moved = fixed + (places - fixed + offset_by * (used - fixed)) % max(1, number_of - fixed)
        return jnp.zeros((number_of,), jnp.int32).at[order[jnp.where(places < fixed, places, moved)]].set(jnp.asarray(lengths, jnp.int32))

    lengths = jnp.where(number % 4 == 0, named(heavy_load, number // 4), named(common, number - number // 4 - 1))
    mixed = jax.random.permutation(jax.random.fold_in(own, 3), number_of)
    giver, taker = mixed[0:number_of // 2 * 2:2], mixed[1:number_of // 2 * 2:2]
    slack = jnp.minimum(lengths[giver] - 1, bound - lengths[taker]) // 2
    slack = jnp.where((giver == order[0]) | (taker == order[0]) | (lengths[taker] == 0), 0, jnp.maximum(slack, 0))
    moved = jax.random.randint(jax.random.fold_in(own, 4), (number_of // 2,), 0, 1 << 20) % (slack + 1)
    lengths = lengths.at[giver].add(-moved).at[taker].add(moved)
    members = jnp.searchsorted(jnp.cumsum(lengths), jnp.arange(rows * top), side="right").astype(jnp.int32)
    table = members.reshape(top, rows).T
    table = table[jax.random.permutation(jax.random.fold_in(own, 1), rows)]
    offset_by = jax.random.randint(jax.random.fold_in(own, 2), (rows, 1), 0, top)
    return jnp.take_along_axis(table, (jnp.arange(top)[None, :] + offset_by) % top, axis=1)


def shares(count, total, reach, lean, full):
    portions = [(1 << 20) // math.isqrt(standing ** lean) + 1 for standing in range(1, count + 1)]
    largest = reach if full else min(reach, max(-(-total // count), total * portions[0] // sum(portions)))
    least = 1 if total - largest >= count - 1 else 0
    given, surplus = [largest] + [least] * (count - 1), total - largest - least * (count - 1)
    while surplus > 0:
        movable = [i for i in range(1, count) if given[i] < largest] or [i for i in range(1, count) if given[i] < reach]
        whole, budget = sum([portions[i] for i in movable]), surplus
        for i in movable:
            more = min(reach - given[i], max(1, budget * portions[i] // whole), surplus)
            given[i] = given[i] + more
            surplus = surplus - more
    return np.array(given)


def centred(rng, dims, spread, bound, split=(), kind=jnp.bfloat16):
    values = jax.random.normal(rng, dims, jnp.float32) * spread
    if len(split) > 0:
        values = block_scale(rng, dims, split, -0.22, 0.18) * values
    return jnp.clip(values, min=-bound, max=bound).astype(kind)


def setup_inputs(seed: int = 0) -> dict:
    arg_keys = jax.random.split(jax.random.key(seed), 15)
    tokens = centred(arg_keys[0], (NSEQ, LEN, D), 1.0, 6.0, ((0, 8), (1, 16)))
    cotangent = centred(arg_keys[1], (NSEQ, LEN, D), 1.0, 6.0, ((0, 8), (1, 16)))
    pair_of = jax.random.permutation(arg_keys[2], N_CTX).astype(jnp.int32)
    routes_keys = jax.random.split(jax.random.fold_in(arg_keys[3], 1), LAYERS * NSEQ * LEN // TOK_DEV)
    routes_turns = jax.random.permutation(jax.random.fold_in(arg_keys[3], 3), LAYERS * NSEQ * LEN // TOK_DEV)
    routes = jax.vmap(lambda own, number: deal_out(jax.random.fold_in(arg_keys[3], 2), own, number, TOK_DEV, EXPERTS, TOPK, CAP, 1))(routes_keys, routes_turns).reshape((LAYERS, NSEQ, LEN, TOPK))
    attn_gain = jnp.clip(1.0 + 0.1 * jax.random.normal(arg_keys[4], (LAYERS, D), jnp.float32), 0.5, 1.5).astype(jnp.bfloat16)
    moe_gain = jnp.clip(1.0 + 0.1 * jax.random.normal(arg_keys[5], (LAYERS, D), jnp.float32), 0.5, 1.5).astype(jnp.bfloat16)
    w_query = centred(arg_keys[6], (LAYERS, D, QW), D ** -0.5, 0.15625, ((1, 128),))
    w_key = centred(arg_keys[7], (LAYERS, D, KW), D ** -0.5, 0.15625, ((1, 128),))
    w_value = centred(arg_keys[8], (LAYERS, D, KW), D ** -0.5, 0.15625, ((1, 128),))
    w_out = centred(arg_keys[9], (LAYERS, QW, D), 4 ** -0.5, 3.0, ((1, 128),))
    w_router = centred(arg_keys[10], (LAYERS, D, EXPERTS), (4 * D) ** -0.5, 0.078125, ((1, 128),))
    w_gate = centred(arg_keys[11], (LAYERS, EXPERTS, D, FF), D ** -0.5, 0.15625, ((1, 8), (2, 16)))
    w_up = centred(arg_keys[12], (LAYERS, EXPERTS, D, FF), D ** -0.5, 0.15625, ((1, 8), (2, 16)))
    w_down = centred(arg_keys[13], (LAYERS, EXPERTS, D, FF), FF ** -0.5, 0.21875, ((1, 8), (2, 16)))
    return dict(tokens=tokens, cotangent=cotangent, pair_of=pair_of, routes=routes, attn_gain=attn_gain, moe_gain=moe_gain, w_query=w_query, w_key=w_key, w_value=w_value, w_out=w_out, w_router=w_router, w_gate=w_gate, w_up=w_up, w_down=w_down)


EPSILON = 1e-06
ROPE_BASE = 1000000.0
NEGATIVE = -1e+30

@jax.custom_vjp
def low(v):
    return lax.optimization_barrier(v.astype(jnp.bfloat16)).astype(jnp.float32)

@jax.custom_vjp
def low_back(v):
    return v

def low_keep(v):
    return (low(v), None)

def low_pass(kept, grad):
    return (grad,)

def back_keep(v):
    return (v, None)

def back_low(kept, grad):
    return (low(grad),)
low.defvjp(low_keep, low_pass)
low_back.defvjp(back_keep, back_low)

def product(left, right):
    return jnp.dot(left, right, precision=lax.Precision.HIGHEST)

def rms_norm(stream, gain):
    return stream * lax.rsqrt(lax.optimization_barrier(jnp.mean(stream * stream, axis=-1, keepdims=True)) + EPSILON) * gain

def place_of(pair_of, row_index):
    half_size = TOK_DEV // 2
    within = row_index % TOK_DEV
    pair_index = pair_of[row_index // TOK_DEV]
    block_index = jnp.where(within < half_size, pair_index, 2 * N_CTX - 1 - pair_index)
    return (block_index * half_size + within % half_size).astype(jnp.int32)

def angles_of(positions):
    freq_index = jnp.arange(HD // 2, dtype=jnp.float32)
    frequency = jnp.exp(freq_index * (-2.0 * math.log(ROPE_BASE) / HD))
    return positions.astype(jnp.float32)[:, None] * frequency[None, :]

def rotate(vectors, angles):
    half_size = vectors.shape[-1] // 2
    cosines = jnp.cos(angles)[:, None, :]
    sine_table = jnp.sin(angles)[:, None, :]
    first_half = vectors[..., :half_size]
    second_half = vectors[..., half_size:]
    return jnp.concatenate([first_half * cosines - second_half * sine_table, second_half * cosines + first_half * sine_table], axis=-1)

def head_attention(queries, key_rows, value_rows, positions):
    scores = low_back(1.0 / math.sqrt(HD) * product(queries, key_rows.T))
    allowed = positions[None, :] <= positions[:, None]
    scores = jnp.where(allowed, scores, NEGATIVE)
    highest = lax.optimization_barrier(jnp.max(scores, axis=-1, keepdims=True))
    exponent = jnp.exp(scores - highest)
    attn_probs = exponent / lax.optimization_barrier(jnp.sum(exponent, axis=-1, keepdims=True))
    return product(low(attn_probs), value_rows)

def destinations(chosen):
    expert_hits = (chosen[:, :, None] == jnp.arange(EXPERTS, dtype=jnp.int32)[None, None, :]).astype(jnp.int32)
    counts = lax.optimization_barrier(jnp.sum(expert_hits, axis=1)).astype(jnp.int32).reshape(N_CTX, TOK_DEV, EXPERTS)
    before = (jnp.cumsum(counts, axis=1).astype(jnp.int32) - counts).reshape(LEN, EXPERTS)
    slot_index = lax.optimization_barrier(jnp.sum(expert_hits * before[:, None, :], axis=-1)).astype(jnp.int32)
    block_index = (jnp.arange(LEN, dtype=jnp.int32) // TOK_DEV)[:, None]
    return (chosen * (N_CTX * CAP) + block_index * CAP + slot_index).astype(jnp.int32)

def layer(stream, weights, chosen, positions, angles):
    attn_gain, moe_gain, w_query, w_key, w_value, w_out, w_router, w_gate, w_up, w_down = weights
    normed = low(rms_norm(stream, attn_gain))
    queries = low(rotate(low_back(product(normed, w_query)).reshape(LEN, H, HD), angles))
    key_rot = low(rotate(low_back(product(normed, w_key)).reshape(LEN, KVH, HD), angles))
    value_rows = low_back(low(product(normed, w_value))).reshape(LEN, KVH, HD)
    per_group = H // KVH
    key_heads = jnp.repeat(key_rot, per_group, axis=1)
    value_heads = jnp.repeat(value_rows, per_group, axis=1)
    attend = jax.checkpoint(lambda triple: head_attention(triple[0], triple[1], triple[2], positions))
    head_outputs = lax.map(attend, (queries.transpose(1, 0, 2), key_heads.transpose(1, 0, 2), value_heads.transpose(1, 0, 2)))
    mixed_heads = low_back(low(head_outputs.transpose(1, 0, 2).reshape(LEN, QW)))
    midway = stream + low_back(product(mixed_heads, w_out))
    moe_input = low(rms_norm(midway, moe_gain))
    logits = low_back(product(moe_input, w_router))
    picked = jnp.take_along_axis(logits, chosen, axis=1)
    highest = lax.optimization_barrier(jnp.max(picked, axis=-1, keepdims=True))
    exponent = jnp.exp(picked - highest)
    gate_values = exponent / lax.optimization_barrier(jnp.sum(exponent, axis=-1, keepdims=True))
    target = destinations(chosen).reshape(-1)
    source_table = jnp.full((EXPERTS * N_CTX * CAP,), LEN, dtype=jnp.int32)
    source_table = source_table.at[target].set(jnp.repeat(jnp.arange(LEN, dtype=jnp.int32), TOPK))
    padded = jnp.concatenate([moe_input, jnp.zeros((1, D), dtype=moe_input.dtype)], axis=0)
    expert_rows = padded[source_table].reshape(EXPERTS, N_CTX * CAP, D)
    gate_pre = low_back(jnp.einsum('erd,edf->erf', expert_rows, w_gate, precision=lax.Precision.HIGHEST))
    up_pre = low_back(jnp.einsum('erd,edf->erf', expert_rows, w_up, precision=lax.Precision.HIGHEST))
    hidden = low(gate_pre * jax.nn.sigmoid(gate_pre) * up_pre)
    expert_out = low_back(low(jnp.einsum('erf,edf->erd', hidden, w_down, precision=lax.Precision.HIGHEST)))
    returned_rows = expert_out.reshape(-1, D)[target].reshape(LEN, TOPK, D)
    return midway + lax.optimization_barrier(jnp.sum(gate_values[:, :, None] * returned_rows, axis=1))

def reference(tokens, cotangent, pair_of, routes, attn_gain, moe_gain, w_query, w_key, w_value, w_out, w_router, w_gate, w_up, w_down):
    weights = tuple((array.astype(jnp.float32) for array in (attn_gain, moe_gain, w_query, w_key, w_value, w_out, w_router, w_gate, w_up, w_down)))
    positions = place_of(pair_of, jnp.arange(LEN, dtype=jnp.int32))
    angles = angles_of(positions)

    def forward(stream, params, chosen):
        for layer_index in range(LAYERS):
            stream = layer(stream, tuple((param[layer_index] for param in params)), chosen[layer_index], positions, angles)
        return stream

    def sequence_step(totals, inputs):
        stream, gradient, chosen = inputs
        result, pullback = jax.vjp(lambda first_arg, second_arg: forward(first_arg, second_arg, chosen), stream.astype(jnp.float32), weights)
        stream_grad, param_grads = pullback(gradient.astype(jnp.float32))
        totals = jax.tree.map(jnp.add, totals, param_grads)
        return (totals, (result.astype(jnp.bfloat16), stream_grad))
    zero_grads = jax.tree.map(jnp.zeros_like, weights)
    totals, (output, input_grad) = lax.scan(sequence_step, zero_grads, (tokens, cotangent, jnp.transpose(routes, (1, 0, 2, 3))))
    return (output, input_grad, totals[0], totals[1], totals[2], totals[3], totals[4], totals[5], totals[6], totals[7], totals[8], totals[9])
```

```python
import math

import jax
import jax.numpy as jnp
from jax import lax
from jax.sharding import Mesh
from jax.sharding import PartitionSpec as P

H = 12
KVH = 2
HD = 128
TOPK = 4

EPSILON = 1e-06
ROPE_BASE = 1000000.0
NEGATIVE = -1e30

AXES = ("ylo", "z", "core", "x", "yhi")
CTX = ("ylo", "z", "core")
FSDP = ("x", "yhi")
OWNERS = ("x", "yhi", "core")
RING = ("ylo", "z")
CHIPS = ("ylo", "z", "x", "yhi")
SLOTS = 40

bf16 = jnp.bfloat16
f32 = jnp.float32


def dot(left, right):
    return jnp.dot(left, right, preferred_element_type=f32)


def dot_t(left, right):
    return lax.dot_general(left, right, (((1,), (1,)), ((), ())), preferred_element_type=f32)


def t_dot(left, right):
    return lax.dot_general(left, right, (((0,), (0,)), ((), ())), preferred_element_type=f32)


def exchange(pieces, axes):
    return lax.all_to_all(pieces, axes, split_axis=0, concat_axis=0, tiled=True)


def spread(piece, count, axes):
    return exchange(jnp.broadcast_to(piece[None], (count,) + piece.shape), axes)


def partner(value):
    return lax.ppermute(value, "core", [(0, 1), (1, 0)])


def crossed(value):
    return lax.ppermute(value, ("ylo", "core"), [(0, 0), (1, 2), (2, 1), (3, 3)])


def rotate(vectors, cosines, sines):
    half = vectors.shape[-1] // 2
    first, second = vectors[..., :half], vectors[..., half:]
    return jnp.concatenate(
        [first * cosines - second * sines, second * cosines + first * sines], axis=-1
    )


def place_of(pair_of, row_index, row_count, ctx_count):
    half_size = row_count // 2
    within = row_index % row_count
    pair_index = pair_of[row_index // row_count]
    block_index = jnp.where(within < half_size, pair_index, 2 * ctx_count - 1 - pair_index)
    return block_index * half_size + within % half_size


def body(
    tokens,
    cotangent,
    pair_of,
    routes,
    attn_gain,
    moe_gain,
    w_query,
    w_key,
    w_value,
    w_out,
    w_router,
    w_gate,
    w_up,
    w_down,
):
    rows = tokens.shape[1]
    half = rows // 2
    width = tokens.shape[2]
    shard = w_query.shape[1]
    ctx_count = 16
    devices = 128
    seq_length = rows * ctx_count
    experts = w_router.shape[2]
    per_group = H // KVH
    qw = per_group * HD
    cols = qw + 2 * HD
    scale = 1.0 / math.sqrt(HD)
    core = lax.axis_index("core")
    chip = lax.axis_index("ylo") * 4 + lax.axis_index("z")

    def halves(matrix):
        return matrix.reshape(shard, 2, -1).transpose(1, 0, 2)

    packed = jnp.concatenate([halves(w_query[0]), halves(w_key[0]), halves(w_value[0])], axis=-1)
    packed = packed.reshape(1, 2, 1, shard * cols // 128, 128)
    packed = jnp.broadcast_to(packed, (8, 2, 8) + packed.shape[3:]).reshape(
        devices, shard * cols // 128, 128
    )
    w_qkv = exchange(packed, AXES).reshape(width, cols)

    small = jnp.concatenate([w_router[0], attn_gain[0][:, None], moe_gain[0][:, None]], axis=-1)
    small_count = experts + 2
    small = jnp.pad(small.reshape(-1), (0, 1024 - shard * small_count)).reshape(8, 128)
    small = spread(small, devices, AXES).reshape(devices, 1024)
    small = small[:, : shard * small_count].reshape(width, small_count)
    router = small[:, :experts]
    gain_one = small[:, experts].astype(f32)
    gain_two = small[:, experts + 1].astype(f32)

    wo = spread(crossed(w_out[0]).reshape(-1, 128), 64, CHIPS)
    wo = wo.reshape(2, 4, 8 * shard, width).transpose(1, 0, 2, 3).reshape(qw, width)

    def whole_expert(matrix):
        piece = jnp.broadcast_to(matrix[0][None], (8,) + matrix.shape[1:])
        return exchange(piece.reshape((ctx_count,) + matrix.shape[2:]), CTX).reshape(width, -1)

    gate_w = whole_expert(w_gate)
    up_w = whole_expert(w_up)
    down_w = whole_expert(w_down)

    chosen = routes[0, 0]
    hits = (chosen[:, :, None] == jnp.arange(experts, dtype=jnp.int32)[None, None, :]).astype(
        jnp.int32
    )
    counts = jnp.sum(hits, axis=1)
    before = jnp.cumsum(counts, axis=0) - counts
    slot_index = jnp.sum(hits * before[:, None, :], axis=-1)
    target = chosen * SLOTS + slot_index
    slots = experts * SLOTS
    slot_row = jnp.arange(slots, dtype=jnp.int32)
    selector = target[:, :, None] == slot_row[None, None, :]
    placer = jnp.any(selector, axis=1).astype(bf16)
    cot = cotangent[0]
    sent_grad = t_dot(placer, cot).astype(bf16).reshape(experts, SLOTS, width)
    arrived_cot = exchange(sent_grad, OWNERS).reshape(slots, width)

    both = jnp.concatenate([tokens[0], partner(tokens[0])], axis=0).astype(f32)
    stream = both[:rows]
    inverse_one = lax.rsqrt(jnp.mean(both * both, axis=-1, keepdims=True) + EPSILON)
    normal_one = both * inverse_one
    normed = (normal_one * gain_one).astype(bf16)

    local_place = place_of(
        pair_of, ordered_all((chip * 2 + core).reshape(1, 1), rows, core), rows, ctx_count
    )
    all_chips = jnp.arange(8, dtype=jnp.int32)[:, None] * 2 + core
    key_place = place_of(pair_of, ordered_all(all_chips, rows, core), rows, ctx_count)
    frequency = jnp.exp(
        jnp.arange(HD // 2, dtype=f32) * (-2.0 * math.log(ROPE_BASE) / HD)
    )
    angles = local_place.astype(f32)[:, None] * frequency[None, :]
    cosines = jnp.cos(angles)[:, None, :]
    sines = jnp.sin(angles)[:, None, :]

    qkv = dot(normed, w_qkv)
    rotated = rotate(qkv[:, : qw + HD].reshape(2 * rows, per_group + 1, HD), cosines, sines)
    queries = rotated[:, :per_group].astype(bf16)
    key_value = jnp.concatenate(
        [rotated[:, per_group].astype(bf16), qkv[:, qw + HD :].astype(bf16)], axis=-1
    )
    all_kv = spread(key_value, 8, RING)

    def lower_of(full):
        shape = full.shape
        return full.reshape((-1, 2, half) + shape[1:])[:, 0].reshape((-1,) + shape[1:])

    def upper_of(full):
        shape = full.shape
        return full.reshape((-1, 2, half) + shape[1:])[:, 1].reshape((-1,) + shape[1:])

    all_kv = all_kv.reshape(seq_length, 2 * HD)
    key_all, value_all = all_kv[:, :HD], all_kv[:, HD:]
    low_kv = lower_of(all_kv)
    key_low, value_low = low_kv[:, :HD], low_kv[:, HD:]
    place_low = lower_of(local_place)
    place_up = upper_of(local_place)
    key_place_low = lower_of(key_place)

    def by_head(matrix):
        return matrix.transpose(1, 0, 2)

    q_low = by_head(lower_of(queries))
    q_up = by_head(upper_of(queries))

    def scores_of(q, keys, q_places, k_places):
        raw = jnp.einsum("hqd,kd->hqk", q, keys, preferred_element_type=f32) * scale
        return jnp.where(k_places[None, None, :] <= q_places[None, :, None], raw, NEGATIVE)

    def attend(q, keys, values, q_places, k_places):
        scores = scores_of(q, keys, q_places, k_places)
        highest = jnp.max(scores, axis=-1, keepdims=True)
        exponent = jnp.exp(scores - highest)
        totals = jnp.sum(exponent, axis=-1, keepdims=True)
        probs = exponent / totals
        mixed = jnp.einsum("hqk,kd->hqd", probs.astype(bf16), values, preferred_element_type=f32)
        return mixed, highest + jnp.log(totals)

    mixed_low, total_low = attend(q_low, key_low, value_low, place_low, key_place_low)
    mixed_up, total_up = attend(q_up, key_all, value_all, place_up, key_place)

    def interleave(low, up):
        parts = jnp.stack([low.reshape(-1, 2, half, HD), up.reshape(-1, 2, half, HD)], axis=2)
        return parts.transpose(1, 2, 3, 0, 4).reshape(2 * rows, -1)

    mixed = interleave(mixed_low.astype(bf16), mixed_up.astype(bf16))
    branch = dot(mixed, wo)
    midway = stream + (branch[:rows] + partner(branch[rows:]))

    inverse_two = lax.rsqrt(jnp.mean(midway * midway, axis=-1, keepdims=True) + EPSILON)
    normal_two = midway * inverse_two
    moe_low = (normal_two * gain_two).astype(bf16)
    logits = dot(moe_low, router)
    picked = jnp.take_along_axis(logits, chosen, axis=1)
    exp_pick = jnp.exp(picked - jnp.max(picked, axis=-1, keepdims=True))
    gates = exp_pick / jnp.sum(exp_pick, axis=-1, keepdims=True)
    gate_at = jnp.sum(jnp.where(selector, gates[:, :, None], 0.0), axis=1)
    gate_slot = jnp.sum(gate_at, axis=0)
    sent_gates = jnp.pad(
        gate_slot.reshape(experts, SLOTS), ((0, 0), (0, 1024 - SLOTS))
    ).reshape(experts, 8, 128)
    sent_rows = t_dot(placer, moe_low).astype(bf16).reshape(experts, SLOTS, width)
    arrived = exchange(sent_rows, OWNERS).reshape(slots, width)
    arrived_gates = (
        exchange(sent_gates, OWNERS).reshape(experts, 1024)[:, :SLOTS].reshape(slots, 1)
    )
    gate_pre = dot(arrived, gate_w)
    up_pre = dot(arrived, up_w)
    sigmoid = jax.nn.sigmoid(gate_pre)
    hidden = (gate_pre * sigmoid * up_pre).astype(bf16)
    expert_out = dot_t(hidden, down_w).astype(bf16)
    out_grad = (arrived_gates * arrived_cot.astype(f32)).astype(bf16)
    hidden_grad = dot(out_grad, down_w)
    gate_grad = (hidden_grad * up_pre * sigmoid * (1.0 + gate_pre * (1.0 - sigmoid))).astype(bf16)
    up_grad = (hidden_grad * gate_pre * sigmoid).astype(bf16)
    rows_grad = (dot_t(gate_grad, gate_w) + dot_t(up_grad, up_w)).astype(bf16)
    back = jnp.concatenate([expert_out, rows_grad], axis=-1).reshape(experts, SLOTS, 2 * width)
    back = exchange(back, OWNERS).reshape(slots, 2 * width)
    returned, home_grad = back[:, :width], back[:, width:]

    def expert_shards(grad):
        grad = exchange(grad.astype(bf16).reshape(ctx_count, -1, grad.shape[1]), CTX)
        return jnp.sum(grad.reshape((8, 2) + grad.shape[1:]).astype(f32), axis=0)[None]

    w_gate_grad = expert_shards(t_dot(arrived, gate_grad))
    w_up_grad = expert_shards(t_dot(arrived, up_grad))
    w_down_grad = expert_shards(t_dot(out_grad, hidden))

    gate_high = gate_at.astype(bf16)
    gate_rest = gate_at - gate_high.astype(f32)
    gate_mid = gate_rest.astype(bf16)
    gate_last = (gate_rest - gate_mid.astype(f32)).astype(bf16)
    result = midway + (
        dot(gate_high, returned) + (dot(gate_mid, returned) + dot(gate_last, returned))
    )
    output = result.astype(bf16)[None]

    gradient = cot.astype(f32)
    agreement = dot_t(cot, returned)
    gates_grad = jnp.sum(jnp.where(selector, agreement[:, None, :], 0.0), axis=-1)
    picked_grad = gates * (gates_grad - jnp.sum(gates * gates_grad, axis=-1, keepdims=True))
    logit_grad = jnp.sum(picked_grad[:, :, None] * hits.astype(f32), axis=1).astype(bf16)
    moe_grad = dot(placer, home_grad) + dot_t(logit_grad, router)
    router_grad = t_dot(moe_low, logit_grad)
    gain_two_grad = jnp.sum(moe_grad * normal_two, axis=0)
    scaled = moe_grad * gain_two
    midway_grad = gradient + inverse_two * (
        scaled - normal_two * jnp.mean(scaled * normal_two, axis=-1, keepdims=True)
    )
    branch_low = midway_grad.astype(bf16)
    branch_both = jnp.concatenate([branch_low, partner(branch_low)], axis=0)
    out_w_grad = t_dot(mixed, branch_both).astype(bf16)
    out_w_grad = (
        out_w_grad.reshape(4, 2, 8, shard * width // 128, 128)
        .transpose(1, 0, 2, 3, 4)
        .reshape(64, shard * width // 128, 128)
    )
    out_w_grad = jnp.sum(exchange(out_w_grad, CHIPS).astype(f32), axis=0).reshape(shard, width)
    out_w_grad = crossed(out_w_grad)
    mixed_grad = dot_t(branch_both, wo).astype(bf16).reshape(2 * rows, per_group, HD)

    def attend_back(q, keys, values, q_places, k_places, log_total, grad):
        scores = scores_of(q, keys, q_places, k_places)
        probs = jnp.exp(scores - log_total)
        prob_grad = jnp.einsum("hqd,kd->hqk", grad, values, preferred_element_type=f32)
        score_grad = (
            probs * (prob_grad - jnp.sum(probs * prob_grad, axis=-1, keepdims=True))
        ).astype(bf16)
        q_part = (
            jnp.einsum("hqk,kd->hqd", score_grad, keys, preferred_element_type=f32) * scale
        )
        k_part = jnp.einsum("hqk,hqd->kd", score_grad, q, preferred_element_type=f32) * scale
        v_part = jnp.einsum("hqk,hqd->kd", probs.astype(bf16), grad, preferred_element_type=f32)
        return q_part, jnp.concatenate([k_part, v_part], axis=-1)

    grad_low = by_head(lower_of(mixed_grad))
    grad_up = by_head(upper_of(mixed_grad))
    dq_low, dkv_low = attend_back(
        q_low, key_low, value_low, place_low, key_place_low, total_low, grad_low
    )
    dq_up, dkv_up = attend_back(q_up, key_all, value_all, place_up, key_place, total_up, grad_up)
    dkv = dkv_up.reshape(ctx_count, 2, half, 2 * HD)
    dkv_low = dkv_low.reshape(ctx_count, 1, half, 2 * HD)
    dkv = dkv + jnp.concatenate([dkv_low, jnp.zeros_like(dkv_low)], axis=1)
    dkv = exchange(dkv.astype(bf16).reshape(8, 2 * rows, 2 * HD), RING)
    dkv = jnp.sum(dkv.astype(f32), axis=0)
    dq = rotate(interleave(dq_low, dq_up).reshape(2 * rows, per_group, HD), cosines, -sines)
    dk = rotate(dkv[:, None, :HD], cosines, -sines)
    dqkv = jnp.concatenate(
        [dq.reshape(2 * rows, qw), dk.reshape(2 * rows, HD), dkv[:, HD:]], axis=-1
    ).astype(bf16)
    qkv_w_grad = t_dot(normed, dqkv).astype(bf16).reshape(devices, shard * cols // 128, 128)
    qkv_w_grad = exchange(qkv_w_grad, AXES).astype(f32)
    qkv_w_grad = jnp.sum(
        qkv_w_grad.reshape(8, 2, 8, shard * cols // 128, 128), axis=(0, 2)
    ).reshape(2, shard, cols)

    def joined(first, last):
        return qkv_w_grad[:, :, first:last].transpose(1, 0, 2).reshape(1, shard, -1)

    w_query_grad = joined(0, qw)
    w_key_grad = joined(qw, qw + HD)
    w_value_grad = joined(qw + HD, cols)

    normed_part = dot_t(dqkv, w_qkv)
    normed_grad = normed_part[:rows] + partner(normed_part[rows:])
    own_normal, own_inverse = normal_one[:rows], inverse_one[:rows]
    gain_one_grad = jnp.sum(normed_grad * own_normal, axis=0)
    scaled = normed_grad * gain_one
    input_grad = midway_grad + own_inverse * (
        scaled - own_normal * jnp.mean(scaled * own_normal, axis=-1, keepdims=True)
    )

    small_grad = jnp.concatenate(
        [router_grad, gain_one_grad[:, None], gain_two_grad[:, None]], axis=-1
    ).reshape(devices, shard * small_count)
    small_grad = jnp.pad(small_grad, ((0, 0), (0, 1024 - shard * small_count)))
    small_grad = exchange(small_grad.reshape(devices, 8, 128), AXES)
    small_grad = jnp.sum(small_grad, axis=0).reshape(1024)[: shard * small_count]
    small_grad = small_grad.reshape(1, shard, small_count)

    return (
        output,
        input_grad[None],
        small_grad[:, :, experts],
        small_grad[:, :, experts + 1],
        w_query_grad,
        w_key_grad,
        w_value_grad,
        out_w_grad[None],
        small_grad[:, :, :experts],
        w_gate_grad,
        w_up_grad,
        w_down_grad,
    )


def ordered_all(first_ctx, rows, core):
    index = jnp.arange(rows, dtype=jnp.int32)[None, :]
    return jnp.concatenate(
        [first_ctx * rows + index, (first_ctx + 1 - 2 * core) * rows + index], axis=-1
    ).reshape(-1)


def solution(mesh):
    fine = Mesh(mesh.devices.reshape(2, 4, 2, 4, 2), AXES)
    seq = P(FSDP, CTX, None)
    vector = P(None, AXES)
    matrix = P(None, AXES, None)
    expert = P(None, FSDP, CTX, None)
    in_specs = (
        seq,
        seq,
        P(),
        P(None, FSDP, CTX, None),
        vector,
        vector,
        matrix,
        matrix,
        matrix,
        matrix,
        matrix,
        expert,
        expert,
        expert,
    )
    out_specs = (
        seq,
        seq,
        vector,
        vector,
        matrix,
        matrix,
        matrix,
        matrix,
        matrix,
        expert,
        expert,
        expert,
    )
    return jax.shard_map(body, mesh=fine, in_specs=in_specs, out_specs=out_specs, check_vma=False)
```

```python
import math

import jax
import jax.numpy as jnp
from jax import lax
from jax.sharding import Mesh
from jax.sharding import PartitionSpec as P

H = 12
KVH = 2
HD = 128
TOPK = 4

EPSILON = 1e-06
ROPE_BASE = 1000000.0
NEGATIVE = -1e30

AXES = ("ylo", "z", "core", "x", "yhi")
CTX = ("ylo", "z", "core")
FSDP = ("x", "yhi")
OWNERS = ("x", "yhi", "core")
RING = ("ylo", "z")
CHIPS = ("ylo", "z", "x", "yhi")
SLOTS = 40

bf16 = jnp.bfloat16
f32 = jnp.float32


def dot(left, right):
    return jnp.dot(left, right, preferred_element_type=f32)


def dot_t(left, right):
    return lax.dot_general(left, right, (((1,), (1,)), ((), ())), preferred_element_type=f32)


def t_dot(left, right):
    return lax.dot_general(left, right, (((0,), (0,)), ((), ())), preferred_element_type=f32)


def exchange(pieces, axes):
    return lax.all_to_all(pieces, axes, split_axis=0, concat_axis=0, tiled=True)


def spread(piece, count, axes):
    return exchange(jnp.broadcast_to(piece[None], (count,) + piece.shape), axes)


def after(value, earlier):
    return lax.optimization_barrier((value, earlier))[0]


def partner(value):
    return lax.ppermute(value, "core", [(0, 1), (1, 0)])


def crossed(value):
    return lax.ppermute(value, ("ylo", "core"), [(0, 0), (1, 2), (2, 1), (3, 3)])


def rotate(vectors, cosines, sines):
    half = vectors.shape[-1] // 2
    first, second = vectors[..., :half], vectors[..., half:]
    return jnp.concatenate(
        [first * cosines - second * sines, second * cosines + first * sines], axis=-1
    )


def place_of(pair_of, row_index, row_count, ctx_count):
    half_size = row_count // 2
    within = row_index % row_count
    pair_index = pair_of[row_index // row_count]
    block_index = jnp.where(within < half_size, pair_index, 2 * ctx_count - 1 - pair_index)
    return block_index * half_size + within % half_size


def body(
    tokens,
    cotangent,
    pair_of,
    routes,
    attn_gain,
    moe_gain,
    w_query,
    w_key,
    w_value,
    w_out,
    w_router,
    w_gate,
    w_up,
    w_down,
):
    rows = tokens.shape[1]
    half = rows // 2
    width = tokens.shape[2]
    shard = w_query.shape[1]
    ctx_count = 16
    devices = 128
    seq_length = rows * ctx_count
    experts = w_router.shape[2]
    per_group = H // KVH
    qw = per_group * HD
    scale = 1.0 / math.sqrt(HD)
    core = lax.axis_index("core")
    chip = lax.axis_index("ylo") * 4 + lax.axis_index("z")

    def halves(matrix):
        return matrix.reshape(shard, 2, -1).transpose(1, 0, 2)

    def to_all(pair):
        pair = jnp.broadcast_to(pair[None, :, None], (8, 2, 8) + pair.shape[1:])
        return exchange(pair.reshape((devices,) + pair.shape[3:]), AXES)

    small_count = experts + 2
    small = jnp.concatenate([w_router[0], attn_gain[0][:, None], moe_gain[0][:, None]], axis=-1)
    small = jnp.pad(small.reshape(-1), (0, 1024 - shard * small_count)).reshape(1, 8, 128)
    kv_rows = shard * 2 * HD // 128
    first = jnp.concatenate([halves(w_key[0]), halves(w_value[0])], axis=-1)
    first = jnp.concatenate(
        [first.reshape(2, kv_rows, 128), jnp.broadcast_to(small, (2, 8, 128))], axis=1
    )
    first = to_all(first)
    w_kv = first[:, :kv_rows].reshape(width, 2 * HD)
    small = first[:, kv_rows:].reshape(devices, 1024)
    small = small[:, : shard * small_count].reshape(width, small_count)
    router = small[:, :experts]
    gain_one = small[:, experts].astype(f32)
    gain_two = small[:, experts + 1].astype(f32)
    second = halves(w_query[0]).reshape(2, shard * qw // 128, 128)
    second = after(second, first)
    w_q = to_all(second).reshape(width, qw)

    def whole_expert(matrix):
        both = lax.all_gather(matrix[0], CTX, axis=1, tiled=True)
        return lax.dynamic_index_in_dim(both, core, axis=0, keepdims=False)

    gate_w = whole_expert(w_gate)
    up_w = whole_expert(w_up)
    down_w = whole_expert(w_down)

    chosen = routes[0, 0]
    hits = (chosen[:, :, None] == jnp.arange(experts, dtype=jnp.int32)[None, None, :]).astype(
        jnp.int32
    )
    counts = jnp.sum(hits, axis=1)
    before = jnp.cumsum(counts, axis=0) - counts
    slot_index = jnp.sum(hits * before[:, None, :], axis=-1)
    target = chosen * SLOTS + slot_index
    slots = experts * SLOTS
    slot_row = jnp.arange(slots, dtype=jnp.int32)
    selector = target[:, :, None] == slot_row[None, None, :]
    placer = jnp.any(selector, axis=1).astype(bf16)
    cot = cotangent[0]
    cot_rows = t_dot(placer, cot)

    both = jnp.concatenate([tokens[0], partner(tokens[0])], axis=0).astype(f32)
    stream = both[:rows]
    inverse_one = lax.rsqrt(jnp.mean(both * both, axis=-1, keepdims=True) + EPSILON)
    normal_one = both * inverse_one
    normed = (normal_one * gain_one).astype(bf16)

    local_place = place_of(
        pair_of, ordered_all((chip * 2 + core).reshape(1, 1), rows, core), rows, ctx_count
    )
    all_chips = jnp.arange(8, dtype=jnp.int32)[:, None] * 2 + core
    key_place = place_of(pair_of, ordered_all(all_chips, rows, core), rows, ctx_count)
    frequency = jnp.exp(
        jnp.arange(HD // 2, dtype=f32) * (-2.0 * math.log(ROPE_BASE) / HD)
    )
    angles = local_place.astype(f32)[:, None] * frequency[None, :]
    cosines = jnp.cos(angles)[:, None, :]
    sines = jnp.sin(angles)[:, None, :]

    kv = dot(normed, w_kv)
    keys = rotate(kv[:, None, :HD], cosines, sines)[:, 0]
    key_value = jnp.concatenate([keys.astype(bf16), kv[:, HD:].astype(bf16)], axis=-1)
    all_kv = spread(after(key_value, w_q), 8, RING)
    queries = dot(normed, w_q).reshape(2 * rows, per_group, HD)
    queries = rotate(queries, cosines, sines).astype(bf16)
    wo = after(crossed(w_out[0]).reshape(-1, 128), all_kv)
    wo = spread(wo, 64, CHIPS)
    wo = wo.reshape(2, 4, 8 * shard, width).transpose(1, 0, 2, 3).reshape(qw, width)

    def lower_of(full):
        shape = full.shape
        return full.reshape((-1, 2, half) + shape[1:])[:, 0].reshape((-1,) + shape[1:])

    def upper_of(full):
        shape = full.shape
        return full.reshape((-1, 2, half) + shape[1:])[:, 1].reshape((-1,) + shape[1:])

    all_kv = all_kv.reshape(seq_length, 2 * HD)
    key_all, value_all = all_kv[:, :HD], all_kv[:, HD:]
    low_kv = lower_of(all_kv)
    key_low, value_low = low_kv[:, :HD], low_kv[:, HD:]
    place_low = lower_of(local_place)
    place_up = upper_of(local_place)
    key_place_low = lower_of(key_place)

    def by_head(matrix):
        return matrix.transpose(1, 0, 2)

    q_low = by_head(lower_of(queries))
    q_up = by_head(upper_of(queries))

    def scores_of(q, keys, q_places, k_places):
        raw = jnp.einsum("hqd,kd->hqk", q, keys, preferred_element_type=f32) * scale
        return jnp.where(k_places[None, None, :] <= q_places[None, :, None], raw, NEGATIVE)

    def attend(q, keys, values, q_places, k_places):
        scores = scores_of(q, keys, q_places, k_places)
        highest = jnp.max(scores, axis=-1, keepdims=True)
        exponent = jnp.exp(scores - highest)
        totals = jnp.sum(exponent, axis=-1, keepdims=True)
        probs = exponent / totals
        mixed = jnp.einsum("hqk,kd->hqd", probs.astype(bf16), values, preferred_element_type=f32)
        return mixed, highest + jnp.log(totals)

    mixed_low, total_low = attend(q_low, key_low, value_low, place_low, key_place_low)
    mixed_up, total_up = attend(q_up, key_all, value_all, place_up, key_place)

    def interleave(low, up):
        parts = jnp.stack([low.reshape(-1, 2, half, HD), up.reshape(-1, 2, half, HD)], axis=2)
        return parts.transpose(1, 2, 3, 0, 4).reshape(2 * rows, -1)

    mixed = interleave(mixed_low.astype(bf16), mixed_up.astype(bf16))
    branch = dot(mixed, wo)
    midway = stream + (branch[:rows] + partner(branch[rows:]))

    inverse_two = lax.rsqrt(jnp.mean(midway * midway, axis=-1, keepdims=True) + EPSILON)
    normal_two = midway * inverse_two
    moe_low = (normal_two * gain_two).astype(bf16)
    logits = dot(moe_low, router)
    picked = jnp.take_along_axis(logits, chosen, axis=1)
    exp_pick = jnp.exp(picked - jnp.max(picked, axis=-1, keepdims=True))
    gates = exp_pick / jnp.sum(exp_pick, axis=-1, keepdims=True)
    gate_at = jnp.sum(jnp.where(selector, gates[:, :, None], 0.0), axis=1)
    gate_slot = jnp.sum(gate_at, axis=0)
    sent = jnp.concatenate(
        [t_dot(placer, moe_low).astype(bf16), (gate_slot[:, None] * cot_rows).astype(bf16)],
        axis=-1,
    )
    sent = exchange(sent.reshape(experts, SLOTS, 2 * width), OWNERS).reshape(slots, 2 * width)
    arrived, out_grad = sent[:, :width], sent[:, width:]
    gate_pre = dot(arrived, gate_w)
    up_pre = dot(arrived, up_w)
    sigmoid = jax.nn.sigmoid(gate_pre)
    hidden = (gate_pre * sigmoid * up_pre).astype(bf16)
    expert_out = dot_t(hidden, down_w).astype(bf16)
    hidden_grad = dot(out_grad, down_w)
    gate_grad = (hidden_grad * up_pre * sigmoid * (1.0 + gate_pre * (1.0 - sigmoid))).astype(bf16)
    up_grad = (hidden_grad * gate_pre * sigmoid).astype(bf16)
    rows_grad = (dot_t(gate_grad, gate_w) + dot_t(up_grad, up_w)).astype(bf16)
    back = jnp.concatenate([expert_out, rows_grad], axis=-1).reshape(experts, SLOTS, 2 * width)
    back = exchange(back, OWNERS).reshape(slots, 2 * width)
    returned, home_grad = back[:, :width], back[:, width:]

    def expert_shards(grad):
        grad = lax.psum_scatter(grad.astype(bf16), RING, scatter_dimension=0, tiled=True)
        count = grad.shape[0] // 2
        kept = lax.dynamic_slice_in_dim(grad, core * count, count)
        given = partner(lax.dynamic_slice_in_dim(grad, (1 - core) * count, count))
        first = jnp.where(core == 0, kept, given)
        last = jnp.where(core == 0, given, kept)
        return jnp.stack([first, last]).astype(f32)[None]

    w_gate_grad = expert_shards(t_dot(arrived, gate_grad))
    w_up_grad = expert_shards(t_dot(arrived, up_grad))
    w_down_grad = expert_shards(t_dot(out_grad, hidden))

    gate_high = gate_at.astype(bf16)
    gate_rest = gate_at - gate_high.astype(f32)
    gate_mid = gate_rest.astype(bf16)
    gate_last = (gate_rest - gate_mid.astype(f32)).astype(bf16)
    result = midway + (
        dot(gate_high, returned) + (dot(gate_mid, returned) + dot(gate_last, returned))
    )
    output = result.astype(bf16)[None]

    gradient = cot.astype(f32)
    agreement = dot_t(cot, returned)
    gates_grad = jnp.sum(jnp.where(selector, agreement[:, None, :], 0.0), axis=-1)
    picked_grad = gates * (gates_grad - jnp.sum(gates * gates_grad, axis=-1, keepdims=True))
    logit_grad = jnp.sum(picked_grad[:, :, None] * hits.astype(f32), axis=1).astype(bf16)
    moe_grad = dot(placer, home_grad) + dot_t(logit_grad, router)
    router_grad = t_dot(moe_low, logit_grad)
    gain_two_grad = jnp.sum(moe_grad * normal_two, axis=0)
    scaled = moe_grad * gain_two
    midway_grad = gradient + inverse_two * (
        scaled - normal_two * jnp.mean(scaled * normal_two, axis=-1, keepdims=True)
    )
    branch_low = midway_grad.astype(bf16)
    branch_both = jnp.concatenate([branch_low, partner(branch_low)], axis=0)
    out_w_grad = t_dot(mixed, branch_both).astype(bf16)
    out_w_grad = (
        out_w_grad.reshape(4, 2, 8, shard * width // 128, 128)
        .transpose(1, 0, 2, 3, 4)
        .reshape(64, shard * width // 128, 128)
    )
    out_w_grad = jnp.sum(exchange(out_w_grad, CHIPS).astype(f32), axis=0).reshape(shard, width)
    out_w_grad = crossed(out_w_grad)
    mixed_grad = dot_t(branch_both, wo).astype(bf16).reshape(2 * rows, per_group, HD)

    def attend_back(q, keys, values, q_places, k_places, log_total, grad):
        scores = scores_of(q, keys, q_places, k_places)
        probs = jnp.exp(scores - log_total)
        prob_grad = jnp.einsum("hqd,kd->hqk", grad, values, preferred_element_type=f32)
        score_grad = (
            probs * (prob_grad - jnp.sum(probs * prob_grad, axis=-1, keepdims=True))
        ).astype(bf16)
        q_part = (
            jnp.einsum("hqk,kd->hqd", score_grad, keys, preferred_element_type=f32) * scale
        )
        k_part = jnp.einsum("hqk,hqd->kd", score_grad, q, preferred_element_type=f32) * scale
        v_part = jnp.einsum("hqk,hqd->kd", probs.astype(bf16), grad, preferred_element_type=f32)
        return q_part, jnp.concatenate([k_part, v_part], axis=-1)

    grad_low = by_head(lower_of(mixed_grad))
    grad_up = by_head(upper_of(mixed_grad))
    dq_low, dkv_low = attend_back(
        q_low, key_low, value_low, place_low, key_place_low, total_low, grad_low
    )
    dq_up, dkv_up = attend_back(q_up, key_all, value_all, place_up, key_place, total_up, grad_up)
    dkv = dkv_up.reshape(ctx_count, 2, half, 2 * HD)
    dkv_low = dkv_low.reshape(ctx_count, 1, half, 2 * HD)
    dkv = dkv + jnp.concatenate([dkv_low, jnp.zeros_like(dkv_low)], axis=1)
    dkv = exchange(dkv.astype(bf16).reshape(8, 2 * rows, 2 * HD), RING)
    dkv = jnp.sum(dkv.astype(f32), axis=0)
    dq = rotate(interleave(dq_low, dq_up).reshape(2 * rows, per_group, HD), cosines, -sines)
    dk = rotate(dkv[:, None, :HD], cosines, -sines)
    dq = dq.reshape(2 * rows, qw).astype(bf16)
    dkv = jnp.concatenate([dk.reshape(2 * rows, HD), dkv[:, HD:]], axis=-1).astype(bf16)

    def summed(pieces):
        count = pieces.shape[1]
        pieces = exchange(pieces, AXES).astype(f32)
        return jnp.sum(pieces.reshape(8, 2, 8, count, 128), axis=(0, 2))

    def joined(pair):
        return pair.transpose(1, 0, 2).reshape(1, shard, -1)

    q_w_grad = t_dot(normed, dq).astype(bf16).reshape(devices, shard * qw // 128, 128)
    q_w_grad = summed(after(q_w_grad, dkv))
    w_query_grad = joined(q_w_grad.reshape(2, shard, qw))

    normed_part = dot_t(dkv, w_kv) + dot_t(dq, w_q)
    normed_grad = normed_part[:rows] + partner(normed_part[rows:])
    own_normal, own_inverse = normal_one[:rows], inverse_one[:rows]
    gain_one_grad = jnp.sum(normed_grad * own_normal, axis=0)
    scaled = normed_grad * gain_one
    input_grad = midway_grad + own_inverse * (
        scaled - own_normal * jnp.mean(scaled * own_normal, axis=-1, keepdims=True)
    )
    kv_w_grad = t_dot(normed, dkv).astype(bf16).reshape(devices, kv_rows, 128)
    small_grad = jnp.concatenate(
        [router_grad, gain_one_grad[:, None], gain_two_grad[:, None]], axis=-1
    ).reshape(devices, shard * small_count)
    small_grad = jnp.pad(small_grad, ((0, 0), (0, 1024 - shard * small_count)))
    small_grad = small_grad.reshape(devices, 8, 128).astype(bf16)
    last = summed(after(jnp.concatenate([kv_w_grad, small_grad], axis=1), q_w_grad))
    kv_w_grad = last[:, :kv_rows].reshape(2, shard, 2 * HD)
    w_key_grad = joined(kv_w_grad[:, :, :HD])
    w_value_grad = joined(kv_w_grad[:, :, HD:])
    small_grad = (last[0, kv_rows:] + last[1, kv_rows:]).reshape(1024)
    small_grad = small_grad[: shard * small_count].reshape(1, shard, small_count)

    return (
        output,
        input_grad[None],
        small_grad[:, :, experts],
        small_grad[:, :, experts + 1],
        w_query_grad,
        w_key_grad,
        w_value_grad,
        out_w_grad[None],
        small_grad[:, :, :experts],
        w_gate_grad,
        w_up_grad,
        w_down_grad,
    )


def ordered_all(first_ctx, rows, core):
    index = jnp.arange(rows, dtype=jnp.int32)[None, :]
    return jnp.concatenate(
        [first_ctx * rows + index, (first_ctx + 1 - 2 * core) * rows + index], axis=-1
    ).reshape(-1)


def solution(mesh):
    fine = Mesh(mesh.devices.reshape(2, 4, 2, 4, 2), AXES)
    seq = P(FSDP, CTX, None)
    vector = P(None, AXES)
    matrix = P(None, AXES, None)
    expert = P(None, FSDP, CTX, None)
    in_specs = (
        seq,
        seq,
        P(),
        P(None, FSDP, CTX, None),
        vector,
        vector,
        matrix,
        matrix,
        matrix,
        matrix,
        matrix,
        expert,
        expert,
        expert,
    )
    out_specs = (
        seq,
        seq,
        vector,
        vector,
        matrix,
        matrix,
        matrix,
        matrix,
        matrix,
        expert,
        expert,
        expert,
    )
    return jax.shard_map(body, mesh=fine, in_specs=in_specs, out_specs=out_specs, check_vma=False)
```

```python
import math

import jax
import jax.numpy as jnp
from jax import lax
from jax.sharding import Mesh
from jax.sharding import PartitionSpec as P

H = 12
KVH = 2
HD = 128
TOPK = 4

EPSILON = 1e-06
ROPE_BASE = 1000000.0
NEGATIVE = -1e30

AXES = ("ylo", "z", "core", "x", "yhi")
CTX = ("ylo", "z", "core")
FSDP = ("x", "yhi")
OWNERS = ("x", "yhi", "core")
RING = ("ylo", "z")
ROWS_ORDER = ("ylo", "z", "yhi", "x")
OUT_ORDER = ("yhi", "z", "ylo", "x")
SLOTS = 40

bf16 = jnp.bfloat16
f32 = jnp.float32


def dot(left, right):
    return jnp.dot(left, right, preferred_element_type=f32)


def dot_t(left, right):
    return lax.dot_general(left, right, (((1,), (1,)), ((), ())), preferred_element_type=f32)


def t_dot(left, right):
    return lax.dot_general(left, right, (((0,), (0,)), ((), ())), preferred_element_type=f32)


def exchange(pieces, axes):
    return lax.all_to_all(pieces, axes, split_axis=0, concat_axis=0, tiled=True)


def spread(piece, count, axes):
    return exchange(jnp.broadcast_to(piece[None], (count,) + piece.shape), axes)


def after(value, earlier):
    return lax.optimization_barrier((value, earlier))[0]


def partner(value):
    return lax.ppermute(value, "core", [(0, 1), (1, 0)])


def route(axes, sizes, move):
    pairs = []
    for source in range(math.prod(sizes)):
        rest, at = source, []
        for size in reversed(sizes):
            at.insert(0, rest % size)
            rest //= size
        target = 0
        for size, value in zip(sizes, move(*at)):
            target = target * size + value
        pairs.append((source, target))
    return pairs


SAME = route(("core", "yhi"), (2, 2), lambda c, h: (h, c))
OTHER = route(("core", "yhi"), (2, 2), lambda c, h: (1 - h, c))
OUT_SAME = route(("ylo", "core", "yhi"), (2, 2, 2), lambda j, c, h: (c, j, h))
OUT_OTHER = route(("ylo", "core", "yhi"), (2, 2, 2), lambda j, c, h: (c, j, 1 - h))


def back(pairs):
    return [(target, source) for source, target in pairs]


def pick(flag, if_zero, if_one):
    return jnp.where(flag == 0, if_zero, if_one)


def gather_pieces(pair, flag, key, axes, same, other):
    first = lax.ppermute(pick(flag, pair[0], pair[1]), axes, same)
    second = lax.ppermute(pick(flag, pair[1], pair[0]), axes, other)
    return pick(
        key, jnp.concatenate([first, second]), jnp.concatenate([second, first])
    )


def scatter_pieces(piece, flag, key, axes, same, other):
    count = piece.shape[0] // 2
    mine, rest = piece[:count], piece[count:]
    first = lax.ppermute(pick(key, mine, rest), axes, back(same))
    second = lax.ppermute(pick(key, rest, mine), axes, back(other))
    return pick(flag, jnp.concatenate([first, second], axis=-1), jnp.concatenate([second, first], axis=-1))


OFFSETS = [(dy, dz) for dy in (0, 1) for dz in (0, 1, 3, 2)]


def ring_send(pieces):
    arrived = [pieces[0]]
    for (dy, dz), piece in zip(OFFSETS[1:], pieces[1:]):
        pairs = route(RING, (2, 4), lambda y, z: (y ^ dy, (z + dz) % 4))
        arrived.append(lax.ppermute(piece, RING, pairs))
    return arrived


def rotate(vectors, cosines, sines):
    half = vectors.shape[-1] // 2
    first, second = vectors[..., :half], vectors[..., half:]
    return jnp.concatenate(
        [first * cosines - second * sines, second * cosines + first * sines], axis=-1
    )


def places(pair_of, ctx, row_count, ctx_count):
    half_size = row_count // 2
    pair = jnp.sum(
        jnp.where(ctx[:, None] == jnp.arange(ctx_count, dtype=jnp.int32)[None], pair_of[None], 0),
        axis=1,
    )
    block = jnp.stack([pair, 2 * ctx_count - 1 - pair], axis=1)
    return block[:, :, None] * half_size + jnp.arange(half_size, dtype=jnp.int32)[None, None]


def body(
    tokens,
    cotangent,
    pair_of,
    routes,
    attn_gain,
    moe_gain,
    w_query,
    w_key,
    w_value,
    w_out,
    w_router,
    w_gate,
    w_up,
    w_down,
):
    rows = tokens.shape[1]
    half = rows // 2
    width = tokens.shape[2]
    shard = w_query.shape[1]
    ctx_count = 16
    experts = w_router.shape[2]
    per_group = H // KVH
    qw = per_group * HD
    scale = 1.0 / math.sqrt(HD)
    core = lax.axis_index("core")
    ylo, z, yhi = lax.axis_index("ylo"), lax.axis_index("z"), lax.axis_index("yhi")
    piece_rows = 2 * shard

    def halves(matrix):
        return [matrix[:, : matrix.shape[1] // 2], matrix[:, matrix.shape[1] // 2 :]]

    small = jnp.concatenate([w_router[0], attn_gain[0][:, None], moe_gain[0][:, None]], axis=-1)
    small = jnp.pad(small, ((0, 0), (0, 128 - experts - 2)))
    query_halves, key_halves, value_halves = halves(w_query[0]), halves(w_key[0]), halves(w_value[0])
    pairs = [
        jnp.concatenate([k, v, small, q], axis=-1)
        for k, v, q in zip(key_halves, value_halves, query_halves)
    ]
    pieces = gather_pieces(pairs, yhi, core, ("core", "yhi"), SAME, OTHER)
    w_kvs = spread(pieces[:, : 3 * HD], 64, ROWS_ORDER)
    w_q = spread(after(pieces[:, 3 * HD :], w_kvs), 64, ROWS_ORDER).reshape(width, qw)
    out_pieces = gather_pieces(
        halves(w_out[0]), yhi, yhi, ("ylo", "core", "yhi"), OUT_SAME, OUT_OTHER
    )
    wo = spread(after(out_pieces, w_q), 64, OUT_ORDER).reshape(2, qw, width // 2)
    w_kvs = w_kvs.reshape(width, 3 * HD)
    w_kv, small = w_kvs[:, : 2 * HD], w_kvs[:, 2 * HD :]
    router = small[:, :experts]
    gain_picker = (
        jnp.arange(small.shape[1])[None, :] == jnp.arange(8)[:, None] + experts
    ).astype(bf16)
    gains = dot_t(gain_picker, small)
    gain_one, gain_two = gains[0], gains[1]

    expert_weights = lax.all_gather(
        jnp.stack([w_gate[0], w_up[0], w_down[0]]), CTX, axis=2, tiled=True
    )
    expert_weights = lax.dynamic_index_in_dim(expert_weights, core, axis=1, keepdims=False)
    gate_w, up_w, down_w = expert_weights[0], expert_weights[1], expert_weights[2]

    chosen = routes[0, 0]
    hits = (chosen[:, :, None] == jnp.arange(experts, dtype=jnp.int32)[None, None, :]).astype(
        jnp.int32
    )
    index = jnp.arange(rows, dtype=jnp.int32)
    earlier = (index[:, None] > index[None, :]).astype(bf16)
    before = dot(earlier, jnp.sum(hits, axis=1).astype(bf16)).astype(jnp.int32)
    slot_index = jnp.sum(hits * before[:, None, :], axis=-1)
    target = chosen * SLOTS + slot_index
    slots = experts * SLOTS
    slot_row = jnp.arange(slots, dtype=jnp.int32)
    selector = target[:, :, None] == slot_row[None, None, :]
    placer = jnp.any(selector, axis=1).astype(bf16)
    cot = cotangent[0]
    cot_rows = t_dot(placer, cot).astype(bf16).reshape(experts, SLOTS, width)
    arrived_cot = exchange(after(cot_rows, wo), OWNERS).reshape(slots, width)

    both = jnp.concatenate([tokens[0], partner(tokens[0])], axis=0).astype(f32)
    stream = both[:rows]
    inverse_one = lax.rsqrt(jnp.mean(both * both, axis=-1, keepdims=True) + EPSILON)
    normal_one = both * inverse_one
    normed = (normal_one * gain_one).astype(bf16)

    def two_cores(ctx):
        return jnp.stack([ctx + core, ctx + 1 - core], axis=-1).reshape(-1)

    ctx_here = (ylo * 4 + z) * 2
    local_place = places(pair_of, two_cores(ctx_here), rows, ctx_count)
    ctx_there = jnp.stack([((ylo ^ dy) * 4 + (z - dz) % 4) * 2 for dy, dz in OFFSETS])
    key_place = places(pair_of, two_cores(ctx_there), rows, ctx_count)
    place_low, place_up = local_place[:, 0].reshape(-1), local_place[:, 1].reshape(-1)
    key_place_low = key_place[:, 0].reshape(-1)
    key_place, local_place = key_place.reshape(-1), local_place.reshape(-1)
    frequency = jnp.exp(
        jnp.arange(HD // 2, dtype=f32) * (-2.0 * math.log(ROPE_BASE) / HD)
    )
    angles = local_place.astype(f32)[:, None] * frequency[None, :]
    cosines = jnp.cos(angles)[:, None, :]
    sines = jnp.sin(angles)[:, None, :]

    kv = dot(normed, w_kv)
    keys = rotate(kv[:, None, :HD], cosines, sines)[:, 0]
    key_value = jnp.concatenate([keys.astype(bf16), kv[:, HD:].astype(bf16)], axis=-1)
    all_kv = jnp.concatenate(ring_send([key_value] * 8))
    queries = dot(normed, w_q).reshape(2 * rows, per_group, HD)
    queries = rotate(queries, cosines, sines).astype(bf16)

    def lower_of(full):
        shape = full.shape
        return full.reshape((-1, 2, half) + shape[1:])[:, 0].reshape((-1,) + shape[1:])

    def upper_of(full):
        shape = full.shape
        return full.reshape((-1, 2, half) + shape[1:])[:, 1].reshape((-1,) + shape[1:])

    key_all, value_all = all_kv[:, :HD], all_kv[:, HD:]
    low_kv = lower_of(all_kv)
    key_low, value_low = low_kv[:, :HD], low_kv[:, HD:]

    def by_head(matrix):
        return matrix.transpose(1, 0, 2)

    q_low = by_head(lower_of(queries))
    q_up = by_head(upper_of(queries))

    def scores_of(q, keys, q_places, k_places):
        raw = jnp.einsum("hqd,kd->hqk", q, keys, preferred_element_type=f32) * scale
        return jnp.where(k_places[None, None, :] <= q_places[None, :, None], raw, NEGATIVE)

    def attend(q, keys, values, q_places, k_places):
        scores = scores_of(q, keys, q_places, k_places)
        highest = jnp.max(scores, axis=-1, keepdims=True)
        exponent = jnp.exp(scores - highest)
        totals = jnp.sum(exponent, axis=-1, keepdims=True)
        probs = exponent / totals
        mixed = jnp.einsum("hqk,kd->hqd", probs.astype(bf16), values, preferred_element_type=f32)
        return mixed, highest + jnp.log(totals)

    mixed_low, total_low = attend(q_low, key_low, value_low, place_low, key_place_low)
    mixed_up, total_up = attend(q_up, key_all, value_all, place_up, key_place)

    def interleave(low, up):
        parts = jnp.stack([low.reshape(-1, 2, half, HD), up.reshape(-1, 2, half, HD)], axis=2)
        return parts.transpose(1, 2, 3, 0, 4).reshape(2 * rows, -1)

    mixed = interleave(mixed_low.astype(bf16), mixed_up.astype(bf16))
    branch = jnp.concatenate([dot(mixed, wo[0]), dot(mixed, wo[1])], axis=-1)
    midway = stream + (branch[:rows] + partner(branch[rows:]))

    inverse_two = lax.rsqrt(jnp.mean(midway * midway, axis=-1, keepdims=True) + EPSILON)
    normal_two = midway * inverse_two
    moe_low = (normal_two * gain_two).astype(bf16)
    logits = dot(moe_low, router)
    picked = jnp.sum(jnp.where(hits == 1, logits[:, None, :], 0.0), axis=-1)
    exp_pick = jnp.exp(picked - jnp.max(picked, axis=-1, keepdims=True))
    gates = exp_pick / jnp.sum(exp_pick, axis=-1, keepdims=True)
    gate_at = jnp.sum(jnp.where(selector, gates[:, :, None], 0.0), axis=1)
    gate_slot = jnp.sum(gate_at, axis=0)
    gate_parts = in_three(gate_slot[:, None])
    sent = jnp.concatenate(
        [t_dot(placer, moe_low).astype(bf16)]
        + gate_parts
        + [jnp.zeros((slots, 128 - len(gate_parts)), bf16)],
        axis=-1,
    )
    sent = exchange(
        after(sent, arrived_cot).reshape(experts, SLOTS, width + 128), OWNERS
    ).reshape(slots, width + 128)
    arrived = sent[:, :width]
    arrived_gates = jnp.sum(sent[:, width:].astype(f32), axis=-1, keepdims=True)
    out_grad = (arrived_gates * arrived_cot.astype(f32)).astype(bf16)
    gate_pre = dot(arrived, gate_w)
    up_pre = dot(arrived, up_w)
    sigmoid = jax.nn.sigmoid(gate_pre)
    hidden = (gate_pre * sigmoid * up_pre).astype(bf16)
    expert_out = dot_t(hidden, down_w).astype(bf16)
    hidden_grad = dot(out_grad, down_w)
    gate_grad = (hidden_grad * up_pre * sigmoid * (1.0 + gate_pre * (1.0 - sigmoid))).astype(bf16)
    up_grad = (hidden_grad * gate_pre * sigmoid).astype(bf16)
    rows_grad = (dot_t(gate_grad, gate_w) + dot_t(up_grad, up_w)).astype(bf16)
    returned = exchange(expert_out.reshape(experts, SLOTS, width), OWNERS)
    rows_grad = after(rows_grad, returned)
    returned = returned.reshape(slots, width)
    home_grad = exchange(rows_grad.reshape(experts, SLOTS, width), OWNERS).reshape(slots, width)

    def expert_sum(left, right):
        grad = t_dot(left, right).astype(bf16)
        return lax.psum_scatter(grad, RING, scatter_dimension=0, tiled=True)

    def expert_shards(grad):
        count = grad.shape[0] // 2
        kept = lax.dynamic_slice_in_dim(grad, core * count, count)
        given = partner(lax.dynamic_slice_in_dim(grad, (1 - core) * count, count))
        first = jnp.where(core == 0, kept, given)
        last = jnp.where(core == 0, given, kept)
        return jnp.stack([first, last]).astype(f32)[None]

    expert_sums = (
        expert_sum(out_grad, hidden),
        expert_sum(arrived, gate_grad),
        expert_sum(arrived, up_grad),
    )

    high, middle, lowest = in_three(gate_at)
    result = midway + (dot(high, returned) + (dot(middle, returned) + dot(lowest, returned)))
    output = result.astype(bf16)[None]

    gradient = cot.astype(f32)
    agreement = dot_t(cot, returned)
    gates_grad = jnp.sum(jnp.where(selector, agreement[:, None, :], 0.0), axis=-1)
    picked_grad = gates * (gates_grad - jnp.sum(gates * gates_grad, axis=-1, keepdims=True))
    logit_grad = jnp.sum(picked_grad[:, :, None] * hits.astype(f32), axis=1).astype(bf16)
    moe_grad = dot(placer, home_grad) + dot_t(logit_grad, router)
    router_grad = t_dot(moe_low, logit_grad)
    gain_two_grad = jnp.sum(moe_grad * normal_two, axis=0)
    scaled = moe_grad * gain_two
    midway_grad = gradient + inverse_two * (
        scaled - normal_two * jnp.mean(scaled * normal_two, axis=-1, keepdims=True)
    )
    branch_low = midway_grad.astype(bf16)
    branch_both = jnp.concatenate([branch_low, partner(branch_low)], axis=0)
    out_w_grad = jnp.stack(
        [t_dot(mixed, part).astype(bf16) for part in jnp.split(branch_both, 2, axis=1)]
    ).reshape(64, piece_rows, width // 2)
    out_w_grad = exchange(after(out_w_grad, home_grad), OUT_ORDER)
    mixed_grad = (
        dot_t(branch_both[:, : width // 2], wo[0]) + dot_t(branch_both[:, width // 2 :], wo[1])
    )
    mixed_grad = mixed_grad.astype(bf16).reshape(2 * rows, per_group, HD)

    def attend_back(q, keys, values, q_places, k_places, log_total, grad):
        scores = scores_of(q, keys, q_places, k_places)
        probs = jnp.exp(scores - log_total)
        prob_grad = jnp.einsum("hqd,kd->hqk", grad, values, preferred_element_type=f32)
        score_grad = (
            probs * (prob_grad - jnp.sum(probs * prob_grad, axis=-1, keepdims=True))
        ).astype(bf16)
        q_part = (
            jnp.einsum("hqk,kd->hqd", score_grad, keys, preferred_element_type=f32) * scale
        )
        k_part = jnp.einsum("hqk,hqd->kd", score_grad, q, preferred_element_type=f32) * scale
        v_part = jnp.einsum("hqk,hqd->kd", probs.astype(bf16), grad, preferred_element_type=f32)
        return q_part, jnp.concatenate([k_part, v_part], axis=-1)

    grad_low = by_head(lower_of(mixed_grad))
    grad_up = by_head(upper_of(mixed_grad))
    dq_low, dkv_low = attend_back(
        q_low, key_low, value_low, place_low, key_place_low, total_low, grad_low
    )
    dq_up, dkv_up = attend_back(q_up, key_all, value_all, place_up, key_place, total_up, grad_up)
    dkv = dkv_up.reshape(ctx_count, 2, half, 2 * HD)
    dkv_low = dkv_low.reshape(ctx_count, 1, half, 2 * HD)
    dkv = dkv + jnp.concatenate([dkv_low, jnp.zeros_like(dkv_low)], axis=1)
    dkv = dkv.astype(bf16).reshape(8, 2 * rows, 2 * HD)
    back_order = [OFFSETS.index((dy, (-dz) % 4)) for dy, dz in OFFSETS]
    dkv = ring_send([dkv[i] for i in back_order])
    dkv = sum(part.astype(f32) for part in dkv)
    dq = rotate(interleave(dq_low, dq_up).reshape(2 * rows, per_group, HD), cosines, -sines)
    dk = rotate(dkv[:, None, :HD], cosines, -sines)
    dq = dq.reshape(2 * rows, qw).astype(bf16)
    dkv = jnp.concatenate([dk.reshape(2 * rows, HD), dkv[:, HD:]], axis=-1).astype(bf16)

    q_w_grad = t_dot(normed, dq).astype(bf16).reshape(64, piece_rows, qw)
    q_w_grad = exchange(after(q_w_grad, out_w_grad), ROWS_ORDER)

    normed_part = dot_t(dkv, w_kv) + dot_t(dq, w_q)
    normed_grad = normed_part[:rows] + partner(normed_part[rows:])
    own_normal, own_inverse = normal_one[:rows], inverse_one[:rows]
    gain_one_grad = jnp.sum(normed_grad * own_normal, axis=0)
    scaled = normed_grad * gain_one
    input_grad = midway_grad + own_inverse * (
        scaled - own_normal * jnp.mean(scaled * own_normal, axis=-1, keepdims=True)
    )
    small_grad = jnp.concatenate(
        [
            router_grad,
            gain_one_grad[:, None],
            gain_two_grad[:, None],
            jnp.zeros((width, 128 - experts - 2), f32),
        ],
        axis=-1,
    )
    kvs_grad = jnp.concatenate([t_dot(normed, dkv), small_grad], axis=-1).astype(bf16)
    kvs_grad = kvs_grad.reshape(64, piece_rows, 3 * HD)
    kvs_grad = exchange(after(kvs_grad, q_w_grad), ROWS_ORDER)

    def summed(pieces):
        return jnp.sum(pieces.astype(f32), axis=0)

    out_w_grad = scatter_pieces(
        summed(out_w_grad), yhi, yhi, ("ylo", "core", "yhi"), OUT_SAME, OUT_OTHER
    )
    q_w_grad = scatter_pieces(summed(q_w_grad), yhi, core, ("core", "yhi"), SAME, OTHER)
    expert_sums = after(expert_sums, q_w_grad)
    w_down_grad, w_gate_grad, w_up_grad = [expert_shards(grad) for grad in expert_sums]
    kvs_grad = scatter_pieces(summed(kvs_grad), yhi, core, ("core", "yhi"), SAME, OTHER)
    first_half, second_half = kvs_grad[:, : 3 * HD], kvs_grad[:, 3 * HD :]
    w_key_grad = jnp.concatenate([first_half[:, :HD], second_half[:, :HD]], axis=-1)
    w_value_grad = jnp.concatenate(
        [first_half[:, HD : 2 * HD], second_half[:, HD : 2 * HD]], axis=-1
    )
    small_grad = first_half[:, 2 * HD :] + second_half[:, 2 * HD :]

    return (
        output,
        input_grad[None],
        small_grad[None, :, experts],
        small_grad[None, :, experts + 1],
        q_w_grad[None],
        w_key_grad[None],
        w_value_grad[None],
        out_w_grad[None],
        small_grad[None, :, :experts],
        w_gate_grad,
        w_up_grad,
        w_down_grad,
    )


def in_three(value):
    high = value.astype(bf16)
    rest = value - high.astype(f32)
    middle = rest.astype(bf16)
    return [high, middle, (rest - middle.astype(f32)).astype(bf16)]


def solution(mesh):
    fine = Mesh(mesh.devices.reshape(2, 4, 2, 4, 2), AXES)
    seq = P(FSDP, CTX, None)
    vector = P(None, AXES)
    matrix = P(None, AXES, None)
    expert = P(None, FSDP, CTX, None)
    in_specs = (
        seq,
        seq,
        P(),
        P(None, FSDP, CTX, None),
        vector,
        vector,
        matrix,
        matrix,
        matrix,
        matrix,
        matrix,
        expert,
        expert,
        expert,
    )
    out_specs = (
        seq,
        seq,
        vector,
        vector,
        matrix,
        matrix,
        matrix,
        matrix,
        matrix,
        expert,
        expert,
        expert,
    )
    return jax.shard_map(body, mesh=fine, in_specs=in_specs, out_specs=out_specs, check_vma=False)
```

```python
import math

import jax
import jax.numpy as jnp
from jax import lax
from jax.sharding import Mesh
from jax.sharding import PartitionSpec as P

H = 12
KVH = 2
HD = 128
TOPK = 4

EPSILON = 1e-06
ROPE_BASE = 1000000.0
NEGATIVE = -1e30

AXES = ("ylo", "z", "core", "x", "yhi")
CTX = ("ylo", "z", "core")
FSDP = ("x", "yhi")
GROUPS = [
    [
        (((group ^ yhi) * 4 + z) * 2 + core) * 8 + x * 2 + yhi
        for x in range(4)
        for yhi in range(2)
        for core in range(2)
    ]
    for group in range(2)
    for z in range(4)
]
RING = ("ylo", "z")
ROWS_ORDER = ("ylo", "z", "yhi", "x")
OUT_ORDER = ("yhi", "z", "ylo", "x")
SLOTS = 40

bf16 = jnp.bfloat16
f32 = jnp.float32


def dot(left, right):
    return jnp.dot(left, right, preferred_element_type=f32)


def dot_t(left, right):
    return lax.dot_general(left, right, (((1,), (1,)), ((), ())), preferred_element_type=f32)


def t_dot(left, right):
    return lax.dot_general(left, right, (((0,), (0,)), ((), ())), preferred_element_type=f32)


def exchange(pieces, axes):
    return lax.all_to_all(pieces, axes, split_axis=0, concat_axis=0, tiled=True)


def to_owners(pieces):
    return lax.all_to_all(
        pieces, AXES, split_axis=0, concat_axis=0, axis_index_groups=GROUPS, tiled=True
    )


def spread(piece, count, axes):
    return exchange(jnp.broadcast_to(piece[None], (count,) + piece.shape), axes)


def after(value, earlier):
    return lax.optimization_barrier((value, earlier))[0]


def partner(value):
    return lax.ppermute(value, "core", [(0, 1), (1, 0)])


def route(axes, sizes, move):
    pairs = []
    for source in range(math.prod(sizes)):
        rest, at = source, []
        for size in reversed(sizes):
            at.insert(0, rest % size)
            rest //= size
        target = 0
        for size, value in zip(sizes, move(*at)):
            target = target * size + value
        pairs.append((source, target))
    return pairs


SAME = route(("core", "yhi"), (2, 2), lambda c, h: (h, c))
OTHER = route(("core", "yhi"), (2, 2), lambda c, h: (1 - h, c))
OUT_SAME = route(("ylo", "core", "yhi"), (2, 2, 2), lambda j, c, h: (c, j, h))
OUT_OTHER = route(("ylo", "core", "yhi"), (2, 2, 2), lambda j, c, h: (c, j, 1 - h))


def back(pairs):
    return [(target, source) for source, target in pairs]


def pick(flag, if_zero, if_one):
    return jnp.where(flag == 0, if_zero, if_one)


def gather_pieces(pair, flag, key, axes, same, other):
    first = lax.ppermute(pick(flag, pair[0], pair[1]), axes, same)
    second = lax.ppermute(pick(flag, pair[1], pair[0]), axes, other)
    return pick(
        key, jnp.concatenate([first, second]), jnp.concatenate([second, first])
    )


def scatter_pieces(piece, flag, key, axes, same, other):
    count = piece.shape[0] // 2
    mine, rest = piece[:count], piece[count:]
    first = lax.ppermute(pick(key, mine, rest), axes, back(same))
    second = lax.ppermute(pick(key, rest, mine), axes, back(other))
    return pick(flag, jnp.concatenate([first, second], axis=-1), jnp.concatenate([second, first], axis=-1))


OFFSETS = [(dy, dz) for dy in (0, 1) for dz in (0, 1, 3, 2)]


def ring_send(pieces):
    arrived = [pieces[0]]
    for (dy, dz), piece in zip(OFFSETS[1:], pieces[1:]):
        pairs = route(RING, (2, 4), lambda y, z: (y ^ dy, (z + dz) % 4))
        arrived.append(lax.ppermute(piece, RING, pairs))
    return arrived


def rotate(vectors, cosines, sines):
    half = vectors.shape[-1] // 2
    first, second = vectors[..., :half], vectors[..., half:]
    return jnp.concatenate(
        [first * cosines - second * sines, second * cosines + first * sines], axis=-1
    )


def places(pair_of, ctx, row_count, ctx_count):
    half_size = row_count // 2
    pair = jnp.sum(
        jnp.where(ctx[:, None] == jnp.arange(ctx_count, dtype=jnp.int32)[None], pair_of[None], 0),
        axis=1,
    )
    block = jnp.stack([pair, 2 * ctx_count - 1 - pair], axis=1)
    return block[:, :, None] * half_size + jnp.arange(half_size, dtype=jnp.int32)[None, None]


def body(
    tokens,
    cotangent,
    pair_of,
    routes,
    attn_gain,
    moe_gain,
    w_query,
    w_key,
    w_value,
    w_out,
    w_router,
    w_gate,
    w_up,
    w_down,
):
    rows = tokens.shape[1]
    half = rows // 2
    width = tokens.shape[2]
    shard = w_query.shape[1]
    ctx_count = 16
    experts = w_router.shape[2]
    per_group = H // KVH
    qw = per_group * HD
    scale = 1.0 / math.sqrt(HD)
    core = lax.axis_index("core")
    ylo, z, yhi = lax.axis_index("ylo"), lax.axis_index("z"), lax.axis_index("yhi")
    piece_rows = 2 * shard

    def halves(matrix):
        return [matrix[:, : matrix.shape[1] // 2], matrix[:, matrix.shape[1] // 2 :]]

    small = jnp.concatenate([w_router[0], attn_gain[0][:, None], moe_gain[0][:, None]], axis=-1)
    small = jnp.pad(small, ((0, 0), (0, 128 - experts - 2)))
    query_halves, key_halves, value_halves = halves(w_query[0]), halves(w_key[0]), halves(w_value[0])
    pairs = [
        jnp.concatenate([k, v, small, q], axis=-1)
        for k, v, q in zip(key_halves, value_halves, query_halves)
    ]
    pieces = gather_pieces(pairs, yhi, core, ("core", "yhi"), SAME, OTHER)
    w_kvs = spread(pieces[:, : 3 * HD], 64, ROWS_ORDER)
    w_q = spread(after(pieces[:, 3 * HD :], w_kvs), 64, ROWS_ORDER).reshape(width, qw)
    out_pieces = gather_pieces(
        halves(w_out[0]), yhi, yhi, ("ylo", "core", "yhi"), OUT_SAME, OUT_OTHER
    )
    wo = spread(after(out_pieces, w_q), 64, OUT_ORDER).reshape(2, qw, width // 2)
    w_kvs = w_kvs.reshape(width, 3 * HD)
    w_kv, small = w_kvs[:, : 2 * HD], w_kvs[:, 2 * HD :]
    router = small[:, :experts]
    gain_picker = (
        jnp.arange(small.shape[1])[None, :] == jnp.arange(8)[:, None] + experts
    ).astype(bf16)
    gains = dot_t(gain_picker, small)
    gain_one, gain_two = gains[0], gains[1]

    expert_weights = lax.all_gather(
        after(jnp.stack([w_gate[0], w_up[0], w_down[0]]), w_q), CTX, axis=2, tiled=True
    )
    expert_weights = lax.dynamic_index_in_dim(expert_weights, core, axis=1, keepdims=False)
    gate_w, up_w, down_w = expert_weights[0], expert_weights[1], expert_weights[2]

    chosen = routes[0, 0]
    hits = (chosen[:, :, None] == jnp.arange(experts, dtype=jnp.int32)[None, None, :]).astype(
        jnp.int32
    )
    index = jnp.arange(rows, dtype=jnp.int32)
    earlier = (index[:, None] > index[None, :]).astype(bf16)
    before = dot(earlier, jnp.sum(hits, axis=1).astype(bf16)).astype(jnp.int32)
    slot_index = jnp.sum(hits * before[:, None, :], axis=-1)
    target = chosen * SLOTS + slot_index
    slots = experts * SLOTS
    slot_row = jnp.arange(slots, dtype=jnp.int32)
    selector = target[:, :, None] == slot_row[None, None, :]
    placer = jnp.any(selector, axis=1).astype(bf16)
    cot = cotangent[0]
    cot_rows = t_dot(placer, cot).astype(bf16).reshape(experts, SLOTS, width)
    arrived_cot = to_owners(after(cot_rows, wo)).reshape(slots, width)

    both = jnp.concatenate([tokens[0], partner(tokens[0])], axis=0).astype(f32)
    stream = both[:rows]
    inverse_one = lax.rsqrt(jnp.mean(both * both, axis=-1, keepdims=True) + EPSILON)
    normal_one = both * inverse_one
    normed = (normal_one * gain_one).astype(bf16)

    def two_cores(ctx):
        return jnp.stack([ctx + core, ctx + 1 - core], axis=-1).reshape(-1)

    ctx_here = (ylo * 4 + z) * 2
    local_place = places(pair_of, two_cores(ctx_here), rows, ctx_count)
    ctx_there = jnp.stack([((ylo ^ dy) * 4 + (z - dz) % 4) * 2 for dy, dz in OFFSETS])
    key_place = places(pair_of, two_cores(ctx_there), rows, ctx_count)
    place_low, place_up = local_place[:, 0].reshape(-1), local_place[:, 1].reshape(-1)
    key_place_low = key_place[:, 0].reshape(-1)
    key_place, local_place = key_place.reshape(-1), local_place.reshape(-1)
    frequency = jnp.exp(
        jnp.arange(HD // 2, dtype=f32) * (-2.0 * math.log(ROPE_BASE) / HD)
    )
    angles = local_place.astype(f32)[:, None] * frequency[None, :]
    cosines = jnp.cos(angles)[:, None, :]
    sines = jnp.sin(angles)[:, None, :]

    kv = dot(normed, w_kv)
    keys = rotate(kv[:, None, :HD], cosines, sines)[:, 0]
    key_value = jnp.concatenate([keys.astype(bf16), kv[:, HD:].astype(bf16)], axis=-1)
    all_kv = jnp.concatenate(ring_send([key_value] * 8))
    queries = dot(normed, w_q).reshape(2 * rows, per_group, HD)
    queries = rotate(queries, cosines, sines).astype(bf16)

    def lower_of(full):
        shape = full.shape
        return full.reshape((-1, 2, half) + shape[1:])[:, 0].reshape((-1,) + shape[1:])

    def upper_of(full):
        shape = full.shape
        return full.reshape((-1, 2, half) + shape[1:])[:, 1].reshape((-1,) + shape[1:])

    key_all, value_all = all_kv[:, :HD], all_kv[:, HD:]
    low_kv = lower_of(all_kv)
    key_low, value_low = low_kv[:, :HD], low_kv[:, HD:]

    def by_head(matrix):
        return matrix.transpose(1, 0, 2)

    q_low = by_head(lower_of(queries))
    q_up = by_head(upper_of(queries))

    def scores_of(q, keys, q_places, k_places):
        raw = jnp.einsum("hqd,kd->hqk", q, keys, preferred_element_type=f32) * scale
        return jnp.where(k_places[None, None, :] <= q_places[None, :, None], raw, NEGATIVE)

    def attend(q, keys, values, q_places, k_places):
        scores = scores_of(q, keys, q_places, k_places)
        highest = jnp.max(scores, axis=-1, keepdims=True)
        exponent = jnp.exp(scores - highest)
        totals = jnp.sum(exponent, axis=-1, keepdims=True)
        probs = exponent / totals
        mixed = jnp.einsum("hqk,kd->hqd", probs.astype(bf16), values, preferred_element_type=f32)
        return mixed, highest + jnp.log(totals)

    mixed_low, total_low = attend(q_low, key_low, value_low, place_low, key_place_low)
    mixed_up, total_up = attend(q_up, key_all, value_all, place_up, key_place)

    def interleave(low, up):
        parts = jnp.stack([low.reshape(-1, 2, half, HD), up.reshape(-1, 2, half, HD)], axis=2)
        return parts.transpose(1, 2, 3, 0, 4).reshape(2 * rows, -1)

    mixed = interleave(mixed_low.astype(bf16), mixed_up.astype(bf16))
    branch = jnp.concatenate([dot(mixed, wo[0]), dot(mixed, wo[1])], axis=-1)
    midway = stream + (branch[:rows] + partner(branch[rows:]))

    inverse_two = lax.rsqrt(jnp.mean(midway * midway, axis=-1, keepdims=True) + EPSILON)
    normal_two = midway * inverse_two
    moe_low = (normal_two * gain_two).astype(bf16)
    logits = dot(moe_low, router)
    picked = jnp.sum(jnp.where(hits == 1, logits[:, None, :], 0.0), axis=-1)
    exp_pick = jnp.exp(picked - jnp.max(picked, axis=-1, keepdims=True))
    gates = exp_pick / jnp.sum(exp_pick, axis=-1, keepdims=True)
    gate_at = jnp.sum(jnp.where(selector, gates[:, :, None], 0.0), axis=1)
    gate_slot = jnp.sum(gate_at, axis=0)
    gate_parts = in_three(gate_slot[:, None])
    sent = jnp.concatenate(
        [t_dot(placer, moe_low).astype(bf16)]
        + gate_parts
        + [jnp.zeros((slots, 128 - len(gate_parts)), bf16)],
        axis=-1,
    )
    sent = to_owners(after(sent, arrived_cot).reshape(experts, SLOTS, width + 128))
    sent = sent.reshape(slots, width + 128)
    arrived = sent[:, :width]
    arrived_gates = jnp.sum(sent[:, width:].astype(f32), axis=-1, keepdims=True)
    out_grad = (arrived_gates * arrived_cot.astype(f32)).astype(bf16)
    gate_pre = dot(arrived, gate_w)
    up_pre = dot(arrived, up_w)
    sigmoid = jax.nn.sigmoid(gate_pre)
    hidden = (gate_pre * sigmoid * up_pre).astype(bf16)
    expert_out = dot_t(hidden, down_w).astype(bf16)
    out_grad = after(out_grad, expert_out)
    hidden_grad = dot(out_grad, down_w)
    gate_grad = (hidden_grad * up_pre * sigmoid * (1.0 + gate_pre * (1.0 - sigmoid))).astype(bf16)
    up_grad = (hidden_grad * gate_pre * sigmoid).astype(bf16)
    rows_grad = (dot_t(gate_grad, gate_w) + dot_t(up_grad, up_w)).astype(bf16)
    returned = to_owners(expert_out.reshape(experts, SLOTS, width))
    rows_grad = after(rows_grad, returned)
    returned = returned.reshape(slots, width)
    home_grad = to_owners(rows_grad.reshape(experts, SLOTS, width)).reshape(slots, width)

    def expert_sum(left, right):
        return t_dot(left, right).astype(bf16)

    def expert_shards(grad):
        count = grad.shape[1] // 2
        kept = lax.dynamic_slice_in_dim(grad, core * count, count, axis=1)
        given = partner(lax.dynamic_slice_in_dim(grad, (1 - core) * count, count, axis=1))
        both = jnp.stack([pick(core, kept, given), pick(core, given, kept)], axis=1)
        return [both[i : i + 1].astype(f32) for i in range(3)]

    arrived_late = after(arrived, rows_grad)
    expert_sums = jnp.stack(
        [
            expert_sum(out_grad, hidden),
            expert_sum(arrived_late, gate_grad),
            expert_sum(arrived_late, up_grad),
        ]
    )
    expert_sums = lax.psum_scatter(expert_sums, RING, scatter_dimension=1, tiled=True)

    high, middle, lowest = in_three(gate_at)
    result = midway + (dot(high, returned) + (dot(middle, returned) + dot(lowest, returned)))
    output = result.astype(bf16)[None]

    gradient = cot.astype(f32)
    agreement = dot_t(cot, returned)
    gates_grad = jnp.sum(jnp.where(selector, agreement[:, None, :], 0.0), axis=-1)
    picked_grad = gates * (gates_grad - jnp.sum(gates * gates_grad, axis=-1, keepdims=True))
    logit_grad = jnp.sum(picked_grad[:, :, None] * hits.astype(f32), axis=1).astype(bf16)
    moe_grad = dot(placer, home_grad) + dot_t(logit_grad, router)
    router_grad = t_dot(moe_low, logit_grad)
    gain_two_grad = jnp.sum(moe_grad * normal_two, axis=0)
    scaled = moe_grad * gain_two
    midway_grad = gradient + inverse_two * (
        scaled - normal_two * jnp.mean(scaled * normal_two, axis=-1, keepdims=True)
    )
    branch_low = midway_grad.astype(bf16)
    branch_both = jnp.concatenate([branch_low, partner(branch_low)], axis=0)
    out_w_grad = jnp.stack(
        [t_dot(mixed, part).astype(bf16) for part in jnp.split(branch_both, 2, axis=1)]
    ).reshape(64, piece_rows, width // 2)
    out_w_grad = exchange(after(out_w_grad, home_grad), OUT_ORDER)
    mixed_grad = (
        dot_t(branch_both[:, : width // 2], wo[0]) + dot_t(branch_both[:, width // 2 :], wo[1])
    )
    mixed_grad = mixed_grad.astype(bf16).reshape(2 * rows, per_group, HD)

    def attend_back(q, keys, values, q_places, k_places, log_total, grad):
        scores = scores_of(q, keys, q_places, k_places)
        probs = jnp.exp(scores - log_total)
        prob_grad = jnp.einsum("hqd,kd->hqk", grad, values, preferred_element_type=f32)
        score_grad = (
            probs * (prob_grad - jnp.sum(probs * prob_grad, axis=-1, keepdims=True))
        ).astype(bf16)
        q_part = (
            jnp.einsum("hqk,kd->hqd", score_grad, keys, preferred_element_type=f32) * scale
        )
        k_part = jnp.einsum("hqk,hqd->kd", score_grad, q, preferred_element_type=f32) * scale
        v_part = jnp.einsum("hqk,hqd->kd", probs.astype(bf16), grad, preferred_element_type=f32)
        return q_part, jnp.concatenate([k_part, v_part], axis=-1)

    grad_low = by_head(lower_of(mixed_grad))
    grad_up = by_head(upper_of(mixed_grad))
    dq_low, dkv_low = attend_back(
        q_low, key_low, value_low, place_low, key_place_low, total_low, grad_low
    )
    dq_up, dkv_up = attend_back(q_up, key_all, value_all, place_up, key_place, total_up, grad_up)
    dkv = dkv_up.reshape(ctx_count, 2, half, 2 * HD)
    dkv_low = dkv_low.reshape(ctx_count, 1, half, 2 * HD)
    dkv = dkv + jnp.concatenate([dkv_low, jnp.zeros_like(dkv_low)], axis=1)
    dkv = dkv.astype(bf16).reshape(8, 2 * rows, 2 * HD)
    back_order = [OFFSETS.index((dy, (-dz) % 4)) for dy, dz in OFFSETS]
    dkv = ring_send([dkv[i] for i in back_order])
    dkv = sum(part.astype(f32) for part in dkv)
    dq = rotate(interleave(dq_low, dq_up).reshape(2 * rows, per_group, HD), cosines, -sines)
    dk = rotate(dkv[:, None, :HD], cosines, -sines)
    dq = dq.reshape(2 * rows, qw).astype(bf16)
    dkv = jnp.concatenate([dk.reshape(2 * rows, HD), dkv[:, HD:]], axis=-1).astype(bf16)

    q_w_grad = t_dot(normed, dq).astype(bf16).reshape(64, piece_rows, qw)
    q_w_grad = exchange(after(q_w_grad, out_w_grad), ROWS_ORDER)

    normed_part = dot_t(dkv, w_kv) + dot_t(dq, w_q)
    normed_grad = normed_part[:rows] + partner(normed_part[rows:])
    own_normal, own_inverse = normal_one[:rows], inverse_one[:rows]
    gain_one_grad = jnp.sum(normed_grad * own_normal, axis=0)
    scaled = normed_grad * gain_one
    input_grad = midway_grad + own_inverse * (
        scaled - own_normal * jnp.mean(scaled * own_normal, axis=-1, keepdims=True)
    )
    small_grad = jnp.concatenate(
        [
            router_grad,
            gain_one_grad[:, None],
            gain_two_grad[:, None],
            jnp.zeros((width, 128 - experts - 2), f32),
        ],
        axis=-1,
    )
    kvs_grad = jnp.concatenate([t_dot(normed, dkv), small_grad], axis=-1).astype(bf16)
    kvs_grad = kvs_grad.reshape(64, piece_rows, 3 * HD)
    kvs_grad = exchange(after(kvs_grad, q_w_grad), ROWS_ORDER)

    def summed(pieces):
        return jnp.sum(pieces.astype(f32), axis=0)

    out_w_grad = scatter_pieces(
        summed(out_w_grad), yhi, yhi, ("ylo", "core", "yhi"), OUT_SAME, OUT_OTHER
    )
    q_w_grad = scatter_pieces(summed(q_w_grad), yhi, core, ("core", "yhi"), SAME, OTHER)
    expert_sums = after(expert_sums, q_w_grad)
    w_down_grad, w_gate_grad, w_up_grad = expert_shards(expert_sums)
    kvs_grad = scatter_pieces(summed(kvs_grad), yhi, core, ("core", "yhi"), SAME, OTHER)
    first_half, second_half = kvs_grad[:, : 3 * HD], kvs_grad[:, 3 * HD :]
    w_key_grad = jnp.concatenate([first_half[:, :HD], second_half[:, :HD]], axis=-1)
    w_value_grad = jnp.concatenate(
        [first_half[:, HD : 2 * HD], second_half[:, HD : 2 * HD]], axis=-1
    )
    small_grad = first_half[:, 2 * HD :] + second_half[:, 2 * HD :]

    return (
        output,
        input_grad[None],
        small_grad[None, :, experts],
        small_grad[None, :, experts + 1],
        q_w_grad[None],
        w_key_grad[None],
        w_value_grad[None],
        out_w_grad[None],
        small_grad[None, :, :experts],
        w_gate_grad,
        w_up_grad,
        w_down_grad,
    )


def in_three(value):
    high = value.astype(bf16)
    rest = value - high.astype(f32)
    middle = rest.astype(bf16)
    return [high, middle, (rest - middle.astype(f32)).astype(bf16)]


def solution(mesh):
    fine = Mesh(mesh.devices.reshape(2, 4, 2, 4, 2), AXES)
    seq = P(FSDP, CTX, None)
    vector = P(None, AXES)
    matrix = P(None, AXES, None)
    expert = P(None, FSDP, CTX, None)
    in_specs = (
        seq,
        seq,
        P(),
        P(None, FSDP, CTX, None),
        vector,
        vector,
        matrix,
        matrix,
        matrix,
        matrix,
        matrix,
        expert,
        expert,
        expert,
    )
    out_specs = (
        seq,
        seq,
        vector,
        vector,
        matrix,
        matrix,
        matrix,
        matrix,
        matrix,
        expert,
        expert,
        expert,
    )
    return jax.shard_map(body, mesh=fine, in_specs=in_specs, out_specs=out_specs, check_vma=False)
```

```python
import functools
import math

import jax
import jax.numpy as jnp
from jax import lax
from jax.experimental import pallas as pl
from jax.experimental.pallas import tpu as pltpu
from jax.sharding import Mesh
from jax.sharding import PartitionSpec as P

H = 12
KVH = 2
HD = 128
TOPK = 4

EPSILON = 1e-06
ROPE_BASE = 1000000.0
NEGATIVE = -1e30

AXES = ("ylo", "z", "core", "x", "yhi")
CTX = ("ylo", "z", "core")
FSDP = ("x", "yhi")
GROUPS = [
    [
        (((group ^ yhi) * 4 + z) * 2 + core) * 8 + x * 2 + yhi
        for x in range(4)
        for yhi in range(2)
        for core in range(2)
    ]
    for group in range(2)
    for z in range(4)
]
RING = ("ylo", "z")
ROWS_ORDER = ("ylo", "z", "yhi", "x")
OUT_ORDER = ("yhi", "z", "ylo", "x")
SLOTS = 40

bf16 = jnp.bfloat16
f32 = jnp.float32


def dot(left, right):
    return jnp.dot(left, right, preferred_element_type=f32)


def dot_t(left, right):
    return lax.dot_general(left, right, (((1,), (1,)), ((), ())), preferred_element_type=f32)


def t_dot(left, right):
    return lax.dot_general(left, right, (((0,), (0,)), ((), ())), preferred_element_type=f32)


def exchange(pieces, axes):
    return lax.all_to_all(pieces, axes, split_axis=0, concat_axis=0, tiled=True)


def to_owners(pieces):
    return lax.all_to_all(
        pieces, AXES, split_axis=0, concat_axis=0, axis_index_groups=GROUPS, tiled=True
    )


def spread(piece, count, axes):
    return exchange(jnp.broadcast_to(piece[None], (count,) + piece.shape), axes)


def after(value, earlier):
    return lax.optimization_barrier((value, earlier))[0]


def partner(value):
    return lax.ppermute(value, "core", [(0, 1), (1, 0)])


def route(axes, sizes, move):
    pairs = []
    for source in range(math.prod(sizes)):
        rest, at = source, []
        for size in reversed(sizes):
            at.insert(0, rest % size)
            rest //= size
        target = 0
        for size, value in zip(sizes, move(*at)):
            target = target * size + value
        pairs.append((source, target))
    return pairs


SAME = route(("core", "yhi"), (2, 2), lambda c, h: (h, c))
OTHER = route(("core", "yhi"), (2, 2), lambda c, h: (1 - h, c))
OUT_SAME = route(("ylo", "core", "yhi"), (2, 2, 2), lambda j, c, h: (c, j, h))
OUT_OTHER = route(("ylo", "core", "yhi"), (2, 2, 2), lambda j, c, h: (c, j, 1 - h))


def back(pairs):
    return [(target, source) for source, target in pairs]


def pick(flag, if_zero, if_one):
    return jnp.where(flag == 0, if_zero, if_one)


def gather_pieces(pair, flag, key, axes, same, other):
    first = lax.ppermute(pick(flag, pair[0], pair[1]), axes, same)
    second = lax.ppermute(pick(flag, pair[1], pair[0]), axes, other)
    return pick(
        key, jnp.concatenate([first, second]), jnp.concatenate([second, first])
    )


def scatter_pieces(piece, flag, key, axes, same, other):
    count = piece.shape[0] // 2
    mine, rest = piece[:count], piece[count:]
    first = lax.ppermute(pick(key, mine, rest), axes, back(same))
    second = lax.ppermute(pick(key, rest, mine), axes, back(other))
    return pick(flag, jnp.concatenate([first, second], axis=-1), jnp.concatenate([second, first], axis=-1))


OFFSETS = [(dy, dz) for dy in (0, 1) for dz in (0, 1, 3, 2)]


def ring_send(pieces):
    arrived = [pieces[0]]
    for (dy, dz), piece in zip(OFFSETS[1:], pieces[1:]):
        pairs = route(RING, (2, 4), lambda y, z: (y ^ dy, (z + dz) % 4))
        arrived.append(lax.ppermute(piece, RING, pairs))
    return arrived


def places(pair_of, ctx, row_count, ctx_count):
    half_size = row_count // 2
    pair = jnp.sum(
        jnp.where(ctx[:, None] == jnp.arange(ctx_count, dtype=jnp.int32)[None], pair_of[None], 0),
        axis=1,
    )
    block = jnp.stack([pair, 2 * ctx_count - 1 - pair], axis=1)
    return block[:, :, None] * half_size + jnp.arange(half_size, dtype=jnp.int32)[None, None]


def in_three(value):
    high = value.astype(bf16)
    rest = value - high.astype(f32)
    middle = rest.astype(bf16)
    return [high, middle, (rest - middle.astype(f32)).astype(bf16)]


def call(kernel, outs, *args, scratch=(), megabytes=32):
    whole = pl.BlockSpec(memory_space=pltpu.VMEM)
    return pl.pallas_call(
        kernel,
        out_shape=[jax.ShapeDtypeStruct(shape, dtype) for shape, dtype in outs],
        in_specs=[whole] * len(args),
        out_specs=[whole] * len(outs),
        scratch_shapes=list(scratch),
        compiler_params=pltpu.CompilerParams(vmem_limit_bytes=megabytes << 20),
        cost_estimate=COST,
    )(*args)


COST = pl.CostEstimate(flops=1 << 20, bytes_accessed=1 << 18, transcendentals=0)
WIDE = 2 * HD
EXPERTS = 16


def turn(vectors, cosines, sines):
    return vectors * cosines + pltpu.roll(vectors, HD // 2, axis=1) * sines


def gain_picker():
    row = lax.broadcasted_iota(jnp.int32, (8, 128), 0)
    column = lax.broadcasted_iota(jnp.int32, (8, 128), 1)
    return jnp.where((column == row + EXPERTS) & (row < 2), 1.0, 0.0).astype(bf16)


def normal_of(stream):
    inverse = lax.rsqrt(jnp.mean(stream * stream, axis=-1, keepdims=True) + EPSILON)
    return stream * inverse, inverse


def norm_back(grad, normal, inverse, gain):
    scaled = grad * gain
    return inverse * (scaled - normal * jnp.mean(scaled * normal, axis=-1, keepdims=True))


def keys_kernel(both, w_kvs, cosines, sines, normed, key_value, gains):
    gains[...] = dot_t(gain_picker(), w_kvs[:, WIDE:])
    normal, _ = normal_of(both[...].astype(f32))
    normed[...] = (normal * gains[0:1]).astype(bf16)
    kv = dot(normed[...], w_kvs[:, :WIDE])
    key_value[:, :HD] = turn(kv[:, :HD], cosines[...], sines[...]).astype(bf16)
    key_value[:, HD:] = kv[:, HD:].astype(bf16)


def attend_kernel(
    normed, w_q, cosines, sines, q_place, low_place, up_place, *refs, scale, pieces, heads
):
    kv, (queries, mixed, logs, kv_low, kv_up) = refs[:pieces], refs[pieces:]
    half = kv[0].shape[0] // 2
    for i in range(pieces):
        kv_low[i * half : (i + 1) * half, :] = kv[i][:half, :]
        kv_up[i * half : (i + 1) * half, :] = kv[i][half:, :]
    allowed_low = low_place[...] <= q_place[...]
    allowed_up = up_place[...] <= q_place[half:, :]
    for h in range(heads):
        at = slice(h * HD, (h + 1) * HD)
        q = turn(dot(normed[...], w_q[:, at]), cosines[...], sines[...]).astype(bf16)
        queries[:, at] = q
        low = jnp.where(allowed_low, dot_t(q, kv_low[:, :HD]) * scale, NEGATIVE)
        up = jnp.where(allowed_up, dot_t(q[half:], kv_up[:, :HD]) * scale, NEGATIVE)
        first, second = low[:half], low[half:]
        top = jnp.max(first, axis=-1, keepdims=True)
        weight = jnp.exp(first - top)
        total = jnp.sum(weight, axis=-1, keepdims=True)
        probs = (weight / total).astype(bf16)
        mixed[:half, at] = dot(probs, kv_low[:, HD:]).astype(bf16)
        logs[h, :half, :] = top + jnp.log(total)
        top = jnp.maximum(
            jnp.max(second, axis=-1, keepdims=True), jnp.max(up, axis=-1, keepdims=True)
        )
        weight, weight_up = jnp.exp(second - top), jnp.exp(up - top)
        total = jnp.sum(weight, axis=-1, keepdims=True) + jnp.sum(
            weight_up, axis=-1, keepdims=True
        )
        mixed[half:, at] = (
            dot((weight / total).astype(bf16), kv_low[:, HD:])
            + dot((weight_up / total).astype(bf16), kv_up[:, HD:])
        ).astype(bf16)
        logs[h, half:, :] = top + jnp.log(total)


def branch_kernel(mixed, w_out, own, other):
    quarter = mixed.shape[0] // 4
    columns = w_out.shape[2]
    for k in range(2):
        part = dot(mixed[...], w_out[k])
        at = slice(k * columns, (k + 1) * columns)
        own[:quarter, at] = part[:quarter]
        other[:quarter, at] = part[quarter : 2 * quarter]
        own[quarter:, at] = part[2 * quarter : 3 * quarter]
        other[quarter:, at] = part[3 * quarter :]


def route_kernel(
    tokens, own, received, w_kvs, gains, hits, places_of, placer, sent, midway, moe_low, gates, parts
):
    middle = tokens[...].astype(f32) + (own[...] + received[...])
    midway[...] = middle
    normal, _ = normal_of(middle)
    moe = (normal * gains[1:2]).astype(bf16)
    moe_low[...] = moe
    sent[:, : moe.shape[1]] = dot(placer[...], moe).astype(bf16)
    logits = dot(moe, w_kvs[:, WIDE:])
    picked = [
        jnp.sum(hits[k].astype(f32) * logits, axis=-1, keepdims=True) for k in range(TOPK)
    ]
    top = picked[0]
    for value in picked[1:]:
        top = jnp.maximum(top, value)
    weights = [jnp.exp(value - top) for value in picked]
    total = weights[0]
    for value in weights[1:]:
        total = total + value
    lane = lax.broadcasted_iota(jnp.int32, gates.shape, 1)
    gate_at = jnp.zeros(places_of.shape[1:], f32)
    kept = jnp.zeros(gates.shape, f32)
    for k in range(TOPK):
        gate = weights[k] / total
        kept = jnp.where(lane == k, gate, kept)
        gate_at = gate_at + places_of[k].astype(f32) * gate
    gates[...] = kept
    block = jnp.zeros((sent.shape[0], 128), f32)
    for i, part in enumerate(in_three(gate_at)):
        parts[i] = part
        block = block + t_dot(part, jnp.where(lane == i, 1.0, 0.0).astype(bf16))
    sent[:, moe.shape[1] :] = block.astype(bf16)


def forward_kernel(core, sent, cot, gate, up, down, out, hidden, out_grad, factor, other_factor):
    del core
    width = out.shape[1]
    rows = sent[:, :width]
    gate_pre, up_pre = dot(rows, gate[...]), dot(rows, up[...])
    sigmoid = 1.0 / (1.0 + jnp.exp(-gate_pre))
    silu = gate_pre * sigmoid
    low = (silu * up_pre).astype(bf16)
    hidden[...] = low
    out[...] = dot_t(low, down[...]).astype(bf16)
    gates = jnp.sum(sent[:, width:].astype(f32), axis=-1, keepdims=True)
    out_grad[...] = (gates * cot[...].astype(f32)).astype(bf16)
    factor[...] = up_pre * sigmoid * (1.0 + gate_pre * (1.0 - sigmoid))
    other_factor[...] = silu


def backward_kernel(
    core, out_grad, factor, other_factor, gate, up, down, rows_grad, gate_grad, up_grad
):
    del core
    hidden_grad = dot(out_grad[...], down[...])
    low = (hidden_grad * factor[...]).astype(bf16)
    other = (hidden_grad * other_factor[...]).astype(bf16)
    gate_grad[...] = low
    up_grad[...] = other
    rows_grad[...] = (dot_t(low, gate[...]) + dot_t(other, up[...])).astype(bf16)


def expert_call(kernel, block, core, arrays, weights, outs):
    count = arrays[0].shape[0]

    def rows(columns):
        return pl.BlockSpec((block, columns), lambda i, core: (i, 0))

    def whole(m):
        return pl.BlockSpec(
            (None, None) + weights.shape[2:],
            lambda i, core: (m, core[0], 0, 0),
            pipeline_mode=pl.Buffered(1),
        )

    return pl.pallas_call(
        kernel,
        out_shape=[jax.ShapeDtypeStruct((count, columns), dtype) for columns, dtype in outs],
        grid_spec=pltpu.PrefetchScalarGridSpec(
            num_scalar_prefetch=1,
            grid=(count // block,),
            in_specs=[rows(a.shape[1]) for a in arrays] + [whole(m) for m in range(3)],
            out_specs=[rows(columns) for columns, _ in outs],
        ),
        compiler_params=pltpu.CompilerParams(vmem_limit_bytes=40 << 20),
        cost_estimate=COST,
    )(core, *arrays, weights, weights, weights)


def weights_kernel(sent, out_grad, hidden, gate_grad, up_grad, sums):
    rows = sent[...]
    sums[0] = t_dot(rows, gate_grad[...]).astype(bf16)
    sums[1] = t_dot(rows, up_grad[...]).astype(bf16)
    sums[2] = t_dot(out_grad[...], hidden[...]).astype(bf16)


def expert_weights_grad(sent, out_grad, hidden, gate_grad, up_grad, block=256):
    count, width = out_grad.shape
    columns = hidden.shape[1]
    part = pl.BlockSpec((count, block), lambda i: (0, i))
    whole = pl.BlockSpec((count, columns), lambda i: (0, 0), pipeline_mode=pl.Buffered(1))
    return pl.pallas_call(
        weights_kernel,
        out_shape=jax.ShapeDtypeStruct((3, width, columns), bf16),
        grid=(width // block,),
        in_specs=[part, part, whole, whole, whole],
        out_specs=pl.BlockSpec((3, block, columns), lambda i: (0, i, 0)),
        compiler_params=pltpu.CompilerParams(vmem_limit_bytes=32 << 20),
        cost_estimate=COST,
    )(sent, out_grad, hidden, gate_grad, up_grad)


def combine_kernel(
    midway, parts, returned, cot, hits, places_of, gates, w_kvs, moe_low, output, moe_part, router_grad
):
    rows = returned[...]
    output[...] = (
        midway[...] + (dot(parts[0], rows) + (dot(parts[1], rows) + dot(parts[2], rows)))
    ).astype(bf16)
    agreement = dot_t(cot[...], rows)
    lane = lax.broadcasted_iota(jnp.int32, gates.shape, 1)
    gate, grad = [], []
    mean = jnp.zeros((gates.shape[0], 1), f32)
    for k in range(TOPK):
        gate.append(jnp.sum(jnp.where(lane == k, gates[...], 0.0), axis=-1, keepdims=True))
        grad.append(jnp.sum(places_of[k].astype(f32) * agreement, axis=-1, keepdims=True))
        mean = mean + gate[k] * grad[k]
    logit_grad = jnp.zeros(gates.shape, f32)
    for k in range(TOPK):
        logit_grad = logit_grad + hits[k].astype(f32) * (gate[k] * (grad[k] - mean))
    logit_grad = logit_grad.astype(bf16)
    moe_part[...] = dot_t(logit_grad, w_kvs[:, WIDE:])
    router_grad[...] = t_dot(moe_low[...], logit_grad)


def home_kernel(placer_t, home, moe_part, midway, cot, gains, midway_grad, branch_low, gain_grad):
    grad = dot(placer_t[...], home[...]) + moe_part[...]
    normal, inverse = normal_of(midway[...])
    result = cot[...].astype(f32) + norm_back(grad, normal, inverse, gains[1:2])
    midway_grad[...] = result
    branch_low[...] = result.astype(bf16)
    gain_grad[...] = jnp.broadcast_to(
        jnp.sum(grad * normal, axis=0, keepdims=True), gain_grad.shape
    )


def out_grad_kernel(mixed, own, other, branch, pieces):
    quarter = own.shape[0] // 2
    branch[:quarter] = own[:quarter]
    branch[quarter : 2 * quarter] = other[:quarter]
    branch[2 * quarter : 3 * quarter] = own[quarter:]
    branch[3 * quarter :] = other[quarter:]
    columns = pieces.shape[2]
    for k in range(2):
        at = slice(k * columns, (k + 1) * columns)
        pieces[k] = t_dot(mixed[...], branch[:, at]).astype(bf16)


def attend_back_kernel(
    branch,
    w_out,
    queries,
    kv_low,
    kv_up,
    logs,
    q_place,
    low_place,
    up_place,
    cosines,
    sines,
    dq,
    dkv,
    grads,
    acc_low,
    acc_up,
    *,
    scale,
    pieces,
    heads,
):
    half = queries.shape[0] // 2
    columns = w_out.shape[2]
    grads[...] = (
        dot_t(branch[:, :columns], w_out[0]) + dot_t(branch[:, columns:], w_out[1])
    ).astype(bf16)
    allowed_low = low_place[...] <= q_place[...]
    allowed_up = up_place[...] <= q_place[half:, :]
    key_low, value_low = kv_low[:, :HD], kv_low[:, HD:]
    key_up, value_up = kv_up[:, :HD], kv_up[:, HD:]
    for h in range(heads):
        at = slice(h * HD, (h + 1) * HD)
        q, grad, log = queries[:, at], grads[:, at], logs[h]
        low = jnp.where(allowed_low, dot_t(q, key_low) * scale, NEGATIVE)
        up = jnp.where(allowed_up, dot_t(q[half:], key_up) * scale, NEGATIVE)
        probs_low, probs_up = jnp.exp(low - log), jnp.exp(up - log[half:])
        grad_low, grad_up = dot_t(grad, value_low), dot_t(grad[half:], value_up)
        along = jnp.sum(probs_low * grad_low, axis=-1, keepdims=True)
        along_up = along[half:] + jnp.sum(probs_up * grad_up, axis=-1, keepdims=True)
        along = jnp.concatenate([along[:half], along_up])
        score_low = (probs_low * (grad_low - along)).astype(bf16)
        score_up = (probs_up * (grad_up - along_up)).astype(bf16)
        part = dot(score_low, key_low)
        part = jnp.concatenate([part[:half], part[half:] + dot(score_up, key_up)]) * scale
        dq[:, at] = turn(part, cosines[...], -sines[...]).astype(bf16)
        terms = (
            (acc_low, slice(0, HD), t_dot(q, score_low)),
            (acc_up, slice(0, HD), t_dot(q[half:], score_up)),
            (acc_low, slice(HD, 2 * HD), t_dot(grad, probs_low.astype(bf16))),
            (acc_up, slice(HD, 2 * HD), t_dot(grad[half:], probs_up.astype(bf16))),
        )
        for acc, rows, term in terms:
            if h == 0:
                acc[rows] = term
            else:
                acc[rows] += term
    for acc, first in ((acc_low, 0), (acc_up, half)):
        dk = (acc[:HD].T * scale).astype(bf16)
        dv = acc[HD:].T.astype(bf16)
        for i in range(pieces):
            dkv[i, first : first + half, :HD] = dk[i * half : (i + 1) * half]
            dkv[i, first : first + half, HD:] = dv[i * half : (i + 1) * half]


def sum_kernel(dq, w_q, w_kvs, cosines, sines, *refs):
    parts, (dkv, own, other) = refs[:-3], refs[-3:]
    total = parts[0][...].astype(f32)
    for part in parts[1:]:
        total = total + part[...].astype(f32)
    dkv[:, :HD] = turn(total[:, :HD], cosines[...], -sines[...]).astype(bf16)
    dkv[:, HD:] = total[:, HD:].astype(bf16)
    grad = dot_t(dq[...], w_q[...]) + dot_t(dkv[...], w_kvs[:, :WIDE])
    quarter = own.shape[0] // 2
    own[:quarter] = grad[:quarter]
    other[:quarter] = grad[quarter : 2 * quarter]
    own[quarter:] = grad[2 * quarter : 3 * quarter]
    other[quarter:] = grad[3 * quarter :]


def input_kernel(
    tokens, own, received, midway_grad, gains, gain_two_grad, router_grad, normed, dkv, out, kvs_grad
):
    grad = own[...] + received[...]
    normal, inverse = normal_of(tokens[...].astype(f32))
    out[...] = midway_grad[...] + norm_back(grad, normal, inverse, gains[0:1])
    gain_grad = jnp.sum(grad * normal, axis=0, keepdims=True)
    row = lax.broadcasted_iota(jnp.int32, gain_two_grad.shape, 0)
    gain_grads = jnp.where(row == 0, gain_grad, jnp.where(row == 1, gain_two_grad[...], 0.0))
    small = router_grad[...] + t_dot(gain_grads.astype(bf16), gain_picker())
    kvs_grad[:, WIDE:] = small.astype(bf16)
    kvs_grad[:, :WIDE] = t_dot(normed[...], dkv[...]).astype(bf16)


def query_grad_kernel(normed, dq, out):
    out[...] = t_dot(normed[...], dq[...]).astype(bf16)


def body(
    tokens,
    cotangent,
    pair_of,
    routes,
    attn_gain,
    moe_gain,
    w_query,
    w_key,
    w_value,
    w_out,
    w_router,
    w_gate,
    w_up,
    w_down,
):
    rows = tokens.shape[1]
    half = rows // 2
    width = tokens.shape[2]
    shard = w_query.shape[1]
    ctx_count = 16
    experts = w_router.shape[2]
    columns = w_gate.shape[3]
    per_group = H // KVH
    qw = per_group * HD
    scale = 1.0 / math.sqrt(HD)
    core = lax.axis_index("core")
    ylo, z, yhi = lax.axis_index("ylo"), lax.axis_index("z"), lax.axis_index("yhi")
    piece_rows = 2 * shard
    slots = experts * SLOTS
    own_tokens, cot = tokens[0], cotangent[0]

    def halves(matrix):
        return [matrix[:, : matrix.shape[1] // 2], matrix[:, matrix.shape[1] // 2 :]]

    small = jnp.concatenate([w_router[0], attn_gain[0][:, None], moe_gain[0][:, None]], axis=-1)
    small = jnp.pad(small, ((0, 0), (0, 128 - experts - 2)))
    query_halves, key_halves, value_halves = halves(w_query[0]), halves(w_key[0]), halves(w_value[0])
    pairs = [
        jnp.concatenate([k, v, small, q], axis=-1)
        for k, v, q in zip(key_halves, value_halves, query_halves)
    ]
    pieces = gather_pieces(pairs, yhi, core, ("core", "yhi"), SAME, OTHER)
    w_kvs = spread(pieces[:, : 3 * HD], 64, ROWS_ORDER)
    w_q = spread(after(pieces[:, 3 * HD :], w_kvs), 64, ROWS_ORDER).reshape(width, qw)
    out_pieces = gather_pieces(
        halves(w_out[0]), yhi, yhi, ("ylo", "core", "yhi"), OUT_SAME, OUT_OTHER
    )
    wo = spread(after(out_pieces, w_q), 64, OUT_ORDER).reshape(2, qw, width // 2)
    w_kvs = w_kvs.reshape(width, 3 * HD)

    expert_weights = lax.all_gather(
        after(jnp.stack([w_gate[0], w_up[0], w_down[0]]), w_q), CTX, axis=2, tiled=True
    )

    chosen = routes[0, 0]
    lanes = jnp.arange(128, dtype=jnp.int32)
    hits = (chosen.T[:, :, None] == lanes[None, None, :]).astype(bf16)
    earlier = (lanes[:, None] > lanes[None, :]).astype(bf16)
    before = dot(earlier, jnp.sum(hits, axis=0))
    slot_index = jnp.sum(hits.astype(f32) * before[None], axis=-1).astype(jnp.int32)
    target = chosen.T * SLOTS + slot_index
    slot_row = jnp.arange(slots, dtype=jnp.int32)
    places_of = (target[:, :, None] == slot_row[None, None, :]).astype(bf16)
    placer_t = jnp.sum(places_of, axis=0)
    placer = placer_t.T
    cot_rows = dot(placer, cot).astype(bf16).reshape(experts, SLOTS, width)
    arrived_cot = to_owners(after(cot_rows, wo)).reshape(slots, width)

    other_tokens = partner(own_tokens)
    both = jnp.concatenate(
        [own_tokens[:half], other_tokens[:half], own_tokens[half:], other_tokens[half:]]
    )

    def two_cores(ctx):
        return jnp.stack([ctx + core, ctx + 1 - core], axis=-1).reshape(-1)

    ctx_here = (ylo * 4 + z) * 2
    q_place = places(pair_of, two_cores(ctx_here), rows, ctx_count)
    q_place = q_place.transpose(1, 0, 2).reshape(2 * rows, 1)
    ctx_there = jnp.stack([((ylo ^ dy) * 4 + (z - dz) % 4) * 2 for dy, dz in OFFSETS])
    key_place = places(pair_of, two_cores(ctx_there), rows, ctx_count)
    low_place, up_place = key_place[:, 0].reshape(1, -1), key_place[:, 1].reshape(1, -1)
    frequency = jnp.exp(jnp.arange(HD // 2, dtype=f32) * (-2.0 * math.log(ROPE_BASE) / HD))
    angles = q_place.astype(f32) * frequency[None, :]
    cosines, sines = jnp.cos(angles), jnp.sin(angles)
    cosines = jnp.concatenate([cosines, cosines], axis=-1)
    sines = jnp.concatenate([-sines, sines], axis=-1)

    normed, key_value, gains = call(
        keys_kernel,
        [((2 * rows, width), bf16), ((2 * rows, 2 * HD), bf16), ((8, width), f32)],
        both,
        w_kvs,
        cosines,
        sines,
    )
    pieces_kv = ring_send([key_value] * len(OFFSETS))
    sizes = dict(scale=scale, pieces=len(OFFSETS), heads=per_group)
    keys = len(OFFSETS) * rows
    queries, mixed, logs, kv_low, kv_up = call(
        functools.partial(attend_kernel, **sizes),
        [
            ((2 * rows, qw), bf16),
            ((2 * rows, qw), bf16),
            ((per_group, 2 * rows, 1), f32),
            ((keys, 2 * HD), bf16),
            ((keys, 2 * HD), bf16),
        ],
        normed,
        w_q,
        cosines,
        sines,
        q_place,
        low_place,
        up_place,
        *pieces_kv,
    )
    branch_own, branch_other = call(
        branch_kernel, [((rows, width), f32), ((rows, width), f32)], mixed, wo
    )

    sent, midway, moe_low, gates, gate_parts = call(
        route_kernel,
        [
            ((slots, width + 128), bf16),
            ((rows, width), f32),
            ((rows, width), bf16),
            ((rows, 128), f32),
            ((3, rows, slots), bf16),
        ],
        own_tokens,
        branch_own,
        partner(branch_other),
        w_kvs,
        gains,
        hits,
        places_of,
        placer,
    )
    sent = to_owners(after(sent, arrived_cot).reshape(experts, SLOTS, width + 128))
    sent = sent.reshape(slots, width + 128)
    mine = core.reshape(1)
    expert_out, hidden, out_grad, factor, other_factor = expert_call(
        forward_kernel,
        128,
        mine,
        [sent, arrived_cot],
        expert_weights,
        [(width, bf16), (columns, bf16), (width, bf16), (columns, f32), (columns, f32)],
    )
    returned = to_owners(expert_out.reshape(experts, SLOTS, width))
    rows_grad, gate_grad, up_grad = expert_call(
        backward_kernel,
        128,
        mine,
        [out_grad, factor, other_factor],
        expert_weights,
        [(width, bf16), (columns, bf16), (columns, bf16)],
    )
    expert_sums = expert_weights_grad(sent, out_grad, hidden, gate_grad, up_grad)
    expert_sums = lax.psum_scatter(expert_sums, RING, scatter_dimension=1, tiled=True)
    rows_grad = after(rows_grad, returned)
    returned = returned.reshape(slots, width)
    home_grad = to_owners(rows_grad.reshape(experts, SLOTS, width)).reshape(slots, width)
    output, moe_part, router_grad = call(
        combine_kernel,
        [((rows, width), bf16), ((rows, width), f32), ((width, 128), f32)],
        midway,
        gate_parts,
        returned,
        cot,
        hits,
        places_of,
        gates,
        w_kvs,
        moe_low,
    )
    midway_grad, branch_low, gain_two_grad = call(
        home_kernel,
        [((rows, width), f32), ((rows, width), bf16), ((8, width), f32)],
        placer_t,
        home_grad,
        moe_part,
        midway,
        cot,
        gains,
    )

    branch, out_w_grad = call(
        out_grad_kernel,
        [((2 * rows, width), bf16), ((2, qw, width // 2), bf16)],
        mixed,
        branch_low,
        partner(branch_low),
    )
    out_w_grad = exchange(out_w_grad.reshape(64, piece_rows, width // 2), OUT_ORDER)
    dq, dkv = call(
        functools.partial(attend_back_kernel, **sizes),
        [((2 * rows, qw), bf16), ((len(OFFSETS), 2 * rows, 2 * HD), bf16)],
        branch,
        wo,
        queries,
        kv_low,
        kv_up,
        logs,
        q_place,
        low_place,
        up_place,
        cosines,
        sines,
        scratch=[
            pltpu.VMEM((2 * rows, qw), bf16),
            pltpu.VMEM((2 * HD, keys), f32),
            pltpu.VMEM((2 * HD, keys), f32),
        ],
    )
    back_order = [OFFSETS.index((dy, (-dz) % 4)) for dy, dz in OFFSETS]
    dkv = ring_send([dkv[i] for i in back_order])
    (q_w_grad,) = call(query_grad_kernel, [((width, qw), bf16)], normed, dq)
    q_w_grad = q_w_grad.reshape(64, piece_rows, qw)
    q_w_grad = exchange(after(q_w_grad, out_w_grad), ROWS_ORDER)
    dkv, normed_own, normed_other = call(
        sum_kernel,
        [((2 * rows, 2 * HD), bf16), ((rows, width), f32), ((rows, width), f32)],
        dq,
        w_q,
        w_kvs,
        cosines,
        sines,
        *dkv,
    )
    input_grad, kvs_grad = call(
        input_kernel,
        [((rows, width), f32), ((width, 3 * HD), bf16)],
        own_tokens,
        normed_own,
        partner(normed_other),
        midway_grad,
        gains,
        gain_two_grad,
        router_grad,
        normed,
        dkv,
    )
    kvs_grad = kvs_grad.reshape(64, piece_rows, 3 * HD)
    kvs_grad = exchange(after(kvs_grad, q_w_grad), ROWS_ORDER)

    def summed(pieces):
        return jnp.sum(pieces.astype(f32), axis=0)

    def expert_shards(grad):
        count = grad.shape[1] // 2
        kept = lax.dynamic_slice_in_dim(grad, core * count, count, axis=1)
        given = partner(lax.dynamic_slice_in_dim(grad, (1 - core) * count, count, axis=1))
        both = jnp.stack([pick(core, kept, given), pick(core, given, kept)], axis=1)
        return [both[i : i + 1].astype(f32) for i in range(3)]

    out_w_grad = scatter_pieces(
        summed(out_w_grad), yhi, yhi, ("ylo", "core", "yhi"), OUT_SAME, OUT_OTHER
    )
    q_w_grad = scatter_pieces(summed(q_w_grad), yhi, core, ("core", "yhi"), SAME, OTHER)
    w_gate_grad, w_up_grad, w_down_grad = expert_shards(after(expert_sums, q_w_grad))
    kvs_grad = scatter_pieces(summed(kvs_grad), yhi, core, ("core", "yhi"), SAME, OTHER)
    first_half, second_half = kvs_grad[:, : 3 * HD], kvs_grad[:, 3 * HD :]
    w_key_grad = jnp.concatenate([first_half[:, :HD], second_half[:, :HD]], axis=-1)
    w_value_grad = jnp.concatenate(
        [first_half[:, HD : 2 * HD], second_half[:, HD : 2 * HD]], axis=-1
    )
    small_grad = first_half[:, 2 * HD :] + second_half[:, 2 * HD :]

    return (
        output[None],
        input_grad[None],
        small_grad[None, :, experts],
        small_grad[None, :, experts + 1],
        q_w_grad[None],
        w_key_grad[None],
        w_value_grad[None],
        out_w_grad[None],
        small_grad[None, :, :experts],
        w_gate_grad,
        w_up_grad,
        w_down_grad,
    )


def solution(mesh):
    fine = Mesh(mesh.devices.reshape(2, 4, 2, 4, 2), AXES)
    seq = P(FSDP, CTX, None)
    vector = P(None, AXES)
    matrix = P(None, AXES, None)
    expert = P(None, FSDP, CTX, None)
    in_specs = (
        seq,
        seq,
        P(),
        P(None, FSDP, CTX, None),
        vector,
        vector,
        matrix,
        matrix,
        matrix,
        matrix,
        matrix,
        expert,
        expert,
        expert,
    )
    out_specs = (
        seq,
        seq,
        vector,
        vector,
        matrix,
        matrix,
        matrix,
        matrix,
        matrix,
        expert,
        expert,
        expert,
    )
    return jax.shard_map(body, mesh=fine, in_specs=in_specs, out_specs=out_specs, check_vma=False)
```

```python
import functools
import math

import jax
import jax.numpy as jnp
from jax import lax
from jax.experimental import pallas as pl
from jax.experimental.pallas import tpu as pltpu
from jax.sharding import Mesh
from jax.sharding import PartitionSpec as P

H = 12
KVH = 2
HD = 128
TOPK = 4

EPSILON = 1e-06
ROPE_BASE = 1000000.0
NEGATIVE = -1e30

AXES = ("ylo", "z", "core", "x", "yhi")
CTX = ("ylo", "z", "core")
FSDP = ("x", "yhi")
GROUPS = [
    [
        (((group ^ yhi) * 4 + z) * 2 + core) * 8 + x * 2 + yhi
        for x in range(4)
        for yhi in range(2)
        for core in range(2)
    ]
    for group in range(2)
    for z in range(4)
]
RING = ("ylo", "z")
ROWS_ORDER = ("ylo", "z", "yhi", "x")
OUT_ORDER = ("yhi", "z", "ylo", "x")
SLOTS = 40

bf16 = jnp.bfloat16
f32 = jnp.float32


def dot(left, right):
    return jnp.dot(left, right, preferred_element_type=f32)


def dot_t(left, right):
    return lax.dot_general(left, right, (((1,), (1,)), ((), ())), preferred_element_type=f32)


def t_dot(left, right):
    return lax.dot_general(left, right, (((0,), (0,)), ((), ())), preferred_element_type=f32)


def exchange(pieces, axes):
    return lax.all_to_all(pieces, axes, split_axis=0, concat_axis=0, tiled=True)


def to_owners(pieces):
    return lax.all_to_all(
        pieces, AXES, split_axis=0, concat_axis=0, axis_index_groups=GROUPS, tiled=True
    )


def spread(piece, count, axes):
    return exchange(jnp.broadcast_to(piece[None], (count,) + piece.shape), axes)


def after(value, earlier):
    return lax.optimization_barrier((value, earlier))[0]


def together(*values):
    return lax.optimization_barrier(values)


def partner(value):
    return lax.ppermute(value, "core", [(0, 1), (1, 0)])


def route(axes, sizes, move):
    pairs = []
    for source in range(math.prod(sizes)):
        rest, at = source, []
        for size in reversed(sizes):
            at.insert(0, rest % size)
            rest //= size
        target = 0
        for size, value in zip(sizes, move(*at)):
            target = target * size + value
        pairs.append((source, target))
    return pairs


SAME = route(("core", "yhi"), (2, 2), lambda c, h: (h, c))
OTHER = route(("core", "yhi"), (2, 2), lambda c, h: (1 - h, c))
OUT_SAME = route(("ylo", "core", "yhi"), (2, 2, 2), lambda j, c, h: (c, j, h))
OUT_OTHER = route(("ylo", "core", "yhi"), (2, 2, 2), lambda j, c, h: (c, j, 1 - h))


def back(pairs):
    return [(target, source) for source, target in pairs]


def pick(flag, if_zero, if_one):
    return jnp.where(flag == 0, if_zero, if_one)


def gather_pieces(pair, flag, key, axes, same, other):
    first = lax.ppermute(pick(flag, pair[0], pair[1]), axes, same)
    second = lax.ppermute(pick(flag, pair[1], pair[0]), axes, other)
    return pick(
        key, jnp.concatenate([first, second]), jnp.concatenate([second, first])
    )


def scatter_pieces(piece, flag, key, axes, same, other):
    count = piece.shape[0] // 2
    mine, rest = piece[:count], piece[count:]
    first = lax.ppermute(pick(key, mine, rest), axes, back(same))
    second = lax.ppermute(pick(key, rest, mine), axes, back(other))
    return pick(flag, jnp.concatenate([first, second], axis=-1), jnp.concatenate([second, first], axis=-1))


OFFSETS = [(dy, dz) for dy in (0, 1) for dz in (0, 1, 3, 2)]


def ring_send(pieces):
    arrived = [pieces[0]]
    for (dy, dz), piece in zip(OFFSETS[1:], pieces[1:]):
        pairs = route(RING, (2, 4), lambda y, z: (y ^ dy, (z + dz) % 4))
        arrived.append(lax.ppermute(piece, RING, pairs))
    return arrived


def places(pair_of, ctx, row_count, ctx_count):
    half_size = row_count // 2
    pair = jnp.sum(
        jnp.where(ctx[:, None] == jnp.arange(ctx_count, dtype=jnp.int32)[None], pair_of[None], 0),
        axis=1,
    )
    block = jnp.stack([pair, 2 * ctx_count - 1 - pair], axis=1)
    return block[:, :, None] * half_size + jnp.arange(half_size, dtype=jnp.int32)[None, None]


def in_three(value):
    high = value.astype(bf16)
    rest = value - high.astype(f32)
    middle = rest.astype(bf16)
    return [high, middle, (rest - middle.astype(f32)).astype(bf16)]


def call(kernel, outs, *args, scratch=(), megabytes=12):
    whole = pl.BlockSpec(memory_space=pltpu.VMEM)
    return pl.pallas_call(
        kernel,
        out_shape=[jax.ShapeDtypeStruct(shape, dtype) for shape, dtype in outs],
        in_specs=[whole] * len(args),
        out_specs=[whole] * len(outs),
        scratch_shapes=list(scratch),
        compiler_params=pltpu.CompilerParams(vmem_limit_bytes=megabytes << 20),
        cost_estimate=COST,
    )(*args)


COST = pl.CostEstimate(flops=1 << 20, bytes_accessed=1 << 18, transcendentals=0)
WIDE = 2 * HD
EXPERTS = 16


def turn(vectors, cosines, sines):
    return vectors * cosines + pltpu.roll(vectors, HD // 2, axis=1) * sines


def gain_picker():
    row = lax.broadcasted_iota(jnp.int32, (8, 128), 0)
    column = lax.broadcasted_iota(jnp.int32, (8, 128), 1)
    return jnp.where((column == row + EXPERTS) & (row < 2), 1.0, 0.0).astype(bf16)


def normal_of(stream):
    inverse = lax.rsqrt(jnp.mean(stream * stream, axis=-1, keepdims=True) + EPSILON)
    return stream * inverse, inverse


def norm_back(grad, normal, inverse, gain):
    scaled = grad * gain
    return inverse * (scaled - normal * jnp.mean(scaled * normal, axis=-1, keepdims=True))


def keys_kernel(both, w_kvs, cosines, sines, normed, key_value, gains):
    gains[...] = dot_t(gain_picker(), w_kvs[:, WIDE:])
    normal, _ = normal_of(both[...].astype(f32))
    normed[...] = (normal * gains[0:1]).astype(bf16)
    kv = dot(normed[...], w_kvs[:, :WIDE])
    key_value[:, :HD] = turn(kv[:, :HD], cosines[...], sines[...]).astype(bf16)
    key_value[:, HD:] = kv[:, HD:].astype(bf16)


def attend_kernel(
    normed, w_q, cosines, sines, q_place, low_place, up_place, *refs, scale, pieces, heads
):
    kv, (queries, mixed, logs, kv_low, kv_up) = refs[:pieces], refs[pieces:]
    half = kv[0].shape[0] // 2
    for i in range(pieces):
        kv_low[i * half : (i + 1) * half, :] = kv[i][:half, :]
        kv_up[i * half : (i + 1) * half, :] = kv[i][half:, :]
    allowed_low = low_place[...] <= q_place[...]
    allowed_up = up_place[...] <= q_place[half:, :]
    for h in range(heads):
        at = slice(h * HD, (h + 1) * HD)
        q = turn(dot(normed[...], w_q[:, at]), cosines[...], sines[...]).astype(bf16)
        queries[:, at] = q
        low = jnp.where(allowed_low, dot_t(q, kv_low[:, :HD]) * scale, NEGATIVE)
        up = jnp.where(allowed_up, dot_t(q[half:], kv_up[:, :HD]) * scale, NEGATIVE)
        first, second = low[:half], low[half:]
        top = jnp.max(first, axis=-1, keepdims=True)
        weight = jnp.exp(first - top)
        total = jnp.sum(weight, axis=-1, keepdims=True)
        probs = (weight / total).astype(bf16)
        mixed[:half, at] = dot(probs, kv_low[:, HD:]).astype(bf16)
        logs[h, :half, :] = top + jnp.log(total)
        top = jnp.maximum(
            jnp.max(second, axis=-1, keepdims=True), jnp.max(up, axis=-1, keepdims=True)
        )
        weight, weight_up = jnp.exp(second - top), jnp.exp(up - top)
        total = jnp.sum(weight, axis=-1, keepdims=True) + jnp.sum(
            weight_up, axis=-1, keepdims=True
        )
        mixed[half:, at] = (
            dot((weight / total).astype(bf16), kv_low[:, HD:])
            + dot((weight_up / total).astype(bf16), kv_up[:, HD:])
        ).astype(bf16)
        logs[h, half:, :] = top + jnp.log(total)


def branch_kernel(mixed, w_out, own, other):
    quarter = mixed.shape[0] // 4
    columns = w_out.shape[2]
    for k in range(2):
        part = dot(mixed[...], w_out[k])
        at = slice(k * columns, (k + 1) * columns)
        own[:quarter, at] = part[:quarter]
        other[:quarter, at] = part[quarter : 2 * quarter]
        own[quarter:, at] = part[2 * quarter : 3 * quarter]
        other[quarter:, at] = part[3 * quarter :]


def route_kernel(
    tokens, own, received, w_kvs, gains, hits, places_of, placer, sent, midway, moe_low, gates, parts
):
    middle = tokens[...].astype(f32) + (own[...] + received[...])
    midway[...] = middle
    normal, _ = normal_of(middle)
    moe = (normal * gains[1:2]).astype(bf16)
    moe_low[...] = moe
    sent[:, : moe.shape[1]] = dot(placer[...], moe).astype(bf16)
    logits = dot(moe, w_kvs[:, WIDE:])
    picked = [
        jnp.sum(hits[k].astype(f32) * logits, axis=-1, keepdims=True) for k in range(TOPK)
    ]
    top = picked[0]
    for value in picked[1:]:
        top = jnp.maximum(top, value)
    weights = [jnp.exp(value - top) for value in picked]
    total = weights[0]
    for value in weights[1:]:
        total = total + value
    lane = lax.broadcasted_iota(jnp.int32, gates.shape, 1)
    gate_at = jnp.zeros(places_of.shape[1:], f32)
    kept = jnp.zeros(gates.shape, f32)
    for k in range(TOPK):
        gate = weights[k] / total
        kept = jnp.where(lane == k, gate, kept)
        gate_at = gate_at + places_of[k].astype(f32) * gate
    gates[...] = kept
    block = jnp.zeros((sent.shape[0], 128), f32)
    for i, part in enumerate(in_three(gate_at)):
        parts[i] = part
        block = block + t_dot(part, jnp.where(lane == i, 1.0, 0.0).astype(bf16))
    sent[:, moe.shape[1] :] = block.astype(bf16)


def forward_kernel(core, sent, cot, gate, up, down, out, hidden, out_grad, factor, other_factor):
    del core
    width = out.shape[1]
    rows = sent[:, :width]
    gate_pre, up_pre = dot(rows, gate[...]), dot(rows, up[...])
    sigmoid = 1.0 / (1.0 + jnp.exp(-gate_pre))
    silu = gate_pre * sigmoid
    low = (silu * up_pre).astype(bf16)
    hidden[...] = low
    out[...] = dot_t(low, down[...]).astype(bf16)
    gates = jnp.sum(sent[:, width:].astype(f32), axis=-1, keepdims=True)
    out_grad[...] = (gates * cot[...].astype(f32)).astype(bf16)
    factor[...] = up_pre * sigmoid * (1.0 + gate_pre * (1.0 - sigmoid))
    other_factor[...] = silu


def backward_kernel(
    core, out_grad, factor, other_factor, gate, up, down, rows_grad, gate_grad, up_grad
):
    del core
    hidden_grad = dot(out_grad[...], down[...])
    low = (hidden_grad * factor[...]).astype(bf16)
    other = (hidden_grad * other_factor[...]).astype(bf16)
    gate_grad[...] = low
    up_grad[...] = other
    rows_grad[...] = (dot_t(low, gate[...]) + dot_t(other, up[...])).astype(bf16)


def expert_call(kernel, block, core, arrays, weights, outs):
    count = arrays[0].shape[0]

    def rows(columns):
        return pl.BlockSpec((block, columns), lambda i, core: (i, 0))

    def whole(m):
        return pl.BlockSpec(
            (None, None) + weights.shape[2:],
            lambda i, core: (m, core[0], 0, 0),
            pipeline_mode=pl.Buffered(1),
        )

    return pl.pallas_call(
        kernel,
        out_shape=[jax.ShapeDtypeStruct((count, columns), dtype) for columns, dtype in outs],
        grid_spec=pltpu.PrefetchScalarGridSpec(
            num_scalar_prefetch=1,
            grid=(count // block,),
            in_specs=[rows(a.shape[1]) for a in arrays] + [whole(m) for m in range(3)],
            out_specs=[rows(columns) for columns, _ in outs],
        ),
        compiler_params=pltpu.CompilerParams(vmem_limit_bytes=20 << 20),
        cost_estimate=COST,
    )(core, *arrays, weights, weights, weights)


def weights_kernel(sent, out_grad, hidden, gate_grad, up_grad, sums):
    rows = sent[...]
    sums[0] = t_dot(rows, gate_grad[...]).astype(bf16)
    sums[1] = t_dot(rows, up_grad[...]).astype(bf16)
    sums[2] = t_dot(out_grad[...], hidden[...]).astype(bf16)


def expert_weights_grad(sent, out_grad, hidden, gate_grad, up_grad, block=256):
    count, width = out_grad.shape
    columns = hidden.shape[1]
    part = pl.BlockSpec((count, block), lambda i: (0, i))
    whole = pl.BlockSpec((count, columns), lambda i: (0, 0), pipeline_mode=pl.Buffered(1))
    return pl.pallas_call(
        weights_kernel,
        out_shape=jax.ShapeDtypeStruct((3, width, columns), bf16),
        grid=(width // block,),
        in_specs=[part, part, whole, whole, whole],
        out_specs=pl.BlockSpec((3, block, columns), lambda i: (0, i, 0)),
        compiler_params=pltpu.CompilerParams(vmem_limit_bytes=16 << 20),
        cost_estimate=COST,
    )(sent, out_grad, hidden, gate_grad, up_grad)


def combine_kernel(
    midway, parts, returned, cot, hits, places_of, gates, w_kvs, moe_low, output, moe_part, router_grad
):
    rows = returned[...]
    output[...] = (
        midway[...] + (dot(parts[0], rows) + (dot(parts[1], rows) + dot(parts[2], rows)))
    ).astype(bf16)
    agreement = dot_t(cot[...], rows)
    lane = lax.broadcasted_iota(jnp.int32, gates.shape, 1)
    gate, grad = [], []
    mean = jnp.zeros((gates.shape[0], 1), f32)
    for k in range(TOPK):
        gate.append(jnp.sum(jnp.where(lane == k, gates[...], 0.0), axis=-1, keepdims=True))
        grad.append(jnp.sum(places_of[k].astype(f32) * agreement, axis=-1, keepdims=True))
        mean = mean + gate[k] * grad[k]
    logit_grad = jnp.zeros(gates.shape, f32)
    for k in range(TOPK):
        logit_grad = logit_grad + hits[k].astype(f32) * (gate[k] * (grad[k] - mean))
    logit_grad = logit_grad.astype(bf16)
    moe_part[...] = dot_t(logit_grad, w_kvs[:, WIDE:])
    router_grad[...] = t_dot(moe_low[...], logit_grad)


def home_kernel(placer_t, home, moe_part, midway, cot, gains, midway_grad, branch_low, gain_grad):
    grad = dot(placer_t[...], home[...]) + moe_part[...]
    normal, inverse = normal_of(midway[...])
    result = cot[...].astype(f32) + norm_back(grad, normal, inverse, gains[1:2])
    midway_grad[...] = result
    branch_low[...] = result.astype(bf16)
    gain_grad[...] = jnp.broadcast_to(
        jnp.sum(grad * normal, axis=0, keepdims=True), gain_grad.shape
    )


def out_grad_kernel(mixed, own, other, branch, pieces):
    quarter = own.shape[0] // 2
    branch[:quarter] = own[:quarter]
    branch[quarter : 2 * quarter] = other[:quarter]
    branch[2 * quarter : 3 * quarter] = own[quarter:]
    branch[3 * quarter :] = other[quarter:]
    columns = pieces.shape[2]
    for k in range(2):
        at = slice(k * columns, (k + 1) * columns)
        pieces[k] = t_dot(mixed[...], branch[:, at]).astype(bf16)


def attend_back_kernel(
    branch,
    w_out,
    queries,
    kv_low,
    kv_up,
    logs,
    q_place,
    low_place,
    up_place,
    cosines,
    sines,
    dq,
    dkv,
    grads,
    acc_low,
    acc_up,
    *,
    scale,
    pieces,
    heads,
):
    half = queries.shape[0] // 2
    columns = w_out.shape[2]
    grads[...] = (
        dot_t(branch[:, :columns], w_out[0]) + dot_t(branch[:, columns:], w_out[1])
    ).astype(bf16)
    allowed_low = low_place[...] <= q_place[...]
    allowed_up = up_place[...] <= q_place[half:, :]
    key_low, value_low = kv_low[:, :HD], kv_low[:, HD:]
    key_up, value_up = kv_up[:, :HD], kv_up[:, HD:]
    for h in range(heads):
        at = slice(h * HD, (h + 1) * HD)
        q, grad, log = queries[:, at], grads[:, at], logs[h]
        low = jnp.where(allowed_low, dot_t(q, key_low) * scale, NEGATIVE)
        up = jnp.where(allowed_up, dot_t(q[half:], key_up) * scale, NEGATIVE)
        probs_low, probs_up = jnp.exp(low - log), jnp.exp(up - log[half:])
        grad_low, grad_up = dot_t(grad, value_low), dot_t(grad[half:], value_up)
        along = jnp.sum(probs_low * grad_low, axis=-1, keepdims=True)
        along_up = along[half:] + jnp.sum(probs_up * grad_up, axis=-1, keepdims=True)
        along = jnp.concatenate([along[:half], along_up])
        score_low = (probs_low * (grad_low - along)).astype(bf16)
        score_up = (probs_up * (grad_up - along_up)).astype(bf16)
        part = dot(score_low, key_low)
        part = jnp.concatenate([part[:half], part[half:] + dot(score_up, key_up)]) * scale
        dq[:, at] = turn(part, cosines[...], -sines[...]).astype(bf16)
        terms = (
            (acc_low, slice(0, HD), t_dot(q, score_low)),
            (acc_up, slice(0, HD), t_dot(q[half:], score_up)),
            (acc_low, slice(HD, 2 * HD), t_dot(grad, probs_low.astype(bf16))),
            (acc_up, slice(HD, 2 * HD), t_dot(grad[half:], probs_up.astype(bf16))),
        )
        for acc, rows, term in terms:
            if h == 0:
                acc[rows] = term
            else:
                acc[rows] += term
    for acc, first in ((acc_low, 0), (acc_up, half)):
        dk = (acc[:HD].T * scale).astype(bf16)
        dv = acc[HD:].T.astype(bf16)
        for i in range(pieces):
            dkv[i, first : first + half, :HD] = dk[i * half : (i + 1) * half]
            dkv[i, first : first + half, HD:] = dv[i * half : (i + 1) * half]


def sum_kernel(dq, w_q, w_kvs, cosines, sines, *refs):
    parts, (dkv, own, other) = refs[:-3], refs[-3:]
    total = parts[0][...].astype(f32)
    for part in parts[1:]:
        total = total + part[...].astype(f32)
    dkv[:, :HD] = turn(total[:, :HD], cosines[...], -sines[...]).astype(bf16)
    dkv[:, HD:] = total[:, HD:].astype(bf16)
    grad = dot_t(dq[...], w_q[...]) + dot_t(dkv[...], w_kvs[:, :WIDE])
    quarter = own.shape[0] // 2
    own[:quarter] = grad[:quarter]
    other[:quarter] = grad[quarter : 2 * quarter]
    own[quarter:] = grad[2 * quarter : 3 * quarter]
    other[quarter:] = grad[3 * quarter :]


def input_kernel(
    tokens, own, received, midway_grad, gains, gain_two_grad, router_grad, normed, dkv, out, kvs_grad
):
    grad = own[...] + received[...]
    normal, inverse = normal_of(tokens[...].astype(f32))
    out[...] = midway_grad[...] + norm_back(grad, normal, inverse, gains[0:1])
    gain_grad = jnp.sum(grad * normal, axis=0, keepdims=True)
    row = lax.broadcasted_iota(jnp.int32, gain_two_grad.shape, 0)
    gain_grads = jnp.where(row == 0, gain_grad, jnp.where(row == 1, gain_two_grad[...], 0.0))
    small = router_grad[...] + t_dot(gain_grads.astype(bf16), gain_picker())
    kvs_grad[:, WIDE:] = small.astype(bf16)
    kvs_grad[:, :WIDE] = t_dot(normed[...], dkv[...]).astype(bf16)


def query_grad_kernel(normed, dq, out):
    out[...] = t_dot(normed[...], dq[...]).astype(bf16)


def body(
    tokens,
    cotangent,
    pair_of,
    routes,
    attn_gain,
    moe_gain,
    w_query,
    w_key,
    w_value,
    w_out,
    w_router,
    w_gate,
    w_up,
    w_down,
):
    rows = tokens.shape[1]
    half = rows // 2
    width = tokens.shape[2]
    shard = w_query.shape[1]
    ctx_count = 16
    experts = w_router.shape[2]
    columns = w_gate.shape[3]
    per_group = H // KVH
    qw = per_group * HD
    scale = 1.0 / math.sqrt(HD)
    core = lax.axis_index("core")
    ylo, z, yhi = lax.axis_index("ylo"), lax.axis_index("z"), lax.axis_index("yhi")
    piece_rows = 2 * shard
    slots = experts * SLOTS
    own_tokens, cot = tokens[0], cotangent[0]

    def halves(matrix):
        return [matrix[:, : matrix.shape[1] // 2], matrix[:, matrix.shape[1] // 2 :]]

    small = jnp.concatenate([w_router[0], attn_gain[0][:, None], moe_gain[0][:, None]], axis=-1)
    small = jnp.pad(small, ((0, 0), (0, 128 - experts - 2)))
    query_halves, key_halves, value_halves = halves(w_query[0]), halves(w_key[0]), halves(w_value[0])
    pairs = [
        jnp.concatenate([k, v, small, q], axis=-1)
        for k, v, q in zip(key_halves, value_halves, query_halves)
    ]
    pieces = gather_pieces(pairs, yhi, core, ("core", "yhi"), SAME, OTHER)
    own_tokens, chosen, pair_of, out_halves, pieces = together(
        own_tokens, routes[0, 0], pair_of, w_out[0], pieces
    )

    w_kvs = spread(pieces[:, : 3 * HD], 64, ROWS_ORDER)
    other_tokens = partner(own_tokens)
    both = jnp.concatenate(
        [own_tokens[:half], other_tokens[:half], own_tokens[half:], other_tokens[half:]]
    )
    out_pieces = gather_pieces(
        halves(out_halves), yhi, yhi, ("ylo", "core", "yhi"), OUT_SAME, OUT_OTHER
    )

    def two_cores(ctx):
        return jnp.stack([ctx + core, ctx + 1 - core], axis=-1).reshape(-1)

    ctx_here = (ylo * 4 + z) * 2
    q_place = places(pair_of, two_cores(ctx_here), rows, ctx_count)
    q_place = q_place.transpose(1, 0, 2).reshape(2 * rows, 1)
    ctx_there = jnp.stack([((ylo ^ dy) * 4 + (z - dz) % 4) * 2 for dy, dz in OFFSETS])
    key_place = places(pair_of, two_cores(ctx_there), rows, ctx_count)
    low_place, up_place = key_place[:, 0].reshape(1, -1), key_place[:, 1].reshape(1, -1)
    frequency = jnp.exp(jnp.arange(HD // 2, dtype=f32) * (-2.0 * math.log(ROPE_BASE) / HD))
    angles = q_place.astype(f32) * frequency[None, :]
    cosines, sines = jnp.cos(angles), jnp.sin(angles)
    cosines = jnp.concatenate([cosines, cosines], axis=-1)
    sines = jnp.concatenate([-sines, sines], axis=-1)
    lanes = jnp.arange(128, dtype=jnp.int32)
    hits = (chosen.T[:, :, None] == lanes[None, None, :]).astype(bf16)
    earlier = (lanes[:, None] > lanes[None, :]).astype(bf16)
    before = dot(earlier, jnp.sum(hits, axis=0))
    slot_index = jnp.sum(hits.astype(f32) * before[None], axis=-1).astype(jnp.int32)
    target = chosen.T * SLOTS + slot_index
    slot_row = jnp.arange(slots, dtype=jnp.int32)
    places_of = (target[:, :, None] == slot_row[None, None, :]).astype(bf16)
    placer_t = jnp.sum(places_of, axis=0)
    placer = placer_t.T
    cot_rows = dot(placer, cot).astype(bf16).reshape(experts, SLOTS, width)
    expert_shards_in = jnp.stack([w_gate[0], w_up[0], w_down[0]])
    (
        w_kvs, pieces, both, out_pieces, q_place, low_place, up_place, cosines, sines,
        hits, places_of, placer_t, placer, cot_rows, expert_shards_in,
    ) = together(
        w_kvs, pieces, both, out_pieces, q_place, low_place, up_place, cosines, sines,
        hits, places_of, placer_t, placer, cot_rows, expert_shards_in,
    )

    w_q = spread(pieces[:, 3 * HD :], 64, ROWS_ORDER)
    w_kvs = w_kvs.reshape(width, 3 * HD)
    normed, key_value, gains = call(
        keys_kernel,
        [((2 * rows, width), bf16), ((2 * rows, 2 * HD), bf16), ((8, width), f32)],
        both,
        w_kvs,
        cosines,
        sines,
    )
    pieces_kv = ring_send([key_value] * len(OFFSETS))
    w_q, pieces_kv, normed, gains, out_pieces, expert_shards_in = together(
        w_q, pieces_kv, normed, gains, out_pieces, expert_shards_in
    )

    wo = spread(out_pieces, 64, OUT_ORDER)
    expert_weights = lax.all_gather(expert_shards_in, CTX, axis=2, tiled=True)
    w_q = w_q.reshape(width, qw)
    sizes = dict(scale=scale, pieces=len(OFFSETS), heads=per_group)
    keys = len(OFFSETS) * rows
    queries, mixed, logs, kv_low, kv_up = call(
        functools.partial(attend_kernel, **sizes),
        [
            ((2 * rows, qw), bf16),
            ((2 * rows, qw), bf16),
            ((per_group, 2 * rows, 1), f32),
            ((keys, 2 * HD), bf16),
            ((keys, 2 * HD), bf16),
        ],
        normed,
        w_q,
        cosines,
        sines,
        q_place,
        low_place,
        up_place,
        *pieces_kv,
    )
    wo, mixed, cot_rows = together(wo, mixed, cot_rows)

    arrived_cot = to_owners(cot_rows)
    wo = wo.reshape(2, qw, width // 2)
    branch_own, branch_other = call(
        branch_kernel, [((rows, width), f32), ((rows, width), f32)], mixed, wo
    )
    sent, midway, moe_low, gates, gate_parts = call(
        route_kernel,
        [
            ((slots, width + 128), bf16),
            ((rows, width), f32),
            ((rows, width), bf16),
            ((rows, 128), f32),
            ((3, rows, slots), bf16),
        ],
        own_tokens,
        branch_own,
        partner(branch_other),
        w_kvs,
        gains,
        hits,
        places_of,
        placer,
    )
    arrived_cot, sent = together(arrived_cot, sent)
    sent = to_owners(sent.reshape(experts, SLOTS, width + 128))
    sent = sent.reshape(slots, width + 128)
    mine = core.reshape(1)
    expert_out, hidden, out_grad, factor, other_factor = expert_call(
        forward_kernel,
        128,
        mine,
        [sent, arrived_cot.reshape(slots, width)],
        expert_weights,
        [(width, bf16), (columns, bf16), (width, bf16), (columns, f32), (columns, f32)],
    )
    expert_out, out_grad = together(expert_out, out_grad)

    returned = to_owners(expert_out.reshape(experts, SLOTS, width))
    rows_grad, gate_grad, up_grad = expert_call(
        backward_kernel,
        128,
        mine,
        [out_grad, factor, other_factor],
        expert_weights,
        [(width, bf16), (columns, bf16), (columns, bf16)],
    )
    expert_sums = expert_weights_grad(sent, out_grad, hidden, gate_grad, up_grad)
    returned, rows_grad, expert_sums = together(returned, rows_grad, expert_sums)

    expert_sums = lax.psum_scatter(expert_sums, RING, scatter_dimension=1, tiled=True)
    home_grad = to_owners(rows_grad.reshape(experts, SLOTS, width))
    output, moe_part, router_grad = call(
        combine_kernel,
        [((rows, width), bf16), ((rows, width), f32), ((width, 128), f32)],
        midway,
        gate_parts,
        returned.reshape(slots, width),
        cot,
        hits,
        places_of,
        gates,
        w_kvs,
        moe_low,
    )
    home_grad, output, moe_part, router_grad = together(home_grad, output, moe_part, router_grad)
    midway_grad, branch_low, gain_two_grad = call(
        home_kernel,
        [((rows, width), f32), ((rows, width), bf16), ((8, width), f32)],
        placer_t,
        home_grad.reshape(slots, width),
        moe_part,
        midway,
        cot,
        gains,
    )
    branch, out_w_grad = call(
        out_grad_kernel,
        [((2 * rows, width), bf16), ((2, qw, width // 2), bf16)],
        mixed,
        branch_low,
        partner(branch_low),
    )
    branch, out_w_grad = together(branch, out_w_grad)

    out_w_grad = exchange(out_w_grad.reshape(64, piece_rows, width // 2), OUT_ORDER)
    dq, dkv = call(
        functools.partial(attend_back_kernel, **sizes),
        [((2 * rows, qw), bf16), ((len(OFFSETS), 2 * rows, 2 * HD), bf16)],
        branch,
        wo,
        queries,
        kv_low,
        kv_up,
        logs,
        q_place,
        low_place,
        up_place,
        cosines,
        sines,
        scratch=[
            pltpu.VMEM((2 * rows, qw), bf16),
            pltpu.VMEM((2 * HD, keys), f32),
            pltpu.VMEM((2 * HD, keys), f32),
        ],
    )
    back_order = [OFFSETS.index((dy, (-dz) % 4)) for dy, dz in OFFSETS]
    dkv = ring_send([dkv[i] for i in back_order])
    (q_w_grad,) = call(query_grad_kernel, [((width, qw), bf16)], normed, dq)
    out_w_grad, dkv, q_w_grad = together(out_w_grad, dkv, q_w_grad)

    q_w_grad = exchange(q_w_grad.reshape(64, piece_rows, qw), ROWS_ORDER)
    dkv, normed_own, normed_other = call(
        sum_kernel,
        [((2 * rows, 2 * HD), bf16), ((rows, width), f32), ((rows, width), f32)],
        dq,
        w_q,
        w_kvs,
        cosines,
        sines,
        *dkv,
    )
    input_grad, kvs_grad = call(
        input_kernel,
        [((rows, width), f32), ((width, 3 * HD), bf16)],
        own_tokens,
        normed_own,
        partner(normed_other),
        midway_grad,
        gains,
        gain_two_grad,
        router_grad,
        normed,
        dkv,
    )
    q_w_grad, kvs_grad, input_grad = together(q_w_grad, kvs_grad, input_grad)
    kvs_grad = exchange(kvs_grad.reshape(64, piece_rows, 3 * HD), ROWS_ORDER)

    def summed(pieces):
        return jnp.sum(pieces.astype(f32), axis=0)

    def expert_shards(grad):
        count = grad.shape[1] // 2
        kept = lax.dynamic_slice_in_dim(grad, core * count, count, axis=1)
        given = partner(lax.dynamic_slice_in_dim(grad, (1 - core) * count, count, axis=1))
        both = jnp.stack([pick(core, kept, given), pick(core, given, kept)], axis=1)
        return [both[i : i + 1].astype(f32) for i in range(3)]

    out_w_grad = scatter_pieces(
        summed(out_w_grad), yhi, yhi, ("ylo", "core", "yhi"), OUT_SAME, OUT_OTHER
    )
    q_w_grad = scatter_pieces(summed(q_w_grad), yhi, core, ("core", "yhi"), SAME, OTHER)
    w_gate_grad, w_up_grad, w_down_grad = expert_shards(after(expert_sums, q_w_grad))
    kvs_grad = scatter_pieces(summed(kvs_grad), yhi, core, ("core", "yhi"), SAME, OTHER)
    first_half, second_half = kvs_grad[:, : 3 * HD], kvs_grad[:, 3 * HD :]
    w_key_grad = jnp.concatenate([first_half[:, :HD], second_half[:, :HD]], axis=-1)
    w_value_grad = jnp.concatenate(
        [first_half[:, HD : 2 * HD], second_half[:, HD : 2 * HD]], axis=-1
    )
    small_grad = first_half[:, 2 * HD :] + second_half[:, 2 * HD :]

    return (
        output[None],
        input_grad[None],
        small_grad[None, :, experts],
        small_grad[None, :, experts + 1],
        q_w_grad[None],
        w_key_grad[None],
        w_value_grad[None],
        out_w_grad[None],
        small_grad[None, :, :experts],
        w_gate_grad,
        w_up_grad,
        w_down_grad,
    )


def solution(mesh):
    fine = Mesh(mesh.devices.reshape(2, 4, 2, 4, 2), AXES)
    seq = P(FSDP, CTX, None)
    vector = P(None, AXES)
    matrix = P(None, AXES, None)
    expert = P(None, FSDP, CTX, None)
    in_specs = (
        seq,
        seq,
        P(),
        P(None, FSDP, CTX, None),
        vector,
        vector,
        matrix,
        matrix,
        matrix,
        matrix,
        matrix,
        expert,
        expert,
        expert,
    )
    out_specs = (
        seq,
        seq,
        vector,
        vector,
        matrix,
        matrix,
        matrix,
        matrix,
        matrix,
        expert,
        expert,
        expert,
    )
    return jax.shard_map(body, mesh=fine, in_specs=in_specs, out_specs=out_specs, check_vma=False)
```

```python
import functools
import math

import jax
import jax.numpy as jnp
from jax import lax
from jax.experimental import pallas as pl
from jax.experimental.pallas import tpu as pltpu
from jax.sharding import Mesh
from jax.sharding import PartitionSpec as P

H = 12
KVH = 2
HD = 128
TOPK = 4

EPSILON = 1e-06
ROPE_BASE = 1000000.0
NEGATIVE = -1e30

AXES = ("ylo", "z", "core", "x", "yhi")
CTX = ("ylo", "z", "core")
FSDP = ("x", "yhi")
GROUPS = [
    [
        (((group ^ yhi) * 4 + z) * 2 + core) * 8 + x * 2 + yhi
        for x in range(4)
        for yhi in range(2)
        for core in range(2)
    ]
    for group in range(2)
    for z in range(4)
]
RING = ("ylo", "z")
PLANE = ("ylo", "z", "yhi")
OUT_PLANE = ("yhi", "z", "ylo")
GROUPS = [
    [
        (((group ^ yhi) * 4 + z) * 2 + core) * 8 + x * 2 + yhi
        for x in range(4)
        for yhi in range(2)
        for core in range(2)
    ]
    for group in range(2)
    for z in range(4)
]
RING = ("ylo", "z")
ROWS_ORDER = ("ylo", "z", "yhi", "x")
OUT_ORDER = ("yhi", "z", "ylo", "x")
SLOTS = 40

bf16 = jnp.bfloat16
f32 = jnp.float32


def dot(left, right):
    return jnp.dot(left, right, preferred_element_type=f32)


def dot_t(left, right):
    return lax.dot_general(left, right, (((1,), (1,)), ((), ())), preferred_element_type=f32)


def t_dot(left, right):
    return lax.dot_general(left, right, (((0,), (0,)), ((), ())), preferred_element_type=f32)


def exchange(pieces, axes):
    return lax.all_to_all(pieces, axes, split_axis=0, concat_axis=0, tiled=True)


def to_owners(pieces):
    return lax.all_to_all(
        pieces, AXES, split_axis=0, concat_axis=0, axis_index_groups=GROUPS, tiled=True
    )


def spread(piece, count, axes):
    return exchange(jnp.broadcast_to(piece[None], (count,) + piece.shape), axes)


def after(value, earlier):
    return lax.optimization_barrier((value, earlier))[0]


def together(*values):
    return lax.optimization_barrier(values)


def partner(value):
    return lax.ppermute(value, "core", [(0, 1), (1, 0)])


def route(axes, sizes, move):
    pairs = []
    for source in range(math.prod(sizes)):
        rest, at = source, []
        for size in reversed(sizes):
            at.insert(0, rest % size)
            rest //= size
        target = 0
        for size, value in zip(sizes, move(*at)):
            target = target * size + value
        pairs.append((source, target))
    return pairs


SAME = route(("core", "yhi"), (2, 2), lambda c, h: (h, c))
OTHER = route(("core", "yhi"), (2, 2), lambda c, h: (1 - h, c))
OUT_SAME = route(("ylo", "core", "yhi"), (2, 2, 2), lambda j, c, h: (c, j, h))
OUT_OTHER = route(("ylo", "core", "yhi"), (2, 2, 2), lambda j, c, h: (c, j, 1 - h))


def back(pairs):
    return [(target, source) for source, target in pairs]


def pick(flag, if_zero, if_one):
    return jnp.where(flag == 0, if_zero, if_one)


def gather_pieces(pair, flag, key, axes, same, other):
    first = lax.ppermute(pick(flag, pair[0], pair[1]), axes, same)
    second = lax.ppermute(pick(flag, pair[1], pair[0]), axes, other)
    return pick(
        key, jnp.concatenate([first, second]), jnp.concatenate([second, first])
    )


def scatter_pieces(piece, flag, key, axes, same, other):
    count = piece.shape[0] // 2
    mine, rest = piece[:count], piece[count:]
    first = lax.ppermute(pick(key, mine, rest), axes, back(same))
    second = lax.ppermute(pick(key, rest, mine), axes, back(other))
    return pick(flag, jnp.concatenate([first, second], axis=-1), jnp.concatenate([second, first], axis=-1))


def along_x(piece):
    return [piece] + [
        lax.ppermute(piece, "x", [(i, (i + s) % 4) for i in range(4)]) for s in (1, 2, 3)
    ]


def back_along_x(blocks):
    arrived = [blocks[0]] + [
        lax.ppermute(blocks[s], "x", [(i, (i - s) % 4) for i in range(4)]) for s in (1, 2, 3)
    ]
    return sum(block.astype(f32) for block in arrived).astype(bf16)


def order_matrix(groups, x):
    index = jnp.arange(groups * 96, dtype=jnp.int32)
    turn_of, group, row = index // (groups * 24), index // 24 % groups, index % 24
    own = group * 96 + (x - turn_of) % 4 * 24 + row
    return (index[:, None] == own[None, :]).astype(bf16)


OFFSETS = [(dy, dz) for dy in (0, 1) for dz in (0, 1, 3, 2)]


def ring_send(pieces):
    arrived = [pieces[0]]
    for (dy, dz), piece in zip(OFFSETS[1:], pieces[1:]):
        pairs = route(RING, (2, 4), lambda y, z: (y ^ dy, (z + dz) % 4))
        arrived.append(lax.ppermute(piece, RING, pairs))
    return arrived


def places(pair_of, ctx, row_count, ctx_count):
    half_size = row_count // 2
    pair = jnp.sum(
        jnp.where(ctx[:, None] == jnp.arange(ctx_count, dtype=jnp.int32)[None], pair_of[None], 0),
        axis=1,
    )
    block = jnp.stack([pair, 2 * ctx_count - 1 - pair], axis=1)
    return block[:, :, None] * half_size + jnp.arange(half_size, dtype=jnp.int32)[None, None]


def in_three(value):
    high = value.astype(bf16)
    rest = value - high.astype(f32)
    middle = rest.astype(bf16)
    return [high, middle, (rest - middle.astype(f32)).astype(bf16)]


def call(kernel, outs, *args, scratch=(), megabytes=12, wait=()):
    whole = pl.BlockSpec(memory_space=pltpu.VMEM)
    count = len(args)

    def body(*refs):
        kernel(*refs[:count], *refs[count + len(wait) :])

    return pl.pallas_call(
        body,
        out_shape=[jax.ShapeDtypeStruct(shape, dtype) for shape, dtype in outs],
        in_specs=[whole] * count + [pl.BlockSpec(memory_space=pl.ANY)] * len(wait),
        out_specs=[whole] * len(outs),
        scratch_shapes=list(scratch),
        compiler_params=pltpu.CompilerParams(vmem_limit_bytes=megabytes << 20),
        cost_estimate=COST,
    )(*args, *wait)


def gate(value, *wait):
    anywhere = pl.BlockSpec(memory_space=pl.ANY)

    def body(*refs):
        del refs

    return pl.pallas_call(
        body,
        out_shape=jax.ShapeDtypeStruct(value.shape, value.dtype),
        in_specs=[anywhere] * (1 + len(wait)),
        out_specs=anywhere,
        input_output_aliases={0: 0},
        cost_estimate=COST,
    )(value, *wait)


COST = pl.CostEstimate(flops=1 << 20, bytes_accessed=1 << 18, transcendentals=0)
WIDE = 2 * HD
EXPERTS = 16


def turn(vectors, cosines, sines):
    return vectors * cosines + pltpu.roll(vectors, HD // 2, axis=1) * sines


def gain_picker():
    row = lax.broadcasted_iota(jnp.int32, (8, 128), 0)
    column = lax.broadcasted_iota(jnp.int32, (8, 128), 1)
    return jnp.where((column == row + EXPERTS) & (row < 2), 1.0, 0.0).astype(bf16)


def normal_of(stream):
    inverse = lax.rsqrt(jnp.mean(stream * stream, axis=-1, keepdims=True) + EPSILON)
    return stream * inverse, inverse


def norm_back(grad, normal, inverse, gain):
    scaled = grad * gain
    return inverse * (scaled - normal * jnp.mean(scaled * normal, axis=-1, keepdims=True))


def column_block(s, count):
    return slice(s * count, (s + 1) * count)


def order_kernel(rows, order, out):
    out[...] = dot(rows[...], order[...]).astype(bf16)


def keys_kernel(both, cosines, sines, *refs):
    kvs, (normed, key_value, gains) = refs[:4], refs[4:]
    count = kvs[0].shape[0]
    for s in range(4):
        gains[:, column_block(s, count)] = dot_t(gain_picker(), kvs[s][:, WIDE:])
    normal, _ = normal_of(both[...].astype(f32))
    normed[...] = (normal * gains[0:1]).astype(bf16)
    kv = dot(normed[:, column_block(0, count)], kvs[0][:, :WIDE])
    for s in range(1, 4):
        kv = kv + dot(normed[:, column_block(s, count)], kvs[s][:, :WIDE])
    key_value[:, :HD] = turn(kv[:, :HD], cosines[...], sines[...]).astype(bf16)
    key_value[:, HD:] = kv[:, HD:].astype(bf16)


def small_kernel(order, kvs0, kvs1, kvs2, kvs3, small, gains):
    count = kvs0.shape[0]
    total = jnp.zeros(small.shape, f32)
    for s, kvs in enumerate((kvs0, kvs1, kvs2, kvs3)):
        total = total + dot(order[:, column_block(s, count)], kvs[:, WIDE:])
    small[...] = total.astype(bf16)
    gains[...] = dot_t(gain_picker(), small[...])


def attend_kernel(
    normed, cosines, sines, q_place, low_place, up_place, order, *refs, scale, pieces, heads
):
    w_q, kv, (queries, ordered, logs, kv_low, kv_up, mixed) = refs[:4], refs[4:-6], refs[-6:]
    count = w_q[0].shape[0]
    half = kv[0].shape[0] // 2
    for i in range(pieces):
        kv_low[i * half : (i + 1) * half, :] = kv[i][:half, :]
        kv_up[i * half : (i + 1) * half, :] = kv[i][half:, :]
    allowed_low = low_place[...] <= q_place[...]
    allowed_up = up_place[...] <= q_place[half:, :]
    for h in range(heads):
        at = slice(h * HD, (h + 1) * HD)
        q = dot(normed[:, column_block(0, count)], w_q[0][:, at])
        for s in range(1, 4):
            q = q + dot(normed[:, column_block(s, count)], w_q[s][:, at])
        q = turn(q, cosines[...], sines[...]).astype(bf16)
        queries[:, at] = q
        low = jnp.where(allowed_low, dot_t(q, kv_low[:, :HD]) * scale, NEGATIVE)
        up = jnp.where(allowed_up, dot_t(q[half:], kv_up[:, :HD]) * scale, NEGATIVE)
        first, second = low[:half], low[half:]
        top = jnp.max(first, axis=-1, keepdims=True)
        weight = jnp.exp(first - top)
        total = jnp.sum(weight, axis=-1, keepdims=True)
        probs = (weight / total).astype(bf16)
        mixed[:half, at] = dot(probs, kv_low[:, HD:]).astype(bf16)
        logs[h, :half, :] = top + jnp.log(total)
        top = jnp.maximum(
            jnp.max(second, axis=-1, keepdims=True), jnp.max(up, axis=-1, keepdims=True)
        )
        weight, weight_up = jnp.exp(second - top), jnp.exp(up - top)
        total = jnp.sum(weight, axis=-1, keepdims=True) + jnp.sum(
            weight_up, axis=-1, keepdims=True
        )
        mixed[half:, at] = (
            dot((weight / total).astype(bf16), kv_low[:, HD:])
            + dot((weight_up / total).astype(bf16), kv_up[:, HD:])
        ).astype(bf16)
        logs[h, half:, :] = top + jnp.log(total)
    ordered[...] = dot(mixed[...], order[...]).astype(bf16)


def branch_kernel(mixed, w_out0, w_out1, w_out2, w_out3, own, other, w_out):
    quarter = mixed.shape[0] // 4
    count, columns = w_out0.shape[1:]
    for s, part in enumerate((w_out0, w_out1, w_out2, w_out3)):
        w_out[:, column_block(s, count)] = part[...]
    for k in range(2):
        part = dot(mixed[...], w_out[k])
        at = slice(k * columns, (k + 1) * columns)
        own[:quarter, at] = part[:quarter]
        other[:quarter, at] = part[quarter : 2 * quarter]
        own[quarter:, at] = part[2 * quarter : 3 * quarter]
        other[quarter:, at] = part[3 * quarter :]


def route_kernel(
    tokens, own, received, small, gains, hits, places_of, placer, sent, midway, moe_low, gates, parts
):
    middle = tokens[...].astype(f32) + (own[...] + received[...])
    midway[...] = middle
    normal, _ = normal_of(middle)
    moe = (normal * gains[1:2]).astype(bf16)
    moe_low[...] = moe
    sent[:, : moe.shape[1]] = dot(placer[...], moe).astype(bf16)
    logits = dot(moe, small[...])
    picked = [
        jnp.sum(hits[k].astype(f32) * logits, axis=-1, keepdims=True) for k in range(TOPK)
    ]
    top = picked[0]
    for value in picked[1:]:
        top = jnp.maximum(top, value)
    weights = [jnp.exp(value - top) for value in picked]
    total = weights[0]
    for value in weights[1:]:
        total = total + value
    lane = lax.broadcasted_iota(jnp.int32, gates.shape, 1)
    gate_at = jnp.zeros(places_of.shape[1:], f32)
    kept = jnp.zeros(gates.shape, f32)
    for k in range(TOPK):
        gate = weights[k] / total
        kept = jnp.where(lane == k, gate, kept)
        gate_at = gate_at + places_of[k].astype(f32) * gate
    gates[...] = kept
    block = jnp.zeros((sent.shape[0], 128), f32)
    for i, part in enumerate(in_three(gate_at)):
        parts[i] = part
        block = block + t_dot(part, jnp.where(lane == i, 1.0, 0.0).astype(bf16))
    sent[:, moe.shape[1] :] = block.astype(bf16)


def fetched(core, weights, held, sems, first):
    copies = [
        pltpu.make_async_copy(weights.at[m, core[0]], held.at[m], sems.at[m]) for m in range(3)
    ]

    @pl.when(pl.program_id(0) == 0)
    def _():
        for m in first:
            copies[m].start()

    def ready(m):
        @pl.when(pl.program_id(0) == 0)
        def _():
            copies[m].wait()

        return held[m]

    return ready


def forward_kernel(
    core, sent, cot, weights, out, hidden, out_grad, factor, other_factor, held, sems
):
    ready = fetched(core, weights, held, sems, (0, 1, 2))
    width = out.shape[1]
    rows = sent[:, :width]
    gate_pre, up_pre = dot(rows, ready(0)), dot(rows, ready(1))
    sigmoid = 1.0 / (1.0 + jnp.exp(-gate_pre))
    silu = gate_pre * sigmoid
    low = (silu * up_pre).astype(bf16)
    hidden[...] = low
    out[...] = dot_t(low, ready(2)).astype(bf16)
    gates = jnp.sum(sent[:, width:].astype(f32), axis=-1, keepdims=True)
    out_grad[...] = (gates * cot[...].astype(f32)).astype(bf16)
    factor[...] = up_pre * sigmoid * (1.0 + gate_pre * (1.0 - sigmoid))
    other_factor[...] = silu


def backward_kernel(
    core, out_grad, factor, other_factor, weights, rows_grad, gate_grad, up_grad, held, sems
):
    ready = fetched(core, weights, held, sems, (2, 0, 1))
    hidden_grad = dot(out_grad[...], ready(2))
    low = (hidden_grad * factor[...]).astype(bf16)
    other = (hidden_grad * other_factor[...]).astype(bf16)
    gate_grad[...] = low
    up_grad[...] = other
    rows_grad[...] = (dot_t(low, ready(0)) + dot_t(other, ready(1))).astype(bf16)


def expert_call(kernel, block, core, arrays, weights, outs):
    count = arrays[0].shape[0]

    def rows(columns):
        return pl.BlockSpec((block, columns), lambda i, core: (i, 0))

    return pl.pallas_call(
        kernel,
        out_shape=[jax.ShapeDtypeStruct((count, columns), dtype) for columns, dtype in outs],
        grid_spec=pltpu.PrefetchScalarGridSpec(
            num_scalar_prefetch=1,
            grid=(count // block,),
            in_specs=[rows(a.shape[1]) for a in arrays] + [pl.BlockSpec(memory_space=pltpu.HBM)],
            out_specs=[rows(columns) for columns, _ in outs],
            scratch_shapes=[
                pltpu.VMEM((3,) + weights.shape[2:], bf16),
                pltpu.SemaphoreType.DMA((3,)),
            ],
        ),
        compiler_params=pltpu.CompilerParams(vmem_limit_bytes=20 << 20),
        cost_estimate=COST,
    )(core, *arrays, weights)


def weights_kernel(sent, out_grad, hidden, gate_grad, up_grad, sums):
    rows = sent[...]
    sums[0] = t_dot(rows, gate_grad[...]).astype(bf16)
    sums[1] = t_dot(rows, up_grad[...]).astype(bf16)
    sums[2] = t_dot(out_grad[...], hidden[...]).astype(bf16)


def expert_weights_grad(sent, out_grad, hidden, gate_grad, up_grad, block=256):
    count, width = out_grad.shape
    columns = hidden.shape[1]
    part = pl.BlockSpec((count, block), lambda i: (0, i))
    whole = pl.BlockSpec((count, columns), lambda i: (0, 0), pipeline_mode=pl.Buffered(1))
    return pl.pallas_call(
        weights_kernel,
        out_shape=jax.ShapeDtypeStruct((3, width, columns), bf16),
        grid=(width // block,),
        in_specs=[part, part, whole, whole, whole],
        out_specs=pl.BlockSpec((3, block, columns), lambda i: (0, i, 0)),
        compiler_params=pltpu.CompilerParams(vmem_limit_bytes=16 << 20),
        cost_estimate=COST,
    )(sent, out_grad, hidden, gate_grad, up_grad)


def combine_kernel(
    midway, parts, returned, cot, hits, places_of, gates, small, moe_low, output, moe_part, router_grad
):
    rows = returned[...]
    output[...] = (
        midway[...] + (dot(parts[0], rows) + (dot(parts[1], rows) + dot(parts[2], rows)))
    ).astype(bf16)
    agreement = dot_t(cot[...], rows)
    lane = lax.broadcasted_iota(jnp.int32, gates.shape, 1)
    gate, grad = [], []
    mean = jnp.zeros((gates.shape[0], 1), f32)
    for k in range(TOPK):
        gate.append(jnp.sum(jnp.where(lane == k, gates[...], 0.0), axis=-1, keepdims=True))
        grad.append(jnp.sum(places_of[k].astype(f32) * agreement, axis=-1, keepdims=True))
        mean = mean + gate[k] * grad[k]
    logit_grad = jnp.zeros(gates.shape, f32)
    for k in range(TOPK):
        logit_grad = logit_grad + hits[k].astype(f32) * (gate[k] * (grad[k] - mean))
    logit_grad = logit_grad.astype(bf16)
    moe_part[...] = dot_t(logit_grad, small[...])
    router_grad[...] = t_dot(moe_low[...], logit_grad)


def home_kernel(placer_t, home, moe_part, midway, cot, gains, midway_grad, branch_low, gain_grad):
    grad = dot(placer_t[...], home[...]) + moe_part[...]
    normal, inverse = normal_of(midway[...])
    result = cot[...].astype(f32) + norm_back(grad, normal, inverse, gains[1:2])
    midway_grad[...] = result
    branch_low[...] = result.astype(bf16)
    gain_grad[...] = jnp.broadcast_to(
        jnp.sum(grad * normal, axis=0, keepdims=True), gain_grad.shape
    )


def out_grad_kernel(mixed, own, other, branch, *blocks):
    quarter = own.shape[0] // 2
    branch[:quarter] = own[:quarter]
    branch[quarter : 2 * quarter] = other[:quarter]
    branch[2 * quarter : 3 * quarter] = own[quarter:]
    branch[3 * quarter :] = other[quarter:]
    count, columns = blocks[0].shape[1:]
    for k in range(2):
        grad = t_dot(mixed[...], branch[:, column_block(k, columns)]).astype(bf16)
        for s in range(4):
            blocks[s][k] = grad[column_block(s, count)]


def attend_back_kernel(
    branch,
    w_out,
    order,
    queries,
    kv_low,
    kv_up,
    logs,
    q_place,
    low_place,
    up_place,
    cosines,
    sines,
    dq,
    dkv,
    grads,
    acc_low,
    acc_up,
    *,
    scale,
    pieces,
    heads,
):
    half = queries.shape[0] // 2
    columns = w_out.shape[2]
    ordered = dot_t(branch[:, :columns], w_out[0]) + dot_t(branch[:, columns:], w_out[1])
    grads[...] = dot_t(ordered.astype(bf16), order[...]).astype(bf16)
    allowed_low = low_place[...] <= q_place[...]
    allowed_up = up_place[...] <= q_place[half:, :]
    key_low, value_low = kv_low[:, :HD], kv_low[:, HD:]
    key_up, value_up = kv_up[:, :HD], kv_up[:, HD:]
    for h in range(heads):
        at = slice(h * HD, (h + 1) * HD)
        q, grad, log = queries[:, at], grads[:, at], logs[h]
        low = jnp.where(allowed_low, dot_t(q, key_low) * scale, NEGATIVE)
        up = jnp.where(allowed_up, dot_t(q[half:], key_up) * scale, NEGATIVE)
        probs_low, probs_up = jnp.exp(low - log), jnp.exp(up - log[half:])
        grad_low, grad_up = dot_t(grad, value_low), dot_t(grad[half:], value_up)
        along = jnp.sum(probs_low * grad_low, axis=-1, keepdims=True)
        along_up = along[half:] + jnp.sum(probs_up * grad_up, axis=-1, keepdims=True)
        along = jnp.concatenate([along[:half], along_up])
        score_low = (probs_low * (grad_low - along)).astype(bf16)
        score_up = (probs_up * (grad_up - along_up)).astype(bf16)
        part = dot(score_low, key_low)
        part = jnp.concatenate([part[:half], part[half:] + dot(score_up, key_up)]) * scale
        dq[:, at] = turn(part, cosines[...], -sines[...]).astype(bf16)
        terms = (
            (acc_low, slice(0, HD), t_dot(q, score_low)),
            (acc_up, slice(0, HD), t_dot(q[half:], score_up)),
            (acc_low, slice(HD, 2 * HD), t_dot(grad, probs_low.astype(bf16))),
            (acc_up, slice(HD, 2 * HD), t_dot(grad[half:], probs_up.astype(bf16))),
        )
        for acc, rows, term in terms:
            if h == 0:
                acc[rows] = term
            else:
                acc[rows] += term
    for acc, first in ((acc_low, 0), (acc_up, half)):
        dk = (acc[:HD].T * scale).astype(bf16)
        dv = acc[HD:].T.astype(bf16)
        for i in range(pieces):
            dkv[i, first : first + half, :HD] = dk[i * half : (i + 1) * half]
            dkv[i, first : first + half, HD:] = dv[i * half : (i + 1) * half]


def sum_kernel(dq, cosines, sines, *refs):
    w_q, kvs, parts, (dkv, own, other) = refs[:4], refs[4:8], refs[8:-3], refs[-3:]
    total = parts[0][...].astype(f32)
    for part in parts[1:]:
        total = total + part[...].astype(f32)
    dkv[:, :HD] = turn(total[:, :HD], cosines[...], -sines[...]).astype(bf16)
    dkv[:, HD:] = total[:, HD:].astype(bf16)
    quarter = own.shape[0] // 2
    for s in range(4):
        grad = dot_t(dq[...], w_q[s][...]) + dot_t(dkv[...], kvs[s][:, :WIDE])
        at = column_block(s, w_q[s].shape[0])
        own[:quarter, at] = grad[:quarter]
        other[:quarter, at] = grad[quarter : 2 * quarter]
        own[quarter:, at] = grad[2 * quarter : 3 * quarter]
        other[quarter:, at] = grad[3 * quarter :]


def small_grad_kernel(order, router_grad, gain_grad, out):
    row = lax.broadcasted_iota(jnp.int32, gain_grad.shape, 0)
    second = jnp.where(row == 1, gain_grad[...], 0.0).astype(bf16)
    small = router_grad[...] + t_dot(second, gain_picker())
    out[...] = t_dot(order[...], small.astype(bf16))


def input_kernel(both, own, received, midway_grad, gains, order, small, normed, dkv, out, *blocks):
    grad = own[...] + received[...]
    quarter = own.shape[0] // 2
    tokens = jnp.concatenate([both[:quarter], both[2 * quarter : 3 * quarter]])
    normal, inverse = normal_of(tokens.astype(f32))
    parts = in_three(norm_back(grad, normal, inverse, gains[0:1]))
    moved = dot_t(jnp.concatenate(parts), order[...])
    count = 2 * quarter
    out[...] = midway_grad[...] + (
        moved[:count] + (moved[count : 2 * count] + moved[2 * count :])
    )
    gain_grad = jnp.sum(grad * normal, axis=0, keepdims=True)
    row = lax.broadcasted_iota(jnp.int32, gains.shape, 0)
    gain_grad = jnp.where(row == 0, gain_grad, 0.0).astype(bf16)
    small = small[...] + t_dot(gain_grad, gain_picker())
    rows = blocks[0].shape[0]
    for s, block in enumerate(blocks):
        at = column_block(s, rows)
        block[:, :WIDE] = t_dot(normed[:, at], dkv[...]).astype(bf16)
        block[:, WIDE:] = small[at].astype(bf16)


def query_grad_kernel(normed, dq, *blocks):
    for s, block in enumerate(blocks):
        block[...] = t_dot(normed[:, column_block(s, block.shape[0])], dq[...]).astype(bf16)


def body(
    tokens,
    cotangent,
    pair_of,
    routes,
    attn_gain,
    moe_gain,
    w_query,
    w_key,
    w_value,
    w_out,
    w_router,
    w_gate,
    w_up,
    w_down,
):
    rows = tokens.shape[1]
    half = rows // 2
    width = tokens.shape[2]
    shard = w_query.shape[1]
    ctx_count = 16
    experts = w_router.shape[2]
    columns = w_gate.shape[3]
    per_group = H // KVH
    qw = per_group * HD
    scale = 1.0 / math.sqrt(HD)
    core = lax.axis_index("core")
    ylo, z, yhi = lax.axis_index("ylo"), lax.axis_index("z"), lax.axis_index("yhi")
    x = lax.axis_index("x")
    piece_rows = 2 * shard
    slots = experts * SLOTS
    own_tokens, cot = tokens[0], cotangent[0]

    def halves(matrix):
        return [matrix[:, : matrix.shape[1] // 2], matrix[:, matrix.shape[1] // 2 :]]

    small = jnp.concatenate([w_router[0], attn_gain[0][:, None], moe_gain[0][:, None]], axis=-1)
    small = jnp.pad(small, ((0, 0), (0, 128 - experts - 2)))
    query_halves, key_halves, value_halves = halves(w_query[0]), halves(w_key[0]), halves(w_value[0])
    pairs = [
        jnp.concatenate([k, v, small, q], axis=-1)
        for k, v, q in zip(key_halves, value_halves, query_halves)
    ]
    pieces = gather_pieces(pairs, yhi, core, ("core", "yhi"), SAME, OTHER)
    own_tokens, chosen, pair_of, out_halves, pieces = together(
        own_tokens, routes[0, 0], pair_of, w_out[0], pieces
    )

    plane_rows = 16 * piece_rows
    plane = spread(pieces, 16, PLANE).reshape(plane_rows, -1)
    w_kvs = along_x(plane[:, : 3 * HD])
    w_q = along_x(plane[:, 3 * HD :])
    other_tokens = partner(own_tokens)
    both = jnp.concatenate(
        [own_tokens[:half], other_tokens[:half], own_tokens[half:], other_tokens[half:]]
    )
    out_pieces = gather_pieces(
        halves(out_halves), yhi, yhi, ("ylo", "core", "yhi"), OUT_SAME, OUT_OTHER
    )

    def two_cores(ctx):
        return jnp.stack([ctx + core, ctx + 1 - core], axis=-1).reshape(-1)

    ctx_here = (ylo * 4 + z) * 2
    q_place = places(pair_of, two_cores(ctx_here), rows, ctx_count)
    q_place = q_place.transpose(1, 0, 2).reshape(2 * rows, 1)
    ctx_there = jnp.stack([((ylo ^ dy) * 4 + (z - dz) % 4) * 2 for dy, dz in OFFSETS])
    key_place = places(pair_of, two_cores(ctx_there), rows, ctx_count)
    low_place, up_place = key_place[:, 0].reshape(1, -1), key_place[:, 1].reshape(1, -1)
    frequency = jnp.exp(jnp.arange(HD // 2, dtype=f32) * (-2.0 * math.log(ROPE_BASE) / HD))
    angles = q_place.astype(f32) * frequency[None, :]
    cosines, sines = jnp.cos(angles), jnp.sin(angles)
    cosines = jnp.concatenate([cosines, cosines], axis=-1)
    sines = jnp.concatenate([-sines, sines], axis=-1)
    lanes = jnp.arange(128, dtype=jnp.int32)
    hits = (chosen.T[:, :, None] == lanes[None, None, :]).astype(bf16)
    earlier = (lanes[:, None] > lanes[None, :]).astype(bf16)
    before = dot(earlier, jnp.sum(hits, axis=0))
    slot_index = jnp.sum(hits.astype(f32) * before[None], axis=-1).astype(jnp.int32)
    target = chosen.T * SLOTS + slot_index
    slot_row = jnp.arange(slots, dtype=jnp.int32)
    places_of = (target[:, :, None] == slot_row[None, None, :]).astype(bf16)
    placer_t = jnp.sum(places_of, axis=0)
    placer = placer_t.T
    order, out_order = order_matrix(16, x), order_matrix(8, x)
    (both,) = call(order_kernel, [((2 * rows, width), bf16)], both, order)

    normed, key_value, gains = call(
        keys_kernel,
        [((2 * rows, width), bf16), ((2 * rows, 2 * HD), bf16), ((8, width), f32)],
        both,
        cosines,
        sines,
        *w_kvs,
    )
    pieces_kv = ring_send([key_value] * len(OFFSETS))

    out_pieces = after(out_pieces, plane[:8, :128])
    wo = along_x(spread(out_pieces, 16, OUT_PLANE).reshape(2, qw // 4, width // 2))
    expert_weights = lax.all_gather(
        after(jnp.stack([w_gate[0], w_up[0], w_down[0]]), plane[:8, :128]),
        CTX,
        axis=2,
        tiled=True,
    )

    sizes = dict(scale=scale, pieces=len(OFFSETS), heads=per_group)
    keys = len(OFFSETS) * rows
    queries, mixed, logs, kv_low, kv_up = call(
        functools.partial(attend_kernel, **sizes),
        [
            ((2 * rows, qw), bf16),
            ((2 * rows, qw), bf16),
            ((per_group, 2 * rows, 1), f32),
            ((keys, 2 * HD), bf16),
            ((keys, 2 * HD), bf16),
        ],
        normed,
        cosines,
        sines,
        q_place,
        low_place,
        up_place,
        out_order,
        *w_q,
        *pieces_kv,
        scratch=[pltpu.VMEM((2 * rows, qw), bf16)],
    )

    (cot_rows,) = call(order_kernel, [((slots, width), bf16)], placer, cot, wait=[mixed])
    arrived_cot = to_owners(cot_rows.reshape(experts, SLOTS, width))
    small, moe_gains = call(
        small_kernel, [((width, 128), bf16), ((8, width), f32)], order, *w_kvs, wait=[mixed]
    )
    branch_own, branch_other, wo = call(
        branch_kernel,
        [((rows, width), f32), ((rows, width), f32), ((2, qw, width // 2), bf16)],
        mixed,
        *wo,
    )
    sent, midway, moe_low, gates, gate_parts = call(
        route_kernel,
        [
            ((slots, width + 128), bf16),
            ((rows, width), f32),
            ((rows, width), bf16),
            ((rows, 128), f32),
            ((3, rows, slots), bf16),
        ],
        own_tokens,
        branch_own,
        partner(branch_other),
        small,
        moe_gains,
        hits,
        places_of,
        placer,
    )
    sent = gate(sent, arrived_cot)
    sent = to_owners(sent.reshape(experts, SLOTS, width + 128)).reshape(slots, width + 128)
    mine = core.reshape(1)
    expert_out, hidden, out_grad, factor, other_factor = expert_call(
        forward_kernel,
        128,
        mine,
        [sent, arrived_cot.reshape(slots, width)],
        expert_weights,
        [(width, bf16), (columns, bf16), (width, bf16), (columns, f32), (columns, f32)],
    )

    returned = to_owners(expert_out.reshape(experts, SLOTS, width))
    rows_grad, gate_grad, up_grad = expert_call(
        backward_kernel,
        128,
        mine,
        [out_grad, factor, other_factor],
        expert_weights,
        [(width, bf16), (columns, bf16), (columns, bf16)],
    )
    expert_sums = expert_weights_grad(sent, out_grad, hidden, gate_grad, up_grad)
    rows_grad, expert_sums = gate(rows_grad, returned), gate(expert_sums, returned)
    home_grad = to_owners(rows_grad.reshape(experts, SLOTS, width))
    expert_sums = lax.psum_scatter(expert_sums, RING, scatter_dimension=1, tiled=True)
    output, moe_part, router_grad = call(
        combine_kernel,
        [((rows, width), bf16), ((rows, width), f32), ((width, 128), f32)],
        midway,
        gate_parts,
        returned.reshape(slots, width),
        cot,
        hits,
        places_of,
        gates,
        small,
        moe_low,
    )
    midway_grad, branch_low, gain_two_grad = call(
        home_kernel,
        [((rows, width), f32), ((rows, width), bf16), ((8, width), f32)],
        placer_t,
        home_grad.reshape(slots, width),
        moe_part,
        midway,
        cot,
        moe_gains,
    )
    branch, *out_w_grad = call(
        out_grad_kernel,
        [((2 * rows, width), bf16)] + [((2, qw // 4, width // 2), bf16)] * 4,
        mixed,
        branch_low,
        partner(branch_low),
    )
    out_w_grad = back_along_x(out_w_grad)

    dq, dkv = call(
        functools.partial(attend_back_kernel, **sizes),
        [((2 * rows, qw), bf16), ((len(OFFSETS), 2 * rows, 2 * HD), bf16)],
        branch,
        wo,
        out_order,
        queries,
        kv_low,
        kv_up,
        logs,
        q_place,
        low_place,
        up_place,
        cosines,
        sines,
        scratch=[
            pltpu.VMEM((2 * rows, qw), bf16),
            pltpu.VMEM((2 * HD, keys), f32),
            pltpu.VMEM((2 * HD, keys), f32),
        ],
        megabytes=16,
    )
    back_order = [OFFSETS.index((dy, (-dz) % 4)) for dy, dz in OFFSETS]
    dkv = ring_send([dkv[i] for i in back_order])
    q_w_grad = back_along_x(call(query_grad_kernel, [((plane_rows, qw), bf16)] * 4, normed, dq))
    dkv, normed_own, normed_other = call(
        sum_kernel,
        [((2 * rows, 2 * HD), bf16), ((rows, width), f32), ((rows, width), f32)],
        dq,
        cosines,
        sines,
        *w_q,
        *w_kvs,
        *dkv,
        wait=[out_w_grad],
    )
    out_w_grad = exchange(out_w_grad.reshape(16, piece_rows, width // 2), OUT_PLANE)
    (small_grad,) = call(
        small_grad_kernel, [((width, 128), f32)], order, router_grad, gain_two_grad, wait=[dq]
    )
    input_grad, *kvs_grad = call(
        input_kernel,
        [((rows, width), f32)] + [((plane_rows, 3 * HD), bf16)] * 4,
        both,
        normed_own,
        partner(normed_other),
        midway_grad,
        gains,
        order,
        small_grad,
        normed,
        dkv,
    )
    kvs_grad = back_along_x(kvs_grad)
    plane_grad = jnp.concatenate([q_w_grad, kvs_grad], axis=-1)
    plane_grad = exchange(plane_grad.reshape(16, piece_rows, qw + 3 * HD), PLANE)

    def summed(pieces):
        return jnp.sum(pieces.astype(f32), axis=0)

    def expert_shards(grad):
        count = grad.shape[1] // 2
        kept = lax.dynamic_slice_in_dim(grad, core * count, count, axis=1)
        given = partner(lax.dynamic_slice_in_dim(grad, (1 - core) * count, count, axis=1))
        both = jnp.stack([pick(core, kept, given), pick(core, given, kept)], axis=1)
        return [both[i : i + 1].astype(f32) for i in range(3)]

    out_w_grad = scatter_pieces(
        summed(out_w_grad), yhi, yhi, ("ylo", "core", "yhi"), OUT_SAME, OUT_OTHER
    )
    w_gate_grad, w_up_grad, w_down_grad = expert_shards(expert_sums)
    plane_grad = scatter_pieces(summed(plane_grad), yhi, core, ("core", "yhi"), SAME, OTHER)
    plane_grad = plane_grad.reshape(shard, 2, -1)

    def joined(first, last):
        return plane_grad[:, :, first:last].reshape(1, shard, -1)

    small_grad = jnp.sum(plane_grad[None, :, :, qw + 2 * HD :], axis=2)

    return (
        output[None],
        input_grad[None],
        small_grad[:, :, experts],
        small_grad[:, :, experts + 1],
        joined(0, qw),
        joined(qw, qw + HD),
        joined(qw + HD, qw + 2 * HD),
        out_w_grad[None],
        small_grad[:, :, :experts],
        w_gate_grad,
        w_up_grad,
        w_down_grad,
    )


def solution(mesh):
    fine = Mesh(mesh.devices.reshape(2, 4, 2, 4, 2), AXES)
    seq = P(FSDP, CTX, None)
    vector = P(None, AXES)
    matrix = P(None, AXES, None)
    expert = P(None, FSDP, CTX, None)
    in_specs = (
        seq,
        seq,
        P(),
        P(None, FSDP, CTX, None),
        vector,
        vector,
        matrix,
        matrix,
        matrix,
        matrix,
        matrix,
        expert,
        expert,
        expert,
    )
    out_specs = (
        seq,
        seq,
        vector,
        vector,
        matrix,
        matrix,
        matrix,
        matrix,
        matrix,
        expert,
        expert,
        expert,
    )
    return jax.shard_map(body, mesh=fine, in_specs=in_specs, out_specs=out_specs, check_vma=False)
```

```python
import functools
import math

import jax
import jax.numpy as jnp
from jax import lax
from jax.experimental import pallas as pl
from jax.experimental.pallas import tpu as pltpu
from jax.sharding import Mesh
from jax.sharding import PartitionSpec as P

H = 12
KVH = 2
HD = 128
TOPK = 4

EPSILON = 1e-06
ROPE_BASE = 1000000.0
NEGATIVE = -1e30

AXES = ("ylo", "z", "core", "x", "yhi")
CTX = ("ylo", "z", "core")
FSDP = ("x", "yhi")
GROUPS = [
    [
        (((group ^ yhi) * 4 + z) * 2 + core) * 8 + x * 2 + yhi
        for x in range(4)
        for yhi in range(2)
        for core in range(2)
    ]
    for group in range(2)
    for z in range(4)
]
RING = ("ylo", "z")
PLANE = ("ylo", "z", "yhi")
OUT_PLANE = ("yhi", "z", "ylo")
GROUPS = [
    [
        (((group ^ yhi) * 4 + z) * 2 + core) * 8 + x * 2 + yhi
        for x in range(4)
        for yhi in range(2)
        for core in range(2)
    ]
    for group in range(2)
    for z in range(4)
]
RING = ("ylo", "z")
ROWS_ORDER = ("ylo", "z", "yhi", "x")
OUT_ORDER = ("yhi", "z", "ylo", "x")
SLOTS = 40

bf16 = jnp.bfloat16
f32 = jnp.float32


def dot(left, right):
    return jnp.dot(left, right, preferred_element_type=f32)


def dot_t(left, right):
    return lax.dot_general(left, right, (((1,), (1,)), ((), ())), preferred_element_type=f32)


def t_dot(left, right):
    return lax.dot_general(left, right, (((0,), (0,)), ((), ())), preferred_element_type=f32)


def exchange(pieces, axes):
    return lax.all_to_all(pieces, axes, split_axis=0, concat_axis=0, tiled=True)


def to_owners(pieces):
    return lax.all_to_all(
        pieces, AXES, split_axis=0, concat_axis=0, axis_index_groups=GROUPS, tiled=True
    )


def spread(piece, count, axes):
    return exchange(jnp.broadcast_to(piece[None], (count,) + piece.shape), axes)


def after(value, earlier):
    return lax.optimization_barrier((value, earlier))[0]


def together(*values):
    return lax.optimization_barrier(values)


def partner(value):
    return lax.ppermute(value, "core", [(0, 1), (1, 0)])


def route(axes, sizes, move):
    pairs = []
    for source in range(math.prod(sizes)):
        rest, at = source, []
        for size in reversed(sizes):
            at.insert(0, rest % size)
            rest //= size
        target = 0
        for size, value in zip(sizes, move(*at)):
            target = target * size + value
        pairs.append((source, target))
    return pairs


SAME = route(("core", "yhi"), (2, 2), lambda c, h: (h, c))
OTHER = route(("core", "yhi"), (2, 2), lambda c, h: (1 - h, c))
OUT_SAME = route(("ylo", "core", "yhi"), (2, 2, 2), lambda j, c, h: (c, j, h))
OUT_OTHER = route(("ylo", "core", "yhi"), (2, 2, 2), lambda j, c, h: (c, j, 1 - h))


def back(pairs):
    return [(target, source) for source, target in pairs]


def pick(flag, if_zero, if_one):
    return jnp.where(flag == 0, if_zero, if_one)


def gather_pieces(pair, flag, key, axes, same, other):
    first = lax.ppermute(pick(flag, pair[0], pair[1]), axes, same)
    second = lax.ppermute(pick(flag, pair[1], pair[0]), axes, other)
    return pick(
        key, jnp.concatenate([first, second]), jnp.concatenate([second, first])
    )


def scatter_pieces(piece, flag, key, axes, same, other):
    count = piece.shape[0] // 2
    mine, rest = piece[:count], piece[count:]
    first = lax.ppermute(pick(key, mine, rest), axes, back(same))
    second = lax.ppermute(pick(key, rest, mine), axes, back(other))
    return pick(flag, jnp.concatenate([first, second], axis=-1), jnp.concatenate([second, first], axis=-1))


def along_x(piece):
    return [piece] + [
        lax.ppermute(piece, "x", [(i, (i + s) % 4) for i in range(4)]) for s in (1, 2, 3)
    ]


def back_along_x(blocks):
    arrived = [blocks[0]] + [
        lax.ppermute(blocks[s], "x", [(i, (i - s) % 4) for i in range(4)]) for s in (1, 2, 3)
    ]
    return sum(block.astype(f32) for block in arrived).astype(bf16)


def order_matrix(groups, x):
    index = jnp.arange(groups * 96, dtype=jnp.int32)
    turn_of, group, row = index // (groups * 24), index // 24 % groups, index % 24
    own = group * 96 + (x - turn_of) % 4 * 24 + row
    return (index[:, None] == own[None, :]).astype(bf16)


def places(pair_of, ctx, row_count, ctx_count):
    half_size = row_count // 2
    pair = jnp.sum(
        jnp.where(ctx[:, None] == jnp.arange(ctx_count, dtype=jnp.int32)[None], pair_of[None], 0),
        axis=1,
    )
    block = jnp.stack([pair, 2 * ctx_count - 1 - pair], axis=1)
    return block[:, :, None] * half_size + jnp.arange(half_size, dtype=jnp.int32)[None, None]


def in_three(value):
    high = value.astype(bf16)
    rest = value - high.astype(f32)
    middle = rest.astype(bf16)
    return [high, middle, (rest - middle.astype(f32)).astype(bf16)]


def call(kernel, outs, *args, scratch=()):
    def whole(shape):
        return pl.BlockSpec(shape, lambda i: (0,) * len(shape))

    return pl.pallas_call(
        kernel,
        out_shape=[jax.ShapeDtypeStruct(shape, dtype) for shape, dtype in outs],
        grid=(1,),
        in_specs=[whole(a.shape) for a in args],
        out_specs=[whole(shape) for shape, _ in outs],
        scratch_shapes=list(scratch),
        compiler_params=pltpu.CompilerParams(vmem_limit_bytes=ROOM),
        cost_estimate=COST,
    )(*args)


ROOM = 58 << 20
COST = pl.CostEstimate(flops=1 << 20, bytes_accessed=1 << 18, transcendentals=0)
WIDE = 2 * HD
EXPERTS = 16


def turn(vectors, cosines, sines):
    return vectors * cosines + pltpu.roll(vectors, HD // 2, axis=1) * sines


def gain_picker():
    row = lax.broadcasted_iota(jnp.int32, (8, 128), 0)
    column = lax.broadcasted_iota(jnp.int32, (8, 128), 1)
    return jnp.where((column == row + EXPERTS) & (row < 2), 1.0, 0.0).astype(bf16)


def normal_of(stream):
    inverse = lax.rsqrt(jnp.mean(stream * stream, axis=-1, keepdims=True) + EPSILON)
    return stream * inverse, inverse


def norm_back(grad, normal, inverse, gain):
    scaled = grad * gain
    return inverse * (scaled - normal * jnp.mean(scaled * normal, axis=-1, keepdims=True))


def column_block(s, count):
    return slice(s * count, (s + 1) * count)


def order_kernel(rows, order, out):
    out[...] = dot(rows[...], order[...]).astype(bf16)


def keys_kernel(both, cosines, sines, *refs):
    kvs, (normed, key_value, gains) = refs[:4], refs[4:]
    count = kvs[0].shape[0]
    for s in range(4):
        gains[:, column_block(s, count)] = dot_t(gain_picker(), kvs[s][:, WIDE:])
    normal, _ = normal_of(both[...].astype(f32))
    normed[...] = (normal * gains[0:1]).astype(bf16)
    kv = dot(normed[:, column_block(0, count)], kvs[0][:, :WIDE])
    for s in range(1, 4):
        kv = kv + dot(normed[:, column_block(s, count)], kvs[s][:, :WIDE])
    key_value[:, :HD] = turn(kv[:, :HD], cosines[...], sines[...]).astype(bf16)
    key_value[:, HD:] = kv[:, HD:].astype(bf16)


def small_kernel(order, kvs0, kvs1, kvs2, kvs3, small, gains):
    count = kvs0.shape[0]
    total = jnp.zeros(small.shape, f32)
    for s, kvs in enumerate((kvs0, kvs1, kvs2, kvs3)):
        total = total + dot(order[:, column_block(s, count)], kvs[:, WIDE:])
    small[...] = total.astype(bf16)
    gains[...] = dot_t(gain_picker(), small[...])


def attend_kernel(
    normed, cosines, sines, q_place, low_place, up_place, order, *refs, scale, pieces, heads
):
    w_q, kv, (queries, ordered, logs, kv_low, kv_up, mixed) = refs[:4], refs[4], refs[5:]
    count = w_q[0].shape[0]
    half = kv.shape[1] // 2
    for i in range(pieces):
        kv_low[i * half : (i + 1) * half, :] = kv[i, :half]
        kv_up[i * half : (i + 1) * half, :] = kv[i, half:]
    allowed_low = low_place[...] <= q_place[...]
    allowed_up = up_place[...] <= q_place[half:, :]
    for h in range(heads):
        at = slice(h * HD, (h + 1) * HD)
        q = dot(normed[:, column_block(0, count)], w_q[0][:, at])
        for s in range(1, 4):
            q = q + dot(normed[:, column_block(s, count)], w_q[s][:, at])
        q = turn(q, cosines[...], sines[...]).astype(bf16)
        queries[:, at] = q
        low = jnp.where(allowed_low, dot_t(q, kv_low[:, :HD]) * scale, NEGATIVE)
        up = jnp.where(allowed_up, dot_t(q[half:], kv_up[:, :HD]) * scale, NEGATIVE)
        first, second = low[:half], low[half:]
        top = jnp.max(first, axis=-1, keepdims=True)
        weight = jnp.exp(first - top)
        total = jnp.sum(weight, axis=-1, keepdims=True)
        probs = (weight / total).astype(bf16)
        mixed[:half, at] = dot(probs, kv_low[:, HD:]).astype(bf16)
        logs[h, :half, :] = top + jnp.log(total)
        top = jnp.maximum(
            jnp.max(second, axis=-1, keepdims=True), jnp.max(up, axis=-1, keepdims=True)
        )
        weight, weight_up = jnp.exp(second - top), jnp.exp(up - top)
        total = jnp.sum(weight, axis=-1, keepdims=True) + jnp.sum(
            weight_up, axis=-1, keepdims=True
        )
        mixed[half:, at] = (
            dot((weight / total).astype(bf16), kv_low[:, HD:])
            + dot((weight_up / total).astype(bf16), kv_up[:, HD:])
        ).astype(bf16)
        logs[h, half:, :] = top + jnp.log(total)
    ordered[...] = dot(mixed[...], order[...]).astype(bf16)


def branch_kernel(mixed, w_out0, w_out1, w_out2, w_out3, own, other, w_out):
    quarter = mixed.shape[0] // 4
    count, columns = w_out0.shape[1:]
    for s, part in enumerate((w_out0, w_out1, w_out2, w_out3)):
        w_out[:, column_block(s, count)] = part[...]
    for k in range(2):
        part = dot(mixed[...], w_out[k])
        at = slice(k * columns, (k + 1) * columns)
        own[:quarter, at] = part[:quarter]
        other[:quarter, at] = part[quarter : 2 * quarter]
        own[quarter:, at] = part[2 * quarter : 3 * quarter]
        other[quarter:, at] = part[3 * quarter :]


def route_kernel(
    tokens,
    own,
    received,
    small,
    gains,
    hits,
    places_of,
    placer,
    cot_rows,
    sent,
    midway,
    moe_low,
    gates,
    parts,
):
    middle = tokens[...].astype(f32) + (own[...] + received[...])
    midway[...] = middle
    normal, _ = normal_of(middle)
    moe = (normal * gains[1:2]).astype(bf16)
    moe_low[...] = moe
    sent[:, : moe.shape[1]] = dot(placer[...], moe).astype(bf16)
    logits = dot(moe, small[...])
    picked = [
        jnp.sum(hits[k].astype(f32) * logits, axis=-1, keepdims=True) for k in range(TOPK)
    ]
    top = picked[0]
    for value in picked[1:]:
        top = jnp.maximum(top, value)
    weights = [jnp.exp(value - top) for value in picked]
    total = weights[0]
    for value in weights[1:]:
        total = total + value
    lane = lax.broadcasted_iota(jnp.int32, gates.shape, 1)
    gate_at = jnp.zeros(places_of.shape[1:], f32)
    kept = jnp.zeros(gates.shape, f32)
    for k in range(TOPK):
        gate = weights[k] / total
        kept = jnp.where(lane == k, gate, kept)
        gate_at = gate_at + places_of[k].astype(f32) * gate
    gates[...] = kept
    ones = jnp.ones(gates.shape, bf16)
    slot_gates = jnp.zeros((sent.shape[0], gates.shape[1]), f32)
    for i, part in enumerate(in_three(gate_at)):
        parts[i] = part
        slot_gates = slot_gates + t_dot(part, ones)
    sent[:, moe.shape[1] :] = (slot_gates[:, :1] * cot_rows[...].astype(f32)).astype(bf16)


def fetched(core, weights, held, sems, first):
    copies = [
        pltpu.make_async_copy(weights.at[m, core[0]], held.at[m], sems.at[m]) for m in range(3)
    ]

    @pl.when(pl.program_id(0) == 0)
    def _():
        for m in first:
            copies[m].start()

    def ready(m):
        @pl.when(pl.program_id(0) == 0)
        def _():
            copies[m].wait()

        return held[m]

    return ready


def forward_kernel(
    core, sent, weights, out, hidden, factor, other_factor, held, sems
):
    ready = fetched(core, weights, held, sems, (0, 1, 2))
    width = out.shape[1]
    rows = sent[:, :width]
    gate_pre, up_pre = dot(rows, ready(0)), dot(rows, ready(1))
    sigmoid = 1.0 / (1.0 + jnp.exp(-gate_pre))
    silu = gate_pre * sigmoid
    low = (silu * up_pre).astype(bf16)
    hidden[...] = low
    out[...] = dot_t(low, ready(2)).astype(bf16)
    factor[...] = up_pre * sigmoid * (1.0 + gate_pre * (1.0 - sigmoid))
    other_factor[...] = silu


def backward_kernel(
    core, sent, factor, other_factor, weights, rows_grad, gate_grad, up_grad, held, sems
):
    ready = fetched(core, weights, held, sems, (2, 0, 1))
    hidden_grad = dot(sent[:, rows_grad.shape[1] :], ready(2))
    low = (hidden_grad * factor[...]).astype(bf16)
    other = (hidden_grad * other_factor[...]).astype(bf16)
    gate_grad[...] = low
    up_grad[...] = other
    rows_grad[...] = (dot_t(low, ready(0)) + dot_t(other, ready(1))).astype(bf16)


def expert_call(kernel, block, core, arrays, weights, outs):
    count = arrays[0].shape[0]

    def rows(columns):
        return pl.BlockSpec((block, columns), lambda i, core: (i, 0))

    return pl.pallas_call(
        kernel,
        out_shape=[jax.ShapeDtypeStruct((count, columns), dtype) for columns, dtype in outs],
        grid_spec=pltpu.PrefetchScalarGridSpec(
            num_scalar_prefetch=1,
            grid=(count // block,),
            in_specs=[rows(a.shape[1]) for a in arrays] + [pl.BlockSpec(memory_space=pltpu.HBM)],
            out_specs=[rows(columns) for columns, _ in outs],
            scratch_shapes=[
                pltpu.VMEM((3,) + weights.shape[2:], bf16),
                pltpu.SemaphoreType.DMA((3,)),
            ],
        ),
        compiler_params=pltpu.CompilerParams(vmem_limit_bytes=ROOM),
        cost_estimate=COST,
    )(core, *arrays, weights)


def weights_kernel(sent, out_grad, hidden, gate_grad, up_grad, sums):
    rows = sent[...]
    sums[0] = t_dot(rows, gate_grad[...]).astype(bf16)
    sums[1] = t_dot(rows, up_grad[...]).astype(bf16)
    sums[2] = t_dot(out_grad[...], hidden[...]).astype(bf16)


def expert_weights_grad(sent, hidden, gate_grad, up_grad, block=256):
    count, width = sent.shape[0], sent.shape[1] // 2
    columns = hidden.shape[1]
    part = pl.BlockSpec((count, block), lambda i: (0, i))
    other_part = pl.BlockSpec((count, block), lambda i: (0, i + width // block))
    whole = pl.BlockSpec((count, columns), lambda i: (0, 0), pipeline_mode=pl.Buffered(1))
    return pl.pallas_call(
        weights_kernel,
        out_shape=jax.ShapeDtypeStruct((3, width, columns), bf16),
        grid=(width // block,),
        in_specs=[part, other_part, whole, whole, whole],
        out_specs=pl.BlockSpec((3, block, columns), lambda i: (0, i, 0)),
        compiler_params=pltpu.CompilerParams(vmem_limit_bytes=ROOM),
        cost_estimate=COST,
    )(sent, sent, hidden, gate_grad, up_grad)


def combine_kernel(
    midway, parts, returned, cot, hits, places_of, gates, small, moe_low, output, moe_part, router_grad
):
    rows = returned[...]
    output[...] = (
        midway[...] + (dot(parts[0], rows) + (dot(parts[1], rows) + dot(parts[2], rows)))
    ).astype(bf16)
    agreement = dot_t(cot[...], rows)
    lane = lax.broadcasted_iota(jnp.int32, gates.shape, 1)
    gate, grad = [], []
    mean = jnp.zeros((gates.shape[0], 1), f32)
    for k in range(TOPK):
        gate.append(jnp.sum(jnp.where(lane == k, gates[...], 0.0), axis=-1, keepdims=True))
        grad.append(jnp.sum(places_of[k].astype(f32) * agreement, axis=-1, keepdims=True))
        mean = mean + gate[k] * grad[k]
    logit_grad = jnp.zeros(gates.shape, f32)
    for k in range(TOPK):
        logit_grad = logit_grad + hits[k].astype(f32) * (gate[k] * (grad[k] - mean))
    logit_grad = logit_grad.astype(bf16)
    moe_part[...] = dot_t(logit_grad, small[...])
    router_grad[...] = t_dot(moe_low[...], logit_grad)


def home_kernel(placer_t, home, moe_part, midway, cot, gains, midway_grad, branch_low, gain_grad):
    grad = dot(placer_t[...], home[...]) + moe_part[...]
    normal, inverse = normal_of(midway[...])
    result = cot[...].astype(f32) + norm_back(grad, normal, inverse, gains[1:2])
    midway_grad[...] = result
    branch_low[...] = result.astype(bf16)
    gain_grad[...] = jnp.broadcast_to(
        jnp.sum(grad * normal, axis=0, keepdims=True), gain_grad.shape
    )


def out_grad_kernel(mixed, own, other, branch, *blocks):
    quarter = own.shape[0] // 2
    branch[:quarter] = own[:quarter]
    branch[quarter : 2 * quarter] = other[:quarter]
    branch[2 * quarter : 3 * quarter] = own[quarter:]
    branch[3 * quarter :] = other[quarter:]
    count, columns = blocks[0].shape[1:]
    for k in range(2):
        grad = t_dot(mixed[...], branch[:, column_block(k, columns)]).astype(bf16)
        for s in range(4):
            blocks[s][k] = grad[column_block(s, count)]


def attend_back_kernel(
    branch,
    w_out,
    order,
    queries,
    kv_low,
    kv_up,
    logs,
    q_place,
    low_place,
    up_place,
    cosines,
    sines,
    dq,
    dkv,
    grads,
    acc_low,
    acc_up,
    *,
    scale,
    pieces,
    heads,
):
    half = queries.shape[0] // 2
    columns = w_out.shape[2]
    ordered = dot_t(branch[:, :columns], w_out[0]) + dot_t(branch[:, columns:], w_out[1])
    grads[...] = dot_t(ordered.astype(bf16), order[...]).astype(bf16)
    allowed_low = low_place[...] <= q_place[...]
    allowed_up = up_place[...] <= q_place[half:, :]
    key_low, value_low = kv_low[:, :HD], kv_low[:, HD:]
    key_up, value_up = kv_up[:, :HD], kv_up[:, HD:]
    for h in range(heads):
        at = slice(h * HD, (h + 1) * HD)
        q, grad, log = queries[:, at], grads[:, at], logs[h]
        low = jnp.where(allowed_low, dot_t(q, key_low) * scale, NEGATIVE)
        up = jnp.where(allowed_up, dot_t(q[half:], key_up) * scale, NEGATIVE)
        probs_low, probs_up = jnp.exp(low - log), jnp.exp(up - log[half:])
        grad_low, grad_up = dot_t(grad, value_low), dot_t(grad[half:], value_up)
        along = jnp.sum(probs_low * grad_low, axis=-1, keepdims=True)
        along_up = along[half:] + jnp.sum(probs_up * grad_up, axis=-1, keepdims=True)
        along = jnp.concatenate([along[:half], along_up])
        score_low = (probs_low * (grad_low - along)).astype(bf16)
        score_up = (probs_up * (grad_up - along_up)).astype(bf16)
        part = dot(score_low, key_low)
        part = jnp.concatenate([part[:half], part[half:] + dot(score_up, key_up)]) * scale
        dq[:, at] = turn(part, cosines[...], -sines[...]).astype(bf16)
        terms = (
            (acc_low, slice(0, HD), t_dot(q, score_low)),
            (acc_up, slice(0, HD), t_dot(q[half:], score_up)),
            (acc_low, slice(HD, 2 * HD), t_dot(grad, probs_low.astype(bf16))),
            (acc_up, slice(HD, 2 * HD), t_dot(grad[half:], probs_up.astype(bf16))),
        )
        for acc, rows, term in terms:
            if h == 0:
                acc[rows] = term
            else:
                acc[rows] += term
    for acc, first in ((acc_low, 0), (acc_up, half)):
        dk = (acc[:HD].T * scale).astype(bf16)
        dv = acc[HD:].T.astype(bf16)
        for i in range(pieces):
            dkv[i, first : first + half, :HD] = dk[i * half : (i + 1) * half]
            dkv[i, first : first + half, HD:] = dv[i * half : (i + 1) * half]


def sum_kernel(dq, cosines, sines, *refs):
    w_q, kvs, (parts, dkv, own, other) = refs[:4], refs[4:8], refs[8:]
    total = jnp.sum(parts[...].astype(f32), axis=0)
    dkv[:, :HD] = turn(total[:, :HD], cosines[...], -sines[...]).astype(bf16)
    dkv[:, HD:] = total[:, HD:].astype(bf16)
    quarter = own.shape[0] // 2
    for s in range(4):
        grad = dot_t(dq[...], w_q[s][...]) + dot_t(dkv[...], kvs[s][:, :WIDE])
        at = column_block(s, w_q[s].shape[0])
        own[:quarter, at] = grad[:quarter]
        other[:quarter, at] = grad[quarter : 2 * quarter]
        own[quarter:, at] = grad[2 * quarter : 3 * quarter]
        other[quarter:, at] = grad[3 * quarter :]


def small_grad_kernel(order, router_grad, gain_grad, out):
    row = lax.broadcasted_iota(jnp.int32, gain_grad.shape, 0)
    second = jnp.where(row == 1, gain_grad[...], 0.0).astype(bf16)
    small = router_grad[...] + t_dot(second, gain_picker())
    out[...] = t_dot(order[...], small.astype(bf16))


def input_kernel(both, own, received, midway_grad, gains, order, small, normed, dkv, out, *blocks):
    grad = own[...] + received[...]
    quarter = own.shape[0] // 2
    tokens = jnp.concatenate([both[:quarter], both[2 * quarter : 3 * quarter]])
    normal, inverse = normal_of(tokens.astype(f32))
    parts = in_three(norm_back(grad, normal, inverse, gains[0:1]))
    moved = dot_t(jnp.concatenate(parts), order[...])
    count = 2 * quarter
    out[...] = midway_grad[...] + (
        moved[:count] + (moved[count : 2 * count] + moved[2 * count :])
    )
    gain_grad = jnp.sum(grad * normal, axis=0, keepdims=True)
    row = lax.broadcasted_iota(jnp.int32, gains.shape, 0)
    gain_grad = jnp.where(row == 0, gain_grad, 0.0).astype(bf16)
    small = small[...] + t_dot(gain_grad, gain_picker())
    rows = blocks[0].shape[0]
    for s, block in enumerate(blocks):
        at = column_block(s, rows)
        block[:, :WIDE] = t_dot(normed[:, at], dkv[...]).astype(bf16)
        block[:, WIDE:] = small[at].astype(bf16)


def query_grad_kernel(normed, dq, *blocks):
    for s, block in enumerate(blocks):
        block[...] = t_dot(normed[:, column_block(s, block.shape[0])], dq[...]).astype(bf16)


def body(
    tokens,
    cotangent,
    pair_of,
    routes,
    attn_gain,
    moe_gain,
    w_query,
    w_key,
    w_value,
    w_out,
    w_router,
    w_gate,
    w_up,
    w_down,
):
    rows = tokens.shape[1]
    half = rows // 2
    width = tokens.shape[2]
    shard = w_query.shape[1]
    ctx_count = 16
    experts = w_router.shape[2]
    columns = w_gate.shape[3]
    per_group = H // KVH
    qw = per_group * HD
    scale = 1.0 / math.sqrt(HD)
    core = lax.axis_index("core")
    ylo, z, yhi = lax.axis_index("ylo"), lax.axis_index("z"), lax.axis_index("yhi")
    x = lax.axis_index("x")
    piece_rows = 2 * shard
    slots = experts * SLOTS
    own_tokens, cot = tokens[0], cotangent[0]

    def halves(matrix):
        return [matrix[:, : matrix.shape[1] // 2], matrix[:, matrix.shape[1] // 2 :]]

    small = jnp.concatenate([w_router[0], attn_gain[0][:, None], moe_gain[0][:, None]], axis=-1)
    small = jnp.pad(small, ((0, 0), (0, 128 - experts - 2)))
    query_halves, key_halves, value_halves = halves(w_query[0]), halves(w_key[0]), halves(w_value[0])
    pairs = [
        jnp.concatenate([k, v, small, q], axis=-1)
        for k, v, q in zip(key_halves, value_halves, query_halves)
    ]
    pieces = gather_pieces(pairs, yhi, core, ("core", "yhi"), SAME, OTHER)
    own_tokens, chosen, pair_of, out_halves, pieces = together(
        own_tokens, routes[0, 0], pair_of, w_out[0], pieces
    )

    plane_rows = 16 * piece_rows
    plane = spread(pieces, 16, PLANE)
    other_tokens = partner(own_tokens)
    both = jnp.concatenate(
        [own_tokens[:half], other_tokens[:half], own_tokens[half:], other_tokens[half:]]
    )
    out_pieces = gather_pieces(
        halves(out_halves), yhi, yhi, ("ylo", "core", "yhi"), OUT_SAME, OUT_OTHER
    )

    def two_cores(ctx):
        return jnp.stack([ctx + core, ctx + 1 - core], axis=-1).reshape(-1)

    ctx_here = (ylo * 4 + z) * 2
    q_place = places(pair_of, two_cores(ctx_here), rows, ctx_count)
    q_place = q_place.transpose(1, 0, 2).reshape(2 * rows, 1)
    key_place = places(
        pair_of, two_cores(jnp.arange(8, dtype=jnp.int32) * 2), rows, ctx_count
    )
    low_place, up_place = key_place[:, 0].reshape(1, -1), key_place[:, 1].reshape(1, -1)
    frequency = jnp.exp(jnp.arange(HD // 2, dtype=f32) * (-2.0 * math.log(ROPE_BASE) / HD))
    angles = q_place.astype(f32) * frequency[None, :]
    cosines, sines = jnp.cos(angles), jnp.sin(angles)
    cosines = jnp.concatenate([cosines, cosines], axis=-1)
    sines = jnp.concatenate([-sines, sines], axis=-1)
    lanes = jnp.arange(128, dtype=jnp.int32)
    hits = (chosen.T[:, :, None] == lanes[None, None, :]).astype(bf16)
    earlier = (lanes[:, None] > lanes[None, :]).astype(bf16)
    before = dot(earlier, jnp.sum(hits, axis=0))
    slot_index = jnp.sum(hits.astype(f32) * before[None], axis=-1).astype(jnp.int32)
    target = chosen.T * SLOTS + slot_index
    slot_row = jnp.arange(slots, dtype=jnp.int32)
    places_of = (target[:, :, None] == slot_row[None, None, :]).astype(bf16)
    placer_t = jnp.sum(places_of, axis=0)
    placer = placer_t.T
    order, out_order = order_matrix(16, x), order_matrix(8, x)
    (both,) = call(order_kernel, [((2 * rows, width), bf16)], both, order)
    (cot_rows,) = call(order_kernel, [((slots, width), bf16)], placer, cot)
    (
        plane, out_pieces, both, q_place, low_place, up_place, cosines, sines,
        hits, places_of, placer_t, placer, cot_rows, order, out_order,
    ) = together(
        plane, out_pieces, both, q_place, low_place, up_place, cosines, sines,
        hits, places_of, placer_t, placer, cot_rows, order, out_order,
    )

    plane = plane.reshape(plane_rows, -1)
    w_kvs = along_x(plane[:, : 3 * HD])
    wo = spread(out_pieces, 16, OUT_PLANE)
    w_q, w_kvs, wo = together(plane[:, 3 * HD :], w_kvs, wo)

    w_q = along_x(w_q)
    normed, key_value, gains = call(
        keys_kernel,
        [((2 * rows, width), bf16), ((2 * rows, 2 * HD), bf16), ((8, width), f32)],
        both,
        cosines,
        sines,
        *w_kvs,
    )
    all_kv = spread(key_value, 8, RING)
    small, moe_gains = call(
        small_kernel, [((width, 128), bf16), ((8, width), f32)], order, *w_kvs
    )
    expert_shards_in = jnp.stack([w_gate[0], w_up[0], w_down[0]])
    w_q, all_kv, wo, small, moe_gains, expert_shards_in = together(
        w_q, all_kv, wo, small, moe_gains, expert_shards_in
    )

    wo = along_x(wo.reshape(2, qw // 4, width // 2))
    expert_weights = lax.all_gather(expert_shards_in, CTX, axis=2, tiled=True)
    sizes = dict(scale=scale, pieces=8, heads=per_group)
    keys = 8 * rows
    queries, mixed, logs, kv_low, kv_up = call(
        functools.partial(attend_kernel, **sizes),
        [
            ((2 * rows, qw), bf16),
            ((2 * rows, qw), bf16),
            ((per_group, 2 * rows, 1), f32),
            ((keys, 2 * HD), bf16),
            ((keys, 2 * HD), bf16),
        ],
        normed,
        cosines,
        sines,
        q_place,
        low_place,
        up_place,
        out_order,
        *w_q,
        all_kv,
        scratch=[pltpu.VMEM((2 * rows, qw), bf16)],
    )
    wo, mixed = together(wo, mixed)

    branch_own, branch_other, wo = call(
        branch_kernel,
        [((rows, width), f32), ((rows, width), f32), ((2, qw, width // 2), bf16)],
        mixed,
        *wo,
    )
    sent, midway, moe_low, gates, gate_parts = call(
        route_kernel,
        [
            ((slots, 2 * width), bf16),
            ((rows, width), f32),
            ((rows, width), bf16),
            ((rows, 128), f32),
            ((3, rows, slots), bf16),
        ],
        own_tokens,
        branch_own,
        partner(branch_other),
        small,
        moe_gains,
        hits,
        places_of,
        placer,
        cot_rows,
    )

    sent = to_owners(sent.reshape(experts, SLOTS, 2 * width)).reshape(slots, 2 * width)
    mine = core.reshape(1)
    expert_out, hidden, factor, other_factor = expert_call(
        forward_kernel,
        128,
        mine,
        [sent],
        expert_weights,
        [(width, bf16), (columns, bf16), (columns, f32), (columns, f32)],
    )
    expert_out, factor = together(expert_out, factor)

    returned = to_owners(expert_out.reshape(experts, SLOTS, width))
    rows_grad, gate_grad, up_grad = expert_call(
        backward_kernel,
        128,
        mine,
        [sent, factor, other_factor],
        expert_weights,
        [(width, bf16), (columns, bf16), (columns, bf16)],
    )
    expert_sums = expert_weights_grad(sent, hidden, gate_grad, up_grad)
    returned, rows_grad, expert_sums = together(returned, rows_grad, expert_sums)
    home_grad = to_owners(rows_grad.reshape(experts, SLOTS, width))
    expert_sums = lax.psum_scatter(expert_sums, RING, scatter_dimension=1, tiled=True)
    output, moe_part, router_grad = call(
        combine_kernel,
        [((rows, width), bf16), ((rows, width), f32), ((width, 128), f32)],
        midway,
        gate_parts,
        returned.reshape(slots, width),
        cot,
        hits,
        places_of,
        gates,
        small,
        moe_low,
    )
    home_grad, moe_part = together(home_grad, moe_part)
    midway_grad, branch_low, gain_two_grad = call(
        home_kernel,
        [((rows, width), f32), ((rows, width), bf16), ((8, width), f32)],
        placer_t,
        home_grad.reshape(slots, width),
        moe_part,
        midway,
        cot,
        moe_gains,
    )
    branch, *out_w_grad = call(
        out_grad_kernel,
        [((2 * rows, width), bf16)] + [((2, qw // 4, width // 2), bf16)] * 4,
        mixed,
        branch_low,
        partner(branch_low),
    )
    branch, out_w_grad = together(branch, out_w_grad)
    out_w_grad = back_along_x(out_w_grad)

    dq, dkv = call(
        functools.partial(attend_back_kernel, **sizes),
        [((2 * rows, qw), bf16), ((8, 2 * rows, 2 * HD), bf16)],
        branch,
        wo,
        out_order,
        queries,
        kv_low,
        kv_up,
        logs,
        q_place,
        low_place,
        up_place,
        cosines,
        sines,
        scratch=[
            pltpu.VMEM((2 * rows, qw), bf16),
            pltpu.VMEM((2 * HD, keys), f32),
            pltpu.VMEM((2 * HD, keys), f32),
        ],
    )
    dkv = exchange(dkv, RING)
    q_w_grad = back_along_x(call(query_grad_kernel, [((plane_rows, qw), bf16)] * 4, normed, dq))
    dkv, out_w_grad = together(dkv, out_w_grad)

    out_w_grad = exchange(out_w_grad.reshape(16, piece_rows, width // 2), OUT_PLANE)
    dkv, normed_own, normed_other = call(
        sum_kernel,
        [((2 * rows, 2 * HD), bf16), ((rows, width), f32), ((rows, width), f32)],
        dq,
        cosines,
        sines,
        *w_q,
        *w_kvs,
        dkv,
    )
    (small_grad,) = call(
        small_grad_kernel, [((width, 128), f32)], order, router_grad, gain_two_grad
    )
    input_grad, *kvs_grad = call(
        input_kernel,
        [((rows, width), f32)] + [((plane_rows, 3 * HD), bf16)] * 4,
        both,
        normed_own,
        partner(normed_other),
        midway_grad,
        gains,
        order,
        small_grad,
        normed,
        dkv,
    )
    kvs_grad, out_w_grad, input_grad = together(kvs_grad, out_w_grad, input_grad)
    kvs_grad = back_along_x(kvs_grad)
    plane_grad = jnp.concatenate([q_w_grad, kvs_grad], axis=-1)
    plane_grad, out_w_grad, expert_sums = together(plane_grad, out_w_grad, expert_sums)
    plane_grad = exchange(plane_grad.reshape(16, piece_rows, qw + 3 * HD), PLANE)

    def summed(pieces):
        return jnp.sum(pieces.astype(f32), axis=0)

    def expert_shards(grad):
        count = grad.shape[1] // 2
        kept = lax.dynamic_slice_in_dim(grad, core * count, count, axis=1)
        given = partner(lax.dynamic_slice_in_dim(grad, (1 - core) * count, count, axis=1))
        both = jnp.stack([pick(core, kept, given), pick(core, given, kept)], axis=1)
        return [both[i : i + 1].astype(f32) for i in range(3)]

    out_w_grad = scatter_pieces(
        summed(out_w_grad), yhi, yhi, ("ylo", "core", "yhi"), OUT_SAME, OUT_OTHER
    )
    w_gate_grad, w_up_grad, w_down_grad = expert_shards(expert_sums)
    plane_grad, out_w_grad, w_gate_grad, w_up_grad, w_down_grad = together(
        plane_grad, out_w_grad, w_gate_grad, w_up_grad, w_down_grad
    )
    plane_grad = scatter_pieces(summed(plane_grad), yhi, core, ("core", "yhi"), SAME, OTHER)
    plane_grad = plane_grad.reshape(shard, 2, -1)

    def joined(first, last):
        return plane_grad[:, :, first:last].reshape(1, shard, -1)

    small_grad = jnp.sum(plane_grad[None, :, :, qw + 2 * HD :], axis=2)

    return (
        output[None],
        input_grad[None],
        small_grad[:, :, experts],
        small_grad[:, :, experts + 1],
        joined(0, qw),
        joined(qw, qw + HD),
        joined(qw + HD, qw + 2 * HD),
        out_w_grad[None],
        small_grad[:, :, :experts],
        w_gate_grad,
        w_up_grad,
        w_down_grad,
    )


def solution(mesh):
    fine = Mesh(mesh.devices.reshape(2, 4, 2, 4, 2), AXES)
    seq = P(FSDP, CTX, None)
    vector = P(None, AXES)
    matrix = P(None, AXES, None)
    expert = P(None, FSDP, CTX, None)
    in_specs = (
        seq,
        seq,
        P(),
        P(None, FSDP, CTX, None),
        vector,
        vector,
        matrix,
        matrix,
        matrix,
        matrix,
        matrix,
        expert,
        expert,
        expert,
    )
    out_specs = (
        seq,
        seq,
        vector,
        vector,
        matrix,
        matrix,
        matrix,
        matrix,
        matrix,
        expert,
        expert,
        expert,
    )
    return jax.shard_map(body, mesh=fine, in_specs=in_specs, out_specs=out_specs, check_vma=False)
```

```python
import functools
import math

import jax
import jax.numpy as jnp
from jax import lax
from jax.experimental import pallas as pl
from jax.experimental.pallas import tpu as pltpu
from jax.sharding import Mesh
from jax.sharding import PartitionSpec as P

H = 12
KVH = 2
HD = 128
TOPK = 4

EPSILON = 1e-06
ROPE_BASE = 1000000.0
NEGATIVE = -1e30

AXES = ("ylo", "z", "core", "x", "yhi")
CTX = ("ylo", "z", "core")
FSDP = ("x", "yhi")
GROUPS = [
    [
        (((group ^ yhi) * 4 + z) * 2 + core) * 8 + x * 2 + yhi
        for x in range(4)
        for yhi in range(2)
        for core in range(2)
    ]
    for group in range(2)
    for z in range(4)
]
RING = ("ylo", "z")
PLANE = ("ylo", "z", "yhi")
GROUPS = [
    [
        (((group ^ yhi) * 4 + z) * 2 + core) * 8 + x * 2 + yhi
        for x in range(4)
        for yhi in range(2)
        for core in range(2)
    ]
    for group in range(2)
    for z in range(4)
]
RING = ("ylo", "z")
ROWS_ORDER = ("ylo", "z", "yhi", "x")
OUT_ORDER = ("yhi", "z", "ylo", "x")
SLOTS = 40

bf16 = jnp.bfloat16
f32 = jnp.float32


def dot(left, right):
    return jnp.dot(left, right, preferred_element_type=f32)


def dot_t(left, right):
    return lax.dot_general(left, right, (((1,), (1,)), ((), ())), preferred_element_type=f32)


def t_dot(left, right):
    return lax.dot_general(left, right, (((0,), (0,)), ((), ())), preferred_element_type=f32)


def exchange(pieces, axes):
    return lax.all_to_all(pieces, axes, split_axis=0, concat_axis=0, tiled=True)


def to_owners(pieces):
    return lax.all_to_all(
        pieces, AXES, split_axis=0, concat_axis=0, axis_index_groups=GROUPS, tiled=True
    )


def spread(piece, count, axes):
    return exchange(jnp.broadcast_to(piece[None], (count,) + piece.shape), axes)


def after(value, earlier):
    return lax.optimization_barrier((value, earlier))[0]


def together(*values):
    return lax.optimization_barrier(values)


def partner(value):
    return lax.ppermute(value, "core", [(0, 1), (1, 0)])


def route(axes, sizes, move):
    pairs = []
    for source in range(math.prod(sizes)):
        rest, at = source, []
        for size in reversed(sizes):
            at.insert(0, rest % size)
            rest //= size
        target = 0
        for size, value in zip(sizes, move(*at)):
            target = target * size + value
        pairs.append((source, target))
    return pairs


SAME = route(("core", "yhi"), (2, 2), lambda c, h: (h, c))
OTHER = route(("core", "yhi"), (2, 2), lambda c, h: (1 - h, c))
OUT_SAME = route(("ylo", "core", "yhi"), (2, 2, 2), lambda j, c, h: (c, j, h))
OUT_OTHER = route(("ylo", "core", "yhi"), (2, 2, 2), lambda j, c, h: (c, j, 1 - h))


def back(pairs):
    return [(target, source) for source, target in pairs]


def pick(flag, if_zero, if_one):
    return jnp.where(flag == 0, if_zero, if_one)


def gather_pieces(pair, flag, key, axes, same, other):
    first = lax.ppermute(pick(flag, pair[0], pair[1]), axes, same)
    second = lax.ppermute(pick(flag, pair[1], pair[0]), axes, other)
    return pick(
        key, jnp.concatenate([first, second]), jnp.concatenate([second, first])
    )


def scatter_pieces(piece, flag, key, axes, same, other):
    count = piece.shape[0] // 2
    mine, rest = piece[:count], piece[count:]
    first = lax.ppermute(pick(key, mine, rest), axes, back(same))
    second = lax.ppermute(pick(key, rest, mine), axes, back(other))
    return pick(flag, jnp.concatenate([first, second], axis=-1), jnp.concatenate([second, first], axis=-1))


def along_x(piece):
    return [piece] + [
        lax.ppermute(piece, "x", [(i, (i + s) % 4) for i in range(4)]) for s in (1, 2, 3)
    ]


def back_along_x(blocks):
    arrived = [blocks[0]] + [
        lax.ppermute(blocks[s], "x", [(i, (i - s) % 4) for i in range(4)]) for s in (1, 2, 3)
    ]
    return sum(block.astype(f32) for block in arrived).astype(bf16)


def order_matrix(groups, x):
    index = jnp.arange(groups * 96, dtype=jnp.int32)
    turn_of, group, row = index // (groups * 24), index // 24 % groups, index % 24
    if groups == 8:
        group = group % 4 * 2 + group // 4
    own = group * 96 + (x - turn_of) % 4 * 24 + row
    return (index[:, None] == own[None, :]).astype(bf16)


def places(pair_of, ctx, row_count, ctx_count):
    half_size = row_count // 2
    pair = jnp.sum(
        jnp.where(ctx[:, None] == jnp.arange(ctx_count, dtype=jnp.int32)[None], pair_of[None], 0),
        axis=1,
    )
    block = jnp.stack([pair, 2 * ctx_count - 1 - pair], axis=1)
    return block[:, :, None] * half_size + jnp.arange(half_size, dtype=jnp.int32)[None, None]


def in_three(value):
    high = value.astype(bf16)
    rest = value - high.astype(f32)
    middle = rest.astype(bf16)
    return [high, middle, (rest - middle.astype(f32)).astype(bf16)]


def call(kernel, outs, *args, scratch=()):
    def whole(shape):
        return pl.BlockSpec(shape, lambda i: (0,) * len(shape))

    return pl.pallas_call(
        kernel,
        out_shape=[jax.ShapeDtypeStruct(shape, dtype) for shape, dtype in outs],
        grid=(1,),
        in_specs=[whole(a.shape) for a in args],
        out_specs=[whole(shape) for shape, _ in outs],
        scratch_shapes=list(scratch),
        compiler_params=pltpu.CompilerParams(vmem_limit_bytes=ROOM),
        cost_estimate=COST,
    )(*args)


ROOM = 58 << 20
COST = pl.CostEstimate(flops=1 << 20, bytes_accessed=1 << 18, transcendentals=0)
WIDE = 2 * HD
EXPERTS = 16


def turn(vectors, cosines, sines):
    return vectors * cosines + pltpu.roll(vectors, HD // 2, axis=1) * sines


def gain_picker():
    row = lax.broadcasted_iota(jnp.int32, (8, 128), 0)
    column = lax.broadcasted_iota(jnp.int32, (8, 128), 1)
    return jnp.where((column == row + EXPERTS) & (row < 2), 1.0, 0.0).astype(bf16)


def normal_of(stream):
    inverse = lax.rsqrt(jnp.mean(stream * stream, axis=-1, keepdims=True) + EPSILON)
    return stream * inverse, inverse


def norm_back(grad, normal, inverse, gain):
    scaled = grad * gain
    return inverse * (scaled - normal * jnp.mean(scaled * normal, axis=-1, keepdims=True))


def column_block(s, count):
    return slice(s * count, (s + 1) * count)


def order_kernel(rows, order, out):
    out[...] = dot(rows[...], order[...]).astype(bf16)


def keys_kernel(both, cosines, sines, *refs):
    kvs, (normed, key_value, gains) = refs[:4], refs[4:]
    count = kvs[0].shape[0]
    for s in range(4):
        gains[:, column_block(s, count)] = dot_t(gain_picker(), kvs[s][:, WIDE : WIDE + HD])
    normal, _ = normal_of(both[...].astype(f32))
    normed[...] = (normal * gains[0:1]).astype(bf16)
    kv = dot(normed[:, column_block(0, count)], kvs[0][:, :WIDE])
    for s in range(1, 4):
        kv = kv + dot(normed[:, column_block(s, count)], kvs[s][:, :WIDE])
    key_value[:, :HD] = turn(kv[:, :HD], cosines[...], sines[...]).astype(bf16)
    key_value[:, HD:] = kv[:, HD:].astype(bf16)


def small_kernel(order, kvs0, kvs1, kvs2, kvs3, small, gains):
    count = kvs0.shape[0]
    total = jnp.zeros(small.shape, f32)
    for s, kvs in enumerate((kvs0, kvs1, kvs2, kvs3)):
        total = total + dot(order[:, column_block(s, count)], kvs[:, WIDE : WIDE + HD])
    small[...] = total.astype(bf16)
    gains[...] = dot_t(gain_picker(), small[...])


def attend_kernel(
    normed, cosines, sines, q_place, low_place, up_place, order, *refs, scale, pieces, heads
):
    w_q, kv, (queries, ordered, logs, kv_low, kv_up, mixed) = refs[:4], refs[4], refs[5:]
    count = w_q[0].shape[0]
    half = kv.shape[1] // 2
    for i in range(pieces):
        kv_low[i * half : (i + 1) * half, :] = kv[i, :half]
        kv_up[i * half : (i + 1) * half, :] = kv[i, half:]
    allowed_low = low_place[...] <= q_place[...]
    allowed_up = up_place[...] <= q_place[half:, :]
    for h in range(heads):
        at = slice(h * HD, (h + 1) * HD)
        place = slice(3 * HD + h * HD, 3 * HD + (h + 1) * HD)
        q = dot(normed[:, column_block(0, count)], w_q[0][:, place])
        for s in range(1, 4):
            q = q + dot(normed[:, column_block(s, count)], w_q[s][:, place])
        q = turn(q, cosines[...], sines[...]).astype(bf16)
        queries[:, at] = q
        low = jnp.where(allowed_low, dot_t(q, kv_low[:, :HD]) * scale, NEGATIVE)
        up = jnp.where(allowed_up, dot_t(q[half:], kv_up[:, :HD]) * scale, NEGATIVE)
        first, second = low[:half], low[half:]
        top = jnp.max(first, axis=-1, keepdims=True)
        weight = jnp.exp(first - top)
        total = jnp.sum(weight, axis=-1, keepdims=True)
        probs = (weight / total).astype(bf16)
        mixed[:half, at] = dot(probs, kv_low[:, HD:]).astype(bf16)
        logs[h, :half, :] = top + jnp.log(total)
        top = jnp.maximum(
            jnp.max(second, axis=-1, keepdims=True), jnp.max(up, axis=-1, keepdims=True)
        )
        weight, weight_up = jnp.exp(second - top), jnp.exp(up - top)
        total = jnp.sum(weight, axis=-1, keepdims=True) + jnp.sum(
            weight_up, axis=-1, keepdims=True
        )
        mixed[half:, at] = (
            dot((weight / total).astype(bf16), kv_low[:, HD:])
            + dot((weight_up / total).astype(bf16), kv_up[:, HD:])
        ).astype(bf16)
        logs[h, half:, :] = top + jnp.log(total)
    ordered[...] = dot(mixed[...], order[...]).astype(bf16)


def branch_kernel(mixed, w_out0, w_out1, w_out2, w_out3, own, other, w_out):
    quarter = mixed.shape[0] // 4
    count, columns = w_out0.shape[1:]
    for s, part in enumerate((w_out0, w_out1, w_out2, w_out3)):
        w_out[:, column_block(s, count)] = part[...]
    for k in range(2):
        part = dot(mixed[...], w_out[k])
        at = slice(k * columns, (k + 1) * columns)
        own[:quarter, at] = part[:quarter]
        other[:quarter, at] = part[quarter : 2 * quarter]
        own[quarter:, at] = part[2 * quarter : 3 * quarter]
        other[quarter:, at] = part[3 * quarter :]


def route_kernel(
    tokens,
    own,
    received,
    small,
    gains,
    hits,
    places_of,
    placer,
    cot_rows,
    sent,
    midway,
    moe_low,
    gates,
    parts,
):
    middle = tokens[...].astype(f32) + (own[...] + received[...])
    midway[...] = middle
    normal, _ = normal_of(middle)
    moe = (normal * gains[1:2]).astype(bf16)
    moe_low[...] = moe
    sent[:, : moe.shape[1]] = dot(placer[...], moe).astype(bf16)
    logits = dot(moe, small[...])
    picked = [
        jnp.sum(hits[k].astype(f32) * logits, axis=-1, keepdims=True) for k in range(TOPK)
    ]
    top = picked[0]
    for value in picked[1:]:
        top = jnp.maximum(top, value)
    weights = [jnp.exp(value - top) for value in picked]
    total = weights[0]
    for value in weights[1:]:
        total = total + value
    lane = lax.broadcasted_iota(jnp.int32, gates.shape, 1)
    gate_at = jnp.zeros(places_of.shape[1:], f32)
    kept = jnp.zeros(gates.shape, f32)
    for k in range(TOPK):
        gate = weights[k] / total
        kept = jnp.where(lane == k, gate, kept)
        gate_at = gate_at + places_of[k].astype(f32) * gate
    gates[...] = kept
    ones = jnp.ones(gates.shape, bf16)
    slot_gates = jnp.zeros((sent.shape[0], gates.shape[1]), f32)
    for i, part in enumerate(in_three(gate_at)):
        parts[i] = part
        slot_gates = slot_gates + t_dot(part, ones)
    sent[:, moe.shape[1] :] = (slot_gates[:, :1] * cot_rows[...].astype(f32)).astype(bf16)


def fetched(core, weights, held, sems, first):
    copies = [
        pltpu.make_async_copy(weights.at[m, core[0]], held.at[m], sems.at[m]) for m in range(3)
    ]

    @pl.when(pl.program_id(0) == 0)
    def _():
        for m in first:
            copies[m].start()

    def ready(m):
        @pl.when(pl.program_id(0) == 0)
        def _():
            copies[m].wait()

        return held[m]

    return ready


def forward_kernel(
    core, sent, weights, out, hidden, factor, other_factor, held, sems
):
    ready = fetched(core, weights, held, sems, (0, 1, 2))
    width = out.shape[1]
    rows = sent[:, :width]
    gate_pre, up_pre = dot(rows, ready(0)), dot(rows, ready(1))
    sigmoid = 1.0 / (1.0 + jnp.exp(-gate_pre))
    silu = gate_pre * sigmoid
    low = (silu * up_pre).astype(bf16)
    hidden[...] = low
    out[...] = dot_t(low, ready(2)).astype(bf16)
    factor[...] = up_pre * sigmoid * (1.0 + gate_pre * (1.0 - sigmoid))
    other_factor[...] = silu


def backward_kernel(
    core, sent, factor, other_factor, weights, rows_grad, gate_grad, up_grad, held, sems
):
    ready = fetched(core, weights, held, sems, (2, 0, 1))
    hidden_grad = dot(sent[:, rows_grad.shape[1] :], ready(2))
    low = (hidden_grad * factor[...]).astype(bf16)
    other = (hidden_grad * other_factor[...]).astype(bf16)
    gate_grad[...] = low
    up_grad[...] = other
    rows_grad[...] = (dot_t(low, ready(0)) + dot_t(other, ready(1))).astype(bf16)


def expert_call(kernel, block, core, arrays, weights, outs):
    count = arrays[0].shape[0]

    def rows(columns):
        return pl.BlockSpec((block, columns), lambda i, core: (i, 0))

    return pl.pallas_call(
        kernel,
        out_shape=[jax.ShapeDtypeStruct((count, columns), dtype) for columns, dtype in outs],
        grid_spec=pltpu.PrefetchScalarGridSpec(
            num_scalar_prefetch=1,
            grid=(count // block,),
            in_specs=[rows(a.shape[1]) for a in arrays] + [pl.BlockSpec(memory_space=pltpu.HBM)],
            out_specs=[rows(columns) for columns, _ in outs],
            scratch_shapes=[
                pltpu.VMEM((3,) + weights.shape[2:], bf16),
                pltpu.SemaphoreType.DMA((3,)),
            ],
        ),
        compiler_params=pltpu.CompilerParams(vmem_limit_bytes=ROOM),
        cost_estimate=COST,
    )(core, *arrays, weights)


def weights_kernel(sent, out_grad, hidden, gate_grad, up_grad, sums):
    rows = sent[...]
    sums[0] = t_dot(rows, gate_grad[...]).astype(bf16)
    sums[1] = t_dot(rows, up_grad[...]).astype(bf16)
    sums[2] = t_dot(out_grad[...], hidden[...]).astype(bf16)


def expert_weights_grad(sent, hidden, gate_grad, up_grad, block=256):
    count, width = sent.shape[0], sent.shape[1] // 2
    columns = hidden.shape[1]
    part = pl.BlockSpec((count, block), lambda i: (0, i))
    other_part = pl.BlockSpec((count, block), lambda i: (0, i + width // block))
    whole = pl.BlockSpec((count, columns), lambda i: (0, 0), pipeline_mode=pl.Buffered(1))
    return pl.pallas_call(
        weights_kernel,
        out_shape=jax.ShapeDtypeStruct((3, width, columns), bf16),
        grid=(width // block,),
        in_specs=[part, other_part, whole, whole, whole],
        out_specs=pl.BlockSpec((3, block, columns), lambda i: (0, i, 0)),
        compiler_params=pltpu.CompilerParams(vmem_limit_bytes=ROOM),
        cost_estimate=COST,
    )(sent, sent, hidden, gate_grad, up_grad)


def combine_kernel(
    midway, parts, returned, cot, hits, places_of, gates, small, moe_low, output, moe_part, router_grad
):
    rows = returned[...]
    output[...] = (
        midway[...] + (dot(parts[0], rows) + (dot(parts[1], rows) + dot(parts[2], rows)))
    ).astype(bf16)
    agreement = dot_t(cot[...], rows)
    lane = lax.broadcasted_iota(jnp.int32, gates.shape, 1)
    gate, grad = [], []
    mean = jnp.zeros((gates.shape[0], 1), f32)
    for k in range(TOPK):
        gate.append(jnp.sum(jnp.where(lane == k, gates[...], 0.0), axis=-1, keepdims=True))
        grad.append(jnp.sum(places_of[k].astype(f32) * agreement, axis=-1, keepdims=True))
        mean = mean + gate[k] * grad[k]
    logit_grad = jnp.zeros(gates.shape, f32)
    for k in range(TOPK):
        logit_grad = logit_grad + hits[k].astype(f32) * (gate[k] * (grad[k] - mean))
    logit_grad = logit_grad.astype(bf16)
    moe_part[...] = dot_t(logit_grad, small[...])
    router_grad[...] = t_dot(moe_low[...], logit_grad)


def home_kernel(placer_t, home, moe_part, midway, cot, gains, midway_grad, branch_low, gain_grad):
    grad = dot(placer_t[...], home[...]) + moe_part[...]
    normal, inverse = normal_of(midway[...])
    result = cot[...].astype(f32) + norm_back(grad, normal, inverse, gains[1:2])
    midway_grad[...] = result
    branch_low[...] = result.astype(bf16)
    gain_grad[...] = jnp.broadcast_to(
        jnp.sum(grad * normal, axis=0, keepdims=True), gain_grad.shape
    )


def out_grad_kernel(mixed, own, other, branch, *blocks):
    quarter = own.shape[0] // 2
    branch[:quarter] = own[:quarter]
    branch[quarter : 2 * quarter] = other[:quarter]
    branch[2 * quarter : 3 * quarter] = own[quarter:]
    branch[3 * quarter :] = other[quarter:]
    count, columns = blocks[0].shape[1:]
    for k in range(2):
        grad = t_dot(mixed[...], branch[:, column_block(k, columns)]).astype(bf16)
        for s in range(4):
            blocks[s][k] = grad[column_block(s, count)]


def attend_back_kernel(
    branch,
    w_out,
    order,
    queries,
    kv_low,
    kv_up,
    logs,
    q_place,
    low_place,
    up_place,
    cosines,
    sines,
    normed,
    dq,
    dkv,
    block0,
    block1,
    block2,
    block3,
    grads,
    acc_low,
    acc_up,
    *,
    scale,
    pieces,
    heads,
):
    half = queries.shape[0] // 2
    columns = w_out.shape[2]
    ordered = dot_t(branch[:, :columns], w_out[0]) + dot_t(branch[:, columns:], w_out[1])
    grads[...] = dot_t(ordered.astype(bf16), order[...]).astype(bf16)
    allowed_low = low_place[...] <= q_place[...]
    allowed_up = up_place[...] <= q_place[half:, :]
    key_low, value_low = kv_low[:, :HD], kv_low[:, HD:]
    key_up, value_up = kv_up[:, :HD], kv_up[:, HD:]
    for h in range(heads):
        at = slice(h * HD, (h + 1) * HD)
        q, grad, log = queries[:, at], grads[:, at], logs[h]
        low = jnp.where(allowed_low, dot_t(q, key_low) * scale, NEGATIVE)
        up = jnp.where(allowed_up, dot_t(q[half:], key_up) * scale, NEGATIVE)
        probs_low, probs_up = jnp.exp(low - log), jnp.exp(up - log[half:])
        grad_low, grad_up = dot_t(grad, value_low), dot_t(grad[half:], value_up)
        along = jnp.sum(probs_low * grad_low, axis=-1, keepdims=True)
        along_up = along[half:] + jnp.sum(probs_up * grad_up, axis=-1, keepdims=True)
        along = jnp.concatenate([along[:half], along_up])
        score_low = (probs_low * (grad_low - along)).astype(bf16)
        score_up = (probs_up * (grad_up - along_up)).astype(bf16)
        part = dot(score_low, key_low)
        part = jnp.concatenate([part[:half], part[half:] + dot(score_up, key_up)]) * scale
        dq[:, at] = turn(part, cosines[...], -sines[...]).astype(bf16)
        terms = (
            (acc_low, slice(0, HD), t_dot(q, score_low)),
            (acc_up, slice(0, HD), t_dot(q[half:], score_up)),
            (acc_low, slice(HD, 2 * HD), t_dot(grad, probs_low.astype(bf16))),
            (acc_up, slice(HD, 2 * HD), t_dot(grad[half:], probs_up.astype(bf16))),
        )
        for acc, rows, term in terms:
            if h == 0:
                acc[rows] = term
            else:
                acc[rows] += term
    for s, block in enumerate((block0, block1, block2, block3)):
        block[...] = t_dot(normed[:, column_block(s, block.shape[0])], dq[...]).astype(bf16)
    for acc, first in ((acc_low, 0), (acc_up, half)):
        dk = (acc[:HD].T * scale).astype(bf16)
        dv = acc[HD:].T.astype(bf16)
        for i in range(pieces):
            dkv[i, first : first + half, :HD] = dk[i * half : (i + 1) * half]
            dkv[i, first : first + half, HD:] = dv[i * half : (i + 1) * half]


def sum_kernel(dq, cosines, sines, *refs):
    w_in, (parts, dkv, own, other) = refs[:4], refs[4:]
    total = jnp.sum(parts[...].astype(f32), axis=0)
    dkv[:, :HD] = turn(total[:, :HD], cosines[...], -sines[...]).astype(bf16)
    dkv[:, HD:] = total[:, HD:].astype(bf16)
    quarter = own.shape[0] // 2
    for s in range(4):
        grad = dot_t(dq[...], w_in[s][:, WIDE + HD :]) + dot_t(dkv[...], w_in[s][:, :WIDE])
        at = column_block(s, w_in[s].shape[0])
        own[:quarter, at] = grad[:quarter]
        other[:quarter, at] = grad[quarter : 2 * quarter]
        own[quarter:, at] = grad[2 * quarter : 3 * quarter]
        other[quarter:, at] = grad[3 * quarter :]


def small_grad_kernel(order, router_grad, gain_grad, out):
    row = lax.broadcasted_iota(jnp.int32, gain_grad.shape, 0)
    second = jnp.where(row == 1, gain_grad[...], 0.0).astype(bf16)
    small = router_grad[...] + t_dot(second, gain_picker())
    out[...] = t_dot(order[...], small.astype(bf16))


def input_kernel(both, own, received, midway_grad, gains, order, small, normed, dkv, out, *blocks):
    grad = own[...] + received[...]
    quarter = own.shape[0] // 2
    tokens = jnp.concatenate([both[:quarter], both[2 * quarter : 3 * quarter]])
    normal, inverse = normal_of(tokens.astype(f32))
    parts = in_three(norm_back(grad, normal, inverse, gains[0:1]))
    moved = dot_t(jnp.concatenate(parts), order[...])
    count = 2 * quarter
    out[...] = midway_grad[...] + (
        moved[:count] + (moved[count : 2 * count] + moved[2 * count :])
    )
    gain_grad = jnp.sum(grad * normal, axis=0, keepdims=True)
    row = lax.broadcasted_iota(jnp.int32, gains.shape, 0)
    gain_grad = jnp.where(row == 0, gain_grad, 0.0).astype(bf16)
    small = small[...] + t_dot(gain_grad, gain_picker())
    rows = blocks[0].shape[0]
    for s, block in enumerate(blocks):
        at = column_block(s, rows)
        block[:, :WIDE] = t_dot(normed[:, at], dkv[...]).astype(bf16)
        block[:, WIDE:] = small[at].astype(bf16)


def body(
    tokens,
    cotangent,
    pair_of,
    routes,
    attn_gain,
    moe_gain,
    w_query,
    w_key,
    w_value,
    w_out,
    w_router,
    w_gate,
    w_up,
    w_down,
):
    rows = tokens.shape[1]
    half = rows // 2
    width = tokens.shape[2]
    shard = w_query.shape[1]
    ctx_count = 16
    experts = w_router.shape[2]
    columns = w_gate.shape[3]
    per_group = H // KVH
    qw = per_group * HD
    scale = 1.0 / math.sqrt(HD)
    core = lax.axis_index("core")
    ylo, z, yhi = lax.axis_index("ylo"), lax.axis_index("z"), lax.axis_index("yhi")
    x = lax.axis_index("x")
    piece_rows = 2 * shard
    slots = experts * SLOTS
    own_tokens, cot = tokens[0], cotangent[0]

    def halves(matrix):
        return [matrix[:, : matrix.shape[1] // 2], matrix[:, matrix.shape[1] // 2 :]]

    small = jnp.concatenate([w_router[0], attn_gain[0][:, None], moe_gain[0][:, None]], axis=-1)
    small = jnp.pad(small, ((0, 0), (0, 128 - experts - 2)))
    query_halves, key_halves, value_halves = halves(w_query[0]), halves(w_key[0]), halves(w_value[0])
    pairs = [
        jnp.concatenate([k, v, small, q], axis=-1)
        for k, v, q in zip(key_halves, value_halves, query_halves)
    ]
    pieces = gather_pieces(pairs, yhi, core, ("core", "yhi"), SAME, OTHER)
    out_pieces = gather_pieces(
        halves(w_out[0]), yhi, yhi, ("ylo", "core", "yhi"), OUT_SAME, OUT_OTHER
    )
    pieces = jnp.concatenate([pieces, out_pieces], axis=-1)
    pieces, x, own_tokens = together(pieces, x, own_tokens)

    plane_rows = 16 * piece_rows
    kvs_width, q_end = 3 * HD, 3 * HD + qw
    plane = spread(pieces, 16, PLANE)
    other_tokens = partner(own_tokens)
    both = jnp.concatenate(
        [own_tokens[:half], other_tokens[:half], own_tokens[half:], other_tokens[half:]]
    )
    order, out_order = order_matrix(16, x), order_matrix(8, x)
    plane, both, order, out_order, pair_of = together(plane, both, order, out_order, pair_of)

    w_in = along_x(plane[:, :, :q_end].reshape(plane_rows, q_end))
    wo = plane[:, :, q_end:].reshape(8, 2, piece_rows, width // 2).transpose(1, 0, 2, 3)
    wo = wo.reshape(2, qw // 4, width // 2)
    (both,) = call(order_kernel, [((2 * rows, width), bf16)], both, order)

    def two_cores(ctx):
        return jnp.stack([ctx + core, ctx + 1 - core], axis=-1).reshape(-1)

    ctx_here = (ylo * 4 + z) * 2
    q_place = places(pair_of, two_cores(ctx_here), rows, ctx_count)
    q_place = q_place.transpose(1, 0, 2).reshape(2 * rows, 1)
    key_place = places(
        pair_of, two_cores(jnp.arange(8, dtype=jnp.int32) * 2), rows, ctx_count
    )
    low_place, up_place = key_place[:, 0].reshape(1, -1), key_place[:, 1].reshape(1, -1)
    frequency = jnp.exp(jnp.arange(HD // 2, dtype=f32) * (-2.0 * math.log(ROPE_BASE) / HD))
    angles = q_place.astype(f32) * frequency[None, :]
    cosines, sines = jnp.cos(angles), jnp.sin(angles)
    cosines = jnp.concatenate([cosines, cosines], axis=-1)
    sines = jnp.concatenate([-sines, sines], axis=-1)
    (
        w_in, wo, both, q_place, low_place, up_place, cosines, sines, chosen, expert_shards_in,
    ) = together(
        w_in, wo, both, q_place, low_place, up_place, cosines, sines, routes[0, 0],
        jnp.stack([w_gate[0], w_up[0], w_down[0]]),
    )

    expert_weights = lax.all_gather(expert_shards_in, CTX, axis=2, tiled=True)
    wo = along_x(wo)
    normed, key_value, gains = call(
        keys_kernel,
        [((2 * rows, width), bf16), ((2 * rows, 2 * HD), bf16), ((8, width), f32)],
        both,
        cosines,
        sines,
        *w_in,
    )
    all_kv = spread(key_value, 8, RING)
    small, moe_gains = call(
        small_kernel, [((width, 128), bf16), ((8, width), f32)], order, *w_in
    )
    lanes = jnp.arange(128, dtype=jnp.int32)
    hits = (chosen.T[:, :, None] == lanes[None, None, :]).astype(bf16)
    earlier = (lanes[:, None] > lanes[None, :]).astype(bf16)
    before = dot(earlier, jnp.sum(hits, axis=0))
    slot_index = jnp.sum(hits.astype(f32) * before[None], axis=-1).astype(jnp.int32)
    target = chosen.T * SLOTS + slot_index
    slot_row = jnp.arange(slots, dtype=jnp.int32)
    places_of = (target[:, :, None] == slot_row[None, None, :]).astype(bf16)
    placer_t = jnp.sum(places_of, axis=0)
    placer = placer_t.T
    (cot_rows,) = call(order_kernel, [((slots, width), bf16)], placer, cot)
    all_kv, small, moe_gains, hits, places_of, placer_t, placer, cot_rows = together(
        all_kv, small, moe_gains, hits, places_of, placer_t, placer, cot_rows
    )

    sizes = dict(scale=scale, pieces=8, heads=per_group)
    keys = 8 * rows
    queries, mixed, logs, kv_low, kv_up = call(
        functools.partial(attend_kernel, **sizes),
        [
            ((2 * rows, qw), bf16),
            ((2 * rows, qw), bf16),
            ((per_group, 2 * rows, 1), f32),
            ((keys, 2 * HD), bf16),
            ((keys, 2 * HD), bf16),
        ],
        normed,
        cosines,
        sines,
        q_place,
        low_place,
        up_place,
        out_order,
        *w_in,
        all_kv,
        scratch=[pltpu.VMEM((2 * rows, qw), bf16)],
    )
    wo, mixed = together(wo, mixed)

    branch_own, branch_other, wo = call(
        branch_kernel,
        [((rows, width), f32), ((rows, width), f32), ((2, qw, width // 2), bf16)],
        mixed,
        *wo,
    )
    sent, midway, moe_low, gates, gate_parts = call(
        route_kernel,
        [
            ((slots, 2 * width), bf16),
            ((rows, width), f32),
            ((rows, width), bf16),
            ((rows, 128), f32),
            ((3, rows, slots), bf16),
        ],
        own_tokens,
        branch_own,
        partner(branch_other),
        small,
        moe_gains,
        hits,
        places_of,
        placer,
        cot_rows,
    )

    sent = to_owners(sent.reshape(experts, SLOTS, 2 * width)).reshape(slots, 2 * width)
    mine = core.reshape(1)
    expert_out, hidden, factor, other_factor = expert_call(
        forward_kernel,
        slots // 2,
        mine,
        [sent],
        expert_weights,
        [(width, bf16), (columns, bf16), (columns, f32), (columns, f32)],
    )
    expert_out, factor = together(expert_out, factor)

    returned = to_owners(expert_out.reshape(experts, SLOTS, width))
    rows_grad, gate_grad, up_grad = expert_call(
        backward_kernel,
        128,
        mine,
        [sent, factor, other_factor],
        expert_weights,
        [(width, bf16), (columns, bf16), (columns, bf16)],
    )
    returned, rows_grad, gate_grad, up_grad = together(returned, rows_grad, gate_grad, up_grad)

    home_grad = to_owners(rows_grad.reshape(experts, SLOTS, width))
    expert_sums = expert_weights_grad(sent, hidden, gate_grad, up_grad)
    expert_sums = lax.psum_scatter(expert_sums, RING, scatter_dimension=1, tiled=True)
    output, moe_part, router_grad = call(
        combine_kernel,
        [((rows, width), bf16), ((rows, width), f32), ((width, 128), f32)],
        midway,
        gate_parts,
        returned.reshape(slots, width),
        cot,
        hits,
        places_of,
        gates,
        small,
        moe_low,
    )
    home_grad, moe_part = together(home_grad, moe_part)
    midway_grad, branch_low, gain_two_grad = call(
        home_kernel,
        [((rows, width), f32), ((rows, width), bf16), ((8, width), f32)],
        placer_t,
        home_grad.reshape(slots, width),
        moe_part,
        midway,
        cot,
        moe_gains,
    )
    branch, *out_w_grad = call(
        out_grad_kernel,
        [((2 * rows, width), bf16)] + [((2, qw // 4, width // 2), bf16)] * 4,
        mixed,
        branch_low,
        partner(branch_low),
    )
    (small_grad,) = call(
        small_grad_kernel, [((width, 128), f32)], order, router_grad, gain_two_grad
    )
    dq, dkv, *q_w_grad = call(
        functools.partial(attend_back_kernel, **sizes),
        [((2 * rows, qw), bf16), ((8, 2 * rows, 2 * HD), bf16)]
        + [((plane_rows, qw), bf16)] * 4,
        branch,
        wo,
        out_order,
        queries,
        kv_low,
        kv_up,
        logs,
        q_place,
        low_place,
        up_place,
        cosines,
        sines,
        normed,
        scratch=[
            pltpu.VMEM((2 * rows, qw), bf16),
            pltpu.VMEM((2 * HD, keys), f32),
            pltpu.VMEM((2 * HD, keys), f32),
        ],
    )
    dkv, q_w_grad, small_grad = together(dkv, q_w_grad, small_grad)
    dkv = exchange(dkv, RING)
    q_w_grad = back_along_x(q_w_grad)
    dkv, q_w_grad, out_w_grad = together(dkv, q_w_grad, out_w_grad)

    out_w_grad = back_along_x(out_w_grad)
    dkv, normed_own, normed_other = call(
        sum_kernel,
        [((2 * rows, 2 * HD), bf16), ((rows, width), f32), ((rows, width), f32)],
        dq,
        cosines,
        sines,
        *w_in,
        dkv,
    )
    input_grad, *kvs_grad = call(
        input_kernel,
        [((rows, width), f32)] + [((plane_rows, 3 * HD), bf16)] * 4,
        both,
        normed_own,
        partner(normed_other),
        midway_grad,
        gains,
        order,
        small_grad,
        normed,
        dkv,
    )
    kvs_grad, out_w_grad, input_grad = together(kvs_grad, out_w_grad, input_grad)
    kvs_grad = back_along_x(kvs_grad)
    out_w_grad = out_w_grad.reshape(2, 8, piece_rows, width // 2).transpose(1, 0, 2, 3)
    plane_grad = jnp.concatenate(
        [
            q_w_grad.reshape(16, piece_rows, qw),
            kvs_grad.reshape(16, piece_rows, kvs_width),
            out_w_grad.reshape(16, piece_rows, width // 2),
        ],
        axis=-1,
    )
    plane_grad, expert_sums = together(plane_grad, expert_sums)
    plane_grad = exchange(plane_grad, PLANE)

    def summed(pieces):
        return jnp.sum(pieces.astype(f32), axis=0)

    def expert_shards(grad):
        count = grad.shape[1] // 2
        kept = lax.dynamic_slice_in_dim(grad, core * count, count, axis=1)
        given = partner(lax.dynamic_slice_in_dim(grad, (1 - core) * count, count, axis=1))
        both = jnp.stack([pick(core, kept, given), pick(core, given, kept)], axis=1)
        return [both[i : i + 1].astype(f32) for i in range(3)]

    w_gate_grad, w_up_grad, w_down_grad = expert_shards(expert_sums)
    plane_grad, w_gate_grad, w_up_grad, w_down_grad = together(
        plane_grad, w_gate_grad, w_up_grad, w_down_grad
    )
    plane_grad = summed(plane_grad)
    out_w_grad = scatter_pieces(
        plane_grad[:, q_end:], yhi, yhi, ("ylo", "core", "yhi"), OUT_SAME, OUT_OTHER
    )
    plane_grad = scatter_pieces(
        plane_grad[:, :q_end], yhi, core, ("core", "yhi"), SAME, OTHER
    )
    plane_grad = plane_grad.reshape(shard, 2, -1)

    def joined(first, last):
        return plane_grad[:, :, first:last].reshape(1, shard, -1)

    small_grad = jnp.sum(plane_grad[None, :, :, qw + 2 * HD :], axis=2)

    return (
        output[None],
        input_grad[None],
        small_grad[:, :, experts],
        small_grad[:, :, experts + 1],
        joined(0, qw),
        joined(qw, qw + HD),
        joined(qw + HD, qw + 2 * HD),
        out_w_grad[None],
        small_grad[:, :, :experts],
        w_gate_grad,
        w_up_grad,
        w_down_grad,
    )


def solution(mesh):
    fine = Mesh(mesh.devices.reshape(2, 4, 2, 4, 2), AXES)
    seq = P(FSDP, CTX, None)
    vector = P(None, AXES)
    matrix = P(None, AXES, None)
    expert = P(None, FSDP, CTX, None)
    in_specs = (
        seq,
        seq,
        P(),
        P(None, FSDP, CTX, None),
        vector,
        vector,
        matrix,
        matrix,
        matrix,
        matrix,
        matrix,
        expert,
        expert,
        expert,
    )
    out_specs = (
        seq,
        seq,
        vector,
        vector,
        matrix,
        matrix,
        matrix,
        matrix,
        matrix,
        expert,
        expert,
        expert,
    )
    return jax.shard_map(body, mesh=fine, in_specs=in_specs, out_specs=out_specs, check_vma=False)
```

```python
import functools
import math

import jax
import jax.numpy as jnp
from jax import lax
from jax.experimental import pallas as pl
from jax.experimental.pallas import tpu as pltpu
from jax.sharding import Mesh
from jax.sharding import PartitionSpec as P

H = 12
KVH = 2
HD = 128
TOPK = 4

EPSILON = 1e-06
ROPE_BASE = 1000000.0
NEGATIVE = -1e30

AXES = ("ylo", "z", "core", "x", "yhi")
CTX = ("ylo", "z", "core")
FSDP = ("x", "yhi")
GROUPS = [
    [
        (((group ^ yhi) * 4 + z) * 2 + core) * 8 + x * 2 + yhi
        for x in range(4)
        for yhi in range(2)
        for core in range(2)
    ]
    for group in range(2)
    for z in range(4)
]
RING = ("ylo", "z")
PLANE = ("ylo", "z", "yhi")
OUT_PLANE = ("yhi", "z", "ylo")
GROUPS = [
    [
        (((group ^ yhi) * 4 + z) * 2 + core) * 8 + x * 2 + yhi
        for x in range(4)
        for yhi in range(2)
        for core in range(2)
    ]
    for group in range(2)
    for z in range(4)
]
RING = ("ylo", "z")
ROWS_ORDER = ("ylo", "z", "yhi", "x")
OUT_ORDER = ("yhi", "z", "ylo", "x")
SLOTS = 40

bf16 = jnp.bfloat16
f32 = jnp.float32


def dot(left, right):
    return jnp.dot(left, right, preferred_element_type=f32)


def dot_t(left, right):
    return lax.dot_general(left, right, (((1,), (1,)), ((), ())), preferred_element_type=f32)


def t_dot(left, right):
    return lax.dot_general(left, right, (((0,), (0,)), ((), ())), preferred_element_type=f32)


def exchange(pieces, axes):
    return lax.all_to_all(pieces, axes, split_axis=0, concat_axis=0, tiled=True)


def to_owners(pieces):
    return lax.all_to_all(
        pieces, AXES, split_axis=0, concat_axis=0, axis_index_groups=GROUPS, tiled=True
    )


def spread(piece, count, axes):
    return exchange(jnp.broadcast_to(piece[None], (count,) + piece.shape), axes)


def after(value, earlier):
    return lax.optimization_barrier((value, earlier))[0]


def together(*values):
    return lax.optimization_barrier(values)


def partner(value):
    return lax.ppermute(value, "core", [(0, 1), (1, 0)])


def route(axes, sizes, move):
    pairs = []
    for source in range(math.prod(sizes)):
        rest, at = source, []
        for size in reversed(sizes):
            at.insert(0, rest % size)
            rest //= size
        target = 0
        for size, value in zip(sizes, move(*at)):
            target = target * size + value
        pairs.append((source, target))
    return pairs


SAME = route(("core", "yhi"), (2, 2), lambda c, h: (h, c))
OTHER = route(("core", "yhi"), (2, 2), lambda c, h: (1 - h, c))
OUT_SAME = route(("ylo", "core", "yhi"), (2, 2, 2), lambda j, c, h: (c, j, h))
OUT_OTHER = route(("ylo", "core", "yhi"), (2, 2, 2), lambda j, c, h: (c, j, 1 - h))


def back(pairs):
    return [(target, source) for source, target in pairs]


def pick(flag, if_zero, if_one):
    return jnp.where(flag == 0, if_zero, if_one)


def gather_pieces(pair, flag, key, axes, same, other):
    first = lax.ppermute(pick(flag, pair[0], pair[1]), axes, same)
    second = lax.ppermute(pick(flag, pair[1], pair[0]), axes, other)
    return pick(
        key, jnp.concatenate([first, second]), jnp.concatenate([second, first])
    )


def scatter_pieces(piece, flag, key, axes, same, other):
    count = piece.shape[0] // 2
    mine, rest = piece[:count], piece[count:]
    first = lax.ppermute(pick(key, mine, rest), axes, back(same))
    second = lax.ppermute(pick(key, rest, mine), axes, back(other))
    return pick(flag, jnp.concatenate([first, second], axis=-1), jnp.concatenate([second, first], axis=-1))


def along_x(piece):
    return [piece] + [
        lax.ppermute(piece, "x", [(i, (i + s) % 4) for i in range(4)]) for s in (1, 2, 3)
    ]


def back_along_x(blocks):
    arrived = [blocks[0]] + [
        lax.ppermute(blocks[s], "x", [(i, (i - s) % 4) for i in range(4)]) for s in (1, 2, 3)
    ]
    (total,) = call(add_kernel, [(blocks[0].shape, bf16)], *arrived, cost=LONG)
    return total


def add_kernel(first, second, third, fourth, total):
    total[...] = (
        (first[...].astype(f32) + second[...].astype(f32))
        + (third[...].astype(f32) + fourth[...].astype(f32))
    ).astype(bf16)


def order_matrix(groups, x):
    index = jnp.arange(groups * 96, dtype=jnp.int32)
    turn_of, group, row = index // (groups * 24), index // 24 % groups, index % 24
    own = group * 96 + (x - turn_of) % 4 * 24 + row
    return (index[:, None] == own[None, :]).astype(bf16)


def places(pair_of, ctx, row_count, ctx_count):
    half_size = row_count // 2
    pair = jnp.sum(
        jnp.where(ctx[:, None] == jnp.arange(ctx_count, dtype=jnp.int32)[None], pair_of[None], 0),
        axis=1,
    )
    block = jnp.stack([pair, 2 * ctx_count - 1 - pair], axis=1)
    return block[:, :, None] * half_size + jnp.arange(half_size, dtype=jnp.int32)[None, None]


def in_three(value):
    high = value.astype(bf16)
    rest = value - high.astype(f32)
    middle = rest.astype(bf16)
    return [high, middle, (rest - middle.astype(f32)).astype(bf16)]


def call(kernel, outs, *args, scratch=(), cost=None):
    def whole(shape):
        return pl.BlockSpec(shape, lambda i: (0,) * len(shape))

    return pl.pallas_call(
        kernel,
        out_shape=[jax.ShapeDtypeStruct(shape, dtype) for shape, dtype in outs],
        grid=(1,),
        in_specs=[whole(a.shape) for a in args],
        out_specs=[whole(shape) for shape, _ in outs],
        scratch_shapes=list(scratch),
        compiler_params=pltpu.CompilerParams(vmem_limit_bytes=ROOM),
        cost_estimate=COST if cost is None else cost,
    )(*args)


ROOM = 58 << 20
COST = pl.CostEstimate(flops=1 << 20, bytes_accessed=1 << 18, transcendentals=0)
LONG = pl.CostEstimate(flops=1 << 35, bytes_accessed=1 << 27, transcendentals=0)
WIDE = 2 * HD
EXPERTS = 16


def turn(vectors, cosines, sines):
    return vectors * cosines + pltpu.roll(vectors, HD // 2, axis=1) * sines


def gain_picker():
    row = lax.broadcasted_iota(jnp.int32, (8, 128), 0)
    column = lax.broadcasted_iota(jnp.int32, (8, 128), 1)
    return jnp.where((column == row + EXPERTS) & (row < 2), 1.0, 0.0).astype(bf16)


def normal_of(stream):
    inverse = lax.rsqrt(jnp.mean(stream * stream, axis=-1, keepdims=True) + EPSILON)
    return stream * inverse, inverse


def norm_back(grad, normal, inverse, gain):
    scaled = grad * gain
    return inverse * (scaled - normal * jnp.mean(scaled * normal, axis=-1, keepdims=True))


def column_block(s, count):
    return slice(s * count, (s + 1) * count)


def order_kernel(rows, order, out):
    out[...] = dot(rows[...], order[...]).astype(bf16)


def keys_kernel(both, cosines, sines, *refs):
    kvs, (normed, key_value, gains) = refs[:4], refs[4:]
    count = kvs[0].shape[0]
    for s in range(4):
        gains[:, column_block(s, count)] = dot_t(gain_picker(), kvs[s][:, WIDE:])
    normal, _ = normal_of(both[...].astype(f32))
    normed[...] = (normal * gains[0:1]).astype(bf16)
    kv = dot(normed[:, column_block(0, count)], kvs[0][:, :WIDE])
    for s in range(1, 4):
        kv = kv + dot(normed[:, column_block(s, count)], kvs[s][:, :WIDE])
    key_value[:, :HD] = turn(kv[:, :HD], cosines[...], sines[...]).astype(bf16)
    key_value[:, HD:] = kv[:, HD:].astype(bf16)


def small_kernel(order, kvs0, kvs1, kvs2, kvs3, small, gains):
    count = kvs0.shape[0]
    total = jnp.zeros(small.shape, f32)
    for s, kvs in enumerate((kvs0, kvs1, kvs2, kvs3)):
        total = total + dot(order[:, column_block(s, count)], kvs[:, WIDE:])
    small[...] = total.astype(bf16)
    gains[...] = dot_t(gain_picker(), small[...])


def query_kernel(normed, cosines, sines, w_q0, w_q1, w_q2, w_q3, queries):
    w_q = (w_q0, w_q1, w_q2, w_q3)
    count = w_q0.shape[0]
    for h in range(queries.shape[1] // HD):
        at = column_block(h, HD)
        q = dot(normed[:, column_block(0, count)], w_q0[:, at])
        for s in range(1, 4):
            q = q + dot(normed[:, column_block(s, count)], w_q[s][:, at])
        queries[:, at] = turn(q, cosines[...], sines[...]).astype(bf16)


def attend_kernel(
    queries,
    q_place,
    low_place,
    up_place,
    order,
    kv,
    ordered,
    logs,
    kv_low,
    kv_up,
    mixed,
    *,
    scale,
    pieces,
    heads,
):
    half = kv.shape[1] // 2
    for i in range(pieces):
        kv_low[i * half : (i + 1) * half, :] = kv[i, :half]
        kv_up[i * half : (i + 1) * half, :] = kv[i, half:]
    allowed_low = low_place[...] <= q_place[...]
    allowed_up = up_place[...] <= q_place[half:, :]
    for h in range(heads):
        at = slice(h * HD, (h + 1) * HD)
        q = queries[:, at]
        low = jnp.where(allowed_low, dot_t(q, kv_low[:, :HD]) * scale, NEGATIVE)
        up = jnp.where(allowed_up, dot_t(q[half:], kv_up[:, :HD]) * scale, NEGATIVE)
        first, second = low[:half], low[half:]
        top = jnp.max(first, axis=-1, keepdims=True)
        weight = jnp.exp(first - top)
        total = jnp.sum(weight, axis=-1, keepdims=True)
        probs = (weight / total).astype(bf16)
        mixed[:half, at] = dot(probs, kv_low[:, HD:]).astype(bf16)
        logs[h, :half, :] = top + jnp.log(total)
        top = jnp.maximum(
            jnp.max(second, axis=-1, keepdims=True), jnp.max(up, axis=-1, keepdims=True)
        )
        weight, weight_up = jnp.exp(second - top), jnp.exp(up - top)
        total = jnp.sum(weight, axis=-1, keepdims=True) + jnp.sum(
            weight_up, axis=-1, keepdims=True
        )
        mixed[half:, at] = (
            dot((weight / total).astype(bf16), kv_low[:, HD:])
            + dot((weight_up / total).astype(bf16), kv_up[:, HD:])
        ).astype(bf16)
        logs[h, half:, :] = top + jnp.log(total)
    ordered[...] = dot(mixed[...], order[...]).astype(bf16)


def branch_kernel(mixed, w_out0, w_out1, w_out2, w_out3, own, other, w_out):
    quarter = mixed.shape[0] // 4
    count, columns = w_out0.shape[1:]
    for s, part in enumerate((w_out0, w_out1, w_out2, w_out3)):
        w_out[:, column_block(s, count)] = part[...]
    for k in range(2):
        part = dot(mixed[...], w_out[k])
        at = slice(k * columns, (k + 1) * columns)
        own[:quarter, at] = part[:quarter]
        other[:quarter, at] = part[quarter : 2 * quarter]
        own[quarter:, at] = part[2 * quarter : 3 * quarter]
        other[quarter:, at] = part[3 * quarter :]


def route_kernel(
    tokens,
    own,
    received,
    small,
    gains,
    hits,
    places_of,
    placer,
    cot_rows,
    sent,
    midway,
    moe_low,
    gates,
    parts,
):
    middle = tokens[...].astype(f32) + (own[...] + received[...])
    midway[...] = middle
    normal, _ = normal_of(middle)
    moe = (normal * gains[1:2]).astype(bf16)
    moe_low[...] = moe
    sent[:, : moe.shape[1]] = dot(placer[...], moe).astype(bf16)
    logits = dot(moe, small[...])
    picked = [
        jnp.sum(hits[k].astype(f32) * logits, axis=-1, keepdims=True) for k in range(TOPK)
    ]
    top = picked[0]
    for value in picked[1:]:
        top = jnp.maximum(top, value)
    weights = [jnp.exp(value - top) for value in picked]
    total = weights[0]
    for value in weights[1:]:
        total = total + value
    lane = lax.broadcasted_iota(jnp.int32, gates.shape, 1)
    gate_at = jnp.zeros(places_of.shape[1:], f32)
    kept = jnp.zeros(gates.shape, f32)
    for k in range(TOPK):
        gate = weights[k] / total
        kept = jnp.where(lane == k, gate, kept)
        gate_at = gate_at + places_of[k].astype(f32) * gate
    gates[...] = kept
    ones = jnp.ones(gates.shape, bf16)
    slot_gates = jnp.zeros((sent.shape[0], gates.shape[1]), f32)
    for i, part in enumerate(in_three(gate_at)):
        parts[i] = part
        slot_gates = slot_gates + t_dot(part, ones)
    sent[:, moe.shape[1] :] = (slot_gates[:, :1] * cot_rows[...].astype(f32)).astype(bf16)


def fetched(core, weights, held, sems, first):
    copies = [
        pltpu.make_async_copy(weights.at[m, core[0]], held.at[m], sems.at[m]) for m in range(3)
    ]

    @pl.when(pl.program_id(0) == 0)
    def _():
        for m in first:
            copies[m].start()

    def ready(m):
        @pl.when(pl.program_id(0) == 0)
        def _():
            copies[m].wait()

        return held[m]

    return ready


def forward_kernel(
    core, sent, weights, out, hidden, factor, other_factor, held, sems
):
    ready = fetched(core, weights, held, sems, (0, 1, 2))
    width = out.shape[1]
    rows = sent[:, :width]
    gate_pre, up_pre = dot(rows, ready(0)), dot(rows, ready(1))
    sigmoid = 1.0 / (1.0 + jnp.exp(-gate_pre))
    silu = gate_pre * sigmoid
    low = (silu * up_pre).astype(bf16)
    hidden[...] = low
    out[...] = dot_t(low, ready(2)).astype(bf16)
    factor[...] = up_pre * sigmoid * (1.0 + gate_pre * (1.0 - sigmoid))
    other_factor[...] = silu


def backward_kernel(
    core, sent, factor, other_factor, weights, rows_grad, gate_grad, up_grad, held, sems
):
    ready = fetched(core, weights, held, sems, (2, 0, 1))
    hidden_grad = dot(sent[:, rows_grad.shape[1] :], ready(2))
    low = (hidden_grad * factor[...]).astype(bf16)
    other = (hidden_grad * other_factor[...]).astype(bf16)
    gate_grad[...] = low
    up_grad[...] = other
    rows_grad[...] = (dot_t(low, ready(0)) + dot_t(other, ready(1))).astype(bf16)


def expert_call(kernel, block, core, arrays, weights, outs):
    count = arrays[0].shape[0]

    def rows(columns):
        return pl.BlockSpec((block, columns), lambda i, core: (i, 0))

    return pl.pallas_call(
        kernel,
        out_shape=[jax.ShapeDtypeStruct((count, columns), dtype) for columns, dtype in outs],
        grid_spec=pltpu.PrefetchScalarGridSpec(
            num_scalar_prefetch=1,
            grid=(count // block,),
            in_specs=[rows(a.shape[1]) for a in arrays] + [pl.BlockSpec(memory_space=pltpu.HBM)],
            out_specs=[rows(columns) for columns, _ in outs],
            scratch_shapes=[
                pltpu.VMEM((3,) + weights.shape[2:], bf16),
                pltpu.SemaphoreType.DMA((3,)),
            ],
        ),
        compiler_params=pltpu.CompilerParams(vmem_limit_bytes=ROOM),
        cost_estimate=COST,
    )(core, *arrays, weights)


def weights_kernel(sent, out_grad, hidden, gate_grad, up_grad, sums):
    rows = sent[...]
    sums[0] = t_dot(rows, gate_grad[...]).astype(bf16)
    sums[1] = t_dot(rows, up_grad[...]).astype(bf16)
    sums[2] = t_dot(out_grad[...], hidden[...]).astype(bf16)


def expert_weights_grad(sent, hidden, gate_grad, up_grad, block=256):
    count, width = sent.shape[0], sent.shape[1] // 2
    columns = hidden.shape[1]
    part = pl.BlockSpec((count, block), lambda i: (0, i))
    other_part = pl.BlockSpec((count, block), lambda i: (0, i + width // block))
    whole = pl.BlockSpec((count, columns), lambda i: (0, 0), pipeline_mode=pl.Buffered(1))
    return pl.pallas_call(
        weights_kernel,
        out_shape=jax.ShapeDtypeStruct((3, width, columns), bf16),
        grid=(width // block,),
        in_specs=[part, other_part, whole, whole, whole],
        out_specs=pl.BlockSpec((3, block, columns), lambda i: (0, i, 0)),
        compiler_params=pltpu.CompilerParams(vmem_limit_bytes=ROOM),
        cost_estimate=COST,
    )(sent, sent, hidden, gate_grad, up_grad)


def combine_kernel(
    midway, parts, returned, cot, hits, places_of, gates, small, moe_low, output, moe_part, router_grad
):
    rows = returned[...]
    output[...] = (
        midway[...] + (dot(parts[0], rows) + (dot(parts[1], rows) + dot(parts[2], rows)))
    ).astype(bf16)
    agreement = dot_t(cot[...], rows)
    lane = lax.broadcasted_iota(jnp.int32, gates.shape, 1)
    gate, grad = [], []
    mean = jnp.zeros((gates.shape[0], 1), f32)
    for k in range(TOPK):
        gate.append(jnp.sum(jnp.where(lane == k, gates[...], 0.0), axis=-1, keepdims=True))
        grad.append(jnp.sum(places_of[k].astype(f32) * agreement, axis=-1, keepdims=True))
        mean = mean + gate[k] * grad[k]
    logit_grad = jnp.zeros(gates.shape, f32)
    for k in range(TOPK):
        logit_grad = logit_grad + hits[k].astype(f32) * (gate[k] * (grad[k] - mean))
    logit_grad = logit_grad.astype(bf16)
    moe_part[...] = dot_t(logit_grad, small[...])
    router_grad[...] = t_dot(moe_low[...], logit_grad)


def home_kernel(placer_t, home, moe_part, midway, cot, gains, midway_grad, branch_low, gain_grad):
    grad = dot(placer_t[...], home[...]) + moe_part[...]
    normal, inverse = normal_of(midway[...])
    result = cot[...].astype(f32) + norm_back(grad, normal, inverse, gains[1:2])
    midway_grad[...] = result
    branch_low[...] = result.astype(bf16)
    gain_grad[...] = jnp.broadcast_to(
        jnp.sum(grad * normal, axis=0, keepdims=True), gain_grad.shape
    )


def out_grad_kernel(mixed, own, other, branch, *blocks):
    quarter = own.shape[0] // 2
    branch[:quarter] = own[:quarter]
    branch[quarter : 2 * quarter] = other[:quarter]
    branch[2 * quarter : 3 * quarter] = own[quarter:]
    branch[3 * quarter :] = other[quarter:]
    count, columns = blocks[0].shape[1:]
    for k in range(2):
        grad = t_dot(mixed[...], branch[:, column_block(k, columns)]).astype(bf16)
        for s in range(4):
            blocks[s][k] = grad[column_block(s, count)]


def attend_back_kernel(
    branch,
    w_out,
    order,
    queries,
    kv_low,
    kv_up,
    logs,
    q_place,
    low_place,
    up_place,
    cosines,
    sines,
    normed,
    dq,
    dkv,
    block0,
    block1,
    block2,
    block3,
    grads,
    acc_low,
    acc_up,
    *,
    scale,
    pieces,
    heads,
):
    half = queries.shape[0] // 2
    columns = w_out.shape[2]
    ordered = dot_t(branch[:, :columns], w_out[0]) + dot_t(branch[:, columns:], w_out[1])
    grads[...] = dot_t(ordered.astype(bf16), order[...]).astype(bf16)
    allowed_low = low_place[...] <= q_place[...]
    allowed_up = up_place[...] <= q_place[half:, :]
    key_low, value_low = kv_low[:, :HD], kv_low[:, HD:]
    key_up, value_up = kv_up[:, :HD], kv_up[:, HD:]
    for h in range(heads):
        at = slice(h * HD, (h + 1) * HD)
        q, grad, log = queries[:, at], grads[:, at], logs[h]
        low = jnp.where(allowed_low, dot_t(q, key_low) * scale, NEGATIVE)
        up = jnp.where(allowed_up, dot_t(q[half:], key_up) * scale, NEGATIVE)
        probs_low, probs_up = jnp.exp(low - log), jnp.exp(up - log[half:])
        grad_low, grad_up = dot_t(grad, value_low), dot_t(grad[half:], value_up)
        along = jnp.sum(probs_low * grad_low, axis=-1, keepdims=True)
        along_up = along[half:] + jnp.sum(probs_up * grad_up, axis=-1, keepdims=True)
        along = jnp.concatenate([along[:half], along_up])
        score_low = (probs_low * (grad_low - along)).astype(bf16)
        score_up = (probs_up * (grad_up - along_up)).astype(bf16)
        part = dot(score_low, key_low)
        part = jnp.concatenate([part[:half], part[half:] + dot(score_up, key_up)]) * scale
        dq[:, at] = turn(part, cosines[...], -sines[...]).astype(bf16)
        terms = (
            (acc_low, slice(0, HD), t_dot(q, score_low)),
            (acc_up, slice(0, HD), t_dot(q[half:], score_up)),
            (acc_low, slice(HD, 2 * HD), t_dot(grad, probs_low.astype(bf16))),
            (acc_up, slice(HD, 2 * HD), t_dot(grad[half:], probs_up.astype(bf16))),
        )
        for acc, rows, term in terms:
            if h == 0:
                acc[rows] = term
            else:
                acc[rows] += term
    for s, block in enumerate((block0, block1, block2, block3)):
        block[...] = t_dot(normed[:, column_block(s, block.shape[0])], dq[...]).astype(bf16)
    for acc, first in ((acc_low, 0), (acc_up, half)):
        dk = (acc[:HD].T * scale).astype(bf16)
        dv = acc[HD:].T.astype(bf16)
        for i in range(pieces):
            dkv[i, first : first + half, :HD] = dk[i * half : (i + 1) * half]
            dkv[i, first : first + half, HD:] = dv[i * half : (i + 1) * half]


def sum_kernel(dq, cosines, sines, *refs):
    w_q, kvs, (parts, dkv, own, other) = refs[:4], refs[4:8], refs[8:]
    total = jnp.sum(parts[...].astype(f32), axis=0)
    dkv[:, :HD] = turn(total[:, :HD], cosines[...], -sines[...]).astype(bf16)
    dkv[:, HD:] = total[:, HD:].astype(bf16)
    quarter = own.shape[0] // 2
    for s in range(4):
        grad = dot_t(dq[...], w_q[s][...]) + dot_t(dkv[...], kvs[s][:, :WIDE])
        at = column_block(s, w_q[s].shape[0])
        own[:quarter, at] = grad[:quarter]
        other[:quarter, at] = grad[quarter : 2 * quarter]
        own[quarter:, at] = grad[2 * quarter : 3 * quarter]
        other[quarter:, at] = grad[3 * quarter :]


def small_grad_kernel(order, router_grad, gain_grad, out):
    row = lax.broadcasted_iota(jnp.int32, gain_grad.shape, 0)
    second = jnp.where(row == 1, gain_grad[...], 0.0).astype(bf16)
    small = router_grad[...] + t_dot(second, gain_picker())
    out[...] = t_dot(order[...], small.astype(bf16))


def input_kernel(both, own, received, midway_grad, gains, order, small, normed, dkv, out, *blocks):
    grad = own[...] + received[...]
    quarter = own.shape[0] // 2
    tokens = jnp.concatenate([both[:quarter], both[2 * quarter : 3 * quarter]])
    normal, inverse = normal_of(tokens.astype(f32))
    parts = in_three(norm_back(grad, normal, inverse, gains[0:1]))
    moved = dot_t(jnp.concatenate(parts), order[...])
    count = 2 * quarter
    out[...] = midway_grad[...] + (
        moved[:count] + (moved[count : 2 * count] + moved[2 * count :])
    )
    gain_grad = jnp.sum(grad * normal, axis=0, keepdims=True)
    row = lax.broadcasted_iota(jnp.int32, gains.shape, 0)
    gain_grad = jnp.where(row == 0, gain_grad, 0.0).astype(bf16)
    small = small[...] + t_dot(gain_grad, gain_picker())
    rows = blocks[0].shape[0]
    for s, block in enumerate(blocks):
        at = column_block(s, rows)
        block[:, :WIDE] = t_dot(normed[:, at], dkv[...]).astype(bf16)
        block[:, WIDE:] = small[at].astype(bf16)


def body(
    tokens,
    cotangent,
    pair_of,
    routes,
    attn_gain,
    moe_gain,
    w_query,
    w_key,
    w_value,
    w_out,
    w_router,
    w_gate,
    w_up,
    w_down,
):
    rows = tokens.shape[1]
    half = rows // 2
    width = tokens.shape[2]
    shard = w_query.shape[1]
    ctx_count = 16
    experts = w_router.shape[2]
    columns = w_gate.shape[3]
    per_group = H // KVH
    qw = per_group * HD
    scale = 1.0 / math.sqrt(HD)
    core = lax.axis_index("core")
    ylo, z, yhi = lax.axis_index("ylo"), lax.axis_index("z"), lax.axis_index("yhi")
    x = lax.axis_index("x")
    piece_rows = 2 * shard
    slots = experts * SLOTS
    own_tokens, cot = tokens[0], cotangent[0]

    def halves(matrix):
        return [matrix[:, : matrix.shape[1] // 2], matrix[:, matrix.shape[1] // 2 :]]

    small = jnp.concatenate([w_router[0], attn_gain[0][:, None], moe_gain[0][:, None]], axis=-1)
    small = jnp.pad(small, ((0, 0), (0, 128 - experts - 2)))
    query_halves, key_halves, value_halves = halves(w_query[0]), halves(w_key[0]), halves(w_value[0])
    pairs = [
        jnp.concatenate([k, v, small, q], axis=-1)
        for k, v, q in zip(key_halves, value_halves, query_halves)
    ]
    pieces = gather_pieces(pairs, yhi, core, ("core", "yhi"), SAME, OTHER)
    pieces, x, own_tokens, out_halves, pair_of = together(
        pieces, x, own_tokens, w_out[0], pair_of
    )

    plane_rows = 16 * piece_rows
    plane = spread(pieces, 16, PLANE)
    other_tokens = partner(own_tokens)
    both = jnp.concatenate(
        [own_tokens[:half], other_tokens[:half], own_tokens[half:], other_tokens[half:]]
    )
    out_pieces = gather_pieces(
        halves(out_halves), yhi, yhi, ("ylo", "core", "yhi"), OUT_SAME, OUT_OTHER
    )
    order, out_order = order_matrix(16, x), order_matrix(8, x)
    plane, both, out_pieces, order, out_order, pair_of = together(
        plane, both, out_pieces, order, out_order, pair_of
    )

    plane = plane.reshape(plane_rows, -1)
    w_kvs = along_x(plane[:, : 3 * HD])
    wo = spread(out_pieces, 16, OUT_PLANE)
    (both,) = call(order_kernel, [((2 * rows, width), bf16)], both, order)

    def two_cores(ctx):
        return jnp.stack([ctx + core, ctx + 1 - core], axis=-1).reshape(-1)

    ctx_here = (ylo * 4 + z) * 2
    q_place = places(pair_of, two_cores(ctx_here), rows, ctx_count)
    q_place = q_place.transpose(1, 0, 2).reshape(2 * rows, 1)
    key_place = places(
        pair_of, two_cores(jnp.arange(8, dtype=jnp.int32) * 2), rows, ctx_count
    )
    low_place, up_place = key_place[:, 0].reshape(1, -1), key_place[:, 1].reshape(1, -1)
    frequency = jnp.exp(jnp.arange(HD // 2, dtype=f32) * (-2.0 * math.log(ROPE_BASE) / HD))
    angles = q_place.astype(f32) * frequency[None, :]
    cosines, sines = jnp.cos(angles), jnp.sin(angles)
    cosines = jnp.concatenate([cosines, cosines], axis=-1)
    sines = jnp.concatenate([-sines, sines], axis=-1)
    w_q, w_kvs, wo, both, q_place, low_place, up_place, cosines, sines, chosen = together(
        plane[:, 3 * HD :], w_kvs, wo, both, q_place, low_place, up_place, cosines, sines, routes[0, 0]
    )

    w_q = along_x(w_q)
    normed, key_value, gains = call(
        keys_kernel,
        [((2 * rows, width), bf16), ((2 * rows, 2 * HD), bf16), ((8, width), f32)],
        both,
        cosines,
        sines,
        *w_kvs,
    )
    all_kv = spread(key_value, 8, RING)
    small, moe_gains = call(
        small_kernel, [((width, 128), bf16), ((8, width), f32)], order, *w_kvs
    )
    lanes = jnp.arange(128, dtype=jnp.int32)
    hits = (chosen.T[:, :, None] == lanes[None, None, :]).astype(bf16)
    earlier = (lanes[:, None] > lanes[None, :]).astype(bf16)
    before = dot(earlier, jnp.sum(hits, axis=0))
    slot_index = jnp.sum(hits.astype(f32) * before[None], axis=-1).astype(jnp.int32)
    target = chosen.T * SLOTS + slot_index
    slot_row = jnp.arange(slots, dtype=jnp.int32)
    places_of = (target[:, :, None] == slot_row[None, None, :]).astype(bf16)
    placer_t = jnp.sum(places_of, axis=0)
    placer = placer_t.T
    (cot_rows,) = call(order_kernel, [((slots, width), bf16)], placer, cot)
    (queries,) = call(
        query_kernel, [((2 * rows, qw), bf16)], normed, cosines, sines, *w_q, cost=LONG
    )
    expert_shards_in = jnp.stack([w_gate[0], w_up[0], w_down[0]])
    (
        queries, all_kv, small, moe_gains, hits, places_of, placer_t, placer, cot_rows,
        expert_shards_in,
    ) = together(
        queries, all_kv, small, moe_gains, hits, places_of, placer_t, placer, cot_rows,
        expert_shards_in,
    )

    wo = along_x(wo.reshape(2, qw // 4, width // 2))
    expert_weights = lax.all_gather(expert_shards_in, CTX, axis=2, tiled=True)
    sizes = dict(scale=scale, pieces=8, heads=per_group)
    keys = 8 * rows
    mixed, logs, kv_low, kv_up = call(
        functools.partial(attend_kernel, **sizes),
        [
            ((2 * rows, qw), bf16),
            ((per_group, 2 * rows, 1), f32),
            ((keys, 2 * HD), bf16),
            ((keys, 2 * HD), bf16),
        ],
        queries,
        q_place,
        low_place,
        up_place,
        out_order,
        all_kv,
        scratch=[pltpu.VMEM((2 * rows, qw), bf16)],
    )
    wo, mixed = together(wo, mixed)

    branch_own, branch_other, wo = call(
        branch_kernel,
        [((rows, width), f32), ((rows, width), f32), ((2, qw, width // 2), bf16)],
        mixed,
        *wo,
    )
    sent, midway, moe_low, gates, gate_parts = call(
        route_kernel,
        [
            ((slots, 2 * width), bf16),
            ((rows, width), f32),
            ((rows, width), bf16),
            ((rows, 128), f32),
            ((3, rows, slots), bf16),
        ],
        own_tokens,
        branch_own,
        partner(branch_other),
        small,
        moe_gains,
        hits,
        places_of,
        placer,
        cot_rows,
    )

    sent = to_owners(sent.reshape(experts, SLOTS, 2 * width)).reshape(slots, 2 * width)
    mine = core.reshape(1)
    expert_out, hidden, factor, other_factor = expert_call(
        forward_kernel,
        slots // 2,
        mine,
        [sent],
        expert_weights,
        [(width, bf16), (columns, bf16), (columns, f32), (columns, f32)],
    )
    expert_out, factor = together(expert_out, factor)

    returned = to_owners(expert_out.reshape(experts, SLOTS, width))
    rows_grad, gate_grad, up_grad = expert_call(
        backward_kernel,
        128,
        mine,
        [sent, factor, other_factor],
        expert_weights,
        [(width, bf16), (columns, bf16), (columns, bf16)],
    )
    expert_sums = expert_weights_grad(sent, hidden, gate_grad, up_grad)
    returned, rows_grad, expert_sums = together(returned, rows_grad, expert_sums)
    home_grad = to_owners(rows_grad.reshape(experts, SLOTS, width))
    expert_sums = lax.psum_scatter(expert_sums, RING, scatter_dimension=1, tiled=True)
    output, moe_part, router_grad = call(
        combine_kernel,
        [((rows, width), bf16), ((rows, width), f32), ((width, 128), f32)],
        midway,
        gate_parts,
        returned.reshape(slots, width),
        cot,
        hits,
        places_of,
        gates,
        small,
        moe_low,
    )
    home_grad, moe_part = together(home_grad, moe_part)
    midway_grad, branch_low, gain_two_grad = call(
        home_kernel,
        [((rows, width), f32), ((rows, width), bf16), ((8, width), f32)],
        placer_t,
        home_grad.reshape(slots, width),
        moe_part,
        midway,
        cot,
        moe_gains,
    )
    branch, *out_w_grad = call(
        out_grad_kernel,
        [((2 * rows, width), bf16)] + [((2, qw // 4, width // 2), bf16)] * 4,
        mixed,
        branch_low,
        partner(branch_low),
    )
    branch, out_w_grad = together(branch, out_w_grad)
    out_w_grad = back_along_x(out_w_grad)

    dq, dkv, *q_w_grad = call(
        functools.partial(attend_back_kernel, **sizes),
        [((2 * rows, qw), bf16), ((8, 2 * rows, 2 * HD), bf16)]
        + [((plane_rows, qw), bf16)] * 4,
        branch,
        wo,
        out_order,
        queries,
        kv_low,
        kv_up,
        logs,
        q_place,
        low_place,
        up_place,
        cosines,
        sines,
        normed,
        scratch=[
            pltpu.VMEM((2 * rows, qw), bf16),
            pltpu.VMEM((2 * HD, keys), f32),
            pltpu.VMEM((2 * HD, keys), f32),
        ],
    )
    dkv = exchange(dkv, RING)
    q_w_grad = back_along_x(q_w_grad)
    (small_grad,) = call(
        small_grad_kernel, [((width, 128), f32)], order, router_grad, gain_two_grad
    )
    dkv, out_w_grad, small_grad = together(dkv, out_w_grad, small_grad)

    dkv, normed_own, normed_other = call(
        sum_kernel,
        [((2 * rows, 2 * HD), bf16), ((rows, width), f32), ((rows, width), f32)],
        dq,
        cosines,
        sines,
        *w_q,
        *w_kvs,
        dkv,
    )
    dkv, normed_own, normed_other, q_w_grad = together(dkv, normed_own, normed_other, q_w_grad)
    input_grad, *kvs_grad = call(
        input_kernel,
        [((rows, width), f32)] + [((plane_rows, 3 * HD), bf16)] * 4,
        both,
        normed_own,
        partner(normed_other),
        midway_grad,
        gains,
        order,
        small_grad,
        normed,
        dkv,
    )
    kvs_grad, out_w_grad, input_grad = together(kvs_grad, out_w_grad, input_grad)

    out_w_grad = exchange(out_w_grad.reshape(16, piece_rows, width // 2), OUT_PLANE)
    kvs_grad = back_along_x(kvs_grad)
    plane_grad = jnp.concatenate([q_w_grad, kvs_grad], axis=-1)
    plane_grad, out_w_grad, expert_sums = together(plane_grad, out_w_grad, expert_sums)
    plane_grad = exchange(plane_grad.reshape(16, piece_rows, qw + 3 * HD), PLANE)

    def summed(pieces):
        return jnp.sum(pieces.astype(f32), axis=0)

    def expert_shards(grad):
        count = grad.shape[1] // 2
        kept = lax.dynamic_slice_in_dim(grad, core * count, count, axis=1)
        given = partner(lax.dynamic_slice_in_dim(grad, (1 - core) * count, count, axis=1))
        both = jnp.stack([pick(core, kept, given), pick(core, given, kept)], axis=1)
        return [both[i : i + 1].astype(f32) for i in range(3)]

    out_w_grad = scatter_pieces(
        summed(out_w_grad), yhi, yhi, ("ylo", "core", "yhi"), OUT_SAME, OUT_OTHER
    )
    w_gate_grad, w_up_grad, w_down_grad = expert_shards(expert_sums)
    plane_grad, out_w_grad, w_gate_grad, w_up_grad, w_down_grad = together(
        plane_grad, out_w_grad, w_gate_grad, w_up_grad, w_down_grad
    )
    plane_grad = scatter_pieces(summed(plane_grad), yhi, core, ("core", "yhi"), SAME, OTHER)
    plane_grad = plane_grad.reshape(shard, 2, -1)

    def joined(first, last):
        return plane_grad[:, :, first:last].reshape(1, shard, -1)

    small_grad = jnp.sum(plane_grad[None, :, :, qw + 2 * HD :], axis=2)

    return (
        output[None],
        input_grad[None],
        small_grad[:, :, experts],
        small_grad[:, :, experts + 1],
        joined(0, qw),
        joined(qw, qw + HD),
        joined(qw + HD, qw + 2 * HD),
        out_w_grad[None],
        small_grad[:, :, :experts],
        w_gate_grad,
        w_up_grad,
        w_down_grad,
    )


def solution(mesh):
    fine = Mesh(mesh.devices.reshape(2, 4, 2, 4, 2), AXES)
    seq = P(FSDP, CTX, None)
    vector = P(None, AXES)
    matrix = P(None, AXES, None)
    expert = P(None, FSDP, CTX, None)
    in_specs = (
        seq,
        seq,
        P(),
        P(None, FSDP, CTX, None),
        vector,
        vector,
        matrix,
        matrix,
        matrix,
        matrix,
        matrix,
        expert,
        expert,
        expert,
    )
    out_specs = (
        seq,
        seq,
        vector,
        vector,
        matrix,
        matrix,
        matrix,
        matrix,
        matrix,
        expert,
        expert,
        expert,
    )
    return jax.shard_map(body, mesh=fine, in_specs=in_specs, out_specs=out_specs, check_vma=False)
```

```python
import functools
import math

import jax
import jax.numpy as jnp
from jax import lax
from jax.experimental import pallas as pl
from jax.experimental.pallas import tpu as pltpu
from jax.sharding import Mesh
from jax.sharding import PartitionSpec as P

H = 12
KVH = 2
HD = 128
TOPK = 4

EPSILON = 1e-06
ROPE_BASE = 1000000.0
NEGATIVE = -1e30

AXES = ("ylo", "z", "core", "x", "yhi")
CTX = ("ylo", "z", "core")
FSDP = ("x", "yhi")
GROUPS = [
    [
        (((group ^ yhi) * 4 + z) * 2 + core) * 8 + x * 2 + yhi
        for x in range(4)
        for yhi in range(2)
        for core in range(2)
    ]
    for group in range(2)
    for z in range(4)
]
RING = ("ylo", "z")
PLANE = ("ylo", "z", "yhi")
OUT_PLANE = ("yhi", "z", "ylo")
LEVEL = ("yhi", "ylo", "x")
GROUPS = [
    [
        (((group ^ yhi) * 4 + z) * 2 + core) * 8 + x * 2 + yhi
        for x in range(4)
        for yhi in range(2)
        for core in range(2)
    ]
    for group in range(2)
    for z in range(4)
]
RING = ("ylo", "z")
ROWS_ORDER = ("ylo", "z", "yhi", "x")
OUT_ORDER = ("yhi", "z", "ylo", "x")
SLOTS = 40

bf16 = jnp.bfloat16
f32 = jnp.float32


def dot(left, right):
    return jnp.dot(left, right, preferred_element_type=f32)


def dot_t(left, right):
    return lax.dot_general(left, right, (((1,), (1,)), ((), ())), preferred_element_type=f32)


def t_dot(left, right):
    return lax.dot_general(left, right, (((0,), (0,)), ((), ())), preferred_element_type=f32)


def exchange(pieces, axes):
    return lax.all_to_all(pieces, axes, split_axis=0, concat_axis=0, tiled=True)


def to_owners(pieces):
    return lax.all_to_all(
        pieces, AXES, split_axis=0, concat_axis=0, axis_index_groups=GROUPS, tiled=True
    )


def spread(piece, count, axes):
    return exchange(jnp.broadcast_to(piece[None], (count,) + piece.shape), axes)


def after(value, earlier):
    return lax.optimization_barrier((value, earlier))[0]


def together(*values):
    return lax.optimization_barrier(values)


def partner(value):
    return lax.ppermute(value, "core", [(0, 1), (1, 0)])


def route(axes, sizes, move):
    pairs = []
    for source in range(math.prod(sizes)):
        rest, at = source, []
        for size in reversed(sizes):
            at.insert(0, rest % size)
            rest //= size
        target = 0
        for size, value in zip(sizes, move(*at)):
            target = target * size + value
        pairs.append((source, target))
    return pairs


SAME = route(("core", "yhi"), (2, 2), lambda c, h: (h, c))
OTHER = route(("core", "yhi"), (2, 2), lambda c, h: (1 - h, c))
OUT_SAME = route(("ylo", "core", "yhi"), (2, 2, 2), lambda j, c, h: (c, j, h))
OUT_OTHER = route(("ylo", "core", "yhi"), (2, 2, 2), lambda j, c, h: (c, j, 1 - h))


def back(pairs):
    return [(target, source) for source, target in pairs]


def pick(flag, if_zero, if_one):
    return jnp.where(flag == 0, if_zero, if_one)


def gather_pieces(pair, flag, key, axes, same, other):
    first = lax.ppermute(pick(flag, pair[0], pair[1]), axes, same)
    second = lax.ppermute(pick(flag, pair[1], pair[0]), axes, other)
    return pick(
        key, jnp.concatenate([first, second]), jnp.concatenate([second, first])
    )


def scatter_pieces(piece, flag, key, axes, same, other):
    count = piece.shape[0] // 2
    mine, rest = piece[:count], piece[count:]
    first = lax.ppermute(pick(key, mine, rest), axes, back(same))
    second = lax.ppermute(pick(key, rest, mine), axes, back(other))
    return pick(flag, jnp.concatenate([first, second], axis=-1), jnp.concatenate([second, first], axis=-1))


def along(axis, piece):
    return [piece] + [
        lax.ppermute(piece, axis, [(i, (i + s) % 4) for i in range(4)]) for s in (1, 2, 3)
    ]


def back_along_x(blocks):
    return [blocks[0]] + [
        lax.ppermute(blocks[s], "x", [(i, (i - s) % 4) for i in range(4)]) for s in (1, 2, 3)
    ]


def added(blocks):
    (total,) = call(add_kernel, [(blocks[0].shape, bf16)], *blocks, cost=LONG)
    return total


def add_kernel(first, second, third, fourth, total):
    total[...] = (
        (first[...].astype(f32) + second[...].astype(f32))
        + (third[...].astype(f32) + fourth[...].astype(f32))
    ).astype(bf16)


def order_matrix(groups, x):
    index = jnp.arange(groups * 96, dtype=jnp.int32)
    turn_of, group, row = index // (groups * 24), index // 24 % groups, index % 24
    own = group * 96 + (x - turn_of) % 4 * 24 + row
    return (index[:, None] == own[None, :]).astype(bf16)


def level_order_matrix(z):
    index = jnp.arange(8 * 96, dtype=jnp.int32)
    own = (z - index // 192) % 4 * 192 + index % 192
    return (index[:, None] == own[None, :]).astype(bf16)


def places(pair_of, ctx, row_count, ctx_count):
    half_size = row_count // 2
    pair = jnp.sum(
        jnp.where(ctx[:, None] == jnp.arange(ctx_count, dtype=jnp.int32)[None], pair_of[None], 0),
        axis=1,
    )
    block = jnp.stack([pair, 2 * ctx_count - 1 - pair], axis=1)
    return block[:, :, None] * half_size + jnp.arange(half_size, dtype=jnp.int32)[None, None]


def in_three(value):
    high = value.astype(bf16)
    rest = value - high.astype(f32)
    middle = rest.astype(bf16)
    return [high, middle, (rest - middle.astype(f32)).astype(bf16)]


def call(kernel, outs, *args, scratch=(), cost=None):
    def whole(shape):
        return pl.BlockSpec(shape, lambda i: (0,) * len(shape))

    return pl.pallas_call(
        kernel,
        out_shape=[jax.ShapeDtypeStruct(shape, dtype) for shape, dtype in outs],
        grid=(1,),
        in_specs=[whole(a.shape) for a in args],
        out_specs=[whole(shape) for shape, _ in outs],
        scratch_shapes=list(scratch),
        compiler_params=pltpu.CompilerParams(vmem_limit_bytes=ROOM),
        cost_estimate=COST if cost is None else cost,
    )(*args)


ROOM = 58 << 20
COST = pl.CostEstimate(flops=1 << 20, bytes_accessed=1 << 18, transcendentals=0)
LONG = pl.CostEstimate(flops=1 << 35, bytes_accessed=1 << 27, transcendentals=0)
WIDE = 2 * HD
EXPERTS = 16


def turn(vectors, cosines, sines):
    return vectors * cosines + pltpu.roll(vectors, HD // 2, axis=1) * sines


def gain_picker():
    row = lax.broadcasted_iota(jnp.int32, (8, 128), 0)
    column = lax.broadcasted_iota(jnp.int32, (8, 128), 1)
    return jnp.where((column == row + EXPERTS) & (row < 2), 1.0, 0.0).astype(bf16)


def normal_of(stream):
    inverse = lax.rsqrt(jnp.mean(stream * stream, axis=-1, keepdims=True) + EPSILON)
    return stream * inverse, inverse


def norm_back(grad, normal, inverse, gain):
    scaled = grad * gain
    return inverse * (scaled - normal * jnp.mean(scaled * normal, axis=-1, keepdims=True))


def column_block(s, count):
    return slice(s * count, (s + 1) * count)


def order_kernel(rows, order, out):
    out[...] = dot(rows[...], order[...]).astype(bf16)


def keys_kernel(both, cosines, sines, *refs):
    kvs, (normed, key_value, gains) = refs[:4], refs[4:]
    count = kvs[0].shape[0]
    for s in range(4):
        gains[:, column_block(s, count)] = dot_t(gain_picker(), kvs[s][:, WIDE:])
    normal, _ = normal_of(both[...].astype(f32))
    normed[...] = (normal * gains[0:1]).astype(bf16)
    kv = dot(normed[:, column_block(0, count)], kvs[0][:, :WIDE])
    for s in range(1, 4):
        kv = kv + dot(normed[:, column_block(s, count)], kvs[s][:, :WIDE])
    key_value[:, :HD] = turn(kv[:, :HD], cosines[...], sines[...]).astype(bf16)
    key_value[:, HD:] = kv[:, HD:].astype(bf16)


def small_kernel(order, kvs0, kvs1, kvs2, kvs3, small, gains):
    count = kvs0.shape[0]
    total = jnp.zeros(small.shape, f32)
    for s, kvs in enumerate((kvs0, kvs1, kvs2, kvs3)):
        total = total + dot(order[:, column_block(s, count)], kvs[:, WIDE:])
    small[...] = total.astype(bf16)
    gains[...] = dot_t(gain_picker(), small[...])


def query_kernel(normed, cosines, sines, w_q0, w_q1, w_q2, w_q3, queries):
    w_q = (w_q0, w_q1, w_q2, w_q3)
    count = w_q0.shape[0]
    for h in range(queries.shape[1] // HD):
        at = column_block(h, HD)
        q = dot(normed[:, column_block(0, count)], w_q0[:, at])
        for s in range(1, 4):
            q = q + dot(normed[:, column_block(s, count)], w_q[s][:, at])
        queries[:, at] = turn(q, cosines[...], sines[...]).astype(bf16)


def attend_kernel(
    queries,
    q_place,
    low_place,
    up_place,
    order,
    order_back,
    kv,
    ordered,
    ordered_back,
    logs,
    kv_low,
    kv_up,
    mixed,
    *,
    scale,
    pieces,
    heads,
):
    half = kv.shape[1] // 2
    for i in range(pieces):
        kv_low[i * half : (i + 1) * half, :] = kv[i, :half]
        kv_up[i * half : (i + 1) * half, :] = kv[i, half:]
    allowed_low = low_place[...] <= q_place[...]
    allowed_up = up_place[...] <= q_place[half:, :]
    for h in range(heads):
        at = slice(h * HD, (h + 1) * HD)
        q = queries[:, at]
        low = jnp.where(allowed_low, dot_t(q, kv_low[:, :HD]) * scale, NEGATIVE)
        up = jnp.where(allowed_up, dot_t(q[half:], kv_up[:, :HD]) * scale, NEGATIVE)
        first, second = low[:half], low[half:]
        top = jnp.max(first, axis=-1, keepdims=True)
        weight = jnp.exp(first - top)
        total = jnp.sum(weight, axis=-1, keepdims=True)
        probs = (weight / total).astype(bf16)
        mixed[:half, at] = dot(probs, kv_low[:, HD:]).astype(bf16)
        logs[h, :half, :] = top + jnp.log(total)
        top = jnp.maximum(
            jnp.max(second, axis=-1, keepdims=True), jnp.max(up, axis=-1, keepdims=True)
        )
        weight, weight_up = jnp.exp(second - top), jnp.exp(up - top)
        total = jnp.sum(weight, axis=-1, keepdims=True) + jnp.sum(
            weight_up, axis=-1, keepdims=True
        )
        mixed[half:, at] = (
            dot((weight / total).astype(bf16), kv_low[:, HD:])
            + dot((weight_up / total).astype(bf16), kv_up[:, HD:])
        ).astype(bf16)
        logs[h, half:, :] = top + jnp.log(total)
    ordered[...] = dot(mixed[...], order[...]).astype(bf16)
    ordered_back[...] = dot(mixed[...], order_back[...]).astype(bf16)


def branch_kernel(mixed, w_out0, w_out1, w_out2, w_out3, own, other, w_out):
    quarter = mixed.shape[0] // 4
    count, columns = w_out0.shape[1:]
    for s, part in enumerate((w_out0, w_out1, w_out2, w_out3)):
        w_out[:, column_block(s, count)] = part[...]
    for k in range(2):
        part = dot(mixed[...], w_out[k])
        at = slice(k * columns, (k + 1) * columns)
        own[:quarter, at] = part[:quarter]
        other[:quarter, at] = part[quarter : 2 * quarter]
        own[quarter:, at] = part[2 * quarter : 3 * quarter]
        other[quarter:, at] = part[3 * quarter :]


def route_kernel(
    tokens,
    own,
    received,
    small,
    gains,
    hits,
    places_of,
    placer,
    sent,
    midway,
    moe_low,
    gates,
    parts,
):
    middle = tokens[...].astype(f32) + (own[...] + received[...])
    midway[...] = middle
    normal, _ = normal_of(middle)
    moe = (normal * gains[1:2]).astype(bf16)
    moe_low[...] = moe
    sent[:, : moe.shape[1]] = dot(placer[...], moe).astype(bf16)
    logits = dot(moe, small[...])
    picked = [
        jnp.sum(hits[k].astype(f32) * logits, axis=-1, keepdims=True) for k in range(TOPK)
    ]
    top = picked[0]
    for value in picked[1:]:
        top = jnp.maximum(top, value)
    weights = [jnp.exp(value - top) for value in picked]
    total = weights[0]
    for value in weights[1:]:
        total = total + value
    lane = lax.broadcasted_iota(jnp.int32, gates.shape, 1)
    gate_at = jnp.zeros(places_of.shape[1:], f32)
    kept = jnp.zeros(gates.shape, f32)
    for k in range(TOPK):
        gate = weights[k] / total
        kept = jnp.where(lane == k, gate, kept)
        gate_at = gate_at + places_of[k].astype(f32) * gate
    gates[...] = kept
    block = jnp.zeros((sent.shape[0], 128), f32)
    for i, part in enumerate(in_three(gate_at)):
        parts[i] = part
        block = block + t_dot(part, jnp.where(lane == i, 1.0, 0.0).astype(bf16))
    sent[:, moe.shape[1] :] = block.astype(bf16)


def fetched(core, weights, held, sems, first):
    copies = [
        pltpu.make_async_copy(weights.at[m, core[0]], held.at[m], sems.at[m]) for m in range(3)
    ]

    @pl.when(pl.program_id(0) == 0)
    def _():
        for m in first:
            copies[m].start()

    def ready(m):
        @pl.when(pl.program_id(0) == 0)
        def _():
            copies[m].wait()

        return held[m]

    return ready


def forward_kernel(
    core, sent, cot, weights, out, hidden, out_grad, factor, other_factor, held, sems
):
    ready = fetched(core, weights, held, sems, (0, 1, 2))
    width = out.shape[1]
    rows = sent[:, :width]
    gate_pre, up_pre = dot(rows, ready(0)), dot(rows, ready(1))
    sigmoid = 1.0 / (1.0 + jnp.exp(-gate_pre))
    silu = gate_pre * sigmoid
    low = (silu * up_pre).astype(bf16)
    hidden[...] = low
    out[...] = dot_t(low, ready(2)).astype(bf16)
    gates = jnp.sum(sent[:, width:].astype(f32), axis=-1, keepdims=True)
    out_grad[...] = (gates * cot[...].astype(f32)).astype(bf16)
    factor[...] = up_pre * sigmoid * (1.0 + gate_pre * (1.0 - sigmoid))
    other_factor[...] = silu


def backward_kernel(
    core, out_grad, factor, other_factor, weights, rows_grad, gate_grad, up_grad, held, sems
):
    ready = fetched(core, weights, held, sems, (2, 0, 1))
    hidden_grad = dot(out_grad[...], ready(2))
    low = (hidden_grad * factor[...]).astype(bf16)
    other = (hidden_grad * other_factor[...]).astype(bf16)
    gate_grad[...] = low
    up_grad[...] = other
    rows_grad[...] = (dot_t(low, ready(0)) + dot_t(other, ready(1))).astype(bf16)


def expert_call(kernel, block, core, arrays, weights, outs):
    count = arrays[0].shape[0]

    def rows(columns):
        return pl.BlockSpec((block, columns), lambda i, core: (i, 0))

    return pl.pallas_call(
        kernel,
        out_shape=[jax.ShapeDtypeStruct((count, columns), dtype) for columns, dtype in outs],
        grid_spec=pltpu.PrefetchScalarGridSpec(
            num_scalar_prefetch=1,
            grid=(count // block,),
            in_specs=[rows(a.shape[1]) for a in arrays] + [pl.BlockSpec(memory_space=pltpu.HBM)],
            out_specs=[rows(columns) for columns, _ in outs],
            scratch_shapes=[
                pltpu.VMEM((3,) + weights.shape[2:], bf16),
                pltpu.SemaphoreType.DMA((3,)),
            ],
        ),
        compiler_params=pltpu.CompilerParams(vmem_limit_bytes=ROOM),
        cost_estimate=COST,
    )(core, *arrays, weights)


def weights_kernel(sent, out_grad, hidden, gate_grad, up_grad, sums):
    rows = sent[...]
    sums[0] = t_dot(rows, gate_grad[...]).astype(bf16)
    sums[1] = t_dot(rows, up_grad[...]).astype(bf16)
    sums[2] = t_dot(out_grad[...], hidden[...]).astype(bf16)


def expert_weights_grad(sent, out_grad, hidden, gate_grad, up_grad, block=256):
    count, width = out_grad.shape
    columns = hidden.shape[1]
    part = pl.BlockSpec((count, block), lambda i: (0, i))
    whole = pl.BlockSpec((count, columns), lambda i: (0, 0), pipeline_mode=pl.Buffered(1))
    return pl.pallas_call(
        weights_kernel,
        out_shape=jax.ShapeDtypeStruct((3, width, columns), bf16),
        grid=(width // block,),
        in_specs=[part, part, whole, whole, whole],
        out_specs=pl.BlockSpec((3, block, columns), lambda i: (0, i, 0)),
        compiler_params=pltpu.CompilerParams(vmem_limit_bytes=ROOM),
        cost_estimate=COST,
    )(sent, out_grad, hidden, gate_grad, up_grad)


def combine_kernel(
    midway, parts, returned, cot, hits, places_of, gates, small, moe_low, output, moe_part, router_grad
):
    rows = returned[...]
    output[...] = (
        midway[...] + (dot(parts[0], rows) + (dot(parts[1], rows) + dot(parts[2], rows)))
    ).astype(bf16)
    agreement = dot_t(cot[...], rows)
    lane = lax.broadcasted_iota(jnp.int32, gates.shape, 1)
    gate, grad = [], []
    mean = jnp.zeros((gates.shape[0], 1), f32)
    for k in range(TOPK):
        gate.append(jnp.sum(jnp.where(lane == k, gates[...], 0.0), axis=-1, keepdims=True))
        grad.append(jnp.sum(places_of[k].astype(f32) * agreement, axis=-1, keepdims=True))
        mean = mean + gate[k] * grad[k]
    logit_grad = jnp.zeros(gates.shape, f32)
    for k in range(TOPK):
        logit_grad = logit_grad + hits[k].astype(f32) * (gate[k] * (grad[k] - mean))
    logit_grad = logit_grad.astype(bf16)
    moe_part[...] = dot_t(logit_grad, small[...])
    router_grad[...] = t_dot(moe_low[...], logit_grad)


def home_kernel(placer_t, home, moe_part, midway, cot, gains, midway_grad, branch_low, gain_grad):
    grad = dot(placer_t[...], home[...]) + moe_part[...]
    normal, inverse = normal_of(midway[...])
    result = cot[...].astype(f32) + norm_back(grad, normal, inverse, gains[1:2])
    midway_grad[...] = result
    branch_low[...] = result.astype(bf16)
    gain_grad[...] = jnp.broadcast_to(
        jnp.sum(grad * normal, axis=0, keepdims=True), gain_grad.shape
    )


def out_grad_kernel(mixed, own, other, branch, *blocks):
    quarter = own.shape[0] // 2
    branch[:quarter] = own[:quarter]
    branch[quarter : 2 * quarter] = other[:quarter]
    branch[2 * quarter : 3 * quarter] = own[quarter:]
    branch[3 * quarter :] = other[quarter:]
    count, columns = blocks[0].shape[1:]
    for k in range(2):
        grad = t_dot(mixed[...], branch[:, column_block(k, columns)]).astype(bf16)
        for s in range(4):
            blocks[s][k] = grad[column_block(s, count)]


def attend_back_kernel(
    branch,
    w_out,
    order,
    queries,
    kv_low,
    kv_up,
    logs,
    q_place,
    low_place,
    up_place,
    cosines,
    sines,
    normed,
    dq,
    dkv,
    block0,
    block1,
    block2,
    block3,
    grads,
    acc_low,
    acc_up,
    *,
    scale,
    pieces,
    heads,
):
    half = queries.shape[0] // 2
    columns = w_out.shape[2]
    ordered = dot_t(branch[:, :columns], w_out[0]) + dot_t(branch[:, columns:], w_out[1])
    grads[...] = dot_t(ordered.astype(bf16), order[...]).astype(bf16)
    allowed_low = low_place[...] <= q_place[...]
    allowed_up = up_place[...] <= q_place[half:, :]
    key_low, value_low = kv_low[:, :HD], kv_low[:, HD:]
    key_up, value_up = kv_up[:, :HD], kv_up[:, HD:]
    for h in range(heads):
        at = slice(h * HD, (h + 1) * HD)
        q, grad, log = queries[:, at], grads[:, at], logs[h]
        low = jnp.where(allowed_low, dot_t(q, key_low) * scale, NEGATIVE)
        up = jnp.where(allowed_up, dot_t(q[half:], key_up) * scale, NEGATIVE)
        probs_low, probs_up = jnp.exp(low - log), jnp.exp(up - log[half:])
        grad_low, grad_up = dot_t(grad, value_low), dot_t(grad[half:], value_up)
        along = jnp.sum(probs_low * grad_low, axis=-1, keepdims=True)
        along_up = along[half:] + jnp.sum(probs_up * grad_up, axis=-1, keepdims=True)
        along = jnp.concatenate([along[:half], along_up])
        score_low = (probs_low * (grad_low - along)).astype(bf16)
        score_up = (probs_up * (grad_up - along_up)).astype(bf16)
        part = dot(score_low, key_low)
        part = jnp.concatenate([part[:half], part[half:] + dot(score_up, key_up)]) * scale
        dq[:, at] = turn(part, cosines[...], -sines[...]).astype(bf16)
        terms = (
            (acc_low, slice(0, HD), t_dot(q, score_low)),
            (acc_up, slice(0, HD), t_dot(q[half:], score_up)),
            (acc_low, slice(HD, 2 * HD), t_dot(grad, probs_low.astype(bf16))),
            (acc_up, slice(HD, 2 * HD), t_dot(grad[half:], probs_up.astype(bf16))),
        )
        for acc, rows, term in terms:
            if h == 0:
                acc[rows] = term
            else:
                acc[rows] += term
    for s, block in enumerate((block0, block1, block2, block3)):
        block[...] = t_dot(normed[:, column_block(s, block.shape[0])], dq[...]).astype(bf16)
    for acc, first in ((acc_low, 0), (acc_up, half)):
        dk = (acc[:HD].T * scale).astype(bf16)
        dv = acc[HD:].T.astype(bf16)
        for i in range(pieces):
            dkv[i, first : first + half, :HD] = dk[i * half : (i + 1) * half]
            dkv[i, first : first + half, HD:] = dv[i * half : (i + 1) * half]


def sum_kernel(dq, cosines, sines, *refs):
    w_q, kvs, (parts, dkv, own, other) = refs[:4], refs[4:8], refs[8:]
    total = jnp.sum(parts[...].astype(f32), axis=0)
    dkv[:, :HD] = turn(total[:, :HD], cosines[...], -sines[...]).astype(bf16)
    dkv[:, HD:] = total[:, HD:].astype(bf16)
    quarter = own.shape[0] // 2
    for s in range(4):
        grad = dot_t(dq[...], w_q[s][...]) + dot_t(dkv[...], kvs[s][:, :WIDE])
        at = column_block(s, w_q[s].shape[0])
        own[:quarter, at] = grad[:quarter]
        other[:quarter, at] = grad[quarter : 2 * quarter]
        own[quarter:, at] = grad[2 * quarter : 3 * quarter]
        other[quarter:, at] = grad[3 * quarter :]


def stack_kernel(gate, up, down, late, out):
    del late
    out[0] = gate[...]
    out[1] = up[...]
    out[2] = down[...]


def small_grad_kernel(order, router_grad, gain_grad, late, out):
    del late
    row = lax.broadcasted_iota(jnp.int32, gain_grad.shape, 0)
    second = jnp.where(row == 1, gain_grad[...], 0.0).astype(bf16)
    small = router_grad[...] + t_dot(second, gain_picker())
    out[...] = t_dot(order[...], small.astype(bf16))


def input_kernel(both, own, received, midway_grad, gains, order, small, normed, dkv, out, *blocks):
    grad = own[...] + received[...]
    quarter = own.shape[0] // 2
    tokens = jnp.concatenate([both[:quarter], both[2 * quarter : 3 * quarter]])
    normal, inverse = normal_of(tokens.astype(f32))
    parts = in_three(norm_back(grad, normal, inverse, gains[0:1]))
    moved = dot_t(jnp.concatenate(parts), order[...])
    count = 2 * quarter
    out[...] = midway_grad[...] + (
        moved[:count] + (moved[count : 2 * count] + moved[2 * count :])
    )
    gain_grad = jnp.sum(grad * normal, axis=0, keepdims=True)
    row = lax.broadcasted_iota(jnp.int32, gains.shape, 0)
    gain_grad = jnp.where(row == 0, gain_grad, 0.0).astype(bf16)
    small = small[...] + t_dot(gain_grad, gain_picker())
    rows = blocks[0].shape[0]
    for s, block in enumerate(blocks):
        at = column_block(s, rows)
        block[:, :WIDE] = t_dot(normed[:, at], dkv[...]).astype(bf16)
        block[:, WIDE:] = small[at].astype(bf16)


def body(
    tokens,
    cotangent,
    pair_of,
    routes,
    attn_gain,
    moe_gain,
    w_query,
    w_key,
    w_value,
    w_out,
    w_router,
    w_gate,
    w_up,
    w_down,
):
    rows = tokens.shape[1]
    half = rows // 2
    width = tokens.shape[2]
    shard = w_query.shape[1]
    ctx_count = 16
    experts = w_router.shape[2]
    columns = w_gate.shape[3]
    per_group = H // KVH
    qw = per_group * HD
    scale = 1.0 / math.sqrt(HD)
    core = lax.axis_index("core")
    ylo, z, yhi = lax.axis_index("ylo"), lax.axis_index("z"), lax.axis_index("yhi")
    x = lax.axis_index("x")
    piece_rows = 2 * shard
    slots = experts * SLOTS
    own_tokens, cot = tokens[0], cotangent[0]

    def halves(matrix):
        return [matrix[:, : matrix.shape[1] // 2], matrix[:, matrix.shape[1] // 2 :]]

    small = jnp.concatenate([w_router[0], attn_gain[0][:, None], moe_gain[0][:, None]], axis=-1)
    small = jnp.pad(small, ((0, 0), (0, 128 - experts - 2)))
    query_halves, key_halves, value_halves = halves(w_query[0]), halves(w_key[0]), halves(w_value[0])
    pairs = [
        jnp.concatenate([k, v, small, q], axis=-1)
        for k, v, q in zip(key_halves, value_halves, query_halves)
    ]
    pieces = gather_pieces(pairs, yhi, core, ("core", "yhi"), SAME, OTHER)
    out_pieces = gather_pieces(
        halves(w_out[0]), yhi, yhi, ("ylo", "core", "yhi"), OUT_SAME, OUT_OTHER
    )
    other_tokens = partner(own_tokens)
    pieces, out_pieces, x, z, own_tokens, other_tokens, pair_of = together(
        pieces, out_pieces, x, z, own_tokens, other_tokens, pair_of
    )

    plane_rows = 16 * piece_rows
    plane = spread(pieces, 16, PLANE)
    both = jnp.concatenate(
        [own_tokens[:half], other_tokens[:half], own_tokens[half:], other_tokens[half:]]
    )
    order, out_order, level_order = order_matrix(16, x), order_matrix(8, x), level_order_matrix(z)
    plane, both, out_pieces, order, out_order, level_order, pair_of = together(
        plane, both, out_pieces, order, out_order, level_order, pair_of
    )

    plane = plane.reshape(plane_rows, -1)
    w_kvs = along("x", plane[:, : 3 * HD])
    wo = spread(out_pieces, 16, LEVEL)
    (both,) = call(order_kernel, [((2 * rows, width), bf16)], both, order)

    def two_cores(ctx):
        return jnp.stack([ctx + core, ctx + 1 - core], axis=-1).reshape(-1)

    ctx_here = (ylo * 4 + z) * 2
    q_place = places(pair_of, two_cores(ctx_here), rows, ctx_count)
    q_place = q_place.transpose(1, 0, 2).reshape(2 * rows, 1)
    key_place = places(
        pair_of, two_cores(jnp.arange(8, dtype=jnp.int32) * 2), rows, ctx_count
    )
    low_place, up_place = key_place[:, 0].reshape(1, -1), key_place[:, 1].reshape(1, -1)
    frequency = jnp.exp(jnp.arange(HD // 2, dtype=f32) * (-2.0 * math.log(ROPE_BASE) / HD))
    angles = q_place.astype(f32) * frequency[None, :]
    cosines, sines = jnp.cos(angles), jnp.sin(angles)
    cosines = jnp.concatenate([cosines, cosines], axis=-1)
    sines = jnp.concatenate([-sines, sines], axis=-1)
    w_q, w_kvs, wo, both, q_place, low_place, up_place, cosines, sines, chosen = together(
        plane[:, 3 * HD :], w_kvs, wo, both, q_place, low_place, up_place, cosines, sines, routes[0, 0]
    )

    w_q = along("x", w_q)
    wo = along("z", wo.reshape(2, qw // 4, width // 2))
    normed, key_value, gains = call(
        keys_kernel,
        [((2 * rows, width), bf16), ((2 * rows, 2 * HD), bf16), ((8, width), f32)],
        both,
        cosines,
        sines,
        *w_kvs,
    )
    all_kv = spread(key_value, 8, RING)
    small, moe_gains = call(
        small_kernel, [((width, 128), bf16), ((8, width), f32)], order, *w_kvs
    )
    lanes = jnp.arange(128, dtype=jnp.int32)
    hits = (chosen.T[:, :, None] == lanes[None, None, :]).astype(bf16)
    earlier = (lanes[:, None] > lanes[None, :]).astype(bf16)
    before = dot(earlier, jnp.sum(hits, axis=0))
    slot_index = jnp.sum(hits.astype(f32) * before[None], axis=-1).astype(jnp.int32)
    target = chosen.T * SLOTS + slot_index
    slot_row = jnp.arange(slots, dtype=jnp.int32)
    places_of = (target[:, :, None] == slot_row[None, None, :]).astype(bf16)
    placer_t = jnp.sum(places_of, axis=0)
    placer = placer_t.T
    (cot_rows,) = call(order_kernel, [((slots, width), bf16)], placer, cot)
    (queries,) = call(
        query_kernel, [((2 * rows, qw), bf16)], normed, cosines, sines, *w_q, cost=LONG
    )
    (expert_shards_in,) = call(
        stack_kernel, [((3,) + w_gate.shape[1:], bf16)], w_gate[0], w_up[0], w_down[0], all_kv
    )
    expert_weights = lax.all_gather(expert_shards_in, CTX, axis=2, tiled=True)
    (
        queries, all_kv, small, moe_gains, hits, places_of, placer_t, placer, cot_rows,
        wo[1], wo[3],
    ) = together(
        queries, all_kv, small, moe_gains, hits, places_of, placer_t, placer, cot_rows,
        wo[1], wo[3],
    )

    arrived_cot = to_owners(cot_rows.reshape(experts, SLOTS, width))
    sizes = dict(scale=scale, pieces=8, heads=per_group)
    keys = 8 * rows
    mixed, mixed_back, logs, kv_low, kv_up = call(
        functools.partial(attend_kernel, **sizes),
        [
            ((2 * rows, qw), bf16),
            ((2 * rows, qw), bf16),
            ((per_group, 2 * rows, 1), f32),
            ((keys, 2 * HD), bf16),
            ((keys, 2 * HD), bf16),
        ],
        queries,
        q_place,
        low_place,
        up_place,
        level_order,
        out_order,
        all_kv,
        scratch=[pltpu.VMEM((2 * rows, qw), bf16)],
    )
    wo[2], mixed = together(wo[2], mixed)

    branch_own, branch_other, wo = call(
        branch_kernel,
        [((rows, width), f32), ((rows, width), f32), ((2, qw, width // 2), bf16)],
        mixed,
        *wo,
    )
    sent, midway, moe_low, gates, gate_parts = call(
        route_kernel,
        [
            ((slots, width + 128), bf16),
            ((rows, width), f32),
            ((rows, width), bf16),
            ((rows, 128), f32),
            ((3, rows, slots), bf16),
        ],
        own_tokens,
        branch_own,
        partner(branch_other),
        small,
        moe_gains,
        hits,
        places_of,
        placer,
    )
    sent, arrived_cot = together(sent, arrived_cot)

    sent = to_owners(sent.reshape(experts, SLOTS, width + 128)).reshape(slots, width + 128)
    mine = core.reshape(1)
    expert_out, hidden, out_grad, factor, other_factor = expert_call(
        forward_kernel,
        slots // 2,
        mine,
        [sent, arrived_cot.reshape(slots, width)],
        expert_weights,
        [(width, bf16), (columns, bf16), (width, bf16), (columns, f32), (columns, f32)],
    )
    expert_out, factor = together(expert_out, factor)

    returned = to_owners(expert_out.reshape(experts, SLOTS, width))
    rows_grad, gate_grad, up_grad = expert_call(
        backward_kernel,
        128,
        mine,
        [out_grad, factor, other_factor],
        expert_weights,
        [(width, bf16), (columns, bf16), (columns, bf16)],
    )
    expert_sums = expert_weights_grad(sent, out_grad, hidden, gate_grad, up_grad)
    returned, rows_grad, expert_sums = together(returned, rows_grad, expert_sums)
    home_grad = to_owners(rows_grad.reshape(experts, SLOTS, width))
    expert_sums = lax.psum_scatter(expert_sums, RING, scatter_dimension=1, tiled=True)
    output, moe_part, router_grad = call(
        combine_kernel,
        [((rows, width), bf16), ((rows, width), f32), ((width, 128), f32)],
        midway,
        gate_parts,
        returned.reshape(slots, width),
        cot,
        hits,
        places_of,
        gates,
        small,
        moe_low,
    )
    home_grad, moe_part = together(home_grad, moe_part)
    midway_grad, branch_low, gain_two_grad = call(
        home_kernel,
        [((rows, width), f32), ((rows, width), bf16), ((8, width), f32)],
        placer_t,
        home_grad.reshape(slots, width),
        moe_part,
        midway,
        cot,
        moe_gains,
    )
    branch, *out_w_grad = call(
        out_grad_kernel,
        [((2 * rows, width), bf16)] + [((2, qw // 4, width // 2), bf16)] * 4,
        mixed_back,
        branch_low,
        partner(branch_low),
    )
    branch, out_w_grad = together(branch, out_w_grad)
    out_w_grad = added(back_along_x(out_w_grad))

    dq, dkv, *q_w_grad = call(
        functools.partial(attend_back_kernel, **sizes),
        [((2 * rows, qw), bf16), ((8, 2 * rows, 2 * HD), bf16)]
        + [((plane_rows, qw), bf16)] * 4,
        branch,
        wo,
        level_order,
        queries,
        kv_low,
        kv_up,
        logs,
        q_place,
        low_place,
        up_place,
        cosines,
        sines,
        normed,
        scratch=[
            pltpu.VMEM((2 * rows, qw), bf16),
            pltpu.VMEM((2 * HD, keys), f32),
            pltpu.VMEM((2 * HD, keys), f32),
        ],
    )
    dkv = exchange(dkv, RING)
    q_w_grad = back_along_x(q_w_grad)
    (small_grad,) = call(
        small_grad_kernel, [((width, 128), f32)], order, router_grad, gain_two_grad, dq
    )
    dkv, out_w_grad, small_grad, q_w_grad[1], q_w_grad[3] = together(
        dkv, out_w_grad, small_grad, q_w_grad[1], q_w_grad[3]
    )

    dkv, normed_own, normed_other = call(
        sum_kernel,
        [((2 * rows, 2 * HD), bf16), ((rows, width), f32), ((rows, width), f32)],
        dq,
        cosines,
        sines,
        *w_q,
        *w_kvs,
        dkv,
    )
    input_grad, *kvs_grad = call(
        input_kernel,
        [((rows, width), f32)] + [((plane_rows, 3 * HD), bf16)] * 4,
        both,
        normed_own,
        partner(normed_other),
        midway_grad,
        gains,
        order,
        small_grad,
        normed,
        dkv,
    )
    q_w_grad = added(q_w_grad)
    kvs_grad, out_w_grad, input_grad, q_w_grad = together(
        kvs_grad, out_w_grad, input_grad, q_w_grad
    )

    out_w_grad = exchange(out_w_grad.reshape(16, piece_rows, width // 2), OUT_PLANE)
    kvs_grad = added(back_along_x(kvs_grad))
    plane_grad = jnp.concatenate([q_w_grad, kvs_grad], axis=-1)
    plane_grad, out_w_grad, expert_sums = together(plane_grad, out_w_grad, expert_sums)
    plane_grad = exchange(plane_grad.reshape(16, piece_rows, qw + 3 * HD), PLANE)

    def summed(pieces):
        return jnp.sum(pieces.astype(f32), axis=0)

    def expert_shards(grad):
        count = grad.shape[1] // 2
        kept = lax.dynamic_slice_in_dim(grad, core * count, count, axis=1)
        given = partner(lax.dynamic_slice_in_dim(grad, (1 - core) * count, count, axis=1))
        both = jnp.stack([pick(core, kept, given), pick(core, given, kept)], axis=1)
        return [both[i : i + 1].astype(f32) for i in range(3)]

    out_w_grad = scatter_pieces(
        summed(out_w_grad), yhi, yhi, ("ylo", "core", "yhi"), OUT_SAME, OUT_OTHER
    )
    w_gate_grad, w_up_grad, w_down_grad = expert_shards(expert_sums)
    plane_grad, out_w_grad, w_gate_grad, w_up_grad, w_down_grad = together(
        plane_grad, out_w_grad, w_gate_grad, w_up_grad, w_down_grad
    )
    plane_grad = scatter_pieces(summed(plane_grad), yhi, core, ("core", "yhi"), SAME, OTHER)
    plane_grad = plane_grad.reshape(shard, 2, -1)

    def joined(first, last):
        return plane_grad[:, :, first:last].reshape(1, shard, -1)

    small_grad = jnp.sum(plane_grad[None, :, :, qw + 2 * HD :], axis=2)

    return (
        output[None],
        input_grad[None],
        small_grad[:, :, experts],
        small_grad[:, :, experts + 1],
        joined(0, qw),
        joined(qw, qw + HD),
        joined(qw + HD, qw + 2 * HD),
        out_w_grad[None],
        small_grad[:, :, :experts],
        w_gate_grad,
        w_up_grad,
        w_down_grad,
    )


def solution(mesh):
    fine = Mesh(mesh.devices.reshape(2, 4, 2, 4, 2), AXES)
    seq = P(FSDP, CTX, None)
    vector = P(None, AXES)
    matrix = P(None, AXES, None)
    expert = P(None, FSDP, CTX, None)
    in_specs = (
        seq,
        seq,
        P(),
        P(None, FSDP, CTX, None),
        vector,
        vector,
        matrix,
        matrix,
        matrix,
        matrix,
        matrix,
        expert,
        expert,
        expert,
    )
    out_specs = (
        seq,
        seq,
        vector,
        vector,
        matrix,
        matrix,
        matrix,
        matrix,
        matrix,
        expert,
        expert,
        expert,
    )
    return jax.shard_map(body, mesh=fine, in_specs=in_specs, out_specs=out_specs, check_vma=False)
```

```python
import functools
import math

import jax
import jax.numpy as jnp
from jax import lax
from jax.experimental import pallas as pl
from jax.experimental.pallas import tpu as pltpu
from jax.sharding import Mesh
from jax.sharding import PartitionSpec as P

H = 12
KVH = 2
HD = 128
TOPK = 4

EPSILON = 1e-06
ROPE_BASE = 1000000.0
NEGATIVE = -1e30

AXES = ("ylo", "z", "core", "x", "yhi")
CTX = ("ylo", "z", "core")
FSDP = ("x", "yhi")
GROUPS = [
    [
        (((group ^ yhi) * 4 + z) * 2 + core) * 8 + x * 2 + yhi
        for x in range(4)
        for yhi in range(2)
        for core in range(2)
    ]
    for group in range(2)
    for z in range(4)
]
RING = ("ylo", "z")
PLANE = ("ylo", "z", "yhi")
OUT_PLANE = ("yhi", "z", "ylo")
LEVEL = ("yhi", "ylo", "x")
GROUPS = [
    [
        (((group ^ yhi) * 4 + z) * 2 + core) * 8 + x * 2 + yhi
        for x in range(4)
        for yhi in range(2)
        for core in range(2)
    ]
    for group in range(2)
    for z in range(4)
]
RING = ("ylo", "z")
ROWS_ORDER = ("ylo", "z", "yhi", "x")
OUT_ORDER = ("yhi", "z", "ylo", "x")
SLOTS = 40

bf16 = jnp.bfloat16
f32 = jnp.float32


def dot(left, right):
    return jnp.dot(left, right, preferred_element_type=f32)


def dot_t(left, right):
    return lax.dot_general(left, right, (((1,), (1,)), ((), ())), preferred_element_type=f32)


def t_dot(left, right):
    return lax.dot_general(left, right, (((0,), (0,)), ((), ())), preferred_element_type=f32)


def exchange(pieces, axes):
    return lax.all_to_all(pieces, axes, split_axis=0, concat_axis=0, tiled=True)


def to_owners(pieces):
    return lax.all_to_all(
        pieces, AXES, split_axis=0, concat_axis=0, axis_index_groups=GROUPS, tiled=True
    )


def spread(piece, count, axes):
    return exchange(jnp.broadcast_to(piece[None], (count,) + piece.shape), axes)


def after(value, earlier):
    return lax.optimization_barrier((value, earlier))[0]


def together(*values):
    return lax.optimization_barrier(values)


def partner(value):
    return lax.ppermute(value, "core", [(0, 1), (1, 0)])


def route(axes, sizes, move):
    pairs = []
    for source in range(math.prod(sizes)):
        rest, at = source, []
        for size in reversed(sizes):
            at.insert(0, rest % size)
            rest //= size
        target = 0
        for size, value in zip(sizes, move(*at)):
            target = target * size + value
        pairs.append((source, target))
    return pairs


SAME = route(("core", "yhi"), (2, 2), lambda c, h: (h, c))
OTHER = route(("core", "yhi"), (2, 2), lambda c, h: (1 - h, c))
OUT_SAME = route(("ylo", "core", "yhi"), (2, 2, 2), lambda j, c, h: (c, j, h))
OUT_OTHER = route(("ylo", "core", "yhi"), (2, 2, 2), lambda j, c, h: (c, j, 1 - h))


def back(pairs):
    return [(target, source) for source, target in pairs]


def pick(flag, if_zero, if_one):
    return jnp.where(flag == 0, if_zero, if_one)


def gather_pieces(pair, flag, key, axes, same, other):
    first = lax.ppermute(pick(flag, pair[0], pair[1]), axes, same)
    second = lax.ppermute(pick(flag, pair[1], pair[0]), axes, other)
    return pick(
        key, jnp.concatenate([first, second]), jnp.concatenate([second, first])
    )


def scatter_pieces(piece, flag, key, axes, same, other):
    count = piece.shape[0] // 2
    mine, rest = piece[:count], piece[count:]
    first = lax.ppermute(pick(key, mine, rest), axes, back(same))
    second = lax.ppermute(pick(key, rest, mine), axes, back(other))
    return pick(flag, jnp.concatenate([first, second], axis=-1), jnp.concatenate([second, first], axis=-1))


def along(axis, piece):
    return [piece] + [
        lax.ppermute(piece, axis, [(i, (i + s) % 4) for i in range(4)]) for s in (1, 2, 3)
    ]


def back_along_x(blocks):
    return [blocks[0]] + [
        lax.ppermute(blocks[s], "x", [(i, (i - s) % 4) for i in range(4)]) for s in (1, 2, 3)
    ]


def added(blocks, *late):
    (total,) = call(add_kernel, [(blocks[0].shape, bf16)], *blocks, *late, cost=LONG)
    return total


def add_kernel(first, second, third, fourth, *refs):
    total = refs[-1]
    total[...] = (
        (first[...].astype(f32) + second[...].astype(f32))
        + (third[...].astype(f32) + fourth[...].astype(f32))
    ).astype(bf16)


def order_matrix(groups, x):
    index = jnp.arange(groups * 96, dtype=jnp.int32)
    turn_of, group, row = index // (groups * 24), index // 24 % groups, index % 24
    own = group * 96 + (x - turn_of) % 4 * 24 + row
    return (index[:, None] == own[None, :]).astype(bf16)


def level_order_matrix(z):
    index = jnp.arange(8 * 96, dtype=jnp.int32)
    own = (z - index // 192) % 4 * 192 + index % 192
    return (index[:, None] == own[None, :]).astype(bf16)


def places(pair_of, ctx, row_count, ctx_count):
    half_size = row_count // 2
    pair = jnp.sum(
        jnp.where(ctx[:, None] == jnp.arange(ctx_count, dtype=jnp.int32)[None], pair_of[None], 0),
        axis=1,
    )
    block = jnp.stack([pair, 2 * ctx_count - 1 - pair], axis=1)
    return block[:, :, None] * half_size + jnp.arange(half_size, dtype=jnp.int32)[None, None]


def in_three(value):
    high = value.astype(bf16)
    rest = value - high.astype(f32)
    middle = rest.astype(bf16)
    return [high, middle, (rest - middle.astype(f32)).astype(bf16)]


def call(kernel, outs, *args, scratch=(), cost=None):
    def whole(shape):
        return pl.BlockSpec(shape, lambda i: (0,) * len(shape))

    return pl.pallas_call(
        kernel,
        out_shape=[jax.ShapeDtypeStruct(shape, dtype) for shape, dtype in outs],
        grid=(1,),
        in_specs=[whole(a.shape) for a in args],
        out_specs=[whole(shape) for shape, _ in outs],
        scratch_shapes=list(scratch),
        compiler_params=pltpu.CompilerParams(vmem_limit_bytes=ROOM),
        cost_estimate=COST if cost is None else cost,
    )(*args)


ROOM = 58 << 20
COST = pl.CostEstimate(flops=1 << 20, bytes_accessed=1 << 18, transcendentals=0)
LONG = pl.CostEstimate(flops=1 << 35, bytes_accessed=1 << 27, transcendentals=0)
WIDE = 2 * HD
EXPERTS = 16


def turn(vectors, cosines, sines):
    return vectors * cosines + pltpu.roll(vectors, HD // 2, axis=1) * sines


def gain_picker():
    row = lax.broadcasted_iota(jnp.int32, (8, 128), 0)
    column = lax.broadcasted_iota(jnp.int32, (8, 128), 1)
    return jnp.where((column == row + EXPERTS) & (row < 2), 1.0, 0.0).astype(bf16)


def normal_of(stream):
    inverse = lax.rsqrt(jnp.mean(stream * stream, axis=-1, keepdims=True) + EPSILON)
    return stream * inverse, inverse


def norm_back(grad, normal, inverse, gain):
    scaled = grad * gain
    return inverse * (scaled - normal * jnp.mean(scaled * normal, axis=-1, keepdims=True))


def column_block(s, count):
    return slice(s * count, (s + 1) * count)


def order_kernel(rows, order, out):
    out[...] = dot(rows[...], order[...]).astype(bf16)


def keys_kernel(both, cosines, sines, *refs):
    kvs, (normed, key_value, gains) = refs[:4], refs[4:]
    count = kvs[0].shape[0]
    for s in range(4):
        gains[:, column_block(s, count)] = dot_t(gain_picker(), kvs[s][:, WIDE:])
    normal, _ = normal_of(both[...].astype(f32))
    normed[...] = (normal * gains[0:1]).astype(bf16)
    kv = dot(normed[:, column_block(0, count)], kvs[0][:, :WIDE])
    for s in range(1, 4):
        kv = kv + dot(normed[:, column_block(s, count)], kvs[s][:, :WIDE])
    key_value[:, :HD] = turn(kv[:, :HD], cosines[...], sines[...]).astype(bf16)
    key_value[:, HD:] = kv[:, HD:].astype(bf16)


def small_kernel(order, kvs0, kvs1, kvs2, kvs3, small, gains):
    count = kvs0.shape[0]
    total = jnp.zeros(small.shape, f32)
    for s, kvs in enumerate((kvs0, kvs1, kvs2, kvs3)):
        total = total + dot(order[:, column_block(s, count)], kvs[:, WIDE:])
    small[...] = total.astype(bf16)
    gains[...] = dot_t(gain_picker(), small[...])


def query_kernel(normed, cosines, sines, w_q0, w_q1, w_q2, w_q3, queries):
    w_q = (w_q0, w_q1, w_q2, w_q3)
    count = w_q0.shape[0]
    for h in range(queries.shape[1] // HD):
        at = column_block(h, HD)
        q = dot(normed[:, column_block(0, count)], w_q0[:, at])
        for s in range(1, 4):
            q = q + dot(normed[:, column_block(s, count)], w_q[s][:, at])
        queries[:, at] = turn(q, cosines[...], sines[...]).astype(bf16)


def attend_kernel(
    queries,
    q_place,
    low_place,
    up_place,
    order,
    order_back,
    kv,
    ordered,
    ordered_back,
    logs,
    kv_low,
    kv_up,
    mixed,
    *,
    scale,
    pieces,
    heads,
):
    half = kv.shape[1] // 2
    for i in range(pieces):
        kv_low[i * half : (i + 1) * half, :] = kv[i, :half]
        kv_up[i * half : (i + 1) * half, :] = kv[i, half:]
    allowed_low = low_place[...] <= q_place[...]
    allowed_up = up_place[...] <= q_place[half:, :]
    for h in range(heads):
        at = slice(h * HD, (h + 1) * HD)
        q = queries[:, at]
        low = jnp.where(allowed_low, dot_t(q, kv_low[:, :HD]) * scale, NEGATIVE)
        up = jnp.where(allowed_up, dot_t(q[half:], kv_up[:, :HD]) * scale, NEGATIVE)
        first, second = low[:half], low[half:]
        top = jnp.max(first, axis=-1, keepdims=True)
        weight = jnp.exp(first - top)
        total = jnp.sum(weight, axis=-1, keepdims=True)
        probs = (weight / total).astype(bf16)
        mixed[:half, at] = dot(probs, kv_low[:, HD:]).astype(bf16)
        logs[h, :half, :] = top + jnp.log(total)
        top = jnp.maximum(
            jnp.max(second, axis=-1, keepdims=True), jnp.max(up, axis=-1, keepdims=True)
        )
        weight, weight_up = jnp.exp(second - top), jnp.exp(up - top)
        total = jnp.sum(weight, axis=-1, keepdims=True) + jnp.sum(
            weight_up, axis=-1, keepdims=True
        )
        mixed[half:, at] = (
            dot((weight / total).astype(bf16), kv_low[:, HD:])
            + dot((weight_up / total).astype(bf16), kv_up[:, HD:])
        ).astype(bf16)
        logs[h, half:, :] = top + jnp.log(total)
    ordered[...] = dot(mixed[...], order[...]).astype(bf16)
    ordered_back[...] = dot(mixed[...], order_back[...]).astype(bf16)


def branch_kernel(mixed, w_out0, w_out1, w_out2, w_out3, own, other, w_out):
    quarter = mixed.shape[0] // 4
    count, columns = w_out0.shape[1:]
    for s, part in enumerate((w_out0, w_out1, w_out2, w_out3)):
        w_out[:, column_block(s, count)] = part[...]
    for k in range(2):
        part = dot(mixed[...], w_out[k])
        at = slice(k * columns, (k + 1) * columns)
        own[:quarter, at] = part[:quarter]
        other[:quarter, at] = part[quarter : 2 * quarter]
        own[quarter:, at] = part[2 * quarter : 3 * quarter]
        other[quarter:, at] = part[3 * quarter :]


def route_kernel(
    tokens,
    own,
    received,
    small,
    gains,
    hits,
    places_of,
    placer,
    sent,
    midway,
    moe_low,
    gates,
    parts,
):
    middle = tokens[...].astype(f32) + (own[...] + received[...])
    midway[...] = middle
    normal, _ = normal_of(middle)
    moe = (normal * gains[1:2]).astype(bf16)
    moe_low[...] = moe
    sent[:, : moe.shape[1]] = dot(placer[...], moe).astype(bf16)
    logits = dot(moe, small[...])
    picked = [
        jnp.sum(hits[k].astype(f32) * logits, axis=-1, keepdims=True) for k in range(TOPK)
    ]
    top = picked[0]
    for value in picked[1:]:
        top = jnp.maximum(top, value)
    weights = [jnp.exp(value - top) for value in picked]
    total = weights[0]
    for value in weights[1:]:
        total = total + value
    lane = lax.broadcasted_iota(jnp.int32, gates.shape, 1)
    gate_at = jnp.zeros(places_of.shape[1:], f32)
    kept = jnp.zeros(gates.shape, f32)
    for k in range(TOPK):
        gate = weights[k] / total
        kept = jnp.where(lane == k, gate, kept)
        gate_at = gate_at + places_of[k].astype(f32) * gate
    gates[...] = kept
    block = jnp.zeros((sent.shape[0], 128), f32)
    for i, part in enumerate(in_three(gate_at)):
        parts[i] = part
        block = block + t_dot(part, jnp.where(lane == i, 1.0, 0.0).astype(bf16))
    sent[:, moe.shape[1] :] = block.astype(bf16)


def fetched(core, weights, held, sems, first):
    copies = [
        pltpu.make_async_copy(weights.at[m, core[0]], held.at[m], sems.at[m]) for m in range(3)
    ]

    @pl.when(pl.program_id(0) == 0)
    def _():
        for m in first:
            copies[m].start()

    def ready(m):
        @pl.when(pl.program_id(0) == 0)
        def _():
            copies[m].wait()

        return held[m]

    return ready


def forward_kernel(
    core, sent, cot, weights, out, hidden, out_grad, factor, other_factor, held, sems
):
    ready = fetched(core, weights, held, sems, (0, 1, 2))
    width = out.shape[1]
    rows = sent[:, :width]
    gate_pre, up_pre = dot(rows, ready(0)), dot(rows, ready(1))
    sigmoid = 1.0 / (1.0 + jnp.exp(-gate_pre))
    silu = gate_pre * sigmoid
    low = (silu * up_pre).astype(bf16)
    hidden[...] = low
    out[...] = dot_t(low, ready(2)).astype(bf16)
    gates = jnp.sum(sent[:, width:].astype(f32), axis=-1, keepdims=True)
    out_grad[...] = (gates * cot[...].astype(f32)).astype(bf16)
    factor[...] = up_pre * sigmoid * (1.0 + gate_pre * (1.0 - sigmoid))
    other_factor[...] = silu


def backward_kernel(
    core, out_grad, factor, other_factor, weights, rows_grad, gate_grad, up_grad, held, sems
):
    ready = fetched(core, weights, held, sems, (2, 0, 1))
    hidden_grad = dot(out_grad[...], ready(2))
    low = (hidden_grad * factor[...]).astype(bf16)
    other = (hidden_grad * other_factor[...]).astype(bf16)
    gate_grad[...] = low
    up_grad[...] = other
    rows_grad[...] = (dot_t(low, ready(0)) + dot_t(other, ready(1))).astype(bf16)


def expert_call(kernel, block, core, arrays, weights, outs):
    count = arrays[0].shape[0]

    def rows(columns):
        return pl.BlockSpec((block, columns), lambda i, core: (i, 0))

    return pl.pallas_call(
        kernel,
        out_shape=[jax.ShapeDtypeStruct((count, columns), dtype) for columns, dtype in outs],
        grid_spec=pltpu.PrefetchScalarGridSpec(
            num_scalar_prefetch=1,
            grid=(count // block,),
            in_specs=[rows(a.shape[1]) for a in arrays] + [pl.BlockSpec(memory_space=pltpu.HBM)],
            out_specs=[rows(columns) for columns, _ in outs],
            scratch_shapes=[
                pltpu.VMEM((3,) + weights.shape[2:], bf16),
                pltpu.SemaphoreType.DMA((3,)),
            ],
        ),
        compiler_params=pltpu.CompilerParams(vmem_limit_bytes=ROOM),
        cost_estimate=COST,
    )(core, *arrays, weights)


def weights_kernel(sent, out_grad, hidden, gate_grad, up_grad, sums):
    rows = sent[...]
    sums[0] = t_dot(rows, gate_grad[...]).astype(bf16)
    sums[1] = t_dot(rows, up_grad[...]).astype(bf16)
    sums[2] = t_dot(out_grad[...], hidden[...]).astype(bf16)


def expert_weights_grad(sent, out_grad, hidden, gate_grad, up_grad, block=256):
    count, width = out_grad.shape
    columns = hidden.shape[1]
    part = pl.BlockSpec((count, block), lambda i: (0, i))
    whole = pl.BlockSpec((count, columns), lambda i: (0, 0), pipeline_mode=pl.Buffered(1))
    return pl.pallas_call(
        weights_kernel,
        out_shape=jax.ShapeDtypeStruct((3, width, columns), bf16),
        grid=(width // block,),
        in_specs=[part, part, whole, whole, whole],
        out_specs=pl.BlockSpec((3, block, columns), lambda i: (0, i, 0)),
        compiler_params=pltpu.CompilerParams(vmem_limit_bytes=ROOM),
        cost_estimate=COST,
    )(sent, out_grad, hidden, gate_grad, up_grad)


def combine_kernel(
    midway, parts, returned, cot, hits, places_of, gates, small, moe_low, output, moe_part, router_grad
):
    rows = returned[...]
    output[...] = (
        midway[...] + (dot(parts[0], rows) + (dot(parts[1], rows) + dot(parts[2], rows)))
    ).astype(bf16)
    agreement = dot_t(cot[...], rows)
    lane = lax.broadcasted_iota(jnp.int32, gates.shape, 1)
    gate, grad = [], []
    mean = jnp.zeros((gates.shape[0], 1), f32)
    for k in range(TOPK):
        gate.append(jnp.sum(jnp.where(lane == k, gates[...], 0.0), axis=-1, keepdims=True))
        grad.append(jnp.sum(places_of[k].astype(f32) * agreement, axis=-1, keepdims=True))
        mean = mean + gate[k] * grad[k]
    logit_grad = jnp.zeros(gates.shape, f32)
    for k in range(TOPK):
        logit_grad = logit_grad + hits[k].astype(f32) * (gate[k] * (grad[k] - mean))
    logit_grad = logit_grad.astype(bf16)
    moe_part[...] = dot_t(logit_grad, small[...])
    router_grad[...] = t_dot(moe_low[...], logit_grad)


def home_kernel(placer_t, home, moe_part, midway, cot, gains, midway_grad, branch_low, gain_grad):
    grad = dot(placer_t[...], home[...]) + moe_part[...]
    normal, inverse = normal_of(midway[...])
    result = cot[...].astype(f32) + norm_back(grad, normal, inverse, gains[1:2])
    midway_grad[...] = result
    branch_low[...] = result.astype(bf16)
    gain_grad[...] = jnp.broadcast_to(
        jnp.sum(grad * normal, axis=0, keepdims=True), gain_grad.shape
    )


def out_grad_kernel(mixed, own, other, branch, *blocks):
    quarter = own.shape[0] // 2
    branch[:quarter] = own[:quarter]
    branch[quarter : 2 * quarter] = other[:quarter]
    branch[2 * quarter : 3 * quarter] = own[quarter:]
    branch[3 * quarter :] = other[quarter:]
    count, columns = blocks[0].shape[1:]
    for k in range(2):
        grad = t_dot(mixed[...], branch[:, column_block(k, columns)]).astype(bf16)
        for s in range(4):
            blocks[s][k] = grad[column_block(s, count)]


def attend_back_kernel(
    branch,
    w_out,
    order,
    queries,
    kv_low,
    kv_up,
    logs,
    q_place,
    low_place,
    up_place,
    cosines,
    sines,
    normed,
    dq,
    dkv,
    block0,
    block1,
    block2,
    block3,
    grads,
    acc_low,
    acc_up,
    *,
    scale,
    pieces,
    heads,
):
    half = queries.shape[0] // 2
    columns = w_out.shape[2]
    ordered = dot_t(branch[:, :columns], w_out[0]) + dot_t(branch[:, columns:], w_out[1])
    grads[...] = dot_t(ordered.astype(bf16), order[...]).astype(bf16)
    allowed_low = low_place[...] <= q_place[...]
    allowed_up = up_place[...] <= q_place[half:, :]
    key_low, value_low = kv_low[:, :HD], kv_low[:, HD:]
    key_up, value_up = kv_up[:, :HD], kv_up[:, HD:]
    for h in range(heads):
        at = slice(h * HD, (h + 1) * HD)
        q, grad, log = queries[:, at], grads[:, at], logs[h]
        low = jnp.where(allowed_low, dot_t(q, key_low) * scale, NEGATIVE)
        up = jnp.where(allowed_up, dot_t(q[half:], key_up) * scale, NEGATIVE)
        probs_low, probs_up = jnp.exp(low - log), jnp.exp(up - log[half:])
        grad_low, grad_up = dot_t(grad, value_low), dot_t(grad[half:], value_up)
        along = jnp.sum(probs_low * grad_low, axis=-1, keepdims=True)
        along_up = along[half:] + jnp.sum(probs_up * grad_up, axis=-1, keepdims=True)
        along = jnp.concatenate([along[:half], along_up])
        score_low = (probs_low * (grad_low - along)).astype(bf16)
        score_up = (probs_up * (grad_up - along_up)).astype(bf16)
        part = dot(score_low, key_low)
        part = jnp.concatenate([part[:half], part[half:] + dot(score_up, key_up)]) * scale
        dq[:, at] = turn(part, cosines[...], -sines[...]).astype(bf16)
        terms = (
            (acc_low, slice(0, HD), t_dot(q, score_low)),
            (acc_up, slice(0, HD), t_dot(q[half:], score_up)),
            (acc_low, slice(HD, 2 * HD), t_dot(grad, probs_low.astype(bf16))),
            (acc_up, slice(HD, 2 * HD), t_dot(grad[half:], probs_up.astype(bf16))),
        )
        for acc, rows, term in terms:
            if h == 0:
                acc[rows] = term
            else:
                acc[rows] += term
    for s, block in enumerate((block0, block1, block2, block3)):
        block[...] = t_dot(normed[:, column_block(s, block.shape[0])], dq[...]).astype(bf16)
    for acc, first in ((acc_low, 0), (acc_up, half)):
        dk = (acc[:HD].T * scale).astype(bf16)
        dv = acc[HD:].T.astype(bf16)
        for i in range(pieces):
            dkv[i, first : first + half, :HD] = dk[i * half : (i + 1) * half]
            dkv[i, first : first + half, HD:] = dv[i * half : (i + 1) * half]


def sum_kernel(dq, cosines, sines, *refs):
    w_q, kvs, (parts, dkv, own, other) = refs[:4], refs[4:8], refs[8:]
    total = jnp.sum(parts[...].astype(f32), axis=0)
    dkv[:, :HD] = turn(total[:, :HD], cosines[...], -sines[...]).astype(bf16)
    dkv[:, HD:] = total[:, HD:].astype(bf16)
    quarter = own.shape[0] // 2
    for s in range(4):
        grad = dot_t(dq[...], w_q[s][...]) + dot_t(dkv[...], kvs[s][:, :WIDE])
        at = column_block(s, w_q[s].shape[0])
        own[:quarter, at] = grad[:quarter]
        other[:quarter, at] = grad[quarter : 2 * quarter]
        own[quarter:, at] = grad[2 * quarter : 3 * quarter]
        other[quarter:, at] = grad[3 * quarter :]


def stack_kernel(gate, up, down, late, out):
    del late
    out[0] = gate[...]
    out[1] = up[...]
    out[2] = down[...]


def small_grad_kernel(order, router_grad, gain_grad, late, out):
    del late
    row = lax.broadcasted_iota(jnp.int32, gain_grad.shape, 0)
    second = jnp.where(row == 1, gain_grad[...], 0.0).astype(bf16)
    small = router_grad[...] + t_dot(second, gain_picker())
    out[...] = t_dot(order[...], small.astype(bf16))


def input_kernel(both, own, received, midway_grad, gains, order, small, normed, dkv, out, *blocks):
    grad = own[...] + received[...]
    quarter = own.shape[0] // 2
    tokens = jnp.concatenate([both[:quarter], both[2 * quarter : 3 * quarter]])
    normal, inverse = normal_of(tokens.astype(f32))
    parts = in_three(norm_back(grad, normal, inverse, gains[0:1]))
    moved = dot_t(jnp.concatenate(parts), order[...])
    count = 2 * quarter
    out[...] = midway_grad[...] + (
        moved[:count] + (moved[count : 2 * count] + moved[2 * count :])
    )
    gain_grad = jnp.sum(grad * normal, axis=0, keepdims=True)
    row = lax.broadcasted_iota(jnp.int32, gains.shape, 0)
    gain_grad = jnp.where(row == 0, gain_grad, 0.0).astype(bf16)
    small = small[...] + t_dot(gain_grad, gain_picker())
    rows = blocks[0].shape[0]
    for s, block in enumerate(blocks):
        at = column_block(s, rows)
        block[:, :WIDE] = t_dot(normed[:, at], dkv[...]).astype(bf16)
        block[:, WIDE:] = small[at].astype(bf16)


def body(
    tokens,
    cotangent,
    pair_of,
    routes,
    attn_gain,
    moe_gain,
    w_query,
    w_key,
    w_value,
    w_out,
    w_router,
    w_gate,
    w_up,
    w_down,
):
    rows = tokens.shape[1]
    half = rows // 2
    width = tokens.shape[2]
    shard = w_query.shape[1]
    ctx_count = 16
    experts = w_router.shape[2]
    columns = w_gate.shape[3]
    per_group = H // KVH
    qw = per_group * HD
    scale = 1.0 / math.sqrt(HD)
    core = lax.axis_index("core")
    ylo, z, yhi = lax.axis_index("ylo"), lax.axis_index("z"), lax.axis_index("yhi")
    x = lax.axis_index("x")
    piece_rows = 2 * shard
    slots = experts * SLOTS
    own_tokens, cot = tokens[0], cotangent[0]

    def halves(matrix):
        return [matrix[:, : matrix.shape[1] // 2], matrix[:, matrix.shape[1] // 2 :]]

    small = jnp.concatenate([w_router[0], attn_gain[0][:, None], moe_gain[0][:, None]], axis=-1)
    small = jnp.pad(small, ((0, 0), (0, 128 - experts - 2)))
    query_halves, key_halves, value_halves = halves(w_query[0]), halves(w_key[0]), halves(w_value[0])
    pairs = [
        jnp.concatenate([k, v, small, q], axis=-1)
        for k, v, q in zip(key_halves, value_halves, query_halves)
    ]
    pieces = gather_pieces(pairs, yhi, core, ("core", "yhi"), SAME, OTHER)
    out_pieces = gather_pieces(
        halves(w_out[0]), yhi, yhi, ("ylo", "core", "yhi"), OUT_SAME, OUT_OTHER
    )
    other_tokens = partner(own_tokens)
    pieces, out_pieces, x, z, own_tokens, other_tokens, pair_of = together(
        pieces, out_pieces, x, z, own_tokens, other_tokens, pair_of
    )

    plane_rows = 16 * piece_rows
    plane = spread(pieces, 16, PLANE)
    both = jnp.concatenate(
        [own_tokens[:half], other_tokens[:half], own_tokens[half:], other_tokens[half:]]
    )
    order, out_order, level_order = order_matrix(16, x), order_matrix(8, x), level_order_matrix(z)
    plane, both, out_pieces, order, out_order, level_order, pair_of = together(
        plane, both, out_pieces, order, out_order, level_order, pair_of
    )

    plane = plane.reshape(plane_rows, -1)
    w_kvs = along("x", plane[:, : 3 * HD])
    wo = spread(out_pieces, 16, LEVEL)
    (both,) = call(order_kernel, [((2 * rows, width), bf16)], both, order)

    def two_cores(ctx):
        return jnp.stack([ctx + core, ctx + 1 - core], axis=-1).reshape(-1)

    ctx_here = (ylo * 4 + z) * 2
    q_place = places(pair_of, two_cores(ctx_here), rows, ctx_count)
    q_place = q_place.transpose(1, 0, 2).reshape(2 * rows, 1)
    key_place = places(
        pair_of, two_cores(jnp.arange(8, dtype=jnp.int32) * 2), rows, ctx_count
    )
    low_place, up_place = key_place[:, 0].reshape(1, -1), key_place[:, 1].reshape(1, -1)
    frequency = jnp.exp(jnp.arange(HD // 2, dtype=f32) * (-2.0 * math.log(ROPE_BASE) / HD))
    angles = q_place.astype(f32) * frequency[None, :]
    cosines, sines = jnp.cos(angles), jnp.sin(angles)
    cosines = jnp.concatenate([cosines, cosines], axis=-1)
    sines = jnp.concatenate([-sines, sines], axis=-1)
    w_q, w_kvs, wo, both, q_place, low_place, up_place, cosines, sines, chosen = together(
        plane[:, 3 * HD :], w_kvs, wo, both, q_place, low_place, up_place, cosines, sines, routes[0, 0]
    )

    w_q = along("x", w_q)
    wo = along("z", wo.reshape(2, qw // 4, width // 2))
    normed, key_value, gains = call(
        keys_kernel,
        [((2 * rows, width), bf16), ((2 * rows, 2 * HD), bf16), ((8, width), f32)],
        both,
        cosines,
        sines,
        *w_kvs,
    )
    all_kv = spread(key_value, 8, RING)
    small, moe_gains = call(
        small_kernel, [((width, 128), bf16), ((8, width), f32)], order, *w_kvs
    )
    lanes = jnp.arange(128, dtype=jnp.int32)
    hits = (chosen.T[:, :, None] == lanes[None, None, :]).astype(bf16)
    earlier = (lanes[:, None] > lanes[None, :]).astype(bf16)
    before = dot(earlier, jnp.sum(hits, axis=0))
    slot_index = jnp.sum(hits.astype(f32) * before[None], axis=-1).astype(jnp.int32)
    target = chosen.T * SLOTS + slot_index
    slot_row = jnp.arange(slots, dtype=jnp.int32)
    places_of = (target[:, :, None] == slot_row[None, None, :]).astype(bf16)
    placer_t = jnp.sum(places_of, axis=0)
    placer = placer_t.T
    (cot_rows,) = call(order_kernel, [((slots, width), bf16)], placer, cot)
    (queries,) = call(
        query_kernel, [((2 * rows, qw), bf16)], normed, cosines, sines, *w_q, cost=LONG
    )
    (expert_shards_in,) = call(
        stack_kernel, [((3,) + w_gate.shape[1:], bf16)], w_gate[0], w_up[0], w_down[0], gains
    )
    (
        queries, all_kv, small, moe_gains, hits, places_of, placer_t, placer, cot_rows,
        expert_shards_in, wo,
    ) = together(
        queries, all_kv, small, moe_gains, hits, places_of, placer_t, placer, cot_rows,
        expert_shards_in, wo,
    )
    expert_weights = lax.all_gather(expert_shards_in, CTX, axis=2, tiled=True)

    arrived_cot = to_owners(cot_rows.reshape(experts, SLOTS, width))
    sizes = dict(scale=scale, pieces=8, heads=per_group)
    keys = 8 * rows
    mixed, mixed_back, logs, kv_low, kv_up = call(
        functools.partial(attend_kernel, **sizes),
        [
            ((2 * rows, qw), bf16),
            ((2 * rows, qw), bf16),
            ((per_group, 2 * rows, 1), f32),
            ((keys, 2 * HD), bf16),
            ((keys, 2 * HD), bf16),
        ],
        queries,
        q_place,
        low_place,
        up_place,
        level_order,
        out_order,
        all_kv,
        scratch=[pltpu.VMEM((2 * rows, qw), bf16)],
    )

    branch_own, branch_other, wo = call(
        branch_kernel,
        [((rows, width), f32), ((rows, width), f32), ((2, qw, width // 2), bf16)],
        mixed,
        *wo,
    )
    sent, midway, moe_low, gates, gate_parts = call(
        route_kernel,
        [
            ((slots, width + 128), bf16),
            ((rows, width), f32),
            ((rows, width), bf16),
            ((rows, 128), f32),
            ((3, rows, slots), bf16),
        ],
        own_tokens,
        branch_own,
        partner(branch_other),
        small,
        moe_gains,
        hits,
        places_of,
        placer,
    )
    sent, arrived_cot = together(sent, arrived_cot)

    sent = to_owners(sent.reshape(experts, SLOTS, width + 128)).reshape(slots, width + 128)
    mine = core.reshape(1)
    expert_out, hidden, out_grad, factor, other_factor = expert_call(
        forward_kernel,
        slots // 2,
        mine,
        [sent, arrived_cot.reshape(slots, width)],
        expert_weights,
        [(width, bf16), (columns, bf16), (width, bf16), (columns, f32), (columns, f32)],
    )
    expert_out, factor = together(expert_out, factor)

    returned = to_owners(expert_out.reshape(experts, SLOTS, width))
    rows_grad, gate_grad, up_grad = expert_call(
        backward_kernel,
        128,
        mine,
        [out_grad, factor, other_factor],
        expert_weights,
        [(width, bf16), (columns, bf16), (columns, bf16)],
    )
    expert_sums = expert_weights_grad(sent, out_grad, hidden, gate_grad, up_grad)
    returned, rows_grad, expert_sums = together(returned, rows_grad, expert_sums)
    home_grad = to_owners(rows_grad.reshape(experts, SLOTS, width))
    expert_sums = lax.psum_scatter(expert_sums, RING, scatter_dimension=1, tiled=True)
    output, moe_part, router_grad = call(
        combine_kernel,
        [((rows, width), bf16), ((rows, width), f32), ((width, 128), f32)],
        midway,
        gate_parts,
        returned.reshape(slots, width),
        cot,
        hits,
        places_of,
        gates,
        small,
        moe_low,
    )
    home_grad, moe_part = together(home_grad, moe_part)
    midway_grad, branch_low, gain_two_grad = call(
        home_kernel,
        [((rows, width), f32), ((rows, width), bf16), ((8, width), f32)],
        placer_t,
        home_grad.reshape(slots, width),
        moe_part,
        midway,
        cot,
        moe_gains,
    )
    branch, *out_w_grad = call(
        out_grad_kernel,
        [((2 * rows, width), bf16)] + [((2, qw // 4, width // 2), bf16)] * 4,
        mixed_back,
        branch_low,
        partner(branch_low),
    )
    branch, out_w_grad = together(branch, out_w_grad)
    out_w_grad = added(back_along_x(out_w_grad))

    dq, dkv, *q_w_grad = call(
        functools.partial(attend_back_kernel, **sizes),
        [((2 * rows, qw), bf16), ((8, 2 * rows, 2 * HD), bf16)]
        + [((plane_rows, qw), bf16)] * 4,
        branch,
        wo,
        level_order,
        queries,
        kv_low,
        kv_up,
        logs,
        q_place,
        low_place,
        up_place,
        cosines,
        sines,
        normed,
        scratch=[
            pltpu.VMEM((2 * rows, qw), bf16),
            pltpu.VMEM((2 * HD, keys), f32),
            pltpu.VMEM((2 * HD, keys), f32),
        ],
    )
    dkv = exchange(dkv, RING)
    q_w_grad = back_along_x(q_w_grad)
    (small_grad,) = call(
        small_grad_kernel, [((width, 128), f32)], order, router_grad, gain_two_grad, dq
    )
    dkv, out_w_grad, small_grad, q_w_grad[1], q_w_grad[3] = together(
        dkv, out_w_grad, small_grad, q_w_grad[1], q_w_grad[3]
    )

    dkv, normed_own, normed_other = call(
        sum_kernel,
        [((2 * rows, 2 * HD), bf16), ((rows, width), f32), ((rows, width), f32)],
        dq,
        cosines,
        sines,
        *w_q,
        *w_kvs,
        dkv,
    )
    input_grad, *kvs_grad = call(
        input_kernel,
        [((rows, width), f32)] + [((plane_rows, 3 * HD), bf16)] * 4,
        both,
        normed_own,
        partner(normed_other),
        midway_grad,
        gains,
        order,
        small_grad,
        normed,
        dkv,
    )
    q_w_grad = added(q_w_grad, kvs_grad[0])
    kvs_grad, out_w_grad, input_grad = together(kvs_grad, out_w_grad, input_grad)

    out_w_grad = exchange(out_w_grad.reshape(16, piece_rows, width // 2), OUT_PLANE)
    kvs_grad = added(back_along_x(kvs_grad))
    plane_grad = jnp.concatenate([q_w_grad, kvs_grad], axis=-1)
    plane_grad, out_w_grad, expert_sums = together(plane_grad, out_w_grad, expert_sums)
    plane_grad = exchange(plane_grad.reshape(16, piece_rows, qw + 3 * HD), PLANE)

    def summed(pieces):
        return jnp.sum(pieces.astype(f32), axis=0)

    def expert_shards(grad):
        count = grad.shape[1] // 2
        kept = lax.dynamic_slice_in_dim(grad, core * count, count, axis=1)
        given = partner(lax.dynamic_slice_in_dim(grad, (1 - core) * count, count, axis=1))
        both = jnp.stack([pick(core, kept, given), pick(core, given, kept)], axis=1)
        return [both[i : i + 1].astype(f32) for i in range(3)]

    out_w_grad = scatter_pieces(
        summed(out_w_grad), yhi, yhi, ("ylo", "core", "yhi"), OUT_SAME, OUT_OTHER
    )
    w_gate_grad, w_up_grad, w_down_grad = expert_shards(expert_sums)
    plane_grad, out_w_grad, w_gate_grad, w_up_grad, w_down_grad = together(
        plane_grad, out_w_grad, w_gate_grad, w_up_grad, w_down_grad
    )
    plane_grad = scatter_pieces(summed(plane_grad), yhi, core, ("core", "yhi"), SAME, OTHER)
    plane_grad = plane_grad.reshape(shard, 2, -1)

    def joined(first, last):
        return plane_grad[:, :, first:last].reshape(1, shard, -1)

    small_grad = jnp.sum(plane_grad[None, :, :, qw + 2 * HD :], axis=2)

    return (
        output[None],
        input_grad[None],
        small_grad[:, :, experts],
        small_grad[:, :, experts + 1],
        joined(0, qw),
        joined(qw, qw + HD),
        joined(qw + HD, qw + 2 * HD),
        out_w_grad[None],
        small_grad[:, :, :experts],
        w_gate_grad,
        w_up_grad,
        w_down_grad,
    )


def solution(mesh):
    fine = Mesh(mesh.devices.reshape(2, 4, 2, 4, 2), AXES)
    seq = P(FSDP, CTX, None)
    vector = P(None, AXES)
    matrix = P(None, AXES, None)
    expert = P(None, FSDP, CTX, None)
    in_specs = (
        seq,
        seq,
        P(),
        P(None, FSDP, CTX, None),
        vector,
        vector,
        matrix,
        matrix,
        matrix,
        matrix,
        matrix,
        expert,
        expert,
        expert,
    )
    out_specs = (
        seq,
        seq,
        vector,
        vector,
        matrix,
        matrix,
        matrix,
        matrix,
        matrix,
        expert,
        expert,
        expert,
    )
    return jax.shard_map(body, mesh=fine, in_specs=in_specs, out_specs=out_specs, check_vma=False)
```

```python
import functools
import math

import jax
import jax.numpy as jnp
from jax import lax
from jax.experimental import pallas as pl
from jax.experimental.pallas import tpu as pltpu
from jax.sharding import Mesh
from jax.sharding import PartitionSpec as P

H = 12
KVH = 2
HD = 128
TOPK = 4

EPSILON = 1e-06
ROPE_BASE = 1000000.0
NEGATIVE = -1e30

AXES = ("ylo", "z", "core", "x", "yhi")
CTX = ("ylo", "z", "core")
FSDP = ("x", "yhi")
GROUPS = [
    [
        (((group ^ yhi) * 4 + z) * 2 + core) * 8 + x * 2 + yhi
        for x in range(4)
        for yhi in range(2)
        for core in range(2)
    ]
    for group in range(2)
    for z in range(4)
]
RING = ("ylo", "z")
PLANE = ("ylo", "z", "yhi")
OUT_PLANE = ("yhi", "z", "ylo")
LEVEL = ("yhi", "ylo", "x")
GROUPS = [
    [
        (((group ^ yhi) * 4 + z) * 2 + core) * 8 + x * 2 + yhi
        for x in range(4)
        for yhi in range(2)
        for core in range(2)
    ]
    for group in range(2)
    for z in range(4)
]
RING = ("ylo", "z")
ROWS_ORDER = ("ylo", "z", "yhi", "x")
OUT_ORDER = ("yhi", "z", "ylo", "x")
SLOTS = 40

bf16 = jnp.bfloat16
f32 = jnp.float32


def dot(left, right):
    return jnp.dot(left, right, preferred_element_type=f32)


def dot_t(left, right):
    return lax.dot_general(left, right, (((1,), (1,)), ((), ())), preferred_element_type=f32)


def t_dot(left, right):
    return lax.dot_general(left, right, (((0,), (0,)), ((), ())), preferred_element_type=f32)


def exchange(pieces, axes):
    return lax.all_to_all(pieces, axes, split_axis=0, concat_axis=0, tiled=True)


def to_owners(pieces):
    return lax.all_to_all(
        pieces, AXES, split_axis=0, concat_axis=0, axis_index_groups=GROUPS, tiled=True
    )


def spread(piece, count, axes):
    return exchange(jnp.broadcast_to(piece[None], (count,) + piece.shape), axes)


def after(value, earlier):
    return lax.optimization_barrier((value, earlier))[0]


def together(*values):
    return lax.optimization_barrier(values)


def partner(value):
    return lax.ppermute(value, "core", [(0, 1), (1, 0)])


def route(axes, sizes, move):
    pairs = []
    for source in range(math.prod(sizes)):
        rest, at = source, []
        for size in reversed(sizes):
            at.insert(0, rest % size)
            rest //= size
        target = 0
        for size, value in zip(sizes, move(*at)):
            target = target * size + value
        pairs.append((source, target))
    return pairs


SAME = route(("core", "yhi"), (2, 2), lambda c, h: (h, c))
OTHER = route(("core", "yhi"), (2, 2), lambda c, h: (1 - h, c))
OUT_SAME = route(("ylo", "core", "yhi"), (2, 2, 2), lambda j, c, h: (c, j, h))
OUT_OTHER = route(("ylo", "core", "yhi"), (2, 2, 2), lambda j, c, h: (c, j, 1 - h))


def back(pairs):
    return [(target, source) for source, target in pairs]


def pick(flag, if_zero, if_one):
    return jnp.where(flag == 0, if_zero, if_one)


def gather_pieces(pair, flag, key, axes, same, other):
    first = lax.ppermute(pick(flag, pair[0], pair[1]), axes, same)
    second = lax.ppermute(pick(flag, pair[1], pair[0]), axes, other)
    return pick(
        key, jnp.concatenate([first, second]), jnp.concatenate([second, first])
    )


def scatter_pieces(piece, flag, key, axes, same, other):
    count = piece.shape[0] // 2
    mine, rest = piece[:count], piece[count:]
    first = lax.ppermute(pick(key, mine, rest), axes, back(same))
    second = lax.ppermute(pick(key, rest, mine), axes, back(other))
    return pick(flag, jnp.concatenate([first, second], axis=-1), jnp.concatenate([second, first], axis=-1))


def along(axis, piece):
    return [piece] + [
        lax.ppermute(piece, axis, [(i, (i + s) % 4) for i in range(4)]) for s in (1, 2, 3)
    ]


def back_along_x(blocks):
    return [blocks[0]] + [
        lax.ppermute(blocks[s], "x", [(i, (i - s) % 4) for i in range(4)]) for s in (1, 2, 3)
    ]


def added(blocks):
    (total,) = call(add_kernel, [(blocks[0].shape, bf16)], *blocks, cost=LONG)
    return total


def sum_of(first, second, third, fourth):
    return (
        (first[...].astype(f32) + second[...].astype(f32))
        + (third[...].astype(f32) + fourth[...].astype(f32))
    ).astype(bf16)


def add_kernel(first, second, third, fourth, total):
    total[...] = sum_of(first, second, third, fourth)


def add_both_kernel(*refs):
    total = refs[8]
    count = refs[0].shape[1]
    total[:, :count] = sum_of(*refs[:4])
    total[:, count:] = sum_of(*refs[4:8])


def order_matrix(groups, x):
    index = jnp.arange(groups * 96, dtype=jnp.int32)
    turn_of, group, row = index // (groups * 24), index // 24 % groups, index % 24
    own = group * 96 + (x - turn_of) % 4 * 24 + row
    return (index[:, None] == own[None, :]).astype(bf16)


def level_order_matrix(z):
    index = jnp.arange(8 * 96, dtype=jnp.int32)
    own = (z - index // 192) % 4 * 192 + index % 192
    return (index[:, None] == own[None, :]).astype(bf16)


def places(pair_of, ctx, row_count, ctx_count):
    half_size = row_count // 2
    pair = jnp.sum(
        jnp.where(ctx[:, None] == jnp.arange(ctx_count, dtype=jnp.int32)[None], pair_of[None], 0),
        axis=1,
    )
    block = jnp.stack([pair, 2 * ctx_count - 1 - pair], axis=1)
    return block[:, :, None] * half_size + jnp.arange(half_size, dtype=jnp.int32)[None, None]


def in_three(value):
    high = value.astype(bf16)
    rest = value - high.astype(f32)
    middle = rest.astype(bf16)
    return [high, middle, (rest - middle.astype(f32)).astype(bf16)]


def call(kernel, outs, *args, scratch=(), cost=None):
    def whole(shape):
        return pl.BlockSpec(shape, lambda i: (0,) * len(shape))

    return pl.pallas_call(
        kernel,
        out_shape=[jax.ShapeDtypeStruct(shape, dtype) for shape, dtype in outs],
        grid=(1,),
        in_specs=[whole(a.shape) for a in args],
        out_specs=[whole(shape) for shape, _ in outs],
        scratch_shapes=list(scratch),
        compiler_params=pltpu.CompilerParams(vmem_limit_bytes=ROOM),
        cost_estimate=COST if cost is None else cost,
    )(*args)


ROOM = 58 << 20
COST = pl.CostEstimate(flops=1 << 20, bytes_accessed=1 << 18, transcendentals=0)
LONG = pl.CostEstimate(flops=1 << 35, bytes_accessed=1 << 27, transcendentals=0)
WIDE = 2 * HD
EXPERTS = 16


def turn(vectors, cosines, sines):
    return vectors * cosines + pltpu.roll(vectors, HD // 2, axis=1) * sines


def gain_picker():
    row = lax.broadcasted_iota(jnp.int32, (8, 128), 0)
    column = lax.broadcasted_iota(jnp.int32, (8, 128), 1)
    return jnp.where((column == row + EXPERTS) & (row < 2), 1.0, 0.0).astype(bf16)


def normal_of(stream):
    inverse = lax.rsqrt(jnp.mean(stream * stream, axis=-1, keepdims=True) + EPSILON)
    return stream * inverse, inverse


def norm_back(grad, normal, inverse, gain):
    scaled = grad * gain
    return inverse * (scaled - normal * jnp.mean(scaled * normal, axis=-1, keepdims=True))


def column_block(s, count):
    return slice(s * count, (s + 1) * count)


def order_kernel(rows, order, out):
    out[...] = dot(rows[...], order[...]).astype(bf16)


def keys_kernel(both, cosines, sines, *refs):
    kvs, (normed, key_value, gains) = refs[:4], refs[4:]
    count = kvs[0].shape[0]
    for s in range(4):
        gains[:, column_block(s, count)] = dot_t(gain_picker(), kvs[s][:, WIDE:])
    normal, _ = normal_of(both[...].astype(f32))
    normed[...] = (normal * gains[0:1]).astype(bf16)
    kv = dot(normed[:, column_block(0, count)], kvs[0][:, :WIDE])
    for s in range(1, 4):
        kv = kv + dot(normed[:, column_block(s, count)], kvs[s][:, :WIDE])
    key_value[:, :HD] = turn(kv[:, :HD], cosines[...], sines[...]).astype(bf16)
    key_value[:, HD:] = kv[:, HD:].astype(bf16)


def small_kernel(order, kvs0, kvs1, kvs2, kvs3, small, gains):
    count = kvs0.shape[0]
    total = jnp.zeros(small.shape, f32)
    for s, kvs in enumerate((kvs0, kvs1, kvs2, kvs3)):
        total = total + dot(order[:, column_block(s, count)], kvs[:, WIDE:])
    small[...] = total.astype(bf16)
    gains[...] = dot_t(gain_picker(), small[...])


def query_kernel(normed, cosines, sines, w_q0, w_q1, w_q2, w_q3, queries):
    w_q = (w_q0, w_q1, w_q2, w_q3)
    count = w_q0.shape[0]
    for h in range(queries.shape[1] // HD):
        at = column_block(h, HD)
        q = dot(normed[:, column_block(0, count)], w_q0[:, at])
        for s in range(1, 4):
            q = q + dot(normed[:, column_block(s, count)], w_q[s][:, at])
        queries[:, at] = turn(q, cosines[...], sines[...]).astype(bf16)


def attend_kernel(
    queries,
    q_place,
    low_place,
    up_place,
    order,
    order_back,
    kv,
    ordered,
    ordered_back,
    logs,
    kv_low,
    kv_up,
    mixed,
    *,
    scale,
    pieces,
    heads,
):
    half = kv.shape[1] // 2
    for i in range(pieces):
        kv_low[i * half : (i + 1) * half, :] = kv[i, :half]
        kv_up[i * half : (i + 1) * half, :] = kv[i, half:]
    allowed_low = low_place[...] <= q_place[...]
    allowed_up = up_place[...] <= q_place[half:, :]
    for h in range(heads):
        at = slice(h * HD, (h + 1) * HD)
        q = queries[:, at]
        low = jnp.where(allowed_low, dot_t(q, kv_low[:, :HD]) * scale, NEGATIVE)
        up = jnp.where(allowed_up, dot_t(q[half:], kv_up[:, :HD]) * scale, NEGATIVE)
        first, second = low[:half], low[half:]
        top = jnp.max(first, axis=-1, keepdims=True)
        weight = jnp.exp(first - top)
        total = jnp.sum(weight, axis=-1, keepdims=True)
        probs = (weight / total).astype(bf16)
        mixed[:half, at] = dot(probs, kv_low[:, HD:]).astype(bf16)
        logs[h, :half, :] = top + jnp.log(total)
        top = jnp.maximum(
            jnp.max(second, axis=-1, keepdims=True), jnp.max(up, axis=-1, keepdims=True)
        )
        weight, weight_up = jnp.exp(second - top), jnp.exp(up - top)
        total = jnp.sum(weight, axis=-1, keepdims=True) + jnp.sum(
            weight_up, axis=-1, keepdims=True
        )
        mixed[half:, at] = (
            dot((weight / total).astype(bf16), kv_low[:, HD:])
            + dot((weight_up / total).astype(bf16), kv_up[:, HD:])
        ).astype(bf16)
        logs[h, half:, :] = top + jnp.log(total)
    ordered[...] = dot(mixed[...], order[...]).astype(bf16)
    ordered_back[...] = dot(mixed[...], order_back[...]).astype(bf16)


def branch_kernel(mixed, w_out0, w_out1, w_out2, w_out3, own, other, w_out):
    quarter = mixed.shape[0] // 4
    count, columns = w_out0.shape[1:]
    for s, part in enumerate((w_out0, w_out1, w_out2, w_out3)):
        w_out[:, column_block(s, count)] = part[...]
    for k in range(2):
        part = dot(mixed[...], w_out[k])
        at = slice(k * columns, (k + 1) * columns)
        own[:quarter, at] = part[:quarter]
        other[:quarter, at] = part[quarter : 2 * quarter]
        own[quarter:, at] = part[2 * quarter : 3 * quarter]
        other[quarter:, at] = part[3 * quarter :]


def route_kernel(
    tokens,
    own,
    received,
    small,
    gains,
    hits,
    places_of,
    placer,
    sent,
    midway,
    moe_low,
    gates,
    parts,
):
    middle = tokens[...].astype(f32) + (own[...] + received[...])
    midway[...] = middle
    normal, _ = normal_of(middle)
    moe = (normal * gains[1:2]).astype(bf16)
    moe_low[...] = moe
    sent[:, : moe.shape[1]] = dot(placer[...], moe).astype(bf16)
    logits = dot(moe, small[...])
    picked = [
        jnp.sum(hits[k].astype(f32) * logits, axis=-1, keepdims=True) for k in range(TOPK)
    ]
    top = picked[0]
    for value in picked[1:]:
        top = jnp.maximum(top, value)
    weights = [jnp.exp(value - top) for value in picked]
    total = weights[0]
    for value in weights[1:]:
        total = total + value
    lane = lax.broadcasted_iota(jnp.int32, gates.shape, 1)
    gate_at = jnp.zeros(places_of.shape[1:], f32)
    kept = jnp.zeros(gates.shape, f32)
    for k in range(TOPK):
        gate = weights[k] / total
        kept = jnp.where(lane == k, gate, kept)
        gate_at = gate_at + places_of[k].astype(f32) * gate
    gates[...] = kept
    block = jnp.zeros((sent.shape[0], 128), f32)
    for i, part in enumerate(in_three(gate_at)):
        parts[i] = part
        block = block + t_dot(part, jnp.where(lane == i, 1.0, 0.0).astype(bf16))
    sent[:, moe.shape[1] :] = block.astype(bf16)


def fetched(core, sources, held, sems):
    copies = [
        pltpu.make_async_copy(weights.at[m, core[0]], held.at[i], sems.at[i])
        for i, (weights, m) in enumerate(sources)
    ]
    for copy in copies:
        copy.start()

    def ready(i):
        copies[i].wait()
        return held[i]

    return ready


def hidden_kernel(
    core, sent, cot, weights, hidden, out_grad, factor, other_factor, held, sems
):
    ready = fetched(core, ((weights, 0), (weights, 1)), held, sems)
    width = out_grad.shape[1]
    gates = jnp.sum(sent[:, width:].astype(f32), axis=-1, keepdims=True)
    out_grad[...] = (gates * cot[...].astype(f32)).astype(bf16)
    rows = sent[:, :width]
    gate_pre = dot(rows, ready(0))
    up_pre = dot(rows, ready(1))
    sigmoid = 1.0 / (1.0 + jnp.exp(-gate_pre))
    silu = gate_pre * sigmoid
    hidden[...] = (silu * up_pre).astype(bf16)
    factor[...] = up_pre * sigmoid * (1.0 + gate_pre * (1.0 - sigmoid))
    other_factor[...] = silu


def output_kernel(core, hidden, weights, out, held, sems):
    ready = fetched(core, ((weights, 0),), held, sems)
    out[...] = dot_t(hidden[...], ready(0)).astype(bf16)


def backward_kernel(
    core, out_grad, factor, other_factor, down, gate_up, rows_grad, gate_grad, up_grad, held, sems
):
    ready = fetched(core, ((down, 0), (gate_up, 0), (gate_up, 1)), held, sems)
    hidden_grad = dot(out_grad[...], ready(0))
    low = (hidden_grad * factor[...]).astype(bf16)
    other = (hidden_grad * other_factor[...]).astype(bf16)
    gate_grad[...] = low
    up_grad[...] = other
    rows_grad[...] = (dot_t(low, ready(1)) + dot_t(other, ready(2))).astype(bf16)


def expert_call(kernel, core, arrays, weights, count, outs):
    rows = arrays[0].shape[0]

    def whole(columns):
        return pl.BlockSpec((rows, columns), lambda i, core: (0, 0))

    return pl.pallas_call(
        kernel,
        out_shape=[jax.ShapeDtypeStruct((rows, columns), dtype) for columns, dtype in outs],
        grid_spec=pltpu.PrefetchScalarGridSpec(
            num_scalar_prefetch=1,
            grid=(1,),
            in_specs=[whole(a.shape[1]) for a in arrays]
            + [pl.BlockSpec(memory_space=pltpu.HBM)] * len(weights),
            out_specs=[whole(columns) for columns, _ in outs],
            scratch_shapes=[
                pltpu.VMEM((count,) + weights[0].shape[2:], bf16),
                pltpu.SemaphoreType.DMA((count,)),
            ],
        ),
        compiler_params=pltpu.CompilerParams(vmem_limit_bytes=ROOM),
        cost_estimate=COST,
    )(core, *arrays, *weights)


def weights_kernel(sent, out_grad, hidden, gate_grad, up_grad, sums):
    rows = sent[...]
    sums[0] = t_dot(rows, gate_grad[...]).astype(bf16)
    sums[1] = t_dot(rows, up_grad[...]).astype(bf16)
    sums[2] = t_dot(out_grad[...], hidden[...]).astype(bf16)


def expert_weights_grad(sent, out_grad, hidden, gate_grad, up_grad, block=256):
    count, width = out_grad.shape
    columns = hidden.shape[1]
    part = pl.BlockSpec((count, block), lambda i: (0, i))
    whole = pl.BlockSpec((count, columns), lambda i: (0, 0), pipeline_mode=pl.Buffered(1))
    return pl.pallas_call(
        weights_kernel,
        out_shape=jax.ShapeDtypeStruct((3, width, columns), bf16),
        grid=(width // block,),
        in_specs=[part, part, whole, whole, whole],
        out_specs=pl.BlockSpec((3, block, columns), lambda i: (0, i, 0)),
        compiler_params=pltpu.CompilerParams(vmem_limit_bytes=ROOM),
        cost_estimate=COST,
    )(sent, out_grad, hidden, gate_grad, up_grad)


def combine_kernel(
    midway, parts, returned, cot, hits, places_of, gates, small, moe_low, output, moe_part, router_grad
):
    rows = returned[...]
    output[...] = (
        midway[...] + (dot(parts[0], rows) + (dot(parts[1], rows) + dot(parts[2], rows)))
    ).astype(bf16)
    agreement = dot_t(cot[...], rows)
    lane = lax.broadcasted_iota(jnp.int32, gates.shape, 1)
    gate, grad = [], []
    mean = jnp.zeros((gates.shape[0], 1), f32)
    for k in range(TOPK):
        gate.append(jnp.sum(jnp.where(lane == k, gates[...], 0.0), axis=-1, keepdims=True))
        grad.append(jnp.sum(places_of[k].astype(f32) * agreement, axis=-1, keepdims=True))
        mean = mean + gate[k] * grad[k]
    logit_grad = jnp.zeros(gates.shape, f32)
    for k in range(TOPK):
        logit_grad = logit_grad + hits[k].astype(f32) * (gate[k] * (grad[k] - mean))
    logit_grad = logit_grad.astype(bf16)
    moe_part[...] = dot_t(logit_grad, small[...])
    router_grad[...] = t_dot(moe_low[...], logit_grad)


def home_kernel(placer_t, home, moe_part, midway, cot, gains, midway_grad, branch_low, gain_grad):
    grad = dot(placer_t[...], home[...]) + moe_part[...]
    normal, inverse = normal_of(midway[...])
    result = cot[...].astype(f32) + norm_back(grad, normal, inverse, gains[1:2])
    midway_grad[...] = result
    branch_low[...] = result.astype(bf16)
    gain_grad[...] = jnp.broadcast_to(
        jnp.sum(grad * normal, axis=0, keepdims=True), gain_grad.shape
    )


def out_grad_kernel(mixed, own, other, branch, *blocks):
    quarter = own.shape[0] // 2
    branch[:quarter] = own[:quarter]
    branch[quarter : 2 * quarter] = other[:quarter]
    branch[2 * quarter : 3 * quarter] = own[quarter:]
    branch[3 * quarter :] = other[quarter:]
    count, columns = blocks[0].shape[1:]
    for k in range(2):
        grad = t_dot(mixed[...], branch[:, column_block(k, columns)]).astype(bf16)
        for s in range(4):
            blocks[s][k] = grad[column_block(s, count)]


def attend_back_kernel(
    branch,
    w_out,
    order,
    queries,
    kv_low,
    kv_up,
    logs,
    q_place,
    low_place,
    up_place,
    cosines,
    sines,
    normed,
    dq,
    dkv,
    block0,
    block1,
    block2,
    block3,
    grads,
    acc_low,
    acc_up,
    *,
    scale,
    pieces,
    heads,
):
    half = queries.shape[0] // 2
    columns = w_out.shape[2]
    ordered = dot_t(branch[:, :columns], w_out[0]) + dot_t(branch[:, columns:], w_out[1])
    grads[...] = dot_t(ordered.astype(bf16), order[...]).astype(bf16)
    allowed_low = low_place[...] <= q_place[...]
    allowed_up = up_place[...] <= q_place[half:, :]
    key_low, value_low = kv_low[:, :HD], kv_low[:, HD:]
    key_up, value_up = kv_up[:, :HD], kv_up[:, HD:]
    for h in range(heads):
        at = slice(h * HD, (h + 1) * HD)
        q, grad, log = queries[:, at], grads[:, at], logs[h]
        low = jnp.where(allowed_low, dot_t(q, key_low) * scale, NEGATIVE)
        up = jnp.where(allowed_up, dot_t(q[half:], key_up) * scale, NEGATIVE)
        probs_low, probs_up = jnp.exp(low - log), jnp.exp(up - log[half:])
        grad_low, grad_up = dot_t(grad, value_low), dot_t(grad[half:], value_up)
        along = jnp.sum(probs_low * grad_low, axis=-1, keepdims=True)
        along_up = along[half:] + jnp.sum(probs_up * grad_up, axis=-1, keepdims=True)
        along = jnp.concatenate([along[:half], along_up])
        score_low = (probs_low * (grad_low - along)).astype(bf16)
        score_up = (probs_up * (grad_up - along_up)).astype(bf16)
        part = dot(score_low, key_low)
        part = jnp.concatenate([part[:half], part[half:] + dot(score_up, key_up)]) * scale
        dq[:, at] = turn(part, cosines[...], -sines[...]).astype(bf16)
        terms = (
            (acc_low, slice(0, HD), t_dot(q, score_low)),
            (acc_up, slice(0, HD), t_dot(q[half:], score_up)),
            (acc_low, slice(HD, 2 * HD), t_dot(grad, probs_low.astype(bf16))),
            (acc_up, slice(HD, 2 * HD), t_dot(grad[half:], probs_up.astype(bf16))),
        )
        for acc, rows, term in terms:
            if h == 0:
                acc[rows] = term
            else:
                acc[rows] += term
    for s, block in enumerate((block0, block1, block2, block3)):
        block[...] = t_dot(normed[:, column_block(s, block.shape[0])], dq[...]).astype(bf16)
    for acc, first in ((acc_low, 0), (acc_up, half)):
        dk = (acc[:HD].T * scale).astype(bf16)
        dv = acc[HD:].T.astype(bf16)
        for i in range(pieces):
            dkv[i, first : first + half, :HD] = dk[i * half : (i + 1) * half]
            dkv[i, first : first + half, HD:] = dv[i * half : (i + 1) * half]


def sum_kernel(dq, cosines, sines, *refs):
    w_q, kvs, (parts, dkv, own, other) = refs[:4], refs[4:8], refs[8:]
    total = jnp.sum(parts[...].astype(f32), axis=0)
    dkv[:, :HD] = turn(total[:, :HD], cosines[...], -sines[...]).astype(bf16)
    dkv[:, HD:] = total[:, HD:].astype(bf16)
    quarter = own.shape[0] // 2
    for s in range(4):
        grad = dot_t(dq[...], w_q[s][...]) + dot_t(dkv[...], kvs[s][:, :WIDE])
        at = column_block(s, w_q[s].shape[0])
        own[:quarter, at] = grad[:quarter]
        other[:quarter, at] = grad[quarter : 2 * quarter]
        own[quarter:, at] = grad[2 * quarter : 3 * quarter]
        other[quarter:, at] = grad[3 * quarter :]


def stack_kernel(gate, up, down, late, gate_up, other):
    del late
    gate_up[0] = gate[...]
    gate_up[1] = up[...]
    other[0] = down[...]


def small_grad_kernel(order, router_grad, gain_grad, late, out):
    del late
    row = lax.broadcasted_iota(jnp.int32, gain_grad.shape, 0)
    second = jnp.where(row == 1, gain_grad[...], 0.0).astype(bf16)
    small = router_grad[...] + t_dot(second, gain_picker())
    out[...] = t_dot(order[...], small.astype(bf16))


def input_kernel(both, own, received, midway_grad, gains, order, small, normed, dkv, out, *blocks):
    grad = own[...] + received[...]
    quarter = own.shape[0] // 2
    tokens = jnp.concatenate([both[:quarter], both[2 * quarter : 3 * quarter]])
    normal, inverse = normal_of(tokens.astype(f32))
    parts = in_three(norm_back(grad, normal, inverse, gains[0:1]))
    moved = dot_t(jnp.concatenate(parts), order[...])
    count = 2 * quarter
    out[...] = midway_grad[...] + (
        moved[:count] + (moved[count : 2 * count] + moved[2 * count :])
    )
    gain_grad = jnp.sum(grad * normal, axis=0, keepdims=True)
    row = lax.broadcasted_iota(jnp.int32, gains.shape, 0)
    gain_grad = jnp.where(row == 0, gain_grad, 0.0).astype(bf16)
    small = small[...] + t_dot(gain_grad, gain_picker())
    rows = blocks[0].shape[0]
    for s, block in enumerate(blocks):
        at = column_block(s, rows)
        block[:, :WIDE] = t_dot(normed[:, at], dkv[...]).astype(bf16)
        block[:, WIDE:] = small[at].astype(bf16)


def body(
    tokens,
    cotangent,
    pair_of,
    routes,
    attn_gain,
    moe_gain,
    w_query,
    w_key,
    w_value,
    w_out,
    w_router,
    w_gate,
    w_up,
    w_down,
):
    rows = tokens.shape[1]
    half = rows // 2
    width = tokens.shape[2]
    shard = w_query.shape[1]
    ctx_count = 16
    experts = w_router.shape[2]
    columns = w_gate.shape[3]
    per_group = H // KVH
    qw = per_group * HD
    scale = 1.0 / math.sqrt(HD)
    core = lax.axis_index("core")
    ylo, z, yhi = lax.axis_index("ylo"), lax.axis_index("z"), lax.axis_index("yhi")
    x = lax.axis_index("x")
    piece_rows = 2 * shard
    slots = experts * SLOTS
    own_tokens, cot = tokens[0], cotangent[0]

    def halves(matrix):
        return [matrix[:, : matrix.shape[1] // 2], matrix[:, matrix.shape[1] // 2 :]]

    small = jnp.concatenate([w_router[0], attn_gain[0][:, None], moe_gain[0][:, None]], axis=-1)
    small = jnp.pad(small, ((0, 0), (0, 128 - experts - 2)))
    query_halves, key_halves, value_halves = halves(w_query[0]), halves(w_key[0]), halves(w_value[0])
    pairs = [
        jnp.concatenate([k, v, small, q], axis=-1)
        for k, v, q in zip(key_halves, value_halves, query_halves)
    ]
    pieces = gather_pieces(pairs, yhi, core, ("core", "yhi"), SAME, OTHER)
    out_pieces = gather_pieces(
        halves(w_out[0]), yhi, yhi, ("ylo", "core", "yhi"), OUT_SAME, OUT_OTHER
    )
    other_tokens = partner(own_tokens)
    pieces, out_pieces, x, z, own_tokens, other_tokens, pair_of = together(
        pieces, out_pieces, x, z, own_tokens, other_tokens, pair_of
    )

    plane_rows = 16 * piece_rows
    plane = spread(pieces, 16, PLANE)
    both = jnp.concatenate(
        [own_tokens[:half], other_tokens[:half], own_tokens[half:], other_tokens[half:]]
    )
    order, out_order, level_order = order_matrix(16, x), order_matrix(8, x), level_order_matrix(z)
    plane, both, out_pieces, order, out_order, level_order, pair_of = together(
        plane, both, out_pieces, order, out_order, level_order, pair_of
    )

    plane = plane.reshape(plane_rows, -1)
    w_kvs = along("x", plane[:, : 3 * HD])
    wo = spread(out_pieces, 16, LEVEL)
    (both,) = call(order_kernel, [((2 * rows, width), bf16)], both, order)

    def two_cores(ctx):
        return jnp.stack([ctx + core, ctx + 1 - core], axis=-1).reshape(-1)

    ctx_here = (ylo * 4 + z) * 2
    q_place = places(pair_of, two_cores(ctx_here), rows, ctx_count)
    q_place = q_place.transpose(1, 0, 2).reshape(2 * rows, 1)
    key_place = places(
        pair_of, two_cores(jnp.arange(8, dtype=jnp.int32) * 2), rows, ctx_count
    )
    low_place, up_place = key_place[:, 0].reshape(1, -1), key_place[:, 1].reshape(1, -1)
    frequency = jnp.exp(jnp.arange(HD // 2, dtype=f32) * (-2.0 * math.log(ROPE_BASE) / HD))
    angles = q_place.astype(f32) * frequency[None, :]
    cosines, sines = jnp.cos(angles), jnp.sin(angles)
    cosines = jnp.concatenate([cosines, cosines], axis=-1)
    sines = jnp.concatenate([-sines, sines], axis=-1)
    w_q = along("x", plane[:, 3 * HD :])
    w_q[1], w_q[3], w_kvs, wo, both, q_place, low_place, up_place, cosines, sines, chosen = together(
        w_q[1], w_q[3], w_kvs, wo, both, q_place, low_place, up_place, cosines, sines, routes[0, 0]
    )

    wo = along("z", wo.reshape(2, qw // 4, width // 2))
    normed, key_value, gains = call(
        keys_kernel,
        [((2 * rows, width), bf16), ((2 * rows, 2 * HD), bf16), ((8, width), f32)],
        both,
        cosines,
        sines,
        *w_kvs,
    )
    all_kv = spread(key_value, 8, RING)
    small, moe_gains = call(
        small_kernel, [((width, 128), bf16), ((8, width), f32)], order, *w_kvs
    )
    lanes = jnp.arange(128, dtype=jnp.int32)
    hits = (chosen.T[:, :, None] == lanes[None, None, :]).astype(bf16)
    earlier = (lanes[:, None] > lanes[None, :]).astype(bf16)
    before = dot(earlier, jnp.sum(hits, axis=0))
    slot_index = jnp.sum(hits.astype(f32) * before[None], axis=-1).astype(jnp.int32)
    target = chosen.T * SLOTS + slot_index
    slot_row = jnp.arange(slots, dtype=jnp.int32)
    places_of = (target[:, :, None] == slot_row[None, None, :]).astype(bf16)
    placer_t = jnp.sum(places_of, axis=0)
    placer = placer_t.T
    (cot_rows,) = call(order_kernel, [((slots, width), bf16)], placer, cot)
    (queries,) = call(
        query_kernel, [((2 * rows, qw), bf16)], normed, cosines, sines, *w_q, cost=LONG
    )
    gate_up, down = call(
        stack_kernel,
        [((2,) + w_gate.shape[1:], bf16), (w_down.shape, bf16)],
        w_gate[0],
        w_up[0],
        w_down[0],
        gains,
    )
    (
        queries, all_kv, small, moe_gains, hits, places_of, placer_t, placer, cot_rows,
        gate_up, down, wo,
    ) = together(
        queries, all_kv, small, moe_gains, hits, places_of, placer_t, placer, cot_rows,
        gate_up, down, wo,
    )
    gate_up = lax.all_gather(gate_up, CTX, axis=2, tiled=True)
    down = lax.all_gather(down, CTX, axis=2, tiled=True)

    arrived_cot = to_owners(cot_rows.reshape(experts, SLOTS, width))
    sizes = dict(scale=scale, pieces=8, heads=per_group)
    keys = 8 * rows
    mixed, mixed_back, logs, kv_low, kv_up = call(
        functools.partial(attend_kernel, **sizes),
        [
            ((2 * rows, qw), bf16),
            ((2 * rows, qw), bf16),
            ((per_group, 2 * rows, 1), f32),
            ((keys, 2 * HD), bf16),
            ((keys, 2 * HD), bf16),
        ],
        queries,
        q_place,
        low_place,
        up_place,
        level_order,
        out_order,
        all_kv,
        scratch=[pltpu.VMEM((2 * rows, qw), bf16)],
    )

    branch_own, branch_other, wo = call(
        branch_kernel,
        [((rows, width), f32), ((rows, width), f32), ((2, qw, width // 2), bf16)],
        mixed,
        *wo,
    )
    sent, midway, moe_low, gates, gate_parts = call(
        route_kernel,
        [
            ((slots, width + 128), bf16),
            ((rows, width), f32),
            ((rows, width), bf16),
            ((rows, 128), f32),
            ((3, rows, slots), bf16),
        ],
        own_tokens,
        branch_own,
        partner(branch_other),
        small,
        moe_gains,
        hits,
        places_of,
        placer,
    )
    sent, arrived_cot = together(sent, arrived_cot)

    sent = to_owners(sent.reshape(experts, SLOTS, width + 128)).reshape(slots, width + 128)
    mine = core.reshape(1)
    hidden, out_grad, factor, other_factor = expert_call(
        hidden_kernel,
        mine,
        [sent, arrived_cot.reshape(slots, width)],
        [gate_up],
        2,
        [(columns, bf16), (width, bf16), (columns, f32), (columns, f32)],
    )
    (expert_out,) = expert_call(output_kernel, mine, [hidden], [down], 1, [(width, bf16)])
    expert_out, factor = together(expert_out, factor)

    returned = to_owners(expert_out.reshape(experts, SLOTS, width))
    rows_grad, gate_grad, up_grad = expert_call(
        backward_kernel,
        mine,
        [out_grad, factor, other_factor],
        [down, gate_up],
        3,
        [(width, bf16), (columns, bf16), (columns, bf16)],
    )
    returned, rows_grad, gate_grad, up_grad = together(returned, rows_grad, gate_grad, up_grad)

    home_grad = to_owners(rows_grad.reshape(experts, SLOTS, width))
    expert_sums = expert_weights_grad(sent, out_grad, hidden, gate_grad, up_grad)
    output, moe_part, router_grad = call(
        combine_kernel,
        [((rows, width), bf16), ((rows, width), f32), ((width, 128), f32)],
        midway,
        gate_parts,
        returned.reshape(slots, width),
        cot,
        hits,
        places_of,
        gates,
        small,
        moe_low,
    )
    home_grad, moe_part, expert_sums = together(home_grad, moe_part, expert_sums)
    expert_sums = lax.psum_scatter(expert_sums, RING, scatter_dimension=1, tiled=True)
    midway_grad, branch_low, gain_two_grad = call(
        home_kernel,
        [((rows, width), f32), ((rows, width), bf16), ((8, width), f32)],
        placer_t,
        home_grad.reshape(slots, width),
        moe_part,
        midway,
        cot,
        moe_gains,
    )
    branch, *out_w_grad = call(
        out_grad_kernel,
        [((2 * rows, width), bf16)] + [((2, qw // 4, width // 2), bf16)] * 4,
        mixed_back,
        branch_low,
        partner(branch_low),
    )
    branch, out_w_grad = together(branch, out_w_grad)
    out_w_grad = added(back_along_x(out_w_grad))

    dq, dkv, *q_w_grad = call(
        functools.partial(attend_back_kernel, **sizes),
        [((2 * rows, qw), bf16), ((8, 2 * rows, 2 * HD), bf16)]
        + [((plane_rows, qw), bf16)] * 4,
        branch,
        wo,
        level_order,
        queries,
        kv_low,
        kv_up,
        logs,
        q_place,
        low_place,
        up_place,
        cosines,
        sines,
        normed,
        scratch=[
            pltpu.VMEM((2 * rows, qw), bf16),
            pltpu.VMEM((2 * HD, keys), f32),
            pltpu.VMEM((2 * HD, keys), f32),
        ],
    )
    dkv = exchange(dkv, RING)
    q_w_grad = back_along_x(q_w_grad)
    (small_grad,) = call(
        small_grad_kernel, [((width, 128), f32)], order, router_grad, gain_two_grad, dq
    )
    dkv, out_w_grad, small_grad, q_w_grad[1], q_w_grad[3] = together(
        dkv, out_w_grad, small_grad, q_w_grad[1], q_w_grad[3]
    )

    dkv, normed_own, normed_other = call(
        sum_kernel,
        [((2 * rows, 2 * HD), bf16), ((rows, width), f32), ((rows, width), f32)],
        dq,
        cosines,
        sines,
        *w_q,
        *w_kvs,
        dkv,
    )
    input_grad, *kvs_grad = call(
        input_kernel,
        [((rows, width), f32)] + [((plane_rows, 3 * HD), bf16)] * 4,
        both,
        normed_own,
        partner(normed_other),
        midway_grad,
        gains,
        order,
        small_grad,
        normed,
        dkv,
    )
    kvs_grad, out_w_grad, input_grad = together(kvs_grad, out_w_grad, input_grad)

    out_w_grad = exchange(out_w_grad.reshape(16, piece_rows, width // 2), OUT_PLANE)
    kvs_grad = back_along_x(kvs_grad)
    (plane_grad,) = call(
        add_both_kernel, [((plane_rows, qw + 3 * HD), bf16)], *q_w_grad, *kvs_grad, cost=LONG
    )
    plane_grad, out_w_grad = together(plane_grad, out_w_grad)
    plane_grad = exchange(plane_grad.reshape(16, piece_rows, qw + 3 * HD), PLANE)

    def summed(pieces):
        return jnp.sum(pieces.astype(f32), axis=0)

    def expert_shards(grad):
        count = grad.shape[1] // 2
        kept = lax.dynamic_slice_in_dim(grad, core * count, count, axis=1)
        given = partner(lax.dynamic_slice_in_dim(grad, (1 - core) * count, count, axis=1))
        both = jnp.stack([pick(core, kept, given), pick(core, given, kept)], axis=1)
        return [both[i : i + 1].astype(f32) for i in range(3)]

    out_w_grad = scatter_pieces(
        summed(out_w_grad), yhi, yhi, ("ylo", "core", "yhi"), OUT_SAME, OUT_OTHER
    )
    w_gate_grad, w_up_grad, w_down_grad = expert_shards(expert_sums)
    plane_grad, out_w_grad, w_gate_grad, w_up_grad, w_down_grad = together(
        plane_grad, out_w_grad, w_gate_grad, w_up_grad, w_down_grad
    )
    plane_grad = scatter_pieces(summed(plane_grad), yhi, core, ("core", "yhi"), SAME, OTHER)
    plane_grad = plane_grad.reshape(shard, 2, -1)

    def joined(first, last):
        return plane_grad[:, :, first:last].reshape(1, shard, -1)

    small_grad = jnp.sum(plane_grad[None, :, :, qw + 2 * HD :], axis=2)

    return (
        output[None],
        input_grad[None],
        small_grad[:, :, experts],
        small_grad[:, :, experts + 1],
        joined(0, qw),
        joined(qw, qw + HD),
        joined(qw + HD, qw + 2 * HD),
        out_w_grad[None],
        small_grad[:, :, :experts],
        w_gate_grad,
        w_up_grad,
        w_down_grad,
    )


def solution(mesh):
    fine = Mesh(mesh.devices.reshape(2, 4, 2, 4, 2), AXES)
    seq = P(FSDP, CTX, None)
    vector = P(None, AXES)
    matrix = P(None, AXES, None)
    expert = P(None, FSDP, CTX, None)
    in_specs = (
        seq,
        seq,
        P(),
        P(None, FSDP, CTX, None),
        vector,
        vector,
        matrix,
        matrix,
        matrix,
        matrix,
        matrix,
        expert,
        expert,
        expert,
    )
    out_specs = (
        seq,
        seq,
        vector,
        vector,
        matrix,
        matrix,
        matrix,
        matrix,
        matrix,
        expert,
        expert,
        expert,
    )
    return jax.shard_map(body, mesh=fine, in_specs=in_specs, out_specs=out_specs, check_vma=False)
```

```python
import functools
import math

import jax
import jax.numpy as jnp
from jax import lax
from jax.experimental import pallas as pl
from jax.experimental.pallas import tpu as pltpu
from jax.sharding import Mesh
from jax.sharding import PartitionSpec as P

H = 12
KVH = 2
HD = 128
TOPK = 4

EPSILON = 1e-06
ROPE_BASE = 1000000.0
NEGATIVE = -1e30

AXES = ("ylo", "z", "core", "x", "yhi")
CTX = ("ylo", "z", "core")
FSDP = ("x", "yhi")
GROUPS = [
    [
        (((group ^ yhi) * 4 + z) * 2 + core) * 8 + x * 2 + yhi
        for x in range(4)
        for yhi in range(2)
        for core in range(2)
    ]
    for group in range(2)
    for z in range(4)
]
RING = ("ylo", "z")
PLANE = ("ylo", "z", "yhi")
OUT_PLANE = ("yhi", "z", "ylo")
LEVEL = ("yhi", "ylo", "x")
GROUPS = [
    [
        (((group ^ yhi) * 4 + z) * 2 + core) * 8 + x * 2 + yhi
        for x in range(4)
        for yhi in range(2)
        for core in range(2)
    ]
    for group in range(2)
    for z in range(4)
]
RING = ("ylo", "z")
ROWS_ORDER = ("ylo", "z", "yhi", "x")
OUT_ORDER = ("yhi", "z", "ylo", "x")
SLOTS = 40

bf16 = jnp.bfloat16
f32 = jnp.float32


def dot(left, right):
    return jnp.dot(left, right, preferred_element_type=f32)


def dot_t(left, right):
    return lax.dot_general(left, right, (((1,), (1,)), ((), ())), preferred_element_type=f32)


def t_dot(left, right):
    return lax.dot_general(left, right, (((0,), (0,)), ((), ())), preferred_element_type=f32)


def exchange(pieces, axes):
    return lax.all_to_all(pieces, axes, split_axis=0, concat_axis=0, tiled=True)


def to_owners(pieces):
    return lax.all_to_all(
        pieces, AXES, split_axis=0, concat_axis=0, axis_index_groups=GROUPS, tiled=True
    )


def spread(piece, count, axes):
    return exchange(jnp.broadcast_to(piece[None], (count,) + piece.shape), axes)


def after(value, earlier):
    return lax.optimization_barrier((value, earlier))[0]


def together(*values):
    return lax.optimization_barrier(values)


def partner(value):
    return lax.ppermute(value, "core", [(0, 1), (1, 0)])


def route(axes, sizes, move):
    pairs = []
    for source in range(math.prod(sizes)):
        rest, at = source, []
        for size in reversed(sizes):
            at.insert(0, rest % size)
            rest //= size
        target = 0
        for size, value in zip(sizes, move(*at)):
            target = target * size + value
        pairs.append((source, target))
    return pairs


SAME = route(("core", "yhi"), (2, 2), lambda c, h: (h, c))
OTHER = route(("core", "yhi"), (2, 2), lambda c, h: (1 - h, c))
OUT_SAME = route(("ylo", "core", "yhi"), (2, 2, 2), lambda j, c, h: (c, j, h))
OUT_OTHER = route(("ylo", "core", "yhi"), (2, 2, 2), lambda j, c, h: (c, j, 1 - h))


def back(pairs):
    return [(target, source) for source, target in pairs]


def pick(flag, if_zero, if_one):
    return jnp.where(flag == 0, if_zero, if_one)


def gather_pieces(pair, flag, key, axes, same, other):
    first = lax.ppermute(pick(flag, pair[0], pair[1]), axes, same)
    second = lax.ppermute(pick(flag, pair[1], pair[0]), axes, other)
    return pick(
        key, jnp.concatenate([first, second]), jnp.concatenate([second, first])
    )


def scatter_pieces(piece, flag, key, axes, same, other):
    count = piece.shape[0] // 2
    mine, rest = piece[:count], piece[count:]
    first = lax.ppermute(pick(key, mine, rest), axes, back(same))
    second = lax.ppermute(pick(key, rest, mine), axes, back(other))
    return pick(flag, jnp.concatenate([first, second], axis=-1), jnp.concatenate([second, first], axis=-1))


def along(axis, piece):
    return [piece] + [
        lax.ppermute(piece, axis, [(i, (i + s) % 4) for i in range(4)]) for s in (1, 2, 3)
    ]


def back_along_x(blocks):
    return [blocks[0]] + [
        lax.ppermute(blocks[s], "x", [(i, (i - s) % 4) for i in range(4)]) for s in (1, 2, 3)
    ]


def added(blocks):
    (total,) = call(add_kernel, [(blocks[0].shape, bf16)], *blocks, cost=LONG)
    return total


def sum_of(first, second, third, fourth):
    return (
        (first[...].astype(f32) + second[...].astype(f32))
        + (third[...].astype(f32) + fourth[...].astype(f32))
    ).astype(bf16)


def add_kernel(first, second, third, fourth, total):
    total[...] = sum_of(first, second, third, fourth)


def add_both_kernel(*refs):
    total = refs[8]
    count = refs[0].shape[1]
    total[:, :count] = sum_of(*refs[:4])
    total[:, count:] = sum_of(*refs[4:8])


def order_matrix(groups, x):
    index = jnp.arange(groups * 96, dtype=jnp.int32)
    turn_of, group, row = index // (groups * 24), index // 24 % groups, index % 24
    own = group * 96 + (x - turn_of) % 4 * 24 + row
    return (index[:, None] == own[None, :]).astype(bf16)


def level_order_matrix(z):
    index = jnp.arange(8 * 96, dtype=jnp.int32)
    own = (z - index // 192) % 4 * 192 + index % 192
    return (index[:, None] == own[None, :]).astype(bf16)


def places(pair_of, ctx, row_count, ctx_count):
    half_size = row_count // 2
    pair = jnp.sum(
        jnp.where(ctx[:, None] == jnp.arange(ctx_count, dtype=jnp.int32)[None], pair_of[None], 0),
        axis=1,
    )
    block = jnp.stack([pair, 2 * ctx_count - 1 - pair], axis=1)
    return block[:, :, None] * half_size + jnp.arange(half_size, dtype=jnp.int32)[None, None]


def in_three(value):
    high = value.astype(bf16)
    rest = value - high.astype(f32)
    middle = rest.astype(bf16)
    return [high, middle, (rest - middle.astype(f32)).astype(bf16)]


def call(kernel, outs, *args, scratch=(), cost=None):
    def whole(shape):
        return pl.BlockSpec(shape, lambda i: (0,) * len(shape))

    return pl.pallas_call(
        kernel,
        out_shape=[jax.ShapeDtypeStruct(shape, dtype) for shape, dtype in outs],
        grid=(1,),
        in_specs=[whole(a.shape) for a in args],
        out_specs=[whole(shape) for shape, _ in outs],
        scratch_shapes=list(scratch),
        compiler_params=pltpu.CompilerParams(vmem_limit_bytes=ROOM),
        cost_estimate=COST if cost is None else cost,
    )(*args)


ROOM = 58 << 20
COST = pl.CostEstimate(flops=1 << 20, bytes_accessed=1 << 18, transcendentals=0)
LONG = pl.CostEstimate(flops=1 << 35, bytes_accessed=1 << 27, transcendentals=0)
WIDE = 2 * HD
EXPERTS = 16


def turn(vectors, cosines, sines):
    return vectors * cosines + pltpu.roll(vectors, HD // 2, axis=1) * sines


def gain_picker():
    row = lax.broadcasted_iota(jnp.int32, (8, 128), 0)
    column = lax.broadcasted_iota(jnp.int32, (8, 128), 1)
    return jnp.where((column == row + EXPERTS) & (row < 2), 1.0, 0.0).astype(bf16)


def normal_of(stream):
    inverse = lax.rsqrt(jnp.mean(stream * stream, axis=-1, keepdims=True) + EPSILON)
    return stream * inverse, inverse


def norm_back(grad, normal, inverse, gain):
    scaled = grad * gain
    return inverse * (scaled - normal * jnp.mean(scaled * normal, axis=-1, keepdims=True))


def column_block(s, count):
    return slice(s * count, (s + 1) * count)


def order_kernel(rows, order, out):
    out[...] = dot(rows[...], order[...]).astype(bf16)


def keys_kernel(both, cosines, sines, *refs):
    kvs, (normed, key_value, gains) = refs[:4], refs[4:]
    count = kvs[0].shape[0]
    for s in range(4):
        gains[:, column_block(s, count)] = dot_t(gain_picker(), kvs[s][:, WIDE:])
    normal, _ = normal_of(both[...].astype(f32))
    normed[...] = (normal * gains[0:1]).astype(bf16)
    kv = dot(normed[:, column_block(0, count)], kvs[0][:, :WIDE])
    for s in range(1, 4):
        kv = kv + dot(normed[:, column_block(s, count)], kvs[s][:, :WIDE])
    keys = turn(kv[:, :HD], cosines[...], sines[...]).astype(bf16)
    values = kv[:, HD:].astype(bf16)
    for i in range(key_value.shape[0]):
        key_value[i, :, :HD] = keys
        key_value[i, :, HD:] = values


def small_kernel(order, kvs0, kvs1, kvs2, kvs3, small, gains):
    count = kvs0.shape[0]
    total = jnp.zeros(small.shape, f32)
    for s, kvs in enumerate((kvs0, kvs1, kvs2, kvs3)):
        total = total + dot(order[:, column_block(s, count)], kvs[:, WIDE:])
    small[...] = total.astype(bf16)
    gains[...] = dot_t(gain_picker(), small[...])


def query_kernel(normed, cosines, sines, w_q0, w_q1, w_q2, w_q3, queries):
    w_q = (w_q0, w_q1, w_q2, w_q3)
    count = w_q0.shape[0]
    for h in range(queries.shape[1] // HD):
        at = column_block(h, HD)
        q = dot(normed[:, column_block(0, count)], w_q0[:, at])
        for s in range(1, 4):
            q = q + dot(normed[:, column_block(s, count)], w_q[s][:, at])
        queries[:, at] = turn(q, cosines[...], sines[...]).astype(bf16)


def attend_kernel(
    queries,
    q_place,
    low_place,
    up_place,
    order,
    order_back,
    kv,
    ordered,
    ordered_back,
    logs,
    kv_low,
    kv_up,
    mixed,
    *,
    scale,
    pieces,
    heads,
):
    half = kv.shape[1] // 2
    for i in range(pieces):
        kv_low[i * half : (i + 1) * half, :] = kv[i, :half]
        kv_up[i * half : (i + 1) * half, :] = kv[i, half:]
    allowed_low = low_place[...] <= q_place[...]
    allowed_up = up_place[...] <= q_place[half:, :]
    for h in range(heads):
        at = slice(h * HD, (h + 1) * HD)
        q = queries[:, at]
        low = jnp.where(allowed_low, dot_t(q, kv_low[:, :HD]) * scale, NEGATIVE)
        up = jnp.where(allowed_up, dot_t(q[half:], kv_up[:, :HD]) * scale, NEGATIVE)
        first, second = low[:half], low[half:]
        top = jnp.max(first, axis=-1, keepdims=True)
        weight = jnp.exp(first - top)
        total = jnp.sum(weight, axis=-1, keepdims=True)
        probs = (weight / total).astype(bf16)
        mixed[:half, at] = dot(probs, kv_low[:, HD:]).astype(bf16)
        logs[h, :half, :] = top + jnp.log(total)
        top = jnp.maximum(
            jnp.max(second, axis=-1, keepdims=True), jnp.max(up, axis=-1, keepdims=True)
        )
        weight, weight_up = jnp.exp(second - top), jnp.exp(up - top)
        total = jnp.sum(weight, axis=-1, keepdims=True) + jnp.sum(
            weight_up, axis=-1, keepdims=True
        )
        mixed[half:, at] = (
            dot((weight / total).astype(bf16), kv_low[:, HD:])
            + dot((weight_up / total).astype(bf16), kv_up[:, HD:])
        ).astype(bf16)
        logs[h, half:, :] = top + jnp.log(total)
    ordered[...] = dot(mixed[...], order[...]).astype(bf16)
    ordered_back[...] = dot(mixed[...], order_back[...]).astype(bf16)


def branch_kernel(mixed, w_out0, w_out1, w_out2, w_out3, own, other, w_out):
    quarter = mixed.shape[0] // 4
    count, columns = w_out0.shape[1:]
    for s, part in enumerate((w_out0, w_out1, w_out2, w_out3)):
        w_out[:, column_block(s, count)] = part[...]
    for k in range(2):
        part = dot(mixed[...], w_out[k])
        at = slice(k * columns, (k + 1) * columns)
        own[:quarter, at] = part[:quarter]
        other[:quarter, at] = part[quarter : 2 * quarter]
        own[quarter:, at] = part[2 * quarter : 3 * quarter]
        other[quarter:, at] = part[3 * quarter :]


def route_kernel(
    tokens,
    own,
    received,
    small,
    gains,
    hits,
    places_of,
    placer,
    sent,
    midway,
    moe_low,
    gates,
    parts,
):
    middle = tokens[...].astype(f32) + (own[...] + received[...])
    midway[...] = middle
    normal, _ = normal_of(middle)
    moe = (normal * gains[1:2]).astype(bf16)
    moe_low[...] = moe
    sent[:, : moe.shape[1]] = dot(placer[...], moe).astype(bf16)
    logits = dot(moe, small[...])
    picked = [
        jnp.sum(hits[k].astype(f32) * logits, axis=-1, keepdims=True) for k in range(TOPK)
    ]
    top = picked[0]
    for value in picked[1:]:
        top = jnp.maximum(top, value)
    weights = [jnp.exp(value - top) for value in picked]
    total = weights[0]
    for value in weights[1:]:
        total = total + value
    lane = lax.broadcasted_iota(jnp.int32, gates.shape, 1)
    gate_at = jnp.zeros(places_of.shape[1:], f32)
    kept = jnp.zeros(gates.shape, f32)
    for k in range(TOPK):
        gate = weights[k] / total
        kept = jnp.where(lane == k, gate, kept)
        gate_at = gate_at + places_of[k].astype(f32) * gate
    gates[...] = kept
    block = jnp.zeros((sent.shape[0], 128), f32)
    for i, part in enumerate(in_three(gate_at)):
        parts[i] = part
        block = block + t_dot(part, jnp.where(lane == i, 1.0, 0.0).astype(bf16))
    sent[:, moe.shape[1] :] = block.astype(bf16)


def fetched(core, weights, held, sems, first):
    copies = [
        pltpu.make_async_copy(weights.at[m, core[0]], held.at[m], sems.at[m]) for m in range(3)
    ]
    for m in first:
        copies[m].start()

    def ready(m):
        copies[m].wait()
        return held[m]

    return ready


def forward_kernel(
    core, sent, cot, weights, out, hidden, out_grad, factor, other_factor, held, sems
):
    ready = fetched(core, weights, held, sems, (0, 1, 2))
    width = out.shape[1]
    gates = jnp.sum(sent[:, width:].astype(f32), axis=-1, keepdims=True)
    out_grad[...] = (gates * cot[...].astype(f32)).astype(bf16)
    rows = sent[:, :width]
    gate_pre = dot(rows, ready(0))
    up_pre = dot(rows, ready(1))
    sigmoid = 1.0 / (1.0 + jnp.exp(-gate_pre))
    silu = gate_pre * sigmoid
    low = (silu * up_pre).astype(bf16)
    hidden[...] = low
    out[...] = dot_t(low, ready(2)).astype(bf16)
    factor[...] = up_pre * sigmoid * (1.0 + gate_pre * (1.0 - sigmoid))
    other_factor[...] = silu


def backward_kernel(
    core, out_grad, factor, other_factor, weights, rows_grad, gate_grad, up_grad, held, sems
):
    ready = fetched(core, weights, held, sems, (2, 0, 1))
    hidden_grad = dot(out_grad[...], ready(2))
    low = (hidden_grad * factor[...]).astype(bf16)
    other = (hidden_grad * other_factor[...]).astype(bf16)
    gate_grad[...] = low
    up_grad[...] = other
    rows_grad[...] = (dot_t(low, ready(0)) + dot_t(other, ready(1))).astype(bf16)


def expert_call(kernel, core, arrays, weights, outs):
    rows = arrays[0].shape[0]

    def whole(columns):
        return pl.BlockSpec((rows, columns), lambda i, core: (0, 0))

    return pl.pallas_call(
        kernel,
        out_shape=[jax.ShapeDtypeStruct((rows, columns), dtype) for columns, dtype in outs],
        grid_spec=pltpu.PrefetchScalarGridSpec(
            num_scalar_prefetch=1,
            grid=(1,),
            in_specs=[whole(a.shape[1]) for a in arrays] + [pl.BlockSpec(memory_space=pltpu.HBM)],
            out_specs=[whole(columns) for columns, _ in outs],
            scratch_shapes=[
                pltpu.VMEM((3,) + weights.shape[2:], bf16),
                pltpu.SemaphoreType.DMA((3,)),
            ],
        ),
        compiler_params=pltpu.CompilerParams(vmem_limit_bytes=ROOM),
        cost_estimate=COST,
    )(core, *arrays, weights)


def weights_kernel(sent, out_grad, hidden, gate_grad, up_grad, sums):
    rows = sent[...]
    sums[0] = t_dot(rows, gate_grad[...]).astype(bf16)
    sums[1] = t_dot(rows, up_grad[...]).astype(bf16)
    sums[2] = t_dot(out_grad[...], hidden[...]).astype(bf16)


def expert_weights_grad(sent, out_grad, hidden, gate_grad, up_grad, block=256):
    count, width = out_grad.shape
    columns = hidden.shape[1]
    part = pl.BlockSpec((count, block), lambda i: (0, i))
    whole = pl.BlockSpec((count, columns), lambda i: (0, 0), pipeline_mode=pl.Buffered(1))
    return pl.pallas_call(
        weights_kernel,
        out_shape=jax.ShapeDtypeStruct((3, width, columns), bf16),
        grid=(width // block,),
        in_specs=[part, part, whole, whole, whole],
        out_specs=pl.BlockSpec((3, block, columns), lambda i: (0, i, 0)),
        compiler_params=pltpu.CompilerParams(vmem_limit_bytes=ROOM),
        cost_estimate=COST,
    )(sent, out_grad, hidden, gate_grad, up_grad)


def combine_kernel(
    midway, parts, returned, cot, hits, places_of, gates, small, moe_low, output, moe_part, router_grad
):
    rows = returned[...]
    output[...] = (
        midway[...] + (dot(parts[0], rows) + (dot(parts[1], rows) + dot(parts[2], rows)))
    ).astype(bf16)
    agreement = dot_t(cot[...], rows)
    lane = lax.broadcasted_iota(jnp.int32, gates.shape, 1)
    gate, grad = [], []
    mean = jnp.zeros((gates.shape[0], 1), f32)
    for k in range(TOPK):
        gate.append(jnp.sum(jnp.where(lane == k, gates[...], 0.0), axis=-1, keepdims=True))
        grad.append(jnp.sum(places_of[k].astype(f32) * agreement, axis=-1, keepdims=True))
        mean = mean + gate[k] * grad[k]
    logit_grad = jnp.zeros(gates.shape, f32)
    for k in range(TOPK):
        logit_grad = logit_grad + hits[k].astype(f32) * (gate[k] * (grad[k] - mean))
    logit_grad = logit_grad.astype(bf16)
    moe_part[...] = dot_t(logit_grad, small[...])
    router_grad[...] = t_dot(moe_low[...], logit_grad)


def home_kernel(placer_t, home, moe_part, midway, cot, gains, midway_grad, branch_low, gain_grad):
    grad = dot(placer_t[...], home[...]) + moe_part[...]
    normal, inverse = normal_of(midway[...])
    result = cot[...].astype(f32) + norm_back(grad, normal, inverse, gains[1:2])
    midway_grad[...] = result
    branch_low[...] = result.astype(bf16)
    gain_grad[...] = jnp.broadcast_to(
        jnp.sum(grad * normal, axis=0, keepdims=True), gain_grad.shape
    )


def out_grad_kernel(mixed, own, other, branch, *blocks):
    quarter = own.shape[0] // 2
    branch[:quarter] = own[:quarter]
    branch[quarter : 2 * quarter] = other[:quarter]
    branch[2 * quarter : 3 * quarter] = own[quarter:]
    branch[3 * quarter :] = other[quarter:]
    count, columns = blocks[0].shape[1:]
    for k in range(2):
        grad = t_dot(mixed[...], branch[:, column_block(k, columns)]).astype(bf16)
        for s in range(4):
            blocks[s][k] = grad[column_block(s, count)]


def attend_back_kernel(
    branch,
    w_out,
    order,
    queries,
    kv_low,
    kv_up,
    logs,
    q_place,
    low_place,
    up_place,
    cosines,
    sines,
    normed,
    dq,
    dkv,
    block0,
    block1,
    block2,
    block3,
    grads,
    acc_low,
    acc_up,
    *,
    scale,
    pieces,
    heads,
):
    half = queries.shape[0] // 2
    columns = w_out.shape[2]
    ordered = dot_t(branch[:, :columns], w_out[0]) + dot_t(branch[:, columns:], w_out[1])
    grads[...] = dot_t(ordered.astype(bf16), order[...]).astype(bf16)
    allowed_low = low_place[...] <= q_place[...]
    allowed_up = up_place[...] <= q_place[half:, :]
    key_low, value_low = kv_low[:, :HD], kv_low[:, HD:]
    key_up, value_up = kv_up[:, :HD], kv_up[:, HD:]
    for h in range(heads):
        at = slice(h * HD, (h + 1) * HD)
        q, grad, log = queries[:, at], grads[:, at], logs[h]
        low = jnp.where(allowed_low, dot_t(q, key_low) * scale, NEGATIVE)
        up = jnp.where(allowed_up, dot_t(q[half:], key_up) * scale, NEGATIVE)
        probs_low, probs_up = jnp.exp(low - log), jnp.exp(up - log[half:])
        grad_low, grad_up = dot_t(grad, value_low), dot_t(grad[half:], value_up)
        along = jnp.sum(probs_low * grad_low, axis=-1, keepdims=True)
        along_up = along[half:] + jnp.sum(probs_up * grad_up, axis=-1, keepdims=True)
        along = jnp.concatenate([along[:half], along_up])
        score_low = (probs_low * (grad_low - along)).astype(bf16)
        score_up = (probs_up * (grad_up - along_up)).astype(bf16)
        part = dot(score_low, key_low)
        part = jnp.concatenate([part[:half], part[half:] + dot(score_up, key_up)]) * scale
        dq[:, at] = turn(part, cosines[...], -sines[...]).astype(bf16)
        terms = (
            (acc_low, slice(0, HD), t_dot(q, score_low)),
            (acc_up, slice(0, HD), t_dot(q[half:], score_up)),
            (acc_low, slice(HD, 2 * HD), t_dot(grad, probs_low.astype(bf16))),
            (acc_up, slice(HD, 2 * HD), t_dot(grad[half:], probs_up.astype(bf16))),
        )
        for acc, rows, term in terms:
            if h == 0:
                acc[rows] = term
            else:
                acc[rows] += term
    for s, block in enumerate((block0, block1, block2, block3)):
        block[...] = t_dot(normed[:, column_block(s, block.shape[0])], dq[...]).astype(bf16)
    for acc, first in ((acc_low, 0), (acc_up, half)):
        dk = (acc[:HD].T * scale).astype(bf16)
        dv = acc[HD:].T.astype(bf16)
        for i in range(pieces):
            dkv[i, first : first + half, :HD] = dk[i * half : (i + 1) * half]
            dkv[i, first : first + half, HD:] = dv[i * half : (i + 1) * half]


def sum_kernel(dq, cosines, sines, *refs):
    w_q, kvs, (parts, dkv, own, other) = refs[:4], refs[4:8], refs[8:]
    total = jnp.sum(parts[...].astype(f32), axis=0)
    dkv[:, :HD] = turn(total[:, :HD], cosines[...], -sines[...]).astype(bf16)
    dkv[:, HD:] = total[:, HD:].astype(bf16)
    quarter = own.shape[0] // 2
    for s in range(4):
        grad = dot_t(dq[...], w_q[s][...]) + dot_t(dkv[...], kvs[s][:, :WIDE])
        at = column_block(s, w_q[s].shape[0])
        own[:quarter, at] = grad[:quarter]
        other[:quarter, at] = grad[quarter : 2 * quarter]
        own[quarter:, at] = grad[2 * quarter : 3 * quarter]
        other[quarter:, at] = grad[3 * quarter :]


def stack_kernel(gate, up, down, late, out):
    del late
    out[0] = gate[...]
    out[1] = up[...]
    out[2] = down[...]


def small_grad_kernel(order, router_grad, gain_grad, late, out):
    del late
    row = lax.broadcasted_iota(jnp.int32, gain_grad.shape, 0)
    second = jnp.where(row == 1, gain_grad[...], 0.0).astype(bf16)
    small = router_grad[...] + t_dot(second, gain_picker())
    out[...] = t_dot(order[...], small.astype(bf16))


def input_kernel(both, own, received, midway_grad, gains, order, small, normed, dkv, out, *blocks):
    grad = own[...] + received[...]
    quarter = own.shape[0] // 2
    tokens = jnp.concatenate([both[:quarter], both[2 * quarter : 3 * quarter]])
    normal, inverse = normal_of(tokens.astype(f32))
    parts = in_three(norm_back(grad, normal, inverse, gains[0:1]))
    moved = dot_t(jnp.concatenate(parts), order[...])
    count = 2 * quarter
    out[...] = midway_grad[...] + (
        moved[:count] + (moved[count : 2 * count] + moved[2 * count :])
    )
    gain_grad = jnp.sum(grad * normal, axis=0, keepdims=True)
    row = lax.broadcasted_iota(jnp.int32, gains.shape, 0)
    gain_grad = jnp.where(row == 0, gain_grad, 0.0).astype(bf16)
    small = small[...] + t_dot(gain_grad, gain_picker())
    rows = blocks[0].shape[0]
    for s, block in enumerate(blocks):
        at = column_block(s, rows)
        block[:, :WIDE] = t_dot(normed[:, at], dkv[...]).astype(bf16)
        block[:, WIDE:] = small[at].astype(bf16)


def body(
    tokens,
    cotangent,
    pair_of,
    routes,
    attn_gain,
    moe_gain,
    w_query,
    w_key,
    w_value,
    w_out,
    w_router,
    w_gate,
    w_up,
    w_down,
):
    rows = tokens.shape[1]
    half = rows // 2
    width = tokens.shape[2]
    shard = w_query.shape[1]
    ctx_count = 16
    experts = w_router.shape[2]
    columns = w_gate.shape[3]
    per_group = H // KVH
    qw = per_group * HD
    scale = 1.0 / math.sqrt(HD)
    core = lax.axis_index("core")
    ylo, z, yhi = lax.axis_index("ylo"), lax.axis_index("z"), lax.axis_index("yhi")
    x = lax.axis_index("x")
    piece_rows = 2 * shard
    slots = experts * SLOTS
    own_tokens, cot = tokens[0], cotangent[0]

    def halves(matrix):
        return [matrix[:, : matrix.shape[1] // 2], matrix[:, matrix.shape[1] // 2 :]]

    small = jnp.concatenate([w_router[0], attn_gain[0][:, None], moe_gain[0][:, None]], axis=-1)
    small = jnp.pad(small, ((0, 0), (0, 128 - experts - 2)))
    query_halves, key_halves, value_halves = halves(w_query[0]), halves(w_key[0]), halves(w_value[0])
    pairs = [
        jnp.concatenate([k, v, small, q], axis=-1)
        for k, v, q in zip(key_halves, value_halves, query_halves)
    ]
    pieces = gather_pieces(pairs, yhi, core, ("core", "yhi"), SAME, OTHER)
    out_pieces = gather_pieces(
        halves(w_out[0]), yhi, yhi, ("ylo", "core", "yhi"), OUT_SAME, OUT_OTHER
    )
    other_tokens = partner(own_tokens)
    pieces, out_pieces, x, z, own_tokens, other_tokens, pair_of = together(
        pieces, out_pieces, x, z, own_tokens, other_tokens, pair_of
    )

    plane_rows = 16 * piece_rows
    plane = spread(pieces, 16, PLANE)
    both = jnp.concatenate(
        [own_tokens[:half], other_tokens[:half], own_tokens[half:], other_tokens[half:]]
    )
    order, out_order, level_order = order_matrix(16, x), order_matrix(8, x), level_order_matrix(z)
    (expert_shards_in,) = call(
        stack_kernel, [((3,) + w_gate.shape[1:], bf16)], w_gate[0], w_up[0], w_down[0], both
    )
    (
        plane, both, out_pieces, order, out_order, level_order, pair_of, expert_shards_in, chosen,
    ) = together(
        plane, both, out_pieces, order, out_order, level_order, pair_of, expert_shards_in,
        routes[0, 0],
    )

    plane = plane.reshape(plane_rows, -1)
    w_kvs = along("x", plane[:, : 3 * HD])
    wo = spread(out_pieces, 16, LEVEL)
    (both,) = call(order_kernel, [((2 * rows, width), bf16)], both, order)

    def two_cores(ctx):
        return jnp.stack([ctx + core, ctx + 1 - core], axis=-1).reshape(-1)

    ctx_here = (ylo * 4 + z) * 2
    q_place = places(pair_of, two_cores(ctx_here), rows, ctx_count)
    q_place = q_place.transpose(1, 0, 2).reshape(2 * rows, 1)
    key_place = places(
        pair_of, two_cores(jnp.arange(8, dtype=jnp.int32) * 2), rows, ctx_count
    )
    low_place, up_place = key_place[:, 0].reshape(1, -1), key_place[:, 1].reshape(1, -1)
    frequency = jnp.exp(jnp.arange(HD // 2, dtype=f32) * (-2.0 * math.log(ROPE_BASE) / HD))
    angles = q_place.astype(f32) * frequency[None, :]
    cosines, sines = jnp.cos(angles), jnp.sin(angles)
    cosines = jnp.concatenate([cosines, cosines], axis=-1)
    sines = jnp.concatenate([-sines, sines], axis=-1)
    lanes = jnp.arange(128, dtype=jnp.int32)
    hits = (chosen.T[:, :, None] == lanes[None, None, :]).astype(bf16)
    earlier = (lanes[:, None] > lanes[None, :]).astype(bf16)
    before = dot(earlier, jnp.sum(hits, axis=0))
    slot_index = jnp.sum(hits.astype(f32) * before[None], axis=-1).astype(jnp.int32)
    target = chosen.T * SLOTS + slot_index
    slot_row = jnp.arange(slots, dtype=jnp.int32)
    places_of = (target[:, :, None] == slot_row[None, None, :]).astype(bf16)
    placer_t = jnp.sum(places_of, axis=0)
    placer = placer_t.T
    (cot_rows,) = call(order_kernel, [((slots, width), bf16)], placer, cot)
    (
        w_q, w_kvs, wo, both, q_place, low_place, up_place, cosines, sines,
        hits, places_of, placer_t, placer, cot_rows,
    ) = together(
        plane[:, 3 * HD :], w_kvs, wo, both, q_place, low_place, up_place, cosines, sines,
        hits, places_of, placer_t, placer, cot_rows,
    )

    w_q = along("x", w_q)
    wo = along("z", wo.reshape(2, qw // 4, width // 2))
    normed, key_value, gains = call(
        keys_kernel,
        [((2 * rows, width), bf16), ((8, 2 * rows, 2 * HD), bf16), ((8, width), f32)],
        both,
        cosines,
        sines,
        *w_kvs,
    )
    all_kv = exchange(key_value, RING)
    small, moe_gains = call(
        small_kernel, [((width, 128), bf16), ((8, width), f32)], order, *w_kvs
    )
    (queries,) = call(
        query_kernel, [((2 * rows, qw), bf16)], normed, cosines, sines, *w_q, cost=LONG
    )
    queries, all_kv, expert_shards_in = together(queries, all_kv, expert_shards_in)
    expert_weights = lax.all_gather(expert_shards_in, CTX, axis=2, tiled=True)
    queries, small, moe_gains, wo, cot_rows = together(queries, small, moe_gains, wo, cot_rows)

    arrived_cot = to_owners(cot_rows.reshape(experts, SLOTS, width))
    sizes = dict(scale=scale, pieces=8, heads=per_group)
    keys = 8 * rows
    mixed, mixed_back, logs, kv_low, kv_up = call(
        functools.partial(attend_kernel, **sizes),
        [
            ((2 * rows, qw), bf16),
            ((2 * rows, qw), bf16),
            ((per_group, 2 * rows, 1), f32),
            ((keys, 2 * HD), bf16),
            ((keys, 2 * HD), bf16),
        ],
        queries,
        q_place,
        low_place,
        up_place,
        level_order,
        out_order,
        all_kv,
        scratch=[pltpu.VMEM((2 * rows, qw), bf16)],
    )

    branch_own, branch_other, wo = call(
        branch_kernel,
        [((rows, width), f32), ((rows, width), f32), ((2, qw, width // 2), bf16)],
        mixed,
        *wo,
    )
    sent, midway, moe_low, gates, gate_parts = call(
        route_kernel,
        [
            ((slots, width + 128), bf16),
            ((rows, width), f32),
            ((rows, width), bf16),
            ((rows, 128), f32),
            ((3, rows, slots), bf16),
        ],
        own_tokens,
        branch_own,
        partner(branch_other),
        small,
        moe_gains,
        hits,
        places_of,
        placer,
    )
    sent, arrived_cot = together(sent, arrived_cot)

    sent = to_owners(sent.reshape(experts, SLOTS, width + 128)).reshape(slots, width + 128)
    mine = core.reshape(1)
    expert_out, hidden, out_grad, factor, other_factor = expert_call(
        forward_kernel,
        mine,
        [sent, arrived_cot.reshape(slots, width)],
        expert_weights,
        [(width, bf16), (columns, bf16), (width, bf16), (columns, f32), (columns, f32)],
    )
    expert_out, factor = together(expert_out, factor)

    returned = to_owners(expert_out.reshape(experts, SLOTS, width))
    rows_grad, gate_grad, up_grad = expert_call(
        backward_kernel,
        mine,
        [out_grad, factor, other_factor],
        expert_weights,
        [(width, bf16), (columns, bf16), (columns, bf16)],
    )
    returned, rows_grad, gate_grad, up_grad = together(returned, rows_grad, gate_grad, up_grad)

    home_grad = to_owners(rows_grad.reshape(experts, SLOTS, width))
    expert_sums = expert_weights_grad(sent, out_grad, hidden, gate_grad, up_grad)
    output, moe_part, router_grad = call(
        combine_kernel,
        [((rows, width), bf16), ((rows, width), f32), ((width, 128), f32)],
        midway,
        gate_parts,
        returned.reshape(slots, width),
        cot,
        hits,
        places_of,
        gates,
        small,
        moe_low,
    )
    home_grad, moe_part, expert_sums = together(home_grad, moe_part, expert_sums)
    expert_sums = lax.psum_scatter(expert_sums, RING, scatter_dimension=1, tiled=True)
    midway_grad, branch_low, gain_two_grad = call(
        home_kernel,
        [((rows, width), f32), ((rows, width), bf16), ((8, width), f32)],
        placer_t,
        home_grad.reshape(slots, width),
        moe_part,
        midway,
        cot,
        moe_gains,
    )
    branch, *out_w_grad = call(
        out_grad_kernel,
        [((2 * rows, width), bf16)] + [((2, qw // 4, width // 2), bf16)] * 4,
        mixed_back,
        branch_low,
        partner(branch_low),
    )
    branch, out_w_grad = together(branch, out_w_grad)
    out_w_grad = added(back_along_x(out_w_grad))

    dq, dkv, *q_w_grad = call(
        functools.partial(attend_back_kernel, **sizes),
        [((2 * rows, qw), bf16), ((8, 2 * rows, 2 * HD), bf16)]
        + [((plane_rows, qw), bf16)] * 4,
        branch,
        wo,
        level_order,
        queries,
        kv_low,
        kv_up,
        logs,
        q_place,
        low_place,
        up_place,
        cosines,
        sines,
        normed,
        scratch=[
            pltpu.VMEM((2 * rows, qw), bf16),
            pltpu.VMEM((2 * HD, keys), f32),
            pltpu.VMEM((2 * HD, keys), f32),
        ],
    )
    dkv = exchange(dkv, RING)
    q_w_grad = back_along_x(q_w_grad)
    (small_grad,) = call(
        small_grad_kernel, [((width, 128), f32)], order, router_grad, gain_two_grad, dq
    )
    dkv, out_w_grad, small_grad, q_w_grad[1], q_w_grad[3] = together(
        dkv, out_w_grad, small_grad, q_w_grad[1], q_w_grad[3]
    )

    dkv, normed_own, normed_other = call(
        sum_kernel,
        [((2 * rows, 2 * HD), bf16), ((rows, width), f32), ((rows, width), f32)],
        dq,
        cosines,
        sines,
        *w_q,
        *w_kvs,
        dkv,
    )
    input_grad, *kvs_grad = call(
        input_kernel,
        [((rows, width), f32)] + [((plane_rows, 3 * HD), bf16)] * 4,
        both,
        normed_own,
        partner(normed_other),
        midway_grad,
        gains,
        order,
        small_grad,
        normed,
        dkv,
    )
    kvs_grad, out_w_grad, input_grad = together(kvs_grad, out_w_grad, input_grad)

    out_w_grad = exchange(out_w_grad.reshape(16, piece_rows, width // 2), OUT_PLANE)
    kvs_grad = back_along_x(kvs_grad)
    (plane_grad,) = call(
        add_both_kernel, [((plane_rows, qw + 3 * HD), bf16)], *q_w_grad, *kvs_grad, cost=LONG
    )
    plane_grad, out_w_grad = together(plane_grad, out_w_grad)
    plane_grad = exchange(plane_grad.reshape(16, piece_rows, qw + 3 * HD), PLANE)

    def summed(pieces):
        return jnp.sum(pieces.astype(f32), axis=0)

    def expert_shards(grad):
        count = grad.shape[1] // 2
        kept = lax.dynamic_slice_in_dim(grad, core * count, count, axis=1)
        given = partner(lax.dynamic_slice_in_dim(grad, (1 - core) * count, count, axis=1))
        both = jnp.stack([pick(core, kept, given), pick(core, given, kept)], axis=1)
        return [both[i : i + 1].astype(f32) for i in range(3)]

    out_w_grad = scatter_pieces(
        summed(out_w_grad), yhi, yhi, ("ylo", "core", "yhi"), OUT_SAME, OUT_OTHER
    )
    w_gate_grad, w_up_grad, w_down_grad = expert_shards(expert_sums)
    plane_grad, out_w_grad, w_gate_grad, w_up_grad, w_down_grad = together(
        plane_grad, out_w_grad, w_gate_grad, w_up_grad, w_down_grad
    )
    plane_grad = scatter_pieces(summed(plane_grad), yhi, core, ("core", "yhi"), SAME, OTHER)
    plane_grad = plane_grad.reshape(shard, 2, -1)

    def joined(first, last):
        return plane_grad[:, :, first:last].reshape(1, shard, -1)

    small_grad = jnp.sum(plane_grad[None, :, :, qw + 2 * HD :], axis=2)

    return (
        output[None],
        input_grad[None],
        small_grad[:, :, experts],
        small_grad[:, :, experts + 1],
        joined(0, qw),
        joined(qw, qw + HD),
        joined(qw + HD, qw + 2 * HD),
        out_w_grad[None],
        small_grad[:, :, :experts],
        w_gate_grad,
        w_up_grad,
        w_down_grad,
    )


def solution(mesh):
    fine = Mesh(mesh.devices.reshape(2, 4, 2, 4, 2), AXES)
    seq = P(FSDP, CTX, None)
    vector = P(None, AXES)
    matrix = P(None, AXES, None)
    expert = P(None, FSDP, CTX, None)
    in_specs = (
        seq,
        seq,
        P(),
        P(None, FSDP, CTX, None),
        vector,
        vector,
        matrix,
        matrix,
        matrix,
        matrix,
        matrix,
        expert,
        expert,
        expert,
    )
    out_specs = (
        seq,
        seq,
        vector,
        vector,
        matrix,
        matrix,
        matrix,
        matrix,
        matrix,
        expert,
        expert,
        expert,
    )
    return jax.shard_map(body, mesh=fine, in_specs=in_specs, out_specs=out_specs, check_vma=False)
```

```python
import functools
import math

import jax
import jax.numpy as jnp
from jax import lax
from jax.experimental import pallas as pl
from jax.experimental.pallas import tpu as pltpu
from jax.sharding import Mesh
from jax.sharding import PartitionSpec as P

H = 12
KVH = 2
HD = 128
TOPK = 4

EPSILON = 1e-06
ROPE_BASE = 1000000.0
NEGATIVE = -1e30

AXES = ("ylo", "z", "core", "x", "yhi")
CTX = ("ylo", "z", "core")
FSDP = ("x", "yhi")
GROUPS = [
    [
        (((group ^ yhi) * 4 + z) * 2 + core) * 8 + x * 2 + yhi
        for x in range(4)
        for yhi in range(2)
        for core in range(2)
    ]
    for group in range(2)
    for z in range(4)
]
RING = ("ylo", "z")
PLANE = ("ylo", "z", "yhi")
OUT_PLANE = ("yhi", "z", "ylo")
LEVEL = ("yhi", "ylo", "x")
GROUPS = [
    [
        (((group ^ yhi) * 4 + z) * 2 + core) * 8 + x * 2 + yhi
        for x in range(4)
        for yhi in range(2)
        for core in range(2)
    ]
    for group in range(2)
    for z in range(4)
]
RING = ("ylo", "z")
ROWS_ORDER = ("ylo", "z", "yhi", "x")
OUT_ORDER = ("yhi", "z", "ylo", "x")
SLOTS = 40

bf16 = jnp.bfloat16
f32 = jnp.float32


def dot(left, right):
    return jnp.dot(left, right, preferred_element_type=f32)


def dot_t(left, right):
    return lax.dot_general(left, right, (((1,), (1,)), ((), ())), preferred_element_type=f32)


def t_dot(left, right):
    return lax.dot_general(left, right, (((0,), (0,)), ((), ())), preferred_element_type=f32)


def exchange(pieces, axes):
    return lax.all_to_all(pieces, axes, split_axis=0, concat_axis=0, tiled=True)


def to_owners(pieces):
    return lax.all_to_all(
        pieces, AXES, split_axis=0, concat_axis=0, axis_index_groups=GROUPS, tiled=True
    )


def spread(piece, count, axes):
    return exchange(jnp.broadcast_to(piece[None], (count,) + piece.shape), axes)


def after(value, earlier):
    return lax.optimization_barrier((value, earlier))[0]


def together(*values):
    return lax.optimization_barrier(values)


def partner(value):
    return lax.ppermute(value, "core", [(0, 1), (1, 0)])


def route(axes, sizes, move):
    pairs = []
    for source in range(math.prod(sizes)):
        rest, at = source, []
        for size in reversed(sizes):
            at.insert(0, rest % size)
            rest //= size
        target = 0
        for size, value in zip(sizes, move(*at)):
            target = target * size + value
        pairs.append((source, target))
    return pairs


SAME = route(("core", "yhi"), (2, 2), lambda c, h: (h, c))
OTHER = route(("core", "yhi"), (2, 2), lambda c, h: (1 - h, c))
OUT_SAME = route(("ylo", "core", "yhi"), (2, 2, 2), lambda j, c, h: (c, j, h))
OUT_OTHER = route(("ylo", "core", "yhi"), (2, 2, 2), lambda j, c, h: (c, j, 1 - h))


def back(pairs):
    return [(target, source) for source, target in pairs]


def pick(flag, if_zero, if_one):
    return jnp.where(flag == 0, if_zero, if_one)


def gather_pieces(pair, flag, key, axes, same, other):
    first = lax.ppermute(pick(flag, pair[0], pair[1]), axes, same)
    second = lax.ppermute(pick(flag, pair[1], pair[0]), axes, other)
    return pick(
        key, jnp.concatenate([first, second]), jnp.concatenate([second, first])
    )


def scatter_pieces(piece, flag, key, axes, same, other):
    count = piece.shape[0] // 2
    mine, rest = piece[:count], piece[count:]
    first = lax.ppermute(pick(key, mine, rest), axes, back(same))
    second = lax.ppermute(pick(key, rest, mine), axes, back(other))
    return pick(flag, jnp.concatenate([first, second], axis=-1), jnp.concatenate([second, first], axis=-1))


def along(axis, piece):
    return [piece] + [
        lax.ppermute(piece, axis, [(i, (i + s) % 4) for i in range(4)]) for s in (1, 2, 3)
    ]


def back_along_x(blocks):
    return [blocks[0]] + [
        lax.ppermute(blocks[s], "x", [(i, (i - s) % 4) for i in range(4)]) for s in (1, 2, 3)
    ]


def added(blocks):
    (total,) = call(add_kernel, [(blocks[0].shape, bf16)], *blocks, cost=LONG)
    return total


def sum_of(first, second, third, fourth):
    return (
        (first[...].astype(f32) + second[...].astype(f32))
        + (third[...].astype(f32) + fourth[...].astype(f32))
    ).astype(bf16)


def add_kernel(first, second, third, fourth, total):
    total[...] = sum_of(first, second, third, fourth)


def add_both_kernel(*refs):
    total = refs[8]
    count = refs[0].shape[1]
    total[:, :count] = sum_of(*refs[:4])
    total[:, count:] = sum_of(*refs[4:8])


def order_matrix(groups, x):
    index = jnp.arange(groups * 96, dtype=jnp.int32)
    turn_of, group, row = index // (groups * 24), index // 24 % groups, index % 24
    own = group * 96 + (x - turn_of) % 4 * 24 + row
    return (index[:, None] == own[None, :]).astype(bf16)


def level_order_matrix(z):
    index = jnp.arange(8 * 96, dtype=jnp.int32)
    own = (z - index // 192) % 4 * 192 + index % 192
    return (index[:, None] == own[None, :]).astype(bf16)


def places(pair_of, ctx, row_count, ctx_count):
    half_size = row_count // 2
    pair = jnp.sum(
        jnp.where(ctx[:, None] == jnp.arange(ctx_count, dtype=jnp.int32)[None], pair_of[None], 0),
        axis=1,
    )
    block = jnp.stack([pair, 2 * ctx_count - 1 - pair], axis=1)
    return block[:, :, None] * half_size + jnp.arange(half_size, dtype=jnp.int32)[None, None]


def in_three(value):
    high = value.astype(bf16)
    rest = value - high.astype(f32)
    middle = rest.astype(bf16)
    return [high, middle, (rest - middle.astype(f32)).astype(bf16)]


def call(kernel, outs, *args, scratch=(), cost=None):
    def whole(shape):
        return pl.BlockSpec(shape, lambda i: (0,) * len(shape))

    return pl.pallas_call(
        kernel,
        out_shape=[jax.ShapeDtypeStruct(shape, dtype) for shape, dtype in outs],
        grid=(1,),
        in_specs=[whole(a.shape) for a in args],
        out_specs=[whole(shape) for shape, _ in outs],
        scratch_shapes=list(scratch),
        compiler_params=pltpu.CompilerParams(vmem_limit_bytes=ROOM),
        cost_estimate=COST if cost is None else cost,
    )(*args)


ROOM = 58 << 20
COST = pl.CostEstimate(flops=1 << 20, bytes_accessed=1 << 18, transcendentals=0)
LONG = pl.CostEstimate(flops=1 << 35, bytes_accessed=1 << 27, transcendentals=0)
WIDE = 2 * HD
EXPERTS = 16


def turn(vectors, cosines, sines):
    return vectors * cosines + pltpu.roll(vectors, HD // 2, axis=1) * sines


def gain_picker():
    row = lax.broadcasted_iota(jnp.int32, (8, 128), 0)
    column = lax.broadcasted_iota(jnp.int32, (8, 128), 1)
    return jnp.where((column == row + EXPERTS) & (row < 2), 1.0, 0.0).astype(bf16)


def normal_of(stream):
    inverse = lax.rsqrt(jnp.mean(stream * stream, axis=-1, keepdims=True) + EPSILON)
    return stream * inverse, inverse


def norm_back(grad, normal, inverse, gain):
    scaled = grad * gain
    return inverse * (scaled - normal * jnp.mean(scaled * normal, axis=-1, keepdims=True))


def column_block(s, count):
    return slice(s * count, (s + 1) * count)


def order_kernel(rows, order, out):
    out[...] = dot(rows[...], order[...]).astype(bf16)


def keys_kernel(both, cosines, sines, *refs):
    kvs, (normed, key_value, gains) = refs[:4], refs[4:]
    count = kvs[0].shape[0]
    for s in range(4):
        gains[:, column_block(s, count)] = dot_t(gain_picker(), kvs[s][:, WIDE:])
    normal, _ = normal_of(both[...].astype(f32))
    normed[...] = (normal * gains[0:1]).astype(bf16)
    kv = dot(normed[:, column_block(0, count)], kvs[0][:, :WIDE])
    for s in range(1, 4):
        kv = kv + dot(normed[:, column_block(s, count)], kvs[s][:, :WIDE])
    keys = turn(kv[:, :HD], cosines[...], sines[...]).astype(bf16)
    values = kv[:, HD:].astype(bf16)
    for i in range(key_value.shape[0]):
        key_value[i, :, :HD] = keys
        key_value[i, :, HD:] = values


def small_kernel(order, kvs0, kvs1, kvs2, kvs3, small, gains):
    count = kvs0.shape[0]
    total = jnp.zeros(small.shape, f32)
    for s, kvs in enumerate((kvs0, kvs1, kvs2, kvs3)):
        total = total + dot(order[:, column_block(s, count)], kvs[:, WIDE:])
    small[...] = total.astype(bf16)
    gains[...] = dot_t(gain_picker(), small[...])


def query_kernel(normed, cosines, sines, w_q0, w_q1, w_q2, w_q3, queries):
    w_q = (w_q0, w_q1, w_q2, w_q3)
    count = w_q0.shape[0]
    for h in range(queries.shape[1] // HD):
        at = column_block(h, HD)
        q = dot(normed[:, column_block(0, count)], w_q0[:, at])
        for s in range(1, 4):
            q = q + dot(normed[:, column_block(s, count)], w_q[s][:, at])
        queries[:, at] = turn(q, cosines[...], sines[...]).astype(bf16)


def attend_kernel(
    queries,
    q_place,
    low_place,
    up_place,
    order,
    order_back,
    kv,
    ordered,
    ordered_back,
    logs,
    kv_low,
    kv_up,
    mixed,
    *,
    scale,
    pieces,
    heads,
):
    half = kv.shape[1] // 2
    for i in range(pieces):
        kv_low[i * half : (i + 1) * half, :] = kv[i, :half]
        kv_up[i * half : (i + 1) * half, :] = kv[i, half:]
    allowed_low = low_place[...] <= q_place[...]
    allowed_up = up_place[...] <= q_place[half:, :]
    for h in range(heads):
        at = slice(h * HD, (h + 1) * HD)
        q = queries[:, at]
        low = jnp.where(allowed_low, dot_t(q, kv_low[:, :HD]) * scale, NEGATIVE)
        up = jnp.where(allowed_up, dot_t(q[half:], kv_up[:, :HD]) * scale, NEGATIVE)
        first, second = low[:half], low[half:]
        top = jnp.max(first, axis=-1, keepdims=True)
        weight = jnp.exp(first - top)
        total = jnp.sum(weight, axis=-1, keepdims=True)
        probs = (weight / total).astype(bf16)
        mixed[:half, at] = dot(probs, kv_low[:, HD:]).astype(bf16)
        logs[h, :half, :] = top + jnp.log(total)
        top = jnp.maximum(
            jnp.max(second, axis=-1, keepdims=True), jnp.max(up, axis=-1, keepdims=True)
        )
        weight, weight_up = jnp.exp(second - top), jnp.exp(up - top)
        total = jnp.sum(weight, axis=-1, keepdims=True) + jnp.sum(
            weight_up, axis=-1, keepdims=True
        )
        mixed[half:, at] = (
            dot((weight / total).astype(bf16), kv_low[:, HD:])
            + dot((weight_up / total).astype(bf16), kv_up[:, HD:])
        ).astype(bf16)
        logs[h, half:, :] = top + jnp.log(total)
    ordered[...] = dot(mixed[...], order[...]).astype(bf16)
    ordered_back[...] = dot(mixed[...], order_back[...]).astype(bf16)


def branch_kernel(mixed, w_out0, w_out1, w_out2, w_out3, own, other, w_out):
    quarter = mixed.shape[0] // 4
    count, columns = w_out0.shape[1:]
    for s, part in enumerate((w_out0, w_out1, w_out2, w_out3)):
        w_out[:, column_block(s, count)] = part[...]
    for k in range(2):
        part = dot(mixed[...], w_out[k])
        at = slice(k * columns, (k + 1) * columns)
        own[:quarter, at] = part[:quarter]
        other[:quarter, at] = part[quarter : 2 * quarter]
        own[quarter:, at] = part[2 * quarter : 3 * quarter]
        other[quarter:, at] = part[3 * quarter :]


def route_kernel(
    tokens,
    own,
    received,
    small,
    gains,
    hits,
    places_of,
    placer,
    sent,
    midway,
    moe_low,
    gates,
    parts,
):
    middle = tokens[...].astype(f32) + (own[...] + received[...])
    midway[...] = middle
    normal, _ = normal_of(middle)
    moe = (normal * gains[1:2]).astype(bf16)
    moe_low[...] = moe
    sent[:, : moe.shape[1]] = dot(placer[...], moe).astype(bf16)
    logits = dot(moe, small[...])
    picked = [
        jnp.sum(hits[k].astype(f32) * logits, axis=-1, keepdims=True) for k in range(TOPK)
    ]
    top = picked[0]
    for value in picked[1:]:
        top = jnp.maximum(top, value)
    weights = [jnp.exp(value - top) for value in picked]
    total = weights[0]
    for value in weights[1:]:
        total = total + value
    lane = lax.broadcasted_iota(jnp.int32, gates.shape, 1)
    gate_at = jnp.zeros(places_of.shape[1:], f32)
    kept = jnp.zeros(gates.shape, f32)
    for k in range(TOPK):
        gate = weights[k] / total
        kept = jnp.where(lane == k, gate, kept)
        gate_at = gate_at + places_of[k].astype(f32) * gate
    gates[...] = kept
    block = jnp.zeros((sent.shape[0], 128), f32)
    for i, part in enumerate(in_three(gate_at)):
        parts[i] = part
        block = block + t_dot(part, jnp.where(lane == i, 1.0, 0.0).astype(bf16))
    sent[:, moe.shape[1] :] = block.astype(bf16)


def fetched(core, weights, held, sems, first):
    copies = [
        pltpu.make_async_copy(weights.at[m, core[0]], held.at[m], sems.at[m]) for m in range(3)
    ]
    for m in first:
        copies[m].start()

    def ready(m):
        copies[m].wait()
        return held[m]

    return ready


def forward_kernel(
    core, sent, cot, weights, out, hidden, out_grad, factor, other_factor, held, sems
):
    ready = fetched(core, weights, held, sems, (0, 1, 2))
    width = out.shape[1]
    gates = jnp.sum(sent[:, width:].astype(f32), axis=-1, keepdims=True)
    out_grad[...] = (gates * cot[...].astype(f32)).astype(bf16)
    rows = sent[:, :width]
    gate_pre = dot(rows, ready(0))
    up_pre = dot(rows, ready(1))
    sigmoid = 1.0 / (1.0 + jnp.exp(-gate_pre))
    silu = gate_pre * sigmoid
    low = (silu * up_pre).astype(bf16)
    hidden[...] = low
    out[...] = dot_t(low, ready(2)).astype(bf16)
    factor[...] = up_pre * sigmoid * (1.0 + gate_pre * (1.0 - sigmoid))
    other_factor[...] = silu


def backward_kernel(
    core, out_grad, factor, other_factor, weights, rows_grad, gate_grad, up_grad, held, sems
):
    ready = fetched(core, weights, held, sems, (2, 0, 1))
    hidden_grad = dot(out_grad[...], ready(2))
    low = (hidden_grad * factor[...]).astype(bf16)
    other = (hidden_grad * other_factor[...]).astype(bf16)
    gate_grad[...] = low
    up_grad[...] = other
    rows_grad[...] = (dot_t(low, ready(0)) + dot_t(other, ready(1))).astype(bf16)


def expert_call(kernel, core, arrays, weights, outs):
    rows = arrays[0].shape[0]

    def whole(columns):
        return pl.BlockSpec((rows, columns), lambda i, core: (0, 0))

    return pl.pallas_call(
        kernel,
        out_shape=[jax.ShapeDtypeStruct((rows, columns), dtype) for columns, dtype in outs],
        grid_spec=pltpu.PrefetchScalarGridSpec(
            num_scalar_prefetch=1,
            grid=(1,),
            in_specs=[whole(a.shape[1]) for a in arrays] + [pl.BlockSpec(memory_space=pltpu.HBM)],
            out_specs=[whole(columns) for columns, _ in outs],
            scratch_shapes=[
                pltpu.VMEM((3,) + weights.shape[2:], bf16),
                pltpu.SemaphoreType.DMA((3,)),
            ],
        ),
        compiler_params=pltpu.CompilerParams(vmem_limit_bytes=ROOM),
        cost_estimate=COST,
    )(core, *arrays, weights)


def weights_kernel(sent, out_grad, hidden, gate_grad, up_grad, sums):
    rows = sent[...]
    sums[0] = t_dot(rows, gate_grad[...]).astype(bf16)
    sums[1] = t_dot(rows, up_grad[...]).astype(bf16)
    sums[2] = t_dot(out_grad[...], hidden[...]).astype(bf16)


def expert_weights_grad(sent, out_grad, hidden, gate_grad, up_grad, block=256):
    count, width = out_grad.shape
    columns = hidden.shape[1]
    part = pl.BlockSpec((count, block), lambda i: (0, i))
    whole = pl.BlockSpec((count, columns), lambda i: (0, 0), pipeline_mode=pl.Buffered(1))
    return pl.pallas_call(
        weights_kernel,
        out_shape=jax.ShapeDtypeStruct((3, width, columns), bf16),
        grid=(width // block,),
        in_specs=[part, part, whole, whole, whole],
        out_specs=pl.BlockSpec((3, block, columns), lambda i: (0, i, 0)),
        compiler_params=pltpu.CompilerParams(vmem_limit_bytes=ROOM),
        cost_estimate=COST,
    )(sent, out_grad, hidden, gate_grad, up_grad)


def combine_kernel(
    midway, parts, returned, cot, hits, places_of, gates, small, moe_low, output, moe_part, router_grad
):
    rows = returned[...]
    output[...] = (
        midway[...] + (dot(parts[0], rows) + (dot(parts[1], rows) + dot(parts[2], rows)))
    ).astype(bf16)
    agreement = dot_t(cot[...], rows)
    lane = lax.broadcasted_iota(jnp.int32, gates.shape, 1)
    gate, grad = [], []
    mean = jnp.zeros((gates.shape[0], 1), f32)
    for k in range(TOPK):
        gate.append(jnp.sum(jnp.where(lane == k, gates[...], 0.0), axis=-1, keepdims=True))
        grad.append(jnp.sum(places_of[k].astype(f32) * agreement, axis=-1, keepdims=True))
        mean = mean + gate[k] * grad[k]
    logit_grad = jnp.zeros(gates.shape, f32)
    for k in range(TOPK):
        logit_grad = logit_grad + hits[k].astype(f32) * (gate[k] * (grad[k] - mean))
    logit_grad = logit_grad.astype(bf16)
    moe_part[...] = dot_t(logit_grad, small[...])
    router_grad[...] = t_dot(moe_low[...], logit_grad)


def home_kernel(placer_t, home, moe_part, midway, cot, gains, midway_grad, branch_low, gain_grad):
    grad = dot(placer_t[...], home[...]) + moe_part[...]
    normal, inverse = normal_of(midway[...])
    result = cot[...].astype(f32) + norm_back(grad, normal, inverse, gains[1:2])
    midway_grad[...] = result
    branch_low[...] = result.astype(bf16)
    gain_grad[...] = jnp.broadcast_to(
        jnp.sum(grad * normal, axis=0, keepdims=True), gain_grad.shape
    )


def out_grad_kernel(mixed, own, other, branch, *blocks):
    quarter = own.shape[0] // 2
    branch[:quarter] = own[:quarter]
    branch[quarter : 2 * quarter] = other[:quarter]
    branch[2 * quarter : 3 * quarter] = own[quarter:]
    branch[3 * quarter :] = other[quarter:]
    count, columns = blocks[0].shape[1:]
    for k in range(2):
        grad = t_dot(mixed[...], branch[:, column_block(k, columns)]).astype(bf16)
        for s in range(4):
            blocks[s][k] = grad[column_block(s, count)]


def attend_back_kernel(
    branch,
    w_out,
    order,
    queries,
    kv_low,
    kv_up,
    logs,
    q_place,
    low_place,
    up_place,
    cosines,
    sines,
    normed,
    dq,
    dkv,
    block0,
    block1,
    block2,
    block3,
    grads,
    acc_low,
    acc_up,
    *,
    scale,
    pieces,
    heads,
):
    half = queries.shape[0] // 2
    columns = w_out.shape[2]
    ordered = dot_t(branch[:, :columns], w_out[0]) + dot_t(branch[:, columns:], w_out[1])
    grads[...] = dot_t(ordered.astype(bf16), order[...]).astype(bf16)
    allowed_low = low_place[...] <= q_place[...]
    allowed_up = up_place[...] <= q_place[half:, :]
    key_low, value_low = kv_low[:, :HD], kv_low[:, HD:]
    key_up, value_up = kv_up[:, :HD], kv_up[:, HD:]
    for h in range(heads):
        at = slice(h * HD, (h + 1) * HD)
        q, grad, log = queries[:, at], grads[:, at], logs[h]
        low = jnp.where(allowed_low, dot_t(q, key_low) * scale, NEGATIVE)
        up = jnp.where(allowed_up, dot_t(q[half:], key_up) * scale, NEGATIVE)
        probs_low, probs_up = jnp.exp(low - log), jnp.exp(up - log[half:])
        grad_low, grad_up = dot_t(grad, value_low), dot_t(grad[half:], value_up)
        along = jnp.sum(probs_low * grad_low, axis=-1, keepdims=True)
        along_up = along[half:] + jnp.sum(probs_up * grad_up, axis=-1, keepdims=True)
        along = jnp.concatenate([along[:half], along_up])
        score_low = (probs_low * (grad_low - along)).astype(bf16)
        score_up = (probs_up * (grad_up - along_up)).astype(bf16)
        part = dot(score_low, key_low)
        part = jnp.concatenate([part[:half], part[half:] + dot(score_up, key_up)]) * scale
        dq[:, at] = turn(part, cosines[...], -sines[...]).astype(bf16)
        terms = (
            (acc_low, slice(0, HD), t_dot(q, score_low)),
            (acc_up, slice(0, HD), t_dot(q[half:], score_up)),
            (acc_low, slice(HD, 2 * HD), t_dot(grad, probs_low.astype(bf16))),
            (acc_up, slice(HD, 2 * HD), t_dot(grad[half:], probs_up.astype(bf16))),
        )
        for acc, rows, term in terms:
            if h == 0:
                acc[rows] = term
            else:
                acc[rows] += term
    for s, block in enumerate((block0, block1, block2, block3)):
        block[...] = t_dot(normed[:, column_block(s, block.shape[0])], dq[...]).astype(bf16)
    for acc, first in ((acc_low, 0), (acc_up, half)):
        dk = (acc[:HD].T * scale).astype(bf16)
        dv = acc[HD:].T.astype(bf16)
        for i in range(pieces):
            dkv[i, first : first + half, :HD] = dk[i * half : (i + 1) * half]
            dkv[i, first : first + half, HD:] = dv[i * half : (i + 1) * half]


def sum_kernel(dq, cosines, sines, *refs):
    w_q, kvs, (parts, dkv, own, other) = refs[:4], refs[4:8], refs[8:]
    total = jnp.sum(parts[...].astype(f32), axis=0)
    dkv[:, :HD] = turn(total[:, :HD], cosines[...], -sines[...]).astype(bf16)
    dkv[:, HD:] = total[:, HD:].astype(bf16)
    quarter = own.shape[0] // 2
    for s in range(4):
        grad = dot_t(dq[...], w_q[s][...]) + dot_t(dkv[...], kvs[s][:, :WIDE])
        at = column_block(s, w_q[s].shape[0])
        own[:quarter, at] = grad[:quarter]
        other[:quarter, at] = grad[quarter : 2 * quarter]
        own[quarter:, at] = grad[2 * quarter : 3 * quarter]
        other[quarter:, at] = grad[3 * quarter :]


def stack_kernel(gate, up, down, late, out):
    del late
    out[0] = gate[...]
    out[1] = up[...]
    out[2] = down[...]


def small_grad_kernel(order, router_grad, gain_grad, late, out):
    del late
    row = lax.broadcasted_iota(jnp.int32, gain_grad.shape, 0)
    second = jnp.where(row == 1, gain_grad[...], 0.0).astype(bf16)
    small = router_grad[...] + t_dot(second, gain_picker())
    out[...] = t_dot(order[...], small.astype(bf16))


def input_kernel(both, own, received, midway_grad, gains, order, small, normed, dkv, out, *blocks):
    grad = own[...] + received[...]
    quarter = own.shape[0] // 2
    tokens = jnp.concatenate([both[:quarter], both[2 * quarter : 3 * quarter]])
    normal, inverse = normal_of(tokens.astype(f32))
    parts = in_three(norm_back(grad, normal, inverse, gains[0:1]))
    moved = dot_t(jnp.concatenate(parts), order[...])
    count = 2 * quarter
    out[...] = midway_grad[...] + (
        moved[:count] + (moved[count : 2 * count] + moved[2 * count :])
    )
    gain_grad = jnp.sum(grad * normal, axis=0, keepdims=True)
    row = lax.broadcasted_iota(jnp.int32, gains.shape, 0)
    gain_grad = jnp.where(row == 0, gain_grad, 0.0).astype(bf16)
    small = small[...] + t_dot(gain_grad, gain_picker())
    rows = blocks[0].shape[0]
    for s, block in enumerate(blocks):
        at = column_block(s, rows)
        block[:, :WIDE] = t_dot(normed[:, at], dkv[...]).astype(bf16)
        block[:, WIDE:] = small[at].astype(bf16)


def body(
    tokens,
    cotangent,
    pair_of,
    routes,
    attn_gain,
    moe_gain,
    w_query,
    w_key,
    w_value,
    w_out,
    w_router,
    w_gate,
    w_up,
    w_down,
):
    rows = tokens.shape[1]
    half = rows // 2
    width = tokens.shape[2]
    shard = w_query.shape[1]
    ctx_count = 16
    experts = w_router.shape[2]
    columns = w_gate.shape[3]
    per_group = H // KVH
    qw = per_group * HD
    scale = 1.0 / math.sqrt(HD)
    core = lax.axis_index("core")
    ylo, z, yhi = lax.axis_index("ylo"), lax.axis_index("z"), lax.axis_index("yhi")
    x = lax.axis_index("x")
    piece_rows = 2 * shard
    slots = experts * SLOTS
    own_tokens, cot = tokens[0], cotangent[0]

    def halves(matrix):
        return [matrix[:, : matrix.shape[1] // 2], matrix[:, matrix.shape[1] // 2 :]]

    small = jnp.concatenate([w_router[0], attn_gain[0][:, None], moe_gain[0][:, None]], axis=-1)
    small = jnp.pad(small, ((0, 0), (0, 128 - experts - 2)))
    query_halves, key_halves, value_halves = halves(w_query[0]), halves(w_key[0]), halves(w_value[0])
    pairs = [
        jnp.concatenate([k, v, small, q], axis=-1)
        for k, v, q in zip(key_halves, value_halves, query_halves)
    ]
    pieces = gather_pieces(pairs, yhi, core, ("core", "yhi"), SAME, OTHER)
    out_pieces = gather_pieces(
        halves(w_out[0]), yhi, yhi, ("ylo", "core", "yhi"), OUT_SAME, OUT_OTHER
    )
    other_tokens = partner(own_tokens)
    pieces, out_pieces, x, z, own_tokens, other_tokens, pair_of, chosen = together(
        pieces, out_pieces, x, z, own_tokens, other_tokens, pair_of, routes[0, 0]
    )

    plane_rows = 16 * piece_rows
    plane = spread(pieces, 16, PLANE)
    both = jnp.concatenate(
        [own_tokens[:half], other_tokens[:half], own_tokens[half:], other_tokens[half:]]
    )
    order, out_order, level_order = order_matrix(16, x), order_matrix(8, x), level_order_matrix(z)
    lanes = jnp.arange(128, dtype=jnp.int32)
    hits = (chosen.T[:, :, None] == lanes[None, None, :]).astype(bf16)
    earlier = (lanes[:, None] > lanes[None, :]).astype(bf16)
    before = dot(earlier, jnp.sum(hits, axis=0))
    slot_index = jnp.sum(hits.astype(f32) * before[None], axis=-1).astype(jnp.int32)
    target = chosen.T * SLOTS + slot_index
    slot_row = jnp.arange(slots, dtype=jnp.int32)
    places_of = (target[:, :, None] == slot_row[None, None, :]).astype(bf16)
    placer_t = jnp.sum(places_of, axis=0)
    placer = placer_t.T
    (expert_shards_in,) = call(
        stack_kernel, [((3,) + w_gate.shape[1:], bf16)], w_gate[0], w_up[0], w_down[0], both
    )
    (
        plane, both, out_pieces, order, out_order, level_order, pair_of, expert_shards_in,
        hits, places_of, placer_t, placer,
    ) = together(
        plane, both, out_pieces, order, out_order, level_order, pair_of, expert_shards_in,
        hits, places_of, placer_t, placer,
    )

    plane = plane.reshape(plane_rows, -1)
    w_kvs = along("x", plane[:, : 3 * HD])
    wo = spread(out_pieces, 16, LEVEL)
    (both,) = call(order_kernel, [((2 * rows, width), bf16)], both, order)

    def two_cores(ctx):
        return jnp.stack([ctx + core, ctx + 1 - core], axis=-1).reshape(-1)

    ctx_here = (ylo * 4 + z) * 2
    q_place = places(pair_of, two_cores(ctx_here), rows, ctx_count)
    q_place = q_place.transpose(1, 0, 2).reshape(2 * rows, 1)
    key_place = places(
        pair_of, two_cores(jnp.arange(8, dtype=jnp.int32) * 2), rows, ctx_count
    )
    low_place, up_place = key_place[:, 0].reshape(1, -1), key_place[:, 1].reshape(1, -1)
    frequency = jnp.exp(jnp.arange(HD // 2, dtype=f32) * (-2.0 * math.log(ROPE_BASE) / HD))
    angles = q_place.astype(f32) * frequency[None, :]
    cosines, sines = jnp.cos(angles), jnp.sin(angles)
    cosines = jnp.concatenate([cosines, cosines], axis=-1)
    sines = jnp.concatenate([-sines, sines], axis=-1)
    (cot_rows,) = call(order_kernel, [((slots, width), bf16)], placer, cot)
    (
        w_q, w_kvs, wo, both, q_place, low_place, up_place, cosines, sines, cot_rows,
    ) = together(
        plane[:, 3 * HD :], w_kvs, wo, both, q_place, low_place, up_place, cosines, sines, cot_rows,
    )

    w_q = along("x", w_q)
    wo = along("z", wo.reshape(2, qw // 4, width // 2))
    normed, key_value, gains = call(
        keys_kernel,
        [((2 * rows, width), bf16), ((8, 2 * rows, 2 * HD), bf16), ((8, width), f32)],
        both,
        cosines,
        sines,
        *w_kvs,
    )
    all_kv = exchange(key_value, RING)
    small, moe_gains = call(
        small_kernel, [((width, 128), bf16), ((8, width), f32)], order, *w_kvs
    )
    (queries,) = call(
        query_kernel, [((2 * rows, qw), bf16)], normed, cosines, sines, *w_q, cost=LONG
    )
    queries, all_kv, expert_shards_in, small, moe_gains, wo, cot_rows = together(
        queries, all_kv, expert_shards_in, small, moe_gains, wo, cot_rows
    )
    expert_weights = lax.all_gather(expert_shards_in, CTX, axis=2, tiled=True)

    arrived_cot = to_owners(cot_rows.reshape(experts, SLOTS, width))
    sizes = dict(scale=scale, pieces=8, heads=per_group)
    keys = 8 * rows
    mixed, mixed_back, logs, kv_low, kv_up = call(
        functools.partial(attend_kernel, **sizes),
        [
            ((2 * rows, qw), bf16),
            ((2 * rows, qw), bf16),
            ((per_group, 2 * rows, 1), f32),
            ((keys, 2 * HD), bf16),
            ((keys, 2 * HD), bf16),
        ],
        queries,
        q_place,
        low_place,
        up_place,
        level_order,
        out_order,
        all_kv,
        scratch=[pltpu.VMEM((2 * rows, qw), bf16)],
    )

    branch_own, branch_other, wo = call(
        branch_kernel,
        [((rows, width), f32), ((rows, width), f32), ((2, qw, width // 2), bf16)],
        mixed,
        *wo,
    )
    sent, midway, moe_low, gates, gate_parts = call(
        route_kernel,
        [
            ((slots, width + 128), bf16),
            ((rows, width), f32),
            ((rows, width), bf16),
            ((rows, 128), f32),
            ((3, rows, slots), bf16),
        ],
        own_tokens,
        branch_own,
        partner(branch_other),
        small,
        moe_gains,
        hits,
        places_of,
        placer,
    )
    sent, arrived_cot = together(sent, arrived_cot)

    sent = to_owners(sent.reshape(experts, SLOTS, width + 128)).reshape(slots, width + 128)
    mine = core.reshape(1)
    expert_out, hidden, out_grad, factor, other_factor = expert_call(
        forward_kernel,
        mine,
        [sent, arrived_cot.reshape(slots, width)],
        expert_weights,
        [(width, bf16), (columns, bf16), (width, bf16), (columns, f32), (columns, f32)],
    )
    expert_out, factor = together(expert_out, factor)

    returned = to_owners(expert_out.reshape(experts, SLOTS, width))
    rows_grad, gate_grad, up_grad = expert_call(
        backward_kernel,
        mine,
        [out_grad, factor, other_factor],
        expert_weights,
        [(width, bf16), (columns, bf16), (columns, bf16)],
    )
    expert_sums = expert_weights_grad(sent, out_grad, hidden, gate_grad, up_grad)
    returned, rows_grad, expert_sums = together(returned, rows_grad, expert_sums)

    expert_sums = lax.psum_scatter(expert_sums, RING, scatter_dimension=1, tiled=True)
    home_grad = to_owners(rows_grad.reshape(experts, SLOTS, width))
    output, moe_part, router_grad = call(
        combine_kernel,
        [((rows, width), bf16), ((rows, width), f32), ((width, 128), f32)],
        midway,
        gate_parts,
        returned.reshape(slots, width),
        cot,
        hits,
        places_of,
        gates,
        small,
        moe_low,
    )
    home_grad, moe_part = together(home_grad, moe_part)
    midway_grad, branch_low, gain_two_grad = call(
        home_kernel,
        [((rows, width), f32), ((rows, width), bf16), ((8, width), f32)],
        placer_t,
        home_grad.reshape(slots, width),
        moe_part,
        midway,
        cot,
        moe_gains,
    )
    branch, *out_w_grad = call(
        out_grad_kernel,
        [((2 * rows, width), bf16)] + [((2, qw // 4, width // 2), bf16)] * 4,
        mixed_back,
        branch_low,
        partner(branch_low),
    )
    branch, out_w_grad = together(branch, out_w_grad)
    out_w_grad = added(back_along_x(out_w_grad))

    dq, dkv, *q_w_grad = call(
        functools.partial(attend_back_kernel, **sizes),
        [((2 * rows, qw), bf16), ((8, 2 * rows, 2 * HD), bf16)]
        + [((plane_rows, qw), bf16)] * 4,
        branch,
        wo,
        level_order,
        queries,
        kv_low,
        kv_up,
        logs,
        q_place,
        low_place,
        up_place,
        cosines,
        sines,
        normed,
        scratch=[
            pltpu.VMEM((2 * rows, qw), bf16),
            pltpu.VMEM((2 * HD, keys), f32),
            pltpu.VMEM((2 * HD, keys), f32),
        ],
    )
    dkv = exchange(dkv, RING)
    q_w_grad = back_along_x(q_w_grad)
    (small_grad,) = call(
        small_grad_kernel, [((width, 128), f32)], order, router_grad, gain_two_grad, dq
    )
    dkv, out_w_grad, small_grad, q_w_grad[1], q_w_grad[3] = together(
        dkv, out_w_grad, small_grad, q_w_grad[1], q_w_grad[3]
    )

    dkv, normed_own, normed_other = call(
        sum_kernel,
        [((2 * rows, 2 * HD), bf16), ((rows, width), f32), ((rows, width), f32)],
        dq,
        cosines,
        sines,
        *w_q,
        *w_kvs,
        dkv,
    )
    input_grad, *kvs_grad = call(
        input_kernel,
        [((rows, width), f32)] + [((plane_rows, 3 * HD), bf16)] * 4,
        both,
        normed_own,
        partner(normed_other),
        midway_grad,
        gains,
        order,
        small_grad,
        normed,
        dkv,
    )
    kvs_grad, out_w_grad, input_grad = together(kvs_grad, out_w_grad, input_grad)

    out_w_grad = exchange(out_w_grad.reshape(16, piece_rows, width // 2), OUT_PLANE)
    kvs_grad = back_along_x(kvs_grad)
    (plane_grad,) = call(
        add_both_kernel, [((plane_rows, qw + 3 * HD), bf16)], *q_w_grad, *kvs_grad, cost=LONG
    )
    plane_grad, out_w_grad = together(plane_grad, out_w_grad)
    plane_grad = exchange(plane_grad.reshape(16, piece_rows, qw + 3 * HD), PLANE)

    def summed(pieces):
        return jnp.sum(pieces.astype(f32), axis=0)

    def expert_shards(grad):
        count = grad.shape[1] // 2
        kept = lax.dynamic_slice_in_dim(grad, core * count, count, axis=1)
        given = partner(lax.dynamic_slice_in_dim(grad, (1 - core) * count, count, axis=1))
        both = jnp.stack([pick(core, kept, given), pick(core, given, kept)], axis=1)
        return [both[i : i + 1].astype(f32) for i in range(3)]

    out_w_grad = scatter_pieces(
        summed(out_w_grad), yhi, yhi, ("ylo", "core", "yhi"), OUT_SAME, OUT_OTHER
    )
    w_gate_grad, w_up_grad, w_down_grad = expert_shards(expert_sums)
    plane_grad, out_w_grad, w_gate_grad, w_up_grad, w_down_grad = together(
        plane_grad, out_w_grad, w_gate_grad, w_up_grad, w_down_grad
    )
    plane_grad = scatter_pieces(summed(plane_grad), yhi, core, ("core", "yhi"), SAME, OTHER)
    plane_grad = plane_grad.reshape(shard, 2, -1)

    def joined(first, last):
        return plane_grad[:, :, first:last].reshape(1, shard, -1)

    small_grad = jnp.sum(plane_grad[None, :, :, qw + 2 * HD :], axis=2)

    return (
        output[None],
        input_grad[None],
        small_grad[:, :, experts],
        small_grad[:, :, experts + 1],
        joined(0, qw),
        joined(qw, qw + HD),
        joined(qw + HD, qw + 2 * HD),
        out_w_grad[None],
        small_grad[:, :, :experts],
        w_gate_grad,
        w_up_grad,
        w_down_grad,
    )


def solution(mesh):
    fine = Mesh(mesh.devices.reshape(2, 4, 2, 4, 2), AXES)
    seq = P(FSDP, CTX, None)
    vector = P(None, AXES)
    matrix = P(None, AXES, None)
    expert = P(None, FSDP, CTX, None)
    in_specs = (
        seq,
        seq,
        P(),
        P(None, FSDP, CTX, None),
        vector,
        vector,
        matrix,
        matrix,
        matrix,
        matrix,
        matrix,
        expert,
        expert,
        expert,
    )
    out_specs = (
        seq,
        seq,
        vector,
        vector,
        matrix,
        matrix,
        matrix,
        matrix,
        matrix,
        expert,
        expert,
        expert,
    )
    return jax.shard_map(body, mesh=fine, in_specs=in_specs, out_specs=out_specs, check_vma=False)
```

```python
import functools
import math

import jax
import jax.numpy as jnp
from jax import lax
from jax.experimental import pallas as pl
from jax.experimental.pallas import tpu as pltpu
from jax.sharding import Mesh
from jax.sharding import PartitionSpec as P

H = 12
KVH = 2
HD = 128
TOPK = 4

EPSILON = 1e-06
ROPE_BASE = 1000000.0
NEGATIVE = -1e30

AXES = ("ylo", "z", "core", "x", "yhi")
CTX = ("ylo", "z", "core")
FSDP = ("x", "yhi")
GROUPS = [
    [
        (((group ^ yhi) * 4 + z) * 2 + core) * 8 + x * 2 + yhi
        for x in range(4)
        for yhi in range(2)
        for core in range(2)
    ]
    for group in range(2)
    for z in range(4)
]
RING = ("ylo", "z")
PLANE = ("ylo", "z", "yhi")
OUT_PLANE = ("yhi", "z", "ylo")
GROUPS = [
    [
        (((group ^ yhi) * 4 + z) * 2 + core) * 8 + x * 2 + yhi
        for x in range(4)
        for yhi in range(2)
        for core in range(2)
    ]
    for group in range(2)
    for z in range(4)
]
RING = ("ylo", "z")
ROWS_ORDER = ("ylo", "z", "yhi", "x")
OUT_ORDER = ("yhi", "z", "ylo", "x")
SLOTS = 40

bf16 = jnp.bfloat16
f32 = jnp.float32


def dot(left, right):
    return jnp.dot(left, right, preferred_element_type=f32)


def dot_t(left, right):
    return lax.dot_general(left, right, (((1,), (1,)), ((), ())), preferred_element_type=f32)


def t_dot(left, right):
    return lax.dot_general(left, right, (((0,), (0,)), ((), ())), preferred_element_type=f32)


def exchange(pieces, axes):
    return lax.all_to_all(pieces, axes, split_axis=0, concat_axis=0, tiled=True)


def to_owners(pieces):
    return lax.all_to_all(
        pieces, AXES, split_axis=0, concat_axis=0, axis_index_groups=GROUPS, tiled=True
    )


def spread(piece, count, axes):
    return exchange(jnp.broadcast_to(piece[None], (count,) + piece.shape), axes)


def after(value, earlier):
    return lax.optimization_barrier((value, earlier))[0]


def together(*values):
    return lax.optimization_barrier(values)


def partner(value):
    return lax.ppermute(value, "core", [(0, 1), (1, 0)])


def route(axes, sizes, move):
    pairs = []
    for source in range(math.prod(sizes)):
        rest, at = source, []
        for size in reversed(sizes):
            at.insert(0, rest % size)
            rest //= size
        target = 0
        for size, value in zip(sizes, move(*at)):
            target = target * size + value
        pairs.append((source, target))
    return pairs


SAME = route(("core", "yhi"), (2, 2), lambda c, h: (h, c))
OTHER = route(("core", "yhi"), (2, 2), lambda c, h: (1 - h, c))
OUT_SAME = route(("ylo", "core", "yhi"), (2, 2, 2), lambda j, c, h: (c, j, h))
OUT_OTHER = route(("ylo", "core", "yhi"), (2, 2, 2), lambda j, c, h: (c, j, 1 - h))


def back(pairs):
    return [(target, source) for source, target in pairs]


def pick(flag, if_zero, if_one):
    return jnp.where(flag == 0, if_zero, if_one)


def gather_pieces(pair, flag, key, axes, same, other):
    first = lax.ppermute(pick(flag, pair[0], pair[1]), axes, same)
    second = lax.ppermute(pick(flag, pair[1], pair[0]), axes, other)
    return pick(
        key, jnp.concatenate([first, second]), jnp.concatenate([second, first])
    )


def scatter_pieces(piece, flag, key, axes, same, other):
    count = piece.shape[0] // 2
    mine, rest = piece[:count], piece[count:]
    first = lax.ppermute(pick(key, mine, rest), axes, back(same))
    second = lax.ppermute(pick(key, rest, mine), axes, back(other))
    return pick(flag, jnp.concatenate([first, second], axis=-1), jnp.concatenate([second, first], axis=-1))


def along(axis, piece):
    return [piece] + [
        lax.ppermute(piece, axis, [(i, (i + s) % 4) for i in range(4)]) for s in (1, 2, 3)
    ]


def back_along_x(blocks):
    return [blocks[0]] + [
        lax.ppermute(blocks[s], "x", [(i, (i - s) % 4) for i in range(4)]) for s in (1, 2, 3)
    ]


def added(blocks):
    (total,) = call(add_kernel, [(blocks[0].shape, bf16)], *blocks, cost=LONG)
    return total


def sum_of(first, second, third, fourth):
    return (
        (first[...].astype(f32) + second[...].astype(f32))
        + (third[...].astype(f32) + fourth[...].astype(f32))
    ).astype(bf16)


def add_kernel(first, second, third, fourth, total):
    total[...] = sum_of(first, second, third, fourth)


def add_both_kernel(*refs):
    total = refs[8]
    count = refs[0].shape[1]
    total[:, :count] = sum_of(*refs[:4])
    total[:, count:] = sum_of(*refs[4:8])


def order_matrix(groups, x):
    index = jnp.arange(groups * 96, dtype=jnp.int32)
    turn_of, group, row = index // (groups * 24), index // 24 % groups, index % 24
    own = group * 96 + (x - turn_of) % 4 * 24 + row
    return (index[:, None] == own[None, :]).astype(bf16)


def places(pair_of, ctx, row_count, ctx_count):
    half_size = row_count // 2
    pair = jnp.sum(
        jnp.where(ctx[:, None] == jnp.arange(ctx_count, dtype=jnp.int32)[None], pair_of[None], 0),
        axis=1,
    )
    block = jnp.stack([pair, 2 * ctx_count - 1 - pair], axis=1)
    return block[:, :, None] * half_size + jnp.arange(half_size, dtype=jnp.int32)[None, None]


def in_three(value):
    high = value.astype(bf16)
    rest = value - high.astype(f32)
    middle = rest.astype(bf16)
    return [high, middle, (rest - middle.astype(f32)).astype(bf16)]


def call(kernel, outs, *args, scratch=(), cost=None):
    def whole(shape):
        return pl.BlockSpec(shape, lambda i: (0,) * len(shape))

    return pl.pallas_call(
        kernel,
        out_shape=[jax.ShapeDtypeStruct(shape, dtype) for shape, dtype in outs],
        grid=(1,),
        in_specs=[whole(a.shape) for a in args],
        out_specs=[whole(shape) for shape, _ in outs],
        scratch_shapes=list(scratch),
        compiler_params=pltpu.CompilerParams(vmem_limit_bytes=ROOM),
        cost_estimate=COST if cost is None else cost,
    )(*args)


ROOM = 58 << 20
COST = pl.CostEstimate(flops=1 << 20, bytes_accessed=1 << 18, transcendentals=0)
LONG = pl.CostEstimate(flops=1 << 35, bytes_accessed=1 << 27, transcendentals=0)
WIDE = 2 * HD
EXPERTS = 16


def turn(vectors, cosines, sines):
    return vectors * cosines + pltpu.roll(vectors, HD // 2, axis=1) * sines


def gain_picker():
    row = lax.broadcasted_iota(jnp.int32, (8, 128), 0)
    column = lax.broadcasted_iota(jnp.int32, (8, 128), 1)
    return jnp.where((column == row + EXPERTS) & (row < 2), 1.0, 0.0).astype(bf16)


def normal_of(stream):
    inverse = lax.rsqrt(jnp.mean(stream * stream, axis=-1, keepdims=True) + EPSILON)
    return stream * inverse, inverse


def norm_back(grad, normal, inverse, gain):
    scaled = grad * gain
    return inverse * (scaled - normal * jnp.mean(scaled * normal, axis=-1, keepdims=True))


def column_block(s, count):
    return slice(s * count, (s + 1) * count)


def order_kernel(rows, order, out):
    out[...] = dot(rows[...], order[...]).astype(bf16)


def keys_kernel(both, cosines, sines, *refs):
    kvs, (normed, key_value, gains) = refs[:4], refs[4:]
    count = kvs[0].shape[0]
    for s in range(4):
        gains[:, column_block(s, count)] = dot_t(gain_picker(), kvs[s][:, WIDE:])
    normal, _ = normal_of(both[...].astype(f32))
    normed[...] = (normal * gains[0:1]).astype(bf16)
    kv = dot(normed[:, column_block(0, count)], kvs[0][:, :WIDE])
    for s in range(1, 4):
        kv = kv + dot(normed[:, column_block(s, count)], kvs[s][:, :WIDE])
    keys = turn(kv[:, :HD], cosines[...], sines[...]).astype(bf16)
    values = kv[:, HD:].astype(bf16)
    for i in range(key_value.shape[0]):
        key_value[i, :, :HD] = keys
        key_value[i, :, HD:] = values


def small_kernel(order, kvs0, kvs1, kvs2, kvs3, small, gains):
    count = kvs0.shape[0]
    total = jnp.zeros(small.shape, f32)
    for s, kvs in enumerate((kvs0, kvs1, kvs2, kvs3)):
        total = total + dot(order[:, column_block(s, count)], kvs[:, WIDE:])
    small[...] = total.astype(bf16)
    gains[...] = dot_t(gain_picker(), small[...])


def query_kernel(normed, cosines, sines, w_q0, w_q1, w_q2, w_q3, queries):
    w_q = (w_q0, w_q1, w_q2, w_q3)
    count = w_q0.shape[0]
    for h in range(queries.shape[1] // HD):
        at = column_block(h, HD)
        q = dot(normed[:, column_block(0, count)], w_q0[:, at])
        for s in range(1, 4):
            q = q + dot(normed[:, column_block(s, count)], w_q[s][:, at])
        queries[:, at] = turn(q, cosines[...], sines[...]).astype(bf16)


def attend_kernel(
    queries,
    q_place,
    low_place,
    up_place,
    order,
    kv,
    ordered,
    logs,
    kv_low,
    kv_up,
    mixed,
    *,
    scale,
    pieces,
    heads,
):
    half = kv.shape[1] // 2
    for i in range(pieces):
        kv_low[i * half : (i + 1) * half, :] = kv[i, :half]
        kv_up[i * half : (i + 1) * half, :] = kv[i, half:]
    allowed_low = low_place[...] <= q_place[...]
    allowed_up = up_place[...] <= q_place[half:, :]
    for h in range(heads):
        at = slice(h * HD, (h + 1) * HD)
        q = queries[:, at]
        low = jnp.where(allowed_low, dot_t(q, kv_low[:, :HD]) * scale, NEGATIVE)
        up = jnp.where(allowed_up, dot_t(q[half:], kv_up[:, :HD]) * scale, NEGATIVE)
        first, second = low[:half], low[half:]
        top = jnp.max(first, axis=-1, keepdims=True)
        weight = jnp.exp(first - top)
        total = jnp.sum(weight, axis=-1, keepdims=True)
        probs = (weight / total).astype(bf16)
        mixed[:half, at] = dot(probs, kv_low[:, HD:]).astype(bf16)
        logs[h, :half, :] = top + jnp.log(total)
        top = jnp.maximum(
            jnp.max(second, axis=-1, keepdims=True), jnp.max(up, axis=-1, keepdims=True)
        )
        weight, weight_up = jnp.exp(second - top), jnp.exp(up - top)
        total = jnp.sum(weight, axis=-1, keepdims=True) + jnp.sum(
            weight_up, axis=-1, keepdims=True
        )
        mixed[half:, at] = (
            dot((weight / total).astype(bf16), kv_low[:, HD:])
            + dot((weight_up / total).astype(bf16), kv_up[:, HD:])
        ).astype(bf16)
        logs[h, half:, :] = top + jnp.log(total)
    ordered[...] = dot(mixed[...], order[...]).astype(bf16)


def branch_kernel(mixed, w_out0, w_out1, w_out2, w_out3, own, other, w_out):
    quarter = mixed.shape[0] // 4
    count, columns = w_out0.shape[1:]
    for s, part in enumerate((w_out0, w_out1, w_out2, w_out3)):
        w_out[:, column_block(s, count)] = part[...]
    for k in range(2):
        part = dot(mixed[...], w_out[k])
        at = slice(k * columns, (k + 1) * columns)
        own[:quarter, at] = part[:quarter]
        other[:quarter, at] = part[quarter : 2 * quarter]
        own[quarter:, at] = part[2 * quarter : 3 * quarter]
        other[quarter:, at] = part[3 * quarter :]


def route_kernel(
    tokens,
    own,
    received,
    small,
    gains,
    hits,
    places_of,
    placer,
    sent,
    midway,
    moe_low,
    gates,
    parts,
):
    middle = tokens[...].astype(f32) + (own[...] + received[...])
    midway[...] = middle
    normal, _ = normal_of(middle)
    moe = (normal * gains[1:2]).astype(bf16)
    moe_low[...] = moe
    sent[:, : moe.shape[1]] = dot(placer[...], moe).astype(bf16)
    logits = dot(moe, small[...])
    picked = [
        jnp.sum(hits[k].astype(f32) * logits, axis=-1, keepdims=True) for k in range(TOPK)
    ]
    top = picked[0]
    for value in picked[1:]:
        top = jnp.maximum(top, value)
    weights = [jnp.exp(value - top) for value in picked]
    total = weights[0]
    for value in weights[1:]:
        total = total + value
    lane = lax.broadcasted_iota(jnp.int32, gates.shape, 1)
    gate_at = jnp.zeros(places_of.shape[1:], f32)
    kept = jnp.zeros(gates.shape, f32)
    for k in range(TOPK):
        gate = weights[k] / total
        kept = jnp.where(lane == k, gate, kept)
        gate_at = gate_at + places_of[k].astype(f32) * gate
    gates[...] = kept
    block = jnp.zeros((sent.shape[0], 128), f32)
    for i, part in enumerate(in_three(gate_at)):
        parts[i] = part
        block = block + t_dot(part, jnp.where(lane == i, 1.0, 0.0).astype(bf16))
    sent[:, moe.shape[1] :] = block.astype(bf16)


def fetched(core, weights, held, sems, first):
    copies = [
        pltpu.make_async_copy(weights.at[m, core[0]], held.at[m], sems.at[m]) for m in range(3)
    ]
    for m in first:
        copies[m].start()

    def ready(m):
        copies[m].wait()
        return held[m]

    return ready


def forward_kernel(
    core, sent, cot, weights, out, hidden, out_grad, factor, other_factor, gate_grads, held, sems
):
    ready = fetched(core, weights, held, sems, (0, 1, 2))
    width = out.shape[1]
    gates = jnp.sum(sent[:, width:].astype(f32), axis=-1, keepdims=True)
    out_grad[...] = (gates * cot[...].astype(f32)).astype(bf16)
    rows = sent[:, :width]
    gate_pre = dot(rows, ready(0))
    up_pre = dot(rows, ready(1))
    sigmoid = 1.0 / (1.0 + jnp.exp(-gate_pre))
    silu = gate_pre * sigmoid
    low = (silu * up_pre).astype(bf16)
    hidden[...] = low
    result = dot_t(low, ready(2)).astype(bf16)
    out[...] = result
    grads = in_three(
        jnp.sum(cot[...].astype(f32) * result.astype(f32), axis=-1, keepdims=True)
    )
    lane = lax.broadcasted_iota(jnp.int32, gate_grads.shape, 1)
    block = jnp.zeros(gate_grads.shape, f32)
    for i, part in enumerate(grads):
        block = jnp.where(lane == i, part.astype(f32), block)
    gate_grads[...] = block.astype(bf16)
    factor[...] = up_pre * sigmoid * (1.0 + gate_pre * (1.0 - sigmoid))
    other_factor[...] = silu


def backward_kernel(
    core,
    out_grad,
    factor,
    other_factor,
    gate_grads,
    weights,
    rows_grad,
    gate_grad,
    up_grad,
    held,
    sems,
):
    width = out_grad.shape[1]
    ready = fetched(core, weights, held, sems, (2, 0, 1))
    hidden_grad = dot(out_grad[...], ready(2))
    low = (hidden_grad * factor[...]).astype(bf16)
    other = (hidden_grad * other_factor[...]).astype(bf16)
    gate_grad[...] = low
    up_grad[...] = other
    rows_grad[:, :width] = (dot_t(low, ready(0)) + dot_t(other, ready(1))).astype(bf16)
    rows_grad[:, width:] = gate_grads[...]


def expert_call(kernel, core, arrays, weights, outs):
    rows = arrays[0].shape[0]

    def whole(columns):
        return pl.BlockSpec((rows, columns), lambda i, core: (0, 0))

    return pl.pallas_call(
        kernel,
        out_shape=[jax.ShapeDtypeStruct((rows, columns), dtype) for columns, dtype in outs],
        grid_spec=pltpu.PrefetchScalarGridSpec(
            num_scalar_prefetch=1,
            grid=(1,),
            in_specs=[whole(a.shape[1]) for a in arrays] + [pl.BlockSpec(memory_space=pltpu.HBM)],
            out_specs=[whole(columns) for columns, _ in outs],
            scratch_shapes=[
                pltpu.VMEM((3,) + weights.shape[2:], bf16),
                pltpu.SemaphoreType.DMA((3,)),
            ],
        ),
        compiler_params=pltpu.CompilerParams(vmem_limit_bytes=ROOM),
        cost_estimate=COST,
    )(core, *arrays, weights)


def weights_kernel(sent, out_grad, hidden, gate_grad, up_grad, sums):
    rows = sent[...]
    sums[0] = t_dot(rows, gate_grad[...]).astype(bf16)
    sums[1] = t_dot(rows, up_grad[...]).astype(bf16)
    sums[2] = t_dot(out_grad[...], hidden[...]).astype(bf16)


def expert_weights_grad(sent, out_grad, hidden, gate_grad, up_grad, block=256):
    count, width = out_grad.shape
    columns = hidden.shape[1]
    part = pl.BlockSpec((count, block), lambda i: (0, i))
    whole = pl.BlockSpec((count, columns), lambda i: (0, 0), pipeline_mode=pl.Buffered(1))
    return pl.pallas_call(
        weights_kernel,
        out_shape=jax.ShapeDtypeStruct((3, width, columns), bf16),
        grid=(width // block,),
        in_specs=[part, part, whole, whole, whole],
        out_specs=pl.BlockSpec((3, block, columns), lambda i: (0, i, 0)),
        compiler_params=pltpu.CompilerParams(vmem_limit_bytes=ROOM),
        cost_estimate=COST,
    )(sent, out_grad, hidden, gate_grad, up_grad)


def combine_kernel(midway, parts, returned, output):
    rows = returned[...]
    output[...] = (
        midway[...] + (dot(parts[0], rows) + (dot(parts[1], rows) + dot(parts[2], rows)))
    ).astype(bf16)


def home_kernel(
    placer_t,
    home,
    midway,
    cot,
    gains,
    hits,
    places_of,
    gates,
    small,
    moe_low,
    midway_grad,
    branch_low,
    gain_grad,
    router_grad,
):
    width = midway.shape[1]
    lane = lax.broadcasted_iota(jnp.int32, gates.shape, 1)
    gate, gate_grad = [], []
    mean = jnp.zeros((gates.shape[0], 1), f32)
    for k in range(TOPK):
        gate.append(jnp.sum(jnp.where(lane == k, gates[...], 0.0), axis=-1, keepdims=True))
        gate_grad.append(
            jnp.sum(dot(places_of[k], home[:, width:]), axis=-1, keepdims=True)
        )
        mean = mean + gate[k] * gate_grad[k]
    logit_grad = jnp.zeros(gates.shape, f32)
    for k in range(TOPK):
        logit_grad = logit_grad + hits[k].astype(f32) * (gate[k] * (gate_grad[k] - mean))
    logit_grad = logit_grad.astype(bf16)
    router_grad[...] = t_dot(moe_low[...], logit_grad)
    grad = dot(placer_t[...], home[:, :width]) + dot_t(logit_grad, small[...])
    normal, inverse = normal_of(midway[...])
    result = cot[...].astype(f32) + norm_back(grad, normal, inverse, gains[1:2])
    midway_grad[...] = result
    branch_low[...] = result.astype(bf16)
    gain_grad[...] = jnp.broadcast_to(
        jnp.sum(grad * normal, axis=0, keepdims=True), gain_grad.shape
    )


def out_grad_kernel(mixed, own, other, branch, *blocks):
    quarter = own.shape[0] // 2
    branch[:quarter] = own[:quarter]
    branch[quarter : 2 * quarter] = other[:quarter]
    branch[2 * quarter : 3 * quarter] = own[quarter:]
    branch[3 * quarter :] = other[quarter:]
    count, columns = blocks[0].shape[1:]
    for k in range(2):
        grad = t_dot(mixed[...], branch[:, column_block(k, columns)]).astype(bf16)
        for s in range(4):
            blocks[s][k] = grad[column_block(s, count)]


def attend_back_kernel(
    branch,
    w_out,
    order,
    queries,
    kv_low,
    kv_up,
    logs,
    q_place,
    low_place,
    up_place,
    cosines,
    sines,
    normed,
    dq,
    dkv,
    block0,
    block1,
    block2,
    block3,
    grads,
    acc_low,
    acc_up,
    *,
    scale,
    pieces,
    heads,
):
    half = queries.shape[0] // 2
    columns = w_out.shape[2]
    ordered = dot_t(branch[:, :columns], w_out[0]) + dot_t(branch[:, columns:], w_out[1])
    grads[...] = dot_t(ordered.astype(bf16), order[...]).astype(bf16)
    allowed_low = low_place[...] <= q_place[...]
    allowed_up = up_place[...] <= q_place[half:, :]
    key_low, value_low = kv_low[:, :HD], kv_low[:, HD:]
    key_up, value_up = kv_up[:, :HD], kv_up[:, HD:]
    for h in range(heads):
        at = slice(h * HD, (h + 1) * HD)
        q, grad, log = queries[:, at], grads[:, at], logs[h]
        low = jnp.where(allowed_low, dot_t(q, key_low) * scale, NEGATIVE)
        up = jnp.where(allowed_up, dot_t(q[half:], key_up) * scale, NEGATIVE)
        probs_low, probs_up = jnp.exp(low - log), jnp.exp(up - log[half:])
        grad_low, grad_up = dot_t(grad, value_low), dot_t(grad[half:], value_up)
        along = jnp.sum(probs_low * grad_low, axis=-1, keepdims=True)
        along_up = along[half:] + jnp.sum(probs_up * grad_up, axis=-1, keepdims=True)
        along = jnp.concatenate([along[:half], along_up])
        score_low = (probs_low * (grad_low - along)).astype(bf16)
        score_up = (probs_up * (grad_up - along_up)).astype(bf16)
        part = dot(score_low, key_low)
        part = jnp.concatenate([part[:half], part[half:] + dot(score_up, key_up)]) * scale
        dq[:, at] = turn(part, cosines[...], -sines[...]).astype(bf16)
        terms = (
            (acc_low, slice(0, HD), t_dot(q, score_low)),
            (acc_up, slice(0, HD), t_dot(q[half:], score_up)),
            (acc_low, slice(HD, 2 * HD), t_dot(grad, probs_low.astype(bf16))),
            (acc_up, slice(HD, 2 * HD), t_dot(grad[half:], probs_up.astype(bf16))),
        )
        for acc, rows, term in terms:
            if h == 0:
                acc[rows] = term
            else:
                acc[rows] += term
    for s, block in enumerate((block0, block1, block2, block3)):
        block[...] = t_dot(normed[:, column_block(s, block.shape[0])], dq[...]).astype(bf16)
    for acc, first in ((acc_low, 0), (acc_up, half)):
        dk = (acc[:HD].T * scale).astype(bf16)
        dv = acc[HD:].T.astype(bf16)
        for i in range(pieces):
            dkv[i, first : first + half, :HD] = dk[i * half : (i + 1) * half]
            dkv[i, first : first + half, HD:] = dv[i * half : (i + 1) * half]


def sum_kernel(dq, cosines, sines, *refs):
    w_q, kvs, (parts, dkv, own, other) = refs[:4], refs[4:8], refs[8:]
    total = jnp.sum(parts[...].astype(f32), axis=0)
    dkv[:, :HD] = turn(total[:, :HD], cosines[...], -sines[...]).astype(bf16)
    dkv[:, HD:] = total[:, HD:].astype(bf16)
    quarter = own.shape[0] // 2
    for s in range(4):
        grad = dot_t(dq[...], w_q[s][...]) + dot_t(dkv[...], kvs[s][:, :WIDE])
        at = column_block(s, w_q[s].shape[0])
        own[:quarter, at] = grad[:quarter]
        other[:quarter, at] = grad[quarter : 2 * quarter]
        own[quarter:, at] = grad[2 * quarter : 3 * quarter]
        other[quarter:, at] = grad[3 * quarter :]


def stack_kernel(gate, up, down, late, out):
    del late
    out[0] = gate[...]
    out[1] = up[...]
    out[2] = down[...]


def small_grad_kernel(order, router_grad, gain_grad, late, out):
    del late
    row = lax.broadcasted_iota(jnp.int32, gain_grad.shape, 0)
    second = jnp.where(row == 1, gain_grad[...], 0.0).astype(bf16)
    small = router_grad[...] + t_dot(second, gain_picker())
    out[...] = t_dot(order[...], small.astype(bf16))


def input_kernel(both, own, received, midway_grad, gains, order, small, normed, dkv, out, *blocks):
    grad = own[...] + received[...]
    quarter = own.shape[0] // 2
    tokens = jnp.concatenate([both[:quarter], both[2 * quarter : 3 * quarter]])
    normal, inverse = normal_of(tokens.astype(f32))
    parts = in_three(norm_back(grad, normal, inverse, gains[0:1]))
    moved = dot_t(jnp.concatenate(parts), order[...])
    count = 2 * quarter
    out[...] = midway_grad[...] + (
        moved[:count] + (moved[count : 2 * count] + moved[2 * count :])
    )
    gain_grad = jnp.sum(grad * normal, axis=0, keepdims=True)
    row = lax.broadcasted_iota(jnp.int32, gains.shape, 0)
    gain_grad = jnp.where(row == 0, gain_grad, 0.0).astype(bf16)
    small = small[...] + t_dot(gain_grad, gain_picker())
    rows = blocks[0].shape[0]
    for s, block in enumerate(blocks):
        at = column_block(s, rows)
        block[:, :WIDE] = t_dot(normed[:, at], dkv[...]).astype(bf16)
        block[:, WIDE:] = small[at].astype(bf16)


def body(
    tokens,
    cotangent,
    pair_of,
    routes,
    attn_gain,
    moe_gain,
    w_query,
    w_key,
    w_value,
    w_out,
    w_router,
    w_gate,
    w_up,
    w_down,
):
    rows = tokens.shape[1]
    half = rows // 2
    width = tokens.shape[2]
    shard = w_query.shape[1]
    ctx_count = 16
    experts = w_router.shape[2]
    columns = w_gate.shape[3]
    per_group = H // KVH
    qw = per_group * HD
    scale = 1.0 / math.sqrt(HD)
    core = lax.axis_index("core")
    ylo, z, yhi = lax.axis_index("ylo"), lax.axis_index("z"), lax.axis_index("yhi")
    x = lax.axis_index("x")
    piece_rows = 2 * shard
    slots = experts * SLOTS
    own_tokens, cot = tokens[0], cotangent[0]

    def halves(matrix):
        return [matrix[:, : matrix.shape[1] // 2], matrix[:, matrix.shape[1] // 2 :]]

    small = jnp.concatenate([w_router[0], attn_gain[0][:, None], moe_gain[0][:, None]], axis=-1)
    small = jnp.pad(small, ((0, 0), (0, 128 - experts - 2)))
    query_halves, key_halves, value_halves = halves(w_query[0]), halves(w_key[0]), halves(w_value[0])
    pairs = [
        jnp.concatenate([k, v, small, q], axis=-1)
        for k, v, q in zip(key_halves, value_halves, query_halves)
    ]
    pieces = gather_pieces(pairs, yhi, core, ("core", "yhi"), SAME, OTHER)
    pieces, x, own_tokens, out_halves, pair_of = together(
        pieces, x, own_tokens, w_out[0], pair_of
    )

    plane_rows = 16 * piece_rows
    plane = spread(pieces, 16, PLANE)
    other_tokens = partner(own_tokens)
    both = jnp.concatenate(
        [own_tokens[:half], other_tokens[:half], own_tokens[half:], other_tokens[half:]]
    )
    out_pieces = gather_pieces(
        halves(out_halves), yhi, yhi, ("ylo", "core", "yhi"), OUT_SAME, OUT_OTHER
    )
    order, out_order = order_matrix(16, x), order_matrix(8, x)
    (expert_shards_in,) = call(
        stack_kernel, [((3,) + w_gate.shape[1:], bf16)], w_gate[0], w_up[0], w_down[0], both
    )
    plane, both, out_pieces, order, out_order, pair_of, expert_shards_in, chosen = together(
        plane, both, out_pieces, order, out_order, pair_of, expert_shards_in, routes[0, 0]
    )

    plane = plane.reshape(plane_rows, -1)
    w_kvs = along("x", plane[:, : 3 * HD])
    wo = spread(out_pieces, 16, OUT_PLANE)
    (both,) = call(order_kernel, [((2 * rows, width), bf16)], both, order)

    def two_cores(ctx):
        return jnp.stack([ctx + core, ctx + 1 - core], axis=-1).reshape(-1)

    ctx_here = (ylo * 4 + z) * 2
    q_place = places(pair_of, two_cores(ctx_here), rows, ctx_count)
    q_place = q_place.transpose(1, 0, 2).reshape(2 * rows, 1)
    key_place = places(
        pair_of, two_cores(jnp.arange(8, dtype=jnp.int32) * 2), rows, ctx_count
    )
    low_place, up_place = key_place[:, 0].reshape(1, -1), key_place[:, 1].reshape(1, -1)
    frequency = jnp.exp(jnp.arange(HD // 2, dtype=f32) * (-2.0 * math.log(ROPE_BASE) / HD))
    angles = q_place.astype(f32) * frequency[None, :]
    cosines, sines = jnp.cos(angles), jnp.sin(angles)
    cosines = jnp.concatenate([cosines, cosines], axis=-1)
    sines = jnp.concatenate([-sines, sines], axis=-1)
    w_q, w_kvs, wo, both, q_place, low_place, up_place, cosines, sines, chosen = together(
        plane[:, 3 * HD :], w_kvs, wo, both, q_place, low_place, up_place, cosines, sines, chosen
    )

    w_q = along("x", w_q)
    normed, key_value, gains = call(
        keys_kernel,
        [((2 * rows, width), bf16), ((8, 2 * rows, 2 * HD), bf16), ((8, width), f32)],
        both,
        cosines,
        sines,
        *w_kvs,
    )
    all_kv = exchange(key_value, RING)
    small, moe_gains = call(
        small_kernel, [((width, 128), bf16), ((8, width), f32)], order, *w_kvs
    )
    (queries,) = call(
        query_kernel, [((2 * rows, qw), bf16)], normed, cosines, sines, *w_q, cost=LONG
    )
    lanes = jnp.arange(128, dtype=jnp.int32)
    hits = (chosen.T[:, :, None] == lanes[None, None, :]).astype(bf16)
    earlier = (lanes[:, None] > lanes[None, :]).astype(bf16)
    before = dot(earlier, jnp.sum(hits, axis=0))
    slot_index = jnp.sum(hits.astype(f32) * before[None], axis=-1).astype(jnp.int32)
    target = chosen.T * SLOTS + slot_index
    slot_row = jnp.arange(slots, dtype=jnp.int32)
    places_of = (target[:, :, None] == slot_row[None, None, :]).astype(bf16)
    placer_t = jnp.sum(places_of, axis=0)
    placer = placer_t.T
    (cot_rows,) = call(order_kernel, [((slots, width), bf16)], placer, cot)
    (
        queries, all_kv, expert_shards_in, small, moe_gains, cot_rows,
        hits, places_of, placer_t, placer,
    ) = together(
        queries, all_kv, expert_shards_in, small, moe_gains, cot_rows,
        hits, places_of, placer_t, placer,
    )
    wo = along("x", wo.reshape(2, qw // 4, width // 2))
    expert_weights = lax.all_gather(expert_shards_in, CTX, axis=2, tiled=True)

    arrived_cot = to_owners(cot_rows.reshape(experts, SLOTS, width))
    sizes = dict(scale=scale, pieces=8, heads=per_group)
    keys = 8 * rows
    mixed, logs, kv_low, kv_up = call(
        functools.partial(attend_kernel, **sizes),
        [
            ((2 * rows, qw), bf16),
            ((per_group, 2 * rows, 1), f32),
            ((keys, 2 * HD), bf16),
            ((keys, 2 * HD), bf16),
        ],
        queries,
        q_place,
        low_place,
        up_place,
        out_order,
        all_kv,
        scratch=[pltpu.VMEM((2 * rows, qw), bf16)],
    )
    wo, mixed = together(wo, mixed)

    branch_own, branch_other, wo = call(
        branch_kernel,
        [((rows, width), f32), ((rows, width), f32), ((2, qw, width // 2), bf16)],
        mixed,
        *wo,
    )
    sent, midway, moe_low, gates, gate_parts = call(
        route_kernel,
        [
            ((slots, width + 128), bf16),
            ((rows, width), f32),
            ((rows, width), bf16),
            ((rows, 128), f32),
            ((3, rows, slots), bf16),
        ],
        own_tokens,
        branch_own,
        partner(branch_other),
        small,
        moe_gains,
        hits,
        places_of,
        placer,
    )
    sent, arrived_cot = together(sent, arrived_cot)

    sent = to_owners(sent.reshape(experts, SLOTS, width + 128)).reshape(slots, width + 128)
    mine = core.reshape(1)
    expert_out, hidden, out_grad, factor, other_factor, gate_grads = expert_call(
        forward_kernel,
        mine,
        [sent, arrived_cot.reshape(slots, width)],
        expert_weights,
        [
            (width, bf16),
            (columns, bf16),
            (width, bf16),
            (columns, f32),
            (columns, f32),
            (128, bf16),
        ],
    )
    rows_grad, gate_grad, up_grad = expert_call(
        backward_kernel,
        mine,
        [out_grad, factor, other_factor, gate_grads],
        expert_weights,
        [(width + 128, bf16), (columns, bf16), (columns, bf16)],
    )
    rows_grad, gate_grad, up_grad = together(rows_grad, gate_grad, up_grad)

    home_grad = to_owners(rows_grad.reshape(experts, SLOTS, width + 128))
    expert_sums = expert_weights_grad(sent, out_grad, hidden, gate_grad, up_grad)
    home_grad, expert_sums, expert_out = together(home_grad, expert_sums, expert_out)
    expert_sums = lax.psum_scatter(expert_sums, RING, scatter_dimension=1, tiled=True)

    returned = to_owners(expert_out.reshape(experts, SLOTS, width))
    midway_grad, branch_low, gain_two_grad, router_grad = call(
        home_kernel,
        [((rows, width), f32), ((rows, width), bf16), ((8, width), f32), ((width, 128), f32)],
        placer_t,
        home_grad.reshape(slots, width + 128),
        midway,
        cot,
        moe_gains,
        hits,
        places_of,
        gates,
        small,
        moe_low,
    )
    branch, *out_w_grad = call(
        out_grad_kernel,
        [((2 * rows, width), bf16)] + [((2, qw // 4, width // 2), bf16)] * 4,
        mixed,
        branch_low,
        partner(branch_low),
    )
    branch, out_w_grad = together(branch, out_w_grad)
    out_w_grad = added(back_along_x(out_w_grad))

    dq, dkv, *q_w_grad = call(
        functools.partial(attend_back_kernel, **sizes),
        [((2 * rows, qw), bf16), ((8, 2 * rows, 2 * HD), bf16)]
        + [((plane_rows, qw), bf16)] * 4,
        branch,
        wo,
        out_order,
        queries,
        kv_low,
        kv_up,
        logs,
        q_place,
        low_place,
        up_place,
        cosines,
        sines,
        normed,
        scratch=[
            pltpu.VMEM((2 * rows, qw), bf16),
            pltpu.VMEM((2 * HD, keys), f32),
            pltpu.VMEM((2 * HD, keys), f32),
        ],
    )
    dkv, q_w_grad, returned = together(dkv, q_w_grad, returned)

    dkv = exchange(dkv, RING)
    q_w_grad = back_along_x(q_w_grad)
    (output,) = call(
        combine_kernel,
        [((rows, width), bf16)],
        midway,
        gate_parts,
        returned.reshape(slots, width),
    )
    (small_grad,) = call(
        small_grad_kernel, [((width, 128), f32)], order, router_grad, gain_two_grad, dq
    )
    dkv, out_w_grad, small_grad, output, q_w_grad[1], q_w_grad[3] = together(
        dkv, out_w_grad, small_grad, output, q_w_grad[1], q_w_grad[3]
    )

    dkv, normed_own, normed_other = call(
        sum_kernel,
        [((2 * rows, 2 * HD), bf16), ((rows, width), f32), ((rows, width), f32)],
        dq,
        cosines,
        sines,
        *w_q,
        *w_kvs,
        dkv,
    )
    input_grad, *kvs_grad = call(
        input_kernel,
        [((rows, width), f32)] + [((plane_rows, 3 * HD), bf16)] * 4,
        both,
        normed_own,
        partner(normed_other),
        midway_grad,
        gains,
        order,
        small_grad,
        normed,
        dkv,
    )
    kvs_grad, out_w_grad, input_grad = together(kvs_grad, out_w_grad, input_grad)

    out_w_grad = exchange(out_w_grad.reshape(16, piece_rows, width // 2), OUT_PLANE)
    kvs_grad = back_along_x(kvs_grad)
    (plane_grad,) = call(
        add_both_kernel, [((plane_rows, qw + 3 * HD), bf16)], *q_w_grad, *kvs_grad, cost=LONG
    )
    plane_grad, out_w_grad = together(plane_grad, out_w_grad)
    plane_grad = exchange(plane_grad.reshape(16, piece_rows, qw + 3 * HD), PLANE)

    def summed(pieces):
        return jnp.sum(pieces.astype(f32), axis=0)

    def expert_shards(grad):
        count = grad.shape[1] // 2
        kept = lax.dynamic_slice_in_dim(grad, core * count, count, axis=1)
        given = partner(lax.dynamic_slice_in_dim(grad, (1 - core) * count, count, axis=1))
        both = jnp.stack([pick(core, kept, given), pick(core, given, kept)], axis=1)
        return [both[i : i + 1].astype(f32) for i in range(3)]

    out_w_grad = scatter_pieces(
        summed(out_w_grad), yhi, yhi, ("ylo", "core", "yhi"), OUT_SAME, OUT_OTHER
    )
    w_gate_grad, w_up_grad, w_down_grad = expert_shards(expert_sums)
    plane_grad, out_w_grad, w_gate_grad, w_up_grad, w_down_grad = together(
        plane_grad, out_w_grad, w_gate_grad, w_up_grad, w_down_grad
    )
    plane_grad = scatter_pieces(summed(plane_grad), yhi, core, ("core", "yhi"), SAME, OTHER)
    plane_grad = plane_grad.reshape(shard, 2, -1)

    def joined(first, last):
        return plane_grad[:, :, first:last].reshape(1, shard, -1)

    small_grad = jnp.sum(plane_grad[None, :, :, qw + 2 * HD :], axis=2)

    return (
        output[None],
        input_grad[None],
        small_grad[:, :, experts],
        small_grad[:, :, experts + 1],
        joined(0, qw),
        joined(qw, qw + HD),
        joined(qw + HD, qw + 2 * HD),
        out_w_grad[None],
        small_grad[:, :, :experts],
        w_gate_grad,
        w_up_grad,
        w_down_grad,
    )


def solution(mesh):
    fine = Mesh(mesh.devices.reshape(2, 4, 2, 4, 2), AXES)
    seq = P(FSDP, CTX, None)
    vector = P(None, AXES)
    matrix = P(None, AXES, None)
    expert = P(None, FSDP, CTX, None)
    in_specs = (
        seq,
        seq,
        P(),
        P(None, FSDP, CTX, None),
        vector,
        vector,
        matrix,
        matrix,
        matrix,
        matrix,
        matrix,
        expert,
        expert,
        expert,
    )
    out_specs = (
        seq,
        seq,
        vector,
        vector,
        matrix,
        matrix,
        matrix,
        matrix,
        matrix,
        expert,
        expert,
        expert,
    )
    return jax.shard_map(body, mesh=fine, in_specs=in_specs, out_specs=out_specs, check_vma=False)
```

```python
import functools
import math

import jax
import jax.numpy as jnp
from jax import lax
from jax.experimental import pallas as pl
from jax.experimental.pallas import tpu as pltpu
from jax.sharding import Mesh
from jax.sharding import PartitionSpec as P

H = 12
KVH = 2
HD = 128
TOPK = 4

EPSILON = 1e-06
ROPE_BASE = 1000000.0
NEGATIVE = -1e30

AXES = ("ylo", "z", "core", "x", "yhi")
CTX = ("ylo", "z", "core")
FSDP = ("x", "yhi")
GROUPS = [
    [
        (((group ^ yhi) * 4 + z) * 2 + core) * 8 + x * 2 + yhi
        for x in range(4)
        for yhi in range(2)
        for core in range(2)
    ]
    for group in range(2)
    for z in range(4)
]
RING = ("ylo", "z")
PLANE = ("ylo", "z", "yhi")
OUT_PLANE = ("yhi", "z", "ylo")
LEVEL = ("yhi", "ylo", "x")
GROUPS = [
    [
        (((group ^ yhi) * 4 + z) * 2 + core) * 8 + x * 2 + yhi
        for x in range(4)
        for yhi in range(2)
        for core in range(2)
    ]
    for group in range(2)
    for z in range(4)
]
RING = ("ylo", "z")
ROWS_ORDER = ("ylo", "z", "yhi", "x")
OUT_ORDER = ("yhi", "z", "ylo", "x")
SLOTS = 40

bf16 = jnp.bfloat16
f32 = jnp.float32


def dot(left, right):
    return jnp.dot(left, right, preferred_element_type=f32)


def dot_t(left, right):
    return lax.dot_general(left, right, (((1,), (1,)), ((), ())), preferred_element_type=f32)


def t_dot(left, right):
    return lax.dot_general(left, right, (((0,), (0,)), ((), ())), preferred_element_type=f32)


def exchange(pieces, axes):
    return lax.all_to_all(pieces, axes, split_axis=0, concat_axis=0, tiled=True)


def to_owners(pieces):
    return lax.all_to_all(
        pieces, AXES, split_axis=0, concat_axis=0, axis_index_groups=GROUPS, tiled=True
    )


def spread(piece, count, axes):
    return exchange(jnp.broadcast_to(piece[None], (count,) + piece.shape), axes)


def after(value, earlier):
    return lax.optimization_barrier((value, earlier))[0]


def together(*values):
    return lax.optimization_barrier(values)


def partner(value):
    return lax.ppermute(value, "core", [(0, 1), (1, 0)])


def route(axes, sizes, move):
    pairs = []
    for source in range(math.prod(sizes)):
        rest, at = source, []
        for size in reversed(sizes):
            at.insert(0, rest % size)
            rest //= size
        target = 0
        for size, value in zip(sizes, move(*at)):
            target = target * size + value
        pairs.append((source, target))
    return pairs


SAME = route(("core", "yhi"), (2, 2), lambda c, h: (h, c))
OTHER = route(("core", "yhi"), (2, 2), lambda c, h: (1 - h, c))
OUT_SAME = route(("ylo", "core", "yhi"), (2, 2, 2), lambda j, c, h: (c, j, h))
OUT_OTHER = route(("ylo", "core", "yhi"), (2, 2, 2), lambda j, c, h: (c, j, 1 - h))


def back(pairs):
    return [(target, source) for source, target in pairs]


def pick(flag, if_zero, if_one):
    return jnp.where(flag == 0, if_zero, if_one)


def gather_pieces(pair, flag, key, axes, same, other):
    first = lax.ppermute(pick(flag, pair[0], pair[1]), axes, same)
    second = lax.ppermute(pick(flag, pair[1], pair[0]), axes, other)
    return pick(
        key, jnp.concatenate([first, second]), jnp.concatenate([second, first])
    )


def scatter_pieces(piece, flag, key, axes, same, other):
    count = piece.shape[0] // 2
    mine, rest = piece[:count], piece[count:]
    first = lax.ppermute(pick(key, mine, rest), axes, back(same))
    second = lax.ppermute(pick(key, rest, mine), axes, back(other))
    return pick(flag, jnp.concatenate([first, second], axis=-1), jnp.concatenate([second, first], axis=-1))


def along(axis, piece):
    return [piece] + [
        lax.ppermute(piece, axis, [(i, (i + s) % 4) for i in range(4)]) for s in (1, 2, 3)
    ]


def back_along_x(blocks):
    return [blocks[0]] + [
        lax.ppermute(blocks[s], "x", [(i, (i - s) % 4) for i in range(4)]) for s in (1, 2, 3)
    ]


def added(blocks):
    (total,) = call(add_kernel, [(blocks[0].shape, bf16)], *blocks, cost=LONG)
    return total


def sum_of(first, second, third, fourth):
    return (
        (first[...].astype(f32) + second[...].astype(f32))
        + (third[...].astype(f32) + fourth[...].astype(f32))
    ).astype(bf16)


def add_kernel(first, second, third, fourth, total):
    total[...] = sum_of(first, second, third, fourth)


def add_both_kernel(*refs):
    total = refs[8]
    count = refs[0].shape[1]
    total[:, :count] = sum_of(*refs[:4])
    total[:, count:] = sum_of(*refs[4:8])


def order_matrix(groups, x):
    index = jnp.arange(groups * 96, dtype=jnp.int32)
    turn_of, group, row = index // (groups * 24), index // 24 % groups, index % 24
    own = group * 96 + (x - turn_of) % 4 * 24 + row
    return (index[:, None] == own[None, :]).astype(bf16)


def level_order_matrix(z):
    index = jnp.arange(8 * 96, dtype=jnp.int32)
    own = (z - index // 192) % 4 * 192 + index % 192
    return (index[:, None] == own[None, :]).astype(bf16)


def places(pair_of, ctx, row_count, ctx_count):
    half_size = row_count // 2
    pair = jnp.sum(
        jnp.where(ctx[:, None] == jnp.arange(ctx_count, dtype=jnp.int32)[None], pair_of[None], 0),
        axis=1,
    )
    block = jnp.stack([pair, 2 * ctx_count - 1 - pair], axis=1)
    return block[:, :, None] * half_size + jnp.arange(half_size, dtype=jnp.int32)[None, None]


def in_three(value):
    high = value.astype(bf16)
    rest = value - high.astype(f32)
    middle = rest.astype(bf16)
    return [high, middle, (rest - middle.astype(f32)).astype(bf16)]


def call(kernel, outs, *args, scratch=(), cost=None):
    def whole(shape):
        return pl.BlockSpec(shape, lambda i: (0,) * len(shape))

    return pl.pallas_call(
        kernel,
        out_shape=[jax.ShapeDtypeStruct(shape, dtype) for shape, dtype in outs],
        grid=(1,),
        in_specs=[whole(a.shape) for a in args],
        out_specs=[whole(shape) for shape, _ in outs],
        scratch_shapes=list(scratch),
        compiler_params=pltpu.CompilerParams(vmem_limit_bytes=ROOM),
        cost_estimate=COST if cost is None else cost,
    )(*args)


ROOM = 58 << 20
COST = pl.CostEstimate(flops=1 << 20, bytes_accessed=1 << 18, transcendentals=0)
LONG = pl.CostEstimate(flops=1 << 35, bytes_accessed=1 << 27, transcendentals=0)
WIDE = 2 * HD
EXPERTS = 16


def turn(vectors, cosines, sines):
    return vectors * cosines + pltpu.roll(vectors, HD // 2, axis=1) * sines


def gain_picker():
    row = lax.broadcasted_iota(jnp.int32, (8, 128), 0)
    column = lax.broadcasted_iota(jnp.int32, (8, 128), 1)
    return jnp.where((column == row + EXPERTS) & (row < 2), 1.0, 0.0).astype(bf16)


def normal_of(stream):
    inverse = lax.rsqrt(jnp.mean(stream * stream, axis=-1, keepdims=True) + EPSILON)
    return stream * inverse, inverse


def norm_back(grad, normal, inverse, gain):
    scaled = grad * gain
    return inverse * (scaled - normal * jnp.mean(scaled * normal, axis=-1, keepdims=True))


def column_block(s, count):
    return slice(s * count, (s + 1) * count)


def order_kernel(rows, order, out):
    out[...] = dot(rows[...], order[...]).astype(bf16)


def keys_kernel(both, cosines, sines, *refs):
    kvs, (normed, key_value, gains) = refs[:4], refs[4:]
    count = kvs[0].shape[0]
    for s in range(4):
        gains[:, column_block(s, count)] = dot_t(gain_picker(), kvs[s][:, WIDE:])
    normal, _ = normal_of(both[...].astype(f32))
    normed[...] = (normal * gains[0:1]).astype(bf16)
    kv = dot(normed[:, column_block(0, count)], kvs[0][:, :WIDE])
    for s in range(1, 4):
        kv = kv + dot(normed[:, column_block(s, count)], kvs[s][:, :WIDE])
    keys = turn(kv[:, :HD], cosines[...], sines[...]).astype(bf16)
    values = kv[:, HD:].astype(bf16)
    for i in range(key_value.shape[0]):
        key_value[i, :, :HD] = keys
        key_value[i, :, HD:] = values


def small_kernel(order, kvs0, kvs1, kvs2, kvs3, small, gains):
    count = kvs0.shape[0]
    total = jnp.zeros(small.shape, f32)
    for s, kvs in enumerate((kvs0, kvs1, kvs2, kvs3)):
        total = total + dot(order[:, column_block(s, count)], kvs[:, WIDE:])
    small[...] = total.astype(bf16)
    gains[...] = dot_t(gain_picker(), small[...])


def query_kernel(normed, cosines, sines, w_q0, w_q1, w_q2, w_q3, queries):
    w_q = (w_q0, w_q1, w_q2, w_q3)
    count = w_q0.shape[0]
    for h in range(queries.shape[1] // HD):
        at = column_block(h, HD)
        q = dot(normed[:, column_block(0, count)], w_q0[:, at])
        for s in range(1, 4):
            q = q + dot(normed[:, column_block(s, count)], w_q[s][:, at])
        queries[:, at] = turn(q, cosines[...], sines[...]).astype(bf16)


def attend_kernel(
    queries,
    q_place,
    low_place,
    up_place,
    order,
    order_back,
    kv,
    ordered,
    ordered_back,
    logs,
    kv_low,
    kv_up,
    mixed,
    *,
    scale,
    pieces,
    heads,
):
    half = kv.shape[1] // 2
    for i in range(pieces):
        kv_low[i * half : (i + 1) * half, :] = kv[i, :half]
        kv_up[i * half : (i + 1) * half, :] = kv[i, half:]
    allowed_low = low_place[...] <= q_place[...]
    allowed_up = up_place[...] <= q_place[half:, :]
    for h in range(heads):
        at = slice(h * HD, (h + 1) * HD)
        q = queries[:, at]
        low = jnp.where(allowed_low, dot_t(q, kv_low[:, :HD]) * scale, NEGATIVE)
        up = jnp.where(allowed_up, dot_t(q[half:], kv_up[:, :HD]) * scale, NEGATIVE)
        first, second = low[:half], low[half:]
        top = jnp.max(first, axis=-1, keepdims=True)
        weight = jnp.exp(first - top)
        total = jnp.sum(weight, axis=-1, keepdims=True)
        probs = (weight / total).astype(bf16)
        mixed[:half, at] = dot(probs, kv_low[:, HD:]).astype(bf16)
        logs[h, :half, :] = top + jnp.log(total)
        top = jnp.maximum(
            jnp.max(second, axis=-1, keepdims=True), jnp.max(up, axis=-1, keepdims=True)
        )
        weight, weight_up = jnp.exp(second - top), jnp.exp(up - top)
        total = jnp.sum(weight, axis=-1, keepdims=True) + jnp.sum(
            weight_up, axis=-1, keepdims=True
        )
        mixed[half:, at] = (
            dot((weight / total).astype(bf16), kv_low[:, HD:])
            + dot((weight_up / total).astype(bf16), kv_up[:, HD:])
        ).astype(bf16)
        logs[h, half:, :] = top + jnp.log(total)
    ordered[...] = dot(mixed[...], order[...]).astype(bf16)
    ordered_back[...] = dot(mixed[...], order_back[...]).astype(bf16)


def branch_kernel(mixed, w_out0, w_out1, w_out2, w_out3, own, other, w_out):
    quarter = mixed.shape[0] // 4
    count, columns = w_out0.shape[1:]
    for s, part in enumerate((w_out0, w_out1, w_out2, w_out3)):
        w_out[:, column_block(s, count)] = part[...]
    for k in range(2):
        part = dot(mixed[...], w_out[k])
        at = slice(k * columns, (k + 1) * columns)
        own[:quarter, at] = part[:quarter]
        other[:quarter, at] = part[quarter : 2 * quarter]
        own[quarter:, at] = part[2 * quarter : 3 * quarter]
        other[quarter:, at] = part[3 * quarter :]


def route_kernel(
    tokens,
    own,
    received,
    small,
    gains,
    hits,
    places_of,
    placer,
    sent,
    midway,
    moe_low,
    gates,
    parts,
):
    middle = tokens[...].astype(f32) + (own[...] + received[...])
    midway[...] = middle
    normal, _ = normal_of(middle)
    moe = (normal * gains[1:2]).astype(bf16)
    moe_low[...] = moe
    sent[:, : moe.shape[1]] = dot(placer[...], moe).astype(bf16)
    logits = dot(moe, small[...])
    picked = [
        jnp.sum(hits[k].astype(f32) * logits, axis=-1, keepdims=True) for k in range(TOPK)
    ]
    top = picked[0]
    for value in picked[1:]:
        top = jnp.maximum(top, value)
    weights = [jnp.exp(value - top) for value in picked]
    total = weights[0]
    for value in weights[1:]:
        total = total + value
    lane = lax.broadcasted_iota(jnp.int32, gates.shape, 1)
    gate_at = jnp.zeros(places_of.shape[1:], f32)
    kept = jnp.zeros(gates.shape, f32)
    for k in range(TOPK):
        gate = weights[k] / total
        kept = jnp.where(lane == k, gate, kept)
        gate_at = gate_at + places_of[k].astype(f32) * gate
    gates[...] = kept
    block = jnp.zeros((sent.shape[0], 128), f32)
    for i, part in enumerate(in_three(gate_at)):
        parts[i] = part
        block = block + t_dot(part, jnp.where(lane == i, 1.0, 0.0).astype(bf16))
    sent[:, moe.shape[1] :] = block.astype(bf16)


def fetched(core, weights, held, sems, first):
    copies = [
        pltpu.make_async_copy(weights.at[m, core[0]], held.at[m], sems.at[m]) for m in range(3)
    ]
    for m in first:
        copies[m].start()

    def ready(m):
        copies[m].wait()
        return held[m]

    return ready


def forward_kernel(
    core, sent, cot, weights, out, hidden, out_grad, factor, other_factor, gate_grads, held, sems
):
    ready = fetched(core, weights, held, sems, (0, 1, 2))
    width = out.shape[1]
    gates = jnp.sum(sent[:, width:].astype(f32), axis=-1, keepdims=True)
    out_grad[...] = (gates * cot[...].astype(f32)).astype(bf16)
    rows = sent[:, :width]
    gate_pre = dot(rows, ready(0))
    up_pre = dot(rows, ready(1))
    sigmoid = 1.0 / (1.0 + jnp.exp(-gate_pre))
    silu = gate_pre * sigmoid
    low = (silu * up_pre).astype(bf16)
    hidden[...] = low
    result = dot_t(low, ready(2)).astype(bf16)
    out[...] = result
    grads = in_three(
        jnp.sum(cot[...].astype(f32) * result.astype(f32), axis=-1, keepdims=True)
    )
    lane = lax.broadcasted_iota(jnp.int32, gate_grads.shape, 1)
    block = jnp.zeros(gate_grads.shape, f32)
    for i, part in enumerate(grads):
        block = jnp.where(lane == i, part.astype(f32), block)
    gate_grads[...] = block.astype(bf16)
    factor[...] = up_pre * sigmoid * (1.0 + gate_pre * (1.0 - sigmoid))
    other_factor[...] = silu


def backward_kernel(
    core,
    out_grad,
    factor,
    other_factor,
    gate_grads,
    weights,
    rows_grad,
    gate_grad,
    up_grad,
    held,
    sems,
):
    width = out_grad.shape[1]
    ready = fetched(core, weights, held, sems, (2, 0, 1))
    hidden_grad = dot(out_grad[...], ready(2))
    low = (hidden_grad * factor[...]).astype(bf16)
    other = (hidden_grad * other_factor[...]).astype(bf16)
    gate_grad[...] = low
    up_grad[...] = other
    rows_grad[:, :width] = (dot_t(low, ready(0)) + dot_t(other, ready(1))).astype(bf16)
    rows_grad[:, width:] = gate_grads[...]


def expert_call(kernel, core, arrays, weights, outs):
    rows = arrays[0].shape[0]

    def whole(columns):
        return pl.BlockSpec((rows, columns), lambda i, core: (0, 0))

    return pl.pallas_call(
        kernel,
        out_shape=[jax.ShapeDtypeStruct((rows, columns), dtype) for columns, dtype in outs],
        grid_spec=pltpu.PrefetchScalarGridSpec(
            num_scalar_prefetch=1,
            grid=(1,),
            in_specs=[whole(a.shape[1]) for a in arrays] + [pl.BlockSpec(memory_space=pltpu.HBM)],
            out_specs=[whole(columns) for columns, _ in outs],
            scratch_shapes=[
                pltpu.VMEM((3,) + weights.shape[2:], bf16),
                pltpu.SemaphoreType.DMA((3,)),
            ],
        ),
        compiler_params=pltpu.CompilerParams(vmem_limit_bytes=ROOM),
        cost_estimate=COST,
    )(core, *arrays, weights)


def weights_kernel(sent, out_grad, hidden, gate_grad, up_grad, sums):
    rows = sent[...]
    sums[0] = t_dot(rows, gate_grad[...]).astype(bf16)
    sums[1] = t_dot(rows, up_grad[...]).astype(bf16)
    sums[2] = t_dot(out_grad[...], hidden[...]).astype(bf16)


def expert_weights_grad(sent, out_grad, hidden, gate_grad, up_grad, block=256):
    count, width = out_grad.shape
    columns = hidden.shape[1]
    part = pl.BlockSpec((count, block), lambda i: (0, i))
    whole = pl.BlockSpec((count, columns), lambda i: (0, 0), pipeline_mode=pl.Buffered(1))
    return pl.pallas_call(
        weights_kernel,
        out_shape=jax.ShapeDtypeStruct((3, width, columns), bf16),
        grid=(width // block,),
        in_specs=[part, part, whole, whole, whole],
        out_specs=pl.BlockSpec((3, block, columns), lambda i: (0, i, 0)),
        compiler_params=pltpu.CompilerParams(vmem_limit_bytes=ROOM),
        cost_estimate=COST,
    )(sent, out_grad, hidden, gate_grad, up_grad)


def combine_kernel(midway, parts, returned, output):
    rows = returned[...]
    output[...] = (
        midway[...] + (dot(parts[0], rows) + (dot(parts[1], rows) + dot(parts[2], rows)))
    ).astype(bf16)


def home_kernel(
    placer_t,
    home,
    midway,
    cot,
    gains,
    hits,
    places_of,
    gates,
    small,
    moe_low,
    midway_grad,
    branch_low,
    gain_grad,
    router_grad,
):
    width = midway.shape[1]
    lane = lax.broadcasted_iota(jnp.int32, gates.shape, 1)
    gate, gate_grad = [], []
    mean = jnp.zeros((gates.shape[0], 1), f32)
    for k in range(TOPK):
        gate.append(jnp.sum(jnp.where(lane == k, gates[...], 0.0), axis=-1, keepdims=True))
        gate_grad.append(
            jnp.sum(dot(places_of[k], home[:, width:]), axis=-1, keepdims=True)
        )
        mean = mean + gate[k] * gate_grad[k]
    logit_grad = jnp.zeros(gates.shape, f32)
    for k in range(TOPK):
        logit_grad = logit_grad + hits[k].astype(f32) * (gate[k] * (gate_grad[k] - mean))
    logit_grad = logit_grad.astype(bf16)
    router_grad[...] = t_dot(moe_low[...], logit_grad)
    grad = dot(placer_t[...], home[:, :width]) + dot_t(logit_grad, small[...])
    normal, inverse = normal_of(midway[...])
    result = cot[...].astype(f32) + norm_back(grad, normal, inverse, gains[1:2])
    midway_grad[...] = result
    branch_low[...] = result.astype(bf16)
    gain_grad[...] = jnp.broadcast_to(
        jnp.sum(grad * normal, axis=0, keepdims=True), gain_grad.shape
    )


def out_grad_kernel(mixed, own, other, branch, *blocks):
    quarter = own.shape[0] // 2
    branch[:quarter] = own[:quarter]
    branch[quarter : 2 * quarter] = other[:quarter]
    branch[2 * quarter : 3 * quarter] = own[quarter:]
    branch[3 * quarter :] = other[quarter:]
    count, columns = blocks[0].shape[1:]
    for k in range(2):
        grad = t_dot(mixed[...], branch[:, column_block(k, columns)]).astype(bf16)
        for s in range(4):
            blocks[s][k] = grad[column_block(s, count)]


def attend_back_kernel(
    branch,
    w_out,
    order,
    queries,
    kv_low,
    kv_up,
    logs,
    q_place,
    low_place,
    up_place,
    cosines,
    sines,
    normed,
    dq,
    dkv,
    block0,
    block1,
    block2,
    block3,
    grads,
    acc_low,
    acc_up,
    *,
    scale,
    pieces,
    heads,
):
    half = queries.shape[0] // 2
    columns = w_out.shape[2]
    ordered = dot_t(branch[:, :columns], w_out[0]) + dot_t(branch[:, columns:], w_out[1])
    grads[...] = dot_t(ordered.astype(bf16), order[...]).astype(bf16)
    allowed_low = low_place[...] <= q_place[...]
    allowed_up = up_place[...] <= q_place[half:, :]
    key_low, value_low = kv_low[:, :HD], kv_low[:, HD:]
    key_up, value_up = kv_up[:, :HD], kv_up[:, HD:]
    for h in range(heads):
        at = slice(h * HD, (h + 1) * HD)
        q, grad, log = queries[:, at], grads[:, at], logs[h]
        low = jnp.where(allowed_low, dot_t(q, key_low) * scale, NEGATIVE)
        up = jnp.where(allowed_up, dot_t(q[half:], key_up) * scale, NEGATIVE)
        probs_low, probs_up = jnp.exp(low - log), jnp.exp(up - log[half:])
        grad_low, grad_up = dot_t(grad, value_low), dot_t(grad[half:], value_up)
        along = jnp.sum(probs_low * grad_low, axis=-1, keepdims=True)
        along_up = along[half:] + jnp.sum(probs_up * grad_up, axis=-1, keepdims=True)
        along = jnp.concatenate([along[:half], along_up])
        score_low = (probs_low * (grad_low - along)).astype(bf16)
        score_up = (probs_up * (grad_up - along_up)).astype(bf16)
        part = dot(score_low, key_low)
        part = jnp.concatenate([part[:half], part[half:] + dot(score_up, key_up)]) * scale
        dq[:, at] = turn(part, cosines[...], -sines[...]).astype(bf16)
        terms = (
            (acc_low, slice(0, HD), t_dot(q, score_low)),
            (acc_up, slice(0, HD), t_dot(q[half:], score_up)),
            (acc_low, slice(HD, 2 * HD), t_dot(grad, probs_low.astype(bf16))),
            (acc_up, slice(HD, 2 * HD), t_dot(grad[half:], probs_up.astype(bf16))),
        )
        for acc, rows, term in terms:
            if h == 0:
                acc[rows] = term
            else:
                acc[rows] += term
    for s, block in enumerate((block0, block1, block2, block3)):
        block[...] = t_dot(normed[:, column_block(s, block.shape[0])], dq[...]).astype(bf16)
    for acc, first in ((acc_low, 0), (acc_up, half)):
        dk = (acc[:HD].T * scale).astype(bf16)
        dv = acc[HD:].T.astype(bf16)
        for i in range(pieces):
            dkv[i, first : first + half, :HD] = dk[i * half : (i + 1) * half]
            dkv[i, first : first + half, HD:] = dv[i * half : (i + 1) * half]


def sum_kernel(dq, cosines, sines, *refs):
    w_q, kvs, (parts, dkv, own, other) = refs[:4], refs[4:8], refs[8:]
    total = jnp.sum(parts[...].astype(f32), axis=0)
    dkv[:, :HD] = turn(total[:, :HD], cosines[...], -sines[...]).astype(bf16)
    dkv[:, HD:] = total[:, HD:].astype(bf16)
    quarter = own.shape[0] // 2
    for s in range(4):
        grad = dot_t(dq[...], w_q[s][...]) + dot_t(dkv[...], kvs[s][:, :WIDE])
        at = column_block(s, w_q[s].shape[0])
        own[:quarter, at] = grad[:quarter]
        other[:quarter, at] = grad[quarter : 2 * quarter]
        own[quarter:, at] = grad[2 * quarter : 3 * quarter]
        other[quarter:, at] = grad[3 * quarter :]


def stack_kernel(gate, up, down, late, out):
    del late
    out[0] = gate[...]
    out[1] = up[...]
    out[2] = down[...]


def small_grad_kernel(order, router_grad, gain_grad, late, out):
    del late
    row = lax.broadcasted_iota(jnp.int32, gain_grad.shape, 0)
    second = jnp.where(row == 1, gain_grad[...], 0.0).astype(bf16)
    small = router_grad[...] + t_dot(second, gain_picker())
    out[...] = t_dot(order[...], small.astype(bf16))


def input_kernel(both, own, received, midway_grad, gains, order, small, normed, dkv, out, *blocks):
    grad = own[...] + received[...]
    quarter = own.shape[0] // 2
    tokens = jnp.concatenate([both[:quarter], both[2 * quarter : 3 * quarter]])
    normal, inverse = normal_of(tokens.astype(f32))
    parts = in_three(norm_back(grad, normal, inverse, gains[0:1]))
    moved = dot_t(jnp.concatenate(parts), order[...])
    count = 2 * quarter
    out[...] = midway_grad[...] + (
        moved[:count] + (moved[count : 2 * count] + moved[2 * count :])
    )
    gain_grad = jnp.sum(grad * normal, axis=0, keepdims=True)
    row = lax.broadcasted_iota(jnp.int32, gains.shape, 0)
    gain_grad = jnp.where(row == 0, gain_grad, 0.0).astype(bf16)
    small = small[...] + t_dot(gain_grad, gain_picker())
    rows = blocks[0].shape[0]
    for s, block in enumerate(blocks):
        at = column_block(s, rows)
        block[:, :WIDE] = t_dot(normed[:, at], dkv[...]).astype(bf16)
        block[:, WIDE:] = small[at].astype(bf16)


def body(
    tokens,
    cotangent,
    pair_of,
    routes,
    attn_gain,
    moe_gain,
    w_query,
    w_key,
    w_value,
    w_out,
    w_router,
    w_gate,
    w_up,
    w_down,
):
    rows = tokens.shape[1]
    half = rows // 2
    width = tokens.shape[2]
    shard = w_query.shape[1]
    ctx_count = 16
    experts = w_router.shape[2]
    columns = w_gate.shape[3]
    per_group = H // KVH
    qw = per_group * HD
    scale = 1.0 / math.sqrt(HD)
    core = lax.axis_index("core")
    ylo, z, yhi = lax.axis_index("ylo"), lax.axis_index("z"), lax.axis_index("yhi")
    x = lax.axis_index("x")
    piece_rows = 2 * shard
    slots = experts * SLOTS
    own_tokens, cot = tokens[0], cotangent[0]

    def halves(matrix):
        return [matrix[:, : matrix.shape[1] // 2], matrix[:, matrix.shape[1] // 2 :]]

    small = jnp.concatenate([w_router[0], attn_gain[0][:, None], moe_gain[0][:, None]], axis=-1)
    small = jnp.pad(small, ((0, 0), (0, 128 - experts - 2)))
    query_halves, key_halves, value_halves = halves(w_query[0]), halves(w_key[0]), halves(w_value[0])
    pairs = [
        jnp.concatenate([k, v, small, q], axis=-1)
        for k, v, q in zip(key_halves, value_halves, query_halves)
    ]
    pieces = gather_pieces(pairs, yhi, core, ("core", "yhi"), SAME, OTHER)
    out_pieces = gather_pieces(
        halves(w_out[0]), yhi, yhi, ("ylo", "core", "yhi"), OUT_SAME, OUT_OTHER
    )
    other_tokens = partner(own_tokens)
    pieces, out_pieces, x, z, own_tokens, other_tokens, pair_of = together(
        pieces, out_pieces, x, z, own_tokens, other_tokens, pair_of
    )

    plane_rows = 16 * piece_rows
    plane = spread(pieces, 16, PLANE)
    both = jnp.concatenate(
        [own_tokens[:half], other_tokens[:half], own_tokens[half:], other_tokens[half:]]
    )
    order, out_order, level_order = order_matrix(16, x), order_matrix(8, x), level_order_matrix(z)
    (expert_shards_in,) = call(
        stack_kernel, [((3,) + w_gate.shape[1:], bf16)], w_gate[0], w_up[0], w_down[0], both
    )
    (
        plane, both, out_pieces, order, out_order, level_order, pair_of, expert_shards_in, chosen,
    ) = together(
        plane, both, out_pieces, order, out_order, level_order, pair_of, expert_shards_in,
        routes[0, 0],
    )

    plane = plane.reshape(plane_rows, -1)
    w_kvs = along("x", plane[:, : 3 * HD])
    wo = spread(out_pieces, 16, LEVEL)
    (both,) = call(order_kernel, [((2 * rows, width), bf16)], both, order)

    def two_cores(ctx):
        return jnp.stack([ctx + core, ctx + 1 - core], axis=-1).reshape(-1)

    ctx_here = (ylo * 4 + z) * 2
    q_place = places(pair_of, two_cores(ctx_here), rows, ctx_count)
    q_place = q_place.transpose(1, 0, 2).reshape(2 * rows, 1)
    key_place = places(
        pair_of, two_cores(jnp.arange(8, dtype=jnp.int32) * 2), rows, ctx_count
    )
    low_place, up_place = key_place[:, 0].reshape(1, -1), key_place[:, 1].reshape(1, -1)
    frequency = jnp.exp(jnp.arange(HD // 2, dtype=f32) * (-2.0 * math.log(ROPE_BASE) / HD))
    angles = q_place.astype(f32) * frequency[None, :]
    cosines, sines = jnp.cos(angles), jnp.sin(angles)
    cosines = jnp.concatenate([cosines, cosines], axis=-1)
    sines = jnp.concatenate([-sines, sines], axis=-1)
    w_q, w_kvs, wo, both, q_place, low_place, up_place, cosines, sines, chosen = together(
        plane[:, 3 * HD :], w_kvs, wo, both, q_place, low_place, up_place, cosines, sines, chosen
    )

    w_q = along("x", w_q)
    wo = along("z", wo.reshape(2, qw // 4, width // 2))
    normed, key_value, gains = call(
        keys_kernel,
        [((2 * rows, width), bf16), ((8, 2 * rows, 2 * HD), bf16), ((8, width), f32)],
        both,
        cosines,
        sines,
        *w_kvs,
    )
    all_kv = exchange(key_value, RING)
    small, moe_gains = call(
        small_kernel, [((width, 128), bf16), ((8, width), f32)], order, *w_kvs
    )
    (queries,) = call(
        query_kernel, [((2 * rows, qw), bf16)], normed, cosines, sines, *w_q, cost=LONG
    )
    lanes = jnp.arange(128, dtype=jnp.int32)
    hits = (chosen.T[:, :, None] == lanes[None, None, :]).astype(bf16)
    earlier = (lanes[:, None] > lanes[None, :]).astype(bf16)
    before = dot(earlier, jnp.sum(hits, axis=0))
    slot_index = jnp.sum(hits.astype(f32) * before[None], axis=-1).astype(jnp.int32)
    target = chosen.T * SLOTS + slot_index
    slot_row = jnp.arange(slots, dtype=jnp.int32)
    places_of = (target[:, :, None] == slot_row[None, None, :]).astype(bf16)
    placer_t = jnp.sum(places_of, axis=0)
    placer = placer_t.T
    (cot_rows,) = call(order_kernel, [((slots, width), bf16)], placer, cot)
    (
        queries, all_kv, expert_shards_in, small, moe_gains, cot_rows,
        hits, places_of, placer_t, placer, wo,
    ) = together(
        queries, all_kv, expert_shards_in, small, moe_gains, cot_rows,
        hits, places_of, placer_t, placer, wo,
    )
    expert_weights = lax.all_gather(expert_shards_in, CTX, axis=2, tiled=True)

    arrived_cot = to_owners(cot_rows.reshape(experts, SLOTS, width))
    sizes = dict(scale=scale, pieces=8, heads=per_group)
    keys = 8 * rows
    mixed, mixed_back, logs, kv_low, kv_up = call(
        functools.partial(attend_kernel, **sizes),
        [
            ((2 * rows, qw), bf16),
            ((2 * rows, qw), bf16),
            ((per_group, 2 * rows, 1), f32),
            ((keys, 2 * HD), bf16),
            ((keys, 2 * HD), bf16),
        ],
        queries,
        q_place,
        low_place,
        up_place,
        level_order,
        out_order,
        all_kv,
        scratch=[pltpu.VMEM((2 * rows, qw), bf16)],
    )

    branch_own, branch_other, wo = call(
        branch_kernel,
        [((rows, width), f32), ((rows, width), f32), ((2, qw, width // 2), bf16)],
        mixed,
        *wo,
    )
    sent, midway, moe_low, gates, gate_parts = call(
        route_kernel,
        [
            ((slots, width + 128), bf16),
            ((rows, width), f32),
            ((rows, width), bf16),
            ((rows, 128), f32),
            ((3, rows, slots), bf16),
        ],
        own_tokens,
        branch_own,
        partner(branch_other),
        small,
        moe_gains,
        hits,
        places_of,
        placer,
    )
    sent, arrived_cot = together(sent, arrived_cot)

    sent = to_owners(sent.reshape(experts, SLOTS, width + 128)).reshape(slots, width + 128)
    mine = core.reshape(1)
    expert_out, hidden, out_grad, factor, other_factor, gate_grads = expert_call(
        forward_kernel,
        mine,
        [sent, arrived_cot.reshape(slots, width)],
        expert_weights,
        [
            (width, bf16),
            (columns, bf16),
            (width, bf16),
            (columns, f32),
            (columns, f32),
            (128, bf16),
        ],
    )
    rows_grad, gate_grad, up_grad = expert_call(
        backward_kernel,
        mine,
        [out_grad, factor, other_factor, gate_grads],
        expert_weights,
        [(width + 128, bf16), (columns, bf16), (columns, bf16)],
    )
    rows_grad, gate_grad, up_grad = together(rows_grad, gate_grad, up_grad)

    home_grad = to_owners(rows_grad.reshape(experts, SLOTS, width + 128))
    expert_sums = expert_weights_grad(sent, out_grad, hidden, gate_grad, up_grad)
    home_grad, expert_sums, expert_out = together(home_grad, expert_sums, expert_out)
    expert_sums = lax.psum_scatter(expert_sums, RING, scatter_dimension=1, tiled=True)

    returned = to_owners(expert_out.reshape(experts, SLOTS, width))
    midway_grad, branch_low, gain_two_grad, router_grad = call(
        home_kernel,
        [((rows, width), f32), ((rows, width), bf16), ((8, width), f32), ((width, 128), f32)],
        placer_t,
        home_grad.reshape(slots, width + 128),
        midway,
        cot,
        moe_gains,
        hits,
        places_of,
        gates,
        small,
        moe_low,
    )
    branch, *out_w_grad = call(
        out_grad_kernel,
        [((2 * rows, width), bf16)] + [((2, qw // 4, width // 2), bf16)] * 4,
        mixed_back,
        branch_low,
        partner(branch_low),
    )
    branch, out_w_grad = together(branch, out_w_grad)
    out_w_grad = added(back_along_x(out_w_grad))

    dq, dkv, *q_w_grad = call(
        functools.partial(attend_back_kernel, **sizes),
        [((2 * rows, qw), bf16), ((8, 2 * rows, 2 * HD), bf16)]
        + [((plane_rows, qw), bf16)] * 4,
        branch,
        wo,
        level_order,
        queries,
        kv_low,
        kv_up,
        logs,
        q_place,
        low_place,
        up_place,
        cosines,
        sines,
        normed,
        scratch=[
            pltpu.VMEM((2 * rows, qw), bf16),
            pltpu.VMEM((2 * HD, keys), f32),
            pltpu.VMEM((2 * HD, keys), f32),
        ],
    )
    dkv, q_w_grad, returned, late = together(dkv, q_w_grad, returned, gain_two_grad)

    dkv = exchange(dkv, RING)
    q_w_grad = back_along_x(q_w_grad)
    (output,) = call(
        combine_kernel,
        [((rows, width), bf16)],
        midway,
        gate_parts,
        returned.reshape(slots, width),
    )
    (small_grad,) = call(
        small_grad_kernel, [((width, 128), f32)], order, router_grad, gain_two_grad, late
    )
    dkv, out_w_grad, small_grad, output, q_w_grad[1], q_w_grad[3] = together(
        dkv, out_w_grad, small_grad, output, q_w_grad[1], q_w_grad[3]
    )

    dkv, normed_own, normed_other = call(
        sum_kernel,
        [((2 * rows, 2 * HD), bf16), ((rows, width), f32), ((rows, width), f32)],
        dq,
        cosines,
        sines,
        *w_q,
        *w_kvs,
        dkv,
    )
    input_grad, *kvs_grad = call(
        input_kernel,
        [((rows, width), f32)] + [((plane_rows, 3 * HD), bf16)] * 4,
        both,
        normed_own,
        partner(normed_other),
        midway_grad,
        gains,
        order,
        small_grad,
        normed,
        dkv,
    )
    kvs_grad, out_w_grad, input_grad = together(kvs_grad, out_w_grad, input_grad)

    out_w_grad = exchange(out_w_grad.reshape(16, piece_rows, width // 2), OUT_PLANE)
    kvs_grad = back_along_x(kvs_grad)
    (plane_grad,) = call(
        add_both_kernel, [((plane_rows, qw + 3 * HD), bf16)], *q_w_grad, *kvs_grad, cost=LONG
    )
    plane_grad, out_w_grad = together(plane_grad, out_w_grad)
    plane_grad = exchange(plane_grad.reshape(16, piece_rows, qw + 3 * HD), PLANE)

    def summed(pieces):
        return jnp.sum(pieces.astype(f32), axis=0)

    def expert_shards(grad):
        count = grad.shape[1] // 2
        kept = lax.dynamic_slice_in_dim(grad, core * count, count, axis=1)
        given = partner(lax.dynamic_slice_in_dim(grad, (1 - core) * count, count, axis=1))
        both = jnp.stack([pick(core, kept, given), pick(core, given, kept)], axis=1)
        return [both[i : i + 1].astype(f32) for i in range(3)]

    out_w_grad = scatter_pieces(
        summed(out_w_grad), yhi, yhi, ("ylo", "core", "yhi"), OUT_SAME, OUT_OTHER
    )
    w_gate_grad, w_up_grad, w_down_grad = expert_shards(expert_sums)
    plane_grad, out_w_grad, w_gate_grad, w_up_grad, w_down_grad = together(
        plane_grad, out_w_grad, w_gate_grad, w_up_grad, w_down_grad
    )
    plane_grad = scatter_pieces(summed(plane_grad), yhi, core, ("core", "yhi"), SAME, OTHER)
    plane_grad = plane_grad.reshape(shard, 2, -1)

    def joined(first, last):
        return plane_grad[:, :, first:last].reshape(1, shard, -1)

    small_grad = jnp.sum(plane_grad[None, :, :, qw + 2 * HD :], axis=2)

    return (
        output[None],
        input_grad[None],
        small_grad[:, :, experts],
        small_grad[:, :, experts + 1],
        joined(0, qw),
        joined(qw, qw + HD),
        joined(qw + HD, qw + 2 * HD),
        out_w_grad[None],
        small_grad[:, :, :experts],
        w_gate_grad,
        w_up_grad,
        w_down_grad,
    )


def solution(mesh):
    fine = Mesh(mesh.devices.reshape(2, 4, 2, 4, 2), AXES)
    seq = P(FSDP, CTX, None)
    vector = P(None, AXES)
    matrix = P(None, AXES, None)
    expert = P(None, FSDP, CTX, None)
    in_specs = (
        seq,
        seq,
        P(),
        P(None, FSDP, CTX, None),
        vector,
        vector,
        matrix,
        matrix,
        matrix,
        matrix,
        matrix,
        expert,
        expert,
        expert,
    )
    out_specs = (
        seq,
        seq,
        vector,
        vector,
        matrix,
        matrix,
        matrix,
        matrix,
        matrix,
        expert,
        expert,
        expert,
    )
    return jax.shard_map(body, mesh=fine, in_specs=in_specs, out_specs=out_specs, check_vma=False)
```

```python
import functools
import math

import jax
import jax.numpy as jnp
from jax import lax
from jax.experimental import pallas as pl
from jax.experimental.pallas import tpu as pltpu
from jax.sharding import Mesh
from jax.sharding import PartitionSpec as P

H = 12
KVH = 2
HD = 128
TOPK = 4

EPSILON = 1e-06
ROPE_BASE = 1000000.0
NEGATIVE = -1e30

AXES = ("ylo", "z", "core", "x", "yhi")
CTX = ("ylo", "z", "core")
FSDP = ("x", "yhi")
GROUPS = [
    [
        (((group ^ yhi) * 4 + z) * 2 + core) * 8 + x * 2 + yhi
        for x in range(4)
        for yhi in range(2)
        for core in range(2)
    ]
    for group in range(2)
    for z in range(4)
]
RING = ("ylo", "z")
PLANE = ("ylo", "z", "yhi")
OUT_PLANE = ("yhi", "z", "ylo")
LEVEL = ("yhi", "ylo", "x")
GROUPS = [
    [
        (((group ^ yhi) * 4 + z) * 2 + core) * 8 + x * 2 + yhi
        for x in range(4)
        for yhi in range(2)
        for core in range(2)
    ]
    for group in range(2)
    for z in range(4)
]
RING = ("ylo", "z")
ROWS_ORDER = ("ylo", "z", "yhi", "x")
OUT_ORDER = ("yhi", "z", "ylo", "x")
SLOTS = 40

bf16 = jnp.bfloat16
f32 = jnp.float32


def dot(left, right):
    return jnp.dot(left, right, preferred_element_type=f32)


def dot_t(left, right):
    return lax.dot_general(left, right, (((1,), (1,)), ((), ())), preferred_element_type=f32)


def t_dot(left, right):
    return lax.dot_general(left, right, (((0,), (0,)), ((), ())), preferred_element_type=f32)


def exchange(pieces, axes):
    return lax.all_to_all(pieces, axes, split_axis=0, concat_axis=0, tiled=True)


def to_owners(pieces):
    return lax.all_to_all(
        pieces, AXES, split_axis=0, concat_axis=0, axis_index_groups=GROUPS, tiled=True
    )


def spread(piece, count, axes):
    return exchange(jnp.broadcast_to(piece[None], (count,) + piece.shape), axes)


def after(value, earlier):
    return lax.optimization_barrier((value, earlier))[0]


def together(*values):
    return lax.optimization_barrier(values)


def partner(value):
    return lax.ppermute(value, "core", [(0, 1), (1, 0)])


def route(axes, sizes, move):
    pairs = []
    for source in range(math.prod(sizes)):
        rest, at = source, []
        for size in reversed(sizes):
            at.insert(0, rest % size)
            rest //= size
        target = 0
        for size, value in zip(sizes, move(*at)):
            target = target * size + value
        pairs.append((source, target))
    return pairs


SAME = route(("core", "yhi"), (2, 2), lambda c, h: (h, c))
OTHER = route(("core", "yhi"), (2, 2), lambda c, h: (1 - h, c))
OUT_SAME = route(("ylo", "core", "yhi"), (2, 2, 2), lambda j, c, h: (c, j, h))
OUT_OTHER = route(("ylo", "core", "yhi"), (2, 2, 2), lambda j, c, h: (c, j, 1 - h))


def back(pairs):
    return [(target, source) for source, target in pairs]


def pick(flag, if_zero, if_one):
    return jnp.where(flag == 0, if_zero, if_one)


def gather_pieces(pair, flag, key, axes, same, other):
    first = lax.ppermute(pick(flag, pair[0], pair[1]), axes, same)
    second = lax.ppermute(pick(flag, pair[1], pair[0]), axes, other)
    return pick(
        key, jnp.concatenate([first, second]), jnp.concatenate([second, first])
    )


def scatter_pieces(piece, flag, key, axes, same, other):
    count = piece.shape[0] // 2
    mine, rest = piece[:count], piece[count:]
    first = lax.ppermute(pick(key, mine, rest), axes, back(same))
    second = lax.ppermute(pick(key, rest, mine), axes, back(other))
    return pick(flag, jnp.concatenate([first, second], axis=-1), jnp.concatenate([second, first], axis=-1))


def along(axis, piece):
    return [piece] + [
        lax.ppermute(piece, axis, [(i, (i + s) % 4) for i in range(4)]) for s in (1, 2, 3)
    ]


def back_along_x(blocks):
    return [blocks[0]] + [
        lax.ppermute(blocks[s], "x", [(i, (i - s) % 4) for i in range(4)]) for s in (1, 2, 3)
    ]


def added(blocks, *late):
    (total,) = call(add_kernel, [(blocks[0].shape, bf16)], *blocks, *late, cost=LONG)
    return total


def sum_of(first, second, third, fourth):
    return (
        (first[...].astype(f32) + second[...].astype(f32))
        + (third[...].astype(f32) + fourth[...].astype(f32))
    ).astype(bf16)


def add_kernel(first, second, third, fourth, *refs):
    refs[-1][...] = sum_of(first, second, third, fourth)


def add_both_kernel(*refs):
    total = refs[8]
    count = refs[0].shape[1]
    total[:, :count] = sum_of(*refs[:4])
    total[:, count:] = sum_of(*refs[4:8])


def order_matrix(groups, x):
    index = jnp.arange(groups * 96, dtype=jnp.int32)
    turn_of, group, row = index // (groups * 24), index // 24 % groups, index % 24
    own = group * 96 + (x - turn_of) % 4 * 24 + row
    return (index[:, None] == own[None, :]).astype(bf16)


def level_order_matrix(z):
    index = jnp.arange(8 * 96, dtype=jnp.int32)
    own = (z - index // 192) % 4 * 192 + index % 192
    return (index[:, None] == own[None, :]).astype(bf16)


def places(pair_of, ctx, row_count, ctx_count):
    half_size = row_count // 2
    pair = jnp.sum(
        jnp.where(ctx[:, None] == jnp.arange(ctx_count, dtype=jnp.int32)[None], pair_of[None], 0),
        axis=1,
    )
    block = jnp.stack([pair, 2 * ctx_count - 1 - pair], axis=1)
    return block[:, :, None] * half_size + jnp.arange(half_size, dtype=jnp.int32)[None, None]


def in_three(value):
    high = value.astype(bf16)
    rest = value - high.astype(f32)
    middle = rest.astype(bf16)
    return [high, middle, (rest - middle.astype(f32)).astype(bf16)]


def call(kernel, outs, *args, scratch=(), cost=None):
    def whole(shape):
        return pl.BlockSpec(shape, lambda i: (0,) * len(shape))

    return pl.pallas_call(
        kernel,
        out_shape=[jax.ShapeDtypeStruct(shape, dtype) for shape, dtype in outs],
        grid=(1,),
        in_specs=[whole(a.shape) for a in args],
        out_specs=[whole(shape) for shape, _ in outs],
        scratch_shapes=list(scratch),
        compiler_params=pltpu.CompilerParams(vmem_limit_bytes=ROOM),
        cost_estimate=COST if cost is None else cost,
    )(*args)


ROOM = 58 << 20
COST = pl.CostEstimate(flops=1 << 20, bytes_accessed=1 << 18, transcendentals=0)
LONG = pl.CostEstimate(flops=1 << 35, bytes_accessed=1 << 27, transcendentals=0)
WIDE = 2 * HD
EXPERTS = 16


def turn(vectors, cosines, sines):
    return vectors * cosines + pltpu.roll(vectors, HD // 2, axis=1) * sines


def gain_picker():
    row = lax.broadcasted_iota(jnp.int32, (8, 128), 0)
    column = lax.broadcasted_iota(jnp.int32, (8, 128), 1)
    return jnp.where((column == row + EXPERTS) & (row < 2), 1.0, 0.0).astype(bf16)


def normal_of(stream):
    inverse = lax.rsqrt(jnp.mean(stream * stream, axis=-1, keepdims=True) + EPSILON)
    return stream * inverse, inverse


def norm_back(grad, normal, inverse, gain):
    scaled = grad * gain
    return inverse * (scaled - normal * jnp.mean(scaled * normal, axis=-1, keepdims=True))


def column_block(s, count):
    return slice(s * count, (s + 1) * count)


def order_kernel(rows, order, out):
    out[...] = dot(rows[...], order[...]).astype(bf16)


def keys_kernel(both, cosines, sines, *refs):
    kvs, (normed, key_value, gains) = refs[:4], refs[4:]
    count = kvs[0].shape[0]
    for s in range(4):
        gains[:, column_block(s, count)] = dot_t(gain_picker(), kvs[s][:, WIDE:])
    normal, _ = normal_of(both[...].astype(f32))
    normed[...] = (normal * gains[0:1]).astype(bf16)
    kv = dot(normed[:, column_block(0, count)], kvs[0][:, :WIDE])
    for s in range(1, 4):
        kv = kv + dot(normed[:, column_block(s, count)], kvs[s][:, :WIDE])
    keys = turn(kv[:, :HD], cosines[...], sines[...]).astype(bf16)
    values = kv[:, HD:].astype(bf16)
    for i in range(key_value.shape[0]):
        key_value[i, :, :HD] = keys
        key_value[i, :, HD:] = values


def small_kernel(order, kvs0, kvs1, kvs2, kvs3, small, gains):
    count = kvs0.shape[0]
    total = jnp.zeros(small.shape, f32)
    for s, kvs in enumerate((kvs0, kvs1, kvs2, kvs3)):
        total = total + dot(order[:, column_block(s, count)], kvs[:, WIDE:])
    small[...] = total.astype(bf16)
    gains[...] = dot_t(gain_picker(), small[...])


def query_kernel(normed, cosines, sines, w_q0, w_q1, w_q2, w_q3, queries):
    w_q = (w_q0, w_q1, w_q2, w_q3)
    count = w_q0.shape[0]
    for h in range(queries.shape[1] // HD):
        at = column_block(h, HD)
        q = dot(normed[:, column_block(0, count)], w_q0[:, at])
        for s in range(1, 4):
            q = q + dot(normed[:, column_block(s, count)], w_q[s][:, at])
        queries[:, at] = turn(q, cosines[...], sines[...]).astype(bf16)


def attend_kernel(
    queries,
    q_place,
    low_place,
    up_place,
    order,
    order_back,
    kv,
    ordered,
    ordered_back,
    logs,
    kv_low,
    kv_up,
    mixed,
    *,
    scale,
    pieces,
    heads,
):
    half = kv.shape[1] // 2
    for i in range(pieces):
        kv_low[i * half : (i + 1) * half, :] = kv[i, :half]
        kv_up[i * half : (i + 1) * half, :] = kv[i, half:]
    allowed_low = low_place[...] <= q_place[...]
    allowed_up = up_place[...] <= q_place[half:, :]
    for h in range(heads):
        at = slice(h * HD, (h + 1) * HD)
        q = queries[:, at]
        low = jnp.where(allowed_low, dot_t(q, kv_low[:, :HD]) * scale, NEGATIVE)
        up = jnp.where(allowed_up, dot_t(q[half:], kv_up[:, :HD]) * scale, NEGATIVE)
        first, second = low[:half], low[half:]
        top = jnp.max(first, axis=-1, keepdims=True)
        weight = jnp.exp(first - top)
        total = jnp.sum(weight, axis=-1, keepdims=True)
        probs = (weight / total).astype(bf16)
        mixed[:half, at] = dot(probs, kv_low[:, HD:]).astype(bf16)
        logs[h, :half, :] = top + jnp.log(total)
        top = jnp.maximum(
            jnp.max(second, axis=-1, keepdims=True), jnp.max(up, axis=-1, keepdims=True)
        )
        weight, weight_up = jnp.exp(second - top), jnp.exp(up - top)
        total = jnp.sum(weight, axis=-1, keepdims=True) + jnp.sum(
            weight_up, axis=-1, keepdims=True
        )
        mixed[half:, at] = (
            dot((weight / total).astype(bf16), kv_low[:, HD:])
            + dot((weight_up / total).astype(bf16), kv_up[:, HD:])
        ).astype(bf16)
        logs[h, half:, :] = top + jnp.log(total)
    ordered[...] = dot(mixed[...], order[...]).astype(bf16)
    ordered_back[...] = dot(mixed[...], order_back[...]).astype(bf16)


def branch_kernel(mixed, w_out0, w_out1, w_out2, w_out3, own, other, w_out):
    quarter = mixed.shape[0] // 4
    count, columns = w_out0.shape[1:]
    for s, part in enumerate((w_out0, w_out1, w_out2, w_out3)):
        w_out[:, column_block(s, count)] = part[...]
    for k in range(2):
        part = dot(mixed[...], w_out[k])
        at = slice(k * columns, (k + 1) * columns)
        own[:quarter, at] = part[:quarter]
        other[:quarter, at] = part[quarter : 2 * quarter]
        own[quarter:, at] = part[2 * quarter : 3 * quarter]
        other[quarter:, at] = part[3 * quarter :]


def route_kernel(
    tokens,
    own,
    received,
    small,
    gains,
    hits,
    places_of,
    placer,
    sent,
    midway,
    moe_low,
    gates,
    parts,
):
    middle = tokens[...].astype(f32) + (own[...] + received[...])
    midway[...] = middle
    normal, _ = normal_of(middle)
    moe = (normal * gains[1:2]).astype(bf16)
    moe_low[...] = moe
    sent[:, : moe.shape[1]] = dot(placer[...], moe).astype(bf16)
    logits = dot(moe, small[...])
    picked = [
        jnp.sum(hits[k].astype(f32) * logits, axis=-1, keepdims=True) for k in range(TOPK)
    ]
    top = picked[0]
    for value in picked[1:]:
        top = jnp.maximum(top, value)
    weights = [jnp.exp(value - top) for value in picked]
    total = weights[0]
    for value in weights[1:]:
        total = total + value
    lane = lax.broadcasted_iota(jnp.int32, gates.shape, 1)
    gate_at = jnp.zeros(places_of.shape[1:], f32)
    kept = jnp.zeros(gates.shape, f32)
    for k in range(TOPK):
        gate = weights[k] / total
        kept = jnp.where(lane == k, gate, kept)
        gate_at = gate_at + places_of[k].astype(f32) * gate
    gates[...] = kept
    block = jnp.zeros((sent.shape[0], 128), f32)
    for i, part in enumerate(in_three(gate_at)):
        parts[i] = part
        block = block + t_dot(part, jnp.where(lane == i, 1.0, 0.0).astype(bf16))
    sent[:, moe.shape[1] :] = block.astype(bf16)


def expert_kernel(
    core, sent, cot, weights, out, rows_grad, hidden, out_grad, gate_grad, up_grad, held, sems
):
    copies = [
        pltpu.make_async_copy(weights.at[m, core[0]], held.at[m], sems.at[m]) for m in range(3)
    ]
    for copy in copies:
        copy.start()
    width = out.shape[1]
    gates = jnp.sum(sent[:, width:].astype(f32), axis=-1, keepdims=True)
    out_grad[...] = (gates * cot[...].astype(f32)).astype(bf16)
    rows = sent[:, :width]
    copies[0].wait()
    gate_pre = dot(rows, held[0])
    copies[1].wait()
    up_pre = dot(rows, held[1])
    sigmoid = 1.0 / (1.0 + jnp.exp(-gate_pre))
    silu = gate_pre * sigmoid
    low = (silu * up_pre).astype(bf16)
    hidden[...] = low
    copies[2].wait()
    hidden_grad = dot(out_grad[...], held[2])
    gate_low = (hidden_grad * up_pre * sigmoid * (1.0 + gate_pre * (1.0 - sigmoid))).astype(bf16)
    up_low = (hidden_grad * silu).astype(bf16)
    gate_grad[...] = gate_low
    up_grad[...] = up_low
    rows_grad[:, :width] = (dot_t(gate_low, held[0]) + dot_t(up_low, held[1])).astype(bf16)
    result = dot_t(low, held[2]).astype(bf16)
    out[...] = result
    grads = in_three(
        jnp.sum(cot[...].astype(f32) * result.astype(f32), axis=-1, keepdims=True)
    )
    lane = lax.broadcasted_iota(jnp.int32, (cot.shape[0], 128), 1)
    block = jnp.zeros(lane.shape, f32)
    for i, part in enumerate(grads):
        block = jnp.where(lane == i, part.astype(f32), block)
    rows_grad[:, width:] = block.astype(bf16)


def expert_call(core, arrays, weights, outs):
    rows = arrays[0].shape[0]

    def whole(columns):
        return pl.BlockSpec(
            (rows, columns), lambda i, core: (0, 0), pipeline_mode=pl.Buffered(1)
        )

    return pl.pallas_call(
        expert_kernel,
        out_shape=[jax.ShapeDtypeStruct((rows, columns), bf16) for columns in outs],
        grid_spec=pltpu.PrefetchScalarGridSpec(
            num_scalar_prefetch=1,
            grid=(1,),
            in_specs=[whole(a.shape[1]) for a in arrays] + [pl.BlockSpec(memory_space=pltpu.HBM)],
            out_specs=[whole(columns) for columns in outs],
            scratch_shapes=[
                pltpu.VMEM((3,) + weights.shape[2:], bf16),
                pltpu.SemaphoreType.DMA((3,)),
            ],
        ),
        compiler_params=pltpu.CompilerParams(vmem_limit_bytes=ROOM),
        cost_estimate=COST,
    )(core, *arrays, weights)


def weights_kernel(sent, out_grad, hidden, gate_grad, up_grad, sums):
    rows = sent[...]
    sums[0] = t_dot(rows, gate_grad[...]).astype(bf16)
    sums[1] = t_dot(rows, up_grad[...]).astype(bf16)
    sums[2] = t_dot(out_grad[...], hidden[...]).astype(bf16)


def expert_weights_grad(sent, out_grad, hidden, gate_grad, up_grad, block=256):
    count, width = out_grad.shape
    columns = hidden.shape[1]
    part = pl.BlockSpec((count, block), lambda i: (0, i))
    whole = pl.BlockSpec((count, columns), lambda i: (0, 0), pipeline_mode=pl.Buffered(1))
    return pl.pallas_call(
        weights_kernel,
        out_shape=jax.ShapeDtypeStruct((3, width, columns), bf16),
        grid=(width // block,),
        in_specs=[part, part, whole, whole, whole],
        out_specs=pl.BlockSpec((3, block, columns), lambda i: (0, i, 0)),
        compiler_params=pltpu.CompilerParams(vmem_limit_bytes=ROOM),
        cost_estimate=COST,
    )(sent, out_grad, hidden, gate_grad, up_grad)


def combine_kernel(midway, parts, returned, output):
    rows = returned[...]
    output[...] = (
        midway[...] + (dot(parts[0], rows) + (dot(parts[1], rows) + dot(parts[2], rows)))
    ).astype(bf16)


def home_kernel(
    placer_t,
    home,
    midway,
    cot,
    gains,
    hits,
    places_of,
    gates,
    small,
    moe_low,
    midway_grad,
    branch_low,
    gain_grad,
    router_grad,
):
    width = midway.shape[1]
    lane = lax.broadcasted_iota(jnp.int32, gates.shape, 1)
    gate, gate_grad = [], []
    mean = jnp.zeros((gates.shape[0], 1), f32)
    for k in range(TOPK):
        gate.append(jnp.sum(jnp.where(lane == k, gates[...], 0.0), axis=-1, keepdims=True))
        gate_grad.append(
            jnp.sum(dot(places_of[k], home[:, width:]), axis=-1, keepdims=True)
        )
        mean = mean + gate[k] * gate_grad[k]
    logit_grad = jnp.zeros(gates.shape, f32)
    for k in range(TOPK):
        logit_grad = logit_grad + hits[k].astype(f32) * (gate[k] * (gate_grad[k] - mean))
    logit_grad = logit_grad.astype(bf16)
    router_grad[...] = t_dot(moe_low[...], logit_grad)
    grad = dot(placer_t[...], home[:, :width]) + dot_t(logit_grad, small[...])
    normal, inverse = normal_of(midway[...])
    result = cot[...].astype(f32) + norm_back(grad, normal, inverse, gains[1:2])
    midway_grad[...] = result
    branch_low[...] = result.astype(bf16)
    gain_grad[...] = jnp.broadcast_to(
        jnp.sum(grad * normal, axis=0, keepdims=True), gain_grad.shape
    )


def out_grad_kernel(mixed, own, other, branch, *blocks):
    quarter = own.shape[0] // 2
    branch[:quarter] = own[:quarter]
    branch[quarter : 2 * quarter] = other[:quarter]
    branch[2 * quarter : 3 * quarter] = own[quarter:]
    branch[3 * quarter :] = other[quarter:]
    count, columns = blocks[0].shape[1:]
    for k in range(2):
        grad = t_dot(mixed[...], branch[:, column_block(k, columns)]).astype(bf16)
        for s in range(4):
            blocks[s][k] = grad[column_block(s, count)]


def attend_back_kernel(
    branch,
    w_out,
    order,
    queries,
    kv_low,
    kv_up,
    logs,
    q_place,
    low_place,
    up_place,
    cosines,
    sines,
    normed,
    dq,
    dkv,
    block0,
    block1,
    block2,
    block3,
    grads,
    acc_low,
    acc_up,
    *,
    scale,
    pieces,
    heads,
):
    half = queries.shape[0] // 2
    columns = w_out.shape[2]
    ordered = dot_t(branch[:, :columns], w_out[0]) + dot_t(branch[:, columns:], w_out[1])
    grads[...] = dot_t(ordered.astype(bf16), order[...]).astype(bf16)
    allowed_low = low_place[...] <= q_place[...]
    allowed_up = up_place[...] <= q_place[half:, :]
    key_low, value_low = kv_low[:, :HD], kv_low[:, HD:]
    key_up, value_up = kv_up[:, :HD], kv_up[:, HD:]
    for h in range(heads):
        at = slice(h * HD, (h + 1) * HD)
        q, grad, log = queries[:, at], grads[:, at], logs[h]
        low = jnp.where(allowed_low, dot_t(q, key_low) * scale, NEGATIVE)
        up = jnp.where(allowed_up, dot_t(q[half:], key_up) * scale, NEGATIVE)
        probs_low, probs_up = jnp.exp(low - log), jnp.exp(up - log[half:])
        grad_low, grad_up = dot_t(grad, value_low), dot_t(grad[half:], value_up)
        along = jnp.sum(probs_low * grad_low, axis=-1, keepdims=True)
        along_up = along[half:] + jnp.sum(probs_up * grad_up, axis=-1, keepdims=True)
        along = jnp.concatenate([along[:half], along_up])
        score_low = (probs_low * (grad_low - along)).astype(bf16)
        score_up = (probs_up * (grad_up - along_up)).astype(bf16)
        part = dot(score_low, key_low)
        part = jnp.concatenate([part[:half], part[half:] + dot(score_up, key_up)]) * scale
        dq[:, at] = turn(part, cosines[...], -sines[...]).astype(bf16)
        terms = (
            (acc_low, slice(0, HD), t_dot(q, score_low)),
            (acc_up, slice(0, HD), t_dot(q[half:], score_up)),
            (acc_low, slice(HD, 2 * HD), t_dot(grad, probs_low.astype(bf16))),
            (acc_up, slice(HD, 2 * HD), t_dot(grad[half:], probs_up.astype(bf16))),
        )
        for acc, rows, term in terms:
            if h == 0:
                acc[rows] = term
            else:
                acc[rows] += term
    for s, block in enumerate((block0, block1, block2, block3)):
        block[...] = t_dot(normed[:, column_block(s, block.shape[0])], dq[...]).astype(bf16)
    for acc, first in ((acc_low, 0), (acc_up, half)):
        dk = (acc[:HD].T * scale).astype(bf16)
        dv = acc[HD:].T.astype(bf16)
        for i in range(pieces):
            dkv[i, first : first + half, :HD] = dk[i * half : (i + 1) * half]
            dkv[i, first : first + half, HD:] = dv[i * half : (i + 1) * half]


def sum_kernel(dq, cosines, sines, *refs):
    w_q, kvs, (parts, dkv, own, other) = refs[:4], refs[4:8], refs[8:]
    total = jnp.sum(parts[...].astype(f32), axis=0)
    dkv[:, :HD] = turn(total[:, :HD], cosines[...], -sines[...]).astype(bf16)
    dkv[:, HD:] = total[:, HD:].astype(bf16)
    quarter = own.shape[0] // 2
    for s in range(4):
        grad = dot_t(dq[...], w_q[s][...]) + dot_t(dkv[...], kvs[s][:, :WIDE])
        at = column_block(s, w_q[s].shape[0])
        own[:quarter, at] = grad[:quarter]
        other[:quarter, at] = grad[quarter : 2 * quarter]
        own[quarter:, at] = grad[2 * quarter : 3 * quarter]
        other[quarter:, at] = grad[3 * quarter :]


def stack_kernel(gate, up, down, late, out):
    del late
    out[0] = gate[...]
    out[1] = up[...]
    out[2] = down[...]


def small_grad_kernel(order, router_grad, gain_grad, late, out):
    del late
    row = lax.broadcasted_iota(jnp.int32, gain_grad.shape, 0)
    second = jnp.where(row == 1, gain_grad[...], 0.0).astype(bf16)
    small = router_grad[...] + t_dot(second, gain_picker())
    out[...] = t_dot(order[...], small.astype(bf16))


def input_kernel(both, own, received, midway_grad, gains, order, small, normed, dkv, out, *blocks):
    grad = own[...] + received[...]
    quarter = own.shape[0] // 2
    tokens = jnp.concatenate([both[:quarter], both[2 * quarter : 3 * quarter]])
    normal, inverse = normal_of(tokens.astype(f32))
    parts = in_three(norm_back(grad, normal, inverse, gains[0:1]))
    moved = dot_t(jnp.concatenate(parts), order[...])
    count = 2 * quarter
    out[...] = midway_grad[...] + (
        moved[:count] + (moved[count : 2 * count] + moved[2 * count :])
    )
    gain_grad = jnp.sum(grad * normal, axis=0, keepdims=True)
    row = lax.broadcasted_iota(jnp.int32, gains.shape, 0)
    gain_grad = jnp.where(row == 0, gain_grad, 0.0).astype(bf16)
    small = small[...] + t_dot(gain_grad, gain_picker())
    rows = blocks[0].shape[0]
    for s, block in enumerate(blocks):
        at = column_block(s, rows)
        block[:, :WIDE] = t_dot(normed[:, at], dkv[...]).astype(bf16)
        block[:, WIDE:] = small[at].astype(bf16)


def body(
    tokens,
    cotangent,
    pair_of,
    routes,
    attn_gain,
    moe_gain,
    w_query,
    w_key,
    w_value,
    w_out,
    w_router,
    w_gate,
    w_up,
    w_down,
):
    rows = tokens.shape[1]
    half = rows // 2
    width = tokens.shape[2]
    shard = w_query.shape[1]
    ctx_count = 16
    experts = w_router.shape[2]
    columns = w_gate.shape[3]
    per_group = H // KVH
    qw = per_group * HD
    scale = 1.0 / math.sqrt(HD)
    core = lax.axis_index("core")
    ylo, z, yhi = lax.axis_index("ylo"), lax.axis_index("z"), lax.axis_index("yhi")
    x = lax.axis_index("x")
    piece_rows = 2 * shard
    slots = experts * SLOTS
    own_tokens, cot = tokens[0], cotangent[0]

    def halves(matrix):
        return [matrix[:, : matrix.shape[1] // 2], matrix[:, matrix.shape[1] // 2 :]]

    small = jnp.concatenate([w_router[0], attn_gain[0][:, None], moe_gain[0][:, None]], axis=-1)
    small = jnp.pad(small, ((0, 0), (0, 128 - experts - 2)))
    query_halves, key_halves, value_halves = halves(w_query[0]), halves(w_key[0]), halves(w_value[0])
    pairs = [
        jnp.concatenate([k, v, small, q], axis=-1)
        for k, v, q in zip(key_halves, value_halves, query_halves)
    ]
    pieces = gather_pieces(pairs, yhi, core, ("core", "yhi"), SAME, OTHER)
    out_pieces = gather_pieces(
        halves(w_out[0]), yhi, yhi, ("ylo", "core", "yhi"), OUT_SAME, OUT_OTHER
    )
    other_tokens = partner(own_tokens)
    pieces, out_pieces, x, z, own_tokens, other_tokens, pair_of = together(
        pieces, out_pieces, x, z, own_tokens, other_tokens, pair_of
    )

    plane_rows = 16 * piece_rows
    plane = spread(pieces, 16, PLANE)
    both = jnp.concatenate(
        [own_tokens[:half], other_tokens[:half], own_tokens[half:], other_tokens[half:]]
    )
    order, out_order, level_order = order_matrix(16, x), order_matrix(8, x), level_order_matrix(z)
    (expert_shards_in,) = call(
        stack_kernel, [((3,) + w_gate.shape[1:], bf16)], w_gate[0], w_up[0], w_down[0], both
    )
    (
        plane, both, out_pieces, order, out_order, level_order, pair_of, expert_shards_in, chosen,
    ) = together(
        plane, both, out_pieces, order, out_order, level_order, pair_of, expert_shards_in,
        routes[0, 0],
    )

    plane = plane.reshape(plane_rows, -1)
    w_kvs = along("x", plane[:, : 3 * HD])
    wo = spread(out_pieces, 16, LEVEL)
    (both,) = call(order_kernel, [((2 * rows, width), bf16)], both, order)

    def two_cores(ctx):
        return jnp.stack([ctx + core, ctx + 1 - core], axis=-1).reshape(-1)

    ctx_here = (ylo * 4 + z) * 2
    q_place = places(pair_of, two_cores(ctx_here), rows, ctx_count)
    q_place = q_place.transpose(1, 0, 2).reshape(2 * rows, 1)
    key_place = places(
        pair_of, two_cores(jnp.arange(8, dtype=jnp.int32) * 2), rows, ctx_count
    )
    low_place, up_place = key_place[:, 0].reshape(1, -1), key_place[:, 1].reshape(1, -1)
    frequency = jnp.exp(jnp.arange(HD // 2, dtype=f32) * (-2.0 * math.log(ROPE_BASE) / HD))
    angles = q_place.astype(f32) * frequency[None, :]
    cosines, sines = jnp.cos(angles), jnp.sin(angles)
    cosines = jnp.concatenate([cosines, cosines], axis=-1)
    sines = jnp.concatenate([-sines, sines], axis=-1)
    w_q, w_kvs, wo, both, q_place, low_place, up_place, cosines, sines, chosen = together(
        plane[:, 3 * HD :], w_kvs, wo, both, q_place, low_place, up_place, cosines, sines, chosen
    )

    w_q = along("x", w_q)
    wo = along("z", wo.reshape(2, qw // 4, width // 2))
    normed, key_value, gains = call(
        keys_kernel,
        [((2 * rows, width), bf16), ((8, 2 * rows, 2 * HD), bf16), ((8, width), f32)],
        both,
        cosines,
        sines,
        *w_kvs,
    )
    all_kv = exchange(key_value, RING)
    small, moe_gains = call(
        small_kernel, [((width, 128), bf16), ((8, width), f32)], order, *w_kvs
    )
    (queries,) = call(
        query_kernel, [((2 * rows, qw), bf16)], normed, cosines, sines, *w_q, cost=LONG
    )
    lanes = jnp.arange(128, dtype=jnp.int32)
    hits = (chosen.T[:, :, None] == lanes[None, None, :]).astype(bf16)
    earlier = (lanes[:, None] > lanes[None, :]).astype(bf16)
    before = dot(earlier, jnp.sum(hits, axis=0))
    slot_index = jnp.sum(hits.astype(f32) * before[None], axis=-1).astype(jnp.int32)
    target = chosen.T * SLOTS + slot_index
    slot_row = jnp.arange(slots, dtype=jnp.int32)
    places_of = (target[:, :, None] == slot_row[None, None, :]).astype(bf16)
    placer_t = jnp.sum(places_of, axis=0)
    placer = placer_t.T
    (cot_rows,) = call(order_kernel, [((slots, width), bf16)], placer, cot)
    (
        queries, all_kv, expert_shards_in, small, moe_gains, cot_rows,
        hits, places_of, placer_t, placer, wo,
    ) = together(
        queries, all_kv, expert_shards_in, small, moe_gains, cot_rows,
        hits, places_of, placer_t, placer, wo,
    )
    expert_weights = lax.all_gather(expert_shards_in, CTX, axis=2, tiled=True)

    arrived_cot = to_owners(cot_rows.reshape(experts, SLOTS, width))
    sizes = dict(scale=scale, pieces=8, heads=per_group)
    keys = 8 * rows
    mixed, mixed_back, logs, kv_low, kv_up = call(
        functools.partial(attend_kernel, **sizes),
        [
            ((2 * rows, qw), bf16),
            ((2 * rows, qw), bf16),
            ((per_group, 2 * rows, 1), f32),
            ((keys, 2 * HD), bf16),
            ((keys, 2 * HD), bf16),
        ],
        queries,
        q_place,
        low_place,
        up_place,
        level_order,
        out_order,
        all_kv,
        scratch=[pltpu.VMEM((2 * rows, qw), bf16)],
    )

    branch_own, branch_other, wo = call(
        branch_kernel,
        [((rows, width), f32), ((rows, width), f32), ((2, qw, width // 2), bf16)],
        mixed,
        *wo,
    )
    sent, midway, moe_low, gates, gate_parts = call(
        route_kernel,
        [
            ((slots, width + 128), bf16),
            ((rows, width), f32),
            ((rows, width), bf16),
            ((rows, 128), f32),
            ((3, rows, slots), bf16),
        ],
        own_tokens,
        branch_own,
        partner(branch_other),
        small,
        moe_gains,
        hits,
        places_of,
        placer,
    )
    sent, arrived_cot = together(sent, arrived_cot)

    sent = to_owners(sent.reshape(experts, SLOTS, width + 128)).reshape(slots, width + 128)
    mine = core.reshape(1)
    expert_out, rows_grad, hidden, out_grad, gate_grad, up_grad = expert_call(
        mine,
        [sent, arrived_cot.reshape(slots, width)],
        expert_weights,
        [width, width + 128, columns, width, columns, columns],
    )
    rows_grad, gate_grad, up_grad = together(rows_grad, gate_grad, up_grad)

    home_grad = to_owners(rows_grad.reshape(experts, SLOTS, width + 128))
    expert_sums = expert_weights_grad(sent, out_grad, hidden, gate_grad, up_grad)
    home_grad, expert_sums = together(home_grad, expert_sums)
    expert_sums = lax.psum_scatter(expert_sums, RING, scatter_dimension=1, tiled=True)

    midway_grad, branch_low, gain_two_grad, router_grad = call(
        home_kernel,
        [((rows, width), f32), ((rows, width), bf16), ((8, width), f32), ((width, 128), f32)],
        placer_t,
        home_grad.reshape(slots, width + 128),
        midway,
        cot,
        moe_gains,
        hits,
        places_of,
        gates,
        small,
        moe_low,
    )
    branch, *out_w_grad = call(
        out_grad_kernel,
        [((2 * rows, width), bf16)] + [((2, qw // 4, width // 2), bf16)] * 4,
        mixed_back,
        branch_low,
        partner(branch_low),
    )
    branch, out_w_grad = together(branch, out_w_grad)
    out_w_grad = back_along_x(out_w_grad)

    dq, dkv, *q_w_grad = call(
        functools.partial(attend_back_kernel, **sizes),
        [((2 * rows, qw), bf16), ((8, 2 * rows, 2 * HD), bf16)]
        + [((plane_rows, qw), bf16)] * 4,
        branch,
        wo,
        level_order,
        queries,
        kv_low,
        kv_up,
        logs,
        q_place,
        low_place,
        up_place,
        cosines,
        sines,
        normed,
        scratch=[
            pltpu.VMEM((2 * rows, qw), bf16),
            pltpu.VMEM((2 * HD, keys), f32),
            pltpu.VMEM((2 * HD, keys), f32),
        ],
    )
    dkv, q_w_grad, late = together(dkv, q_w_grad, gain_two_grad)

    dkv = exchange(dkv, RING)
    q_w_grad = back_along_x(q_w_grad)
    (small_grad,) = call(
        small_grad_kernel, [((width, 128), f32)], order, router_grad, gain_two_grad, late
    )
    out_w_grad = added(out_w_grad, small_grad)
    dkv, out_w_grad, small_grad, expert_out, q_w_grad[1], q_w_grad[3] = together(
        dkv, out_w_grad, small_grad, expert_out, q_w_grad[1], q_w_grad[3]
    )

    returned = to_owners(expert_out.reshape(experts, SLOTS, width))
    dkv, normed_own, normed_other = call(
        sum_kernel,
        [((2 * rows, 2 * HD), bf16), ((rows, width), f32), ((rows, width), f32)],
        dq,
        cosines,
        sines,
        *w_q,
        *w_kvs,
        dkv,
    )
    input_grad, *kvs_grad = call(
        input_kernel,
        [((rows, width), f32)] + [((plane_rows, 3 * HD), bf16)] * 4,
        both,
        normed_own,
        partner(normed_other),
        midway_grad,
        gains,
        order,
        small_grad,
        normed,
        dkv,
    )
    kvs_grad, out_w_grad, input_grad = together(kvs_grad, out_w_grad, input_grad)

    out_w_grad = exchange(out_w_grad.reshape(16, piece_rows, width // 2), OUT_PLANE)
    kvs_grad = back_along_x(kvs_grad)
    (plane_grad,) = call(
        add_both_kernel, [((plane_rows, qw + 3 * HD), bf16)], *q_w_grad, *kvs_grad, cost=LONG
    )
    plane_grad, out_w_grad, returned = together(plane_grad, out_w_grad, returned)
    plane_grad = exchange(plane_grad.reshape(16, piece_rows, qw + 3 * HD), PLANE)

    (output,) = call(
        combine_kernel,
        [((rows, width), bf16)],
        midway,
        gate_parts,
        returned.reshape(slots, width),
    )

    def summed(pieces):
        return jnp.sum(pieces.astype(f32), axis=0)

    def expert_shards(grad):
        count = grad.shape[1] // 2
        kept = lax.dynamic_slice_in_dim(grad, core * count, count, axis=1)
        given = partner(lax.dynamic_slice_in_dim(grad, (1 - core) * count, count, axis=1))
        both = jnp.stack([pick(core, kept, given), pick(core, given, kept)], axis=1)
        return [both[i : i + 1].astype(f32) for i in range(3)]

    out_w_grad = scatter_pieces(
        summed(out_w_grad), yhi, yhi, ("ylo", "core", "yhi"), OUT_SAME, OUT_OTHER
    )
    w_gate_grad, w_up_grad, w_down_grad = expert_shards(expert_sums)
    plane_grad, out_w_grad, w_gate_grad, w_up_grad, w_down_grad, output = together(
        plane_grad, out_w_grad, w_gate_grad, w_up_grad, w_down_grad, output
    )
    plane_grad = scatter_pieces(summed(plane_grad), yhi, core, ("core", "yhi"), SAME, OTHER)
    plane_grad = plane_grad.reshape(shard, 2, -1)

    def joined(first, last):
        return plane_grad[:, :, first:last].reshape(1, shard, -1)

    small_grad = jnp.sum(plane_grad[None, :, :, qw + 2 * HD :], axis=2)

    return (
        output[None],
        input_grad[None],
        small_grad[:, :, experts],
        small_grad[:, :, experts + 1],
        joined(0, qw),
        joined(qw, qw + HD),
        joined(qw + HD, qw + 2 * HD),
        out_w_grad[None],
        small_grad[:, :, :experts],
        w_gate_grad,
        w_up_grad,
        w_down_grad,
    )


def solution(mesh):
    fine = Mesh(mesh.devices.reshape(2, 4, 2, 4, 2), AXES)
    seq = P(FSDP, CTX, None)
    vector = P(None, AXES)
    matrix = P(None, AXES, None)
    expert = P(None, FSDP, CTX, None)
    in_specs = (
        seq,
        seq,
        P(),
        P(None, FSDP, CTX, None),
        vector,
        vector,
        matrix,
        matrix,
        matrix,
        matrix,
        matrix,
        expert,
        expert,
        expert,
    )
    out_specs = (
        seq,
        seq,
        vector,
        vector,
        matrix,
        matrix,
        matrix,
        matrix,
        matrix,
        expert,
        expert,
        expert,
    )
    return jax.shard_map(body, mesh=fine, in_specs=in_specs, out_specs=out_specs, check_vma=False)
```

```python
import functools
import math

import jax
import jax.numpy as jnp
from jax import lax
from jax.experimental import pallas as pl
from jax.experimental.pallas import tpu as pltpu
from jax.sharding import Mesh
from jax.sharding import PartitionSpec as P

H = 12
KVH = 2
HD = 128
TOPK = 4

EPSILON = 1e-06
ROPE_BASE = 1000000.0
NEGATIVE = -1e30

AXES = ("ylo", "z", "core", "x", "yhi")
CTX = ("ylo", "z", "core")
FSDP = ("x", "yhi")
GROUPS = [
    [
        (((group ^ yhi) * 4 + z) * 2 + core) * 8 + x * 2 + yhi
        for x in range(4)
        for yhi in range(2)
        for core in range(2)
    ]
    for group in range(2)
    for z in range(4)
]
RING = ("ylo", "z")
PLANE = ("ylo", "z", "yhi")
LEVEL = ("yhi", "ylo", "x")
GROUPS = [
    [
        (((group ^ yhi) * 4 + z) * 2 + core) * 8 + x * 2 + yhi
        for x in range(4)
        for yhi in range(2)
        for core in range(2)
    ]
    for group in range(2)
    for z in range(4)
]
RING = ("ylo", "z")
ROWS_ORDER = ("ylo", "z", "yhi", "x")
OUT_ORDER = ("yhi", "z", "ylo", "x")
SLOTS = 40

bf16 = jnp.bfloat16
f32 = jnp.float32


def dot(left, right):
    return jnp.dot(left, right, preferred_element_type=f32)


def dot_t(left, right):
    return lax.dot_general(left, right, (((1,), (1,)), ((), ())), preferred_element_type=f32)


def t_dot(left, right):
    return lax.dot_general(left, right, (((0,), (0,)), ((), ())), preferred_element_type=f32)


def exchange(pieces, axes):
    return lax.all_to_all(pieces, axes, split_axis=0, concat_axis=0, tiled=True)


def to_owners(pieces):
    return lax.all_to_all(
        pieces, AXES, split_axis=0, concat_axis=0, axis_index_groups=GROUPS, tiled=True
    )


def spread(piece, count, axes):
    return exchange(jnp.broadcast_to(piece[None], (count,) + piece.shape), axes)


def after(value, earlier):
    return lax.optimization_barrier((value, earlier))[0]


def together(*values):
    return lax.optimization_barrier(values)


def partner(value):
    return lax.ppermute(value, "core", [(0, 1), (1, 0)])


def route(axes, sizes, move):
    pairs = []
    for source in range(math.prod(sizes)):
        rest, at = source, []
        for size in reversed(sizes):
            at.insert(0, rest % size)
            rest //= size
        target = 0
        for size, value in zip(sizes, move(*at)):
            target = target * size + value
        pairs.append((source, target))
    return pairs


SAME = route(("core", "yhi"), (2, 2), lambda c, h: (h, c))
OTHER = route(("core", "yhi"), (2, 2), lambda c, h: (1 - h, c))
OUT_SAME = route(("ylo", "core", "yhi"), (2, 2, 2), lambda j, c, h: (c, j, h))
OUT_OTHER = route(("ylo", "core", "yhi"), (2, 2, 2), lambda j, c, h: (c, j, 1 - h))


def back(pairs):
    return [(target, source) for source, target in pairs]


def pick(flag, if_zero, if_one):
    return jnp.where(flag == 0, if_zero, if_one)


def gather_pieces(pair, flag, key, axes, same, other):
    first = lax.ppermute(pick(flag, pair[0], pair[1]), axes, same)
    second = lax.ppermute(pick(flag, pair[1], pair[0]), axes, other)
    return pick(
        key, jnp.concatenate([first, second]), jnp.concatenate([second, first])
    )


def scatter_pieces(piece, flag, key, axes, same, other):
    count = piece.shape[0] // 2
    mine, rest = piece[:count], piece[count:]
    first = lax.ppermute(pick(key, mine, rest), axes, back(same))
    second = lax.ppermute(pick(key, rest, mine), axes, back(other))
    return pick(flag, jnp.concatenate([first, second], axis=-1), jnp.concatenate([second, first], axis=-1))


def along(axis, piece):
    return [piece] + [
        lax.ppermute(piece, axis, [(i, (i + s) % 4) for i in range(4)]) for s in (1, 2, 3)
    ]


def back_along_x(blocks):
    return [blocks[0]] + [
        lax.ppermute(blocks[s], "x", [(i, (i - s) % 4) for i in range(4)]) for s in (1, 2, 3)
    ]


def added(blocks, *late):
    (total,) = call(add_kernel, [(blocks[0].shape, bf16)], *blocks, *late, cost=LONG)
    return total


def sum_of(first, second, third, fourth):
    return (
        (first[...].astype(f32) + second[...].astype(f32))
        + (third[...].astype(f32) + fourth[...].astype(f32))
    ).astype(bf16)


def add_kernel(first, second, third, fourth, *refs):
    refs[-1][...] = sum_of(first, second, third, fourth)


def add_both_kernel(*refs):
    total = refs[8]
    count = refs[0].shape[1]
    total[:, :count] = sum_of(*refs[:4])
    total[:, count:] = sum_of(*refs[4:8])


def order_matrix(groups, x):
    index = jnp.arange(groups * 96, dtype=jnp.int32)
    turn_of, group, row = index // (groups * 24), index // 24 % groups, index % 24
    if groups == 8:
        group = group % 4 * 2 + group // 4
    own = group * 96 + (x - turn_of) % 4 * 24 + row
    return (index[:, None] == own[None, :]).astype(bf16)


def level_order_matrix(z):
    index = jnp.arange(8 * 96, dtype=jnp.int32)
    own = (z - index // 192) % 4 * 192 + index % 192
    return (index[:, None] == own[None, :]).astype(bf16)


def places(pair_of, ctx, row_count, ctx_count):
    half_size = row_count // 2
    pair = jnp.sum(
        jnp.where(ctx[:, None] == jnp.arange(ctx_count, dtype=jnp.int32)[None], pair_of[None], 0),
        axis=1,
    )
    block = jnp.stack([pair, 2 * ctx_count - 1 - pair], axis=1)
    return block[:, :, None] * half_size + jnp.arange(half_size, dtype=jnp.int32)[None, None]


def in_three(value):
    high = value.astype(bf16)
    rest = value - high.astype(f32)
    middle = rest.astype(bf16)
    return [high, middle, (rest - middle.astype(f32)).astype(bf16)]


def call(kernel, outs, *args, scratch=(), cost=None):
    def whole(shape):
        return pl.BlockSpec(shape, lambda i: (0,) * len(shape))

    return pl.pallas_call(
        kernel,
        out_shape=[jax.ShapeDtypeStruct(shape, dtype) for shape, dtype in outs],
        grid=(1,),
        in_specs=[whole(a.shape) for a in args],
        out_specs=[whole(shape) for shape, _ in outs],
        scratch_shapes=list(scratch),
        compiler_params=pltpu.CompilerParams(vmem_limit_bytes=ROOM),
        cost_estimate=COST if cost is None else cost,
    )(*args)


ROOM = 58 << 20
COST = pl.CostEstimate(flops=1 << 20, bytes_accessed=1 << 18, transcendentals=0)
LONG = pl.CostEstimate(flops=1 << 35, bytes_accessed=1 << 27, transcendentals=0)
WIDE = 2 * HD
EXPERTS = 16


def turn(vectors, cosines, sines):
    return vectors * cosines + pltpu.roll(vectors, HD // 2, axis=1) * sines


def gain_picker():
    row = lax.broadcasted_iota(jnp.int32, (8, 128), 0)
    column = lax.broadcasted_iota(jnp.int32, (8, 128), 1)
    return jnp.where((column == row + EXPERTS) & (row < 2), 1.0, 0.0).astype(bf16)


def normal_of(stream):
    inverse = lax.rsqrt(jnp.mean(stream * stream, axis=-1, keepdims=True) + EPSILON)
    return stream * inverse, inverse


def norm_back(grad, normal, inverse, gain):
    scaled = grad * gain
    return inverse * (scaled - normal * jnp.mean(scaled * normal, axis=-1, keepdims=True))


def column_block(s, count):
    return slice(s * count, (s + 1) * count)


def order_kernel(rows, order, out):
    out[...] = dot(rows[...], order[...]).astype(bf16)


def keys_kernel(both, cosines, sines, *refs):
    kvs, (normed, key_value, gains) = refs[:4], refs[4:]
    count = kvs[0].shape[0]
    for s in range(4):
        gains[:, column_block(s, count)] = dot_t(gain_picker(), kvs[s][:, WIDE:])
    normal, _ = normal_of(both[...].astype(f32))
    normed[...] = (normal * gains[0:1]).astype(bf16)
    kv = dot(normed[:, column_block(0, count)], kvs[0][:, :WIDE])
    for s in range(1, 4):
        kv = kv + dot(normed[:, column_block(s, count)], kvs[s][:, :WIDE])
    keys = turn(kv[:, :HD], cosines[...], sines[...]).astype(bf16)
    values = kv[:, HD:].astype(bf16)
    for i in range(key_value.shape[0]):
        key_value[i, :, :HD] = keys
        key_value[i, :, HD:] = values


def small_kernel(order, kvs0, kvs1, kvs2, kvs3, small, gains):
    count = kvs0.shape[0]
    total = jnp.zeros(small.shape, f32)
    for s, kvs in enumerate((kvs0, kvs1, kvs2, kvs3)):
        total = total + dot(order[:, column_block(s, count)], kvs[:, WIDE:])
    small[...] = total.astype(bf16)
    gains[...] = dot_t(gain_picker(), small[...])


def query_kernel(normed, cosines, sines, w_q0, w_q1, w_q2, w_q3, queries):
    w_q = (w_q0, w_q1, w_q2, w_q3)
    count = w_q0.shape[0]
    for h in range(queries.shape[1] // HD):
        at = column_block(h, HD)
        q = dot(normed[:, column_block(0, count)], w_q0[:, at])
        for s in range(1, 4):
            q = q + dot(normed[:, column_block(s, count)], w_q[s][:, at])
        queries[:, at] = turn(q, cosines[...], sines[...]).astype(bf16)


def attend_kernel(
    queries,
    q_place,
    low_place,
    up_place,
    order,
    order_back,
    kv,
    ordered,
    ordered_back,
    logs,
    kv_low,
    kv_up,
    mixed,
    *,
    scale,
    pieces,
    heads,
):
    half = kv.shape[1] // 2
    for i in range(pieces):
        kv_low[i * half : (i + 1) * half, :] = kv[i, :half]
        kv_up[i * half : (i + 1) * half, :] = kv[i, half:]
    allowed_low = low_place[...] <= q_place[...]
    allowed_up = up_place[...] <= q_place[half:, :]
    for h in range(heads):
        at = slice(h * HD, (h + 1) * HD)
        q = queries[:, at]
        low = jnp.where(allowed_low, dot_t(q, kv_low[:, :HD]) * scale, NEGATIVE)
        up = jnp.where(allowed_up, dot_t(q[half:], kv_up[:, :HD]) * scale, NEGATIVE)
        first, second = low[:half], low[half:]
        top = jnp.max(first, axis=-1, keepdims=True)
        weight = jnp.exp(first - top)
        total = jnp.sum(weight, axis=-1, keepdims=True)
        probs = (weight / total).astype(bf16)
        mixed[:half, at] = dot(probs, kv_low[:, HD:]).astype(bf16)
        logs[h, :half, :] = top + jnp.log(total)
        top = jnp.maximum(
            jnp.max(second, axis=-1, keepdims=True), jnp.max(up, axis=-1, keepdims=True)
        )
        weight, weight_up = jnp.exp(second - top), jnp.exp(up - top)
        total = jnp.sum(weight, axis=-1, keepdims=True) + jnp.sum(
            weight_up, axis=-1, keepdims=True
        )
        mixed[half:, at] = (
            dot((weight / total).astype(bf16), kv_low[:, HD:])
            + dot((weight_up / total).astype(bf16), kv_up[:, HD:])
        ).astype(bf16)
        logs[h, half:, :] = top + jnp.log(total)
    ordered[...] = dot(mixed[...], order[...]).astype(bf16)
    ordered_back[...] = dot(mixed[...], order_back[...]).astype(bf16)


def branch_kernel(mixed, w_out0, w_out1, w_out2, w_out3, own, other, w_out):
    quarter = mixed.shape[0] // 4
    count, columns = w_out0.shape[1:]
    for s, part in enumerate((w_out0, w_out1, w_out2, w_out3)):
        w_out[:, column_block(s, count)] = part[...]
    for k in range(2):
        part = dot(mixed[...], w_out[k])
        at = slice(k * columns, (k + 1) * columns)
        own[:quarter, at] = part[:quarter]
        other[:quarter, at] = part[quarter : 2 * quarter]
        own[quarter:, at] = part[2 * quarter : 3 * quarter]
        other[quarter:, at] = part[3 * quarter :]


def route_kernel(
    tokens,
    own,
    received,
    small,
    gains,
    hits,
    places_of,
    placer,
    sent,
    midway,
    moe_low,
    gates,
    parts,
):
    middle = tokens[...].astype(f32) + (own[...] + received[...])
    midway[...] = middle
    normal, _ = normal_of(middle)
    moe = (normal * gains[1:2]).astype(bf16)
    moe_low[...] = moe
    sent[:, : moe.shape[1]] = dot(placer[...], moe).astype(bf16)
    logits = dot(moe, small[...])
    picked = [
        jnp.sum(hits[k].astype(f32) * logits, axis=-1, keepdims=True) for k in range(TOPK)
    ]
    top = picked[0]
    for value in picked[1:]:
        top = jnp.maximum(top, value)
    weights = [jnp.exp(value - top) for value in picked]
    total = weights[0]
    for value in weights[1:]:
        total = total + value
    lane = lax.broadcasted_iota(jnp.int32, gates.shape, 1)
    gate_at = jnp.zeros(places_of.shape[1:], f32)
    kept = jnp.zeros(gates.shape, f32)
    for k in range(TOPK):
        gate = weights[k] / total
        kept = jnp.where(lane == k, gate, kept)
        gate_at = gate_at + places_of[k].astype(f32) * gate
    gates[...] = kept
    block = jnp.zeros((sent.shape[0], 128), f32)
    for i, part in enumerate(in_three(gate_at)):
        parts[i] = part
        block = block + t_dot(part, jnp.where(lane == i, 1.0, 0.0).astype(bf16))
    sent[:, moe.shape[1] :] = block.astype(bf16)


def expert_kernel(
    core, sent, cot, weights, out, rows_grad, hidden, out_grad, gate_grad, up_grad, held, sems
):
    copies = [
        pltpu.make_async_copy(weights.at[m, core[0]], held.at[m], sems.at[m]) for m in range(3)
    ]
    for copy in copies:
        copy.start()
    width = out.shape[1]
    gates = jnp.sum(sent[:, width:].astype(f32), axis=-1, keepdims=True)
    out_grad[...] = (gates * cot[...].astype(f32)).astype(bf16)
    rows = sent[:, :width]
    copies[0].wait()
    gate_pre = dot(rows, held[0])
    copies[1].wait()
    up_pre = dot(rows, held[1])
    sigmoid = 1.0 / (1.0 + jnp.exp(-gate_pre))
    silu = gate_pre * sigmoid
    low = (silu * up_pre).astype(bf16)
    hidden[...] = low
    copies[2].wait()
    hidden_grad = dot(out_grad[...], held[2])
    gate_low = (hidden_grad * up_pre * sigmoid * (1.0 + gate_pre * (1.0 - sigmoid))).astype(bf16)
    up_low = (hidden_grad * silu).astype(bf16)
    gate_grad[...] = gate_low
    up_grad[...] = up_low
    rows_grad[:, :width] = (dot_t(gate_low, held[0]) + dot_t(up_low, held[1])).astype(bf16)
    result = dot_t(low, held[2]).astype(bf16)
    out[...] = result
    grads = in_three(
        jnp.sum(cot[...].astype(f32) * result.astype(f32), axis=-1, keepdims=True)
    )
    lane = lax.broadcasted_iota(jnp.int32, (cot.shape[0], 128), 1)
    block = jnp.zeros(lane.shape, f32)
    for i, part in enumerate(grads):
        block = jnp.where(lane == i, part.astype(f32), block)
    rows_grad[:, width:] = block.astype(bf16)


def expert_call(core, arrays, weights, outs):
    rows = arrays[0].shape[0]

    def whole(columns):
        return pl.BlockSpec(
            (rows, columns), lambda i, core: (0, 0), pipeline_mode=pl.Buffered(1)
        )

    return pl.pallas_call(
        expert_kernel,
        out_shape=[jax.ShapeDtypeStruct((rows, columns), bf16) for columns in outs],
        grid_spec=pltpu.PrefetchScalarGridSpec(
            num_scalar_prefetch=1,
            grid=(1,),
            in_specs=[whole(a.shape[1]) for a in arrays] + [pl.BlockSpec(memory_space=pltpu.HBM)],
            out_specs=[whole(columns) for columns in outs],
            scratch_shapes=[
                pltpu.VMEM((3,) + weights.shape[2:], bf16),
                pltpu.SemaphoreType.DMA((3,)),
            ],
        ),
        compiler_params=pltpu.CompilerParams(vmem_limit_bytes=ROOM),
        cost_estimate=COST,
    )(core, *arrays, weights)


def weights_kernel(sent, out_grad, hidden, gate_grad, up_grad, sums):
    rows = sent[...]
    sums[0] = t_dot(rows, gate_grad[...]).astype(bf16)
    sums[1] = t_dot(rows, up_grad[...]).astype(bf16)
    sums[2] = t_dot(out_grad[...], hidden[...]).astype(bf16)


def expert_weights_grad(sent, out_grad, hidden, gate_grad, up_grad, block=256):
    count, width = out_grad.shape
    columns = hidden.shape[1]
    part = pl.BlockSpec((count, block), lambda i: (0, i))
    whole = pl.BlockSpec((count, columns), lambda i: (0, 0), pipeline_mode=pl.Buffered(1))
    return pl.pallas_call(
        weights_kernel,
        out_shape=jax.ShapeDtypeStruct((3, width, columns), bf16),
        grid=(width // block,),
        in_specs=[part, part, whole, whole, whole],
        out_specs=pl.BlockSpec((3, block, columns), lambda i: (0, i, 0)),
        compiler_params=pltpu.CompilerParams(vmem_limit_bytes=ROOM),
        cost_estimate=COST,
    )(sent, out_grad, hidden, gate_grad, up_grad)


def combine_kernel(midway, parts, returned, output):
    rows = returned[...]
    output[...] = (
        midway[...] + (dot(parts[0], rows) + (dot(parts[1], rows) + dot(parts[2], rows)))
    ).astype(bf16)


def home_kernel(
    placer_t,
    home,
    midway,
    cot,
    gains,
    hits,
    places_of,
    gates,
    small,
    moe_low,
    midway_grad,
    branch_low,
    gain_grad,
    router_grad,
):
    width = midway.shape[1]
    lane = lax.broadcasted_iota(jnp.int32, gates.shape, 1)
    gate, gate_grad = [], []
    mean = jnp.zeros((gates.shape[0], 1), f32)
    for k in range(TOPK):
        gate.append(jnp.sum(jnp.where(lane == k, gates[...], 0.0), axis=-1, keepdims=True))
        gate_grad.append(
            jnp.sum(dot(places_of[k], home[:, width:]), axis=-1, keepdims=True)
        )
        mean = mean + gate[k] * gate_grad[k]
    logit_grad = jnp.zeros(gates.shape, f32)
    for k in range(TOPK):
        logit_grad = logit_grad + hits[k].astype(f32) * (gate[k] * (gate_grad[k] - mean))
    logit_grad = logit_grad.astype(bf16)
    router_grad[...] = t_dot(moe_low[...], logit_grad)
    grad = dot(placer_t[...], home[:, :width]) + dot_t(logit_grad, small[...])
    normal, inverse = normal_of(midway[...])
    result = cot[...].astype(f32) + norm_back(grad, normal, inverse, gains[1:2])
    midway_grad[...] = result
    branch_low[...] = result.astype(bf16)
    gain_grad[...] = jnp.broadcast_to(
        jnp.sum(grad * normal, axis=0, keepdims=True), gain_grad.shape
    )


def out_grad_kernel(mixed, own, other, branch, *blocks):
    quarter = own.shape[0] // 2
    branch[:quarter] = own[:quarter]
    branch[quarter : 2 * quarter] = other[:quarter]
    branch[2 * quarter : 3 * quarter] = own[quarter:]
    branch[3 * quarter :] = other[quarter:]
    count, columns = blocks[0].shape[1:]
    for k in range(2):
        grad = t_dot(mixed[...], branch[:, column_block(k, columns)]).astype(bf16)
        for s in range(4):
            blocks[s][k] = grad[column_block(s, count)]


def attend_back_kernel(
    branch,
    w_out,
    order,
    queries,
    kv_low,
    kv_up,
    logs,
    q_place,
    low_place,
    up_place,
    cosines,
    sines,
    normed,
    dq,
    dkv,
    block0,
    block1,
    block2,
    block3,
    grads,
    acc_low,
    acc_up,
    *,
    scale,
    pieces,
    heads,
):
    half = queries.shape[0] // 2
    columns = w_out.shape[2]
    ordered = dot_t(branch[:, :columns], w_out[0]) + dot_t(branch[:, columns:], w_out[1])
    grads[...] = dot_t(ordered.astype(bf16), order[...]).astype(bf16)
    allowed_low = low_place[...] <= q_place[...]
    allowed_up = up_place[...] <= q_place[half:, :]
    key_low, value_low = kv_low[:, :HD], kv_low[:, HD:]
    key_up, value_up = kv_up[:, :HD], kv_up[:, HD:]
    for h in range(heads):
        at = slice(h * HD, (h + 1) * HD)
        q, grad, log = queries[:, at], grads[:, at], logs[h]
        low = jnp.where(allowed_low, dot_t(q, key_low) * scale, NEGATIVE)
        up = jnp.where(allowed_up, dot_t(q[half:], key_up) * scale, NEGATIVE)
        probs_low, probs_up = jnp.exp(low - log), jnp.exp(up - log[half:])
        grad_low, grad_up = dot_t(grad, value_low), dot_t(grad[half:], value_up)
        along = jnp.sum(probs_low * grad_low, axis=-1, keepdims=True)
        along_up = along[half:] + jnp.sum(probs_up * grad_up, axis=-1, keepdims=True)
        along = jnp.concatenate([along[:half], along_up])
        score_low = (probs_low * (grad_low - along)).astype(bf16)
        score_up = (probs_up * (grad_up - along_up)).astype(bf16)
        part = dot(score_low, key_low)
        part = jnp.concatenate([part[:half], part[half:] + dot(score_up, key_up)]) * scale
        dq[:, at] = turn(part, cosines[...], -sines[...]).astype(bf16)
        terms = (
            (acc_low, slice(0, HD), t_dot(q, score_low)),
            (acc_up, slice(0, HD), t_dot(q[half:], score_up)),
            (acc_low, slice(HD, 2 * HD), t_dot(grad, probs_low.astype(bf16))),
            (acc_up, slice(HD, 2 * HD), t_dot(grad[half:], probs_up.astype(bf16))),
        )
        for acc, rows, term in terms:
            if h == 0:
                acc[rows] = term
            else:
                acc[rows] += term
    for s, block in enumerate((block0, block1, block2, block3)):
        block[...] = t_dot(normed[:, column_block(s, block.shape[0])], dq[...]).astype(bf16)
    for acc, first in ((acc_low, 0), (acc_up, half)):
        dk = (acc[:HD].T * scale).astype(bf16)
        dv = acc[HD:].T.astype(bf16)
        for i in range(pieces):
            dkv[i, first : first + half, :HD] = dk[i * half : (i + 1) * half]
            dkv[i, first : first + half, HD:] = dv[i * half : (i + 1) * half]


def sum_kernel(dq, cosines, sines, *refs):
    w_q, kvs, (parts, dkv, own, other) = refs[:4], refs[4:8], refs[8:]
    total = jnp.sum(parts[...].astype(f32), axis=0)
    dkv[:, :HD] = turn(total[:, :HD], cosines[...], -sines[...]).astype(bf16)
    dkv[:, HD:] = total[:, HD:].astype(bf16)
    quarter = own.shape[0] // 2
    for s in range(4):
        grad = dot_t(dq[...], w_q[s][...]) + dot_t(dkv[...], kvs[s][:, :WIDE])
        at = column_block(s, w_q[s].shape[0])
        own[:quarter, at] = grad[:quarter]
        other[:quarter, at] = grad[quarter : 2 * quarter]
        own[quarter:, at] = grad[2 * quarter : 3 * quarter]
        other[quarter:, at] = grad[3 * quarter :]


def stack_kernel(gate, up, down, late, out):
    del late
    out[0] = gate[...]
    out[1] = up[...]
    out[2] = down[...]


def small_grad_kernel(order, router_grad, gain_grad, late, out):
    del late
    row = lax.broadcasted_iota(jnp.int32, gain_grad.shape, 0)
    second = jnp.where(row == 1, gain_grad[...], 0.0).astype(bf16)
    small = router_grad[...] + t_dot(second, gain_picker())
    out[...] = t_dot(order[...], small.astype(bf16))


def input_kernel(both, own, received, midway_grad, gains, order, small, normed, dkv, out, *blocks):
    grad = own[...] + received[...]
    quarter = own.shape[0] // 2
    tokens = jnp.concatenate([both[:quarter], both[2 * quarter : 3 * quarter]])
    normal, inverse = normal_of(tokens.astype(f32))
    parts = in_three(norm_back(grad, normal, inverse, gains[0:1]))
    moved = dot_t(jnp.concatenate(parts), order[...])
    count = 2 * quarter
    out[...] = midway_grad[...] + (
        moved[:count] + (moved[count : 2 * count] + moved[2 * count :])
    )
    gain_grad = jnp.sum(grad * normal, axis=0, keepdims=True)
    row = lax.broadcasted_iota(jnp.int32, gains.shape, 0)
    gain_grad = jnp.where(row == 0, gain_grad, 0.0).astype(bf16)
    small = small[...] + t_dot(gain_grad, gain_picker())
    rows = blocks[0].shape[0]
    for s, block in enumerate(blocks):
        at = column_block(s, rows)
        block[:, :WIDE] = t_dot(normed[:, at], dkv[...]).astype(bf16)
        block[:, WIDE:] = small[at].astype(bf16)


def body(
    tokens,
    cotangent,
    pair_of,
    routes,
    attn_gain,
    moe_gain,
    w_query,
    w_key,
    w_value,
    w_out,
    w_router,
    w_gate,
    w_up,
    w_down,
):
    rows = tokens.shape[1]
    half = rows // 2
    width = tokens.shape[2]
    shard = w_query.shape[1]
    ctx_count = 16
    experts = w_router.shape[2]
    columns = w_gate.shape[3]
    per_group = H // KVH
    qw = per_group * HD
    scale = 1.0 / math.sqrt(HD)
    core = lax.axis_index("core")
    ylo, z, yhi = lax.axis_index("ylo"), lax.axis_index("z"), lax.axis_index("yhi")
    x = lax.axis_index("x")
    piece_rows = 2 * shard
    slots = experts * SLOTS
    own_tokens, cot = tokens[0], cotangent[0]

    def halves(matrix):
        return [matrix[:, : matrix.shape[1] // 2], matrix[:, matrix.shape[1] // 2 :]]

    small = jnp.concatenate([w_router[0], attn_gain[0][:, None], moe_gain[0][:, None]], axis=-1)
    small = jnp.pad(small, ((0, 0), (0, 128 - experts - 2)))
    query_halves, key_halves, value_halves = halves(w_query[0]), halves(w_key[0]), halves(w_value[0])
    pairs = [
        jnp.concatenate([k, v, small, q], axis=-1)
        for k, v, q in zip(key_halves, value_halves, query_halves)
    ]
    pieces = gather_pieces(pairs, yhi, core, ("core", "yhi"), SAME, OTHER)
    out_pieces = gather_pieces(
        halves(w_out[0]), yhi, yhi, ("ylo", "core", "yhi"), OUT_SAME, OUT_OTHER
    )
    other_tokens = partner(own_tokens)
    pieces, out_pieces, x, z, own_tokens, other_tokens, pair_of = together(
        pieces, out_pieces, x, z, own_tokens, other_tokens, pair_of
    )

    plane_rows = 16 * piece_rows
    plane = spread(pieces, 16, PLANE)
    both = jnp.concatenate(
        [own_tokens[:half], other_tokens[:half], own_tokens[half:], other_tokens[half:]]
    )
    order, out_order, level_order = order_matrix(16, x), order_matrix(8, x), level_order_matrix(z)
    (expert_shards_in,) = call(
        stack_kernel, [((3,) + w_gate.shape[1:], bf16)], w_gate[0], w_up[0], w_down[0], both
    )
    (
        plane, both, out_pieces, order, out_order, level_order, pair_of, expert_shards_in, chosen,
    ) = together(
        plane, both, out_pieces, order, out_order, level_order, pair_of, expert_shards_in,
        routes[0, 0],
    )

    plane = plane.reshape(plane_rows, -1)
    w_kvs = along("x", plane[:, : 3 * HD])
    wo = spread(out_pieces, 16, LEVEL)
    (both,) = call(order_kernel, [((2 * rows, width), bf16)], both, order)

    def two_cores(ctx):
        return jnp.stack([ctx + core, ctx + 1 - core], axis=-1).reshape(-1)

    ctx_here = (ylo * 4 + z) * 2
    q_place = places(pair_of, two_cores(ctx_here), rows, ctx_count)
    q_place = q_place.transpose(1, 0, 2).reshape(2 * rows, 1)
    key_place = places(
        pair_of, two_cores(jnp.arange(8, dtype=jnp.int32) * 2), rows, ctx_count
    )
    low_place, up_place = key_place[:, 0].reshape(1, -1), key_place[:, 1].reshape(1, -1)
    frequency = jnp.exp(jnp.arange(HD // 2, dtype=f32) * (-2.0 * math.log(ROPE_BASE) / HD))
    angles = q_place.astype(f32) * frequency[None, :]
    cosines, sines = jnp.cos(angles), jnp.sin(angles)
    cosines = jnp.concatenate([cosines, cosines], axis=-1)
    sines = jnp.concatenate([-sines, sines], axis=-1)
    w_q, w_kvs, wo, both, q_place, low_place, up_place, cosines, sines, chosen = together(
        plane[:, 3 * HD :], w_kvs, wo, both, q_place, low_place, up_place, cosines, sines, chosen
    )

    w_q = along("x", w_q)
    wo = along("z", wo.reshape(2, qw // 4, width // 2))
    normed, key_value, gains = call(
        keys_kernel,
        [((2 * rows, width), bf16), ((8, 2 * rows, 2 * HD), bf16), ((8, width), f32)],
        both,
        cosines,
        sines,
        *w_kvs,
    )
    all_kv = exchange(key_value, RING)
    small, moe_gains = call(
        small_kernel, [((width, 128), bf16), ((8, width), f32)], order, *w_kvs
    )
    (queries,) = call(
        query_kernel, [((2 * rows, qw), bf16)], normed, cosines, sines, *w_q, cost=LONG
    )
    lanes = jnp.arange(128, dtype=jnp.int32)
    hits = (chosen.T[:, :, None] == lanes[None, None, :]).astype(bf16)
    earlier = (lanes[:, None] > lanes[None, :]).astype(bf16)
    before = dot(earlier, jnp.sum(hits, axis=0))
    slot_index = jnp.sum(hits.astype(f32) * before[None], axis=-1).astype(jnp.int32)
    target = chosen.T * SLOTS + slot_index
    slot_row = jnp.arange(slots, dtype=jnp.int32)
    places_of = (target[:, :, None] == slot_row[None, None, :]).astype(bf16)
    placer_t = jnp.sum(places_of, axis=0)
    placer = placer_t.T
    (cot_rows,) = call(order_kernel, [((slots, width), bf16)], placer, cot)
    (
        queries, all_kv, expert_shards_in, small, moe_gains, cot_rows,
        hits, places_of, placer_t, placer, wo,
    ) = together(
        queries, all_kv, expert_shards_in, small, moe_gains, cot_rows,
        hits, places_of, placer_t, placer, wo,
    )
    expert_weights = lax.all_gather(expert_shards_in, CTX, axis=2, tiled=True)

    arrived_cot = to_owners(cot_rows.reshape(experts, SLOTS, width))
    sizes = dict(scale=scale, pieces=8, heads=per_group)
    keys = 8 * rows
    mixed, mixed_back, logs, kv_low, kv_up = call(
        functools.partial(attend_kernel, **sizes),
        [
            ((2 * rows, qw), bf16),
            ((2 * rows, qw), bf16),
            ((per_group, 2 * rows, 1), f32),
            ((keys, 2 * HD), bf16),
            ((keys, 2 * HD), bf16),
        ],
        queries,
        q_place,
        low_place,
        up_place,
        level_order,
        out_order,
        all_kv,
        scratch=[pltpu.VMEM((2 * rows, qw), bf16)],
    )

    branch_own, branch_other, wo = call(
        branch_kernel,
        [((rows, width), f32), ((rows, width), f32), ((2, qw, width // 2), bf16)],
        mixed,
        *wo,
    )
    sent, midway, moe_low, gates, gate_parts = call(
        route_kernel,
        [
            ((slots, width + 128), bf16),
            ((rows, width), f32),
            ((rows, width), bf16),
            ((rows, 128), f32),
            ((3, rows, slots), bf16),
        ],
        own_tokens,
        branch_own,
        partner(branch_other),
        small,
        moe_gains,
        hits,
        places_of,
        placer,
    )
    sent, arrived_cot = together(sent, arrived_cot)

    sent = to_owners(sent.reshape(experts, SLOTS, width + 128)).reshape(slots, width + 128)
    mine = core.reshape(1)
    expert_out, rows_grad, hidden, out_grad, gate_grad, up_grad = expert_call(
        mine,
        [sent, arrived_cot.reshape(slots, width)],
        expert_weights,
        [width, width + 128, columns, width, columns, columns],
    )
    rows_grad, gate_grad, up_grad = together(rows_grad, gate_grad, up_grad)

    home_grad = to_owners(rows_grad.reshape(experts, SLOTS, width + 128))
    expert_sums = expert_weights_grad(sent, out_grad, hidden, gate_grad, up_grad)
    home_grad, expert_sums = together(home_grad, expert_sums)
    expert_sums = lax.psum_scatter(expert_sums, RING, scatter_dimension=1, tiled=True)

    midway_grad, branch_low, gain_two_grad, router_grad = call(
        home_kernel,
        [((rows, width), f32), ((rows, width), bf16), ((8, width), f32), ((width, 128), f32)],
        placer_t,
        home_grad.reshape(slots, width + 128),
        midway,
        cot,
        moe_gains,
        hits,
        places_of,
        gates,
        small,
        moe_low,
    )
    branch, *out_w_grad = call(
        out_grad_kernel,
        [((2 * rows, width), bf16)] + [((2, qw // 4, width // 2), bf16)] * 4,
        mixed_back,
        branch_low,
        partner(branch_low),
    )
    branch, out_w_grad = together(branch, out_w_grad)
    out_w_grad = back_along_x(out_w_grad)

    dq, dkv, *q_w_grad = call(
        functools.partial(attend_back_kernel, **sizes),
        [((2 * rows, qw), bf16), ((8, 2 * rows, 2 * HD), bf16)]
        + [((plane_rows, qw), bf16)] * 4,
        branch,
        wo,
        level_order,
        queries,
        kv_low,
        kv_up,
        logs,
        q_place,
        low_place,
        up_place,
        cosines,
        sines,
        normed,
        scratch=[
            pltpu.VMEM((2 * rows, qw), bf16),
            pltpu.VMEM((2 * HD, keys), f32),
            pltpu.VMEM((2 * HD, keys), f32),
        ],
    )
    dkv, q_w_grad, late = together(dkv, q_w_grad, gain_two_grad)

    dkv = exchange(dkv, RING)
    q_w_grad = back_along_x(q_w_grad)
    (small_grad,) = call(
        small_grad_kernel, [((width, 128), f32)], order, router_grad, gain_two_grad, late
    )
    out_w_grad = added(out_w_grad, small_grad)
    dkv, out_w_grad, small_grad, expert_out, q_w_grad = together(
        dkv, out_w_grad, small_grad, expert_out, q_w_grad
    )

    returned = to_owners(expert_out.reshape(experts, SLOTS, width))
    dkv, normed_own, normed_other = call(
        sum_kernel,
        [((2 * rows, 2 * HD), bf16), ((rows, width), f32), ((rows, width), f32)],
        dq,
        cosines,
        sines,
        *w_q,
        *w_kvs,
        dkv,
    )
    input_grad, *kvs_grad = call(
        input_kernel,
        [((rows, width), f32)] + [((plane_rows, 3 * HD), bf16)] * 4,
        both,
        normed_own,
        partner(normed_other),
        midway_grad,
        gains,
        order,
        small_grad,
        normed,
        dkv,
    )
    kvs_grad, input_grad = together(kvs_grad, input_grad)

    kvs_grad = back_along_x(kvs_grad)
    (plane_grad,) = call(
        add_both_kernel, [((plane_rows, qw + 3 * HD), bf16)], *q_w_grad, *kvs_grad
    )
    out_w_grad = out_w_grad.reshape(2, 8, piece_rows, width // 2).transpose(1, 0, 2, 3)
    plane_grad = jnp.concatenate(
        [
            plane_grad.reshape(16, piece_rows, qw + 3 * HD),
            out_w_grad.reshape(16, piece_rows, width // 2),
        ],
        axis=-1,
    )
    plane_grad, returned = together(plane_grad, returned)
    plane_grad = exchange(plane_grad, PLANE)

    (output,) = call(
        combine_kernel,
        [((rows, width), bf16)],
        midway,
        gate_parts,
        returned.reshape(slots, width),
    )

    def summed(pieces):
        return jnp.sum(pieces.astype(f32), axis=0)

    def expert_shards(grad):
        count = grad.shape[1] // 2
        kept = lax.dynamic_slice_in_dim(grad, core * count, count, axis=1)
        given = partner(lax.dynamic_slice_in_dim(grad, (1 - core) * count, count, axis=1))
        both = jnp.stack([pick(core, kept, given), pick(core, given, kept)], axis=1)
        return [both[i : i + 1].astype(f32) for i in range(3)]

    w_gate_grad, w_up_grad, w_down_grad = expert_shards(expert_sums)
    plane_grad, w_gate_grad, w_up_grad, w_down_grad, output = together(
        plane_grad, w_gate_grad, w_up_grad, w_down_grad, output
    )
    plane_grad = summed(plane_grad)
    out_w_grad = scatter_pieces(
        plane_grad[:, qw + 3 * HD :], yhi, yhi, ("ylo", "core", "yhi"), OUT_SAME, OUT_OTHER
    )
    plane_grad = scatter_pieces(
        plane_grad[:, : qw + 3 * HD], yhi, core, ("core", "yhi"), SAME, OTHER
    )
    plane_grad = plane_grad.reshape(shard, 2, -1)

    def joined(first, last):
        return plane_grad[:, :, first:last].reshape(1, shard, -1)

    small_grad = jnp.sum(plane_grad[None, :, :, qw + 2 * HD :], axis=2)

    return (
        output[None],
        input_grad[None],
        small_grad[:, :, experts],
        small_grad[:, :, experts + 1],
        joined(0, qw),
        joined(qw, qw + HD),
        joined(qw + HD, qw + 2 * HD),
        out_w_grad[None],
        small_grad[:, :, :experts],
        w_gate_grad,
        w_up_grad,
        w_down_grad,
    )


def solution(mesh):
    fine = Mesh(mesh.devices.reshape(2, 4, 2, 4, 2), AXES)
    seq = P(FSDP, CTX, None)
    vector = P(None, AXES)
    matrix = P(None, AXES, None)
    expert = P(None, FSDP, CTX, None)
    in_specs = (
        seq,
        seq,
        P(),
        P(None, FSDP, CTX, None),
        vector,
        vector,
        matrix,
        matrix,
        matrix,
        matrix,
        matrix,
        expert,
        expert,
        expert,
    )
    out_specs = (
        seq,
        seq,
        vector,
        vector,
        matrix,
        matrix,
        matrix,
        matrix,
        matrix,
        expert,
        expert,
        expert,
    )
    return jax.shard_map(body, mesh=fine, in_specs=in_specs, out_specs=out_specs, check_vma=False)
```

```python
import functools
import math

import jax
import jax.numpy as jnp
from jax import lax
from jax.experimental import pallas as pl
from jax.experimental.pallas import tpu as pltpu
from jax.sharding import Mesh
from jax.sharding import PartitionSpec as P

H = 12
KVH = 2
HD = 128
TOPK = 4

EPSILON = 1e-06
ROPE_BASE = 1000000.0
NEGATIVE = -1e30

AXES = ("ylo", "z", "core", "x", "yhi")
CTX = ("ylo", "z", "core")
FSDP = ("x", "yhi")
GROUPS = [
    [
        (((group ^ yhi) * 4 + z) * 2 + core) * 8 + x * 2 + yhi
        for x in range(4)
        for yhi in range(2)
        for core in range(2)
    ]
    for group in range(2)
    for z in range(4)
]
RING = ("ylo", "z")
PLANE = ("ylo", "z", "yhi")
OUT_PLANE = ("yhi", "z", "ylo")
LEVEL = ("yhi", "ylo", "x")
GROUPS = [
    [
        (((group ^ yhi) * 4 + z) * 2 + core) * 8 + x * 2 + yhi
        for x in range(4)
        for yhi in range(2)
        for core in range(2)
    ]
    for group in range(2)
    for z in range(4)
]
RING = ("ylo", "z")
ROWS_ORDER = ("ylo", "z", "yhi", "x")
OUT_ORDER = ("yhi", "z", "ylo", "x")
SLOTS = 40

bf16 = jnp.bfloat16
f32 = jnp.float32


def dot(left, right):
    return jnp.dot(left, right, preferred_element_type=f32)


def dot_t(left, right):
    return lax.dot_general(left, right, (((1,), (1,)), ((), ())), preferred_element_type=f32)


def t_dot(left, right):
    return lax.dot_general(left, right, (((0,), (0,)), ((), ())), preferred_element_type=f32)


def exchange(pieces, axes):
    return lax.all_to_all(pieces, axes, split_axis=0, concat_axis=0, tiled=True)


def to_owners(pieces):
    return lax.all_to_all(
        pieces, AXES, split_axis=0, concat_axis=0, axis_index_groups=GROUPS, tiled=True
    )


def spread(piece, count, axes):
    return exchange(jnp.broadcast_to(piece[None], (count,) + piece.shape), axes)


def after(value, earlier):
    return lax.optimization_barrier((value, earlier))[0]


def together(*values):
    return lax.optimization_barrier(values)


def partner(value):
    return lax.ppermute(value, "core", [(0, 1), (1, 0)])


def route(axes, sizes, move):
    pairs = []
    for source in range(math.prod(sizes)):
        rest, at = source, []
        for size in reversed(sizes):
            at.insert(0, rest % size)
            rest //= size
        target = 0
        for size, value in zip(sizes, move(*at)):
            target = target * size + value
        pairs.append((source, target))
    return pairs


SAME = route(("core", "yhi"), (2, 2), lambda c, h: (h, c))
OTHER = route(("core", "yhi"), (2, 2), lambda c, h: (1 - h, c))
OUT_SAME = route(("ylo", "core", "yhi"), (2, 2, 2), lambda j, c, h: (c, j, h))
OUT_OTHER = route(("ylo", "core", "yhi"), (2, 2, 2), lambda j, c, h: (c, j, 1 - h))


def back(pairs):
    return [(target, source) for source, target in pairs]


def pick(flag, if_zero, if_one):
    return jnp.where(flag == 0, if_zero, if_one)


def gather_pieces(pair, flag, key, axes, same, other):
    first = lax.ppermute(pick(flag, pair[0], pair[1]), axes, same)
    second = lax.ppermute(pick(flag, pair[1], pair[0]), axes, other)
    return pick(
        key, jnp.concatenate([first, second]), jnp.concatenate([second, first])
    )


def scatter_pieces(piece, flag, key, axes, same, other):
    count = piece.shape[0] // 2
    mine, rest = piece[:count], piece[count:]
    first = lax.ppermute(pick(key, mine, rest), axes, back(same))
    second = lax.ppermute(pick(key, rest, mine), axes, back(other))
    return pick(flag, jnp.concatenate([first, second], axis=-1), jnp.concatenate([second, first], axis=-1))


def along(axis, piece):
    return [piece] + [
        lax.ppermute(piece, axis, [(i, (i + s) % 4) for i in range(4)]) for s in (1, 2, 3)
    ]


def back_along_x(blocks):
    return [blocks[0]] + [
        lax.ppermute(blocks[s], "x", [(i, (i - s) % 4) for i in range(4)]) for s in (1, 2, 3)
    ]


def added(blocks, *late):
    (total,) = call(add_kernel, [(blocks[0].shape, bf16)], *blocks, *late, cost=LONG)
    return total


def sum_of(first, second, third, fourth):
    return (
        (first[...].astype(f32) + second[...].astype(f32))
        + (third[...].astype(f32) + fourth[...].astype(f32))
    ).astype(bf16)


def add_kernel(first, second, third, fourth, *refs):
    refs[-1][...] = sum_of(first, second, third, fourth)


def add_both_kernel(*refs):
    total = refs[8]
    count = refs[0].shape[1]
    total[:, :count] = sum_of(*refs[:4])
    total[:, count:] = sum_of(*refs[4:8])


def order_matrix(groups, x):
    index = jnp.arange(groups * 96, dtype=jnp.int32)
    turn_of, group, row = index // (groups * 24), index // 24 % groups, index % 24
    own = group * 96 + (x - turn_of) % 4 * 24 + row
    return (index[:, None] == own[None, :]).astype(bf16)


def level_order_matrix(z):
    index = jnp.arange(8 * 96, dtype=jnp.int32)
    own = (z - index // 192) % 4 * 192 + index % 192
    return (index[:, None] == own[None, :]).astype(bf16)


def places(pair_of, ctx, row_count, ctx_count):
    half_size = row_count // 2
    pair = jnp.sum(
        jnp.where(ctx[:, None] == jnp.arange(ctx_count, dtype=jnp.int32)[None], pair_of[None], 0),
        axis=1,
    )
    block = jnp.stack([pair, 2 * ctx_count - 1 - pair], axis=1)
    return block[:, :, None] * half_size + jnp.arange(half_size, dtype=jnp.int32)[None, None]


def in_three(value):
    high = value.astype(bf16)
    rest = value - high.astype(f32)
    middle = rest.astype(bf16)
    return [high, middle, (rest - middle.astype(f32)).astype(bf16)]


def call(kernel, outs, *args, scratch=(), cost=None):
    def whole(shape):
        return pl.BlockSpec(shape, lambda i: (0,) * len(shape))

    return pl.pallas_call(
        kernel,
        out_shape=[jax.ShapeDtypeStruct(shape, dtype) for shape, dtype in outs],
        grid=(1,),
        in_specs=[whole(a.shape) for a in args],
        out_specs=[whole(shape) for shape, _ in outs],
        scratch_shapes=list(scratch),
        compiler_params=pltpu.CompilerParams(vmem_limit_bytes=ROOM),
        cost_estimate=COST if cost is None else cost,
    )(*args)


ROOM = 58 << 20
COST = pl.CostEstimate(flops=1 << 20, bytes_accessed=1 << 18, transcendentals=0)
LONG = pl.CostEstimate(flops=1 << 35, bytes_accessed=1 << 27, transcendentals=0)
WIDE = 2 * HD
EXPERTS = 16


def turn(vectors, cosines, sines):
    return vectors * cosines + pltpu.roll(vectors, HD // 2, axis=1) * sines


def gain_picker():
    row = lax.broadcasted_iota(jnp.int32, (8, 128), 0)
    column = lax.broadcasted_iota(jnp.int32, (8, 128), 1)
    return jnp.where((column == row + EXPERTS) & (row < 2), 1.0, 0.0).astype(bf16)


def normal_of(stream):
    inverse = lax.rsqrt(jnp.mean(stream * stream, axis=-1, keepdims=True) + EPSILON)
    return stream * inverse, inverse


def norm_back(grad, normal, inverse, gain):
    scaled = grad * gain
    return inverse * (scaled - normal * jnp.mean(scaled * normal, axis=-1, keepdims=True))


def column_block(s, count):
    return slice(s * count, (s + 1) * count)


def order_kernel(rows, order, out):
    out[...] = dot(rows[...], order[...]).astype(bf16)


def keys_kernel(both, cosines, sines, *refs):
    kvs, (normed, key_value, gains) = refs[:4], refs[4:]
    count = kvs[0].shape[0]
    for s in range(4):
        gains[:, column_block(s, count)] = dot_t(gain_picker(), kvs[s][:, WIDE:])
    normal, _ = normal_of(both[...].astype(f32))
    normed[...] = (normal * gains[0:1]).astype(bf16)
    kv = dot(normed[:, column_block(0, count)], kvs[0][:, :WIDE])
    for s in range(1, 4):
        kv = kv + dot(normed[:, column_block(s, count)], kvs[s][:, :WIDE])
    keys = turn(kv[:, :HD], cosines[...], sines[...]).astype(bf16)
    values = kv[:, HD:].astype(bf16)
    for i in range(key_value.shape[0]):
        key_value[i, :, :HD] = keys
        key_value[i, :, HD:] = values


def small_kernel(order, kvs0, kvs1, kvs2, kvs3, small, gains):
    count = kvs0.shape[0]
    total = jnp.zeros(small.shape, f32)
    for s, kvs in enumerate((kvs0, kvs1, kvs2, kvs3)):
        total = total + dot(order[:, column_block(s, count)], kvs[:, WIDE:])
    small[...] = total.astype(bf16)
    gains[...] = dot_t(gain_picker(), small[...])


def query_kernel(normed, cosines, sines, w_q0, w_q1, w_q2, w_q3, queries):
    w_q = (w_q0, w_q1, w_q2, w_q3)
    count = w_q0.shape[0]
    for h in range(queries.shape[1] // HD):
        at = column_block(h, HD)
        q = dot(normed[:, column_block(0, count)], w_q0[:, at])
        for s in range(1, 4):
            q = q + dot(normed[:, column_block(s, count)], w_q[s][:, at])
        queries[:, at] = turn(q, cosines[...], sines[...]).astype(bf16)


def attend_kernel(
    queries,
    q_place,
    low_place,
    up_place,
    order,
    order_back,
    kv,
    ordered,
    ordered_back,
    logs,
    kv_low,
    kv_up,
    mixed,
    *,
    scale,
    pieces,
    heads,
):
    half = kv.shape[1] // 2
    for i in range(pieces):
        kv_low[i * half : (i + 1) * half, :] = kv[i, :half]
        kv_up[i * half : (i + 1) * half, :] = kv[i, half:]
    allowed_low = low_place[...] <= q_place[...]
    allowed_up = up_place[...] <= q_place[half:, :]
    for h in range(heads):
        at = slice(h * HD, (h + 1) * HD)
        q = queries[:, at]
        low = jnp.where(allowed_low, dot_t(q, kv_low[:, :HD]) * scale, NEGATIVE)
        up = jnp.where(allowed_up, dot_t(q[half:], kv_up[:, :HD]) * scale, NEGATIVE)
        first, second = low[:half], low[half:]
        top = jnp.max(first, axis=-1, keepdims=True)
        weight = jnp.exp(first - top)
        total = jnp.sum(weight, axis=-1, keepdims=True)
        probs = (weight / total).astype(bf16)
        mixed[:half, at] = dot(probs, kv_low[:, HD:]).astype(bf16)
        logs[h, :half, :] = top + jnp.log(total)
        top = jnp.maximum(
            jnp.max(second, axis=-1, keepdims=True), jnp.max(up, axis=-1, keepdims=True)
        )
        weight, weight_up = jnp.exp(second - top), jnp.exp(up - top)
        total = jnp.sum(weight, axis=-1, keepdims=True) + jnp.sum(
            weight_up, axis=-1, keepdims=True
        )
        mixed[half:, at] = (
            dot((weight / total).astype(bf16), kv_low[:, HD:])
            + dot((weight_up / total).astype(bf16), kv_up[:, HD:])
        ).astype(bf16)
        logs[h, half:, :] = top + jnp.log(total)
    ordered[...] = dot(mixed[...], order[...]).astype(bf16)
    ordered_back[...] = dot(mixed[...], order_back[...]).astype(bf16)


def branch_kernel(mixed, w_out0, w_out1, w_out2, w_out3, own, other, w_out):
    quarter = mixed.shape[0] // 4
    count, columns = w_out0.shape[1:]
    for s, part in enumerate((w_out0, w_out1, w_out2, w_out3)):
        w_out[:, column_block(s, count)] = part[...]
    for k in range(2):
        part = dot(mixed[...], w_out[k])
        at = slice(k * columns, (k + 1) * columns)
        own[:quarter, at] = part[:quarter]
        other[:quarter, at] = part[quarter : 2 * quarter]
        own[quarter:, at] = part[2 * quarter : 3 * quarter]
        other[quarter:, at] = part[3 * quarter :]


def route_kernel(
    tokens,
    own,
    received,
    small,
    gains,
    hits,
    places_of,
    placer,
    sent,
    midway,
    moe_low,
    gates,
    parts,
):
    middle = tokens[...].astype(f32) + (own[...] + received[...])
    midway[...] = middle
    normal, _ = normal_of(middle)
    moe = (normal * gains[1:2]).astype(bf16)
    moe_low[...] = moe
    sent[:, : moe.shape[1]] = dot(placer[...], moe).astype(bf16)
    logits = dot(moe, small[...])
    picked = [
        jnp.sum(hits[k].astype(f32) * logits, axis=-1, keepdims=True) for k in range(TOPK)
    ]
    top = picked[0]
    for value in picked[1:]:
        top = jnp.maximum(top, value)
    weights = [jnp.exp(value - top) for value in picked]
    total = weights[0]
    for value in weights[1:]:
        total = total + value
    lane = lax.broadcasted_iota(jnp.int32, gates.shape, 1)
    gate_at = jnp.zeros(places_of.shape[1:], f32)
    kept = jnp.zeros(gates.shape, f32)
    for k in range(TOPK):
        gate = weights[k] / total
        kept = jnp.where(lane == k, gate, kept)
        gate_at = gate_at + places_of[k].astype(f32) * gate
    gates[...] = kept
    block = jnp.zeros((sent.shape[0], 128), f32)
    for i, part in enumerate(in_three(gate_at)):
        parts[i] = part
        block = block + t_dot(part, jnp.where(lane == i, 1.0, 0.0).astype(bf16))
    sent[:, moe.shape[1] :] = block.astype(bf16)


def expert_kernel(
    core, sent, cot, weights, out, rows_grad, hidden, out_grad, gate_grad, up_grad, held, sems
):
    copies = [
        pltpu.make_async_copy(weights.at[m, core[0]], held.at[m], sems.at[m]) for m in range(3)
    ]
    for copy in copies:
        copy.start()
    width = out.shape[1]
    gates = jnp.sum(sent[:, width:].astype(f32), axis=-1, keepdims=True)
    out_grad[...] = (gates * cot[...].astype(f32)).astype(bf16)
    rows = sent[:, :width]
    copies[0].wait()
    gate_pre = dot(rows, held[0])
    copies[1].wait()
    up_pre = dot(rows, held[1])
    sigmoid = 1.0 / (1.0 + jnp.exp(-gate_pre))
    silu = gate_pre * sigmoid
    low = (silu * up_pre).astype(bf16)
    hidden[...] = low
    copies[2].wait()
    hidden_grad = dot(out_grad[...], held[2])
    gate_low = (hidden_grad * up_pre * sigmoid * (1.0 + gate_pre * (1.0 - sigmoid))).astype(bf16)
    up_low = (hidden_grad * silu).astype(bf16)
    gate_grad[...] = gate_low
    up_grad[...] = up_low
    rows_grad[:, :width] = (dot_t(gate_low, held[0]) + dot_t(up_low, held[1])).astype(bf16)
    result = dot_t(low, held[2]).astype(bf16)
    out[...] = result
    grads = in_three(
        jnp.sum(cot[...].astype(f32) * result.astype(f32), axis=-1, keepdims=True)
    )
    lane = lax.broadcasted_iota(jnp.int32, (cot.shape[0], 128), 1)
    block = jnp.zeros(lane.shape, f32)
    for i, part in enumerate(grads):
        block = jnp.where(lane == i, part.astype(f32), block)
    rows_grad[:, width:] = block.astype(bf16)


def expert_call(core, arrays, weights, outs):
    rows = arrays[0].shape[0]

    def whole(columns):
        return pl.BlockSpec(
            (rows, columns), lambda i, core: (0, 0), pipeline_mode=pl.Buffered(1)
        )

    return pl.pallas_call(
        expert_kernel,
        out_shape=[jax.ShapeDtypeStruct((rows, columns), bf16) for columns in outs],
        grid_spec=pltpu.PrefetchScalarGridSpec(
            num_scalar_prefetch=1,
            grid=(1,),
            in_specs=[whole(a.shape[1]) for a in arrays] + [pl.BlockSpec(memory_space=pltpu.HBM)],
            out_specs=[whole(columns) for columns in outs],
            scratch_shapes=[
                pltpu.VMEM((3,) + weights.shape[2:], bf16),
                pltpu.SemaphoreType.DMA((3,)),
            ],
        ),
        compiler_params=pltpu.CompilerParams(vmem_limit_bytes=ROOM),
        cost_estimate=COST,
    )(core, *arrays, weights)


def weights_kernel(sent, out_grad, hidden, gate_grad, up_grad, sums):
    rows = sent[...]
    sums[0] = t_dot(rows, gate_grad[...]).astype(bf16)
    sums[1] = t_dot(rows, up_grad[...]).astype(bf16)
    sums[2] = t_dot(out_grad[...], hidden[...]).astype(bf16)


def expert_weights_grad(sent, out_grad, hidden, gate_grad, up_grad, block=256):
    count, width = out_grad.shape
    columns = hidden.shape[1]
    part = pl.BlockSpec((count, block), lambda i: (0, i))
    whole = pl.BlockSpec((count, columns), lambda i: (0, 0), pipeline_mode=pl.Buffered(1))
    return pl.pallas_call(
        weights_kernel,
        out_shape=jax.ShapeDtypeStruct((3, width, columns), bf16),
        grid=(width // block,),
        in_specs=[part, part, whole, whole, whole],
        out_specs=pl.BlockSpec((3, block, columns), lambda i: (0, i, 0)),
        compiler_params=pltpu.CompilerParams(vmem_limit_bytes=ROOM),
        cost_estimate=COST,
    )(sent, out_grad, hidden, gate_grad, up_grad)


def combine_kernel(midway, parts, returned, output):
    rows = returned[...]
    output[...] = (
        midway[...] + (dot(parts[0], rows) + (dot(parts[1], rows) + dot(parts[2], rows)))
    ).astype(bf16)


def home_kernel(
    placer_t,
    home,
    midway,
    cot,
    gains,
    hits,
    places_of,
    gates,
    small,
    moe_low,
    midway_grad,
    branch_low,
    gain_grad,
    router_grad,
):
    width = midway.shape[1]
    lane = lax.broadcasted_iota(jnp.int32, gates.shape, 1)
    gate, gate_grad = [], []
    mean = jnp.zeros((gates.shape[0], 1), f32)
    for k in range(TOPK):
        gate.append(jnp.sum(jnp.where(lane == k, gates[...], 0.0), axis=-1, keepdims=True))
        gate_grad.append(
            jnp.sum(dot(places_of[k], home[:, width:]), axis=-1, keepdims=True)
        )
        mean = mean + gate[k] * gate_grad[k]
    logit_grad = jnp.zeros(gates.shape, f32)
    for k in range(TOPK):
        logit_grad = logit_grad + hits[k].astype(f32) * (gate[k] * (gate_grad[k] - mean))
    logit_grad = logit_grad.astype(bf16)
    router_grad[...] = t_dot(moe_low[...], logit_grad)
    grad = dot(placer_t[...], home[:, :width]) + dot_t(logit_grad, small[...])
    normal, inverse = normal_of(midway[...])
    result = cot[...].astype(f32) + norm_back(grad, normal, inverse, gains[1:2])
    midway_grad[...] = result
    branch_low[...] = result.astype(bf16)
    gain_grad[...] = jnp.broadcast_to(
        jnp.sum(grad * normal, axis=0, keepdims=True), gain_grad.shape
    )


def out_grad_kernel(mixed, own, other, branch, *blocks):
    quarter = own.shape[0] // 2
    branch[:quarter] = own[:quarter]
    branch[quarter : 2 * quarter] = other[:quarter]
    branch[2 * quarter : 3 * quarter] = own[quarter:]
    branch[3 * quarter :] = other[quarter:]
    count, columns = blocks[0].shape[1:]
    for k in range(2):
        grad = t_dot(mixed[...], branch[:, column_block(k, columns)]).astype(bf16)
        for s in range(4):
            blocks[s][k] = grad[column_block(s, count)]


def attend_back_kernel(
    branch,
    w_out,
    order,
    queries,
    kv_low,
    kv_up,
    logs,
    q_place,
    low_place,
    up_place,
    cosines,
    sines,
    normed,
    dq,
    dkv,
    block0,
    block1,
    block2,
    block3,
    grads,
    acc_low,
    acc_up,
    *,
    scale,
    pieces,
    heads,
):
    half = queries.shape[0] // 2
    columns = w_out.shape[2]
    ordered = dot_t(branch[:, :columns], w_out[0]) + dot_t(branch[:, columns:], w_out[1])
    grads[...] = dot_t(ordered.astype(bf16), order[...]).astype(bf16)
    allowed_low = low_place[...] <= q_place[...]
    allowed_up = up_place[...] <= q_place[half:, :]
    key_low, value_low = kv_low[:, :HD], kv_low[:, HD:]
    key_up, value_up = kv_up[:, :HD], kv_up[:, HD:]
    for h in range(heads):
        at = slice(h * HD, (h + 1) * HD)
        q, grad, log = queries[:, at], grads[:, at], logs[h]
        low = jnp.where(allowed_low, dot_t(q, key_low) * scale, NEGATIVE)
        up = jnp.where(allowed_up, dot_t(q[half:], key_up) * scale, NEGATIVE)
        probs_low, probs_up = jnp.exp(low - log), jnp.exp(up - log[half:])
        grad_low, grad_up = dot_t(grad, value_low), dot_t(grad[half:], value_up)
        along = jnp.sum(probs_low * grad_low, axis=-1, keepdims=True)
        along_up = along[half:] + jnp.sum(probs_up * grad_up, axis=-1, keepdims=True)
        along = jnp.concatenate([along[:half], along_up])
        score_low = (probs_low * (grad_low - along)).astype(bf16)
        score_up = (probs_up * (grad_up - along_up)).astype(bf16)
        part = dot(score_low, key_low)
        part = jnp.concatenate([part[:half], part[half:] + dot(score_up, key_up)]) * scale
        dq[:, at] = turn(part, cosines[...], -sines[...]).astype(bf16)
        terms = (
            (acc_low, slice(0, HD), t_dot(q, score_low)),
            (acc_up, slice(0, HD), t_dot(q[half:], score_up)),
            (acc_low, slice(HD, 2 * HD), t_dot(grad, probs_low.astype(bf16))),
            (acc_up, slice(HD, 2 * HD), t_dot(grad[half:], probs_up.astype(bf16))),
        )
        for acc, rows, term in terms:
            if h == 0:
                acc[rows] = term
            else:
                acc[rows] += term
    for s, block in enumerate((block0, block1, block2, block3)):
        block[...] = t_dot(normed[:, column_block(s, block.shape[0])], dq[...]).astype(bf16)
    for acc, first in ((acc_low, 0), (acc_up, half)):
        dk = (acc[:HD].T * scale).astype(bf16)
        dv = acc[HD:].T.astype(bf16)
        for i in range(pieces):
            dkv[i, first : first + half, :HD] = dk[i * half : (i + 1) * half]
            dkv[i, first : first + half, HD:] = dv[i * half : (i + 1) * half]


def sum_kernel(dq, cosines, sines, *refs):
    w_q, kvs, (parts, dkv, own, other) = refs[:4], refs[4:8], refs[8:]
    total = jnp.sum(parts[...].astype(f32), axis=0)
    dkv[:, :HD] = turn(total[:, :HD], cosines[...], -sines[...]).astype(bf16)
    dkv[:, HD:] = total[:, HD:].astype(bf16)
    quarter = own.shape[0] // 2
    for s in range(4):
        grad = dot_t(dq[...], w_q[s][...]) + dot_t(dkv[...], kvs[s][:, :WIDE])
        at = column_block(s, w_q[s].shape[0])
        own[:quarter, at] = grad[:quarter]
        other[:quarter, at] = grad[quarter : 2 * quarter]
        own[quarter:, at] = grad[2 * quarter : 3 * quarter]
        other[quarter:, at] = grad[3 * quarter :]


def stack_kernel(gate, up, down, late, out):
    del late
    out[0] = gate[...]
    out[1] = up[...]
    out[2] = down[...]


def small_grad_kernel(order, router_grad, gain_grad, late, out):
    del late
    row = lax.broadcasted_iota(jnp.int32, gain_grad.shape, 0)
    second = jnp.where(row == 1, gain_grad[...], 0.0).astype(bf16)
    small = router_grad[...] + t_dot(second, gain_picker())
    out[...] = t_dot(order[...], small.astype(bf16))


def input_kernel(both, own, received, midway_grad, gains, order, small, normed, dkv, out, *blocks):
    grad = own[...] + received[...]
    quarter = own.shape[0] // 2
    tokens = jnp.concatenate([both[:quarter], both[2 * quarter : 3 * quarter]])
    normal, inverse = normal_of(tokens.astype(f32))
    parts = in_three(norm_back(grad, normal, inverse, gains[0:1]))
    moved = dot_t(jnp.concatenate(parts), order[...])
    count = 2 * quarter
    out[...] = midway_grad[...] + (
        moved[:count] + (moved[count : 2 * count] + moved[2 * count :])
    )
    gain_grad = jnp.sum(grad * normal, axis=0, keepdims=True)
    row = lax.broadcasted_iota(jnp.int32, gains.shape, 0)
    gain_grad = jnp.where(row == 0, gain_grad, 0.0).astype(bf16)
    small = small[...] + t_dot(gain_grad, gain_picker())
    rows = blocks[0].shape[0]
    for s, block in enumerate(blocks):
        at = column_block(s, rows)
        block[:, :WIDE] = t_dot(normed[:, at], dkv[...]).astype(bf16)
        block[:, WIDE:] = small[at].astype(bf16)


def body(
    tokens,
    cotangent,
    pair_of,
    routes,
    attn_gain,
    moe_gain,
    w_query,
    w_key,
    w_value,
    w_out,
    w_router,
    w_gate,
    w_up,
    w_down,
):
    rows = tokens.shape[1]
    half = rows // 2
    width = tokens.shape[2]
    shard = w_query.shape[1]
    ctx_count = 16
    experts = w_router.shape[2]
    columns = w_gate.shape[3]
    per_group = H // KVH
    qw = per_group * HD
    scale = 1.0 / math.sqrt(HD)
    core = lax.axis_index("core")
    ylo, z, yhi = lax.axis_index("ylo"), lax.axis_index("z"), lax.axis_index("yhi")
    x = lax.axis_index("x")
    piece_rows = 2 * shard
    slots = experts * SLOTS
    own_tokens, cot = tokens[0], cotangent[0]

    def halves(matrix):
        return [matrix[:, : matrix.shape[1] // 2], matrix[:, matrix.shape[1] // 2 :]]

    small = jnp.concatenate([w_router[0], attn_gain[0][:, None], moe_gain[0][:, None]], axis=-1)
    small = jnp.pad(small, ((0, 0), (0, 128 - experts - 2)))
    query_halves, key_halves, value_halves = halves(w_query[0]), halves(w_key[0]), halves(w_value[0])
    pairs = [
        jnp.concatenate([k, v, small, q], axis=-1)
        for k, v, q in zip(key_halves, value_halves, query_halves)
    ]
    pieces = gather_pieces(pairs, yhi, core, ("core", "yhi"), SAME, OTHER)
    out_pieces = gather_pieces(
        halves(w_out[0]), yhi, yhi, ("ylo", "core", "yhi"), OUT_SAME, OUT_OTHER
    )
    other_tokens = partner(own_tokens)
    pieces, out_pieces, x, z, own_tokens, other_tokens, pair_of = together(
        pieces, out_pieces, x, z, own_tokens, other_tokens, pair_of
    )

    plane_rows = 16 * piece_rows
    plane = spread(pieces, 16, PLANE)
    both = jnp.concatenate(
        [own_tokens[:half], other_tokens[:half], own_tokens[half:], other_tokens[half:]]
    )
    order, out_order, level_order = order_matrix(16, x), order_matrix(8, x), level_order_matrix(z)
    (expert_shards_in,) = call(
        stack_kernel, [((3,) + w_gate.shape[1:], bf16)], w_gate[0], w_up[0], w_down[0], both
    )
    (
        plane, both, out_pieces, order, out_order, level_order, pair_of, expert_shards_in, chosen,
    ) = together(
        plane, both, out_pieces, order, out_order, level_order, pair_of, expert_shards_in,
        routes[0, 0],
    )

    plane = plane.reshape(plane_rows, -1)
    w_kvs = along("x", plane[:, : 3 * HD])
    wo = spread(out_pieces, 16, LEVEL)
    (both,) = call(order_kernel, [((2 * rows, width), bf16)], both, order)

    def two_cores(ctx):
        return jnp.stack([ctx + core, ctx + 1 - core], axis=-1).reshape(-1)

    ctx_here = (ylo * 4 + z) * 2
    q_place = places(pair_of, two_cores(ctx_here), rows, ctx_count)
    q_place = q_place.transpose(1, 0, 2).reshape(2 * rows, 1)
    key_place = places(
        pair_of, two_cores(jnp.arange(8, dtype=jnp.int32) * 2), rows, ctx_count
    )
    low_place, up_place = key_place[:, 0].reshape(1, -1), key_place[:, 1].reshape(1, -1)
    frequency = jnp.exp(jnp.arange(HD // 2, dtype=f32) * (-2.0 * math.log(ROPE_BASE) / HD))
    angles = q_place.astype(f32) * frequency[None, :]
    cosines, sines = jnp.cos(angles), jnp.sin(angles)
    cosines = jnp.concatenate([cosines, cosines], axis=-1)
    sines = jnp.concatenate([-sines, sines], axis=-1)
    w_q, w_kvs, wo, both, q_place, low_place, up_place, cosines, sines, chosen = together(
        plane[:, 3 * HD :], w_kvs, wo, both, q_place, low_place, up_place, cosines, sines, chosen
    )

    w_q = along("x", w_q)
    wo = along("z", wo.reshape(2, qw // 4, width // 2))
    normed, key_value, gains = call(
        keys_kernel,
        [((2 * rows, width), bf16), ((8, 2 * rows, 2 * HD), bf16), ((8, width), f32)],
        both,
        cosines,
        sines,
        *w_kvs,
    )
    all_kv = exchange(key_value, RING)
    small, moe_gains = call(
        small_kernel, [((width, 128), bf16), ((8, width), f32)], order, *w_kvs
    )
    (queries,) = call(
        query_kernel, [((2 * rows, qw), bf16)], normed, cosines, sines, *w_q, cost=LONG
    )
    lanes = jnp.arange(128, dtype=jnp.int32)
    hits = (chosen.T[:, :, None] == lanes[None, None, :]).astype(bf16)
    earlier = (lanes[:, None] > lanes[None, :]).astype(bf16)
    before = dot(earlier, jnp.sum(hits, axis=0))
    slot_index = jnp.sum(hits.astype(f32) * before[None], axis=-1).astype(jnp.int32)
    target = chosen.T * SLOTS + slot_index
    slot_row = jnp.arange(slots, dtype=jnp.int32)
    places_of = (target[:, :, None] == slot_row[None, None, :]).astype(bf16)
    placer_t = jnp.sum(places_of, axis=0)
    placer = placer_t.T
    (cot_rows,) = call(order_kernel, [((slots, width), bf16)], placer, cot)
    (
        queries, all_kv, expert_shards_in, small, moe_gains, cot_rows,
        hits, places_of, placer_t, placer, wo,
    ) = together(
        queries, all_kv, expert_shards_in, small, moe_gains, cot_rows,
        hits, places_of, placer_t, placer, wo,
    )
    expert_weights = lax.all_gather(expert_shards_in, CTX, axis=2, tiled=True)

    arrived_cot = to_owners(cot_rows.reshape(experts, SLOTS, width))
    sizes = dict(scale=scale, pieces=8, heads=per_group)
    keys = 8 * rows
    mixed, mixed_back, logs, kv_low, kv_up = call(
        functools.partial(attend_kernel, **sizes),
        [
            ((2 * rows, qw), bf16),
            ((2 * rows, qw), bf16),
            ((per_group, 2 * rows, 1), f32),
            ((keys, 2 * HD), bf16),
            ((keys, 2 * HD), bf16),
        ],
        queries,
        q_place,
        low_place,
        up_place,
        level_order,
        out_order,
        all_kv,
        scratch=[pltpu.VMEM((2 * rows, qw), bf16)],
    )

    branch_own, branch_other, wo = call(
        branch_kernel,
        [((rows, width), f32), ((rows, width), f32), ((2, qw, width // 2), bf16)],
        mixed,
        *wo,
    )
    sent, midway, moe_low, gates, gate_parts = call(
        route_kernel,
        [
            ((slots, width + 128), bf16),
            ((rows, width), f32),
            ((rows, width), bf16),
            ((rows, 128), f32),
            ((3, rows, slots), bf16),
        ],
        own_tokens,
        branch_own,
        partner(branch_other),
        small,
        moe_gains,
        hits,
        places_of,
        placer,
    )
    sent, arrived_cot = together(sent, arrived_cot)

    sent = to_owners(sent.reshape(experts, SLOTS, width + 128)).reshape(slots, width + 128)
    mine = core.reshape(1)
    expert_out, rows_grad, hidden, out_grad, gate_grad, up_grad = expert_call(
        mine,
        [sent, arrived_cot.reshape(slots, width)],
        expert_weights,
        [width, width + 128, columns, width, columns, columns],
    )
    rows_grad, gate_grad, up_grad = together(rows_grad, gate_grad, up_grad)

    home_grad = to_owners(rows_grad.reshape(experts, SLOTS, width + 128))
    expert_sums = expert_weights_grad(sent, out_grad, hidden, gate_grad, up_grad)
    home_grad, expert_sums, expert_out = together(home_grad, expert_sums, expert_out)
    expert_sums = lax.psum_scatter(expert_sums, RING, scatter_dimension=1, tiled=True)

    returned = to_owners(expert_out.reshape(experts, SLOTS, width))
    midway_grad, branch_low, gain_two_grad, router_grad = call(
        home_kernel,
        [((rows, width), f32), ((rows, width), bf16), ((8, width), f32), ((width, 128), f32)],
        placer_t,
        home_grad.reshape(slots, width + 128),
        midway,
        cot,
        moe_gains,
        hits,
        places_of,
        gates,
        small,
        moe_low,
    )
    branch, *out_w_grad = call(
        out_grad_kernel,
        [((2 * rows, width), bf16)] + [((2, qw // 4, width // 2), bf16)] * 4,
        mixed_back,
        branch_low,
        partner(branch_low),
    )
    branch, out_w_grad = together(branch, out_w_grad)
    out_w_grad = back_along_x(out_w_grad)

    dq, dkv, *q_w_grad = call(
        functools.partial(attend_back_kernel, **sizes),
        [((2 * rows, qw), bf16), ((8, 2 * rows, 2 * HD), bf16)]
        + [((plane_rows, qw), bf16)] * 4,
        branch,
        wo,
        level_order,
        queries,
        kv_low,
        kv_up,
        logs,
        q_place,
        low_place,
        up_place,
        cosines,
        sines,
        normed,
        scratch=[
            pltpu.VMEM((2 * rows, qw), bf16),
            pltpu.VMEM((2 * HD, keys), f32),
            pltpu.VMEM((2 * HD, keys), f32),
        ],
    )
    dkv, q_w_grad, returned, late = together(dkv, q_w_grad, returned, gain_two_grad)

    dkv = exchange(dkv, RING)
    q_w_grad = back_along_x(q_w_grad)
    (small_grad,) = call(
        small_grad_kernel, [((width, 128), f32)], order, router_grad, gain_two_grad, late
    )
    out_w_grad = added(out_w_grad, small_grad)
    dkv, out_w_grad, small_grad, q_w_grad[1], q_w_grad[3] = together(
        dkv, out_w_grad, small_grad, q_w_grad[1], q_w_grad[3]
    )

    dkv, normed_own, normed_other = call(
        sum_kernel,
        [((2 * rows, 2 * HD), bf16), ((rows, width), f32), ((rows, width), f32)],
        dq,
        cosines,
        sines,
        *w_q,
        *w_kvs,
        dkv,
    )
    input_grad, *kvs_grad = call(
        input_kernel,
        [((rows, width), f32)] + [((plane_rows, 3 * HD), bf16)] * 4,
        both,
        normed_own,
        partner(normed_other),
        midway_grad,
        gains,
        order,
        small_grad,
        normed,
        dkv,
    )
    kvs_grad, out_w_grad, input_grad = together(kvs_grad, out_w_grad, input_grad)

    out_w_grad = exchange(out_w_grad.reshape(16, piece_rows, width // 2), OUT_PLANE)
    kvs_grad = back_along_x(kvs_grad)
    (plane_grad,) = call(
        add_both_kernel, [((plane_rows, qw + 3 * HD), bf16)], *q_w_grad, *kvs_grad, cost=LONG
    )
    plane_grad, out_w_grad, returned = together(plane_grad, out_w_grad, returned)
    plane_grad = exchange(plane_grad.reshape(16, piece_rows, qw + 3 * HD), PLANE)

    (output,) = call(
        combine_kernel,
        [((rows, width), bf16)],
        midway,
        gate_parts,
        returned.reshape(slots, width),
    )

    def summed(pieces):
        return jnp.sum(pieces.astype(f32), axis=0)

    def expert_shards(grad):
        count = grad.shape[1] // 2
        kept = lax.dynamic_slice_in_dim(grad, core * count, count, axis=1)
        given = partner(lax.dynamic_slice_in_dim(grad, (1 - core) * count, count, axis=1))
        both = jnp.stack([pick(core, kept, given), pick(core, given, kept)], axis=1)
        return [both[i : i + 1].astype(f32) for i in range(3)]

    out_w_grad = scatter_pieces(
        summed(out_w_grad), yhi, yhi, ("ylo", "core", "yhi"), OUT_SAME, OUT_OTHER
    )
    w_gate_grad, w_up_grad, w_down_grad = expert_shards(expert_sums)
    plane_grad, out_w_grad, w_gate_grad, w_up_grad, w_down_grad, output = together(
        plane_grad, out_w_grad, w_gate_grad, w_up_grad, w_down_grad, output
    )
    plane_grad = scatter_pieces(summed(plane_grad), yhi, core, ("core", "yhi"), SAME, OTHER)
    plane_grad = plane_grad.reshape(shard, 2, -1)

    def joined(first, last):
        return plane_grad[:, :, first:last].reshape(1, shard, -1)

    small_grad = jnp.sum(plane_grad[None, :, :, qw + 2 * HD :], axis=2)

    return (
        output[None],
        input_grad[None],
        small_grad[:, :, experts],
        small_grad[:, :, experts + 1],
        joined(0, qw),
        joined(qw, qw + HD),
        joined(qw + HD, qw + 2 * HD),
        out_w_grad[None],
        small_grad[:, :, :experts],
        w_gate_grad,
        w_up_grad,
        w_down_grad,
    )


def solution(mesh):
    fine = Mesh(mesh.devices.reshape(2, 4, 2, 4, 2), AXES)
    seq = P(FSDP, CTX, None)
    vector = P(None, AXES)
    matrix = P(None, AXES, None)
    expert = P(None, FSDP, CTX, None)
    in_specs = (
        seq,
        seq,
        P(),
        P(None, FSDP, CTX, None),
        vector,
        vector,
        matrix,
        matrix,
        matrix,
        matrix,
        matrix,
        expert,
        expert,
        expert,
    )
    out_specs = (
        seq,
        seq,
        vector,
        vector,
        matrix,
        matrix,
        matrix,
        matrix,
        matrix,
        expert,
        expert,
        expert,
    )
    return jax.shard_map(body, mesh=fine, in_specs=in_specs, out_specs=out_specs, check_vma=False)
```

```python
import functools
import math

import jax
import jax.numpy as jnp
from jax import lax
from jax.experimental import pallas as pl
from jax.experimental.pallas import tpu as pltpu
from jax.sharding import Mesh
from jax.sharding import PartitionSpec as P

H = 12
KVH = 2
HD = 128
TOPK = 4

EPSILON = 1e-06
ROPE_BASE = 1000000.0
NEGATIVE = -1e30

AXES = ("ylo", "z", "core", "x", "yhi")
CTX = ("ylo", "z", "core")
FSDP = ("x", "yhi")
GROUPS = [
    [
        (((group ^ yhi) * 4 + z) * 2 + core) * 8 + x * 2 + yhi
        for x in range(4)
        for yhi in range(2)
        for core in range(2)
    ]
    for group in range(2)
    for z in range(4)
]
RING = ("ylo", "z")
PLANE = ("ylo", "z", "yhi")
OUT_PLANE = ("yhi", "z", "ylo")
LEVEL = ("yhi", "ylo", "x")
GROUPS = [
    [
        (((group ^ yhi) * 4 + z) * 2 + core) * 8 + x * 2 + yhi
        for x in range(4)
        for yhi in range(2)
        for core in range(2)
    ]
    for group in range(2)
    for z in range(4)
]
RING = ("ylo", "z")
ROWS_ORDER = ("ylo", "z", "yhi", "x")
OUT_ORDER = ("yhi", "z", "ylo", "x")
SLOTS = 40

bf16 = jnp.bfloat16
f32 = jnp.float32


def dot(left, right):
    return jnp.dot(left, right, preferred_element_type=f32)


def dot_t(left, right):
    return lax.dot_general(left, right, (((1,), (1,)), ((), ())), preferred_element_type=f32)


def t_dot(left, right):
    return lax.dot_general(left, right, (((0,), (0,)), ((), ())), preferred_element_type=f32)


def exchange(pieces, axes):
    return lax.all_to_all(pieces, axes, split_axis=0, concat_axis=0, tiled=True)


def to_owners(pieces):
    return lax.all_to_all(
        pieces, AXES, split_axis=0, concat_axis=0, axis_index_groups=GROUPS, tiled=True
    )


def spread(piece, count, axes):
    return exchange(jnp.broadcast_to(piece[None], (count,) + piece.shape), axes)


def after(value, earlier):
    return lax.optimization_barrier((value, earlier))[0]


def together(*values):
    return lax.optimization_barrier(values)


def partner(value):
    return lax.ppermute(value, "core", [(0, 1), (1, 0)])


def route(axes, sizes, move):
    pairs = []
    for source in range(math.prod(sizes)):
        rest, at = source, []
        for size in reversed(sizes):
            at.insert(0, rest % size)
            rest //= size
        target = 0
        for size, value in zip(sizes, move(*at)):
            target = target * size + value
        pairs.append((source, target))
    return pairs


SAME = route(("core", "yhi"), (2, 2), lambda c, h: (h, c))
OTHER = route(("core", "yhi"), (2, 2), lambda c, h: (1 - h, c))
OUT_SAME = route(("ylo", "core", "yhi"), (2, 2, 2), lambda j, c, h: (c, j, h))
OUT_OTHER = route(("ylo", "core", "yhi"), (2, 2, 2), lambda j, c, h: (c, j, 1 - h))


def back(pairs):
    return [(target, source) for source, target in pairs]


def pick(flag, if_zero, if_one):
    return jnp.where(flag == 0, if_zero, if_one)


def gather_pieces(first, second, key, axes, same, other):
    first = lax.ppermute(first, axes, same)
    second = lax.ppermute(second, axes, other)
    return pick(
        key, jnp.concatenate([first, second]), jnp.concatenate([second, first])
    )


def scatter_pieces(piece, flag, key, axes, same, other):
    count = piece.shape[0] // 2
    mine, rest = piece[:count], piece[count:]
    first = lax.ppermute(pick(key, mine, rest), axes, back(same))
    second = lax.ppermute(pick(key, rest, mine), axes, back(other))
    return pick(flag, jnp.concatenate([first, second], axis=-1), jnp.concatenate([second, first], axis=-1))


def along(axis, piece):
    return [piece] + [
        lax.ppermute(piece, axis, [(i, (i + s) % 4) for i in range(4)]) for s in (1, 2, 3)
    ]


def back_along_x(blocks):
    return [blocks[0]] + [
        lax.ppermute(blocks[s], "x", [(i, (i - s) % 4) for i in range(4)]) for s in (1, 2, 3)
    ]


def added(blocks, *late):
    (total,) = call(add_kernel, [(blocks[0].shape, bf16)], *blocks, *late, cost=LONG)
    return total


def sum_of(first, second, third, fourth):
    return (
        (first[...].astype(f32) + second[...].astype(f32))
        + (third[...].astype(f32) + fourth[...].astype(f32))
    ).astype(bf16)


def add_kernel(first, second, third, fourth, *refs):
    refs[-1][...] = sum_of(first, second, third, fourth)


def add_both_kernel(*refs):
    total = refs[8]
    count = refs[0].shape[1]
    total[:, :count] = sum_of(*refs[:4])
    total[:, count:] = sum_of(*refs[4:8])


def order_matrix(groups, x):
    index = jnp.arange(groups * 96, dtype=jnp.int32)
    turn_of, group, row = index // (groups * 24), index // 24 % groups, index % 24
    own = group * 96 + (x - turn_of) % 4 * 24 + row
    return (index[:, None] == own[None, :]).astype(bf16)


def level_order_matrix(z):
    index = jnp.arange(8 * 96, dtype=jnp.int32)
    own = (z - index // 192) % 4 * 192 + index % 192
    return (index[:, None] == own[None, :]).astype(bf16)


def places(pair_of, ctx, row_count, ctx_count):
    half_size = row_count // 2
    pair = jnp.sum(
        jnp.where(ctx[:, None] == jnp.arange(ctx_count, dtype=jnp.int32)[None], pair_of[None], 0),
        axis=1,
    )
    block = jnp.stack([pair, 2 * ctx_count - 1 - pair], axis=1)
    return block[:, :, None] * half_size + jnp.arange(half_size, dtype=jnp.int32)[None, None]


def in_three(value):
    high = value.astype(bf16)
    rest = value - high.astype(f32)
    middle = rest.astype(bf16)
    return [high, middle, (rest - middle.astype(f32)).astype(bf16)]


def call(kernel, outs, *args, scratch=(), cost=None):
    def whole(shape):
        return pl.BlockSpec(shape, lambda i: (0,) * len(shape))

    return pl.pallas_call(
        kernel,
        out_shape=[jax.ShapeDtypeStruct(shape, dtype) for shape, dtype in outs],
        grid=(1,),
        in_specs=[whole(a.shape) for a in args],
        out_specs=[whole(shape) for shape, _ in outs],
        scratch_shapes=list(scratch),
        compiler_params=pltpu.CompilerParams(vmem_limit_bytes=ROOM),
        cost_estimate=COST if cost is None else cost,
    )(*args)


ROOM = 58 << 20
COST = pl.CostEstimate(flops=1 << 20, bytes_accessed=1 << 18, transcendentals=0)
LONG = pl.CostEstimate(flops=1 << 35, bytes_accessed=1 << 27, transcendentals=0)
WIDE = 2 * HD
EXPERTS = 16


def turn(vectors, cosines, sines):
    return vectors * cosines + pltpu.roll(vectors, HD // 2, axis=1) * sines


def gain_picker():
    row = lax.broadcasted_iota(jnp.int32, (8, 128), 0)
    column = lax.broadcasted_iota(jnp.int32, (8, 128), 1)
    return jnp.where((column == row + EXPERTS) & (row < 2), 1.0, 0.0).astype(bf16)


def normal_of(stream):
    inverse = lax.rsqrt(jnp.mean(stream * stream, axis=-1, keepdims=True) + EPSILON)
    return stream * inverse, inverse


def norm_back(grad, normal, inverse, gain):
    scaled = grad * gain
    return inverse * (scaled - normal * jnp.mean(scaled * normal, axis=-1, keepdims=True))


def column_block(s, count):
    return slice(s * count, (s + 1) * count)


def pack_kernel(
    flag, query, key, value, router, gain_one, gain_two, w_out, same, other, out_same, out_other
):
    last = flag[0].astype(f32)
    rows = query.shape[0]

    def store(target, rest, at, matrix):
        count = matrix.shape[1] // 2
        left, right = matrix[:, :count].astype(f32), matrix[:, count:].astype(f32)
        target[:, at : at + count] = (left * (1.0 - last) + right * last).astype(bf16)
        rest[:, at : at + count] = (right * (1.0 - last) + left * last).astype(bf16)

    store(same, other, 0, key)
    store(same, other, HD, value)
    store(same, other, 3 * HD, query)
    store(out_same, out_other, 0, w_out)
    row = lax.broadcasted_iota(jnp.int32, (rows, rows), 0)
    column = lax.broadcasted_iota(jnp.int32, (rows, rows), 1)

    def upright(gain):
        return jnp.sum(
            jnp.where(row == column, gain[...].astype(f32), 0.0), axis=1, keepdims=True
        )

    shape = (router.shape[1], 128)
    spread_out = lax.broadcasted_iota(jnp.int32, shape, 0) == lax.broadcasted_iota(
        jnp.int32, shape, 1
    )
    small = dot(router[...], jnp.where(spread_out, 1.0, 0.0).astype(bf16))
    lane = lax.broadcasted_iota(jnp.int32, small.shape, 1)
    small = small + jnp.where(lane == EXPERTS, upright(gain_one), 0.0)
    small = small + jnp.where(lane == EXPERTS + 1, upright(gain_two), 0.0)
    same[:, 2 * HD : 3 * HD] = small.astype(bf16)
    other[:, 2 * HD : 3 * HD] = small.astype(bf16)


def packed(flag, query, *arrays):
    rows, width = query.shape
    columns = 3 * HD + width // 2

    def whole(shape):
        return pl.BlockSpec(shape, lambda i, flag: (0,) * len(shape))

    outs = [(rows, columns), (rows, columns), (rows, width // 2), (rows, width // 2)]
    return pl.pallas_call(
        pack_kernel,
        out_shape=[jax.ShapeDtypeStruct(shape, bf16) for shape in outs],
        grid_spec=pltpu.PrefetchScalarGridSpec(
            num_scalar_prefetch=1,
            grid=(1,),
            in_specs=[whole(a.shape) for a in (query,) + arrays],
            out_specs=[whole(shape) for shape in outs],
        ),
        compiler_params=pltpu.CompilerParams(vmem_limit_bytes=ROOM),
        cost_estimate=COST,
    )(flag, query, *arrays)


def order_kernel(rows, order, out):
    out[...] = dot(rows[...], order[...]).astype(bf16)


def keys_kernel(both, cosines, sines, *refs):
    kvs, (normed, key_value, gains) = refs[:4], refs[4:]
    count = kvs[0].shape[0]
    for s in range(4):
        gains[:, column_block(s, count)] = dot_t(gain_picker(), kvs[s][:, WIDE:])
    normal, _ = normal_of(both[...].astype(f32))
    normed[...] = (normal * gains[0:1]).astype(bf16)
    kv = dot(normed[:, column_block(0, count)], kvs[0][:, :WIDE])
    for s in range(1, 4):
        kv = kv + dot(normed[:, column_block(s, count)], kvs[s][:, :WIDE])
    keys = turn(kv[:, :HD], cosines[...], sines[...]).astype(bf16)
    values = kv[:, HD:].astype(bf16)
    for i in range(key_value.shape[0]):
        key_value[i, :, :HD] = keys
        key_value[i, :, HD:] = values


def small_kernel(order, kvs0, kvs1, kvs2, kvs3, small, gains):
    count = kvs0.shape[0]
    total = jnp.zeros(small.shape, f32)
    for s, kvs in enumerate((kvs0, kvs1, kvs2, kvs3)):
        total = total + dot(order[:, column_block(s, count)], kvs[:, WIDE:])
    small[...] = total.astype(bf16)
    gains[...] = dot_t(gain_picker(), small[...])


def query_kernel(normed, cosines, sines, w_q0, w_q1, w_q2, w_q3, queries):
    w_q = (w_q0, w_q1, w_q2, w_q3)
    count = w_q0.shape[0]
    for h in range(queries.shape[1] // HD):
        at = column_block(h, HD)
        q = dot(normed[:, column_block(0, count)], w_q0[:, at])
        for s in range(1, 4):
            q = q + dot(normed[:, column_block(s, count)], w_q[s][:, at])
        queries[:, at] = turn(q, cosines[...], sines[...]).astype(bf16)


def attend_kernel(
    queries,
    q_place,
    low_place,
    up_place,
    order,
    order_back,
    kv,
    ordered,
    ordered_back,
    logs,
    kv_low,
    kv_up,
    mixed,
    *,
    scale,
    pieces,
    heads,
):
    half = kv.shape[1] // 2
    for i in range(pieces):
        kv_low[i * half : (i + 1) * half, :] = kv[i, :half]
        kv_up[i * half : (i + 1) * half, :] = kv[i, half:]
    allowed_low = low_place[...] <= q_place[...]
    allowed_up = up_place[...] <= q_place[half:, :]
    for h in range(heads):
        at = slice(h * HD, (h + 1) * HD)
        q = queries[:, at]
        low = jnp.where(allowed_low, dot_t(q, kv_low[:, :HD]) * scale, NEGATIVE)
        up = jnp.where(allowed_up, dot_t(q[half:], kv_up[:, :HD]) * scale, NEGATIVE)
        first, second = low[:half], low[half:]
        top = jnp.max(first, axis=-1, keepdims=True)
        weight = jnp.exp(first - top)
        total = jnp.sum(weight, axis=-1, keepdims=True)
        probs = (weight / total).astype(bf16)
        mixed[:half, at] = dot(probs, kv_low[:, HD:]).astype(bf16)
        logs[h, :half, :] = top + jnp.log(total)
        top = jnp.maximum(
            jnp.max(second, axis=-1, keepdims=True), jnp.max(up, axis=-1, keepdims=True)
        )
        weight, weight_up = jnp.exp(second - top), jnp.exp(up - top)
        total = jnp.sum(weight, axis=-1, keepdims=True) + jnp.sum(
            weight_up, axis=-1, keepdims=True
        )
        mixed[half:, at] = (
            dot((weight / total).astype(bf16), kv_low[:, HD:])
            + dot((weight_up / total).astype(bf16), kv_up[:, HD:])
        ).astype(bf16)
        logs[h, half:, :] = top + jnp.log(total)
    ordered[...] = dot(mixed[...], order[...]).astype(bf16)
    ordered_back[...] = dot(mixed[...], order_back[...]).astype(bf16)


def branch_kernel(mixed, w_out0, w_out1, w_out2, w_out3, own, other, w_out):
    quarter = mixed.shape[0] // 4
    count, columns = w_out0.shape[1:]
    for s, part in enumerate((w_out0, w_out1, w_out2, w_out3)):
        w_out[:, column_block(s, count)] = part[...]
    for k in range(2):
        part = dot(mixed[...], w_out[k])
        at = slice(k * columns, (k + 1) * columns)
        own[:quarter, at] = part[:quarter]
        other[:quarter, at] = part[quarter : 2 * quarter]
        own[quarter:, at] = part[2 * quarter : 3 * quarter]
        other[quarter:, at] = part[3 * quarter :]


def route_kernel(
    tokens,
    own,
    received,
    small,
    gains,
    hits,
    places_of,
    placer,
    sent,
    midway,
    moe_low,
    gates,
    parts,
):
    middle = tokens[...].astype(f32) + (own[...] + received[...])
    midway[...] = middle
    normal, _ = normal_of(middle)
    moe = (normal * gains[1:2]).astype(bf16)
    moe_low[...] = moe
    sent[:, : moe.shape[1]] = dot(placer[...], moe).astype(bf16)
    logits = dot(moe, small[...])
    picked = [
        jnp.sum(hits[k].astype(f32) * logits, axis=-1, keepdims=True) for k in range(TOPK)
    ]
    top = picked[0]
    for value in picked[1:]:
        top = jnp.maximum(top, value)
    weights = [jnp.exp(value - top) for value in picked]
    total = weights[0]
    for value in weights[1:]:
        total = total + value
    lane = lax.broadcasted_iota(jnp.int32, gates.shape, 1)
    gate_at = jnp.zeros(places_of.shape[1:], f32)
    kept = jnp.zeros(gates.shape, f32)
    for k in range(TOPK):
        gate = weights[k] / total
        kept = jnp.where(lane == k, gate, kept)
        gate_at = gate_at + places_of[k].astype(f32) * gate
    gates[...] = kept
    block = jnp.zeros((sent.shape[0], 128), f32)
    for i, part in enumerate(in_three(gate_at)):
        parts[i] = part
        block = block + t_dot(part, jnp.where(lane == i, 1.0, 0.0).astype(bf16))
    sent[:, moe.shape[1] :] = block.astype(bf16)


def expert_kernel(
    core, sent, cot, weights, out, rows_grad, hidden, out_grad, gate_grad, up_grad, held, sems
):
    copies = [
        pltpu.make_async_copy(weights.at[m, core[0]], held.at[m], sems.at[m]) for m in range(3)
    ]
    for copy in copies:
        copy.start()
    width = out.shape[1]
    gates = jnp.sum(sent[:, width:].astype(f32), axis=-1, keepdims=True)
    out_grad[...] = (gates * cot[...].astype(f32)).astype(bf16)
    rows = sent[:, :width]
    copies[0].wait()
    gate_pre = dot(rows, held[0])
    copies[1].wait()
    up_pre = dot(rows, held[1])
    sigmoid = 1.0 / (1.0 + jnp.exp(-gate_pre))
    silu = gate_pre * sigmoid
    low = (silu * up_pre).astype(bf16)
    hidden[...] = low
    copies[2].wait()
    hidden_grad = dot(out_grad[...], held[2])
    gate_low = (hidden_grad * up_pre * sigmoid * (1.0 + gate_pre * (1.0 - sigmoid))).astype(bf16)
    up_low = (hidden_grad * silu).astype(bf16)
    gate_grad[...] = gate_low
    up_grad[...] = up_low
    rows_grad[:, :width] = (dot_t(gate_low, held[0]) + dot_t(up_low, held[1])).astype(bf16)
    result = dot_t(low, held[2]).astype(bf16)
    out[...] = result
    grads = in_three(
        jnp.sum(cot[...].astype(f32) * result.astype(f32), axis=-1, keepdims=True)
    )
    lane = lax.broadcasted_iota(jnp.int32, (cot.shape[0], 128), 1)
    block = jnp.zeros(lane.shape, f32)
    for i, part in enumerate(grads):
        block = jnp.where(lane == i, part.astype(f32), block)
    rows_grad[:, width:] = block.astype(bf16)


def expert_call(core, arrays, weights, outs):
    rows = arrays[0].shape[0]

    def whole(columns):
        return pl.BlockSpec(
            (rows, columns), lambda i, core: (0, 0), pipeline_mode=pl.Buffered(1)
        )

    return pl.pallas_call(
        expert_kernel,
        out_shape=[jax.ShapeDtypeStruct((rows, columns), bf16) for columns in outs],
        grid_spec=pltpu.PrefetchScalarGridSpec(
            num_scalar_prefetch=1,
            grid=(1,),
            in_specs=[whole(a.shape[1]) for a in arrays] + [pl.BlockSpec(memory_space=pltpu.HBM)],
            out_specs=[whole(columns) for columns in outs],
            scratch_shapes=[
                pltpu.VMEM((3,) + weights.shape[2:], bf16),
                pltpu.SemaphoreType.DMA((3,)),
            ],
        ),
        compiler_params=pltpu.CompilerParams(vmem_limit_bytes=ROOM),
        cost_estimate=COST,
    )(core, *arrays, weights)


def weights_kernel(sent, out_grad, hidden, gate_grad, up_grad, sums):
    rows = sent[...]
    sums[0] = t_dot(rows, gate_grad[...]).astype(bf16)
    sums[1] = t_dot(rows, up_grad[...]).astype(bf16)
    sums[2] = t_dot(out_grad[...], hidden[...]).astype(bf16)


def expert_weights_grad(sent, out_grad, hidden, gate_grad, up_grad, block=256):
    count, width = out_grad.shape
    columns = hidden.shape[1]
    part = pl.BlockSpec((count, block), lambda i: (0, i))
    whole = pl.BlockSpec((count, columns), lambda i: (0, 0), pipeline_mode=pl.Buffered(1))
    return pl.pallas_call(
        weights_kernel,
        out_shape=jax.ShapeDtypeStruct((3, width, columns), bf16),
        grid=(width // block,),
        in_specs=[part, part, whole, whole, whole],
        out_specs=pl.BlockSpec((3, block, columns), lambda i: (0, i, 0)),
        compiler_params=pltpu.CompilerParams(vmem_limit_bytes=ROOM),
        cost_estimate=COST,
    )(sent, out_grad, hidden, gate_grad, up_grad)


def combine_kernel(midway, parts, returned, output):
    rows = returned[...]
    output[...] = (
        midway[...] + (dot(parts[0], rows) + (dot(parts[1], rows) + dot(parts[2], rows)))
    ).astype(bf16)


def home_kernel(
    placer_t,
    home,
    midway,
    cot,
    gains,
    hits,
    places_of,
    gates,
    small,
    moe_low,
    midway_grad,
    branch_low,
    gain_grad,
    router_grad,
):
    width = midway.shape[1]
    lane = lax.broadcasted_iota(jnp.int32, gates.shape, 1)
    gate, gate_grad = [], []
    mean = jnp.zeros((gates.shape[0], 1), f32)
    for k in range(TOPK):
        gate.append(jnp.sum(jnp.where(lane == k, gates[...], 0.0), axis=-1, keepdims=True))
        gate_grad.append(
            jnp.sum(dot(places_of[k], home[:, width:]), axis=-1, keepdims=True)
        )
        mean = mean + gate[k] * gate_grad[k]
    logit_grad = jnp.zeros(gates.shape, f32)
    for k in range(TOPK):
        logit_grad = logit_grad + hits[k].astype(f32) * (gate[k] * (gate_grad[k] - mean))
    logit_grad = logit_grad.astype(bf16)
    router_grad[...] = t_dot(moe_low[...], logit_grad)
    grad = dot(placer_t[...], home[:, :width]) + dot_t(logit_grad, small[...])
    normal, inverse = normal_of(midway[...])
    result = cot[...].astype(f32) + norm_back(grad, normal, inverse, gains[1:2])
    midway_grad[...] = result
    branch_low[...] = result.astype(bf16)
    gain_grad[...] = jnp.broadcast_to(
        jnp.sum(grad * normal, axis=0, keepdims=True), gain_grad.shape
    )


def out_grad_kernel(mixed, own, other, branch, *blocks):
    quarter = own.shape[0] // 2
    branch[:quarter] = own[:quarter]
    branch[quarter : 2 * quarter] = other[:quarter]
    branch[2 * quarter : 3 * quarter] = own[quarter:]
    branch[3 * quarter :] = other[quarter:]
    count, columns = blocks[0].shape[1:]
    for k in range(2):
        grad = t_dot(mixed[...], branch[:, column_block(k, columns)]).astype(bf16)
        for s in range(4):
            blocks[s][k] = grad[column_block(s, count)]


def attend_back_kernel(
    branch,
    w_out,
    order,
    queries,
    kv_low,
    kv_up,
    logs,
    q_place,
    low_place,
    up_place,
    cosines,
    sines,
    normed,
    dq,
    dkv,
    block0,
    block1,
    block2,
    block3,
    grads,
    acc_low,
    acc_up,
    *,
    scale,
    pieces,
    heads,
):
    half = queries.shape[0] // 2
    columns = w_out.shape[2]
    ordered = dot_t(branch[:, :columns], w_out[0]) + dot_t(branch[:, columns:], w_out[1])
    grads[...] = dot_t(ordered.astype(bf16), order[...]).astype(bf16)
    allowed_low = low_place[...] <= q_place[...]
    allowed_up = up_place[...] <= q_place[half:, :]
    key_low, value_low = kv_low[:, :HD], kv_low[:, HD:]
    key_up, value_up = kv_up[:, :HD], kv_up[:, HD:]
    for h in range(heads):
        at = slice(h * HD, (h + 1) * HD)
        q, grad, log = queries[:, at], grads[:, at], logs[h]
        low = jnp.where(allowed_low, dot_t(q, key_low) * scale, NEGATIVE)
        up = jnp.where(allowed_up, dot_t(q[half:], key_up) * scale, NEGATIVE)
        probs_low, probs_up = jnp.exp(low - log), jnp.exp(up - log[half:])
        grad_low, grad_up = dot_t(grad, value_low), dot_t(grad[half:], value_up)
        along = jnp.sum(probs_low * grad_low, axis=-1, keepdims=True)
        along_up = along[half:] + jnp.sum(probs_up * grad_up, axis=-1, keepdims=True)
        along = jnp.concatenate([along[:half], along_up])
        score_low = (probs_low * (grad_low - along)).astype(bf16)
        score_up = (probs_up * (grad_up - along_up)).astype(bf16)
        part = dot(score_low, key_low)
        part = jnp.concatenate([part[:half], part[half:] + dot(score_up, key_up)]) * scale
        dq[:, at] = turn(part, cosines[...], -sines[...]).astype(bf16)
        terms = (
            (acc_low, slice(0, HD), t_dot(q, score_low)),
            (acc_up, slice(0, HD), t_dot(q[half:], score_up)),
            (acc_low, slice(HD, 2 * HD), t_dot(grad, probs_low.astype(bf16))),
            (acc_up, slice(HD, 2 * HD), t_dot(grad[half:], probs_up.astype(bf16))),
        )
        for acc, rows, term in terms:
            if h == 0:
                acc[rows] = term
            else:
                acc[rows] += term
    for s, block in enumerate((block0, block1, block2, block3)):
        block[...] = t_dot(normed[:, column_block(s, block.shape[0])], dq[...]).astype(bf16)
    for acc, first in ((acc_low, 0), (acc_up, half)):
        dk = (acc[:HD].T * scale).astype(bf16)
        dv = acc[HD:].T.astype(bf16)
        for i in range(pieces):
            dkv[i, first : first + half, :HD] = dk[i * half : (i + 1) * half]
            dkv[i, first : first + half, HD:] = dv[i * half : (i + 1) * half]


def sum_kernel(dq, cosines, sines, *refs):
    w_q, kvs, (parts, dkv, own, other) = refs[:4], refs[4:8], refs[8:]
    total = jnp.sum(parts[...].astype(f32), axis=0)
    dkv[:, :HD] = turn(total[:, :HD], cosines[...], -sines[...]).astype(bf16)
    dkv[:, HD:] = total[:, HD:].astype(bf16)
    quarter = own.shape[0] // 2
    for s in range(4):
        grad = dot_t(dq[...], w_q[s][...]) + dot_t(dkv[...], kvs[s][:, :WIDE])
        at = column_block(s, w_q[s].shape[0])
        own[:quarter, at] = grad[:quarter]
        other[:quarter, at] = grad[quarter : 2 * quarter]
        own[quarter:, at] = grad[2 * quarter : 3 * quarter]
        other[quarter:, at] = grad[3 * quarter :]


def stack_kernel(gate, up, down, late, out):
    del late
    out[0] = gate[...]
    out[1] = up[...]
    out[2] = down[...]


def small_grad_kernel(order, router_grad, gain_grad, late, out):
    del late
    row = lax.broadcasted_iota(jnp.int32, gain_grad.shape, 0)
    second = jnp.where(row == 1, gain_grad[...], 0.0).astype(bf16)
    small = router_grad[...] + t_dot(second, gain_picker())
    out[...] = t_dot(order[...], small.astype(bf16))


def input_kernel(both, own, received, midway_grad, gains, order, small, normed, dkv, out, *blocks):
    grad = own[...] + received[...]
    quarter = own.shape[0] // 2
    tokens = jnp.concatenate([both[:quarter], both[2 * quarter : 3 * quarter]])
    normal, inverse = normal_of(tokens.astype(f32))
    parts = in_three(norm_back(grad, normal, inverse, gains[0:1]))
    moved = dot_t(jnp.concatenate(parts), order[...])
    count = 2 * quarter
    out[...] = midway_grad[...] + (
        moved[:count] + (moved[count : 2 * count] + moved[2 * count :])
    )
    gain_grad = jnp.sum(grad * normal, axis=0, keepdims=True)
    row = lax.broadcasted_iota(jnp.int32, gains.shape, 0)
    gain_grad = jnp.where(row == 0, gain_grad, 0.0).astype(bf16)
    small = small[...] + t_dot(gain_grad, gain_picker())
    rows = blocks[0].shape[0]
    for s, block in enumerate(blocks):
        at = column_block(s, rows)
        block[:, :WIDE] = t_dot(normed[:, at], dkv[...]).astype(bf16)
        block[:, WIDE:] = small[at].astype(bf16)


def body(
    tokens,
    cotangent,
    pair_of,
    routes,
    attn_gain,
    moe_gain,
    w_query,
    w_key,
    w_value,
    w_out,
    w_router,
    w_gate,
    w_up,
    w_down,
):
    rows = tokens.shape[1]
    half = rows // 2
    width = tokens.shape[2]
    shard = w_query.shape[1]
    ctx_count = 16
    experts = w_router.shape[2]
    columns = w_gate.shape[3]
    per_group = H // KVH
    qw = per_group * HD
    scale = 1.0 / math.sqrt(HD)
    core = lax.axis_index("core")
    ylo, z, yhi = lax.axis_index("ylo"), lax.axis_index("z"), lax.axis_index("yhi")
    x = lax.axis_index("x")
    piece_rows = 2 * shard
    slots = experts * SLOTS
    own_tokens, cot = tokens[0], cotangent[0]

    same, other, out_same, out_other = packed(
        yhi.reshape(1), w_query[0], w_key[0], w_value[0], w_router[0], attn_gain, moe_gain, w_out[0]
    )
    pieces = gather_pieces(same, other, core, ("core", "yhi"), SAME, OTHER)
    out_pieces = gather_pieces(
        out_same, out_other, yhi, ("ylo", "core", "yhi"), OUT_SAME, OUT_OTHER
    )
    other_tokens = partner(own_tokens)
    pieces, out_pieces, x, z, own_tokens, other_tokens, pair_of = together(
        pieces, out_pieces, x, z, own_tokens, other_tokens, pair_of
    )

    plane_rows = 16 * piece_rows
    plane = spread(pieces, 16, PLANE)
    both = jnp.concatenate(
        [own_tokens[:half], other_tokens[:half], own_tokens[half:], other_tokens[half:]]
    )
    order, out_order, level_order = order_matrix(16, x), order_matrix(8, x), level_order_matrix(z)
    (expert_shards_in,) = call(
        stack_kernel, [((3,) + w_gate.shape[1:], bf16)], w_gate[0], w_up[0], w_down[0], both
    )
    (
        plane, both, out_pieces, order, out_order, level_order, pair_of, expert_shards_in, chosen,
    ) = together(
        plane, both, out_pieces, order, out_order, level_order, pair_of, expert_shards_in,
        routes[0, 0],
    )

    plane = plane.reshape(plane_rows, -1)
    w_kvs = along("x", plane[:, : 3 * HD])
    wo = spread(out_pieces, 16, LEVEL)
    (both,) = call(order_kernel, [((2 * rows, width), bf16)], both, order)

    def two_cores(ctx):
        return jnp.stack([ctx + core, ctx + 1 - core], axis=-1).reshape(-1)

    ctx_here = (ylo * 4 + z) * 2
    q_place = places(pair_of, two_cores(ctx_here), rows, ctx_count)
    q_place = q_place.transpose(1, 0, 2).reshape(2 * rows, 1)
    key_place = places(
        pair_of, two_cores(jnp.arange(8, dtype=jnp.int32) * 2), rows, ctx_count
    )
    low_place, up_place = key_place[:, 0].reshape(1, -1), key_place[:, 1].reshape(1, -1)
    frequency = jnp.exp(jnp.arange(HD // 2, dtype=f32) * (-2.0 * math.log(ROPE_BASE) / HD))
    angles = q_place.astype(f32) * frequency[None, :]
    cosines, sines = jnp.cos(angles), jnp.sin(angles)
    cosines = jnp.concatenate([cosines, cosines], axis=-1)
    sines = jnp.concatenate([-sines, sines], axis=-1)
    w_q, w_kvs, wo, both, q_place, low_place, up_place, cosines, sines, chosen = together(
        plane[:, 3 * HD :], w_kvs, wo, both, q_place, low_place, up_place, cosines, sines, chosen
    )

    w_q = along("x", w_q)
    wo = along("z", wo.reshape(2, qw // 4, width // 2))
    normed, key_value, gains = call(
        keys_kernel,
        [((2 * rows, width), bf16), ((8, 2 * rows, 2 * HD), bf16), ((8, width), f32)],
        both,
        cosines,
        sines,
        *w_kvs,
    )
    all_kv = exchange(key_value, RING)
    small, moe_gains = call(
        small_kernel, [((width, 128), bf16), ((8, width), f32)], order, *w_kvs
    )
    (queries,) = call(
        query_kernel, [((2 * rows, qw), bf16)], normed, cosines, sines, *w_q, cost=LONG
    )
    lanes = jnp.arange(128, dtype=jnp.int32)
    hits = (chosen.T[:, :, None] == lanes[None, None, :]).astype(bf16)
    earlier = (lanes[:, None] > lanes[None, :]).astype(bf16)
    before = dot(earlier, jnp.sum(hits, axis=0))
    slot_index = jnp.sum(hits.astype(f32) * before[None], axis=-1).astype(jnp.int32)
    target = chosen.T * SLOTS + slot_index
    slot_row = jnp.arange(slots, dtype=jnp.int32)
    places_of = (target[:, :, None] == slot_row[None, None, :]).astype(bf16)
    placer_t = jnp.sum(places_of, axis=0)
    placer = placer_t.T
    (cot_rows,) = call(order_kernel, [((slots, width), bf16)], placer, cot)
    (
        queries, all_kv, expert_shards_in, small, moe_gains, cot_rows,
        hits, places_of, placer_t, placer, wo,
    ) = together(
        queries, all_kv, expert_shards_in, small, moe_gains, cot_rows,
        hits, places_of, placer_t, placer, wo,
    )
    expert_weights = lax.all_gather(expert_shards_in, CTX, axis=2, tiled=True)

    arrived_cot = to_owners(cot_rows.reshape(experts, SLOTS, width))
    sizes = dict(scale=scale, pieces=8, heads=per_group)
    keys = 8 * rows
    mixed, mixed_back, logs, kv_low, kv_up = call(
        functools.partial(attend_kernel, **sizes),
        [
            ((2 * rows, qw), bf16),
            ((2 * rows, qw), bf16),
            ((per_group, 2 * rows, 1), f32),
            ((keys, 2 * HD), bf16),
            ((keys, 2 * HD), bf16),
        ],
        queries,
        q_place,
        low_place,
        up_place,
        level_order,
        out_order,
        all_kv,
        scratch=[pltpu.VMEM((2 * rows, qw), bf16)],
    )

    branch_own, branch_other, wo = call(
        branch_kernel,
        [((rows, width), f32), ((rows, width), f32), ((2, qw, width // 2), bf16)],
        mixed,
        *wo,
    )
    sent, midway, moe_low, gates, gate_parts = call(
        route_kernel,
        [
            ((slots, width + 128), bf16),
            ((rows, width), f32),
            ((rows, width), bf16),
            ((rows, 128), f32),
            ((3, rows, slots), bf16),
        ],
        own_tokens,
        branch_own,
        partner(branch_other),
        small,
        moe_gains,
        hits,
        places_of,
        placer,
    )
    sent, arrived_cot = together(sent, arrived_cot)

    sent = to_owners(sent.reshape(experts, SLOTS, width + 128)).reshape(slots, width + 128)
    mine = core.reshape(1)
    expert_out, rows_grad, hidden, out_grad, gate_grad, up_grad = expert_call(
        mine,
        [sent, arrived_cot.reshape(slots, width)],
        expert_weights,
        [width, width + 128, columns, width, columns, columns],
    )
    rows_grad, gate_grad, up_grad = together(rows_grad, gate_grad, up_grad)

    home_grad = to_owners(rows_grad.reshape(experts, SLOTS, width + 128))
    expert_sums = expert_weights_grad(sent, out_grad, hidden, gate_grad, up_grad)
    home_grad, expert_sums, expert_out = together(home_grad, expert_sums, expert_out)
    expert_sums = lax.psum_scatter(expert_sums, RING, scatter_dimension=1, tiled=True)

    returned = to_owners(expert_out.reshape(experts, SLOTS, width))
    midway_grad, branch_low, gain_two_grad, router_grad = call(
        home_kernel,
        [((rows, width), f32), ((rows, width), bf16), ((8, width), f32), ((width, 128), f32)],
        placer_t,
        home_grad.reshape(slots, width + 128),
        midway,
        cot,
        moe_gains,
        hits,
        places_of,
        gates,
        small,
        moe_low,
    )
    branch, *out_w_grad = call(
        out_grad_kernel,
        [((2 * rows, width), bf16)] + [((2, qw // 4, width // 2), bf16)] * 4,
        mixed_back,
        branch_low,
        partner(branch_low),
    )
    branch, out_w_grad = together(branch, out_w_grad)
    out_w_grad = back_along_x(out_w_grad)

    dq, dkv, *q_w_grad = call(
        functools.partial(attend_back_kernel, **sizes),
        [((2 * rows, qw), bf16), ((8, 2 * rows, 2 * HD), bf16)]
        + [((plane_rows, qw), bf16)] * 4,
        branch,
        wo,
        level_order,
        queries,
        kv_low,
        kv_up,
        logs,
        q_place,
        low_place,
        up_place,
        cosines,
        sines,
        normed,
        scratch=[
            pltpu.VMEM((2 * rows, qw), bf16),
            pltpu.VMEM((2 * HD, keys), f32),
            pltpu.VMEM((2 * HD, keys), f32),
        ],
    )
    dkv, q_w_grad, returned, late = together(dkv, q_w_grad, returned, gain_two_grad)

    dkv = exchange(dkv, RING)
    q_w_grad = back_along_x(q_w_grad)
    (small_grad,) = call(
        small_grad_kernel, [((width, 128), f32)], order, router_grad, gain_two_grad, late
    )
    out_w_grad = added(out_w_grad, small_grad)
    dkv, out_w_grad, small_grad, q_w_grad[1], q_w_grad[3] = together(
        dkv, out_w_grad, small_grad, q_w_grad[1], q_w_grad[3]
    )

    dkv, normed_own, normed_other = call(
        sum_kernel,
        [((2 * rows, 2 * HD), bf16), ((rows, width), f32), ((rows, width), f32)],
        dq,
        cosines,
        sines,
        *w_q,
        *w_kvs,
        dkv,
    )
    input_grad, *kvs_grad = call(
        input_kernel,
        [((rows, width), f32)] + [((plane_rows, 3 * HD), bf16)] * 4,
        both,
        normed_own,
        partner(normed_other),
        midway_grad,
        gains,
        order,
        small_grad,
        normed,
        dkv,
    )
    kvs_grad, out_w_grad, input_grad = together(kvs_grad, out_w_grad, input_grad)

    out_w_grad = exchange(out_w_grad.reshape(16, piece_rows, width // 2), OUT_PLANE)
    kvs_grad = back_along_x(kvs_grad)
    (plane_grad,) = call(
        add_both_kernel, [((plane_rows, qw + 3 * HD), bf16)], *q_w_grad, *kvs_grad, cost=LONG
    )
    plane_grad, out_w_grad, returned = together(plane_grad, out_w_grad, returned)
    plane_grad = exchange(plane_grad.reshape(16, piece_rows, qw + 3 * HD), PLANE)

    (output,) = call(
        combine_kernel,
        [((rows, width), bf16)],
        midway,
        gate_parts,
        returned.reshape(slots, width),
    )

    def summed(pieces):
        return jnp.sum(pieces.astype(f32), axis=0)

    def expert_shards(grad):
        count = grad.shape[1] // 2
        kept = lax.dynamic_slice_in_dim(grad, core * count, count, axis=1)
        given = partner(lax.dynamic_slice_in_dim(grad, (1 - core) * count, count, axis=1))
        both = jnp.stack([pick(core, kept, given), pick(core, given, kept)], axis=1)
        return [both[i : i + 1].astype(f32) for i in range(3)]

    out_w_grad = scatter_pieces(
        summed(out_w_grad), yhi, yhi, ("ylo", "core", "yhi"), OUT_SAME, OUT_OTHER
    )
    w_gate_grad, w_up_grad, w_down_grad = expert_shards(expert_sums)
    plane_grad, out_w_grad, w_gate_grad, w_up_grad, w_down_grad, output = together(
        plane_grad, out_w_grad, w_gate_grad, w_up_grad, w_down_grad, output
    )
    plane_grad = scatter_pieces(summed(plane_grad), yhi, core, ("core", "yhi"), SAME, OTHER)
    plane_grad = plane_grad.reshape(shard, 2, -1)

    def joined(first, last):
        return plane_grad[:, :, first:last].reshape(1, shard, -1)

    small_grad = jnp.sum(plane_grad[None, :, :, qw + 2 * HD :], axis=2)

    return (
        output[None],
        input_grad[None],
        small_grad[:, :, experts],
        small_grad[:, :, experts + 1],
        joined(0, qw),
        joined(qw, qw + HD),
        joined(qw + HD, qw + 2 * HD),
        out_w_grad[None],
        small_grad[:, :, :experts],
        w_gate_grad,
        w_up_grad,
        w_down_grad,
    )


def solution(mesh):
    fine = Mesh(mesh.devices.reshape(2, 4, 2, 4, 2), AXES)
    seq = P(FSDP, CTX, None)
    vector = P(None, AXES)
    matrix = P(None, AXES, None)
    expert = P(None, FSDP, CTX, None)
    in_specs = (
        seq,
        seq,
        P(),
        P(None, FSDP, CTX, None),
        vector,
        vector,
        matrix,
        matrix,
        matrix,
        matrix,
        matrix,
        expert,
        expert,
        expert,
    )
    out_specs = (
        seq,
        seq,
        vector,
        vector,
        matrix,
        matrix,
        matrix,
        matrix,
        matrix,
        expert,
        expert,
        expert,
    )
    return jax.shard_map(body, mesh=fine, in_specs=in_specs, out_specs=out_specs, check_vma=False)
```

```python
import functools
import math

import jax
import jax.numpy as jnp
from jax import lax
from jax.experimental import pallas as pl
from jax.experimental.pallas import tpu as pltpu
from jax.sharding import Mesh
from jax.sharding import PartitionSpec as P

H = 12
KVH = 2
HD = 128
TOPK = 4

EPSILON = 1e-06
ROPE_BASE = 1000000.0
NEGATIVE = -1e30

AXES = ("ylo", "z", "core", "x", "yhi")
CTX = ("ylo", "z", "core")
FSDP = ("x", "yhi")
GROUPS = [
    [
        (((group ^ yhi) * 4 + z) * 2 + core) * 8 + x * 2 + yhi
        for x in range(4)
        for yhi in range(2)
        for core in range(2)
    ]
    for group in range(2)
    for z in range(4)
]
RING = ("ylo", "z")
PLANE = ("ylo", "z", "yhi")
OUT_PLANE = ("yhi", "z", "ylo")
LEVEL = ("yhi", "ylo", "x")
GROUPS = [
    [
        (((group ^ yhi) * 4 + z) * 2 + core) * 8 + x * 2 + yhi
        for x in range(4)
        for yhi in range(2)
        for core in range(2)
    ]
    for group in range(2)
    for z in range(4)
]
RING = ("ylo", "z")
ROWS_ORDER = ("ylo", "z", "yhi", "x")
OUT_ORDER = ("yhi", "z", "ylo", "x")
SLOTS = 40

bf16 = jnp.bfloat16
f32 = jnp.float32


def dot(left, right):
    return jnp.dot(left, right, preferred_element_type=f32)


def dot_t(left, right):
    return lax.dot_general(left, right, (((1,), (1,)), ((), ())), preferred_element_type=f32)


def t_dot(left, right):
    return lax.dot_general(left, right, (((0,), (0,)), ((), ())), preferred_element_type=f32)


def exchange(pieces, axes):
    return lax.all_to_all(pieces, axes, split_axis=0, concat_axis=0, tiled=True)


def to_owners(pieces):
    return lax.all_to_all(
        pieces, AXES, split_axis=0, concat_axis=0, axis_index_groups=GROUPS, tiled=True
    )


def spread(piece, count, axes):
    return exchange(jnp.broadcast_to(piece[None], (count,) + piece.shape), axes)


def after(value, earlier):
    return lax.optimization_barrier((value, earlier))[0]


def together(*values):
    return lax.optimization_barrier(values)


def partner(value):
    return lax.ppermute(value, "core", [(0, 1), (1, 0)])


def route(axes, sizes, move):
    pairs = []
    for source in range(math.prod(sizes)):
        rest, at = source, []
        for size in reversed(sizes):
            at.insert(0, rest % size)
            rest //= size
        target = 0
        for size, value in zip(sizes, move(*at)):
            target = target * size + value
        pairs.append((source, target))
    return pairs


SAME = route(("core", "yhi"), (2, 2), lambda c, h: (h, c))
OTHER = route(("core", "yhi"), (2, 2), lambda c, h: (1 - h, c))
OUT_SAME = route(("ylo", "core", "yhi"), (2, 2, 2), lambda j, c, h: (c, j, h))
OUT_OTHER = route(("ylo", "core", "yhi"), (2, 2, 2), lambda j, c, h: (c, j, 1 - h))


def back(pairs):
    return [(target, source) for source, target in pairs]


def pick(flag, if_zero, if_one):
    return jnp.where(flag == 0, if_zero, if_one)


def gather_pieces(first, second, key, axes, same, other):
    first = lax.ppermute(first, axes, same)
    second = lax.ppermute(second, axes, other)
    return pick(
        key, jnp.concatenate([first, second]), jnp.concatenate([second, first])
    )


def scatter_pieces(piece, flag, key, axes, same, other):
    count = piece.shape[0] // 2
    mine, rest = piece[:count], piece[count:]
    first = lax.ppermute(pick(key, mine, rest), axes, back(same))
    second = lax.ppermute(pick(key, rest, mine), axes, back(other))
    return pick(flag, jnp.concatenate([first, second], axis=-1), jnp.concatenate([second, first], axis=-1))


def along(axis, piece):
    return [piece] + [
        lax.ppermute(piece, axis, [(i, (i + s) % 4) for i in range(4)]) for s in (1, 2, 3)
    ]


def back_along_x(blocks):
    return [blocks[0]] + [
        lax.ppermute(blocks[s], "x", [(i, (i - s) % 4) for i in range(4)]) for s in (1, 2, 3)
    ]


def added(blocks, *late):
    (total,) = call(add_kernel, [(blocks[0].shape, bf16)], *blocks, *late, cost=LONG)
    return total


def sum_of(first, second, third, fourth):
    return (
        (first[...].astype(f32) + second[...].astype(f32))
        + (third[...].astype(f32) + fourth[...].astype(f32))
    ).astype(bf16)


def add_kernel(first, second, third, fourth, *refs):
    refs[-1][...] = sum_of(first, second, third, fourth)


def add_both_kernel(*refs):
    total = refs[8]
    count = refs[0].shape[1]
    total[:, :count] = sum_of(*refs[:4])
    total[:, count:] = sum_of(*refs[4:8])


def order_matrix(groups, x):
    index = jnp.arange(groups * 96, dtype=jnp.int32)
    turn_of, group, row = index // (groups * 24), index // 24 % groups, index % 24
    own = group * 96 + (x - turn_of) % 4 * 24 + row
    return (index[:, None] == own[None, :]).astype(bf16)


def level_order_matrix(z):
    index = jnp.arange(8 * 96, dtype=jnp.int32)
    own = (z - index // 192) % 4 * 192 + index % 192
    return (index[:, None] == own[None, :]).astype(bf16)


def places(pair_of, ctx, row_count, ctx_count):
    half_size = row_count // 2
    pair = jnp.sum(
        jnp.where(ctx[:, None] == jnp.arange(ctx_count, dtype=jnp.int32)[None], pair_of[None], 0),
        axis=1,
    )
    block = jnp.stack([pair, 2 * ctx_count - 1 - pair], axis=1)
    return block[:, :, None] * half_size + jnp.arange(half_size, dtype=jnp.int32)[None, None]


def in_three(value):
    high = value.astype(bf16)
    rest = value - high.astype(f32)
    middle = rest.astype(bf16)
    return [high, middle, (rest - middle.astype(f32)).astype(bf16)]


def call(kernel, outs, *args, scratch=(), cost=None):
    def whole(shape):
        return pl.BlockSpec(shape, lambda i: (0,) * len(shape))

    return pl.pallas_call(
        kernel,
        out_shape=[jax.ShapeDtypeStruct(shape, dtype) for shape, dtype in outs],
        grid=(1,),
        in_specs=[whole(a.shape) for a in args],
        out_specs=[whole(shape) for shape, _ in outs],
        scratch_shapes=list(scratch),
        compiler_params=pltpu.CompilerParams(vmem_limit_bytes=ROOM),
        cost_estimate=COST if cost is None else cost,
    )(*args)


ROOM = 58 << 20
COST = pl.CostEstimate(flops=1 << 20, bytes_accessed=1 << 18, transcendentals=0)
LONG = pl.CostEstimate(flops=1 << 35, bytes_accessed=1 << 27, transcendentals=0)
WIDE = 2 * HD
EXPERTS = 16


def turn(vectors, cosines, sines):
    return vectors * cosines + pltpu.roll(vectors, HD // 2, axis=1) * sines


def gain_picker():
    row = lax.broadcasted_iota(jnp.int32, (8, 128), 0)
    column = lax.broadcasted_iota(jnp.int32, (8, 128), 1)
    return jnp.where((column == row + EXPERTS) & (row < 2), 1.0, 0.0).astype(bf16)


def normal_of(stream):
    inverse = lax.rsqrt(jnp.mean(stream * stream, axis=-1, keepdims=True) + EPSILON)
    return stream * inverse, inverse


def norm_back(grad, normal, inverse, gain):
    scaled = grad * gain
    return inverse * (scaled - normal * jnp.mean(scaled * normal, axis=-1, keepdims=True))


def column_block(s, count):
    return slice(s * count, (s + 1) * count)


def pack_kernel(
    flag, query, key, value, router, gain_one, gain_two, w_out, same, other, out_same, out_other
):
    last = flag[0].astype(f32)
    rows = query.shape[0]

    def store(target, rest, at, matrix):
        count = matrix.shape[1] // 2
        left, right = matrix[:, :count].astype(f32), matrix[:, count:].astype(f32)
        target[:, at : at + count] = (left * (1.0 - last) + right * last).astype(bf16)
        rest[:, at : at + count] = (right * (1.0 - last) + left * last).astype(bf16)

    store(same, other, 0, key)
    store(same, other, HD, value)
    store(same, other, 3 * HD, query)
    store(out_same, out_other, 0, w_out)
    row = lax.broadcasted_iota(jnp.int32, (rows, rows), 0)
    column = lax.broadcasted_iota(jnp.int32, (rows, rows), 1)

    def upright(gain):
        return jnp.sum(
            jnp.where(row == column, gain[...].astype(f32), 0.0), axis=1, keepdims=True
        )

    shape = (router.shape[1], 128)
    spread_out = lax.broadcasted_iota(jnp.int32, shape, 0) == lax.broadcasted_iota(
        jnp.int32, shape, 1
    )
    small = dot(router[...], jnp.where(spread_out, 1.0, 0.0).astype(bf16))
    lane = lax.broadcasted_iota(jnp.int32, small.shape, 1)
    small = small + jnp.where(lane == EXPERTS, upright(gain_one), 0.0)
    small = small + jnp.where(lane == EXPERTS + 1, upright(gain_two), 0.0)
    same[:, 2 * HD : 3 * HD] = small.astype(bf16)
    other[:, 2 * HD : 3 * HD] = small.astype(bf16)


def packed(flag, query, *arrays):
    rows, width = query.shape
    columns = 3 * HD + width // 2

    def whole(shape):
        return pl.BlockSpec(shape, lambda i, flag: (0,) * len(shape))

    outs = [(rows, columns), (rows, columns), (rows, width // 2), (rows, width // 2)]
    return pl.pallas_call(
        pack_kernel,
        out_shape=[jax.ShapeDtypeStruct(shape, bf16) for shape in outs],
        grid_spec=pltpu.PrefetchScalarGridSpec(
            num_scalar_prefetch=1,
            grid=(1,),
            in_specs=[whole(a.shape) for a in (query,) + arrays],
            out_specs=[whole(shape) for shape in outs],
        ),
        compiler_params=pltpu.CompilerParams(vmem_limit_bytes=ROOM),
        cost_estimate=COST,
    )(flag, query, *arrays)


def order_kernel(rows, order, out):
    out[...] = dot(rows[...], order[...]).astype(bf16)


def keys_kernel(both, cosines, sines, *refs):
    kvs, (normed, key_value, gains) = refs[:4], refs[4:]
    count = kvs[0].shape[0]
    for s in range(4):
        gains[:, column_block(s, count)] = dot_t(gain_picker(), kvs[s][:, WIDE:])
    normal, _ = normal_of(both[...].astype(f32))
    normed[...] = (normal * gains[0:1]).astype(bf16)
    kv = dot(normed[:, column_block(0, count)], kvs[0][:, :WIDE])
    for s in range(1, 4):
        kv = kv + dot(normed[:, column_block(s, count)], kvs[s][:, :WIDE])
    keys = turn(kv[:, :HD], cosines[...], sines[...]).astype(bf16)
    values = kv[:, HD:].astype(bf16)
    for i in range(key_value.shape[0]):
        key_value[i, :, :HD] = keys
        key_value[i, :, HD:] = values


def small_kernel(order, kvs0, kvs1, kvs2, kvs3, small, gains):
    count = kvs0.shape[0]
    total = jnp.zeros(small.shape, f32)
    for s, kvs in enumerate((kvs0, kvs1, kvs2, kvs3)):
        total = total + dot(order[:, column_block(s, count)], kvs[:, WIDE:])
    small[...] = total.astype(bf16)
    gains[...] = dot_t(gain_picker(), small[...])


def query_kernel(normed, cosines, sines, w_q0, w_q1, w_q2, w_q3, queries):
    w_q = (w_q0, w_q1, w_q2, w_q3)
    count = w_q0.shape[0]
    for h in range(queries.shape[1] // HD):
        at = column_block(h, HD)
        q = dot(normed[:, column_block(0, count)], w_q0[:, at])
        for s in range(1, 4):
            q = q + dot(normed[:, column_block(s, count)], w_q[s][:, at])
        queries[:, at] = turn(q, cosines[...], sines[...]).astype(bf16)


def attend_kernel(
    queries,
    q_place,
    low_place,
    up_place,
    order,
    order_back,
    kv,
    ordered,
    ordered_back,
    logs,
    kv_low,
    kv_up,
    mixed,
    *,
    scale,
    pieces,
    heads,
):
    half = kv.shape[1] // 2
    for i in range(pieces):
        kv_low[i * half : (i + 1) * half, :] = kv[i, :half]
        kv_up[i * half : (i + 1) * half, :] = kv[i, half:]
    allowed_low = low_place[...] <= q_place[...]
    allowed_up = up_place[...] <= q_place[half:, :]
    for h in range(heads):
        at = slice(h * HD, (h + 1) * HD)
        q = queries[:, at]
        low = jnp.where(allowed_low, dot_t(q, kv_low[:, :HD]) * scale, NEGATIVE)
        up = jnp.where(allowed_up, dot_t(q[half:], kv_up[:, :HD]) * scale, NEGATIVE)
        first, second = low[:half], low[half:]
        top = jnp.max(first, axis=-1, keepdims=True)
        weight = jnp.exp(first - top)
        total = jnp.sum(weight, axis=-1, keepdims=True)
        probs = (weight / total).astype(bf16)
        mixed[:half, at] = dot(probs, kv_low[:, HD:]).astype(bf16)
        logs[h, :half, :] = top + jnp.log(total)
        top = jnp.maximum(
            jnp.max(second, axis=-1, keepdims=True), jnp.max(up, axis=-1, keepdims=True)
        )
        weight, weight_up = jnp.exp(second - top), jnp.exp(up - top)
        total = jnp.sum(weight, axis=-1, keepdims=True) + jnp.sum(
            weight_up, axis=-1, keepdims=True
        )
        mixed[half:, at] = (
            dot((weight / total).astype(bf16), kv_low[:, HD:])
            + dot((weight_up / total).astype(bf16), kv_up[:, HD:])
        ).astype(bf16)
        logs[h, half:, :] = top + jnp.log(total)
    ordered[...] = dot(mixed[...], order[...]).astype(bf16)
    ordered_back[...] = dot(mixed[...], order_back[...]).astype(bf16)


def branch_kernel(mixed, w_out0, w_out1, w_out2, w_out3, own, other, w_out):
    quarter = mixed.shape[0] // 4
    count, columns = w_out0.shape[1:]
    for s, part in enumerate((w_out0, w_out1, w_out2, w_out3)):
        w_out[:, column_block(s, count)] = part[...]
    for k in range(2):
        part = dot(mixed[...], w_out[k])
        at = slice(k * columns, (k + 1) * columns)
        own[:quarter, at] = part[:quarter]
        other[:quarter, at] = part[quarter : 2 * quarter]
        own[quarter:, at] = part[2 * quarter : 3 * quarter]
        other[quarter:, at] = part[3 * quarter :]


def route_kernel(
    tokens,
    own,
    received,
    small,
    gains,
    hits,
    places_of,
    placer,
    sent,
    midway,
    moe_low,
    gates,
    parts,
):
    middle = tokens[...].astype(f32) + (own[...] + received[...])
    midway[...] = middle
    normal, _ = normal_of(middle)
    moe = (normal * gains[1:2]).astype(bf16)
    moe_low[...] = moe
    sent[:, : moe.shape[1]] = dot(placer[...], moe).astype(bf16)
    logits = dot(moe, small[...])
    picked = [
        jnp.sum(hits[k].astype(f32) * logits, axis=-1, keepdims=True) for k in range(TOPK)
    ]
    top = picked[0]
    for value in picked[1:]:
        top = jnp.maximum(top, value)
    weights = [jnp.exp(value - top) for value in picked]
    total = weights[0]
    for value in weights[1:]:
        total = total + value
    lane = lax.broadcasted_iota(jnp.int32, gates.shape, 1)
    gate_at = jnp.zeros(places_of.shape[1:], f32)
    kept = jnp.zeros(gates.shape, f32)
    for k in range(TOPK):
        gate = weights[k] / total
        kept = jnp.where(lane == k, gate, kept)
        gate_at = gate_at + places_of[k].astype(f32) * gate
    gates[...] = kept
    block = jnp.zeros((sent.shape[0], 128), f32)
    for i, part in enumerate(in_three(gate_at)):
        parts[i] = part
        block = block + t_dot(part, jnp.where(lane == i, 1.0, 0.0).astype(bf16))
    sent[:, moe.shape[1] :] = block.astype(bf16)


def expert_kernel(
    core, sent, cot, weights, out, rows_grad, hidden, out_grad, gate_grad, up_grad, held, sems
):
    copies = [
        pltpu.make_async_copy(weights.at[m, core[0]], held.at[m], sems.at[m]) for m in range(3)
    ]
    for copy in copies:
        copy.start()
    width = out.shape[1]
    gates = jnp.sum(sent[:, width:].astype(f32), axis=-1, keepdims=True)
    out_grad[...] = (gates * cot[...].astype(f32)).astype(bf16)
    rows = sent[:, :width]
    copies[0].wait()
    gate_pre = dot(rows, held[0])
    copies[1].wait()
    up_pre = dot(rows, held[1])
    sigmoid = 1.0 / (1.0 + jnp.exp(-gate_pre))
    silu = gate_pre * sigmoid
    low = (silu * up_pre).astype(bf16)
    hidden[...] = low
    copies[2].wait()
    hidden_grad = dot(out_grad[...], held[2])
    gate_low = (hidden_grad * up_pre * sigmoid * (1.0 + gate_pre * (1.0 - sigmoid))).astype(bf16)
    up_low = (hidden_grad * silu).astype(bf16)
    gate_grad[...] = gate_low
    up_grad[...] = up_low
    rows_grad[:, :width] = (dot_t(gate_low, held[0]) + dot_t(up_low, held[1])).astype(bf16)
    result = dot_t(low, held[2]).astype(bf16)
    out[...] = result
    grads = in_three(
        jnp.sum(cot[...].astype(f32) * result.astype(f32), axis=-1, keepdims=True)
    )
    lane = lax.broadcasted_iota(jnp.int32, (cot.shape[0], 128), 1)
    block = jnp.zeros(lane.shape, f32)
    for i, part in enumerate(grads):
        block = jnp.where(lane == i, part.astype(f32), block)
    rows_grad[:, width:] = block.astype(bf16)


def expert_call(core, arrays, weights, outs):
    rows = arrays[0].shape[0]

    def whole(columns):
        return pl.BlockSpec(
            (rows, columns), lambda i, core: (0, 0), pipeline_mode=pl.Buffered(1)
        )

    return pl.pallas_call(
        expert_kernel,
        out_shape=[jax.ShapeDtypeStruct((rows, columns), bf16) for columns in outs],
        grid_spec=pltpu.PrefetchScalarGridSpec(
            num_scalar_prefetch=1,
            grid=(1,),
            in_specs=[whole(a.shape[1]) for a in arrays] + [pl.BlockSpec(memory_space=pltpu.HBM)],
            out_specs=[whole(columns) for columns in outs],
            scratch_shapes=[
                pltpu.VMEM((3,) + weights.shape[2:], bf16),
                pltpu.SemaphoreType.DMA((3,)),
            ],
        ),
        compiler_params=pltpu.CompilerParams(vmem_limit_bytes=ROOM),
        cost_estimate=COST,
    )(core, *arrays, weights)


def weights_kernel(sent, out_grad, hidden, gate_grad, up_grad, sums):
    rows = sent[...]
    sums[0] = t_dot(rows, gate_grad[...]).astype(bf16)
    sums[1] = t_dot(rows, up_grad[...]).astype(bf16)
    sums[2] = t_dot(out_grad[...], hidden[...]).astype(bf16)


def expert_weights_grad(sent, out_grad, hidden, gate_grad, up_grad, block=256):
    count, width = out_grad.shape
    columns = hidden.shape[1]
    part = pl.BlockSpec((count, block), lambda i: (0, i))
    whole = pl.BlockSpec((count, columns), lambda i: (0, 0), pipeline_mode=pl.Buffered(1))
    return pl.pallas_call(
        weights_kernel,
        out_shape=jax.ShapeDtypeStruct((3, width, columns), bf16),
        grid=(width // block,),
        in_specs=[part, part, whole, whole, whole],
        out_specs=pl.BlockSpec((3, block, columns), lambda i: (0, i, 0)),
        compiler_params=pltpu.CompilerParams(vmem_limit_bytes=ROOM),
        cost_estimate=COST,
    )(sent, out_grad, hidden, gate_grad, up_grad)


def combine_kernel(midway, parts, returned, output):
    rows = returned[...]
    output[...] = (
        midway[...] + (dot(parts[0], rows) + (dot(parts[1], rows) + dot(parts[2], rows)))
    ).astype(bf16)


def home_kernel(
    placer_t,
    home,
    midway,
    cot,
    gains,
    hits,
    places_of,
    gates,
    small,
    moe_low,
    midway_grad,
    branch_low,
    gain_grad,
    router_grad,
):
    width = midway.shape[1]
    lane = lax.broadcasted_iota(jnp.int32, gates.shape, 1)
    gate, gate_grad = [], []
    mean = jnp.zeros((gates.shape[0], 1), f32)
    for k in range(TOPK):
        gate.append(jnp.sum(jnp.where(lane == k, gates[...], 0.0), axis=-1, keepdims=True))
        gate_grad.append(
            jnp.sum(dot(places_of[k], home[:, width:]), axis=-1, keepdims=True)
        )
        mean = mean + gate[k] * gate_grad[k]
    logit_grad = jnp.zeros(gates.shape, f32)
    for k in range(TOPK):
        logit_grad = logit_grad + hits[k].astype(f32) * (gate[k] * (gate_grad[k] - mean))
    logit_grad = logit_grad.astype(bf16)
    router_grad[...] = t_dot(moe_low[...], logit_grad)
    grad = dot(placer_t[...], home[:, :width]) + dot_t(logit_grad, small[...])
    normal, inverse = normal_of(midway[...])
    result = cot[...].astype(f32) + norm_back(grad, normal, inverse, gains[1:2])
    midway_grad[...] = result
    branch_low[...] = result.astype(bf16)
    gain_grad[...] = jnp.broadcast_to(
        jnp.sum(grad * normal, axis=0, keepdims=True), gain_grad.shape
    )


def out_grad_kernel(mixed, own, other, branch, *blocks):
    quarter = own.shape[0] // 2
    branch[:quarter] = own[:quarter]
    branch[quarter : 2 * quarter] = other[:quarter]
    branch[2 * quarter : 3 * quarter] = own[quarter:]
    branch[3 * quarter :] = other[quarter:]
    count, columns = blocks[0].shape[1:]
    for k in range(2):
        grad = t_dot(mixed[...], branch[:, column_block(k, columns)]).astype(bf16)
        for s in range(4):
            blocks[s][k] = grad[column_block(s, count)]


def attend_back_kernel(
    branch,
    w_out,
    order,
    queries,
    kv_low,
    kv_up,
    logs,
    q_place,
    low_place,
    up_place,
    cosines,
    sines,
    normed,
    dq,
    dkv,
    block0,
    block1,
    block2,
    block3,
    grads,
    acc_low,
    acc_up,
    *,
    scale,
    pieces,
    heads,
):
    half = queries.shape[0] // 2
    columns = w_out.shape[2]
    ordered = dot_t(branch[:, :columns], w_out[0]) + dot_t(branch[:, columns:], w_out[1])
    grads[...] = dot_t(ordered.astype(bf16), order[...]).astype(bf16)
    allowed_low = low_place[...] <= q_place[...]
    allowed_up = up_place[...] <= q_place[half:, :]
    key_low, value_low = kv_low[:, :HD], kv_low[:, HD:]
    key_up, value_up = kv_up[:, :HD], kv_up[:, HD:]
    for h in range(heads):
        at = slice(h * HD, (h + 1) * HD)
        q, grad, log = queries[:, at], grads[:, at], logs[h]
        low = jnp.where(allowed_low, dot_t(q, key_low) * scale, NEGATIVE)
        up = jnp.where(allowed_up, dot_t(q[half:], key_up) * scale, NEGATIVE)
        probs_low, probs_up = jnp.exp(low - log), jnp.exp(up - log[half:])
        grad_low, grad_up = dot_t(grad, value_low), dot_t(grad[half:], value_up)
        along = jnp.sum(probs_low * grad_low, axis=-1, keepdims=True)
        along_up = along[half:] + jnp.sum(probs_up * grad_up, axis=-1, keepdims=True)
        along = jnp.concatenate([along[:half], along_up])
        score_low = (probs_low * (grad_low - along)).astype(bf16)
        score_up = (probs_up * (grad_up - along_up)).astype(bf16)
        part = dot(score_low, key_low)
        part = jnp.concatenate([part[:half], part[half:] + dot(score_up, key_up)]) * scale
        dq[:, at] = turn(part, cosines[...], -sines[...]).astype(bf16)
        terms = (
            (acc_low, slice(0, HD), t_dot(q, score_low)),
            (acc_up, slice(0, HD), t_dot(q[half:], score_up)),
            (acc_low, slice(HD, 2 * HD), t_dot(grad, probs_low.astype(bf16))),
            (acc_up, slice(HD, 2 * HD), t_dot(grad[half:], probs_up.astype(bf16))),
        )
        for acc, rows, term in terms:
            if h == 0:
                acc[rows] = term
            else:
                acc[rows] += term
    for s, block in enumerate((block0, block1, block2, block3)):
        block[...] = t_dot(normed[:, column_block(s, block.shape[0])], dq[...]).astype(bf16)
    for acc, first in ((acc_low, 0), (acc_up, half)):
        dk = (acc[:HD].T * scale).astype(bf16)
        dv = acc[HD:].T.astype(bf16)
        for i in range(pieces):
            dkv[i, first : first + half, :HD] = dk[i * half : (i + 1) * half]
            dkv[i, first : first + half, HD:] = dv[i * half : (i + 1) * half]


def sum_kernel(dq, cosines, sines, *refs):
    w_q, kvs, (parts, dkv, own, other) = refs[:4], refs[4:8], refs[8:]
    total = jnp.sum(parts[...].astype(f32), axis=0)
    dkv[:, :HD] = turn(total[:, :HD], cosines[...], -sines[...]).astype(bf16)
    dkv[:, HD:] = total[:, HD:].astype(bf16)
    quarter = own.shape[0] // 2
    for s in range(4):
        grad = dot_t(dq[...], w_q[s][...]) + dot_t(dkv[...], kvs[s][:, :WIDE])
        at = column_block(s, w_q[s].shape[0])
        own[:quarter, at] = grad[:quarter]
        other[:quarter, at] = grad[quarter : 2 * quarter]
        own[quarter:, at] = grad[2 * quarter : 3 * quarter]
        other[quarter:, at] = grad[3 * quarter :]


def stack_kernel(gate, up, down, late, out):
    del late
    out[0] = gate[...]
    out[1] = up[...]
    out[2] = down[...]


def small_grad_kernel(order, router_grad, gain_grad, late, out):
    del late
    row = lax.broadcasted_iota(jnp.int32, gain_grad.shape, 0)
    second = jnp.where(row == 1, gain_grad[...], 0.0).astype(bf16)
    small = router_grad[...] + t_dot(second, gain_picker())
    out[...] = t_dot(order[...], small.astype(bf16))


def input_kernel(both, own, received, midway_grad, gains, order, small, normed, dkv, out, *blocks):
    grad = own[...] + received[...]
    quarter = own.shape[0] // 2
    tokens = jnp.concatenate([both[:quarter], both[2 * quarter : 3 * quarter]])
    normal, inverse = normal_of(tokens.astype(f32))
    parts = in_three(norm_back(grad, normal, inverse, gains[0:1]))
    moved = dot_t(jnp.concatenate(parts), order[...])
    count = 2 * quarter
    out[...] = midway_grad[...] + (
        moved[:count] + (moved[count : 2 * count] + moved[2 * count :])
    )
    gain_grad = jnp.sum(grad * normal, axis=0, keepdims=True)
    row = lax.broadcasted_iota(jnp.int32, gains.shape, 0)
    gain_grad = jnp.where(row == 0, gain_grad, 0.0).astype(bf16)
    small = small[...] + t_dot(gain_grad, gain_picker())
    rows = blocks[0].shape[0]
    for s, block in enumerate(blocks):
        at = column_block(s, rows)
        block[:, :WIDE] = t_dot(normed[:, at], dkv[...]).astype(bf16)
        block[:, WIDE:] = small[at].astype(bf16)


def body(
    tokens,
    cotangent,
    pair_of,
    routes,
    attn_gain,
    moe_gain,
    w_query,
    w_key,
    w_value,
    w_out,
    w_router,
    w_gate,
    w_up,
    w_down,
):
    rows = tokens.shape[1]
    half = rows // 2
    width = tokens.shape[2]
    shard = w_query.shape[1]
    ctx_count = 16
    experts = w_router.shape[2]
    columns = w_gate.shape[3]
    per_group = H // KVH
    qw = per_group * HD
    scale = 1.0 / math.sqrt(HD)
    core = lax.axis_index("core")
    ylo, z, yhi = lax.axis_index("ylo"), lax.axis_index("z"), lax.axis_index("yhi")
    x = lax.axis_index("x")
    piece_rows = 2 * shard
    slots = experts * SLOTS
    own_tokens, cot = tokens[0], cotangent[0]

    same, other, out_same, out_other = packed(
        yhi.reshape(1), w_query[0], w_key[0], w_value[0], w_router[0], attn_gain, moe_gain, w_out[0]
    )
    pieces = gather_pieces(same, other, core, ("core", "yhi"), SAME, OTHER)
    out_pieces = gather_pieces(
        out_same, out_other, yhi, ("ylo", "core", "yhi"), OUT_SAME, OUT_OTHER
    )
    other_tokens = partner(own_tokens)
    pieces, out_pieces, x, z, own_tokens, other_tokens, pair_of = together(
        pieces, out_pieces, x, z, own_tokens, other_tokens, pair_of
    )

    plane_rows = 16 * piece_rows
    plane = spread(pieces, 16, PLANE)
    both = jnp.concatenate(
        [own_tokens[:half], other_tokens[:half], own_tokens[half:], other_tokens[half:]]
    )
    order, out_order, level_order = order_matrix(16, x), order_matrix(8, x), level_order_matrix(z)
    (expert_shards_in,) = call(
        stack_kernel, [((3,) + w_gate.shape[1:], bf16)], w_gate[0], w_up[0], w_down[0], both
    )
    (
        plane, both, out_pieces, order, out_order, level_order, pair_of, expert_shards_in, chosen,
    ) = together(
        plane, both, out_pieces, order, out_order, level_order, pair_of, expert_shards_in,
        routes[0, 0],
    )

    plane = plane.reshape(plane_rows, -1)
    w_kvs = along("x", plane[:, : 3 * HD])
    wo = spread(out_pieces, 16, LEVEL)
    (both,) = call(order_kernel, [((2 * rows, width), bf16)], both, order)

    def two_cores(ctx):
        return jnp.stack([ctx + core, ctx + 1 - core], axis=-1).reshape(-1)

    ctx_here = (ylo * 4 + z) * 2
    q_place = places(pair_of, two_cores(ctx_here), rows, ctx_count)
    q_place = q_place.transpose(1, 0, 2).reshape(2 * rows, 1)
    key_place = places(
        pair_of, two_cores(jnp.arange(8, dtype=jnp.int32) * 2), rows, ctx_count
    )
    low_place, up_place = key_place[:, 0].reshape(1, -1), key_place[:, 1].reshape(1, -1)
    frequency = jnp.exp(jnp.arange(HD // 2, dtype=f32) * (-2.0 * math.log(ROPE_BASE) / HD))
    angles = q_place.astype(f32) * frequency[None, :]
    cosines, sines = jnp.cos(angles), jnp.sin(angles)
    cosines = jnp.concatenate([cosines, cosines], axis=-1)
    sines = jnp.concatenate([-sines, sines], axis=-1)
    w_q, w_kvs, wo, both, q_place, low_place, up_place, cosines, sines, chosen = together(
        plane[:, 3 * HD :], w_kvs, wo, both, q_place, low_place, up_place, cosines, sines, chosen
    )

    w_q = along("x", w_q)
    wo = along("z", wo.reshape(2, qw // 4, width // 2))
    normed, key_value, gains = call(
        keys_kernel,
        [((2 * rows, width), bf16), ((8, 2 * rows, 2 * HD), bf16), ((8, width), f32)],
        both,
        cosines,
        sines,
        *w_kvs,
    )
    all_kv = exchange(key_value, RING)
    small, moe_gains = call(
        small_kernel, [((width, 128), bf16), ((8, width), f32)], order, *w_kvs
    )
    (queries,) = call(
        query_kernel, [((2 * rows, qw), bf16)], normed, cosines, sines, *w_q, cost=LONG
    )
    lanes = jnp.arange(128, dtype=jnp.int32)
    hits = (chosen.T[:, :, None] == lanes[None, None, :]).astype(bf16)
    earlier = (lanes[:, None] > lanes[None, :]).astype(bf16)
    before = dot(earlier, jnp.sum(hits, axis=0))
    slot_index = jnp.sum(hits.astype(f32) * before[None], axis=-1).astype(jnp.int32)
    target = chosen.T * SLOTS + slot_index
    slot_row = jnp.arange(slots, dtype=jnp.int32)
    places_of = (target[:, :, None] == slot_row[None, None, :]).astype(bf16)
    placer_t = jnp.sum(places_of, axis=0)
    placer = placer_t.T
    (cot_rows,) = call(order_kernel, [((slots, width), bf16)], placer, cot)
    (
        queries, all_kv, expert_shards_in, small, moe_gains, cot_rows,
        hits, places_of, placer_t, placer, wo,
    ) = together(
        queries, all_kv, expert_shards_in, small, moe_gains, cot_rows,
        hits, places_of, placer_t, placer, wo,
    )
    expert_weights = lax.all_gather(expert_shards_in, CTX, axis=2, tiled=True)

    arrived_cot = to_owners(cot_rows.reshape(experts, SLOTS, width))
    sizes = dict(scale=scale, pieces=8, heads=per_group)
    keys = 8 * rows
    mixed, mixed_back, logs, kv_low, kv_up = call(
        functools.partial(attend_kernel, **sizes),
        [
            ((2 * rows, qw), bf16),
            ((2 * rows, qw), bf16),
            ((per_group, 2 * rows, 1), f32),
            ((keys, 2 * HD), bf16),
            ((keys, 2 * HD), bf16),
        ],
        queries,
        q_place,
        low_place,
        up_place,
        level_order,
        out_order,
        all_kv,
        scratch=[pltpu.VMEM((2 * rows, qw), bf16)],
    )

    branch_own, branch_other, wo = call(
        branch_kernel,
        [((rows, width), f32), ((rows, width), f32), ((2, qw, width // 2), bf16)],
        mixed,
        *wo,
    )
    sent, midway, moe_low, gates, gate_parts = call(
        route_kernel,
        [
            ((slots, width + 128), bf16),
            ((rows, width), f32),
            ((rows, width), bf16),
            ((rows, 128), f32),
            ((3, rows, slots), bf16),
        ],
        own_tokens,
        branch_own,
        partner(branch_other),
        small,
        moe_gains,
        hits,
        places_of,
        placer,
    )
    sent, arrived_cot = together(sent, arrived_cot)

    sent = to_owners(sent.reshape(experts, SLOTS, width + 128)).reshape(slots, width + 128)
    mine = core.reshape(1)
    expert_out, rows_grad, hidden, out_grad, gate_grad, up_grad = expert_call(
        mine,
        [sent, arrived_cot.reshape(slots, width)],
        expert_weights,
        [width, width + 128, columns, width, columns, columns],
    )
    rows_grad, gate_grad, up_grad = together(rows_grad, gate_grad, up_grad)

    home_grad = to_owners(rows_grad.reshape(experts, SLOTS, width + 128))
    expert_sums = expert_weights_grad(sent, out_grad, hidden, gate_grad, up_grad)
    home_grad, expert_sums, expert_out = together(home_grad, expert_sums, expert_out)
    expert_sums = lax.psum_scatter(expert_sums, RING, scatter_dimension=1, tiled=True)

    returned = to_owners(expert_out.reshape(experts, SLOTS, width))
    midway_grad, branch_low, gain_two_grad, router_grad = call(
        home_kernel,
        [((rows, width), f32), ((rows, width), bf16), ((8, width), f32), ((width, 128), f32)],
        placer_t,
        home_grad.reshape(slots, width + 128),
        midway,
        cot,
        moe_gains,
        hits,
        places_of,
        gates,
        small,
        moe_low,
    )
    branch, *out_w_grad = call(
        out_grad_kernel,
        [((2 * rows, width), bf16)] + [((2, qw // 4, width // 2), bf16)] * 4,
        mixed_back,
        branch_low,
        partner(branch_low),
    )
    branch, out_w_grad = together(branch, out_w_grad)
    out_w_grad = back_along_x(out_w_grad)

    dq, dkv, *q_w_grad = call(
        functools.partial(attend_back_kernel, **sizes),
        [((2 * rows, qw), bf16), ((8, 2 * rows, 2 * HD), bf16)]
        + [((plane_rows, qw), bf16)] * 4,
        branch,
        wo,
        level_order,
        queries,
        kv_low,
        kv_up,
        logs,
        q_place,
        low_place,
        up_place,
        cosines,
        sines,
        normed,
        scratch=[
            pltpu.VMEM((2 * rows, qw), bf16),
            pltpu.VMEM((2 * HD, keys), f32),
            pltpu.VMEM((2 * HD, keys), f32),
        ],
    )
    dkv, q_w_grad, returned, late = together(dkv, q_w_grad, returned, gain_two_grad)

    dkv = exchange(dkv, RING)
    q_w_grad = back_along_x(q_w_grad)
    (small_grad,) = call(
        small_grad_kernel, [((width, 128), f32)], order, router_grad, gain_two_grad, late
    )
    out_w_grad = added(out_w_grad, small_grad)
    dkv, out_w_grad, small_grad, q_w_grad[1], q_w_grad[3] = together(
        dkv, out_w_grad, small_grad, q_w_grad[1], q_w_grad[3]
    )

    dkv, normed_own, normed_other = call(
        sum_kernel,
        [((2 * rows, 2 * HD), bf16), ((rows, width), f32), ((rows, width), f32)],
        dq,
        cosines,
        sines,
        *w_q,
        *w_kvs,
        dkv,
    )
    input_grad, *kvs_grad = call(
        input_kernel,
        [((rows, width), f32)] + [((plane_rows, 3 * HD), bf16)] * 4,
        both,
        normed_own,
        partner(normed_other),
        midway_grad,
        gains,
        order,
        small_grad,
        normed,
        dkv,
    )
    kvs_grad, out_w_grad, input_grad = together(kvs_grad, out_w_grad, input_grad)

    out_w_grad = exchange(out_w_grad.reshape(16, piece_rows, width // 2), OUT_PLANE)
    kvs_grad = back_along_x(kvs_grad)
    (plane_grad,) = call(
        add_both_kernel, [((plane_rows, qw + 3 * HD), bf16)], *q_w_grad, *kvs_grad, cost=LONG
    )
    plane_grad, out_w_grad, returned = together(plane_grad, out_w_grad, returned)
    plane_grad = exchange(plane_grad.reshape(16, piece_rows, qw + 3 * HD), PLANE)

    (output,) = call(
        combine_kernel,
        [((rows, width), bf16)],
        midway,
        gate_parts,
        returned.reshape(slots, width),
    )

    def summed(pieces):
        return jnp.sum(pieces.astype(f32), axis=0)

    def expert_shards(grad):
        count = grad.shape[1] // 2
        kept = lax.dynamic_slice_in_dim(grad, core * count, count, axis=1)
        given = partner(lax.dynamic_slice_in_dim(grad, (1 - core) * count, count, axis=1))
        both = jnp.stack([pick(core, kept, given), pick(core, given, kept)], axis=1)
        return [both[i : i + 1].astype(f32) for i in range(3)]

    out_w_grad = scatter_pieces(
        summed(out_w_grad), yhi, yhi, ("ylo", "core", "yhi"), OUT_SAME, OUT_OTHER
    )
    w_gate_grad, w_up_grad, w_down_grad = expert_shards(expert_sums)
    plane_grad, w_gate_grad, w_up_grad, w_down_grad, output = together(
        plane_grad, w_gate_grad, w_up_grad, w_down_grad, output
    )
    plane_grad = scatter_pieces(summed(plane_grad), yhi, core, ("core", "yhi"), SAME, OTHER)
    plane_grad = plane_grad.reshape(shard, 2, -1)

    def joined(first, last):
        return plane_grad[:, :, first:last].reshape(1, shard, -1)

    small_grad = jnp.sum(plane_grad[None, :, :, qw + 2 * HD :], axis=2)

    return (
        output[None],
        input_grad[None],
        small_grad[:, :, experts],
        small_grad[:, :, experts + 1],
        joined(0, qw),
        joined(qw, qw + HD),
        joined(qw + HD, qw + 2 * HD),
        out_w_grad[None],
        small_grad[:, :, :experts],
        w_gate_grad,
        w_up_grad,
        w_down_grad,
    )


def solution(mesh):
    fine = Mesh(mesh.devices.reshape(2, 4, 2, 4, 2), AXES)
    seq = P(FSDP, CTX, None)
    vector = P(None, AXES)
    matrix = P(None, AXES, None)
    expert = P(None, FSDP, CTX, None)
    in_specs = (
        seq,
        seq,
        P(),
        P(None, FSDP, CTX, None),
        vector,
        vector,
        matrix,
        matrix,
        matrix,
        matrix,
        matrix,
        expert,
        expert,
        expert,
    )
    out_specs = (
        seq,
        seq,
        vector,
        vector,
        matrix,
        matrix,
        matrix,
        matrix,
        matrix,
        expert,
        expert,
        expert,
    )
    return jax.shard_map(body, mesh=fine, in_specs=in_specs, out_specs=out_specs, check_vma=False)
```

```python
import functools
import math

import jax
import jax.numpy as jnp
from jax import lax
from jax.experimental import pallas as pl
from jax.experimental.pallas import tpu as pltpu
from jax.sharding import Mesh
from jax.sharding import PartitionSpec as P

H = 12
KVH = 2
HD = 128
TOPK = 4

EPSILON = 1e-06
ROPE_BASE = 1000000.0
NEGATIVE = -1e30

AXES = ("ylo", "z", "core", "x", "yhi")
CTX = ("ylo", "z", "core")
FSDP = ("x", "yhi")
GROUPS = [
    [
        (((group ^ yhi) * 4 + z) * 2 + core) * 8 + x * 2 + yhi
        for x in range(4)
        for yhi in range(2)
        for core in range(2)
    ]
    for group in range(2)
    for z in range(4)
]
RING = ("ylo", "z")
PLANE = ("ylo", "z", "yhi")
OUT_PLANE = ("yhi", "z", "ylo")
LEVEL = ("yhi", "ylo", "x")
GROUPS = [
    [
        (((group ^ yhi) * 4 + z) * 2 + core) * 8 + x * 2 + yhi
        for x in range(4)
        for yhi in range(2)
        for core in range(2)
    ]
    for group in range(2)
    for z in range(4)
]
RING = ("ylo", "z")
ROWS_ORDER = ("ylo", "z", "yhi", "x")
OUT_ORDER = ("yhi", "z", "ylo", "x")
SLOTS = 40

bf16 = jnp.bfloat16
f32 = jnp.float32


def dot(left, right):
    return jnp.dot(left, right, preferred_element_type=f32)


def dot_t(left, right):
    return lax.dot_general(left, right, (((1,), (1,)), ((), ())), preferred_element_type=f32)


def t_dot(left, right):
    return lax.dot_general(left, right, (((0,), (0,)), ((), ())), preferred_element_type=f32)


def exchange(pieces, axes):
    return lax.all_to_all(pieces, axes, split_axis=0, concat_axis=0, tiled=True)


def to_owners(pieces):
    return lax.all_to_all(
        pieces, AXES, split_axis=0, concat_axis=0, axis_index_groups=GROUPS, tiled=True
    )


def spread(piece, count, axes):
    return exchange(jnp.broadcast_to(piece[None], (count,) + piece.shape), axes)


def after(value, earlier):
    return lax.optimization_barrier((value, earlier))[0]


def together(*values):
    return lax.optimization_barrier(values)


def partner(value):
    return lax.ppermute(value, "core", [(0, 1), (1, 0)])


def route(axes, sizes, move):
    pairs = []
    for source in range(math.prod(sizes)):
        rest, at = source, []
        for size in reversed(sizes):
            at.insert(0, rest % size)
            rest //= size
        target = 0
        for size, value in zip(sizes, move(*at)):
            target = target * size + value
        pairs.append((source, target))
    return pairs


SAME = route(("core", "yhi"), (2, 2), lambda c, h: (h, c))
OTHER = route(("core", "yhi"), (2, 2), lambda c, h: (1 - h, c))
OUT_SAME = route(("ylo", "core", "yhi"), (2, 2, 2), lambda j, c, h: (c, j, h))
OUT_OTHER = route(("ylo", "core", "yhi"), (2, 2, 2), lambda j, c, h: (c, j, 1 - h))


def back(pairs):
    return [(target, source) for source, target in pairs]


def pick(flag, if_zero, if_one):
    return jnp.where(flag == 0, if_zero, if_one)


def gather_pieces(first, second, key, axes, same, other):
    first = lax.ppermute(first, axes, same)
    second = lax.ppermute(second, axes, other)
    return pick(
        key, jnp.concatenate([first, second]), jnp.concatenate([second, first])
    )


def scatter_pieces(piece, flag, key, axes, same, other):
    count = piece.shape[0] // 2
    mine, rest = piece[:count], piece[count:]
    first = lax.ppermute(pick(key, mine, rest), axes, back(same))
    second = lax.ppermute(pick(key, rest, mine), axes, back(other))
    return pick(flag, jnp.concatenate([first, second], axis=-1), jnp.concatenate([second, first], axis=-1))


def along(axis, piece):
    return [piece] + [
        lax.ppermute(piece, axis, [(i, (i + s) % 4) for i in range(4)]) for s in (1, 2, 3)
    ]


def back_along_x(blocks):
    return [blocks[0]] + [
        lax.ppermute(blocks[s], "x", [(i, (i - s) % 4) for i in range(4)]) for s in (1, 2, 3)
    ]


def added(blocks, *late):
    (total,) = call(add_kernel, [(blocks[0].shape, bf16)], *blocks, *late, cost=LONG)
    return total


def sum_of(first, second, third, fourth):
    return (
        (first[...].astype(f32) + second[...].astype(f32))
        + (third[...].astype(f32) + fourth[...].astype(f32))
    ).astype(bf16)


def add_kernel(first, second, third, fourth, *refs):
    refs[-1][...] = sum_of(first, second, third, fourth)


def add_both_kernel(*refs):
    total = refs[8]
    count = refs[0].shape[1]
    total[:, :count] = sum_of(*refs[:4])
    total[:, count:] = sum_of(*refs[4:8])


def order_matrix(groups, x):
    index = jnp.arange(groups * 96, dtype=jnp.int32)
    turn_of, group, row = index // (groups * 24), index // 24 % groups, index % 24
    own = group * 96 + (x - turn_of) % 4 * 24 + row
    return (index[:, None] == own[None, :]).astype(bf16)


def level_order_matrix(z):
    index = jnp.arange(8 * 96, dtype=jnp.int32)
    own = (z - index // 192) % 4 * 192 + index % 192
    return (index[:, None] == own[None, :]).astype(bf16)


def places(pair_of, ctx, row_count, ctx_count):
    half_size = row_count // 2
    pair = jnp.sum(
        jnp.where(ctx[:, None] == jnp.arange(ctx_count, dtype=jnp.int32)[None], pair_of[None], 0),
        axis=1,
    )
    block = jnp.stack([pair, 2 * ctx_count - 1 - pair], axis=1)
    return block[:, :, None] * half_size + jnp.arange(half_size, dtype=jnp.int32)[None, None]


def in_three(value):
    high = value.astype(bf16)
    rest = value - high.astype(f32)
    middle = rest.astype(bf16)
    return [high, middle, (rest - middle.astype(f32)).astype(bf16)]


def call(kernel, outs, *args, scratch=(), cost=None):
    def whole(shape):
        return pl.BlockSpec(shape, lambda i: (0,) * len(shape))

    return pl.pallas_call(
        kernel,
        out_shape=[jax.ShapeDtypeStruct(shape, dtype) for shape, dtype in outs],
        grid=(1,),
        in_specs=[whole(a.shape) for a in args],
        out_specs=[whole(shape) for shape, _ in outs],
        scratch_shapes=list(scratch),
        compiler_params=pltpu.CompilerParams(vmem_limit_bytes=ROOM),
        cost_estimate=COST if cost is None else cost,
    )(*args)


ROOM = 58 << 20
COST = pl.CostEstimate(flops=1 << 20, bytes_accessed=1 << 18, transcendentals=0)
LONG = pl.CostEstimate(flops=1 << 35, bytes_accessed=1 << 27, transcendentals=0)
WIDE = 2 * HD
EXPERTS = 16


def turn(vectors, cosines, sines):
    return vectors * cosines + pltpu.roll(vectors, HD // 2, axis=1) * sines


def gain_picker():
    row = lax.broadcasted_iota(jnp.int32, (8, 128), 0)
    column = lax.broadcasted_iota(jnp.int32, (8, 128), 1)
    return jnp.where((column == row + EXPERTS) & (row < 2), 1.0, 0.0).astype(bf16)


def normal_of(stream):
    inverse = lax.rsqrt(jnp.mean(stream * stream, axis=-1, keepdims=True) + EPSILON)
    return stream * inverse, inverse


def norm_back(grad, normal, inverse, gain):
    scaled = grad * gain
    return inverse * (scaled - normal * jnp.mean(scaled * normal, axis=-1, keepdims=True))


def column_block(s, count):
    return slice(s * count, (s + 1) * count)


def pack_kernel(
    flag, query, key, value, router, gain_one, gain_two, w_out, same, other, out_same, out_other
):
    last = flag[0].astype(f32)
    rows = query.shape[0]

    def store(target, rest, at, matrix):
        count = matrix.shape[1] // 2
        left, right = matrix[:, :count].astype(f32), matrix[:, count:].astype(f32)
        target[:, at : at + count] = (left * (1.0 - last) + right * last).astype(bf16)
        rest[:, at : at + count] = (right * (1.0 - last) + left * last).astype(bf16)

    store(same, other, 0, key)
    store(same, other, HD, value)
    store(same, other, 3 * HD, query)
    store(out_same, out_other, 0, w_out)
    row = lax.broadcasted_iota(jnp.int32, (rows, rows), 0)
    column = lax.broadcasted_iota(jnp.int32, (rows, rows), 1)

    def upright(gain):
        return jnp.sum(
            jnp.where(row == column, gain[...].astype(f32), 0.0), axis=1, keepdims=True
        )

    shape = (router.shape[1], 128)
    spread_out = lax.broadcasted_iota(jnp.int32, shape, 0) == lax.broadcasted_iota(
        jnp.int32, shape, 1
    )
    small = dot(router[...], jnp.where(spread_out, 1.0, 0.0).astype(bf16))
    lane = lax.broadcasted_iota(jnp.int32, small.shape, 1)
    small = small + jnp.where(lane == EXPERTS, upright(gain_one), 0.0)
    small = small + jnp.where(lane == EXPERTS + 1, upright(gain_two), 0.0)
    same[:, 2 * HD : 3 * HD] = small.astype(bf16)
    other[:, 2 * HD : 3 * HD] = small.astype(bf16)


def packed(flag, query, *arrays):
    rows, width = query.shape
    columns = 3 * HD + width // 2

    def whole(shape):
        return pl.BlockSpec(shape, lambda i, flag: (0,) * len(shape))

    outs = [(rows, columns), (rows, columns), (rows, width // 2), (rows, width // 2)]
    return pl.pallas_call(
        pack_kernel,
        out_shape=[jax.ShapeDtypeStruct(shape, bf16) for shape in outs],
        grid_spec=pltpu.PrefetchScalarGridSpec(
            num_scalar_prefetch=1,
            grid=(1,),
            in_specs=[whole(a.shape) for a in (query,) + arrays],
            out_specs=[whole(shape) for shape in outs],
        ),
        compiler_params=pltpu.CompilerParams(vmem_limit_bytes=ROOM),
        cost_estimate=COST,
    )(flag, query, *arrays)


def order_kernel(rows, order, out):
    out[...] = dot(rows[...], order[...]).astype(bf16)


def keys_kernel(both, cosines, sines, *refs):
    kvs, (normed, key_value, gains) = refs[:4], refs[4:]
    count = kvs[0].shape[0]
    for s in range(4):
        gains[:, column_block(s, count)] = dot_t(gain_picker(), kvs[s][:, WIDE:])
    normal, _ = normal_of(both[...].astype(f32))
    normed[...] = (normal * gains[0:1]).astype(bf16)
    kv = dot(normed[:, column_block(0, count)], kvs[0][:, :WIDE])
    for s in range(1, 4):
        kv = kv + dot(normed[:, column_block(s, count)], kvs[s][:, :WIDE])
    keys = turn(kv[:, :HD], cosines[...], sines[...]).astype(bf16)
    values = kv[:, HD:].astype(bf16)
    for i in range(key_value.shape[0]):
        key_value[i, :, :HD] = keys
        key_value[i, :, HD:] = values


def small_kernel(order, kvs0, kvs1, kvs2, kvs3, small, gains):
    count = kvs0.shape[0]
    total = jnp.zeros(small.shape, f32)
    for s, kvs in enumerate((kvs0, kvs1, kvs2, kvs3)):
        total = total + dot(order[:, column_block(s, count)], kvs[:, WIDE:])
    small[...] = total.astype(bf16)
    gains[...] = dot_t(gain_picker(), small[...])


def query_kernel(normed, cosines, sines, w_q0, w_q1, w_q2, w_q3, queries):
    w_q = (w_q0, w_q1, w_q2, w_q3)
    count = w_q0.shape[0]
    for h in range(queries.shape[1] // HD):
        at = column_block(h, HD)
        q = dot(normed[:, column_block(0, count)], w_q0[:, at])
        for s in range(1, 4):
            q = q + dot(normed[:, column_block(s, count)], w_q[s][:, at])
        queries[:, at] = turn(q, cosines[...], sines[...]).astype(bf16)


def attend_kernel(
    queries,
    q_place,
    low_place,
    up_place,
    order,
    order_back,
    kv,
    ordered,
    ordered_back,
    logs,
    kv_low,
    kv_up,
    mixed,
    *,
    scale,
    pieces,
    heads,
):
    half = kv.shape[1] // 2
    for i in range(pieces):
        kv_low[i * half : (i + 1) * half, :] = kv[i, :half]
        kv_up[i * half : (i + 1) * half, :] = kv[i, half:]
    allowed_low = low_place[...] <= q_place[...]
    allowed_up = up_place[...] <= q_place[half:, :]
    for h in range(heads):
        at = slice(h * HD, (h + 1) * HD)
        q = queries[:, at]
        low = jnp.where(allowed_low, dot_t(q, kv_low[:, :HD]) * scale, NEGATIVE)
        up = jnp.where(allowed_up, dot_t(q[half:], kv_up[:, :HD]) * scale, NEGATIVE)
        first, second = low[:half], low[half:]
        top = jnp.max(first, axis=-1, keepdims=True)
        weight = jnp.exp(first - top)
        total = jnp.sum(weight, axis=-1, keepdims=True)
        probs = (weight / total).astype(bf16)
        mixed[:half, at] = dot(probs, kv_low[:, HD:]).astype(bf16)
        logs[h, :half, :] = top + jnp.log(total)
        top = jnp.maximum(
            jnp.max(second, axis=-1, keepdims=True), jnp.max(up, axis=-1, keepdims=True)
        )
        weight, weight_up = jnp.exp(second - top), jnp.exp(up - top)
        total = jnp.sum(weight, axis=-1, keepdims=True) + jnp.sum(
            weight_up, axis=-1, keepdims=True
        )
        mixed[half:, at] = (
            dot((weight / total).astype(bf16), kv_low[:, HD:])
            + dot((weight_up / total).astype(bf16), kv_up[:, HD:])
        ).astype(bf16)
        logs[h, half:, :] = top + jnp.log(total)
    ordered[...] = dot(mixed[...], order[...]).astype(bf16)
    ordered_back[...] = dot(mixed[...], order_back[...]).astype(bf16)


def branch_kernel(mixed, w_out0, w_out1, w_out2, w_out3, own, other, w_out):
    quarter = mixed.shape[0] // 4
    count, columns = w_out0.shape[1:]
    for s, part in enumerate((w_out0, w_out1, w_out2, w_out3)):
        w_out[:, column_block(s, count)] = part[...]
    for k in range(2):
        part = dot(mixed[...], w_out[k])
        at = slice(k * columns, (k + 1) * columns)
        own[:quarter, at] = part[:quarter]
        other[:quarter, at] = part[quarter : 2 * quarter]
        own[quarter:, at] = part[2 * quarter : 3 * quarter]
        other[quarter:, at] = part[3 * quarter :]


def route_kernel(
    tokens,
    own,
    received,
    small,
    gains,
    hits,
    places_of,
    placer,
    sent,
    midway,
    moe_low,
    gates,
    parts,
):
    middle = tokens[...].astype(f32) + (own[...] + received[...])
    midway[...] = middle
    normal, _ = normal_of(middle)
    moe = (normal * gains[1:2]).astype(bf16)
    moe_low[...] = moe
    sent[:, : moe.shape[1]] = dot(placer[...], moe).astype(bf16)
    logits = dot(moe, small[...])
    picked = [
        jnp.sum(hits[k].astype(f32) * logits, axis=-1, keepdims=True) for k in range(TOPK)
    ]
    top = picked[0]
    for value in picked[1:]:
        top = jnp.maximum(top, value)
    weights = [jnp.exp(value - top) for value in picked]
    total = weights[0]
    for value in weights[1:]:
        total = total + value
    lane = lax.broadcasted_iota(jnp.int32, gates.shape, 1)
    gate_at = jnp.zeros(places_of.shape[1:], f32)
    kept = jnp.zeros(gates.shape, f32)
    for k in range(TOPK):
        gate = weights[k] / total
        kept = jnp.where(lane == k, gate, kept)
        gate_at = gate_at + places_of[k].astype(f32) * gate
    gates[...] = kept
    block = jnp.zeros((sent.shape[0], 128), f32)
    for i, part in enumerate(in_three(gate_at)):
        parts[i] = part
        block = block + t_dot(part, jnp.where(lane == i, 1.0, 0.0).astype(bf16))
    sent[:, moe.shape[1] :] = block.astype(bf16)


def expert_kernel(
    core, sent, cot, weights, out, rows_grad, hidden, gate_grad, up_grad, held, sems
):
    copies = [
        pltpu.make_async_copy(weights.at[m, core[0]], held.at[m], sems.at[m]) for m in range(3)
    ]
    for copy in copies:
        copy.start()
    width = out.shape[1]
    gates = jnp.sum(sent[:, width:].astype(f32), axis=-1, keepdims=True)
    out_grad = (gates * cot[...].astype(f32)).astype(bf16)
    rows = sent[:, :width]
    copies[0].wait()
    gate_pre = dot(rows, held[0])
    copies[1].wait()
    up_pre = dot(rows, held[1])
    sigmoid = 1.0 / (1.0 + jnp.exp(-gate_pre))
    silu = gate_pre * sigmoid
    low = (silu * up_pre).astype(bf16)
    hidden[...] = low
    copies[2].wait()
    hidden_grad = dot(out_grad, held[2])
    gate_low = (hidden_grad * up_pre * sigmoid * (1.0 + gate_pre * (1.0 - sigmoid))).astype(bf16)
    up_low = (hidden_grad * silu).astype(bf16)
    gate_grad[...] = gate_low
    up_grad[...] = up_low
    rows_grad[:, :width] = (dot_t(gate_low, held[0]) + dot_t(up_low, held[1])).astype(bf16)
    result = dot_t(low, held[2]).astype(bf16)
    out[...] = result
    grads = in_three(
        jnp.sum(cot[...].astype(f32) * result.astype(f32), axis=-1, keepdims=True)
    )
    lane = lax.broadcasted_iota(jnp.int32, (cot.shape[0], 128), 1)
    block = jnp.zeros(lane.shape, f32)
    for i, part in enumerate(grads):
        block = jnp.where(lane == i, part.astype(f32), block)
    rows_grad[:, width:] = block.astype(bf16)


def expert_call(core, arrays, weights, outs):
    rows = arrays[0].shape[0]

    def whole(columns):
        return pl.BlockSpec(
            (rows, columns), lambda i, core: (0, 0), pipeline_mode=pl.Buffered(1)
        )

    return pl.pallas_call(
        expert_kernel,
        out_shape=[jax.ShapeDtypeStruct((rows, columns), bf16) for columns in outs],
        grid_spec=pltpu.PrefetchScalarGridSpec(
            num_scalar_prefetch=1,
            grid=(1,),
            in_specs=[whole(a.shape[1]) for a in arrays] + [pl.BlockSpec(memory_space=pltpu.HBM)],
            out_specs=[whole(columns) for columns in outs],
            scratch_shapes=[
                pltpu.VMEM((3,) + weights.shape[2:], bf16),
                pltpu.SemaphoreType.DMA((3,)),
            ],
        ),
        compiler_params=pltpu.CompilerParams(vmem_limit_bytes=ROOM),
        cost_estimate=COST,
    )(core, *arrays, weights)


def weights_kernel(sent, gates, cot, hidden, gate_grad, up_grad, sums):
    rows = sent[...]
    gate = jnp.sum(gates[...].astype(f32), axis=-1, keepdims=True)
    out_grad = (gate * cot[...].astype(f32)).astype(bf16)
    sums[0] = t_dot(rows, gate_grad[...]).astype(bf16)
    sums[1] = t_dot(rows, up_grad[...]).astype(bf16)
    sums[2] = t_dot(out_grad, hidden[...]).astype(bf16)


def expert_weights_grad(sent, cot, hidden, gate_grad, up_grad, block=256):
    count, width = cot.shape
    columns = hidden.shape[1]
    part = pl.BlockSpec((count, block), lambda i: (0, i))
    gates = pl.BlockSpec((count, 128), lambda i: (0, width // 128))
    whole = pl.BlockSpec((count, columns), lambda i: (0, 0), pipeline_mode=pl.Buffered(1))
    return pl.pallas_call(
        weights_kernel,
        out_shape=jax.ShapeDtypeStruct((3, width, columns), bf16),
        grid=(width // block,),
        in_specs=[part, gates, part, whole, whole, whole],
        out_specs=pl.BlockSpec((3, block, columns), lambda i: (0, i, 0)),
        compiler_params=pltpu.CompilerParams(vmem_limit_bytes=ROOM),
        cost_estimate=COST,
    )(sent, sent, cot, hidden, gate_grad, up_grad)


def combine_kernel(midway, parts, returned, output):
    rows = returned[...]
    output[...] = (
        midway[...] + (dot(parts[0], rows) + (dot(parts[1], rows) + dot(parts[2], rows)))
    ).astype(bf16)


def home_kernel(
    placer_t,
    home,
    midway,
    cot,
    gains,
    hits,
    places_of,
    gates,
    small,
    moe_low,
    midway_grad,
    branch_low,
    gain_grad,
    router_grad,
):
    width = midway.shape[1]
    lane = lax.broadcasted_iota(jnp.int32, gates.shape, 1)
    gate, gate_grad = [], []
    count = gates.shape[0]
    mean = jnp.zeros((count, 1), f32)
    picked = dot(places_of[...].reshape(TOPK * count, -1), home[:, width:])
    for k in range(TOPK):
        gate.append(jnp.sum(jnp.where(lane == k, gates[...], 0.0), axis=-1, keepdims=True))
        gate_grad.append(
            jnp.sum(picked[k * count : (k + 1) * count], axis=-1, keepdims=True)
        )
        mean = mean + gate[k] * gate_grad[k]
    logit_grad = jnp.zeros(gates.shape, f32)
    for k in range(TOPK):
        logit_grad = logit_grad + hits[k].astype(f32) * (gate[k] * (gate_grad[k] - mean))
    logit_grad = logit_grad.astype(bf16)
    router_grad[...] = t_dot(moe_low[...], logit_grad)
    grad = dot(placer_t[...], home[:, :width]) + dot_t(logit_grad, small[...])
    normal, inverse = normal_of(midway[...])
    result = cot[...].astype(f32) + norm_back(grad, normal, inverse, gains[1:2])
    midway_grad[...] = result
    branch_low[...] = result.astype(bf16)
    gain_grad[...] = jnp.broadcast_to(
        jnp.sum(grad * normal, axis=0, keepdims=True), gain_grad.shape
    )


def out_grad_kernel(mixed, own, other, branch, *blocks):
    quarter = own.shape[0] // 2
    branch[:quarter] = own[:quarter]
    branch[quarter : 2 * quarter] = other[:quarter]
    branch[2 * quarter : 3 * quarter] = own[quarter:]
    branch[3 * quarter :] = other[quarter:]
    count, columns = blocks[0].shape[1:]
    for k in range(2):
        grad = t_dot(mixed[...], branch[:, column_block(k, columns)]).astype(bf16)
        for s in range(4):
            blocks[s][k] = grad[column_block(s, count)]


def attend_back_kernel(
    branch,
    w_out,
    order,
    queries,
    kv_low,
    kv_up,
    logs,
    q_place,
    low_place,
    up_place,
    cosines,
    sines,
    normed,
    dq,
    dkv,
    block0,
    block1,
    block2,
    block3,
    grads,
    acc_low,
    acc_up,
    *,
    scale,
    pieces,
    heads,
):
    half = queries.shape[0] // 2
    columns = w_out.shape[2]
    ordered = dot_t(branch[:, :columns], w_out[0]) + dot_t(branch[:, columns:], w_out[1])
    grads[...] = dot_t(ordered.astype(bf16), order[...]).astype(bf16)
    allowed_low = low_place[...] <= q_place[...]
    allowed_up = up_place[...] <= q_place[half:, :]
    key_low, value_low = kv_low[:, :HD], kv_low[:, HD:]
    key_up, value_up = kv_up[:, :HD], kv_up[:, HD:]
    for h in range(heads):
        at = slice(h * HD, (h + 1) * HD)
        q, grad, log = queries[:, at], grads[:, at], logs[h]
        low = jnp.where(allowed_low, dot_t(q, key_low) * scale, NEGATIVE)
        up = jnp.where(allowed_up, dot_t(q[half:], key_up) * scale, NEGATIVE)
        probs_low, probs_up = jnp.exp(low - log), jnp.exp(up - log[half:])
        grad_low, grad_up = dot_t(grad, value_low), dot_t(grad[half:], value_up)
        along = jnp.sum(probs_low * grad_low, axis=-1, keepdims=True)
        along_up = along[half:] + jnp.sum(probs_up * grad_up, axis=-1, keepdims=True)
        along = jnp.concatenate([along[:half], along_up])
        score_low = (probs_low * (grad_low - along)).astype(bf16)
        score_up = (probs_up * (grad_up - along_up)).astype(bf16)
        part = dot(score_low, key_low)
        part = jnp.concatenate([part[:half], part[half:] + dot(score_up, key_up)]) * scale
        dq[:, at] = turn(part, cosines[...], -sines[...]).astype(bf16)
        terms = (
            (acc_low, slice(0, HD), t_dot(q, score_low)),
            (acc_up, slice(0, HD), t_dot(q[half:], score_up)),
            (acc_low, slice(HD, 2 * HD), t_dot(grad, probs_low.astype(bf16))),
            (acc_up, slice(HD, 2 * HD), t_dot(grad[half:], probs_up.astype(bf16))),
        )
        for acc, rows, term in terms:
            if h == 0:
                acc[rows] = term
            else:
                acc[rows] += term
    for s, block in enumerate((block0, block1, block2, block3)):
        block[...] = t_dot(normed[:, column_block(s, block.shape[0])], dq[...]).astype(bf16)
    for acc, first in ((acc_low, 0), (acc_up, half)):
        dk = (acc[:HD].T * scale).astype(bf16)
        dv = acc[HD:].T.astype(bf16)
        for i in range(pieces):
            dkv[i, first : first + half, :HD] = dk[i * half : (i + 1) * half]
            dkv[i, first : first + half, HD:] = dv[i * half : (i + 1) * half]


def sum_kernel(dq, cosines, sines, *refs):
    w_q, kvs, (parts, dkv, own, other) = refs[:4], refs[4:8], refs[8:]
    total = jnp.sum(parts[...].astype(f32), axis=0)
    dkv[:, :HD] = turn(total[:, :HD], cosines[...], -sines[...]).astype(bf16)
    dkv[:, HD:] = total[:, HD:].astype(bf16)
    quarter = own.shape[0] // 2
    for s in range(4):
        grad = dot_t(dq[...], w_q[s][...]) + dot_t(dkv[...], kvs[s][:, :WIDE])
        at = column_block(s, w_q[s].shape[0])
        own[:quarter, at] = grad[:quarter]
        other[:quarter, at] = grad[quarter : 2 * quarter]
        own[quarter:, at] = grad[2 * quarter : 3 * quarter]
        other[quarter:, at] = grad[3 * quarter :]


def stack_kernel(gate, up, down, late, out):
    del late
    out[0] = gate[...]
    out[1] = up[...]
    out[2] = down[...]


def small_grad_kernel(order, router_grad, gain_grad, late, out):
    del late
    row = lax.broadcasted_iota(jnp.int32, gain_grad.shape, 0)
    second = jnp.where(row == 1, gain_grad[...], 0.0).astype(bf16)
    small = router_grad[...] + t_dot(second, gain_picker())
    out[...] = t_dot(order[...], small.astype(bf16))


def input_kernel(both, own, received, midway_grad, gains, order, small, normed, dkv, out, *blocks):
    grad = own[...] + received[...]
    quarter = own.shape[0] // 2
    tokens = jnp.concatenate([both[:quarter], both[2 * quarter : 3 * quarter]])
    normal, inverse = normal_of(tokens.astype(f32))
    parts = in_three(norm_back(grad, normal, inverse, gains[0:1]))
    moved = dot_t(jnp.concatenate(parts), order[...])
    count = 2 * quarter
    out[...] = midway_grad[...] + (
        moved[:count] + (moved[count : 2 * count] + moved[2 * count :])
    )
    gain_grad = jnp.sum(grad * normal, axis=0, keepdims=True)
    row = lax.broadcasted_iota(jnp.int32, gains.shape, 0)
    gain_grad = jnp.where(row == 0, gain_grad, 0.0).astype(bf16)
    small = small[...] + t_dot(gain_grad, gain_picker())
    rows = blocks[0].shape[0]
    for s, block in enumerate(blocks):
        at = column_block(s, rows)
        block[:, :WIDE] = t_dot(normed[:, at], dkv[...]).astype(bf16)
        block[:, WIDE:] = small[at].astype(bf16)


def body(
    tokens,
    cotangent,
    pair_of,
    routes,
    attn_gain,
    moe_gain,
    w_query,
    w_key,
    w_value,
    w_out,
    w_router,
    w_gate,
    w_up,
    w_down,
):
    rows = tokens.shape[1]
    half = rows // 2
    width = tokens.shape[2]
    shard = w_query.shape[1]
    ctx_count = 16
    experts = w_router.shape[2]
    columns = w_gate.shape[3]
    per_group = H // KVH
    qw = per_group * HD
    scale = 1.0 / math.sqrt(HD)
    core = lax.axis_index("core")
    ylo, z, yhi = lax.axis_index("ylo"), lax.axis_index("z"), lax.axis_index("yhi")
    x = lax.axis_index("x")
    piece_rows = 2 * shard
    slots = experts * SLOTS
    own_tokens, cot = tokens[0], cotangent[0]

    same, other, out_same, out_other = packed(
        yhi.reshape(1), w_query[0], w_key[0], w_value[0], w_router[0], attn_gain, moe_gain, w_out[0]
    )
    pieces = gather_pieces(same, other, core, ("core", "yhi"), SAME, OTHER)
    out_pieces = gather_pieces(
        out_same, out_other, yhi, ("ylo", "core", "yhi"), OUT_SAME, OUT_OTHER
    )
    other_tokens = partner(own_tokens)
    pieces, out_pieces, x, z, own_tokens, other_tokens, pair_of = together(
        pieces, out_pieces, x, z, own_tokens, other_tokens, pair_of
    )

    plane_rows = 16 * piece_rows
    plane = spread(pieces, 16, PLANE)
    both = jnp.concatenate(
        [own_tokens[:half], other_tokens[:half], own_tokens[half:], other_tokens[half:]]
    )
    out_pieces = jnp.broadcast_to(out_pieces[None], (16,) + out_pieces.shape)
    order, out_order, level_order = order_matrix(16, x), order_matrix(8, x), level_order_matrix(z)
    (expert_shards_in,) = call(
        stack_kernel, [((3,) + w_gate.shape[1:], bf16)], w_gate[0], w_up[0], w_down[0], both
    )
    (
        plane, both, out_pieces, order, out_order, level_order, pair_of, expert_shards_in, chosen,
    ) = together(
        plane, both, out_pieces, order, out_order, level_order, pair_of, expert_shards_in,
        routes[0, 0],
    )

    plane = plane.reshape(plane_rows, -1)
    w_kvs = along("x", plane[:, : 3 * HD])
    wo = exchange(out_pieces, LEVEL)
    (both,) = call(order_kernel, [((2 * rows, width), bf16)], both, order)

    def two_cores(ctx):
        return jnp.stack([ctx + core, ctx + 1 - core], axis=-1).reshape(-1)

    ctx_here = (ylo * 4 + z) * 2
    q_place = places(pair_of, two_cores(ctx_here), rows, ctx_count)
    q_place = q_place.transpose(1, 0, 2).reshape(2 * rows, 1)
    key_place = places(
        pair_of, two_cores(jnp.arange(8, dtype=jnp.int32) * 2), rows, ctx_count
    )
    low_place, up_place = key_place[:, 0].reshape(1, -1), key_place[:, 1].reshape(1, -1)
    frequency = jnp.exp(jnp.arange(HD // 2, dtype=f32) * (-2.0 * math.log(ROPE_BASE) / HD))
    angles = q_place.astype(f32) * frequency[None, :]
    cosines, sines = jnp.cos(angles), jnp.sin(angles)
    cosines = jnp.concatenate([cosines, cosines], axis=-1)
    sines = jnp.concatenate([-sines, sines], axis=-1)
    w_q, w_kvs, wo, both, q_place, low_place, up_place, cosines, sines, chosen = together(
        plane[:, 3 * HD :], w_kvs, wo, both, q_place, low_place, up_place, cosines, sines, chosen
    )

    w_q = along("x", w_q)
    wo = along("z", wo.reshape(2, qw // 4, width // 2))
    normed, key_value, gains = call(
        keys_kernel,
        [((2 * rows, width), bf16), ((8, 2 * rows, 2 * HD), bf16), ((8, width), f32)],
        both,
        cosines,
        sines,
        *w_kvs,
    )
    all_kv = exchange(key_value, RING)
    small, moe_gains = call(
        small_kernel, [((width, 128), bf16), ((8, width), f32)], order, *w_kvs
    )
    (queries,) = call(
        query_kernel, [((2 * rows, qw), bf16)], normed, cosines, sines, *w_q, cost=LONG
    )
    lanes = jnp.arange(128, dtype=jnp.int32)
    hits = (chosen.T[:, :, None] == lanes[None, None, :]).astype(bf16)
    earlier = (lanes[:, None] > lanes[None, :]).astype(bf16)
    before = dot(earlier, jnp.sum(hits, axis=0))
    slot_index = jnp.sum(hits.astype(f32) * before[None], axis=-1).astype(jnp.int32)
    target = chosen.T * SLOTS + slot_index
    slot_row = jnp.arange(slots, dtype=jnp.int32)
    places_of = (target[:, :, None] == slot_row[None, None, :]).astype(bf16)
    placer_t = jnp.sum(places_of, axis=0)
    placer = placer_t.T
    (cot_rows,) = call(order_kernel, [((slots, width), bf16)], placer, cot)
    (
        queries, all_kv, expert_shards_in, small, moe_gains, cot_rows,
        hits, places_of, placer_t, placer, wo,
    ) = together(
        queries, all_kv, expert_shards_in, small, moe_gains, cot_rows,
        hits, places_of, placer_t, placer, wo,
    )
    expert_weights = lax.all_gather(expert_shards_in, CTX, axis=2, tiled=True)

    arrived_cot = to_owners(cot_rows.reshape(experts, SLOTS, width))
    sizes = dict(scale=scale, pieces=8, heads=per_group)
    keys = 8 * rows
    mixed, mixed_back, logs, kv_low, kv_up = call(
        functools.partial(attend_kernel, **sizes),
        [
            ((2 * rows, qw), bf16),
            ((2 * rows, qw), bf16),
            ((per_group, 2 * rows, 1), f32),
            ((keys, 2 * HD), bf16),
            ((keys, 2 * HD), bf16),
        ],
        queries,
        q_place,
        low_place,
        up_place,
        level_order,
        out_order,
        all_kv,
        scratch=[pltpu.VMEM((2 * rows, qw), bf16)],
    )

    branch_own, branch_other, wo = call(
        branch_kernel,
        [((rows, width), f32), ((rows, width), f32), ((2, qw, width // 2), bf16)],
        mixed,
        *wo,
    )
    sent, midway, moe_low, gates, gate_parts = call(
        route_kernel,
        [
            ((slots, width + 128), bf16),
            ((rows, width), f32),
            ((rows, width), bf16),
            ((rows, 128), f32),
            ((3, rows, slots), bf16),
        ],
        own_tokens,
        branch_own,
        partner(branch_other),
        small,
        moe_gains,
        hits,
        places_of,
        placer,
    )
    sent, arrived_cot = together(sent, arrived_cot)

    sent = to_owners(sent.reshape(experts, SLOTS, width + 128)).reshape(slots, width + 128)
    mine = core.reshape(1)
    arrived_cot = arrived_cot.reshape(slots, width)
    expert_out, rows_grad, hidden, gate_grad, up_grad = expert_call(
        mine,
        [sent, arrived_cot],
        expert_weights,
        [width, width + 128, columns, columns, columns],
    )
    rows_grad, gate_grad, up_grad = together(rows_grad, gate_grad, up_grad)

    home_grad = to_owners(rows_grad.reshape(experts, SLOTS, width + 128))
    expert_sums = expert_weights_grad(sent, arrived_cot, hidden, gate_grad, up_grad)
    home_grad, expert_sums, expert_out = together(home_grad, expert_sums, expert_out)
    expert_sums = lax.psum_scatter(expert_sums, RING, scatter_dimension=1, tiled=True)

    returned = to_owners(expert_out.reshape(experts, SLOTS, width))
    midway_grad, branch_low, gain_two_grad, router_grad = call(
        home_kernel,
        [((rows, width), f32), ((rows, width), bf16), ((8, width), f32), ((width, 128), f32)],
        placer_t,
        home_grad.reshape(slots, width + 128),
        midway,
        cot,
        moe_gains,
        hits,
        places_of,
        gates,
        small,
        moe_low,
    )
    branch, *out_w_grad = call(
        out_grad_kernel,
        [((2 * rows, width), bf16)] + [((2, qw // 4, width // 2), bf16)] * 4,
        mixed_back,
        branch_low,
        partner(branch_low),
    )
    branch, out_w_grad = together(branch, out_w_grad)
    out_w_grad = back_along_x(out_w_grad)

    dq, dkv, *q_w_grad = call(
        functools.partial(attend_back_kernel, **sizes),
        [((2 * rows, qw), bf16), ((8, 2 * rows, 2 * HD), bf16)]
        + [((plane_rows, qw), bf16)] * 4,
        branch,
        wo,
        level_order,
        queries,
        kv_low,
        kv_up,
        logs,
        q_place,
        low_place,
        up_place,
        cosines,
        sines,
        normed,
        scratch=[
            pltpu.VMEM((2 * rows, qw), bf16),
            pltpu.VMEM((2 * HD, keys), f32),
            pltpu.VMEM((2 * HD, keys), f32),
        ],
    )
    dkv, q_w_grad, returned, late = together(dkv, q_w_grad, returned, gain_two_grad)

    dkv = exchange(dkv, RING)
    q_w_grad = back_along_x(q_w_grad)
    (small_grad,) = call(
        small_grad_kernel, [((width, 128), f32)], order, router_grad, gain_two_grad, late
    )
    out_w_grad = added(out_w_grad, small_grad)
    dkv, out_w_grad, small_grad, q_w_grad[1], q_w_grad[3] = together(
        dkv, out_w_grad, small_grad, q_w_grad[1], q_w_grad[3]
    )

    dkv, normed_own, normed_other = call(
        sum_kernel,
        [((2 * rows, 2 * HD), bf16), ((rows, width), f32), ((rows, width), f32)],
        dq,
        cosines,
        sines,
        *w_q,
        *w_kvs,
        dkv,
    )
    input_grad, *kvs_grad = call(
        input_kernel,
        [((rows, width), f32)] + [((plane_rows, 3 * HD), bf16)] * 4,
        both,
        normed_own,
        partner(normed_other),
        midway_grad,
        gains,
        order,
        small_grad,
        normed,
        dkv,
    )
    kvs_grad, out_w_grad, input_grad = together(kvs_grad, out_w_grad, input_grad)

    out_w_grad = exchange(out_w_grad.reshape(16, piece_rows, width // 2), OUT_PLANE)
    kvs_grad = back_along_x(kvs_grad)
    (plane_grad,) = call(
        add_both_kernel, [((plane_rows, qw + 3 * HD), bf16)], *q_w_grad, *kvs_grad, cost=LONG
    )
    plane_grad, out_w_grad, returned = together(plane_grad, out_w_grad, returned)
    plane_grad = exchange(plane_grad.reshape(16, piece_rows, qw + 3 * HD), PLANE)

    (output,) = call(
        combine_kernel,
        [((rows, width), bf16)],
        midway,
        gate_parts,
        returned.reshape(slots, width),
    )

    def summed(pieces):
        return jnp.sum(pieces.astype(f32), axis=0)

    def expert_shards(grad):
        count = grad.shape[1] // 2
        kept = lax.dynamic_slice_in_dim(grad, core * count, count, axis=1)
        given = partner(lax.dynamic_slice_in_dim(grad, (1 - core) * count, count, axis=1))
        both = jnp.stack([pick(core, kept, given), pick(core, given, kept)], axis=1)
        return [both[i : i + 1].astype(f32) for i in range(3)]

    out_w_grad = scatter_pieces(
        summed(out_w_grad), yhi, yhi, ("ylo", "core", "yhi"), OUT_SAME, OUT_OTHER
    )
    w_gate_grad, w_up_grad, w_down_grad = expert_shards(expert_sums)
    plane_grad, w_gate_grad, w_up_grad, w_down_grad, output = together(
        plane_grad, w_gate_grad, w_up_grad, w_down_grad, output
    )
    plane_grad = scatter_pieces(summed(plane_grad), yhi, core, ("core", "yhi"), SAME, OTHER)
    plane_grad = plane_grad.reshape(shard, 2, -1)

    def joined(first, last):
        return plane_grad[:, :, first:last].reshape(1, shard, -1)

    small_grad = jnp.sum(plane_grad[None, :, :, qw + 2 * HD :], axis=2)

    return (
        output[None],
        input_grad[None],
        small_grad[:, :, experts],
        small_grad[:, :, experts + 1],
        joined(0, qw),
        joined(qw, qw + HD),
        joined(qw + HD, qw + 2 * HD),
        out_w_grad[None],
        small_grad[:, :, :experts],
        w_gate_grad,
        w_up_grad,
        w_down_grad,
    )


def solution(mesh):
    fine = Mesh(mesh.devices.reshape(2, 4, 2, 4, 2), AXES)
    seq = P(FSDP, CTX, None)
    vector = P(None, AXES)
    matrix = P(None, AXES, None)
    expert = P(None, FSDP, CTX, None)
    in_specs = (
        seq,
        seq,
        P(),
        P(None, FSDP, CTX, None),
        vector,
        vector,
        matrix,
        matrix,
        matrix,
        matrix,
        matrix,
        expert,
        expert,
        expert,
    )
    out_specs = (
        seq,
        seq,
        vector,
        vector,
        matrix,
        matrix,
        matrix,
        matrix,
        matrix,
        expert,
        expert,
        expert,
    )
    return jax.shard_map(body, mesh=fine, in_specs=in_specs, out_specs=out_specs, check_vma=False)
```
